32 devices in a mesh: gx: 8 (over y, x, core), gy: 4 (over z).
Axes of the slice: x: 2, y: 2, z: 4, core: 2. Of those that a mesh axis runs over, the one named last changes fastest.
Arguments:
- forces: float32 [3, 24, 16, 32, 128], P(None, None, 'gx', 'gy'), may hold values from -6 to 6
- levels: int32 [16, 32, 128], P('gx', 'gy'), may hold values from 0 to 15
- supports: int32 [16, 32, 128], P('gx', 'gy'), may hold values 0 or 1
Outputs:
- filtered: float32 [16, 32, 128], P('gx', 'gy')
The draws below stay inside these ranges and needn't reach their ends.
All inputs are finite; a program needn't handle non-finite values. No bound on the sum of `supports` on one device may be relied on, other than what follows from the above.
Results may differ from the reference program's by a relative error of at most 0.0001.
Values sent between devices are 32-bit elements; how exact they have to be, the bound alone decides.
No kernel may reach another device: no remote copies, remote signals or barrier semaphores. Data moves between devices by JAX's collectives and lax.ppermute only.
A program may use at most 128 MiB of HBM per device.

```python
import math
import jax
import jax.numpy as jnp
import numpy as np
from jax import lax

NZ = 128
CASES = 24
LEVELS = 16
ITERS = 2
NX = 16
NY = 32


def place_ends(values, own_key, least, largest):
    dims = values.shape
    place = [jax.random.randint(jax.random.fold_in(own_key, axis), (), 0, dims[axis]) for axis in range(len(dims))]
    values = values.at[tuple(place)].set(least)
    longest = dims.index(max(dims))
    place[longest] = (place[longest] + 1) % dims[longest]
    return values.at[tuple(place)].set(largest)


def shard_levels(key, shape, shards, low, top_value):
    def one(dim, blocks):
        steps = jax.random.uniform(jax.random.fold_in(jax.random.fold_in(key, 6), dim), (blocks,), jnp.float32, low / len(shards), top_value / len(shards))
        return jnp.repeat(jnp.exp(steps), shape[dim] // blocks).reshape((-1,) + (1,) * (len(shape) - dim - 1))

    level = one(*shards[0])
    for cut in shards[1:]:
        level = level * one(*cut)
    return level


def noise(stream_key, dims, deviation, limit, shards=(), held_as=jnp.bfloat16):
    array = jax.random.normal(stream_key, dims, jnp.float32) * deviation
    if len(shards) > 0:
        array = shard_levels(stream_key, dims, shards, -0.22, 0.18) * array
    return jnp.clip(array, min=-limit, max=limit).astype(held_as)


def setup_inputs(seed: int = 0) -> dict:
    splits = jax.random.split(jax.random.key(seed), 4)
    return {
        "forces": noise(splits[0], (3, CASES, NX, NY, NZ), 1.0, 6.0, ((2, 8), (3, 4)), jnp.float32),
        "levels": place_ends(jax.random.randint(splits[1], (NX, NY, NZ), 0, LEVELS), jax.random.fold_in(splits[1], 1), 0, LEVELS - 1).astype(jnp.int32),
        "supports": place_ends((jax.random.randint(splits[2], (NX, NY, NZ), 0, 16) < 1).astype(jnp.int32), jax.random.fold_in(splits[2], 1), 0, 1),
    }


load_factor = 0.2

def element_matrix():
    poisson = 0.3
    lame_first = poisson / ((1.0 + poisson) * (1.0 - 2.0 * poisson))
    lame_shear = 1.0 / (2.0 * (1.0 + poisson))
    elastic = np.zeros((6, 6))
    elastic[:3, :3] = lame_first
    for position in range(3):
        elastic[position, position] += 2.0 * lame_shear
        elastic[position + 3, position + 3] = lame_shear
    points = [0.5 - 0.5 / math.sqrt(3.0), 0.5 + 0.5 / math.sqrt(3.0)]
    matrix = np.zeros((24, 24))
    for point_x in points:
        for point_y in points:
            for point_z in points:
                coords = (point_x, point_y, point_z)
                strain = np.zeros((6, 24))
                for corner in range(8):
                    corner_bits = (corner >> 2 & 1, corner >> 1 & 1, corner & 1)
                    shape_values = [coords[axis_n] if corner_bits[axis_n] else 1.0 - coords[axis_n] for axis_n in range(3)]
                    slopes = [1.0 if corner_bits[axis_n] else -1.0 for axis_n in range(3)]
                    slope_x = slopes[0] * shape_values[1] * shape_values[2]
                    slope_y = shape_values[0] * slopes[1] * shape_values[2]
                    slope_z = shape_values[0] * shape_values[1] * slopes[2]
                    offset = 3 * corner
                    strain[0, offset] = slope_x
                    strain[1, offset + 1] = slope_y
                    strain[2, offset + 2] = slope_z
                    strain[3, offset] = slope_y
                    strain[3, offset + 1] = slope_x
                    strain[4, offset + 1] = slope_z
                    strain[4, offset + 2] = slope_y
                    strain[5, offset] = slope_z
                    strain[5, offset + 2] = slope_x
                matrix = matrix + strain.T @ elastic @ strain / 8.0
    return matrix

def corner_stack(field_in, lead_in, span_x, span_y, span_z):
    pieces = []
    for corner in range(8):
        step_x, step_y, step_z = (corner >> 2 & 1, corner >> 1 & 1, corner & 1)
        pieces.append(field_in[:, :, lead_in + step_x:lead_in + step_x + span_x, lead_in + step_y:lead_in + step_y + span_y, lead_in + step_z:lead_in + step_z + span_z])
    stacked = jnp.stack(pieces, 0)
    return stacked.reshape((24,) + stacked.shape[2:])

def element_forces(extended, stiff_ext, element_stiff):
    span_x, span_y, span_z = (extended.shape[2] - 2, extended.shape[3] - 2, extended.shape[4] - 2)
    outputs = []
    for first_case in range(0, extended.shape[1], 6):
        case_group = extended[:, first_case:first_case + 6]
        gathered = corner_stack(case_group, 0, span_x + 1, span_y + 1, span_z + 1)
        product = jnp.einsum('ab,bcxyz->acxyz', element_stiff, gathered, precision=lax.Precision.HIGHEST) * stiff_ext
        product = product.reshape((8, 3) + product.shape[1:])
        summed = jnp.zeros((3, case_group.shape[1], span_x, span_y, span_z), jnp.float32)
        for corner in range(8):
            step_x, step_y, step_z = (corner >> 2 & 1, corner >> 1 & 1, corner & 1)
            summed = summed + product[corner][:, :, 1 - step_x:1 - step_x + span_x, 1 - step_y:1 - step_y + span_y, 1 - step_z:1 - step_z + span_z]
        outputs.append(summed)
    return jnp.concatenate(outputs, 1)

def element_energy(extended, element_stiff):
    span_x, span_y, span_z = (extended.shape[2] - 2, extended.shape[3] - 2, extended.shape[4] - 2)
    summed = jnp.zeros((span_x, span_y, span_z), jnp.float32)
    for first_case in range(0, extended.shape[1], 6):
        case_group = extended[:, first_case:first_case + 6]
        gathered = corner_stack(case_group, 1, span_x, span_y, span_z)
        product = jnp.einsum('ab,bcxyz->acxyz', element_stiff, gathered, precision=lax.Precision.HIGHEST)
        summed = summed + lax.optimization_barrier(jnp.sum(gathered * product, axis=(0, 1)))
    return summed

def node_diagonal(stiff_ext, free_mask, element_stiff):
    span_x, span_y, span_z = free_mask.shape
    parts = []
    for component in range(3):
        summed = jnp.zeros((span_x, span_y, span_z), jnp.float32)
        for corner in range(8):
            step_x, step_y, step_z = (corner >> 2 & 1, corner >> 1 & 1, corner & 1)
            summed = summed + stiff_ext[1 - step_x:1 - step_x + span_x, 1 - step_y:1 - step_y + span_y, 1 - step_z:1 - step_z + span_z] * element_stiff[3 * corner + component, 3 * corner + component]
        parts.append(summed)
    diagonal = jnp.stack(parts, 0)[:, None]
    return 1.0 / (free_mask * diagonal + (1.0 - free_mask))

def block_gram(first_field, second_field):
    return jnp.einsum('kcxyz,kdxyz->cd', first_field, second_field, precision=lax.Precision.HIGHEST)

def combine(field_in, mixing):
    return jnp.einsum('kcxyz,cd->kdxyz', field_in, mixing, precision=lax.Precision.HIGHEST)

def cone_filter(rimmed, density):
    span_x, span_y, span_z = density.shape
    numerator = jnp.zeros((span_x, span_y, span_z), jnp.float32)
    denominator = jnp.zeros((span_x, span_y, span_z), jnp.float32)
    for shift_x in range(-2, 3):
        for shift_y in range(-2, 3):
            for shift_z in range(-2, 3):
                weight = 2.5 - math.sqrt(shift_x * shift_x + shift_y * shift_y + shift_z * shift_z)
                if weight > 0.0:
                    window = rimmed[:, 2 + shift_x:2 + shift_x + span_x, 2 + shift_y:2 + shift_y + span_y, 2 + shift_z:2 + shift_z + span_z]
                    numerator = numerator + weight * window[0]
                    denominator = denominator + weight * window[1]
    return numerator / (density * denominator)

def reference(forces, levels, supports):
    element_stiff = jnp.asarray(element_matrix(), jnp.float32)
    free_mask = (1 - supports).astype(jnp.float32)
    density = 0.3 + 0.7 * levels.astype(jnp.float32) / (LEVELS - 1)
    stiffness = density ** 3
    stiff_ext = jnp.pad(stiffness, ((1, 0), (1, 0), (1, 0)))
    inverse = node_diagonal(stiff_ext, free_mask, element_stiff)

    def operate(field_in):
        extended = jnp.pad(free_mask * field_in, ((0, 0), (0, 0), (1, 1), (1, 1), (1, 1)))
        return free_mask * element_forces(extended, stiff_ext, element_stiff) + (1.0 - free_mask) * field_in
    load_field = load_factor * free_mask * forces
    solution = jnp.zeros_like(load_field)
    residual = load_field
    direction = inverse * residual
    for iteration in range(ITERS):
        image_field = operate(direction)
        curvature = block_gram(direction, image_field)
        factor = jnp.linalg.cholesky(curvature)
        step_alpha = jax.scipy.linalg.cho_solve((factor, True), block_gram(direction, residual))
        solution = solution + combine(direction, step_alpha)
        residual = residual - combine(image_field, step_alpha)
        if iteration + 1 < ITERS:
            scaled_res = inverse * residual
            step_beta = -jax.scipy.linalg.cho_solve((factor, True), block_gram(image_field, scaled_res))
            direction = scaled_res + combine(direction, step_beta)
    extended = jnp.pad(free_mask * solution, ((0, 0), (0, 0), (1, 1), (1, 1), (1, 1)))
    energy = element_energy(extended, element_stiff)
    sensitivity = -3.0 * density ** 2 * energy / CASES
    stacked = jnp.stack([density * sensitivity, jnp.ones_like(density)], 0)
    rimmed = jnp.pad(stacked, ((0, 0), (2, 2), (2, 2), (2, 2)))
    return cone_filter(rimmed, density)
```

```python
import functools
import math

import jax
import jax.numpy as jnp
from jax import lax
from jax.experimental import pallas as pl
from jax.experimental.pallas import tpu as pltpu
from jax.sharding import PartitionSpec as P

LEVELS = 16
LOAD = 0.2
LANES = 128
POISSON = 0.3
LAME = POISSON / ((1.0 + POISSON) * (1.0 - 2.0 * POISSON))
SHEAR = 1.0 / (2.0 * (1.0 + POISSON))
DIAGONAL = (LAME + 2.0 * SHEAR) / 9.0 + 2.0 * SHEAR / 9.0
VMEM = pl.BlockSpec(memory_space=pltpu.VMEM)
PARAMS = pltpu.CompilerParams(vmem_limit_bytes=50 * 2**20)
f32 = jnp.float32
bf16 = jnp.bfloat16


def up8(count):
    return -(-count // 8) * 8


def shift_down(value):
    lane = lax.broadcasted_iota(jnp.int32, value.shape, value.ndim - 1)
    rolled = pltpu.roll(value, LANES - 1, value.ndim - 1)
    return jnp.where(lane == LANES - 1, 0.0, rolled)


def shift_up(value):
    lane = lax.broadcasted_iota(jnp.int32, value.shape, value.ndim - 1)
    return jnp.where(lane == 0, 0.0, pltpu.roll(value, 1, value.ndim - 1))


def split(value):
    high = value.astype(bf16)
    return high, (value - high.astype(f32)).astype(bf16)


def modes_of(lower, upper):
    out = [[[[None] * 3 for _ in range(2)] for _ in range(2)] for _ in range(2)]
    for a in range(2):
        for c in range(2):
            for k in range(3):
                if a or c:
                    out[a][0][c][k] = lower[a][c][k] + upper[a][c][k]
                out[a][1][c][k] = upper[a][c][k] - lower[a][c][k]
    return out


PAIRS = (((1, 1, 0, 0), (0, 1, 1, 2)), ((1, 0, 1, 0), (0, 1, 1, 1)), ((1, 1, 0, 1), (1, 0, 1, 2)))
TRIPLE = ((0, 1, 1, 0), (1, 0, 1, 1), (1, 1, 0, 2))
SHEARS = (((0, 1, 0, 0), (1, 0, 0, 1)), ((0, 0, 1, 0), (1, 0, 0, 2)), ((0, 0, 1, 1), (0, 1, 0, 2)))
AXIAL = ((1, 0, 0, 0), (0, 1, 0, 1), (0, 0, 1, 2))


def at(modes, place):
    a, b, c, k = place
    return modes[a][b][c][k]


def mode_forces(modes, stiff):
    out = [[[[None] * 3 for _ in range(2)] for _ in range(2)] for _ in range(2)]

    def put(place, value):
        a, b, c, k = place
        out[a][b][c][k] = value

    shear = stiff * (SHEAR / 16)
    for first, second in SHEARS:
        force = shear * (at(modes, first) + at(modes, second))
        put(first, force)
        put(second, force)
    one, two, three = (at(modes, place) for place in AXIAL)
    volume = (stiff * (LAME / 16)) * (one + two + three)
    axial = stiff * (SHEAR / 8)
    for place in AXIAL:
        put(place, volume + axial * at(modes, place))
    own, cross = stiff * ((LAME + 3 * SHEAR) / 48), stiff * (LAME / 48)
    for first, second in PAIRS:
        one, two = at(modes, first), at(modes, second)
        put(first, own * one + cross * two)
        put(second, own * two + cross * one)
    twist = stiff * (SHEAR / 48)
    one, two, three = (at(modes, place) for place in TRIPLE)
    total = one + two + three
    for place in TRIPLE:
        put(place, twist * (total + at(modes, place)))
    last = stiff * ((LAME + 4 * SHEAR) / 144)
    for k in range(3):
        put((1, 1, 1, k), last * modes[1][1][1][k])
    return out


def mode_energy(modes):
    def square(value):
        return value * value

    shear = None
    for first, second in SHEARS:
        term = square(at(modes, first) + at(modes, second))
        shear = term if shear is None else shear + term
    one, two, three = (at(modes, place) for place in AXIAL)
    energy = (SHEAR / 16) * shear + (LAME / 16) * square(one + two + three)
    energy = energy + (SHEAR / 8) * (square(one) + square(two) + square(three))
    squares, products = None, None
    for first, second in PAIRS:
        one, two = at(modes, first), at(modes, second)
        term, product = square(one) + square(two), one * two
        squares = term if squares is None else squares + term
        products = product if products is None else products + product
    energy = energy + ((LAME + 3 * SHEAR) / 48) * squares + (LAME / 24) * products
    one, two, three = (at(modes, place) for place in TRIPLE)
    twist = square(one + two + three) + square(one) + square(two) + square(three)
    energy = energy + (SHEAR / 48) * twist
    last = square(modes[1][1][1][0]) + square(modes[1][1][1][1]) + square(modes[1][1][1][2])
    return energy + ((LAME + 4 * SHEAR) / 144) * last


def x_modes(sums, diffs, plane, row, tile, cases, columns):
    out = [[[None] * 3 for _ in range(2)] for _ in range(2)]
    for c, ref in enumerate((sums, diffs)):
        for k in range(3):
            rows = pl.ds(pl.multiple_of(k * cases + tile * 8, 8), 8)
            one = ref[plane * columns + row, rows, :]
            two = ref[(plane + 1) * columns + row, rows, :]
            out[0][c][k] = one + two
            out[1][c][k] = two - one
    return out


def apply_elements(
    sums, diffs, stiff_ref, acc_s, acc_d, planes, rows, skip, stiff_x, stiff_y, cases
):
    columns = rows + 1
    acc_columns = columns - 2 * skip
    tiles = cases // 8

    def step(index, _):
        plane, tile = index // tiles, index % tiles

        def emit(row, total):
            if not skip <= row < columns - skip:
                return
            for c, acc in enumerate((acc_s, acc_d)):
                for k in range(3):
                    lines = pl.ds(pl.multiple_of(k * cases + tile * 8, 8), 8)
                    low = plane * acc_columns + row - skip
                    acc[low, lines, :] += total[0][c][k] - total[1][c][k]
                    acc[low + acc_columns, lines, :] = total[0][c][k] + total[1][c][k]

        lower = x_modes(sums, diffs, plane, 0, tile, cases, columns)
        carry = None
        for row in range(rows):
            upper = x_modes(sums, diffs, plane, row + 1, tile, cases, columns)
            stiff = jnp.broadcast_to(
                stiff_ref[plane + stiff_x, pl.ds(row + stiff_y, 1), :], (8, LANES)
            )
            forces = mode_forces(modes_of(lower, upper), stiff)
            here = [[[None] * 3 for _ in range(2)] for _ in range(2)]
            following = [[[None] * 3 for _ in range(2)] for _ in range(2)]
            for a in range(2):
                for c in range(2):
                    for k in range(3):
                        one, two = forces[a][0][c][k], forces[a][1][c][k]
                        low = -two if one is None else one - two
                        high = two if one is None else one + two
                        here[a][c][k] = low if carry is None else carry[a][c][k] + low
                        following[a][c][k] = high
            emit(row, here)
            carry, lower = following, upper
        emit(rows, carry)
        return 0

    lax.fori_loop(0, planes * tiles, step, 0)


def pack_kernel(sizes, forces, levels, supports, own, up, *rest):
    planes, rows, cases = sizes
    block = 3 * cases
    base = planes * rows * block
    *down, ym, yp, mm, mp, pm, pp = rest
    for x in range(planes):
        density = 0.3 + 0.7 * levels[x].astype(f32) / (LEVELS - 1)
        stiff = density * density * density
        free = supports[x] == 0
        own[base + x * rows : base + (x + 1) * rows, :] = jnp.where(free, stiff, -stiff)
        scale = jnp.where(free, LOAD, 0.0)
        for k in range(3):
            for c in range(cases):
                start = x * rows * block + k * cases + c
                own[pl.ds(start, rows, stride=block), :] = forces[k, c, x] * scale

    def fill(ref, xs, ys, code_xs, code_ys):
        line = 0
        for x in xs:
            for y in ys:
                start = (x * rows + y) * block
                ref[line : line + block, :] = own[start : start + block, :]
                line += block
        for x in code_xs:
            for y in code_ys:
                start = base + x * rows + y
                ref[line : line + 1, :] = own[start : start + 1, :]
                line += 1
        if line < ref.shape[0]:
            ref[line:, :] = jnp.zeros((ref.shape[0] - line, LANES), f32)

    every_x, every_y = range(planes), range(rows)
    first_x, last_x = range(2), range(planes - 2, planes)
    first_y, last_y = range(2), range(rows - 2, rows)
    fill(up, last_x[1:], every_y, last_x, every_y)
    for ref in down:
        fill(ref, first_x, every_y, first_x, every_y)
    fill(ym, every_x, first_y, every_x, first_y)
    fill(yp, every_x, last_y[1:], every_x, last_y)
    fill(mm, first_x, first_y, first_x, first_y)
    fill(mp, first_x, last_y[1:], first_x, last_y)
    fill(pm, last_x[1:], first_y, last_x, first_y)
    fill(pp, last_x[1:], last_y[1:], last_x, last_y)


def main_kernel(
    sizes, own, xm, xp, ym, yp, mm, mp, pm, pp, both_out, system_out, stiff_ref, inverse,
    start, sums, diffs, acc_s, acc_d, w_sums, w_diffs, acc2_s, acc2_d, right, second,
):
    planes, rows, cases = sizes
    block = 3 * cases
    xs, ys = planes + 3, rows + 3
    every_x, every_y = range(planes), range(rows)
    low, high_x, high_y = (-1,), (planes, planes + 1), (rows, rows + 1)
    low2 = (-2, -1)
    regions = (
        (own, every_x, every_y, every_x, every_y),
        (xm, low, every_y, low2, every_y),
        (xp, high_x, every_y, high_x, every_y),
        (ym, every_x, low, every_x, low2),
        (yp, every_x, high_y, every_x, high_y),
        (mm, low, low, low2, low2),
        (mp, low, high_y, low2, high_y),
        (pm, high_x, low, high_x, low2),
        (pp, high_x, high_y, high_x, high_y),
    )
    for ref, bx, by, cx, cy in regions:
        base = len(bx) * len(by) * block
        for i, x in enumerate(cx):
            line = base + i * len(cy)
            stiff_ref[x + 2, cy[0] + 2 : cy[0] + 2 + len(cy), :] = ref[line : line + len(cy), :]
    for x in range(-1, planes + 2):
        codes = stiff_ref[x + 2, 0 : ys + 1, :]
        total = jnp.abs(stiff_ref[x + 1, 0 : ys + 1, :]) + jnp.abs(codes)
        total = total[:-1] + total[1:]
        total = total + shift_up(total)
        free = codes[1:] > 0.0
        value = 1.0 / (DIAGONAL * jnp.where(free, total, 1.0))
        inverse[x + 1, 0:ys, :] = jnp.where(free, value, 0.0)
    for x in range(planes + 4):
        stiff_ref[x] = jnp.abs(stiff_ref[x])

    for ref, bx, by, _, _ in regions:
        for i, x in enumerate(bx):

            def place(j, _, ref=ref, i=i, x=x, by=by):
                y = j + by[0] + 1
                load = ref[pl.ds(pl.multiple_of((i * len(by) + j) * block, 8), block), :]
                value = load * inverse[x + 1, pl.ds(y, 1), :]
                column = (x + 1) * ys + y
                start[column] = value
                moved = shift_down(value)
                sums[column] = value + moved
                diffs[column] = moved - value
                return 0

            lax.fori_loop(0, len(by), place, 0)

    nodes_y = rows + 1
    apply_elements(
        sums, diffs, stiff_ref, acc_s, acc_d, planes + 2, rows + 2, 1, 1, 1, cases
    )

    def image(x, y, place):
        column = (x + 1) * nodes_y + y
        s, d = acc_s[column], acc_d[column]
        force = s - d + shift_up(s + d)
        scaled = force * inverse[x + 1, pl.ds(y + 1, 1), :]
        moved = shift_down(scaled)
        w_sums[x * nodes_y + y] = scaled + moved
        w_diffs[x * nodes_y + y] = moved - scaled
        value = start[(x + 1) * ys + y + 1]
        for k in range(3):
            lines = slice(k * cases, (k + 1) * cases)
            pair = jnp.concatenate([value[lines], scaled[lines]], 0)
            lane = pl.ds(pl.multiple_of((place * 3 + k) * LANES, LANES), LANES)
            high, rest = split(pair)
            both_out[0 : 2 * cases, lane] = high
            both_out[2 * cases : 4 * cases, lane] = rest
        return force

    def inside(index, _):
        x, y = index // rows, index % rows
        force = image(x, y, index)
        load = own[pl.ds(pl.multiple_of(index * block, 8), block), :]
        for k in range(3):
            lines = slice(k * cases, (k + 1) * cases)
            pair = jnp.concatenate([load[lines], force[lines]], 0)
            lane = pl.ds(pl.multiple_of((index * 3 + k) * LANES, LANES), LANES)
            high, rest = split(pair)
            right[0 : 2 * cases, lane] = high
            right[2 * cases : 4 * cases, lane] = rest
        return 0

    count = planes * rows
    lax.fori_loop(0, count, inside, 0)

    def beyond_y(x, _):
        image(x, rows, count + x)
        return 0

    lax.fori_loop(0, planes, beyond_y, 0)

    def beyond_x(y, _):
        image(planes, y, count + planes + y)
        return 0

    lax.fori_loop(0, nodes_y, beyond_x, 0)

    for column in range(nodes_y):
        acc2_s[column] = jnp.zeros((block, LANES), f32)
        acc2_d[column] = jnp.zeros((block, LANES), f32)
    apply_elements(w_sums, w_diffs, stiff_ref, acc2_s, acc2_d, planes, rows, 0, 2, 2, cases)

    def second_force(x, y, place):
        column = x * nodes_y + y
        s, d = acc2_s[column], acc2_d[column]
        force = s - d + shift_up(s + d)
        for k in range(3):
            value = force[k * cases : (k + 1) * cases]
            high = value.astype(bf16).astype(f32)
            lane = pl.ds(pl.multiple_of((place * 3 + k) * LANES, LANES), LANES)
            second[:, lane] = jnp.concatenate([high, value - high], 0).astype(bf16)

    def second_inside(index, _):
        second_force(index // rows, index % rows, index)
        return 0

    def second_y(x, _):
        second_force(x, rows, count + x)
        return 0

    def second_x(y, _):
        second_force(planes, y, count + planes + y)
        return 0

    lax.fori_loop(0, count, second_inside, 0)
    lax.fori_loop(0, planes, second_y, 0)
    lax.fori_loop(0, nodes_y, second_x, 0)

    contract = (((1,), (1,)), ((), ()))
    width = count * 3 * LANES
    two = 2 * cases
    gram = lax.dot_general(both_out[:, :width], right[...], contract, preferred_element_type=f32)
    gram = gram[:two] + gram[two:]
    gram = gram[:, :two] + gram[:, two:]
    other = lax.dot_general(both_out[...], second[...], contract, preferred_element_type=f32)
    other = other[:two] + other[two:]
    other = other[:, :cases] + other[:, cases:]
    system_out[...] = jnp.zeros(system_out.shape, f32)
    system_out[0:cases, 0:cases] = gram[:cases, cases:]
    system_out[0:cases, cases:two] = other[:cases]
    system_out[cases:two, 0:cases] = gram[cases:, cases:]
    system_out[cases:two, cases:two] = other[cases:]
    system_out[two : two + cases, 0:two] = gram[:cases]


def solve_kernel(sizes, system, both, levels, out, mixing, sums, diffs, energy):
    planes, rows, cases = sizes
    two = 2 * cases
    nodes_y = rows + 1
    count = planes * rows
    table = system[...]
    lane = lax.broadcasted_iota(jnp.int32, (1, LANES), 1)
    gone = 0
    for pivot in range(two):
        drop = pivot // 8 * 8 - gone
        table = table[drop:]
        gone += drop
        line = pivot - gone
        row = table[line : line + 1, :]
        inverse = 1.0 / row[:, pivot : pivot + 1]
        row = jnp.where(lane == pivot, -inverse, row * inverse)
        column = table[:, pivot : pivot + 1]
        table = jnp.where(lane == pivot, 0.0, table) - column * row
    answer = table[two - gone :, :two]
    high = answer.astype(bf16).astype(f32)
    mixing[...] = jnp.zeros(mixing.shape, f32)
    mixing[0:cases, 0:two] = high
    mixing[0:cases, two : 2 * two] = high
    mixing[cases:two, 0:two] = answer - high
    mix = mixing[...][:, : 2 * two].astype(bf16)

    def combined(place, width):
        lanes = pl.ds(pl.multiple_of(place * 3 * LANES, LANES), width * 3 * LANES)
        value = jnp.dot(mix, both[:, lanes], preferred_element_type=f32)
        return value[:cases] + value[cases:]

    def keep(value, index, column):
        for k in range(3):
            part = value[:, (index * 3 + k) * LANES : (index * 3 + k + 1) * LANES]
            moved = shift_down(part)
            sums[column, k * cases : (k + 1) * cases, :] = part + moved
            diffs[column, k * cases : (k + 1) * cases, :] = moved - part

    def inside(x, _):
        value = combined(x * rows, rows)
        for y in range(rows):
            keep(value, y, x * nodes_y + y)
        return 0

    lax.fori_loop(0, planes, inside, 0)
    value = combined(count, planes + nodes_y)
    for x in range(planes):
        keep(value, x, x * nodes_y + rows)
    for y in range(nodes_y):
        keep(value, planes + y, planes * nodes_y + y)

    tiles = cases // 8

    def step(plane, _):
        for tile in range(tiles):
            lower = x_modes(sums, diffs, plane, 0, tile, cases, nodes_y)
            for row in range(rows):
                upper = x_modes(sums, diffs, plane, row + 1, tile, cases, nodes_y)
                part = mode_energy(modes_of(lower, upper))
                if tile == 0:
                    energy[row] = part
                else:
                    energy[row] += part
                lower = upper
        total = jnp.sum(energy[...], axis=1)
        density = 0.3 + 0.7 * levels[plane].astype(f32) / (LEVELS - 1)
        out[plane] = (-3.0 / cases) * (density * density * density) * total
        return 0

    lax.fori_loop(0, planes, step, 0)


def filter_kernel(sizes, totals, start, below, above, own, left, right, levels, out, wide, there):
    planes, rows, _ = sizes
    weight = [2.5 - math.sqrt(q) for q in range(7)]
    wide[0:2, 2 : 2 + rows, :] = below[...]
    wide[2 : 2 + planes, 2 : 2 + rows, :] = own[...]
    wide[2 + planes :, 2 : 2 + rows, :] = above[...]
    wide[:, 0:2, :] = left[...]
    wide[:, 2 + rows : 4 + rows, :] = right[...]
    y = lax.broadcasted_iota(jnp.int32, (rows + 4, LANES), 0) + (start[1] - 2)
    in_y = jnp.logical_and(y >= 0, y < totals[1])
    for x in range(planes + 4):
        global_x = start[0] + (x - 2)
        in_x = jnp.logical_and(global_x >= 0, global_x < totals[0])
        there[x] = jnp.where(jnp.logical_and(in_y, in_x), 1.0, 0.0)

    def smooth(ref, x):
        near = {}
        for dx in range(-2, 3):
            for dy in range(-2, 3):
                q = dx * dx + dy * dy
                if q <= 5:
                    value = ref[x + 2 + dx, 2 + dy : 2 + dy + rows, :]
                    near[q] = value if q not in near else near[q] + value
        result = 0.0
        for dz in range(3):
            part = None
            for q, value in near.items():
                if q + dz * dz <= 6:
                    term = weight[q + dz * dz] * value
                    part = term if part is None else part + term
            if dz == 0:
                result = part
            else:
                place = lax.broadcasted_iota(jnp.int32, part.shape, 1)
                forward = jnp.where(place >= LANES - dz, 0.0, pltpu.roll(part, LANES - dz, 1))
                backward = jnp.where(place < dz, 0.0, pltpu.roll(part, dz, 1))
                result = result + (forward + backward)
        return result

    for x in range(planes):
        density = 0.3 + 0.7 * levels[x].astype(f32) / (LEVELS - 1)
        out[x] = smooth(wide, x) / (density * smooth(there, x))


def local(forces, levels, supports):
    _, cases, planes, rows, _ = forces.shape
    sizes = (planes, rows, cases)
    block = 3 * cases
    count_x, count_y = lax.axis_size("gx"), lax.axis_size("gy")

    def shape(blocks, codes):
        return jax.ShapeDtypeStruct((blocks * block + up8(codes), LANES), f32)

    whole = shape(planes * rows, planes * rows)
    down = [] if planes == 2 else [shape(2 * rows, 2 * rows)]
    packed = pl.pallas_call(
        functools.partial(pack_kernel, sizes),
        out_shape=[
            whole, shape(rows, 2 * rows), *down, shape(2 * planes, 2 * planes),
            shape(planes, 2 * planes), shape(4, 4), shape(2, 4), shape(2, 4), shape(1, 4),
        ],
        in_specs=[VMEM] * 3,
        out_specs=[VMEM] * (8 + len(down)),
        compiler_params=PARAMS,
        name="pack",
    )(forces, levels, supports)
    own, up, *rest = packed
    down = own if planes == 2 else rest.pop(0)
    ym, yp, mm, mp, pm, pp = rest

    def moved(value, step_x, step_y):
        pairs = []
        for x in range(count_x):
            for y in range(count_y):
                if 0 <= x + step_x < count_x and 0 <= y + step_y < count_y:
                    pairs.append((x * count_y + y, (x + step_x) * count_y + y + step_y))
        return lax.ppermute(value, ("gx", "gy"), pairs)

    from_xp, from_xm = moved(down, -1, 0), moved(up, 1, 0)
    from_yp, from_ym = moved(ym, 0, -1), moved(yp, 0, 1)
    from_pp, from_pm = moved(mm, -1, -1), moved(mp, -1, 1)
    from_mp, from_mm = moved(pm, 1, -1), moved(pp, 1, 1)

    nodes = (planes + 1) * (rows + 1)
    wide = (planes + 3) * (rows + 3)
    acc = pltpu.VMEM(((planes + 3) * (rows + 1), block, LANES), f32)
    field = pltpu.VMEM((nodes, block, LANES), f32)
    both, system = pl.pallas_call(
        functools.partial(main_kernel, sizes),
        out_shape=[
            jax.ShapeDtypeStruct((4 * cases, nodes * 3 * LANES), bf16),
            jax.ShapeDtypeStruct((3 * cases, LANES), f32),
        ],
        in_specs=[VMEM] * 9,
        out_specs=[VMEM] * 2,
        scratch_shapes=[
            pltpu.VMEM((planes + 4, up8(rows + 4), LANES), f32),
            pltpu.VMEM((planes + 3, up8(rows + 3), LANES), f32),
            pltpu.VMEM((wide, block, LANES), f32),
            pltpu.VMEM((wide, block, LANES), f32),
            pltpu.VMEM((wide, block, LANES), f32),
            acc, acc, field, field, field, field,
            pltpu.VMEM((4 * cases, planes * rows * 3 * LANES), bf16),
            pltpu.VMEM((2 * cases, nodes * 3 * LANES), bf16),
        ],
        compiler_params=PARAMS,
        name="operator",
    )(own, from_xm, from_xp, from_ym, from_yp, from_mm, from_mp, from_pm, from_pp)

    system = lax.psum(system, ("gx", "gy"))

    weighted = pl.pallas_call(
        functools.partial(solve_kernel, sizes),
        out_shape=jax.ShapeDtypeStruct((planes, rows, LANES), f32),
        in_specs=[VMEM] * 3,
        out_specs=VMEM,
        scratch_shapes=[
            pltpu.VMEM((2 * cases, LANES), f32),
            field,
            field,
            pltpu.VMEM((rows, 8, LANES), f32),
        ],
        compiler_params=PARAMS,
        name="solve",
    )(system, both, levels)

    below = moved(weighted[planes - 2 :], 1, 0)
    above = moved(weighted[:2], -1, 0)
    column = jnp.concatenate([below, weighted, above], 0)
    left = moved(column[:, rows - 2 :], 0, 1)
    right = moved(column[:, :2], 0, -1)
    start = jnp.stack([lax.axis_index("gx") * planes, lax.axis_index("gy") * rows])
    totals = (count_x * planes, count_y * rows)
    return pl.pallas_call(
        functools.partial(filter_kernel, sizes, totals),
        out_shape=jax.ShapeDtypeStruct((planes, rows, LANES), f32),
        in_specs=[pl.BlockSpec(memory_space=pltpu.SMEM)] + [VMEM] * 6,
        out_specs=VMEM,
        scratch_shapes=[pltpu.VMEM((planes + 4, rows + 4, LANES), f32)] * 2,
        compiler_params=PARAMS,
        name="cone",
    )(start.astype(jnp.int32), below, above, weighted, left, right, levels)


def solution(mesh):
    return jax.shard_map(
        local,
        mesh=mesh,
        in_specs=(P(None, None, "gx", "gy", None), P("gx", "gy", None), P("gx", "gy", None)),
        out_specs=P("gx", "gy", None),
        check_vma=False,
    )
```

```python
import functools
import math

import jax
import jax.numpy as jnp
from jax import lax
from jax.experimental import pallas as pl
from jax.experimental.pallas import tpu as pltpu
from jax.sharding import PartitionSpec as P

LEVELS = 16
LOAD = 0.2
LANES = 128
POISSON = 0.3
LAME = POISSON / ((1.0 + POISSON) * (1.0 - 2.0 * POISSON))
SHEAR = 1.0 / (2.0 * (1.0 + POISSON))
DIAGONAL = (LAME + 2.0 * SHEAR) / 9.0 + 2.0 * SHEAR / 9.0
VMEM = pl.BlockSpec(memory_space=pltpu.VMEM)
PARAMS = pltpu.CompilerParams(vmem_limit_bytes=50 * 2**20)
f32 = jnp.float32
bf16 = jnp.bfloat16


def up8(count):
    return -(-count // 8) * 8


def shift_down(value):
    lane = lax.broadcasted_iota(jnp.int32, value.shape, value.ndim - 1)
    rolled = pltpu.roll(value, LANES - 1, value.ndim - 1)
    return jnp.where(lane == LANES - 1, 0.0, rolled)


def shift_up(value):
    lane = lax.broadcasted_iota(jnp.int32, value.shape, value.ndim - 1)
    return jnp.where(lane == 0, 0.0, pltpu.roll(value, 1, value.ndim - 1))


def split(value):
    high = value.astype(bf16)
    return high, (value - high.astype(f32)).astype(bf16)


def modes_of(lower, upper):
    out = [[[[None] * 3 for _ in range(2)] for _ in range(2)] for _ in range(2)]
    for a in range(2):
        for c in range(2):
            for k in range(3):
                if a or c:
                    out[a][0][c][k] = lower[a][c][k] + upper[a][c][k]
                out[a][1][c][k] = upper[a][c][k] - lower[a][c][k]
    return out


PAIRS = (((1, 1, 0, 0), (0, 1, 1, 2)), ((1, 0, 1, 0), (0, 1, 1, 1)), ((1, 1, 0, 1), (1, 0, 1, 2)))
TRIPLE = ((0, 1, 1, 0), (1, 0, 1, 1), (1, 1, 0, 2))
SHEARS = (((0, 1, 0, 0), (1, 0, 0, 1)), ((0, 0, 1, 0), (1, 0, 0, 2)), ((0, 0, 1, 1), (0, 1, 0, 2)))
AXIAL = ((1, 0, 0, 0), (0, 1, 0, 1), (0, 0, 1, 2))


def at(modes, place):
    a, b, c, k = place
    return modes[a][b][c][k]


def mode_forces(modes, stiff):
    out = [[[[None] * 3 for _ in range(2)] for _ in range(2)] for _ in range(2)]

    def put(place, value):
        a, b, c, k = place
        out[a][b][c][k] = value

    shear = stiff * (SHEAR / 16)
    for first, second in SHEARS:
        force = shear * (at(modes, first) + at(modes, second))
        put(first, force)
        put(second, force)
    one, two, three = (at(modes, place) for place in AXIAL)
    volume = (stiff * (LAME / 16)) * (one + two + three)
    axial = stiff * (SHEAR / 8)
    for place in AXIAL:
        put(place, volume + axial * at(modes, place))
    own, cross = stiff * ((LAME + 3 * SHEAR) / 48), stiff * (LAME / 48)
    for first, second in PAIRS:
        one, two = at(modes, first), at(modes, second)
        put(first, own * one + cross * two)
        put(second, own * two + cross * one)
    twist = stiff * (SHEAR / 48)
    one, two, three = (at(modes, place) for place in TRIPLE)
    total = one + two + three
    for place in TRIPLE:
        put(place, twist * (total + at(modes, place)))
    last = stiff * ((LAME + 4 * SHEAR) / 144)
    for k in range(3):
        put((1, 1, 1, k), last * modes[1][1][1][k])
    return out


def mode_energy(modes):
    def square(value):
        return value * value

    shear = None
    for first, second in SHEARS:
        term = square(at(modes, first) + at(modes, second))
        shear = term if shear is None else shear + term
    one, two, three = (at(modes, place) for place in AXIAL)
    energy = (SHEAR / 16) * shear + (LAME / 16) * square(one + two + three)
    energy = energy + (SHEAR / 8) * (square(one) + square(two) + square(three))
    squares, products = None, None
    for first, second in PAIRS:
        one, two = at(modes, first), at(modes, second)
        term, product = square(one) + square(two), one * two
        squares = term if squares is None else squares + term
        products = product if products is None else products + product
    energy = energy + ((LAME + 3 * SHEAR) / 48) * squares + (LAME / 24) * products
    one, two, three = (at(modes, place) for place in TRIPLE)
    twist = square(one + two + three) + square(one) + square(two) + square(three)
    energy = energy + (SHEAR / 48) * twist
    last = square(modes[1][1][1][0]) + square(modes[1][1][1][1]) + square(modes[1][1][1][2])
    return energy + ((LAME + 4 * SHEAR) / 144) * last


def x_modes(sums, diffs, plane, row, tile, cases, columns):
    out = [[[None] * 3 for _ in range(2)] for _ in range(2)]
    for c, ref in enumerate((sums, diffs)):
        for k in range(3):
            rows = pl.ds(pl.multiple_of(k * cases + tile * 8, 8), 8)
            one = ref[plane * columns + row, rows, :]
            two = ref[(plane + 1) * columns + row, rows, :]
            out[0][c][k] = one + two
            out[1][c][k] = two - one
    return out


def apply_elements(
    sums, diffs, stiff_ref, acc_s, acc_d, planes, rows, skip, stiff_x, stiff_y, cases
):
    columns = rows + 1
    acc_columns = columns - 2 * skip
    tiles = cases // 8

    def step(index, _):
        plane, tile = index // tiles, index % tiles

        def emit(row, total):
            if not skip <= row < columns - skip:
                return
            for c, acc in enumerate((acc_s, acc_d)):
                for k in range(3):
                    lines = pl.ds(pl.multiple_of(k * cases + tile * 8, 8), 8)
                    low = plane * acc_columns + row - skip
                    acc[low, lines, :] += total[0][c][k] - total[1][c][k]
                    acc[low + acc_columns, lines, :] = total[0][c][k] + total[1][c][k]

        lower = x_modes(sums, diffs, plane, 0, tile, cases, columns)
        carry = None
        for row in range(rows):
            upper = x_modes(sums, diffs, plane, row + 1, tile, cases, columns)
            stiff = jnp.broadcast_to(
                stiff_ref[plane + stiff_x, pl.ds(row + stiff_y, 1), :], (8, LANES)
            )
            forces = mode_forces(modes_of(lower, upper), stiff)
            here = [[[None] * 3 for _ in range(2)] for _ in range(2)]
            following = [[[None] * 3 for _ in range(2)] for _ in range(2)]
            for a in range(2):
                for c in range(2):
                    for k in range(3):
                        one, two = forces[a][0][c][k], forces[a][1][c][k]
                        low = -two if one is None else one - two
                        high = two if one is None else one + two
                        here[a][c][k] = low if carry is None else carry[a][c][k] + low
                        following[a][c][k] = high
            emit(row, here)
            carry, lower = following, upper
        emit(rows, carry)
        return 0

    lax.fori_loop(0, planes * tiles, step, 0)


def pack_kernel(sizes, forces, levels, supports, own, up, *rest):
    planes, rows, cases = sizes
    block = 3 * cases
    base = planes * rows * block
    for x in range(planes):
        density = 0.3 + 0.7 * levels[x].astype(f32) / (LEVELS - 1)
        stiff = density * density * density
        free = supports[x] == 0
        own[base + x * rows : base + (x + 1) * rows, :] = jnp.where(free, stiff, -stiff)
        scale = jnp.where(free, LOAD, 0.0)
        for k in range(3):
            for c in range(cases):
                start = x * rows * block + k * cases + c
                own[pl.ds(start, rows, stride=block), :] = forces[k, c, x] * scale

    def fill(ref, xs, code_xs):
        size = len(xs) * rows * block
        ref[:size, :] = own[xs[0] * rows * block : xs[0] * rows * block + size, :]
        codes = base + code_xs[0] * rows
        ref[size:, :] = own[codes : codes + len(code_xs) * rows, :]

    fill(up, range(planes - 1, planes), range(planes - 2, planes))
    for ref in rest:
        fill(ref, range(2), range(2))


def edge_kernel(sizes, own, xm, xp, ym, yp):
    planes, rows, cases = sizes
    block = 3 * cases
    parts = (
        (xm, rows * block, range(1), range(2)),
        (own, planes * rows * block, range(planes), range(planes)),
        (xp, 2 * rows * block, range(2), range(2)),
    )
    for ref, low, count, code in ((ym, 0, 2, 2), (yp, rows - 1, 1, 2)):
        line = 0
        for source, _, xs, _ in parts:
            for x in xs:
                start = (x * rows + low) * block
                ref[line : line + count * block, :] = source[start : start + count * block, :]
                line += count * block
        for source, base, _, xs in parts:
            for x in xs:
                start = base + x * rows + (0 if low == 0 else rows - 2)
                ref[line : line + code, :] = source[start : start + code, :]
                line += code
        if line < ref.shape[0]:
            ref[line:, :] = jnp.zeros((ref.shape[0] - line, LANES), f32)


def main_kernel(
    sizes, own, xm, xp, ym, yp, both_out, system_out, stiff_ref, inverse,
    start, sums, diffs, acc_s, acc_d, w_sums, w_diffs, acc2_s, acc2_d, right, second,
):
    planes, rows, cases = sizes
    block = 3 * cases
    xs, ys = planes + 3, rows + 3
    every_x, every_y = range(planes), range(rows)
    low, high_x, high_y = (-1,), (planes, planes + 1), (rows, rows + 1)
    low2 = (-2, -1)
    regions = (
        (own, every_x, every_y, every_x, every_y),
        (xm, low, every_y, low2, every_y),
        (xp, high_x, every_y, high_x, every_y),
        (ym, range(-1, planes + 2), low, range(-2, planes + 2), low2),
        (yp, range(-1, planes + 2), high_y, range(-2, planes + 2), high_y),
    )
    for ref, bx, by, cx, cy in regions:
        base = len(bx) * len(by) * block
        for i, x in enumerate(cx):
            line = base + i * len(cy)
            stiff_ref[x + 2, cy[0] + 2 : cy[0] + 2 + len(cy), :] = ref[line : line + len(cy), :]
    for x in range(-1, planes + 2):
        codes = stiff_ref[x + 2, 0 : ys + 1, :]
        total = jnp.abs(stiff_ref[x + 1, 0 : ys + 1, :]) + jnp.abs(codes)
        total = total[:-1] + total[1:]
        total = total + shift_up(total)
        free = codes[1:] > 0.0
        value = 1.0 / (DIAGONAL * jnp.where(free, total, 1.0))
        inverse[x + 1, 0:ys, :] = jnp.where(free, value, 0.0)
    for x in range(planes + 4):
        stiff_ref[x] = jnp.abs(stiff_ref[x])

    for ref, bx, by, _, _ in regions:
        for i, x in enumerate(bx):

            def place(j, _, ref=ref, i=i, x=x, by=by):
                y = j + by[0] + 1
                load = ref[pl.ds(pl.multiple_of((i * len(by) + j) * block, 8), block), :]
                value = load * inverse[x + 1, pl.ds(y, 1), :]
                column = (x + 1) * ys + y
                start[column] = value
                moved = shift_down(value)
                sums[column] = value + moved
                diffs[column] = moved - value
                return 0

            lax.fori_loop(0, len(by), place, 0)

    nodes_y = rows + 1
    apply_elements(
        sums, diffs, stiff_ref, acc_s, acc_d, planes + 2, rows + 2, 1, 1, 1, cases
    )

    def image(x, y, place):
        column = (x + 1) * nodes_y + y
        s, d = acc_s[column], acc_d[column]
        force = s - d + shift_up(s + d)
        scaled = force * inverse[x + 1, pl.ds(y + 1, 1), :]
        moved = shift_down(scaled)
        w_sums[x * nodes_y + y] = scaled + moved
        w_diffs[x * nodes_y + y] = moved - scaled
        value = start[(x + 1) * ys + y + 1]
        for k in range(3):
            lines = slice(k * cases, (k + 1) * cases)
            pair = jnp.concatenate([value[lines], scaled[lines]], 0)
            lane = pl.ds(pl.multiple_of((place * 3 + k) * LANES, LANES), LANES)
            high, rest = split(pair)
            both_out[0 : 2 * cases, lane] = high
            both_out[2 * cases : 4 * cases, lane] = rest
        return force

    def inside(index, _):
        x, y = index // rows, index % rows
        force = image(x, y, index)
        load = own[pl.ds(pl.multiple_of(index * block, 8), block), :]
        for k in range(3):
            lines = slice(k * cases, (k + 1) * cases)
            pair = jnp.concatenate([load[lines], force[lines]], 0)
            lane = pl.ds(pl.multiple_of((index * 3 + k) * LANES, LANES), LANES)
            high, rest = split(pair)
            right[0 : 2 * cases, lane] = high
            right[2 * cases : 4 * cases, lane] = rest
        return 0

    count = planes * rows
    lax.fori_loop(0, count, inside, 0)

    def beyond_y(x, _):
        image(x, rows, count + x)
        return 0

    lax.fori_loop(0, planes, beyond_y, 0)

    def beyond_x(y, _):
        image(planes, y, count + planes + y)
        return 0

    lax.fori_loop(0, nodes_y, beyond_x, 0)

    for column in range(nodes_y):
        acc2_s[column] = jnp.zeros((block, LANES), f32)
        acc2_d[column] = jnp.zeros((block, LANES), f32)
    apply_elements(w_sums, w_diffs, stiff_ref, acc2_s, acc2_d, planes, rows, 0, 2, 2, cases)

    def second_force(x, y, place):
        column = x * nodes_y + y
        s, d = acc2_s[column], acc2_d[column]
        force = s - d + shift_up(s + d)
        for k in range(3):
            value = force[k * cases : (k + 1) * cases]
            high = value.astype(bf16).astype(f32)
            lane = pl.ds(pl.multiple_of((place * 3 + k) * LANES, LANES), LANES)
            second[:, lane] = jnp.concatenate([high, value - high], 0).astype(bf16)

    def second_inside(index, _):
        second_force(index // rows, index % rows, index)
        return 0

    def second_y(x, _):
        second_force(x, rows, count + x)
        return 0

    def second_x(y, _):
        second_force(planes, y, count + planes + y)
        return 0

    lax.fori_loop(0, count, second_inside, 0)
    lax.fori_loop(0, planes, second_y, 0)
    lax.fori_loop(0, nodes_y, second_x, 0)

    contract = (((1,), (1,)), ((), ()))
    width = count * 3 * LANES
    two = 2 * cases
    gram = lax.dot_general(both_out[:, :width], right[...], contract, preferred_element_type=f32)
    gram = gram[:two] + gram[two:]
    gram = gram[:, :two] + gram[:, two:]
    other = lax.dot_general(both_out[...], second[...], contract, preferred_element_type=f32)
    other = other[:two] + other[two:]
    other = other[:, :cases] + other[:, cases:]
    system_out[...] = jnp.zeros(system_out.shape, f32)
    system_out[:, 0:two] = gram[:cases]
    system_out[:, two : two + cases] = other[:cases]
    system_out[:, two + cases : 2 * two] = other[cases:]


def solve_kernel(sizes, system, both, levels, out, mixing, sums, diffs, energy):
    planes, rows, cases = sizes
    two = 2 * cases
    nodes_y = rows + 1
    count = planes * rows
    total = jnp.sum(system[...], axis=0)
    table = jnp.concatenate(
        [pltpu.roll(total, LANES - cases, 1), pltpu.roll(total, LANES - two, 1), total], 0
    )
    lane = lax.broadcasted_iota(jnp.int32, (1, LANES), 1)
    gone = 0
    for pivot in range(two):
        drop = pivot // 8 * 8 - gone
        table = table[drop:]
        gone += drop
        line = pivot - gone
        row = table[line : line + 1, :]
        inverse = 1.0 / row[:, pivot : pivot + 1]
        row = jnp.where(lane == pivot, -inverse, row * inverse)
        column = table[:, pivot : pivot + 1]
        table = jnp.where(lane == pivot, 0.0, table) - column * row
    answer = table[two - gone :, :two]
    high = answer.astype(bf16).astype(f32)
    mixing[...] = jnp.zeros(mixing.shape, f32)
    mixing[0:cases, 0:two] = high
    mixing[0:cases, two : 2 * two] = high
    mixing[cases:two, 0:two] = answer - high
    mix = mixing[...][:, : 2 * two].astype(bf16)

    def combined(place, width):
        lanes = pl.ds(pl.multiple_of(place * 3 * LANES, LANES), width * 3 * LANES)
        value = jnp.dot(mix, both[:, lanes], preferred_element_type=f32)
        return value[:cases] + value[cases:]

    def keep(value, index, column):
        for k in range(3):
            part = value[:, (index * 3 + k) * LANES : (index * 3 + k + 1) * LANES]
            moved = shift_down(part)
            sums[column, k * cases : (k + 1) * cases, :] = part + moved
            diffs[column, k * cases : (k + 1) * cases, :] = moved - part

    def inside(x, _):
        value = combined(x * rows, rows)
        for y in range(rows):
            keep(value, y, x * nodes_y + y)
        return 0

    lax.fori_loop(0, planes, inside, 0)
    value = combined(count, planes + nodes_y)
    for x in range(planes):
        keep(value, x, x * nodes_y + rows)
    for y in range(nodes_y):
        keep(value, planes + y, planes * nodes_y + y)

    tiles = cases // 8

    def step(plane, _):
        for tile in range(tiles):
            lower = x_modes(sums, diffs, plane, 0, tile, cases, nodes_y)
            for row in range(rows):
                upper = x_modes(sums, diffs, plane, row + 1, tile, cases, nodes_y)
                part = mode_energy(modes_of(lower, upper))
                if tile == 0:
                    energy[row] = part
                else:
                    energy[row] += part
                lower = upper
        total = jnp.sum(energy[...], axis=1)
        density = 0.3 + 0.7 * levels[plane].astype(f32) / (LEVELS - 1)
        out[plane] = (-3.0 / cases) * (density * density * density) * total
        return 0

    lax.fori_loop(0, planes, step, 0)


def filter_kernel(sizes, counts, start, blocks, levels, out, wide, there):
    planes, rows, _ = sizes
    totals = (counts[0] * planes, counts[1] * rows)
    weight = [2.5 - math.sqrt(q) for q in range(7)]
    sides_x = ((-1, planes - 2, planes, 0), (0, 0, planes, 2), (1, 0, 2, 2 + planes))
    sides_y = ((-1, rows - 2, rows, 0), (0, 0, rows, 2), (1, 0, 2, 2 + rows))
    for step_x, x0, x1, to_x in sides_x:
        for step_y, y0, y1, to_y in sides_y:
            at_x = start[0] // planes + step_x
            at_y = start[1] // rows + step_y
            inside = (at_x >= 0) & (at_x < counts[0]) & (at_y >= 0) & (at_y < counts[1])
            index = jnp.where(inside, at_x * counts[1] + at_y, 0)
            value = blocks[index, x0:x1, y0:y1, :]
            wide[to_x : to_x + x1 - x0, to_y : to_y + y1 - y0, :] = jnp.where(inside, value, 0.0)
    y = lax.broadcasted_iota(jnp.int32, (rows + 4, LANES), 0) + (start[1] - 2)
    in_y = jnp.logical_and(y >= 0, y < totals[1])
    for x in range(planes + 4):
        global_x = start[0] + (x - 2)
        in_x = jnp.logical_and(global_x >= 0, global_x < totals[0])
        there[x] = jnp.where(jnp.logical_and(in_y, in_x), 1.0, 0.0)

    def smooth(ref, x):
        near = {}
        for dx in range(-2, 3):
            for dy in range(-2, 3):
                q = dx * dx + dy * dy
                if q <= 5:
                    value = ref[x + 2 + dx, 2 + dy : 2 + dy + rows, :]
                    near[q] = value if q not in near else near[q] + value
        result = 0.0
        for dz in range(3):
            part = None
            for q, value in near.items():
                if q + dz * dz <= 6:
                    term = weight[q + dz * dz] * value
                    part = term if part is None else part + term
            if dz == 0:
                result = part
            else:
                place = lax.broadcasted_iota(jnp.int32, part.shape, 1)
                forward = jnp.where(place >= LANES - dz, 0.0, pltpu.roll(part, LANES - dz, 1))
                backward = jnp.where(place < dz, 0.0, pltpu.roll(part, dz, 1))
                result = result + (forward + backward)
        return result

    for x in range(planes):
        density = 0.3 + 0.7 * levels[x].astype(f32) / (LEVELS - 1)
        out[x] = smooth(wide, x) / (density * smooth(there, x))


def local(forces, levels, supports):
    _, cases, planes, rows, _ = forces.shape
    sizes = (planes, rows, cases)
    block = 3 * cases
    count_x, count_y = lax.axis_size("gx"), lax.axis_size("gy")

    def shape(blocks, codes):
        return jax.ShapeDtypeStruct((blocks * block + up8(codes), LANES), f32)

    whole = shape(planes * rows, planes * rows)
    down = [] if planes == 2 else [shape(2 * rows, 2 * rows)]
    own, up, *down = pl.pallas_call(
        functools.partial(pack_kernel, sizes),
        out_shape=[whole, shape(rows, 2 * rows), *down],
        in_specs=[VMEM] * 3,
        out_specs=[VMEM] * (2 + len(down)),
        compiler_params=PARAMS,
        name="pack",
    )(forces, levels, supports)

    def moved(value, axis, step):
        count = lax.axis_size(axis)
        pairs = [(i, i + step) for i in range(count) if 0 <= i + step < count]
        return lax.ppermute(value, axis, pairs)

    from_xp = moved(down[0] if down else own, "gx", -1)
    from_xm = moved(up, "gx", 1)
    ym, yp = pl.pallas_call(
        functools.partial(edge_kernel, sizes),
        out_shape=[
            shape(2 * (planes + 3), 2 * (planes + 4)), shape(planes + 3, 2 * (planes + 4))
        ],
        in_specs=[VMEM] * 3,
        out_specs=[VMEM] * 2,
        compiler_params=PARAMS,
        name="edges",
    )(own, from_xm, from_xp)
    from_yp, from_ym = moved(ym, "gy", -1), moved(yp, "gy", 1)

    nodes = (planes + 1) * (rows + 1)
    wide = (planes + 3) * (rows + 3)
    acc = pltpu.VMEM(((planes + 3) * (rows + 1), block, LANES), f32)
    field = pltpu.VMEM((nodes, block, LANES), f32)
    both, system = pl.pallas_call(
        functools.partial(main_kernel, sizes),
        out_shape=[
            jax.ShapeDtypeStruct((4 * cases, nodes * 3 * LANES), bf16),
            jax.ShapeDtypeStruct((cases, LANES), f32),
        ],
        in_specs=[VMEM] * 5,
        out_specs=[VMEM] * 2,
        scratch_shapes=[
            pltpu.VMEM((planes + 4, up8(rows + 4), LANES), f32),
            pltpu.VMEM((planes + 3, up8(rows + 3), LANES), f32),
            pltpu.VMEM((wide, block, LANES), f32),
            pltpu.VMEM((wide, block, LANES), f32),
            pltpu.VMEM((wide, block, LANES), f32),
            acc, acc, field, field, field, field,
            pltpu.VMEM((4 * cases, planes * rows * 3 * LANES), bf16),
            pltpu.VMEM((2 * cases, nodes * 3 * LANES), bf16),
        ],
        compiler_params=PARAMS,
        name="operator",
    )(own, from_xm, from_xp, from_ym, from_yp)

    system = lax.all_gather(system, ("gx", "gy"))

    weighted = pl.pallas_call(
        functools.partial(solve_kernel, sizes),
        out_shape=jax.ShapeDtypeStruct((planes, rows, LANES), f32),
        in_specs=[VMEM] * 3,
        out_specs=VMEM,
        scratch_shapes=[
            pltpu.VMEM((2 * cases, LANES), f32),
            field,
            field,
            pltpu.VMEM((rows, 8, LANES), f32),
        ],
        compiler_params=PARAMS,
        name="solve",
    )(system, both, levels)

    blocks = lax.all_gather(weighted, ("gx", "gy"))
    start = jnp.stack([lax.axis_index("gx") * planes, lax.axis_index("gy") * rows])
    return pl.pallas_call(
        functools.partial(filter_kernel, sizes, (count_x, count_y)),
        out_shape=jax.ShapeDtypeStruct((planes, rows, LANES), f32),
        in_specs=[pl.BlockSpec(memory_space=pltpu.SMEM)] + [VMEM] * 2,
        out_specs=VMEM,
        scratch_shapes=[pltpu.VMEM((planes + 4, rows + 4, LANES), f32)] * 2,
        compiler_params=PARAMS,
        name="cone",
    )(start.astype(jnp.int32), blocks, levels)


def solution(mesh):
    return jax.shard_map(
        local,
        mesh=mesh,
        in_specs=(P(None, None, "gx", "gy", None), P("gx", "gy", None), P("gx", "gy", None)),
        out_specs=P("gx", "gy", None),
        check_vma=False,
    )
```

```python
import functools
import math

import jax
import jax.numpy as jnp
from jax import lax
from jax.experimental import pallas as pl
from jax.experimental.pallas import tpu as pltpu
from jax.sharding import PartitionSpec as P

LEVELS = 16
LOAD = 0.2
LANES = 128
POISSON = 0.3
LAME = POISSON / ((1.0 + POISSON) * (1.0 - 2.0 * POISSON))
SHEAR = 1.0 / (2.0 * (1.0 + POISSON))
DIAGONAL = (LAME + 2.0 * SHEAR) / 9.0 + 2.0 * SHEAR / 9.0
VMEM = pl.BlockSpec(memory_space=pltpu.VMEM)
PARAMS = pltpu.CompilerParams(vmem_limit_bytes=50 * 2**20)
f32 = jnp.float32
bf16 = jnp.bfloat16


def up8(count):
    return -(-count // 8) * 8


def shift_down(value):
    lane = lax.broadcasted_iota(jnp.int32, value.shape, value.ndim - 1)
    rolled = pltpu.roll(value, LANES - 1, value.ndim - 1)
    return jnp.where(lane == LANES - 1, 0.0, rolled)


def shift_up(value):
    lane = lax.broadcasted_iota(jnp.int32, value.shape, value.ndim - 1)
    return jnp.where(lane == 0, 0.0, pltpu.roll(value, 1, value.ndim - 1))


def split(value):
    high = value.astype(bf16)
    return high, (value - high.astype(f32)).astype(bf16)


def modes_of(lower, upper):
    out = [[[[None] * 3 for _ in range(2)] for _ in range(2)] for _ in range(2)]
    for a in range(2):
        for c in range(2):
            for k in range(3):
                if a or c:
                    out[a][0][c][k] = lower[a][c][k] + upper[a][c][k]
                out[a][1][c][k] = upper[a][c][k] - lower[a][c][k]
    return out


PAIRS = (((1, 1, 0, 0), (0, 1, 1, 2)), ((1, 0, 1, 0), (0, 1, 1, 1)), ((1, 1, 0, 1), (1, 0, 1, 2)))
TRIPLE = ((0, 1, 1, 0), (1, 0, 1, 1), (1, 1, 0, 2))
SHEARS = (((0, 1, 0, 0), (1, 0, 0, 1)), ((0, 0, 1, 0), (1, 0, 0, 2)), ((0, 0, 1, 1), (0, 1, 0, 2)))
AXIAL = ((1, 0, 0, 0), (0, 1, 0, 1), (0, 0, 1, 2))


def at(modes, place):
    a, b, c, k = place
    return modes[a][b][c][k]


def mode_forces(modes, stiff):
    out = [[[[None] * 3 for _ in range(2)] for _ in range(2)] for _ in range(2)]

    def put(place, value):
        a, b, c, k = place
        out[a][b][c][k] = value

    shear = stiff * (SHEAR / 16)
    for first, second in SHEARS:
        force = shear * (at(modes, first) + at(modes, second))
        put(first, force)
        put(second, force)
    one, two, three = (at(modes, place) for place in AXIAL)
    volume = (stiff * (LAME / 16)) * (one + two + three)
    axial = stiff * (SHEAR / 8)
    for place in AXIAL:
        put(place, volume + axial * at(modes, place))
    own, cross = stiff * ((LAME + 3 * SHEAR) / 48), stiff * (LAME / 48)
    for first, second in PAIRS:
        one, two = at(modes, first), at(modes, second)
        put(first, own * one + cross * two)
        put(second, own * two + cross * one)
    twist = stiff * (SHEAR / 48)
    one, two, three = (at(modes, place) for place in TRIPLE)
    total = one + two + three
    for place in TRIPLE:
        put(place, twist * (total + at(modes, place)))
    last = stiff * ((LAME + 4 * SHEAR) / 144)
    for k in range(3):
        put((1, 1, 1, k), last * modes[1][1][1][k])
    return out


def mode_energy(modes):
    def square(value):
        return value * value

    shear = None
    for first, second in SHEARS:
        term = square(at(modes, first) + at(modes, second))
        shear = term if shear is None else shear + term
    one, two, three = (at(modes, place) for place in AXIAL)
    energy = (SHEAR / 16) * shear + (LAME / 16) * square(one + two + three)
    energy = energy + (SHEAR / 8) * (square(one) + square(two) + square(three))
    squares, products = None, None
    for first, second in PAIRS:
        one, two = at(modes, first), at(modes, second)
        term, product = square(one) + square(two), one * two
        squares = term if squares is None else squares + term
        products = product if products is None else products + product
    energy = energy + ((LAME + 3 * SHEAR) / 48) * squares + (LAME / 24) * products
    one, two, three = (at(modes, place) for place in TRIPLE)
    twist = square(one + two + three) + square(one) + square(two) + square(three)
    energy = energy + (SHEAR / 48) * twist
    last = square(modes[1][1][1][0]) + square(modes[1][1][1][1]) + square(modes[1][1][1][2])
    return energy + ((LAME + 4 * SHEAR) / 144) * last


def x_modes(sums, diffs, plane, row, tile, cases, columns):
    out = [[[None] * 3 for _ in range(2)] for _ in range(2)]
    for c, ref in enumerate((sums, diffs)):
        for k in range(3):
            rows = pl.ds(pl.multiple_of(k * cases + tile * 8, 8), 8)
            one = ref[plane * columns + row, rows, :]
            two = ref[(plane + 1) * columns + row, rows, :]
            out[0][c][k] = one + two
            out[1][c][k] = two - one
    return out


def apply_elements(
    sums, diffs, stiff_ref, acc_s, acc_d, planes, rows, skip, stiff_x, stiff_y, cases
):
    columns = rows + 1
    acc_columns = columns - 2 * skip
    tiles = cases // 8

    def step(index, _):
        plane, tile = index // tiles, index % tiles

        def emit(row, total):
            if not skip <= row < columns - skip:
                return
            for c, acc in enumerate((acc_s, acc_d)):
                for k in range(3):
                    lines = pl.ds(pl.multiple_of(k * cases + tile * 8, 8), 8)
                    low = plane * acc_columns + row - skip
                    acc[low, lines, :] += total[0][c][k] - total[1][c][k]
                    acc[low + acc_columns, lines, :] = total[0][c][k] + total[1][c][k]

        lower = x_modes(sums, diffs, plane, 0, tile, cases, columns)
        carry = None
        for row in range(rows):
            upper = x_modes(sums, diffs, plane, row + 1, tile, cases, columns)
            stiff = jnp.broadcast_to(
                stiff_ref[plane + stiff_x, pl.ds(row + stiff_y, 1), :], (8, LANES)
            )
            forces = mode_forces(modes_of(lower, upper), stiff)
            here = [[[None] * 3 for _ in range(2)] for _ in range(2)]
            following = [[[None] * 3 for _ in range(2)] for _ in range(2)]
            for a in range(2):
                for c in range(2):
                    for k in range(3):
                        one, two = forces[a][0][c][k], forces[a][1][c][k]
                        low = -two if one is None else one - two
                        high = two if one is None else one + two
                        here[a][c][k] = low if carry is None else carry[a][c][k] + low
                        following[a][c][k] = high
            emit(row, here)
            carry, lower = following, upper
        emit(rows, carry)
        return 0

    lax.fori_loop(0, planes * tiles, step, 0)


def pack_kernel(sizes, forces, levels, supports, own, up, *rest):
    planes, rows, cases = sizes
    block = 3 * cases
    base = planes * rows * block
    for x in range(planes):
        density = 0.3 + 0.7 * levels[x].astype(f32) / (LEVELS - 1)
        stiff = density * density * density
        free = supports[x] == 0
        own[base + x * rows : base + (x + 1) * rows, :] = jnp.where(free, stiff, -stiff)
        scale = jnp.where(free, LOAD, 0.0)
        for k in range(3):
            for c in range(cases):
                start = x * rows * block + k * cases + c
                own[pl.ds(start, rows, stride=block), :] = forces[k, c, x] * scale

    def fill(ref, xs, code_xs):
        size = len(xs) * rows * block
        ref[:size, :] = own[xs[0] * rows * block : xs[0] * rows * block + size, :]
        codes = base + code_xs[0] * rows
        ref[size:, :] = own[codes : codes + len(code_xs) * rows, :]

    fill(up, range(planes - 1, planes), range(planes - 2, planes))
    for ref in rest:
        fill(ref, range(2), range(2))


def edge_kernel(sizes, own, xm, xp, ym, yp):
    planes, rows, cases = sizes
    block = 3 * cases
    parts = (
        (xm, rows * block, range(1), range(2)),
        (own, planes * rows * block, range(planes), range(planes)),
        (xp, 2 * rows * block, range(2), range(2)),
    )
    for ref, low, count, code in ((ym, 0, 2, 2), (yp, rows - 1, 1, 2)):
        line = 0
        for source, _, xs, _ in parts:
            for x in xs:
                start = (x * rows + low) * block
                ref[line : line + count * block, :] = source[start : start + count * block, :]
                line += count * block
        for source, base, _, xs in parts:
            for x in xs:
                start = base + x * rows + (0 if low == 0 else rows - 2)
                ref[line : line + code, :] = source[start : start + code, :]
                line += code
        if line < ref.shape[0]:
            ref[line:, :] = jnp.zeros((ref.shape[0] - line, LANES), f32)


def main_kernel(
    sizes, own, xm, xp, ym, yp, both_out, system_out, stiff_ref, inverse,
    start, sums, diffs, acc_s, acc_d, w_sums, w_diffs, acc2_s, acc2_d, right, second,
):
    planes, rows, cases = sizes
    block = 3 * cases
    xs, ys = planes + 3, rows + 3
    every_x, every_y = range(planes), range(rows)
    low, high_x, high_y = (-1,), (planes, planes + 1), (rows, rows + 1)
    low2 = (-2, -1)
    regions = (
        (own, every_x, every_y, every_x, every_y),
        (xm, low, every_y, low2, every_y),
        (xp, high_x, every_y, high_x, every_y),
        (ym, range(-1, planes + 2), low, range(-2, planes + 2), low2),
        (yp, range(-1, planes + 2), high_y, range(-2, planes + 2), high_y),
    )
    for ref, bx, by, cx, cy in regions:
        base = len(bx) * len(by) * block
        for i, x in enumerate(cx):
            line = base + i * len(cy)
            stiff_ref[x + 2, cy[0] + 2 : cy[0] + 2 + len(cy), :] = ref[line : line + len(cy), :]
    for x in range(-1, planes + 2):
        codes = stiff_ref[x + 2, 0 : ys + 1, :]
        total = jnp.abs(stiff_ref[x + 1, 0 : ys + 1, :]) + jnp.abs(codes)
        total = total[:-1] + total[1:]
        total = total + shift_up(total)
        free = codes[1:] > 0.0
        value = 1.0 / (DIAGONAL * jnp.where(free, total, 1.0))
        inverse[x + 1, 0:ys, :] = jnp.where(free, value, 0.0)
    for x in range(planes + 4):
        stiff_ref[x] = jnp.abs(stiff_ref[x])

    for ref, bx, by, _, _ in regions:
        for i, x in enumerate(bx):

            def place(j, _, ref=ref, i=i, x=x, by=by):
                y = j + by[0] + 1
                load = ref[pl.ds(pl.multiple_of((i * len(by) + j) * block, 8), block), :]
                value = load * inverse[x + 1, pl.ds(y, 1), :]
                column = (x + 1) * ys + y
                start[column] = value
                moved = shift_down(value)
                sums[column] = value + moved
                diffs[column] = moved - value
                return 0

            lax.fori_loop(0, len(by), place, 0)

    nodes_y = rows + 1
    apply_elements(
        sums, diffs, stiff_ref, acc_s, acc_d, planes + 2, rows + 2, 1, 1, 1, cases
    )

    def image(x, y, place):
        column = (x + 1) * nodes_y + y
        s, d = acc_s[column], acc_d[column]
        force = s - d + shift_up(s + d)
        scaled = force * inverse[x + 1, pl.ds(y + 1, 1), :]
        moved = shift_down(scaled)
        w_sums[x * nodes_y + y] = scaled + moved
        w_diffs[x * nodes_y + y] = moved - scaled
        value = start[(x + 1) * ys + y + 1]
        for k in range(3):
            lines = slice(k * cases, (k + 1) * cases)
            pair = jnp.concatenate([value[lines], scaled[lines]], 0)
            lane = pl.ds(pl.multiple_of((place * 3 + k) * LANES, LANES), LANES)
            high, rest = split(pair)
            both_out[0 : 2 * cases, lane] = high
            both_out[2 * cases : 4 * cases, lane] = rest
        return force

    def inside(index, _):
        x, y = index // rows, index % rows
        force = image(x, y, index)
        load = own[pl.ds(pl.multiple_of(index * block, 8), block), :]
        for k in range(3):
            lines = slice(k * cases, (k + 1) * cases)
            pair = jnp.concatenate([load[lines], force[lines]], 0)
            lane = pl.ds(pl.multiple_of((index * 3 + k) * LANES, LANES), LANES)
            high, rest = split(pair)
            right[0 : 2 * cases, lane] = high
            right[2 * cases : 4 * cases, lane] = rest
        return 0

    count = planes * rows
    lax.fori_loop(0, count, inside, 0)

    def beyond_y(x, _):
        image(x, rows, count + x)
        return 0

    lax.fori_loop(0, planes, beyond_y, 0)

    def beyond_x(y, _):
        image(planes, y, count + planes + y)
        return 0

    lax.fori_loop(0, nodes_y, beyond_x, 0)

    for column in range(nodes_y):
        acc2_s[column] = jnp.zeros((block, LANES), f32)
        acc2_d[column] = jnp.zeros((block, LANES), f32)
    apply_elements(w_sums, w_diffs, stiff_ref, acc2_s, acc2_d, planes, rows, 0, 2, 2, cases)

    def second_force(x, y, place):
        column = x * nodes_y + y
        s, d = acc2_s[column], acc2_d[column]
        force = s - d + shift_up(s + d)
        for k in range(3):
            value = force[k * cases : (k + 1) * cases]
            high = value.astype(bf16).astype(f32)
            lane = pl.ds(pl.multiple_of((place * 3 + k) * LANES, LANES), LANES)
            second[:, lane] = jnp.concatenate([high, value - high], 0).astype(bf16)

    def second_inside(index, _):
        second_force(index // rows, index % rows, index)
        return 0

    def second_y(x, _):
        second_force(x, rows, count + x)
        return 0

    def second_x(y, _):
        second_force(planes, y, count + planes + y)
        return 0

    lax.fori_loop(0, count, second_inside, 0)
    lax.fori_loop(0, planes, second_y, 0)
    lax.fori_loop(0, nodes_y, second_x, 0)

    contract = (((1,), (1,)), ((), ()))
    width = count * 3 * LANES
    two = 2 * cases
    gram = lax.dot_general(both_out[:, :width], right[...], contract, preferred_element_type=f32)
    gram = gram[:two] + gram[two:]
    gram = gram[:, :two] + gram[:, two:]
    other = lax.dot_general(both_out[...], second[...], contract, preferred_element_type=f32)
    other = other[:two] + other[two:]
    other = other[:, :cases] + other[:, cases:]
    system_out[...] = jnp.zeros(system_out.shape, f32)
    system_out[:, 0:two] = gram[:cases]
    system_out[:, two : two + cases] = other[:cases]
    system_out[:, two + cases : 2 * two] = other[cases:]


def solve_kernel(sizes, system, both, levels, out, mixing, sums, diffs, energy):
    planes, rows, cases = sizes
    two = 2 * cases
    nodes_y = rows + 1
    count = planes * rows
    total = jnp.sum(system[...], axis=0)
    table = jnp.concatenate(
        [pltpu.roll(total, LANES - cases, 1), pltpu.roll(total, LANES - two, 1), total], 0
    )
    lane = lax.broadcasted_iota(jnp.int32, (1, LANES), 1)
    gone = 0
    for pivot in range(two):
        drop = pivot // 8 * 8 - gone
        table = table[drop:]
        gone += drop
        line = pivot - gone
        row = table[line : line + 1, :]
        inverse = 1.0 / row[:, pivot : pivot + 1]
        row = jnp.where(lane == pivot, -inverse, row * inverse)
        column = table[:, pivot : pivot + 1]
        table = jnp.where(lane == pivot, 0.0, table) - column * row
    answer = table[two - gone :, :two]
    high = answer.astype(bf16).astype(f32)
    mixing[...] = jnp.zeros(mixing.shape, f32)
    mixing[0:cases, 0:two] = high
    mixing[0:cases, two : 2 * two] = high
    mixing[cases:two, 0:two] = answer - high
    mix = mixing[...][:, : 2 * two].astype(bf16)

    def combined(place, width):
        lanes = pl.ds(pl.multiple_of(place * 3 * LANES, LANES), width * 3 * LANES)
        value = jnp.dot(mix, both[:, lanes], preferred_element_type=f32)
        return value[:cases] + value[cases:]

    def keep(value, index, column):
        for k in range(3):
            part = value[:, (index * 3 + k) * LANES : (index * 3 + k + 1) * LANES]
            moved = shift_down(part)
            sums[column, k * cases : (k + 1) * cases, :] = part + moved
            diffs[column, k * cases : (k + 1) * cases, :] = moved - part

    def inside(x, _):
        value = combined(x * rows, rows)
        for y in range(rows):
            keep(value, y, x * nodes_y + y)
        return 0

    lax.fori_loop(0, planes, inside, 0)
    value = combined(count, planes + nodes_y)
    for x in range(planes):
        keep(value, x, x * nodes_y + rows)
    for y in range(nodes_y):
        keep(value, planes + y, planes * nodes_y + y)

    tiles = cases // 8

    def step(plane, _):
        for tile in range(tiles):
            lower = x_modes(sums, diffs, plane, 0, tile, cases, nodes_y)
            for row in range(rows):
                upper = x_modes(sums, diffs, plane, row + 1, tile, cases, nodes_y)
                part = mode_energy(modes_of(lower, upper))
                if tile == 0:
                    energy[row] = part
                else:
                    energy[row] += part
                lower = upper
        total = jnp.sum(energy[...], axis=1)
        density = 0.3 + 0.7 * levels[plane].astype(f32) / (LEVELS - 1)
        out[plane] = (-3.0 / cases) * (density * density * density) * total
        return 0

    lax.fori_loop(0, planes, step, 0)


def filter_kernel(sizes, counts, start, blocks, levels, out, wide, there):
    planes, rows, _ = sizes
    totals = (counts[0] * planes, counts[1] * rows)
    weight = [2.5 - math.sqrt(q) for q in range(7)]
    sides_x = ((-1, planes - 2, planes, 0), (0, 0, planes, 2), (1, 0, 2, 2 + planes))
    sides_y = ((-1, rows - 2, rows, 0), (0, 0, rows, 2), (1, 0, 2, 2 + rows))
    for step_x, x0, x1, to_x in sides_x:
        for step_y, y0, y1, to_y in sides_y:
            at_x = start[0] // planes + step_x
            at_y = start[1] // rows + step_y
            inside = (at_x >= 0) & (at_x < counts[0]) & (at_y >= 0) & (at_y < counts[1])
            index = jnp.where(inside, at_x * counts[1] + at_y, 0)
            value = blocks[index, x0:x1, y0:y1, :]
            wide[to_x : to_x + x1 - x0, to_y : to_y + y1 - y0, :] = jnp.where(inside, value, 0.0)
    y = lax.broadcasted_iota(jnp.int32, (rows + 4, LANES), 0) + (start[1] - 2)
    in_y = jnp.logical_and(y >= 0, y < totals[1])
    for x in range(planes + 4):
        global_x = start[0] + (x - 2)
        in_x = jnp.logical_and(global_x >= 0, global_x < totals[0])
        there[x] = jnp.where(jnp.logical_and(in_y, in_x), 1.0, 0.0)

    def smooth(ref, x):
        near = {}
        for dx in range(-2, 3):
            for dy in range(-2, 3):
                q = dx * dx + dy * dy
                if q <= 5:
                    value = ref[x + 2 + dx, 2 + dy : 2 + dy + rows, :]
                    near[q] = value if q not in near else near[q] + value
        result = 0.0
        for dz in range(3):
            part = None
            for q, value in near.items():
                if q + dz * dz <= 6:
                    term = weight[q + dz * dz] * value
                    part = term if part is None else part + term
            if dz == 0:
                result = part
            else:
                place = lax.broadcasted_iota(jnp.int32, part.shape, 1)
                forward = jnp.where(place >= LANES - dz, 0.0, pltpu.roll(part, LANES - dz, 1))
                backward = jnp.where(place < dz, 0.0, pltpu.roll(part, dz, 1))
                result = result + (forward + backward)
        return result

    for x in range(planes):
        density = 0.3 + 0.7 * levels[x].astype(f32) / (LEVELS - 1)
        out[x] = smooth(wide, x) / (density * smooth(there, x))


def local(forces, levels, supports):
    _, cases, planes, rows, _ = forces.shape
    sizes = (planes, rows, cases)
    block = 3 * cases
    count_x, count_y = lax.axis_size("gx"), lax.axis_size("gy")

    def shape(blocks, codes):
        return jax.ShapeDtypeStruct((blocks * block + up8(codes), LANES), f32)

    whole = shape(planes * rows, planes * rows)
    down = [] if planes == 2 else [shape(2 * rows, 2 * rows)]
    own, up, *down = pl.pallas_call(
        functools.partial(pack_kernel, sizes),
        out_shape=[whole, shape(rows, 2 * rows), *down],
        in_specs=[VMEM] * 3,
        out_specs=[VMEM] * (2 + len(down)),
        compiler_params=PARAMS,
        name="pack",
    )(forces, levels, supports)

    def moved(value, axis, step):
        count = lax.axis_size(axis)
        pairs = [(i, i + step) for i in range(count) if 0 <= i + step < count]
        return lax.ppermute(value, axis, pairs)

    from_xp = moved(down[0] if down else own, "gx", -1)
    from_xm = moved(up, "gx", 1)
    ym, yp = pl.pallas_call(
        functools.partial(edge_kernel, sizes),
        out_shape=[
            shape(2 * (planes + 3), 2 * (planes + 4)), shape(planes + 3, 2 * (planes + 4))
        ],
        in_specs=[VMEM] * 3,
        out_specs=[VMEM] * 2,
        compiler_params=PARAMS,
        name="edges",
    )(own, from_xm, from_xp)
    from_yp, from_ym = moved(ym, "gy", -1), moved(yp, "gy", 1)

    nodes = (planes + 1) * (rows + 1)
    wide = (planes + 3) * (rows + 3)
    acc = pltpu.VMEM(((planes + 3) * (rows + 1), block, LANES), f32)
    field = pltpu.VMEM((nodes, block, LANES), f32)
    both, system = pl.pallas_call(
        functools.partial(main_kernel, sizes),
        out_shape=[
            jax.ShapeDtypeStruct((4 * cases, nodes * 3 * LANES), bf16),
            jax.ShapeDtypeStruct((cases, LANES), f32),
        ],
        in_specs=[VMEM] * 5,
        out_specs=[VMEM] * 2,
        scratch_shapes=[
            pltpu.VMEM((planes + 4, up8(rows + 4), LANES), f32),
            pltpu.VMEM((planes + 3, up8(rows + 3), LANES), f32),
            pltpu.VMEM((wide, block, LANES), f32),
            pltpu.VMEM((wide, block, LANES), f32),
            pltpu.VMEM((wide, block, LANES), f32),
            acc, acc, field, field, field, field,
            pltpu.VMEM((4 * cases, planes * rows * 3 * LANES), bf16),
            pltpu.VMEM((2 * cases, nodes * 3 * LANES), bf16),
        ],
        compiler_params=PARAMS,
        name="operator",
    )(own, from_xm, from_xp, from_ym, from_yp)

    def gathered(value):
        copies = jnp.broadcast_to(value[None], (count_x * count_y, *value.shape))
        return lax.all_to_all(copies, ("gx", "gy"), 0, 0)

    system = gathered(system)

    weighted = pl.pallas_call(
        functools.partial(solve_kernel, sizes),
        out_shape=jax.ShapeDtypeStruct((planes, rows, LANES), f32),
        in_specs=[VMEM] * 3,
        out_specs=VMEM,
        scratch_shapes=[
            pltpu.VMEM((2 * cases, LANES), f32),
            field,
            field,
            pltpu.VMEM((rows, 8, LANES), f32),
        ],
        compiler_params=PARAMS,
        name="solve",
    )(system, both, levels)

    blocks = gathered(weighted)
    start = jnp.stack([lax.axis_index("gx") * planes, lax.axis_index("gy") * rows])
    return pl.pallas_call(
        functools.partial(filter_kernel, sizes, (count_x, count_y)),
        out_shape=jax.ShapeDtypeStruct((planes, rows, LANES), f32),
        in_specs=[pl.BlockSpec(memory_space=pltpu.SMEM)] + [VMEM] * 2,
        out_specs=VMEM,
        scratch_shapes=[pltpu.VMEM((planes + 4, rows + 4, LANES), f32)] * 2,
        compiler_params=PARAMS,
        name="cone",
    )(start.astype(jnp.int32), blocks, levels)


def solution(mesh):
    return jax.shard_map(
        local,
        mesh=mesh,
        in_specs=(P(None, None, "gx", "gy", None), P("gx", "gy", None), P("gx", "gy", None)),
        out_specs=P("gx", "gy", None),
        check_vma=False,
    )
```

```python
import functools
import math

import jax
import jax.numpy as jnp
from jax import lax
from jax.experimental import pallas as pl
from jax.experimental.pallas import tpu as pltpu
from jax.sharding import PartitionSpec as P

LEVELS = 16
LOAD = 0.2
LANES = 128
POISSON = 0.3
LAME = POISSON / ((1.0 + POISSON) * (1.0 - 2.0 * POISSON))
SHEAR = 1.0 / (2.0 * (1.0 + POISSON))
DIAGONAL = (LAME + 2.0 * SHEAR) / 9.0 + 2.0 * SHEAR / 9.0
VMEM = pl.BlockSpec(memory_space=pltpu.VMEM)
PARAMS = pltpu.CompilerParams(vmem_limit_bytes=50 * 2**20)
f32 = jnp.float32
bf16 = jnp.bfloat16


def up8(count):
    return -(-count // 8) * 8


def shift_down(value):
    lane = lax.broadcasted_iota(jnp.int32, value.shape, value.ndim - 1)
    rolled = pltpu.roll(value, LANES - 1, value.ndim - 1)
    return jnp.where(lane == LANES - 1, 0.0, rolled)


def shift_up(value):
    lane = lax.broadcasted_iota(jnp.int32, value.shape, value.ndim - 1)
    return jnp.where(lane == 0, 0.0, pltpu.roll(value, 1, value.ndim - 1))


def split(value):
    high = value.astype(bf16)
    return high, (value - high.astype(f32)).astype(bf16)


def modes_of(lower, upper):
    out = [[[[None] * 3 for _ in range(2)] for _ in range(2)] for _ in range(2)]
    for a in range(2):
        for c in range(2):
            for k in range(3):
                if a or c:
                    out[a][0][c][k] = lower[a][c][k] + upper[a][c][k]
                out[a][1][c][k] = upper[a][c][k] - lower[a][c][k]
    return out


PAIRS = (((1, 1, 0, 0), (0, 1, 1, 2)), ((1, 0, 1, 0), (0, 1, 1, 1)), ((1, 1, 0, 1), (1, 0, 1, 2)))
TRIPLE = ((0, 1, 1, 0), (1, 0, 1, 1), (1, 1, 0, 2))
SHEARS = (((0, 1, 0, 0), (1, 0, 0, 1)), ((0, 0, 1, 0), (1, 0, 0, 2)), ((0, 0, 1, 1), (0, 1, 0, 2)))
AXIAL = ((1, 0, 0, 0), (0, 1, 0, 1), (0, 0, 1, 2))


def at(modes, place):
    a, b, c, k = place
    return modes[a][b][c][k]


def mode_forces(modes, stiff):
    out = [[[[None] * 3 for _ in range(2)] for _ in range(2)] for _ in range(2)]

    def put(place, value):
        a, b, c, k = place
        out[a][b][c][k] = value

    shear = stiff * (SHEAR / 16)
    for first, second in SHEARS:
        force = shear * (at(modes, first) + at(modes, second))
        put(first, force)
        put(second, force)
    one, two, three = (at(modes, place) for place in AXIAL)
    volume = (stiff * (LAME / 16)) * (one + two + three)
    axial = stiff * (SHEAR / 8)
    for place in AXIAL:
        put(place, volume + axial * at(modes, place))
    own, cross = stiff * ((LAME + 3 * SHEAR) / 48), stiff * (LAME / 48)
    for first, second in PAIRS:
        one, two = at(modes, first), at(modes, second)
        put(first, own * one + cross * two)
        put(second, own * two + cross * one)
    twist = stiff * (SHEAR / 48)
    one, two, three = (at(modes, place) for place in TRIPLE)
    total = one + two + three
    for place in TRIPLE:
        put(place, twist * (total + at(modes, place)))
    last = stiff * ((LAME + 4 * SHEAR) / 144)
    for k in range(3):
        put((1, 1, 1, k), last * modes[1][1][1][k])
    return out


def mode_energy(modes):
    def square(value):
        return value * value

    shear = None
    for first, second in SHEARS:
        term = square(at(modes, first) + at(modes, second))
        shear = term if shear is None else shear + term
    one, two, three = (at(modes, place) for place in AXIAL)
    energy = (SHEAR / 16) * shear + (LAME / 16) * square(one + two + three)
    energy = energy + (SHEAR / 8) * (square(one) + square(two) + square(three))
    squares, products = None, None
    for first, second in PAIRS:
        one, two = at(modes, first), at(modes, second)
        term, product = square(one) + square(two), one * two
        squares = term if squares is None else squares + term
        products = product if products is None else products + product
    energy = energy + ((LAME + 3 * SHEAR) / 48) * squares + (LAME / 24) * products
    one, two, three = (at(modes, place) for place in TRIPLE)
    twist = square(one + two + three) + square(one) + square(two) + square(three)
    energy = energy + (SHEAR / 48) * twist
    last = square(modes[1][1][1][0]) + square(modes[1][1][1][1]) + square(modes[1][1][1][2])
    return energy + ((LAME + 4 * SHEAR) / 144) * last


def x_modes(sums, diffs, plane, row, tile, cases, columns):
    out = [[[None] * 3 for _ in range(2)] for _ in range(2)]
    for c, ref in enumerate((sums, diffs)):
        for k in range(3):
            rows = pl.ds(pl.multiple_of(k * cases + tile * 8, 8), 8)
            one = ref[plane * columns + row, rows, :]
            two = ref[(plane + 1) * columns + row, rows, :]
            out[0][c][k] = one + two
            out[1][c][k] = two - one
    return out


def apply_elements(
    sums, diffs, stiff_ref, acc_s, acc_d, planes, rows, skip, stiff_x, stiff_y, cases
):
    columns = rows + 1
    acc_columns = columns - 2 * skip
    tiles = cases // 8

    def step(index, _):
        plane, tile = index // tiles, index % tiles

        def emit(row, total):
            if not skip <= row < columns - skip:
                return
            for c, acc in enumerate((acc_s, acc_d)):
                for k in range(3):
                    lines = pl.ds(pl.multiple_of(k * cases + tile * 8, 8), 8)
                    low = plane * acc_columns + row - skip
                    acc[low, lines, :] += total[0][c][k] - total[1][c][k]
                    acc[low + acc_columns, lines, :] = total[0][c][k] + total[1][c][k]

        lower = x_modes(sums, diffs, plane, 0, tile, cases, columns)
        carry = None
        for row in range(rows):
            upper = x_modes(sums, diffs, plane, row + 1, tile, cases, columns)
            stiff = jnp.broadcast_to(
                stiff_ref[plane + stiff_x, pl.ds(row + stiff_y, 1), :], (8, LANES)
            )
            forces = mode_forces(modes_of(lower, upper), stiff)
            here = [[[None] * 3 for _ in range(2)] for _ in range(2)]
            following = [[[None] * 3 for _ in range(2)] for _ in range(2)]
            for a in range(2):
                for c in range(2):
                    for k in range(3):
                        one, two = forces[a][0][c][k], forces[a][1][c][k]
                        low = -two if one is None else one - two
                        high = two if one is None else one + two
                        here[a][c][k] = low if carry is None else carry[a][c][k] + low
                        following[a][c][k] = high
            emit(row, here)
            carry, lower = following, upper
        emit(rows, carry)
        return 0

    lax.fori_loop(0, planes * tiles, step, 0)


def pack_kernel(sizes, forces, levels, supports, own, up, *rest):
    planes, rows, cases = sizes
    block = 3 * cases
    base = planes * rows * block
    for x in range(planes):
        density = 0.3 + 0.7 * levels[x].astype(f32) / (LEVELS - 1)
        stiff = density * density * density
        free = supports[x] == 0
        own[base + x * rows : base + (x + 1) * rows, :] = jnp.where(free, stiff, -stiff)
        scale = jnp.where(free, LOAD, 0.0)
        for k in range(3):
            for c in range(cases):
                start = x * rows * block + k * cases + c
                own[pl.ds(start, rows, stride=block), :] = forces[k, c, x] * scale

    def fill(ref, xs, code_xs):
        size = len(xs) * rows * block
        ref[:size, :] = own[xs[0] * rows * block : xs[0] * rows * block + size, :]
        codes = base + code_xs[0] * rows
        ref[size:, :] = own[codes : codes + len(code_xs) * rows, :]

    fill(up, range(planes - 1, planes), range(planes - 2, planes))
    for ref in rest:
        fill(ref, range(2), range(2))


def edge_kernel(sizes, own, xm, xp, ym, yp):
    planes, rows, cases = sizes
    block = 3 * cases
    parts = (
        (xm, rows * block, range(1), range(2)),
        (own, planes * rows * block, range(planes), range(planes)),
        (xp, 2 * rows * block, range(2), range(2)),
    )
    for ref, low, count, code in ((ym, 0, 2, 2), (yp, rows - 1, 1, 2)):
        line = 0
        for source, _, xs, _ in parts:
            for x in xs:
                start = (x * rows + low) * block
                ref[line : line + count * block, :] = source[start : start + count * block, :]
                line += count * block
        for source, base, _, xs in parts:
            for x in xs:
                start = base + x * rows + (0 if low == 0 else rows - 2)
                ref[line : line + code, :] = source[start : start + code, :]
                line += code
        if line < ref.shape[0]:
            ref[line:, :] = jnp.zeros((ref.shape[0] - line, LANES), f32)


def main_kernel(
    sizes, own, xm, xp, ym, yp, both_out, system_out, stiff_ref, inverse,
    start, sums, diffs, acc_s, acc_d, w_sums, w_diffs, acc2_s, acc2_d, right, second, table,
):
    planes, rows, cases = sizes
    block = 3 * cases
    xs, ys = planes + 3, rows + 3
    every_x, every_y = range(planes), range(rows)
    low, high_x, high_y = (-1,), (planes, planes + 1), (rows, rows + 1)
    low2 = (-2, -1)
    regions = (
        (own, every_x, every_y, every_x, every_y),
        (xm, low, every_y, low2, every_y),
        (xp, high_x, every_y, high_x, every_y),
        (ym, range(-1, planes + 2), low, range(-2, planes + 2), low2),
        (yp, range(-1, planes + 2), high_y, range(-2, planes + 2), high_y),
    )
    for ref, bx, by, cx, cy in regions:
        base = len(bx) * len(by) * block
        for i, x in enumerate(cx):
            line = base + i * len(cy)
            stiff_ref[x + 2, cy[0] + 2 : cy[0] + 2 + len(cy), :] = ref[line : line + len(cy), :]
    for x in range(-1, planes + 2):
        codes = stiff_ref[x + 2, 0 : ys + 1, :]
        total = jnp.abs(stiff_ref[x + 1, 0 : ys + 1, :]) + jnp.abs(codes)
        total = total[:-1] + total[1:]
        total = total + shift_up(total)
        free = codes[1:] > 0.0
        value = 1.0 / (DIAGONAL * jnp.where(free, total, 1.0))
        inverse[x + 1, 0:ys, :] = jnp.where(free, value, 0.0)
    for x in range(planes + 4):
        stiff_ref[x] = jnp.abs(stiff_ref[x])

    for ref, bx, by, _, _ in regions:
        for i, x in enumerate(bx):

            def place(j, _, ref=ref, i=i, x=x, by=by):
                y = j + by[0] + 1
                load = ref[pl.ds(pl.multiple_of((i * len(by) + j) * block, 8), block), :]
                value = load * inverse[x + 1, pl.ds(y, 1), :]
                column = (x + 1) * ys + y
                start[column] = value
                moved = shift_down(value)
                sums[column] = value + moved
                diffs[column] = moved - value
                return 0

            lax.fori_loop(0, len(by), place, 0)

    nodes_y = rows + 1
    apply_elements(
        sums, diffs, stiff_ref, acc_s, acc_d, planes + 2, rows + 2, 1, 1, 1, cases
    )

    def image(x, y, place):
        column = (x + 1) * nodes_y + y
        s, d = acc_s[column], acc_d[column]
        force = s - d + shift_up(s + d)
        scaled = force * inverse[x + 1, pl.ds(y + 1, 1), :]
        moved = shift_down(scaled)
        w_sums[x * nodes_y + y] = scaled + moved
        w_diffs[x * nodes_y + y] = moved - scaled
        value = start[(x + 1) * ys + y + 1]
        for k in range(3):
            lines = slice(k * cases, (k + 1) * cases)
            pair = jnp.concatenate([value[lines], scaled[lines]], 0)
            lane = pl.ds(pl.multiple_of((place * 3 + k) * LANES, LANES), LANES)
            high, rest = split(pair)
            both_out[0 : 2 * cases, lane] = high
            both_out[2 * cases : 4 * cases, lane] = rest
        return force

    def inside(index, _):
        x, y = index // rows, index % rows
        force = image(x, y, index)
        load = own[pl.ds(pl.multiple_of(index * block, 8), block), :]
        for k in range(3):
            lines = slice(k * cases, (k + 1) * cases)
            pair = jnp.concatenate([load[lines], force[lines]], 0)
            lane = pl.ds(pl.multiple_of((index * 3 + k) * LANES, LANES), LANES)
            high, rest = split(pair)
            right[0 : 2 * cases, lane] = high
            right[2 * cases : 4 * cases, lane] = rest
        return 0

    count = planes * rows
    lax.fori_loop(0, count, inside, 0)

    def beyond_y(x, _):
        image(x, rows, count + x)
        return 0

    lax.fori_loop(0, planes, beyond_y, 0)

    def beyond_x(y, _):
        image(planes, y, count + planes + y)
        return 0

    lax.fori_loop(0, nodes_y, beyond_x, 0)

    for column in range(nodes_y):
        acc2_s[column] = jnp.zeros((block, LANES), f32)
        acc2_d[column] = jnp.zeros((block, LANES), f32)
    apply_elements(w_sums, w_diffs, stiff_ref, acc2_s, acc2_d, planes, rows, 0, 2, 2, cases)

    def second_force(x, y, place):
        column = x * nodes_y + y
        s, d = acc2_s[column], acc2_d[column]
        force = s - d + shift_up(s + d)
        for k in range(3):
            value = force[k * cases : (k + 1) * cases]
            high = value.astype(bf16).astype(f32)
            lane = pl.ds(pl.multiple_of((place * 3 + k) * LANES, LANES), LANES)
            second[:, lane] = jnp.concatenate([high, value - high], 0).astype(bf16)

    def second_inside(index, _):
        second_force(index // rows, index % rows, index)
        return 0

    def second_y(x, _):
        second_force(x, rows, count + x)
        return 0

    def second_x(y, _):
        second_force(planes, y, count + planes + y)
        return 0

    lax.fori_loop(0, count, second_inside, 0)
    lax.fori_loop(0, planes, second_y, 0)
    lax.fori_loop(0, nodes_y, second_x, 0)

    contract = (((1,), (1,)), ((), ()))
    width = count * 3 * LANES
    two = 2 * cases
    gram = lax.dot_general(both_out[:, :width], right[...], contract, preferred_element_type=f32)
    gram = gram[:two] + gram[two:]
    gram = gram[:, :two] + gram[:, two:]
    other = lax.dot_general(both_out[...], second[...], contract, preferred_element_type=f32)
    other = other[:two] + other[two:]
    other = other[:, :cases] + other[:, cases:]
    table[...] = jnp.zeros(table.shape, f32)
    table[:, 0:two] = gram[:cases]
    table[:, two : two + cases] = other[:cases]
    table[:, two + cases : 2 * two] = other[cases:]
    per = system_out.shape[1]
    for index in range(system_out.shape[0] * per):
        line = table[index : index + 1, :] if index < cases else jnp.zeros((1, LANES), f32)
        system_out[index // per, index % per : index % per + 1, :] = line


def sum_kernel(parts, out):
    total = jnp.sum(parts[...], axis=0)
    for index in range(out.shape[0]):
        out[index] = total


def solve_kernel(sizes, system, both, levels, out, mixing, sums, diffs, energy, lines):
    planes, rows, cases = sizes
    two = 2 * cases
    nodes_y = rows + 1
    count = planes * rows
    per = system.shape[1]
    for index in range(cases):
        lines[index : index + 1, :] = system[index // per, index % per : index % per + 1, :]
    total = lines[...]
    table = jnp.concatenate(
        [pltpu.roll(total, LANES - cases, 1), pltpu.roll(total, LANES - two, 1), total], 0
    )
    lane = lax.broadcasted_iota(jnp.int32, (1, LANES), 1)
    gone = 0
    for pivot in range(two):
        drop = pivot // 8 * 8 - gone
        table = table[drop:]
        gone += drop
        line = pivot - gone
        row = table[line : line + 1, :]
        inverse = 1.0 / row[:, pivot : pivot + 1]
        row = jnp.where(lane == pivot, -inverse, row * inverse)
        column = table[:, pivot : pivot + 1]
        table = jnp.where(lane == pivot, 0.0, table) - column * row
    answer = table[two - gone :, :two]
    high = answer.astype(bf16).astype(f32)
    mixing[...] = jnp.zeros(mixing.shape, f32)
    mixing[0:cases, 0:two] = high
    mixing[0:cases, two : 2 * two] = high
    mixing[cases:two, 0:two] = answer - high
    mix = mixing[...][:, : 2 * two].astype(bf16)

    def combined(place, width):
        lanes = pl.ds(pl.multiple_of(place * 3 * LANES, LANES), width * 3 * LANES)
        value = jnp.dot(mix, both[:, lanes], preferred_element_type=f32)
        return value[:cases] + value[cases:]

    def keep(value, index, column):
        for k in range(3):
            part = value[:, (index * 3 + k) * LANES : (index * 3 + k + 1) * LANES]
            moved = shift_down(part)
            sums[column, k * cases : (k + 1) * cases, :] = part + moved
            diffs[column, k * cases : (k + 1) * cases, :] = moved - part

    def inside(x, _):
        value = combined(x * rows, rows)
        for y in range(rows):
            keep(value, y, x * nodes_y + y)
        return 0

    lax.fori_loop(0, planes, inside, 0)
    value = combined(count, planes + nodes_y)
    for x in range(planes):
        keep(value, x, x * nodes_y + rows)
    for y in range(nodes_y):
        keep(value, planes + y, planes * nodes_y + y)

    tiles = cases // 8

    def step(plane, _):
        for tile in range(tiles):
            lower = x_modes(sums, diffs, plane, 0, tile, cases, nodes_y)
            for row in range(rows):
                upper = x_modes(sums, diffs, plane, row + 1, tile, cases, nodes_y)
                part = mode_energy(modes_of(lower, upper))
                if tile == 0:
                    energy[row] = part
                else:
                    energy[row] += part
                lower = upper
        total = jnp.sum(energy[...], axis=1)
        density = 0.3 + 0.7 * levels[plane].astype(f32) / (LEVELS - 1)
        total = (-3.0 / cases) * (density * density * density) * total
        for index in range(out.shape[0]):
            out[index, plane] = total
        return 0

    lax.fori_loop(0, planes, step, 0)


def border_kernel(sizes, counts, start, blocks, column, edges):
    planes, rows, _ = sizes
    for step, low, high, to in ((-1, planes - 2, planes, 0), (0, 0, planes, 2), (1, 0, 2, 2 + planes)):
        place = start[0] // planes + step
        inside = (place >= 0) & (place < counts[0])
        value = blocks[jnp.where(inside, place, 0), low:high]
        column[to : to + high - low] = jnp.where(inside, value, 0.0)
    for index in range(counts[1]):
        first, last = column[:, 0:2, :], column[:, rows - 2 : rows, :]
        edges[index] = jnp.where(index < start[1] // rows, first, last)


def filter_kernel(sizes, counts, start, column, edges, levels, out, wide, there):
    planes, rows, _ = sizes
    totals = (counts[0] * planes, counts[1] * rows)
    weight = [2.5 - math.sqrt(q) for q in range(7)]
    wide[:, 2 : 2 + rows, :] = column[...]
    for step, to in ((-1, 0), (1, 2 + rows)):
        place = start[1] // rows + step
        inside = (place >= 0) & (place < counts[1])
        value = edges[jnp.where(inside, place, 0)]
        wide[:, to : to + 2, :] = jnp.where(inside, value, 0.0)
    y = lax.broadcasted_iota(jnp.int32, (rows + 4, LANES), 0) + (start[1] - 2)
    in_y = jnp.logical_and(y >= 0, y < totals[1])
    for x in range(planes + 4):
        global_x = start[0] + (x - 2)
        in_x = jnp.logical_and(global_x >= 0, global_x < totals[0])
        there[x] = jnp.where(jnp.logical_and(in_y, in_x), 1.0, 0.0)

    def smooth(ref, x):
        near = {}
        for dx in range(-2, 3):
            for dy in range(-2, 3):
                q = dx * dx + dy * dy
                if q <= 5:
                    value = ref[x + 2 + dx, 2 + dy : 2 + dy + rows, :]
                    near[q] = value if q not in near else near[q] + value
        result = 0.0
        for dz in range(3):
            part = None
            for q, value in near.items():
                if q + dz * dz <= 6:
                    term = weight[q + dz * dz] * value
                    part = term if part is None else part + term
            if dz == 0:
                result = part
            else:
                place = lax.broadcasted_iota(jnp.int32, part.shape, 1)
                forward = jnp.where(place >= LANES - dz, 0.0, pltpu.roll(part, LANES - dz, 1))
                backward = jnp.where(place < dz, 0.0, pltpu.roll(part, dz, 1))
                result = result + (forward + backward)
        return result

    for x in range(planes):
        density = 0.3 + 0.7 * levels[x].astype(f32) / (LEVELS - 1)
        out[x] = smooth(wide, x) / (density * smooth(there, x))


def local(forces, levels, supports):
    _, cases, planes, rows, _ = forces.shape
    sizes = (planes, rows, cases)
    block = 3 * cases
    count_x, count_y = lax.axis_size("gx"), lax.axis_size("gy")

    def shape(blocks, codes):
        return jax.ShapeDtypeStruct((blocks * block + up8(codes), LANES), f32)

    whole = shape(planes * rows, planes * rows)
    down = [] if planes == 2 else [shape(2 * rows, 2 * rows)]
    own, up, *down = pl.pallas_call(
        functools.partial(pack_kernel, sizes),
        out_shape=[whole, shape(rows, 2 * rows), *down],
        in_specs=[VMEM] * 3,
        out_specs=[VMEM] * (2 + len(down)),
        compiler_params=PARAMS,
        name="pack",
    )(forces, levels, supports)

    def moved(value, axis, step):
        count = lax.axis_size(axis)
        pairs = [(i, i + step) for i in range(count) if 0 <= i + step < count]
        return lax.ppermute(value, axis, pairs)

    from_xp = moved(down[0] if down else own, "gx", -1)
    from_xm = moved(up, "gx", 1)
    ym, yp = pl.pallas_call(
        functools.partial(edge_kernel, sizes),
        out_shape=[
            shape(2 * (planes + 3), 2 * (planes + 4)), shape(planes + 3, 2 * (planes + 4))
        ],
        in_specs=[VMEM] * 3,
        out_specs=[VMEM] * 2,
        compiler_params=PARAMS,
        name="edges",
    )(own, from_xm, from_xp)
    from_yp, from_ym = moved(ym, "gy", -1), moved(yp, "gy", 1)

    devices = count_x * count_y
    nodes = (planes + 1) * (rows + 1)
    wide = (planes + 3) * (rows + 3)
    acc = pltpu.VMEM(((planes + 3) * (rows + 1), block, LANES), f32)
    field = pltpu.VMEM((nodes, block, LANES), f32)
    both, system = pl.pallas_call(
        functools.partial(main_kernel, sizes),
        out_shape=[
            jax.ShapeDtypeStruct((4 * cases, nodes * 3 * LANES), bf16),
            jax.ShapeDtypeStruct((devices, -(-cases // devices), LANES), f32),
        ],
        in_specs=[VMEM] * 5,
        out_specs=[VMEM] * 2,
        scratch_shapes=[
            pltpu.VMEM((planes + 4, up8(rows + 4), LANES), f32),
            pltpu.VMEM((planes + 3, up8(rows + 3), LANES), f32),
            pltpu.VMEM((wide, block, LANES), f32),
            pltpu.VMEM((wide, block, LANES), f32),
            pltpu.VMEM((wide, block, LANES), f32),
            acc, acc, field, field, field, field,
            pltpu.VMEM((4 * cases, planes * rows * 3 * LANES), bf16),
            pltpu.VMEM((2 * cases, nodes * 3 * LANES), bf16),
            pltpu.VMEM((cases, LANES), f32),
        ],
        compiler_params=PARAMS,
        name="operator",
    )(own, from_xm, from_xp, from_ym, from_yp)

    def exchanged(value, axes):
        return lax.all_to_all(value, axes, 0, 0)

    system = exchanged(system, ("gx", "gy"))
    system = pl.pallas_call(
        sum_kernel,
        out_shape=jax.ShapeDtypeStruct(system.shape, f32),
        in_specs=[VMEM],
        out_specs=VMEM,
        name="sums",
    )(system)
    system = exchanged(system, ("gx", "gy"))

    weighted = pl.pallas_call(
        functools.partial(solve_kernel, sizes),
        out_shape=jax.ShapeDtypeStruct((count_x, planes, rows, LANES), f32),
        in_specs=[VMEM] * 3,
        out_specs=VMEM,
        scratch_shapes=[
            pltpu.VMEM((2 * cases, LANES), f32),
            field,
            field,
            pltpu.VMEM((rows, 8, LANES), f32),
            pltpu.VMEM((cases, LANES), f32),
        ],
        compiler_params=PARAMS,
        name="solve",
    )(system, both, levels)

    blocks = exchanged(weighted, "gx")
    start = jnp.stack([lax.axis_index("gx") * planes, lax.axis_index("gy") * rows])
    start = start.astype(jnp.int32)
    scalars = pl.BlockSpec(memory_space=pltpu.SMEM)
    counts = (count_x, count_y)
    column, edges = pl.pallas_call(
        functools.partial(border_kernel, sizes, counts),
        out_shape=[
            jax.ShapeDtypeStruct((planes + 4, rows, LANES), f32),
            jax.ShapeDtypeStruct((count_y, planes + 4, 2, LANES), f32),
        ],
        in_specs=[scalars, VMEM],
        out_specs=[VMEM] * 2,
        name="borders",
    )(start, blocks)
    edges = exchanged(edges, "gy")
    return pl.pallas_call(
        functools.partial(filter_kernel, sizes, counts),
        out_shape=jax.ShapeDtypeStruct((planes, rows, LANES), f32),
        in_specs=[scalars] + [VMEM] * 3,
        out_specs=VMEM,
        scratch_shapes=[pltpu.VMEM((planes + 4, rows + 4, LANES), f32)] * 2,
        compiler_params=PARAMS,
        name="cone",
    )(start, column, edges, levels)


def solution(mesh):
    return jax.shard_map(
        local,
        mesh=mesh,
        in_specs=(P(None, None, "gx", "gy", None), P("gx", "gy", None), P("gx", "gy", None)),
        out_specs=P("gx", "gy", None),
        check_vma=False,
    )
```

```python
import functools
import math

import jax
import jax.numpy as jnp
from jax import lax
from jax.experimental import pallas as pl
from jax.experimental.pallas import tpu as pltpu
from jax.sharding import PartitionSpec as P

LEVELS = 16
LOAD = 0.2
LANES = 128
POISSON = 0.3
LAME = POISSON / ((1.0 + POISSON) * (1.0 - 2.0 * POISSON))
SHEAR = 1.0 / (2.0 * (1.0 + POISSON))
DIAGONAL = (LAME + 2.0 * SHEAR) / 9.0 + 2.0 * SHEAR / 9.0
VMEM = pl.BlockSpec(memory_space=pltpu.VMEM)
PARAMS = pltpu.CompilerParams(vmem_limit_bytes=50 * 2**20)
f32 = jnp.float32
bf16 = jnp.bfloat16


def up8(count):
    return -(-count // 8) * 8


def shift_down(value):
    lane = lax.broadcasted_iota(jnp.int32, value.shape, value.ndim - 1)
    rolled = pltpu.roll(value, LANES - 1, value.ndim - 1)
    return jnp.where(lane == LANES - 1, 0.0, rolled)


def shift_up(value):
    lane = lax.broadcasted_iota(jnp.int32, value.shape, value.ndim - 1)
    return jnp.where(lane == 0, 0.0, pltpu.roll(value, 1, value.ndim - 1))


def unrolled(count, factor, body):
    def turn(step, _):
        for offset in range(factor):
            body(step * factor + offset)
        return 0

    turns = count // factor
    if turns:
        lax.fori_loop(0, turns, turn, 0)
    for index in range(turns * factor, count):
        body(index)


def split(value):
    high = value.astype(bf16)
    return high, (value - high.astype(f32)).astype(bf16)


def modes_of(lower, upper):
    out = [[[[None] * 3 for _ in range(2)] for _ in range(2)] for _ in range(2)]
    for a in range(2):
        for c in range(2):
            for k in range(3):
                if a or c:
                    out[a][0][c][k] = lower[a][c][k] + upper[a][c][k]
                out[a][1][c][k] = upper[a][c][k] - lower[a][c][k]
    return out


PAIRS = (((1, 1, 0, 0), (0, 1, 1, 2)), ((1, 0, 1, 0), (0, 1, 1, 1)), ((1, 1, 0, 1), (1, 0, 1, 2)))
TRIPLE = ((0, 1, 1, 0), (1, 0, 1, 1), (1, 1, 0, 2))
SHEARS = (((0, 1, 0, 0), (1, 0, 0, 1)), ((0, 0, 1, 0), (1, 0, 0, 2)), ((0, 0, 1, 1), (0, 1, 0, 2)))
AXIAL = ((1, 0, 0, 0), (0, 1, 0, 1), (0, 0, 1, 2))


def at(modes, place):
    a, b, c, k = place
    return modes[a][b][c][k]


def mode_forces(modes, stiff):
    out = [[[[None] * 3 for _ in range(2)] for _ in range(2)] for _ in range(2)]

    def put(place, value):
        a, b, c, k = place
        out[a][b][c][k] = value

    shear = stiff * (SHEAR / 16)
    for first, second in SHEARS:
        force = shear * (at(modes, first) + at(modes, second))
        put(first, force)
        put(second, force)
    one, two, three = (at(modes, place) for place in AXIAL)
    volume = (stiff * (LAME / 16)) * (one + two + three)
    axial = stiff * (SHEAR / 8)
    for place in AXIAL:
        put(place, volume + axial * at(modes, place))
    own, cross = stiff * ((LAME + 3 * SHEAR) / 48), stiff * (LAME / 48)
    for first, second in PAIRS:
        one, two = at(modes, first), at(modes, second)
        put(first, own * one + cross * two)
        put(second, own * two + cross * one)
    twist = stiff * (SHEAR / 48)
    one, two, three = (at(modes, place) for place in TRIPLE)
    total = one + two + three
    for place in TRIPLE:
        put(place, twist * (total + at(modes, place)))
    last = stiff * ((LAME + 4 * SHEAR) / 144)
    for k in range(3):
        put((1, 1, 1, k), last * modes[1][1][1][k])
    return out


def mode_energy(modes):
    def square(value):
        return value * value

    shear = None
    for first, second in SHEARS:
        term = square(at(modes, first) + at(modes, second))
        shear = term if shear is None else shear + term
    one, two, three = (at(modes, place) for place in AXIAL)
    energy = (SHEAR / 16) * shear + (LAME / 16) * square(one + two + three)
    energy = energy + (SHEAR / 8) * (square(one) + square(two) + square(three))
    squares, products = None, None
    for first, second in PAIRS:
        one, two = at(modes, first), at(modes, second)
        term, product = square(one) + square(two), one * two
        squares = term if squares is None else squares + term
        products = product if products is None else products + product
    energy = energy + ((LAME + 3 * SHEAR) / 48) * squares + (LAME / 24) * products
    one, two, three = (at(modes, place) for place in TRIPLE)
    twist = square(one + two + three) + square(one) + square(two) + square(three)
    energy = energy + (SHEAR / 48) * twist
    last = square(modes[1][1][1][0]) + square(modes[1][1][1][1]) + square(modes[1][1][1][2])
    return energy + ((LAME + 4 * SHEAR) / 144) * last


def x_modes(sums, diffs, plane, row, tile, cases, columns):
    out = [[[None] * 3 for _ in range(2)] for _ in range(2)]
    for c, ref in enumerate((sums, diffs)):
        for k in range(3):
            rows = pl.ds(pl.multiple_of(k * cases + tile * 8, 8), 8)
            one = ref[plane * columns + row, rows, :]
            two = ref[(plane + 1) * columns + row, rows, :]
            out[0][c][k] = one + two
            out[1][c][k] = two - one
    return out


def apply_elements(
    sums, diffs, stiff_ref, acc_s, acc_d, planes, rows, skip, stiff_x, stiff_y, cases
):
    columns = rows + 1
    acc_columns = columns - 2 * skip
    tiles = cases // 8

    def step(index, _):
        plane, tile = index // tiles, index % tiles

        def emit(row, total):
            if not skip <= row < columns - skip:
                return
            for c, acc in enumerate((acc_s, acc_d)):
                for k in range(3):
                    lines = pl.ds(pl.multiple_of(k * cases + tile * 8, 8), 8)
                    low = plane * acc_columns + row - skip
                    acc[low, lines, :] += total[0][c][k] - total[1][c][k]
                    acc[low + acc_columns, lines, :] = total[0][c][k] + total[1][c][k]

        lower = x_modes(sums, diffs, plane, 0, tile, cases, columns)
        carry = None
        for row in range(rows):
            upper = x_modes(sums, diffs, plane, row + 1, tile, cases, columns)
            stiff = jnp.broadcast_to(
                stiff_ref[plane + stiff_x, pl.ds(row + stiff_y, 1), :], (8, LANES)
            )
            forces = mode_forces(modes_of(lower, upper), stiff)
            here = [[[None] * 3 for _ in range(2)] for _ in range(2)]
            following = [[[None] * 3 for _ in range(2)] for _ in range(2)]
            for a in range(2):
                for c in range(2):
                    for k in range(3):
                        one, two = forces[a][0][c][k], forces[a][1][c][k]
                        low = -two if one is None else one - two
                        high = two if one is None else one + two
                        here[a][c][k] = low if carry is None else carry[a][c][k] + low
                        following[a][c][k] = high
            emit(row, here)
            carry, lower = following, upper
        emit(rows, carry)
        return 0

    lax.fori_loop(0, planes * tiles, step, 0)


def pack_kernel(sizes, forces_hbm, levels_hbm, supports_hbm, own, up, *rest):
    planes, rows, cases = sizes
    block = 3 * cases
    base = planes * rows * block
    *rest, forces, levels, supports, arrived = rest
    copies = [
        pltpu.make_async_copy(levels_hbm, levels, arrived.at[3]),
        pltpu.make_async_copy(supports_hbm, supports, arrived.at[4]),
    ]
    copies += [
        pltpu.make_async_copy(forces_hbm.at[k], forces.at[k], arrived.at[k]) for k in range(3)
    ]
    for copy in copies:
        copy.start()
    copies[0].wait()
    copies[1].wait()
    scales = []
    for x in range(planes):
        density = 0.3 + 0.7 * levels[x].astype(f32) / (LEVELS - 1)
        stiff = density * density * density
        free = supports[x] == 0
        own[base + x * rows : base + (x + 1) * rows, :] = jnp.where(free, stiff, -stiff)
        scales.append(jnp.where(free, LOAD, 0.0))
    for k in range(3):
        copies[2 + k].wait()
        for x in range(planes):
            for c in range(cases):
                start = x * rows * block + k * cases + c
                own[pl.ds(start, rows, stride=block), :] = forces[k, c, x] * scales[x]

    def fill(ref, xs, code_xs):
        size = len(xs) * rows * block
        ref[:size, :] = own[xs[0] * rows * block : xs[0] * rows * block + size, :]
        codes = base + code_xs[0] * rows
        ref[size:, :] = own[codes : codes + len(code_xs) * rows, :]

    fill(up, range(planes - 1, planes), range(planes - 2, planes))
    for ref in rest:
        fill(ref, range(2), range(2))


def edge_kernel(sizes, own, xm, xp, ym, yp):
    planes, rows, cases = sizes
    block = 3 * cases
    parts = (
        (xm, rows * block, range(1), range(2)),
        (own, planes * rows * block, range(planes), range(planes)),
        (xp, 2 * rows * block, range(2), range(2)),
    )
    for ref, low, count, code in ((ym, 0, 2, 2), (yp, rows - 1, 1, 2)):
        line = 0
        for source, _, xs, _ in parts:
            for x in xs:
                start = (x * rows + low) * block
                ref[line : line + count * block, :] = source[start : start + count * block, :]
                line += count * block
        for source, base, _, xs in parts:
            for x in xs:
                start = base + x * rows + (0 if low == 0 else rows - 2)
                ref[line : line + code, :] = source[start : start + code, :]
                line += code
        if line < ref.shape[0]:
            ref[line:, :] = jnp.zeros((ref.shape[0] - line, LANES), f32)


def main_kernel(
    sizes, own, xm, xp, ym, yp, both_out, system_out, stiff_ref, inverse,
    start, sums, diffs, acc_s, acc_d, w_sums, w_diffs, acc2_s, acc2_d, right, table,
):
    planes, rows, cases = sizes
    block = 3 * cases
    xs, ys = planes + 3, rows + 3
    every_x, every_y = range(planes), range(rows)
    low, high_x, high_y = (-1,), (planes, planes + 1), (rows, rows + 1)
    low2 = (-2, -1)
    regions = (
        (own, every_x, every_y, every_x, every_y),
        (xm, low, every_y, low2, every_y),
        (xp, high_x, every_y, high_x, every_y),
        (ym, range(-1, planes + 2), low, range(-2, planes + 2), low2),
        (yp, range(-1, planes + 2), high_y, range(-2, planes + 2), high_y),
    )
    for ref, bx, by, cx, cy in regions:
        base = len(bx) * len(by) * block
        for i, x in enumerate(cx):
            line = base + i * len(cy)
            stiff_ref[x + 2, cy[0] + 2 : cy[0] + 2 + len(cy), :] = ref[line : line + len(cy), :]
    for x in range(-1, planes + 2):
        codes = stiff_ref[x + 2, 0 : ys + 1, :]
        total = jnp.abs(stiff_ref[x + 1, 0 : ys + 1, :]) + jnp.abs(codes)
        total = total[:-1] + total[1:]
        total = total + shift_up(total)
        free = codes[1:] > 0.0
        value = 1.0 / (DIAGONAL * jnp.where(free, total, 1.0))
        inverse[x + 1, 0:ys, :] = jnp.where(free, value, 0.0)
    for x in range(planes + 4):
        stiff_ref[x] = jnp.abs(stiff_ref[x])

    for ref, bx, by, _, _ in regions:
        for i, x in enumerate(bx):

            for j in range(len(by)):
                y = j + by[0] + 1
                line = (i * len(by) + j) * block
                load = ref[line : line + block, :]
                value = load * inverse[x + 1, y : y + 1, :]
                column = (x + 1) * ys + y
                start[column] = value
                moved = shift_down(value)
                sums[column] = value + moved
                diffs[column] = moved - value

    nodes_y = rows + 1
    apply_elements(
        sums, diffs, stiff_ref, acc_s, acc_d, planes + 2, rows + 2, 1, 1, 1, cases
    )

    def image(x, y, place):
        column = (x + 1) * nodes_y + y
        s, d = acc_s[column], acc_d[column]
        force = s - d + shift_up(s + d)
        scaled = force * inverse[x + 1, pl.ds(y + 1, 1), :]
        moved = shift_down(scaled)
        w_sums[x * nodes_y + y] = scaled + moved
        w_diffs[x * nodes_y + y] = moved - scaled
        value = start[(x + 1) * ys + y + 1]
        for k in range(3):
            lines = slice(k * cases, (k + 1) * cases)
            pair = jnp.concatenate([value[lines], scaled[lines]], 0)
            lane = pl.ds(pl.multiple_of((place * 3 + k) * LANES, LANES), LANES)
            high, rest = split(pair)
            both_out[0 : 2 * cases, lane] = high
            both_out[2 * cases : 4 * cases, lane] = rest
        return force

    two = 2 * cases
    count = planes * rows

    def inside(index):
        force = image(index // rows, index % rows, index)
        load = own[pl.ds(pl.multiple_of(index * block, 8), block), :]
        for k in range(3):
            lines = slice(k * cases, (k + 1) * cases)
            pair = jnp.concatenate([load[lines], force[lines]], 0)
            lane = pl.ds(pl.multiple_of((index * 3 + k) * LANES, LANES), LANES)
            high, rest = split(pair)
            right[0:two, lane] = high
            right[two : 2 * two, lane] = rest

    unrolled(count, 4, inside)
    unrolled(planes, 2, lambda x: image(x, rows, count + x))
    unrolled(nodes_y, 3, lambda y: image(planes, y, count + planes + y))
    beyond = right.shape[1] - count * 3 * LANES
    right[0 : 2 * two, count * 3 * LANES :] = jnp.zeros((2 * two, beyond), bf16)

    for column in range(nodes_y):
        acc2_s[column] = jnp.zeros((block, LANES), f32)
        acc2_d[column] = jnp.zeros((block, LANES), f32)
    apply_elements(w_sums, w_diffs, stiff_ref, acc2_s, acc2_d, planes, rows, 0, 2, 2, cases)

    def second_force(x, y, place):
        column = x * nodes_y + y
        s, d = acc2_s[column], acc2_d[column]
        force = s - d + shift_up(s + d)
        for k in range(3):
            value = force[k * cases : (k + 1) * cases]
            high = value.astype(bf16).astype(f32)
            lane = pl.ds(pl.multiple_of((place * 3 + k) * LANES, LANES), LANES)
            right[2 * two :, lane] = jnp.concatenate([high, value - high], 0).astype(bf16)

    unrolled(count, 4, lambda index: second_force(index // rows, index % rows, index))
    unrolled(planes, 2, lambda x: second_force(x, rows, count + x))
    unrolled(nodes_y, 3, lambda y: second_force(planes, y, count + planes + y))

    contract = (((1,), (1,)), ((), ()))
    product = lax.dot_general(both_out[...], right[...], contract, preferred_element_type=f32)
    product = product[:two] + product[two:]
    gram = product[:, :two] + product[:, two : 2 * two]
    other = product[:, 2 * two : 2 * two + cases] + product[:, 2 * two + cases :]
    row = lax.broadcasted_iota(jnp.int32, (cases, cases), 0)
    column = lax.broadcasted_iota(jnp.int32, (cases, cases), 1)
    load_load, load_image = gram[:cases, :cases], gram[:cases, cases:]
    mixed, image_image = other[:cases], other[cases:]
    table[...] = jnp.zeros(table.shape, f32)
    table[:, 0:cases] = jnp.where(row <= column, load_load, load_image)
    table[:, cases:two] = jnp.where(row <= column, mixed, image_image)
    for lane, value in ((two, load_image), (two + 1, image_image)):
        own_entries = jnp.where(row == column, value, 0.0)
        table[:, lane : lane + 1] = jnp.sum(own_entries, axis=1, keepdims=True)
    half = cases // 2
    folded = table[:half, :] + pltpu.roll(table[half:, :], LANES // 2, 1)
    depth = system_out.shape[2]
    for index in range(system_out.shape[0]):
        for part in range(half // depth):
            system_out[index, part] = folded[part * depth : (part + 1) * depth]


def solve_kernel(
    sizes, system, both, levels, out, mixing, sums, diffs, energy, square, full
):
    planes, rows, cases = sizes
    two = 2 * cases
    nodes_y = rows + 1
    count = planes * rows
    total = jnp.sum(system[...], axis=0)
    half, depth = cases // 2, system.shape[2]
    square[...] = jnp.zeros(square.shape, f32)
    for part in range(half // depth):
        value = total[part]
        square[part * depth : (part + 1) * depth, :] = value
        lines = slice(half + part * depth, half + (part + 1) * depth)
        square[lines, :] = pltpu.roll(value, LANES // 2, 1)
    value, turned = square[0:cases, :], jnp.transpose(square[...])
    line = lax.broadcasted_iota(jnp.int32, (cases, cases), 0)
    place = lax.broadcasted_iota(jnp.int32, (cases, cases), 1)

    def mended(start, diagonal=None):
        kept, other = value[:, start : start + cases], turned[start : start + cases, :cases]
        if diagonal is None:
            return jnp.where(line <= place, kept, other)
        inner = jnp.where(line < place, other, value[:, diagonal : diagonal + 1])
        return jnp.where(line > place, kept, inner)

    load_image, mixed = mended(0, two), mended(cases)
    parts = ((load_image, mixed), (mixed, mended(cases, two + 1)), (mended(0), load_image))
    full[...] = jnp.zeros(full.shape, f32)
    for index, (left, right) in enumerate(parts):
        full[index * cases : (index + 1) * cases, 0:cases] = left
        full[index * cases : (index + 1) * cases, cases:two] = right
    table = full[...]
    lane = lax.broadcasted_iota(jnp.int32, (1, LANES), 1)
    gone = 0
    for pivot in range(two):
        drop = pivot // 8 * 8 - gone
        table = table[drop:]
        gone += drop
        line = pivot - gone
        row = table[line : line + 1, :]
        inverse = 1.0 / row[:, pivot : pivot + 1]
        row = jnp.where(lane == pivot, -inverse, row * inverse)
        column = table[:, pivot : pivot + 1]
        table = jnp.where(lane == pivot, 0.0, table) - column * row
    answer = table[two - gone :, :two]
    high = answer.astype(bf16).astype(f32)
    mixing[...] = jnp.zeros(mixing.shape, f32)
    mixing[0:cases, 0:two] = high
    mixing[0:cases, two : 2 * two] = high
    mixing[cases:two, 0:two] = answer - high
    mix = mixing[...][:, : 2 * two].astype(bf16)

    def combined(place, width):
        lanes = pl.ds(pl.multiple_of(place * 3 * LANES, LANES), width * 3 * LANES)
        value = jnp.dot(mix, both[:, lanes], preferred_element_type=f32)
        return value[:cases] + value[cases:]

    def keep(value, index, column):
        for k in range(3):
            part = value[:, (index * 3 + k) * LANES : (index * 3 + k + 1) * LANES]
            moved = shift_down(part)
            sums[column, k * cases : (k + 1) * cases, :] = part + moved
            diffs[column, k * cases : (k + 1) * cases, :] = moved - part

    def inside(x, _):
        value = combined(x * rows, rows)
        for y in range(rows):
            keep(value, y, x * nodes_y + y)
        return 0

    lax.fori_loop(0, planes, inside, 0)
    value = combined(count, planes + nodes_y)
    for x in range(planes):
        keep(value, x, x * nodes_y + rows)
    for y in range(nodes_y):
        keep(value, planes + y, planes * nodes_y + y)

    tiles = cases // 8

    def step(plane, _):
        for tile in range(tiles):
            lower = x_modes(sums, diffs, plane, 0, tile, cases, nodes_y)
            for row in range(rows):
                upper = x_modes(sums, diffs, plane, row + 1, tile, cases, nodes_y)
                part = mode_energy(modes_of(lower, upper))
                if tile == 0:
                    energy[row] = part
                else:
                    energy[row] += part
                lower = upper
        total = jnp.sum(energy[...], axis=1)
        density = 0.3 + 0.7 * levels[plane].astype(f32) / (LEVELS - 1)
        total = (-3.0 / cases) * (density * density * density) * total
        for index in range(out.shape[0]):
            out[index, plane] = total
        return 0

    lax.fori_loop(0, planes, step, 0)


def filter_kernel(sizes, counts, start, blocks, levels, out, wide, there):
    planes, rows, _ = sizes
    totals = (counts[0] * planes, counts[1] * rows)
    weight = [2.5 - math.sqrt(q) for q in range(7)]
    sides_x = ((-1, planes - 2, planes, 0), (0, 0, planes, 2), (1, 0, 2, 2 + planes))
    sides_y = ((-1, rows - 2, rows, 0), (0, 0, rows, 2), (1, 0, 2, 2 + rows))
    for step_x, x0, x1, to_x in sides_x:
        for step_y, y0, y1, to_y in sides_y:
            at_x = start[0] // planes + step_x
            at_y = start[1] // rows + step_y
            inside = (at_x >= 0) & (at_x < counts[0]) & (at_y >= 0) & (at_y < counts[1])
            index = jnp.where(inside, at_x * counts[1] + at_y, 0)
            value = blocks[index, x0:x1, y0:y1, :]
            wide[to_x : to_x + x1 - x0, to_y : to_y + y1 - y0, :] = jnp.where(inside, value, 0.0)
    y = lax.broadcasted_iota(jnp.int32, (rows + 4, LANES), 0) + (start[1] - 2)
    in_y = jnp.logical_and(y >= 0, y < totals[1])
    for x in range(planes + 4):
        global_x = start[0] + (x - 2)
        in_x = jnp.logical_and(global_x >= 0, global_x < totals[0])
        there[x] = jnp.where(jnp.logical_and(in_y, in_x), 1.0, 0.0)

    def smooth(ref, x):
        near = {}
        for dx in range(-2, 3):
            for dy in range(-2, 3):
                q = dx * dx + dy * dy
                if q <= 5:
                    value = ref[x + 2 + dx, 2 + dy : 2 + dy + rows, :]
                    near[q] = value if q not in near else near[q] + value
        result = 0.0
        for dz in range(3):
            part = None
            for q, value in near.items():
                if q + dz * dz <= 6:
                    term = weight[q + dz * dz] * value
                    part = term if part is None else part + term
            if dz == 0:
                result = part
            else:
                place = lax.broadcasted_iota(jnp.int32, part.shape, 1)
                forward = jnp.where(place >= LANES - dz, 0.0, pltpu.roll(part, LANES - dz, 1))
                backward = jnp.where(place < dz, 0.0, pltpu.roll(part, dz, 1))
                result = result + (forward + backward)
        return result

    for x in range(planes):
        density = 0.3 + 0.7 * levels[x].astype(f32) / (LEVELS - 1)
        out[x] = smooth(wide, x) / (density * smooth(there, x))


def local(forces, levels, supports):
    _, cases, planes, rows, _ = forces.shape
    sizes = (planes, rows, cases)
    block = 3 * cases
    count_x, count_y = lax.axis_size("gx"), lax.axis_size("gy")

    def shape(blocks, codes):
        return jax.ShapeDtypeStruct((blocks * block + up8(codes), LANES), f32)

    whole = shape(planes * rows, planes * rows)
    down = [] if planes == 2 else [shape(2 * rows, 2 * rows)]
    own, up, *down = pl.pallas_call(
        functools.partial(pack_kernel, sizes),
        out_shape=[whole, shape(rows, 2 * rows), *down],
        in_specs=[pl.BlockSpec(memory_space=pltpu.HBM)] * 3,
        out_specs=[VMEM] * (2 + len(down)),
        scratch_shapes=[
            pltpu.VMEM(forces.shape, f32),
            pltpu.VMEM(levels.shape, jnp.int32),
            pltpu.VMEM(levels.shape, jnp.int32),
            pltpu.SemaphoreType.DMA((5,)),
        ],
        compiler_params=PARAMS,
        name="pack",
    )(forces, levels, supports)

    def moved(value, axis, step):
        count = lax.axis_size(axis)
        pairs = [(i, i + step) for i in range(count) if 0 <= i + step < count]
        return lax.ppermute(value, axis, pairs)

    from_xp = moved(down[0] if down else own, "gx", -1)
    from_xm = moved(up, "gx", 1)
    ym, yp = pl.pallas_call(
        functools.partial(edge_kernel, sizes),
        out_shape=[
            shape(2 * (planes + 3), 2 * (planes + 4)), shape(planes + 3, 2 * (planes + 4))
        ],
        in_specs=[VMEM] * 3,
        out_specs=[VMEM] * 2,
        compiler_params=PARAMS,
        name="edges",
    )(own, from_xm, from_xp)
    from_yp, from_ym = moved(ym, "gy", -1), moved(yp, "gy", 1)

    devices = count_x * count_y
    nodes = (planes + 1) * (rows + 1)
    wide = (planes + 3) * (rows + 3)
    acc = pltpu.VMEM(((planes + 3) * (rows + 1), block, LANES), f32)
    field = pltpu.VMEM((nodes, block, LANES), f32)
    both, system = pl.pallas_call(
        functools.partial(main_kernel, sizes),
        out_shape=[
            jax.ShapeDtypeStruct((4 * cases, nodes * 3 * LANES), bf16),
            jax.ShapeDtypeStruct((devices, cases // 8, 4, LANES), f32),
        ],
        in_specs=[VMEM] * 5,
        out_specs=[VMEM] * 2,
        scratch_shapes=[
            pltpu.VMEM((planes + 4, up8(rows + 4), LANES), f32),
            pltpu.VMEM((planes + 3, up8(rows + 3), LANES), f32),
            pltpu.VMEM((wide, block, LANES), f32),
            pltpu.VMEM((wide, block, LANES), f32),
            pltpu.VMEM((wide, block, LANES), f32),
            acc, acc, field, field, field, field,
            pltpu.VMEM((6 * cases, nodes * 3 * LANES), bf16),
            pltpu.VMEM((cases, LANES), f32),
        ],
        compiler_params=PARAMS,
        name="operator",
    )(own, from_xm, from_xp, from_ym, from_yp)

    def gathered(copies):
        return lax.all_to_all(copies, ("gx", "gy"), 0, 0)

    system = gathered(system)

    weighted = pl.pallas_call(
        functools.partial(solve_kernel, sizes),
        out_shape=jax.ShapeDtypeStruct((devices, planes, rows, LANES), f32),
        in_specs=[VMEM] * 3,
        out_specs=VMEM,
        scratch_shapes=[
            pltpu.VMEM((2 * cases, LANES), f32),
            field,
            field,
            pltpu.VMEM((rows, 8, LANES), f32),
            pltpu.VMEM((LANES, LANES), f32),
            pltpu.VMEM((3 * cases, LANES), f32),
        ],
        compiler_params=PARAMS,
        name="solve",
    )(system, both, levels)

    blocks = gathered(weighted)
    start = jnp.stack([lax.axis_index("gx") * planes, lax.axis_index("gy") * rows])
    return pl.pallas_call(
        functools.partial(filter_kernel, sizes, (count_x, count_y)),
        out_shape=jax.ShapeDtypeStruct((planes, rows, LANES), f32),
        in_specs=[pl.BlockSpec(memory_space=pltpu.SMEM)] + [VMEM] * 2,
        out_specs=VMEM,
        scratch_shapes=[pltpu.VMEM((planes + 4, rows + 4, LANES), f32)] * 2,
        compiler_params=PARAMS,
        name="cone",
    )(start.astype(jnp.int32), blocks, levels)


def solution(mesh):
    return jax.shard_map(
        local,
        mesh=mesh,
        in_specs=(P(None, None, "gx", "gy", None), P("gx", "gy", None), P("gx", "gy", None)),
        out_specs=P("gx", "gy", None),
        check_vma=False,
    )
```

```python
import functools
import math

import jax
import jax.numpy as jnp
from jax import lax
from jax.experimental import pallas as pl
from jax.experimental.pallas import tpu as pltpu
from jax.sharding import PartitionSpec as P

LEVELS = 16
LOAD = 0.2
LANES = 128
POISSON = 0.3
LAME = POISSON / ((1.0 + POISSON) * (1.0 - 2.0 * POISSON))
SHEAR = 1.0 / (2.0 * (1.0 + POISSON))
DIAGONAL = (LAME + 2.0 * SHEAR) / 9.0 + 2.0 * SHEAR / 9.0
VMEM = pl.BlockSpec(memory_space=pltpu.VMEM)
PARAMS = pltpu.CompilerParams(vmem_limit_bytes=30 * 2**20)
f32 = jnp.float32
bf16 = jnp.bfloat16


def up8(count):
    return -(-count // 8) * 8


def shift_down(value):
    lane = lax.broadcasted_iota(jnp.int32, value.shape, value.ndim - 1)
    rolled = pltpu.roll(value, LANES - 1, value.ndim - 1)
    return jnp.where(lane == LANES - 1, 0.0, rolled)


def shift_up(value):
    lane = lax.broadcasted_iota(jnp.int32, value.shape, value.ndim - 1)
    return jnp.where(lane == 0, 0.0, pltpu.roll(value, 1, value.ndim - 1))


def unrolled(count, factor, body):
    def turn(step, _):
        for offset in range(factor):
            body(step * factor + offset)
        return 0

    turns = count // factor
    if turns:
        lax.fori_loop(0, turns, turn, 0)
    for index in range(turns * factor, count):
        body(index)


def split(value):
    high = value.astype(bf16)
    return high, (value - high.astype(f32)).astype(bf16)


def modes_of(lower, upper):
    out = [[[[None] * 3 for _ in range(2)] for _ in range(2)] for _ in range(2)]
    for a in range(2):
        for c in range(2):
            for k in range(3):
                if a or c:
                    out[a][0][c][k] = lower[a][c][k] + upper[a][c][k]
                out[a][1][c][k] = upper[a][c][k] - lower[a][c][k]
    return out


PAIRS = (((1, 1, 0, 0), (0, 1, 1, 2)), ((1, 0, 1, 0), (0, 1, 1, 1)), ((1, 1, 0, 1), (1, 0, 1, 2)))
TRIPLE = ((0, 1, 1, 0), (1, 0, 1, 1), (1, 1, 0, 2))
SHEARS = (((0, 1, 0, 0), (1, 0, 0, 1)), ((0, 0, 1, 0), (1, 0, 0, 2)), ((0, 0, 1, 1), (0, 1, 0, 2)))
AXIAL = ((1, 0, 0, 0), (0, 1, 0, 1), (0, 0, 1, 2))


def at(modes, place):
    a, b, c, k = place
    return modes[a][b][c][k]


def mode_forces(modes, stiff):
    out = [[[[None] * 3 for _ in range(2)] for _ in range(2)] for _ in range(2)]

    def put(place, value):
        a, b, c, k = place
        out[a][b][c][k] = value

    shear = stiff * (SHEAR / 16)
    for first, second in SHEARS:
        force = shear * (at(modes, first) + at(modes, second))
        put(first, force)
        put(second, force)
    one, two, three = (at(modes, place) for place in AXIAL)
    volume = (stiff * (LAME / 16)) * (one + two + three)
    axial = stiff * (SHEAR / 8)
    for place in AXIAL:
        put(place, volume + axial * at(modes, place))
    own, cross = stiff * ((LAME + 3 * SHEAR) / 48), stiff * (LAME / 48)
    for first, second in PAIRS:
        one, two = at(modes, first), at(modes, second)
        put(first, own * one + cross * two)
        put(second, own * two + cross * one)
    twist = stiff * (SHEAR / 48)
    one, two, three = (at(modes, place) for place in TRIPLE)
    total = one + two + three
    for place in TRIPLE:
        put(place, twist * (total + at(modes, place)))
    last = stiff * ((LAME + 4 * SHEAR) / 144)
    for k in range(3):
        put((1, 1, 1, k), last * modes[1][1][1][k])
    return out


def mode_energy(modes):
    def square(value):
        return value * value

    shear = None
    for first, second in SHEARS:
        term = square(at(modes, first) + at(modes, second))
        shear = term if shear is None else shear + term
    one, two, three = (at(modes, place) for place in AXIAL)
    energy = (SHEAR / 16) * shear + (LAME / 16) * square(one + two + three)
    energy = energy + (SHEAR / 8) * (square(one) + square(two) + square(three))
    squares, products = None, None
    for first, second in PAIRS:
        one, two = at(modes, first), at(modes, second)
        term, product = square(one) + square(two), one * two
        squares = term if squares is None else squares + term
        products = product if products is None else products + product
    energy = energy + ((LAME + 3 * SHEAR) / 48) * squares + (LAME / 24) * products
    one, two, three = (at(modes, place) for place in TRIPLE)
    twist = square(one + two + three) + square(one) + square(two) + square(three)
    energy = energy + (SHEAR / 48) * twist
    last = square(modes[1][1][1][0]) + square(modes[1][1][1][1]) + square(modes[1][1][1][2])
    return energy + ((LAME + 4 * SHEAR) / 144) * last


def x_modes(sums, diffs, plane, row, tile, cases, columns):
    out = [[[None] * 3 for _ in range(2)] for _ in range(2)]
    for c, ref in enumerate((sums, diffs)):
        for k in range(3):
            rows = pl.ds(pl.multiple_of(k * cases + tile * 8, 8), 8)
            one = ref[plane * columns + row, rows, :]
            two = ref[(plane + 1) * columns + row, rows, :]
            out[0][c][k] = one + two
            out[1][c][k] = two - one
    return out


def apply_elements(
    sums, diffs, stiff_ref, acc_s, acc_d, planes, rows, skip, stiff_x, stiff_y, cases
):
    columns = rows + 1
    acc_columns = columns - 2 * skip
    tiles = cases // 8

    def step(index, _):
        plane, tile = index // tiles, index % tiles

        def emit(row, total):
            if not skip <= row < columns - skip:
                return
            for c, acc in enumerate((acc_s, acc_d)):
                for k in range(3):
                    lines = pl.ds(pl.multiple_of(k * cases + tile * 8, 8), 8)
                    low = plane * acc_columns + row - skip
                    acc[low, lines, :] += total[0][c][k] - total[1][c][k]
                    acc[low + acc_columns, lines, :] = total[0][c][k] + total[1][c][k]

        lower = x_modes(sums, diffs, plane, 0, tile, cases, columns)
        carry = None
        for row in range(rows):
            upper = x_modes(sums, diffs, plane, row + 1, tile, cases, columns)
            stiff = jnp.broadcast_to(
                stiff_ref[plane + stiff_x, pl.ds(row + stiff_y, 1), :], (8, LANES)
            )
            forces = mode_forces(modes_of(lower, upper), stiff)
            here = [[[None] * 3 for _ in range(2)] for _ in range(2)]
            following = [[[None] * 3 for _ in range(2)] for _ in range(2)]
            for a in range(2):
                for c in range(2):
                    for k in range(3):
                        one, two = forces[a][0][c][k], forces[a][1][c][k]
                        low = -two if one is None else one - two
                        high = two if one is None else one + two
                        here[a][c][k] = low if carry is None else carry[a][c][k] + low
                        following[a][c][k] = high
            emit(row, here)
            carry, lower = following, upper
        emit(rows, carry)
        return 0

    lax.fori_loop(0, planes * tiles, step, 0)


def pack_kernel(sizes, forces, codes, own, up, *rest):
    planes, rows, cases = sizes
    block = 3 * cases
    base = planes * rows * block
    for x in range(planes):
        own[base + x * rows : base + (x + 1) * rows, :] = codes[x]
        scale = jnp.where(codes[x] > 0.0, LOAD, 0.0)
        for k in range(3):
            for c in range(cases):
                start = x * rows * block + k * cases + c
                own[pl.ds(start, rows, stride=block), :] = forces[k, c, x] * scale

    def fill(ref, xs, code_xs):
        size = len(xs) * rows * block
        ref[:size, :] = own[xs[0] * rows * block : xs[0] * rows * block + size, :]
        codes = base + code_xs[0] * rows
        ref[size:, :] = own[codes : codes + len(code_xs) * rows, :]

    fill(up, range(planes - 1, planes), range(planes - 2, planes))
    for ref in rest:
        fill(ref, range(2), range(2))


def beside(sizes, first, pair, lower, upper):
    planes, rows, cases = sizes
    size = rows * 3 * cases
    even = first // planes % 2 == 0

    def below(line, count):
        other = pair[pl.ds((planes - 1) * size + line, count), :]
        return jnp.where(even, lower[pl.ds(line, count), :], other)

    def below_codes(line, count):
        other = pair[pl.ds(planes * size + (planes - 2) * rows + line, count), :]
        return jnp.where(even, lower[pl.ds(size + line, count), :], other)

    def above(line, count):
        return jnp.where(even, pair[pl.ds(line, count), :], upper[pl.ds(line, count), :])

    def above_codes(line, count):
        other = upper[pl.ds(2 * size + line, count), :]
        return jnp.where(even, pair[pl.ds(planes * size + line, count), :], other)

    return below, below_codes, above, above_codes


def edge_kernel(sizes, start, own, pair, lower, upper, ym, yp):
    planes, rows, cases = sizes
    block = 3 * cases
    base = planes * rows * block
    below, below_codes, above, above_codes = beside(sizes, start[0], pair, lower, upper)
    parts = (
        (below, below_codes, 1, 2),
        (
            lambda line, count: own[line : line + count, :],
            lambda line, count: own[base + line : base + line + count, :],
            planes,
            planes,
        ),
        (above, above_codes, 2, 2),
    )
    for ref, low, count in ((ym, 0, 2), (yp, rows - 1, 1)):
        line = 0
        for read, _, xs, _ in parts:
            for x in range(xs):
                ref[line : line + count * block, :] = read((x * rows + low) * block, count * block)
                line += count * block
        for _, read, _, xs in parts:
            for x in range(xs):
                ref[line : line + 2, :] = read(x * rows + (0 if low == 0 else rows - 2), 2)
                line += 2
        if line < ref.shape[0]:
            ref[line:, :] = jnp.zeros((ref.shape[0] - line, LANES), f32)


def main_kernel(
    sizes, first, own, pair, lower, upper, ym, yp, both_out, system_out, stiff_ref, inverse,
    start, sums, diffs, acc_s, acc_d, w_sums, w_diffs, acc2_s, acc2_d, right, table,
):
    planes, rows, cases = sizes
    block = 3 * cases
    xs, ys = planes + 3, rows + 3
    every_x, every_y = range(planes), range(rows)
    low, high_x, high_y = (-1,), (planes, planes + 1), (rows, rows + 1)
    low2 = (-2, -1)
    below, below_codes, above, above_codes = beside(sizes, first[0], pair, lower, upper)

    def reader(ref, base=0):
        return lambda line, count: ref[base + line : base + line + count, :]

    def region(ref, bx, by, cx, cy):
        return (reader(ref), reader(ref, len(bx) * len(by) * block), bx, by, cx, cy)

    regions = (
        region(own, every_x, every_y, every_x, every_y),
        (below, below_codes, low, every_y, low2, every_y),
        (above, above_codes, high_x, every_y, high_x, every_y),
        region(ym, range(-1, planes + 2), low, range(-2, planes + 2), low2),
        region(yp, range(-1, planes + 2), high_y, range(-2, planes + 2), high_y),
    )
    for _, read, _, _, cx, cy in regions:
        for i, x in enumerate(cx):
            stiff_ref[x + 2, cy[0] + 2 : cy[0] + 2 + len(cy), :] = read(i * len(cy), len(cy))
    for x in range(-1, planes + 2):
        codes = stiff_ref[x + 2, 0 : ys + 1, :]
        total = jnp.abs(stiff_ref[x + 1, 0 : ys + 1, :]) + jnp.abs(codes)
        total = total[:-1] + total[1:]
        total = total + shift_up(total)
        free = codes[1:] > 0.0
        value = 1.0 / (DIAGONAL * jnp.where(free, total, 1.0))
        inverse[x + 1, 0:ys, :] = jnp.where(free, value, 0.0)
    for x in range(planes + 4):
        stiff_ref[x] = jnp.abs(stiff_ref[x])

    for read, _, bx, by, _, _ in regions:
        for i, x in enumerate(bx):

            for j in range(len(by)):
                y = j + by[0] + 1
                line = (i * len(by) + j) * block
                load = read(line, block)
                value = load * inverse[x + 1, y : y + 1, :]
                column = (x + 1) * ys + y
                start[column] = value
                moved = shift_down(value)
                sums[column] = value + moved
                diffs[column] = moved - value

    nodes_y = rows + 1
    apply_elements(
        sums, diffs, stiff_ref, acc_s, acc_d, planes + 2, rows + 2, 1, 1, 1, cases
    )

    def image(x, y, place):
        column = (x + 1) * nodes_y + y
        s, d = acc_s[column], acc_d[column]
        force = s - d + shift_up(s + d)
        scaled = force * inverse[x + 1, pl.ds(y + 1, 1), :]
        moved = shift_down(scaled)
        w_sums[x * nodes_y + y] = scaled + moved
        w_diffs[x * nodes_y + y] = moved - scaled
        value = start[(x + 1) * ys + y + 1]
        for k in range(3):
            lines = slice(k * cases, (k + 1) * cases)
            pair = jnp.concatenate([value[lines], scaled[lines]], 0)
            lane = pl.ds(pl.multiple_of((place * 3 + k) * LANES, LANES), LANES)
            high, rest = split(pair)
            both_out[0 : 2 * cases, lane] = high
            both_out[2 * cases : 4 * cases, lane] = rest
        return force

    two = 2 * cases
    count = planes * rows

    def inside(index):
        force = image(index // rows, index % rows, index)
        load = own[pl.ds(pl.multiple_of(index * block, 8), block), :]
        for k in range(3):
            lines = slice(k * cases, (k + 1) * cases)
            pair = jnp.concatenate([load[lines], force[lines]], 0)
            lane = pl.ds(pl.multiple_of((index * 3 + k) * LANES, LANES), LANES)
            high, rest = split(pair)
            right[0:two, lane] = high
            right[two : 2 * two, lane] = rest

    unrolled(count, 4, inside)
    unrolled(planes, 2, lambda x: image(x, rows, count + x))
    unrolled(nodes_y, 3, lambda y: image(planes, y, count + planes + y))
    beyond = right.shape[1] - count * 3 * LANES
    right[0 : 2 * two, count * 3 * LANES :] = jnp.zeros((2 * two, beyond), bf16)

    for column in range(nodes_y):
        acc2_s[column] = jnp.zeros((block, LANES), f32)
        acc2_d[column] = jnp.zeros((block, LANES), f32)
    apply_elements(w_sums, w_diffs, stiff_ref, acc2_s, acc2_d, planes, rows, 0, 2, 2, cases)

    def second_force(x, y, place):
        column = x * nodes_y + y
        s, d = acc2_s[column], acc2_d[column]
        force = s - d + shift_up(s + d)
        for k in range(3):
            value = force[k * cases : (k + 1) * cases]
            high = value.astype(bf16).astype(f32)
            lane = pl.ds(pl.multiple_of((place * 3 + k) * LANES, LANES), LANES)
            right[2 * two :, lane] = jnp.concatenate([high, value - high], 0).astype(bf16)

    unrolled(count, 4, lambda index: second_force(index // rows, index % rows, index))
    unrolled(planes, 2, lambda x: second_force(x, rows, count + x))
    unrolled(nodes_y, 3, lambda y: second_force(planes, y, count + planes + y))

    contract = (((1,), (1,)), ((), ()))
    product = lax.dot_general(both_out[...], right[...], contract, preferred_element_type=f32)
    product = product[:two] + product[two:]
    gram = product[:, :two] + product[:, two : 2 * two]
    other = product[:, 2 * two : 2 * two + cases] + product[:, 2 * two + cases :]
    row = lax.broadcasted_iota(jnp.int32, (cases, cases), 0)
    column = lax.broadcasted_iota(jnp.int32, (cases, cases), 1)
    load_load, load_image = gram[:cases, :cases], gram[:cases, cases:]
    mixed, image_image = other[:cases], other[cases:]
    table[...] = jnp.zeros(table.shape, f32)
    table[:, 0:cases] = jnp.where(row <= column, load_load, load_image)
    table[:, cases:two] = jnp.where(row <= column, mixed, image_image)
    for lane, value in ((two, load_image), (two + 1, image_image)):
        own_entries = jnp.where(row == column, value, 0.0)
        table[:, lane : lane + 1] = jnp.sum(own_entries, axis=1, keepdims=True)
    half = cases // 2
    folded = table[:half, :] + pltpu.roll(table[half:, :], LANES // 2, 1)
    depth = system_out.shape[2]
    for index in range(system_out.shape[0]):
        for part in range(half // depth):
            system_out[index, part] = folded[part * depth : (part + 1) * depth]


def solve_kernel(
    sizes, system, both, codes, out, mixing, sums, diffs, energy, square, full
):
    planes, rows, cases = sizes
    two = 2 * cases
    nodes_y = rows + 1
    count = planes * rows
    total = jnp.sum(system[...], axis=0)
    half, depth = cases // 2, system.shape[2]
    square[...] = jnp.zeros(square.shape, f32)
    for part in range(half // depth):
        value = total[part]
        square[part * depth : (part + 1) * depth, :] = value
        lines = slice(half + part * depth, half + (part + 1) * depth)
        square[lines, :] = pltpu.roll(value, LANES // 2, 1)
    value, turned = square[0:cases, :], jnp.transpose(square[...])
    line = lax.broadcasted_iota(jnp.int32, (cases, cases), 0)
    place = lax.broadcasted_iota(jnp.int32, (cases, cases), 1)

    def mended(start, diagonal=None):
        kept, other = value[:, start : start + cases], turned[start : start + cases, :cases]
        if diagonal is None:
            return jnp.where(line <= place, kept, other)
        inner = jnp.where(line < place, other, value[:, diagonal : diagonal + 1])
        return jnp.where(line > place, kept, inner)

    load_image, mixed = mended(0, two), mended(cases)
    parts = ((load_image, mixed), (mixed, mended(cases, two + 1)), (mended(0), load_image))
    full[...] = jnp.zeros(full.shape, f32)
    for index, (left, right) in enumerate(parts):
        full[index * cases : (index + 1) * cases, 0:cases] = left
        full[index * cases : (index + 1) * cases, cases:two] = right
    table = full[...]
    lane = lax.broadcasted_iota(jnp.int32, (1, LANES), 1)
    gone, wide = 0, 4
    for pivot in range(0, two, wide):
        drop = pivot // 8 * 8 - gone
        table = table[drop:]
        gone += drop
        line = pivot - gone
        inner = (lane >= pivot) & (lane < pivot + wide)
        found = [table[line + p : line + p + 1, :] for p in range(wide)]
        block = [
            [jnp.broadcast_to(row[:, pivot + q : pivot + q + 1], row.shape) for q in range(wide)]
            for row in found
        ]
        solved = [
            jnp.where(lane == pivot + p, -1.0, jnp.where(inner, 0.0, found[p]))
            for p in range(wide)
        ]
        for p in range(wide):
            inverse = 1.0 / block[p][p]
            solved[p] = solved[p] * inverse
            block[p] = [value * inverse for value in block[p]]
            for q in range(wide):
                if q != p:
                    factor = block[q][p]
                    solved[q] = solved[q] - factor * solved[p]
                    for r in range(p + 1, wide):
                        block[q][r] = block[q][r] - factor * block[p][r]
        update = None
        for q in range(wide):
            term = table[:, pivot + q : pivot + q + 1] * solved[q]
            update = term if update is None else update + term
        table = jnp.where(inner, 0.0, table) - update
    answer = table[two - gone :, :two]
    high = answer.astype(bf16).astype(f32)
    mixing[...] = jnp.zeros(mixing.shape, f32)
    mixing[0:cases, 0:two] = high
    mixing[0:cases, two : 2 * two] = high
    mixing[cases:two, 0:two] = answer - high
    mix = mixing[...][:, : 2 * two].astype(bf16)

    def combined(place, width):
        lanes = pl.ds(pl.multiple_of(place * 3 * LANES, LANES), width * 3 * LANES)
        value = jnp.dot(mix, both[:, lanes], preferred_element_type=f32)
        return value[:cases] + value[cases:]

    def keep(value, index, column):
        for k in range(3):
            part = value[:, (index * 3 + k) * LANES : (index * 3 + k + 1) * LANES]
            moved = shift_down(part)
            sums[column, k * cases : (k + 1) * cases, :] = part + moved
            diffs[column, k * cases : (k + 1) * cases, :] = moved - part

    def inside(x, _):
        value = combined(x * rows, rows)
        for y in range(rows):
            keep(value, y, x * nodes_y + y)
        return 0

    lax.fori_loop(0, planes, inside, 0)
    value = combined(count, planes + nodes_y)
    for x in range(planes):
        keep(value, x, x * nodes_y + rows)
    for y in range(nodes_y):
        keep(value, planes + y, planes * nodes_y + y)

    tiles = cases // 8

    def step(plane, _):
        for tile in range(tiles):
            lower = x_modes(sums, diffs, plane, 0, tile, cases, nodes_y)
            for row in range(rows):
                upper = x_modes(sums, diffs, plane, row + 1, tile, cases, nodes_y)
                part = mode_energy(modes_of(lower, upper))
                if tile == 0:
                    energy[row] = part
                else:
                    energy[row] += part
                lower = upper
        total = jnp.sum(energy[...], axis=1)
        total = (-3.0 / cases) * jnp.abs(codes[plane]) * total
        for index in range(out.shape[0]):
            out[index, plane] = total
        return 0

    lax.fori_loop(0, planes, step, 0)


def smooth(ref, x, rows):
    weight = [2.5 - math.sqrt(q) for q in range(7)]
    near = {}
    for dx in range(-2, 3):
        for dy in range(-2, 3):
            q = dx * dx + dy * dy
            if q <= 5:
                value = ref[x + 2 + dx, 2 + dy : 2 + dy + rows, :]
                near[q] = value if q not in near else near[q] + value
    result = None
    for dz in range(3):
        part = None
        for q, value in near.items():
            if q + dz * dz <= 6:
                term = weight[q + dz * dz] * value
                part = term if part is None else part + term
        if dz == 0:
            result = part
        else:
            place = lax.broadcasted_iota(jnp.int32, part.shape, 1)
            forward = jnp.where(place >= LANES - dz, 0.0, pltpu.roll(part, LANES - dz, 1))
            backward = jnp.where(place < dz, 0.0, pltpu.roll(part, dz, 1))
            result = result + (forward + backward)
    return result


def scale_kernel(sizes, counts, start, levels, out, there):
    planes, rows, _ = sizes
    y = lax.broadcasted_iota(jnp.int32, (rows + 4, LANES), 0) + (start[1] - 2)
    in_y = (y >= 0) & (y < counts[1] * rows)
    for x in range(planes + 4):
        global_x = start[0] + (x - 2)
        in_x = (global_x >= 0) & (global_x < counts[0] * planes)
        there[x] = jnp.where(in_y & in_x, 1.0, 0.0)
    for x in range(planes):
        density = 0.3 + 0.7 * levels[x].astype(f32) / (LEVELS - 1)
        out[x] = 1.0 / (density * smooth(there, x, rows))


def filter_kernel(sizes, counts, start, blocks, scale, out, wide):
    planes, rows, _ = sizes
    sides_x = ((-1, planes - 2, planes, 0), (0, 0, planes, 2), (1, 0, 2, 2 + planes))
    sides_y = ((-1, rows - 2, rows, 0), (0, 0, rows, 2), (1, 0, 2, 2 + rows))
    for step_x, x0, x1, to_x in sides_x:
        for step_y, y0, y1, to_y in sides_y:
            at_x = start[0] // planes + step_x
            at_y = start[1] // rows + step_y
            inside = (at_x >= 0) & (at_x < counts[0]) & (at_y >= 0) & (at_y < counts[1])
            index = jnp.where(inside, at_x * counts[1] + at_y, 0)
            value = blocks[index, x0:x1, y0:y1, :]
            wide[to_x : to_x + x1 - x0, to_y : to_y + y1 - y0, :] = jnp.where(inside, value, 0.0)
    for x in range(planes):
        out[x] = smooth(wide, x, rows) * scale[x]


def local(forces, levels, supports):
    _, cases, planes, rows, _ = forces.shape
    sizes = (planes, rows, cases)
    block = 3 * cases
    count_x, count_y = lax.axis_size("gx"), lax.axis_size("gy")

    def shape(blocks, codes):
        return jax.ShapeDtypeStruct((blocks * block + up8(codes), LANES), f32)

    density = 0.3 + 0.7 * levels.astype(f32) / (LEVELS - 1)
    codes = density * density * density
    codes = jnp.where(supports == 0, codes, -codes)
    whole = shape(planes * rows, planes * rows)
    down = [] if planes == 2 else [shape(2 * rows, 2 * rows)]
    own, up, *down = pl.pallas_call(
        functools.partial(pack_kernel, sizes),
        out_shape=[whole, shape(rows, 2 * rows), *down],
        in_specs=[VMEM] * 2,
        out_specs=[VMEM] * (2 + len(down)),
        compiler_params=PARAMS,
        name="pack",
    )(forces, codes)

    start = jnp.stack([lax.axis_index("gx") * planes, lax.axis_index("gy") * rows])
    start = start.astype(jnp.int32)
    counts = (count_x, count_y)
    scalars = pl.BlockSpec(memory_space=pltpu.SMEM)
    scale = pl.pallas_call(
        functools.partial(scale_kernel, sizes, counts),
        out_shape=jax.ShapeDtypeStruct((planes, rows, LANES), f32),
        in_specs=[scalars, VMEM],
        out_specs=VMEM,
        scratch_shapes=[pltpu.VMEM((planes + 4, rows + 4, LANES), f32)],
        compiler_params=PARAMS,
        name="scale",
    )(start, levels)

    def moved(value, axis, step):
        count = lax.axis_size(axis)
        pairs = [(i, i + step) for i in range(count) if 0 <= i + step < count]
        return lax.ppermute(value, axis, pairs)

    def links(first, step):
        return [(i, i + step) for i in range(first, count_x, 2) if 0 <= i + step < count_x]

    upper = lax.ppermute(down[0] if down else own, "gx", links(2, -1))
    lower = lax.ppermute(up, "gx", links(1, 1))
    pair = lax.ppermute(own, "gx", links(0, 1) + links(1, -1))
    ym, yp = pl.pallas_call(
        functools.partial(edge_kernel, sizes),
        out_shape=[
            shape(2 * (planes + 3), 2 * (planes + 4)), shape(planes + 3, 2 * (planes + 4))
        ],
        in_specs=[scalars] + [VMEM] * 4,
        out_specs=[VMEM] * 2,
        compiler_params=PARAMS,
        name="edges",
    )(start, own, pair, lower, upper)
    from_yp, from_ym = moved(ym, "gy", -1), moved(yp, "gy", 1)

    devices = count_x * count_y
    nodes = (planes + 1) * (rows + 1)
    wide = (planes + 3) * (rows + 3)
    acc = pltpu.VMEM(((planes + 3) * (rows + 1), block, LANES), f32)
    field = pltpu.VMEM((nodes, block, LANES), f32)
    both, system = pl.pallas_call(
        functools.partial(main_kernel, sizes),
        out_shape=[
            jax.ShapeDtypeStruct((4 * cases, nodes * 3 * LANES), bf16),
            jax.ShapeDtypeStruct((devices, cases // 8, 4, LANES), f32),
        ],
        in_specs=[scalars] + [VMEM] * 6,
        out_specs=[VMEM] * 2,
        scratch_shapes=[
            pltpu.VMEM((planes + 4, up8(rows + 4), LANES), f32),
            pltpu.VMEM((planes + 3, up8(rows + 3), LANES), f32),
            pltpu.VMEM((wide, block, LANES), f32),
            pltpu.VMEM((wide, block, LANES), f32),
            pltpu.VMEM((wide, block, LANES), f32),
            acc, acc, field, field, field, field,
            pltpu.VMEM((6 * cases, nodes * 3 * LANES), bf16),
            pltpu.VMEM((cases, LANES), f32),
        ],
        compiler_params=PARAMS,
        name="operator",
    )(start, own, pair, lower, upper, from_ym, from_yp)

    def gathered(copies):
        return lax.all_to_all(copies, ("gx", "gy"), 0, 0)

    system = gathered(system)

    weighted = pl.pallas_call(
        functools.partial(solve_kernel, sizes),
        out_shape=jax.ShapeDtypeStruct((devices, planes, rows, LANES), f32),
        in_specs=[VMEM] * 3,
        out_specs=VMEM,
        scratch_shapes=[
            pltpu.VMEM((2 * cases, LANES), f32),
            field,
            field,
            pltpu.VMEM((rows, 8, LANES), f32),
            pltpu.VMEM((LANES, LANES), f32),
            pltpu.VMEM((3 * cases, LANES), f32),
        ],
        compiler_params=PARAMS,
        name="solve",
    )(system, both, codes)

    blocks = gathered(weighted)
    return pl.pallas_call(
        functools.partial(filter_kernel, sizes, counts),
        out_shape=jax.ShapeDtypeStruct((planes, rows, LANES), f32),
        in_specs=[scalars] + [VMEM] * 2,
        out_specs=VMEM,
        scratch_shapes=[pltpu.VMEM((planes + 4, rows + 4, LANES), f32)],
        compiler_params=PARAMS,
        name="cone",
    )(start, blocks, scale)


def solution(mesh):
    return jax.shard_map(
        local,
        mesh=mesh,
        in_specs=(P(None, None, "gx", "gy", None), P("gx", "gy", None), P("gx", "gy", None)),
        out_specs=P("gx", "gy", None),
        check_vma=False,
    )
```

```python
import functools
import math

import jax
import jax.numpy as jnp
from jax import lax
from jax.experimental import pallas as pl
from jax.experimental.pallas import tpu as pltpu
from jax.sharding import PartitionSpec as P

LEVELS = 16
LOAD = 0.2
LANES = 128
POISSON = 0.3
LAME = POISSON / ((1.0 + POISSON) * (1.0 - 2.0 * POISSON))
SHEAR = 1.0 / (2.0 * (1.0 + POISSON))
DIAGONAL = (LAME + 2.0 * SHEAR) / 9.0 + 2.0 * SHEAR / 9.0
VMEM = pl.BlockSpec(memory_space=pltpu.VMEM)
PARAMS = pltpu.CompilerParams(vmem_limit_bytes=30 * 2**20)
f32 = jnp.float32
bf16 = jnp.bfloat16


def up8(count):
    return -(-count // 8) * 8


def shift_down(value):
    lane = lax.broadcasted_iota(jnp.int32, value.shape, value.ndim - 1)
    rolled = pltpu.roll(value, LANES - 1, value.ndim - 1)
    return jnp.where(lane == LANES - 1, 0.0, rolled)


def shift_up(value):
    lane = lax.broadcasted_iota(jnp.int32, value.shape, value.ndim - 1)
    return jnp.where(lane == 0, 0.0, pltpu.roll(value, 1, value.ndim - 1))


def unrolled(count, factor, body):
    def turn(step, _):
        for offset in range(factor):
            body(step * factor + offset)
        return 0

    turns = count // factor
    if turns:
        lax.fori_loop(0, turns, turn, 0)
    for index in range(turns * factor, count):
        body(index)


def split(value):
    high = value.astype(bf16)
    return high, (value - high.astype(f32)).astype(bf16)


def modes_of(lower, upper):
    out = [[[[None] * 3 for _ in range(2)] for _ in range(2)] for _ in range(2)]
    for a in range(2):
        for c in range(2):
            for k in range(3):
                if a or c:
                    out[a][0][c][k] = lower[a][c][k] + upper[a][c][k]
                out[a][1][c][k] = upper[a][c][k] - lower[a][c][k]
    return out


PAIRS = (((1, 1, 0, 0), (0, 1, 1, 2)), ((1, 0, 1, 0), (0, 1, 1, 1)), ((1, 1, 0, 1), (1, 0, 1, 2)))
TRIPLE = ((0, 1, 1, 0), (1, 0, 1, 1), (1, 1, 0, 2))
SHEARS = (((0, 1, 0, 0), (1, 0, 0, 1)), ((0, 0, 1, 0), (1, 0, 0, 2)), ((0, 0, 1, 1), (0, 1, 0, 2)))
AXIAL = ((1, 0, 0, 0), (0, 1, 0, 1), (0, 0, 1, 2))


def at(modes, place):
    a, b, c, k = place
    return modes[a][b][c][k]


def mode_forces(modes, stiff):
    out = [[[[None] * 3 for _ in range(2)] for _ in range(2)] for _ in range(2)]

    def put(place, value):
        a, b, c, k = place
        out[a][b][c][k] = value

    shear = stiff * (SHEAR / 16)
    for first, second in SHEARS:
        force = shear * (at(modes, first) + at(modes, second))
        put(first, force)
        put(second, force)
    one, two, three = (at(modes, place) for place in AXIAL)
    volume = (stiff * (LAME / 16)) * (one + two + three)
    axial = stiff * (SHEAR / 8)
    for place in AXIAL:
        put(place, volume + axial * at(modes, place))
    own, cross = stiff * ((LAME + 3 * SHEAR) / 48), stiff * (LAME / 48)
    for first, second in PAIRS:
        one, two = at(modes, first), at(modes, second)
        put(first, own * one + cross * two)
        put(second, own * two + cross * one)
    twist = stiff * (SHEAR / 48)
    one, two, three = (at(modes, place) for place in TRIPLE)
    total = one + two + three
    for place in TRIPLE:
        put(place, twist * (total + at(modes, place)))
    last = stiff * ((LAME + 4 * SHEAR) / 144)
    for k in range(3):
        put((1, 1, 1, k), last * modes[1][1][1][k])
    return out


def mode_energy(modes):
    def square(value):
        return value * value

    shear = None
    for first, second in SHEARS:
        term = square(at(modes, first) + at(modes, second))
        shear = term if shear is None else shear + term
    one, two, three = (at(modes, place) for place in AXIAL)
    energy = (SHEAR / 16) * shear + (LAME / 16) * square(one + two + three)
    energy = energy + (SHEAR / 8) * (square(one) + square(two) + square(three))
    squares, products = None, None
    for first, second in PAIRS:
        one, two = at(modes, first), at(modes, second)
        term, product = square(one) + square(two), one * two
        squares = term if squares is None else squares + term
        products = product if products is None else products + product
    energy = energy + ((LAME + 3 * SHEAR) / 48) * squares + (LAME / 24) * products
    one, two, three = (at(modes, place) for place in TRIPLE)
    twist = square(one + two + three) + square(one) + square(two) + square(three)
    energy = energy + (SHEAR / 48) * twist
    last = square(modes[1][1][1][0]) + square(modes[1][1][1][1]) + square(modes[1][1][1][2])
    return energy + ((LAME + 4 * SHEAR) / 144) * last


def x_modes(sums, diffs, plane, row, tile, cases, columns):
    out = [[[None] * 3 for _ in range(2)] for _ in range(2)]
    for c, ref in enumerate((sums, diffs)):
        for k in range(3):
            rows = pl.ds(pl.multiple_of(k * cases + tile * 8, 8), 8)
            one = ref[plane * columns + row, rows, :]
            two = ref[(plane + 1) * columns + row, rows, :]
            out[0][c][k] = one + two
            out[1][c][k] = two - one
    return out


def apply_elements(
    sums, diffs, stiff_ref, acc_s, acc_d, planes, rows, skip, stiff_x, stiff_y, cases
):
    columns = rows + 1
    acc_columns = columns - 2 * skip
    tiles = cases // 8

    def step(index, _):
        plane, tile = index // tiles, index % tiles

        def emit(row, total):
            if not skip <= row < columns - skip:
                return
            for c, acc in enumerate((acc_s, acc_d)):
                for k in range(3):
                    lines = pl.ds(pl.multiple_of(k * cases + tile * 8, 8), 8)
                    low = plane * acc_columns + row - skip
                    acc[low, lines, :] += total[0][c][k] - total[1][c][k]
                    acc[low + acc_columns, lines, :] = total[0][c][k] + total[1][c][k]

        lower = x_modes(sums, diffs, plane, 0, tile, cases, columns)
        carry = None
        for row in range(rows):
            upper = x_modes(sums, diffs, plane, row + 1, tile, cases, columns)
            stiff = jnp.broadcast_to(
                stiff_ref[plane + stiff_x, pl.ds(row + stiff_y, 1), :], (8, LANES)
            )
            forces = mode_forces(modes_of(lower, upper), stiff)
            here = [[[None] * 3 for _ in range(2)] for _ in range(2)]
            following = [[[None] * 3 for _ in range(2)] for _ in range(2)]
            for a in range(2):
                for c in range(2):
                    for k in range(3):
                        one, two = forces[a][0][c][k], forces[a][1][c][k]
                        low = -two if one is None else one - two
                        high = two if one is None else one + two
                        here[a][c][k] = low if carry is None else carry[a][c][k] + low
                        following[a][c][k] = high
            emit(row, here)
            carry, lower = following, upper
        emit(rows, carry)
        return 0

    lax.fori_loop(0, planes * tiles, step, 0)


def edge_rows(rows):
    return (0, 1, rows - 1)


def inner_rows(rows):
    return tuple(range(2, rows - 1))


def pack_kernel(sizes, forces, codes, own, up_e, up_i, down_e, down_i, ym, yp):
    planes, rows, cases = sizes
    block = 3 * cases
    base = planes * rows * block
    for x in range(planes):
        own[base + x * rows : base + (x + 1) * rows, :] = codes[x]
        scale = jnp.where(codes[x] > 0.0, LOAD, 0.0)
        for k in range(3):
            for c in range(cases):
                start = x * rows * block + k * cases + c
                own[pl.ds(start, rows, stride=block), :] = forces[k, c, x] * scale

    def fill(ref, xs, ys, code_xs, code_ys):
        line = 0
        for x in xs:
            for y in ys:
                start = (x * rows + y) * block
                ref[line : line + block, :] = own[start : start + block, :]
                line += block
        for x in code_xs:
            start = base + x * rows + (code_ys[0] if code_ys else 0)
            ref[line : line + len(code_ys), :] = own[start : start + len(code_ys), :]
            line += len(code_ys)
        if line < ref.shape[0]:
            ref[line:, :] = jnp.zeros((ref.shape[0] - line, LANES), f32)

    every_x, every_y = range(planes), range(rows)
    first, last = (0, 1), (planes - 2, planes - 1)
    fill(up_e, last[1:], edge_rows(rows), last, every_y)
    fill(up_i, last[1:], inner_rows(rows), (), ())
    fill(down_e, first, edge_rows(rows), first, every_y)
    fill(down_i, first, inner_rows(rows), (), ())
    fill(ym, every_x, (0, 1), every_x, (0, 1))
    fill(yp, every_x, (rows - 1,), every_x, (rows - 2, rows - 1))


def corner_kernel(sizes, start, lower_e, upper_e, ym, yp):
    planes, rows, cases = sizes
    block = 3 * cases
    even = start[0] // planes % 2 == 0
    for ref, edges, code in ((ym, (0, 1), 0), (yp, (2,), rows - 2)):
        line = 0
        for slot in range(2):
            for edge in edges:
                above = upper_e[(slot * 3 + edge) * block : (slot * 3 + edge + 1) * block, :]
                below = lower_e[edge * block : (edge + 1) * block, :] if slot == 1 else 0.0
                ref[line : line + block, :] = jnp.where(even, below, above)
                line += block
        for slot in range(2):
            at = slot * rows + code
            above = upper_e[6 * block + at : 6 * block + at + 2, :]
            below = lower_e[3 * block + at : 3 * block + at + 2, :]
            ref[line : line + 2, :] = jnp.where(even, below, above)
            line += 2
        if line < ref.shape[0]:
            ref[line:, :] = jnp.zeros((ref.shape[0] - line, LANES), f32)


def readers(sizes, first, own, pair, lower, upper, y_own, y_pair, y_corner):
    planes, rows, cases = sizes
    block = 3 * cases
    even = first // planes % 2 == 0

    def lines(ref, start, count):
        return ref[start : start + count, :]

    def inside(ref, x, y):
        return lines(ref, (x * rows + y) * block, block)

    def split_rows(refs, slot, y):
        edges, inner = edge_rows(rows), inner_rows(rows)
        ref, place = (refs[0], edges) if y in edges else (refs[1], inner)
        return lines(ref, (slot * len(place) + place.index(y)) * block, block)

    def beyond(refs, slot, y):
        below, above = refs
        if y < 0:
            return lines(below, slot * block, block)
        return lines(above, (slot * 2 + y - rows) * block, block)

    def load(x, y):
        in_y = 0 <= y < rows
        if 0 <= x < planes:
            return inside(own, x, y) if in_y else beyond(y_own, x, y)
        if x < 0:
            if in_y:
                return jnp.where(even, split_rows(lower, 0, y), inside(pair, planes - 1, y))
            return jnp.where(even, beyond(y_corner, 1, y), beyond(y_pair, planes - 1, y))
        if in_y:
            return jnp.where(even, inside(pair, x - planes, y), split_rows(upper, x - planes, y))
        return jnp.where(even, beyond(y_pair, x - planes, y), beyond(y_corner, x - planes, y))

    def inside_codes(ref, x):
        return lines(ref, planes * rows * block + x * rows, rows)

    def beyond_codes(refs, slots, slot, y):
        below, above = refs
        if y < 0:
            return lines(below, slots * block + slot * 2, 2)
        return lines(above, slots * 2 * block + slot * 2, 2)

    def codes(x, y):
        if 0 <= x < planes:
            return inside_codes(own, x) if y == 0 else beyond_codes(y_own, planes, x, y)
        if x < 0:
            slot = x + 2
            if y == 0:
                other = inside_codes(pair, planes + x)
                return jnp.where(even, lines(lower[0], 3 * block + slot * rows, rows), other)
            other = beyond_codes(y_pair, planes, planes + x, y)
            return jnp.where(even, beyond_codes(y_corner, 2, slot, y), other)
        slot = x - planes
        if y == 0:
            other = lines(upper[0], 6 * block + slot * rows, rows)
            return jnp.where(even, inside_codes(pair, slot), other)
        other = beyond_codes(y_corner, 2, slot, y)
        return jnp.where(even, beyond_codes(y_pair, planes, slot, y), other)

    return load, codes


def main_kernel(
    sizes, first, own, pair, lower_e, lower_i, upper_e, upper_i, ym, yp, ym_pair, yp_pair,
    ym_corner, yp_corner, both_out, system_out, stiff_ref, inverse,
    start, sums, diffs, acc_s, acc_d, w_sums, w_diffs, acc2_s, acc2_d, right, table,
):
    planes, rows, cases = sizes
    block = 3 * cases
    xs, ys = planes + 3, rows + 3
    load, signed = readers(
        sizes, first[0], own, pair, (lower_e, lower_i), (upper_e, upper_i),
        (ym, yp), (ym_pair, yp_pair), (ym_corner, yp_corner),
    )
    for x in range(-2, planes + 2):
        for y, count in ((-2, 2), (0, rows), (rows, 2)):
            stiff_ref[x + 2, y + 2 : y + 2 + count, :] = signed(x, y)
    for x in range(-1, planes + 2):
        codes = stiff_ref[x + 2, 0 : ys + 1, :]
        total = jnp.abs(stiff_ref[x + 1, 0 : ys + 1, :]) + jnp.abs(codes)
        total = total[:-1] + total[1:]
        total = total + shift_up(total)
        free = codes[1:] > 0.0
        value = 1.0 / (DIAGONAL * jnp.where(free, total, 1.0))
        inverse[x + 1, 0:ys, :] = jnp.where(free, value, 0.0)
    for x in range(planes + 4):
        stiff_ref[x] = jnp.abs(stiff_ref[x])

    for x in range(-1, planes + 2):
        for y in range(-1, rows + 2):
            value = load(x, y) * inverse[x + 1, y + 1 : y + 2, :]
            column = (x + 1) * ys + y + 1
            start[column] = value
            moved = shift_down(value)
            sums[column] = value + moved
            diffs[column] = moved - value

    nodes_y = rows + 1
    apply_elements(
        sums, diffs, stiff_ref, acc_s, acc_d, planes + 2, rows + 2, 1, 1, 1, cases
    )

    def image(x, y, place):
        column = (x + 1) * nodes_y + y
        s, d = acc_s[column], acc_d[column]
        force = s - d + shift_up(s + d)
        scaled = force * inverse[x + 1, pl.ds(y + 1, 1), :]
        moved = shift_down(scaled)
        w_sums[x * nodes_y + y] = scaled + moved
        w_diffs[x * nodes_y + y] = moved - scaled
        value = start[(x + 1) * ys + y + 1]
        for k in range(3):
            lines = slice(k * cases, (k + 1) * cases)
            pair = jnp.concatenate([value[lines], scaled[lines]], 0)
            lane = pl.ds(pl.multiple_of((place * 3 + k) * LANES, LANES), LANES)
            high, rest = split(pair)
            both_out[0 : 2 * cases, lane] = high
            both_out[2 * cases : 4 * cases, lane] = rest
        return force

    two = 2 * cases
    count = planes * rows

    def inside(index):
        force = image(index // rows, index % rows, index)
        given = own[pl.ds(pl.multiple_of(index * block, 8), block), :]
        for k in range(3):
            lines = slice(k * cases, (k + 1) * cases)
            pair = jnp.concatenate([given[lines], force[lines]], 0)
            lane = pl.ds(pl.multiple_of((index * 3 + k) * LANES, LANES), LANES)
            high, rest = split(pair)
            right[0:two, lane] = high
            right[two : 2 * two, lane] = rest

    unrolled(count, 4, inside)
    unrolled(planes, 2, lambda x: image(x, rows, count + x))
    unrolled(nodes_y, 3, lambda y: image(planes, y, count + planes + y))
    beyond = right.shape[1] - count * 3 * LANES
    right[0 : 2 * two, count * 3 * LANES :] = jnp.zeros((2 * two, beyond), bf16)

    for column in range(nodes_y):
        acc2_s[column] = jnp.zeros((block, LANES), f32)
        acc2_d[column] = jnp.zeros((block, LANES), f32)
    apply_elements(w_sums, w_diffs, stiff_ref, acc2_s, acc2_d, planes, rows, 0, 2, 2, cases)

    def second_force(x, y, place):
        column = x * nodes_y + y
        s, d = acc2_s[column], acc2_d[column]
        force = s - d + shift_up(s + d)
        for k in range(3):
            value = force[k * cases : (k + 1) * cases]
            high = value.astype(bf16).astype(f32)
            lane = pl.ds(pl.multiple_of((place * 3 + k) * LANES, LANES), LANES)
            right[2 * two :, lane] = jnp.concatenate([high, value - high], 0).astype(bf16)

    unrolled(count, 4, lambda index: second_force(index // rows, index % rows, index))
    unrolled(planes, 2, lambda x: second_force(x, rows, count + x))
    unrolled(nodes_y, 3, lambda y: second_force(planes, y, count + planes + y))

    contract = (((1,), (1,)), ((), ()))
    product = lax.dot_general(both_out[...], right[...], contract, preferred_element_type=f32)
    product = product[:two] + product[two:]
    gram = product[:, :two] + product[:, two : 2 * two]
    other = product[:, 2 * two : 2 * two + cases] + product[:, 2 * two + cases :]
    row = lax.broadcasted_iota(jnp.int32, (cases, cases), 0)
    column = lax.broadcasted_iota(jnp.int32, (cases, cases), 1)
    load_load, load_image = gram[:cases, :cases], gram[:cases, cases:]
    mixed, image_image = other[:cases], other[cases:]
    table[...] = jnp.zeros(table.shape, f32)
    table[:, 0:cases] = jnp.where(row <= column, load_load, load_image)
    table[:, cases:two] = jnp.where(row <= column, mixed, image_image)
    for lane, value in ((two, load_image), (two + 1, image_image)):
        own_entries = jnp.where(row == column, value, 0.0)
        table[:, lane : lane + 1] = jnp.sum(own_entries, axis=1, keepdims=True)
    half = cases // 2
    folded = table[:half, :] + pltpu.roll(table[half:, :], LANES // 2, 1)
    depth = system_out.shape[2]
    for index in range(system_out.shape[0]):
        for part in range(half // depth):
            system_out[index, part] = folded[part * depth : (part + 1) * depth]


def solve_kernel(
    sizes, system, both, codes, out, mixing, sums, diffs, energy, square, full
):
    planes, rows, cases = sizes
    two = 2 * cases
    nodes_y = rows + 1
    count = planes * rows
    total = jnp.sum(system[...], axis=0)
    half, depth = cases // 2, system.shape[2]
    square[...] = jnp.zeros(square.shape, f32)
    for part in range(half // depth):
        value = total[part]
        square[part * depth : (part + 1) * depth, :] = value
        lines = slice(half + part * depth, half + (part + 1) * depth)
        square[lines, :] = pltpu.roll(value, LANES // 2, 1)
    value, turned = square[0:cases, :], jnp.transpose(square[...])
    line = lax.broadcasted_iota(jnp.int32, (cases, cases), 0)
    place = lax.broadcasted_iota(jnp.int32, (cases, cases), 1)

    def mended(start, diagonal=None):
        kept, other = value[:, start : start + cases], turned[start : start + cases, :cases]
        if diagonal is None:
            return jnp.where(line <= place, kept, other)
        inner = jnp.where(line < place, other, value[:, diagonal : diagonal + 1])
        return jnp.where(line > place, kept, inner)

    load_image, mixed = mended(0, two), mended(cases)
    parts = ((load_image, mixed), (mixed, mended(cases, two + 1)), (mended(0), load_image))
    full[...] = jnp.zeros(full.shape, f32)
    for index, (left, right) in enumerate(parts):
        full[index * cases : (index + 1) * cases, 0:cases] = left
        full[index * cases : (index + 1) * cases, cases:two] = right
    table = full[...]
    lane = lax.broadcasted_iota(jnp.int32, (1, LANES), 1)
    gone, wide = 0, 4
    for pivot in range(0, two, wide):
        drop = pivot // 8 * 8 - gone
        table = table[drop:]
        gone += drop
        line = pivot - gone
        inner = (lane >= pivot) & (lane < pivot + wide)
        found = [table[line + p : line + p + 1, :] for p in range(wide)]
        block = [
            [jnp.broadcast_to(row[:, pivot + q : pivot + q + 1], row.shape) for q in range(wide)]
            for row in found
        ]
        solved = [
            jnp.where(lane == pivot + p, -1.0, jnp.where(inner, 0.0, found[p]))
            for p in range(wide)
        ]
        for p in range(wide):
            inverse = 1.0 / block[p][p]
            solved[p] = solved[p] * inverse
            block[p] = [value * inverse for value in block[p]]
            for q in range(wide):
                if q != p:
                    factor = block[q][p]
                    solved[q] = solved[q] - factor * solved[p]
                    for r in range(p + 1, wide):
                        block[q][r] = block[q][r] - factor * block[p][r]
        update = None
        for q in range(wide):
            term = table[:, pivot + q : pivot + q + 1] * solved[q]
            update = term if update is None else update + term
        table = jnp.where(inner, 0.0, table) - update
    answer = table[two - gone :, :two]
    high = answer.astype(bf16).astype(f32)
    mixing[...] = jnp.zeros(mixing.shape, f32)
    mixing[0:cases, 0:two] = high
    mixing[0:cases, two : 2 * two] = high
    mixing[cases:two, 0:two] = answer - high
    mix = mixing[...][:, : 2 * two].astype(bf16)

    def combined(place, width):
        lanes = pl.ds(pl.multiple_of(place * 3 * LANES, LANES), width * 3 * LANES)
        value = jnp.dot(mix, both[:, lanes], preferred_element_type=f32)
        return value[:cases] + value[cases:]

    def keep(value, index, column):
        for k in range(3):
            part = value[:, (index * 3 + k) * LANES : (index * 3 + k + 1) * LANES]
            moved = shift_down(part)
            sums[column, k * cases : (k + 1) * cases, :] = part + moved
            diffs[column, k * cases : (k + 1) * cases, :] = moved - part

    def inside(x, _):
        value = combined(x * rows, rows)
        for y in range(rows):
            keep(value, y, x * nodes_y + y)
        return 0

    lax.fori_loop(0, planes, inside, 0)
    value = combined(count, planes + nodes_y)
    for x in range(planes):
        keep(value, x, x * nodes_y + rows)
    for y in range(nodes_y):
        keep(value, planes + y, planes * nodes_y + y)

    tiles = cases // 8

    def step(plane, _):
        for tile in range(tiles):
            lower = x_modes(sums, diffs, plane, 0, tile, cases, nodes_y)
            for row in range(rows):
                upper = x_modes(sums, diffs, plane, row + 1, tile, cases, nodes_y)
                part = mode_energy(modes_of(lower, upper))
                if tile == 0:
                    energy[row] = part
                else:
                    energy[row] += part
                lower = upper
        total = jnp.sum(energy[...], axis=1)
        total = (-3.0 / cases) * jnp.abs(codes[plane]) * total
        for index in range(out.shape[0]):
            out[index, plane] = total
        return 0

    lax.fori_loop(0, planes, step, 0)


def smooth(ref, x, rows):
    weight = [2.5 - math.sqrt(q) for q in range(7)]
    near = {}
    for dx in range(-2, 3):
        for dy in range(-2, 3):
            q = dx * dx + dy * dy
            if q <= 5:
                value = ref[x + 2 + dx, 2 + dy : 2 + dy + rows, :]
                near[q] = value if q not in near else near[q] + value
    result = None
    for dz in range(3):
        part = None
        for q, value in near.items():
            if q + dz * dz <= 6:
                term = weight[q + dz * dz] * value
                part = term if part is None else part + term
        if dz == 0:
            result = part
        else:
            place = lax.broadcasted_iota(jnp.int32, part.shape, 1)
            forward = jnp.where(place >= LANES - dz, 0.0, pltpu.roll(part, LANES - dz, 1))
            backward = jnp.where(place < dz, 0.0, pltpu.roll(part, dz, 1))
            result = result + (forward + backward)
    return result


def scale_kernel(sizes, counts, start, levels, out, there):
    planes, rows, _ = sizes
    y = lax.broadcasted_iota(jnp.int32, (rows + 4, LANES), 0) + (start[1] - 2)
    in_y = (y >= 0) & (y < counts[1] * rows)
    for x in range(planes + 4):
        global_x = start[0] + (x - 2)
        in_x = (global_x >= 0) & (global_x < counts[0] * planes)
        there[x] = jnp.where(in_y & in_x, 1.0, 0.0)
    for x in range(planes):
        density = 0.3 + 0.7 * levels[x].astype(f32) / (LEVELS - 1)
        out[x] = 1.0 / (density * smooth(there, x, rows))


def filter_kernel(sizes, counts, start, blocks, scale, out, wide):
    planes, rows, _ = sizes
    sides_x = ((-1, planes - 2, planes, 0), (0, 0, planes, 2), (1, 0, 2, 2 + planes))
    sides_y = ((-1, rows - 2, rows, 0), (0, 0, rows, 2), (1, 0, 2, 2 + rows))
    for step_x, x0, x1, to_x in sides_x:
        for step_y, y0, y1, to_y in sides_y:
            at_x = start[0] // planes + step_x
            at_y = start[1] // rows + step_y
            inside = (at_x >= 0) & (at_x < counts[0]) & (at_y >= 0) & (at_y < counts[1])
            index = jnp.where(inside, at_x * counts[1] + at_y, 0)
            value = blocks[index, x0:x1, y0:y1, :]
            wide[to_x : to_x + x1 - x0, to_y : to_y + y1 - y0, :] = jnp.where(inside, value, 0.0)
    for x in range(planes):
        out[x] = smooth(wide, x, rows) * scale[x]


def local(forces, levels, supports):
    _, cases, planes, rows, _ = forces.shape
    sizes = (planes, rows, cases)
    block = 3 * cases
    count_x, count_y = lax.axis_size("gx"), lax.axis_size("gy")

    def shape(blocks, codes):
        return jax.ShapeDtypeStruct((blocks * block + up8(codes), LANES), f32)

    density = 0.3 + 0.7 * levels.astype(f32) / (LEVELS - 1)
    codes = density * density * density
    codes = jnp.where(supports == 0, codes, -codes)
    edge, inner = len(edge_rows(rows)), len(inner_rows(rows))
    own, up_e, up_i, down_e, down_i, ym, yp = pl.pallas_call(
        functools.partial(pack_kernel, sizes),
        out_shape=[
            shape(planes * rows, planes * rows),
            shape(edge, 2 * rows),
            shape(inner, 0),
            shape(2 * edge, 2 * rows),
            shape(2 * inner, 0),
            shape(2 * planes, 2 * planes),
            shape(planes, 2 * planes),
        ],
        in_specs=[VMEM] * 2,
        out_specs=[VMEM] * 7,
        compiler_params=PARAMS,
        name="pack",
    )(forces, codes)

    start = jnp.stack([lax.axis_index("gx") * planes, lax.axis_index("gy") * rows])
    start = start.astype(jnp.int32)
    counts = (count_x, count_y)
    scalars = pl.BlockSpec(memory_space=pltpu.SMEM)
    scale = pl.pallas_call(
        functools.partial(scale_kernel, sizes, counts),
        out_shape=jax.ShapeDtypeStruct((planes, rows, LANES), f32),
        in_specs=[scalars, VMEM],
        out_specs=VMEM,
        scratch_shapes=[pltpu.VMEM((planes + 4, rows + 4, LANES), f32)],
        compiler_params=PARAMS,
        name="scale",
    )(start, levels)

    def moved(value, axis, step):
        count = lax.axis_size(axis)
        pairs = [(i, i + step) for i in range(count) if 0 <= i + step < count]
        return lax.ppermute(value, axis, pairs)

    def links(first, step):
        return [(i, i + step) for i in range(first, count_x, 2) if 0 <= i + step < count_x]

    def swapped(value):
        return lax.ppermute(value, "gx", links(0, 1) + links(1, -1))

    upper_e = lax.ppermute(down_e, "gx", links(2, -1))
    lower_e = lax.ppermute(up_e, "gx", links(1, 1))
    pair = swapped(own)
    from_yp, from_ym = moved(ym, "gy", -1), moved(yp, "gy", 1)
    upper_i = lax.ppermute(down_i, "gx", links(2, -1))
    lower_i = lax.ppermute(up_i, "gx", links(1, 1))
    corner_m, corner_p = pl.pallas_call(
        functools.partial(corner_kernel, sizes),
        out_shape=[shape(4, 4), shape(2, 4)],
        in_specs=[scalars] + [VMEM] * 2,
        out_specs=[VMEM] * 2,
        compiler_params=PARAMS,
        name="corners",
    )(start, lower_e, upper_e)
    corner_yp, corner_ym = moved(corner_m, "gy", -1), moved(corner_p, "gy", 1)
    pair_yp, pair_ym = swapped(from_yp), swapped(from_ym)

    devices = count_x * count_y
    nodes = (planes + 1) * (rows + 1)
    wide = (planes + 3) * (rows + 3)
    acc = pltpu.VMEM(((planes + 3) * (rows + 1), block, LANES), f32)
    field = pltpu.VMEM((nodes, block, LANES), f32)
    both, system = pl.pallas_call(
        functools.partial(main_kernel, sizes),
        out_shape=[
            jax.ShapeDtypeStruct((4 * cases, nodes * 3 * LANES), bf16),
            jax.ShapeDtypeStruct((devices, cases // 8, 4, LANES), f32),
        ],
        in_specs=[scalars] + [VMEM] * 12,
        out_specs=[VMEM] * 2,
        scratch_shapes=[
            pltpu.VMEM((planes + 4, up8(rows + 4), LANES), f32),
            pltpu.VMEM((planes + 3, up8(rows + 3), LANES), f32),
            pltpu.VMEM((wide, block, LANES), f32),
            pltpu.VMEM((wide, block, LANES), f32),
            pltpu.VMEM((wide, block, LANES), f32),
            acc, acc, field, field, field, field,
            pltpu.VMEM((6 * cases, nodes * 3 * LANES), bf16),
            pltpu.VMEM((cases, LANES), f32),
        ],
        compiler_params=PARAMS,
        name="operator",
    )(
        start, own, pair, lower_e, lower_i, upper_e, upper_i, from_ym, from_yp,
        pair_ym, pair_yp, corner_ym, corner_yp,
    )

    def gathered(copies):
        return lax.all_to_all(copies, ("gx", "gy"), 0, 0)

    system = gathered(system)

    weighted = pl.pallas_call(
        functools.partial(solve_kernel, sizes),
        out_shape=jax.ShapeDtypeStruct((devices, planes, rows, LANES), f32),
        in_specs=[VMEM] * 3,
        out_specs=VMEM,
        scratch_shapes=[
            pltpu.VMEM((2 * cases, LANES), f32),
            field,
            field,
            pltpu.VMEM((rows, 8, LANES), f32),
            pltpu.VMEM((LANES, LANES), f32),
            pltpu.VMEM((3 * cases, LANES), f32),
        ],
        compiler_params=PARAMS,
        name="solve",
    )(system, both, codes)

    blocks = gathered(weighted)
    return pl.pallas_call(
        functools.partial(filter_kernel, sizes, counts),
        out_shape=jax.ShapeDtypeStruct((planes, rows, LANES), f32),
        in_specs=[scalars] + [VMEM] * 2,
        out_specs=VMEM,
        scratch_shapes=[pltpu.VMEM((planes + 4, rows + 4, LANES), f32)],
        compiler_params=PARAMS,
        name="cone",
    )(start, blocks, scale)


def solution(mesh):
    return jax.shard_map(
        local,
        mesh=mesh,
        in_specs=(P(None, None, "gx", "gy", None), P("gx", "gy", None), P("gx", "gy", None)),
        out_specs=P("gx", "gy", None),
        check_vma=False,
    )
```

```python
import functools
import math

import jax
import jax.numpy as jnp
from jax import lax
from jax.experimental import pallas as pl
from jax.experimental.pallas import tpu as pltpu
from jax.sharding import PartitionSpec as P

LEVELS = 16
LOAD = 0.2
LANES = 128
POISSON = 0.3
LAME = POISSON / ((1.0 + POISSON) * (1.0 - 2.0 * POISSON))
SHEAR = 1.0 / (2.0 * (1.0 + POISSON))
DIAGONAL = (LAME + 2.0 * SHEAR) / 9.0 + 2.0 * SHEAR / 9.0
VMEM = pl.BlockSpec(memory_space=pltpu.VMEM)
PARAMS = pltpu.CompilerParams(vmem_limit_bytes=30 * 2**20)
f32 = jnp.float32
bf16 = jnp.bfloat16


def up8(count):
    return -(-count // 8) * 8


def shift_down(value):
    lane = lax.broadcasted_iota(jnp.int32, value.shape, value.ndim - 1)
    rolled = pltpu.roll(value, LANES - 1, value.ndim - 1)
    return jnp.where(lane == LANES - 1, 0.0, rolled)


def shift_up(value):
    lane = lax.broadcasted_iota(jnp.int32, value.shape, value.ndim - 1)
    return jnp.where(lane == 0, 0.0, pltpu.roll(value, 1, value.ndim - 1))


def unrolled(count, factor, body):
    def turn(step, _):
        for offset in range(factor):
            body(step * factor + offset)
        return 0

    turns = count // factor
    if turns:
        lax.fori_loop(0, turns, turn, 0)
    for index in range(turns * factor, count):
        body(index)


def split(value):
    high = value.astype(bf16)
    return high, (value - high.astype(f32)).astype(bf16)


def modes_of(lower, upper):
    out = [[[[None] * 3 for _ in range(2)] for _ in range(2)] for _ in range(2)]
    for a in range(2):
        for c in range(2):
            for k in range(3):
                if a or c:
                    out[a][0][c][k] = lower[a][c][k] + upper[a][c][k]
                out[a][1][c][k] = upper[a][c][k] - lower[a][c][k]
    return out


PAIRS = (((1, 1, 0, 0), (0, 1, 1, 2)), ((1, 0, 1, 0), (0, 1, 1, 1)), ((1, 1, 0, 1), (1, 0, 1, 2)))
TRIPLE = ((0, 1, 1, 0), (1, 0, 1, 1), (1, 1, 0, 2))
SHEARS = (((0, 1, 0, 0), (1, 0, 0, 1)), ((0, 0, 1, 0), (1, 0, 0, 2)), ((0, 0, 1, 1), (0, 1, 0, 2)))
AXIAL = ((1, 0, 0, 0), (0, 1, 0, 1), (0, 0, 1, 2))


def at(modes, place):
    a, b, c, k = place
    return modes[a][b][c][k]


def mode_forces(modes, stiff):
    out = [[[[None] * 3 for _ in range(2)] for _ in range(2)] for _ in range(2)]

    def put(place, value):
        a, b, c, k = place
        out[a][b][c][k] = value

    shear = stiff * (SHEAR / 16)
    for first, second in SHEARS:
        force = shear * (at(modes, first) + at(modes, second))
        put(first, force)
        put(second, force)
    one, two, three = (at(modes, place) for place in AXIAL)
    volume = (stiff * (LAME / 16)) * (one + two + three)
    axial = stiff * (SHEAR / 8)
    for place in AXIAL:
        put(place, volume + axial * at(modes, place))
    own, cross = stiff * ((LAME + 3 * SHEAR) / 48), stiff * (LAME / 48)
    for first, second in PAIRS:
        one, two = at(modes, first), at(modes, second)
        put(first, own * one + cross * two)
        put(second, own * two + cross * one)
    twist = stiff * (SHEAR / 48)
    one, two, three = (at(modes, place) for place in TRIPLE)
    total = one + two + three
    for place in TRIPLE:
        put(place, twist * (total + at(modes, place)))
    last = stiff * ((LAME + 4 * SHEAR) / 144)
    for k in range(3):
        put((1, 1, 1, k), last * modes[1][1][1][k])
    return out


def mode_energy(modes):
    def square(value):
        return value * value

    shear = None
    for first, second in SHEARS:
        term = square(at(modes, first) + at(modes, second))
        shear = term if shear is None else shear + term
    one, two, three = (at(modes, place) for place in AXIAL)
    energy = (SHEAR / 16) * shear + (LAME / 16) * square(one + two + three)
    energy = energy + (SHEAR / 8) * (square(one) + square(two) + square(three))
    squares, products = None, None
    for first, second in PAIRS:
        one, two = at(modes, first), at(modes, second)
        term, product = square(one) + square(two), one * two
        squares = term if squares is None else squares + term
        products = product if products is None else products + product
    energy = energy + ((LAME + 3 * SHEAR) / 48) * squares + (LAME / 24) * products
    one, two, three = (at(modes, place) for place in TRIPLE)
    twist = square(one + two + three) + square(one) + square(two) + square(three)
    energy = energy + (SHEAR / 48) * twist
    last = square(modes[1][1][1][0]) + square(modes[1][1][1][1]) + square(modes[1][1][1][2])
    return energy + ((LAME + 4 * SHEAR) / 144) * last


def x_modes(sums, diffs, plane, row, tile, cases, columns):
    out = [[[None] * 3 for _ in range(2)] for _ in range(2)]
    for c, ref in enumerate((sums, diffs)):
        for k in range(3):
            rows = pl.ds(pl.multiple_of(k * cases + tile * 8, 8), 8)
            one = ref[plane * columns + row, rows, :]
            two = ref[(plane + 1) * columns + row, rows, :]
            out[0][c][k] = one + two
            out[1][c][k] = two - one
    return out


def apply_elements(
    sums, diffs, stiff_ref, acc_s, acc_d, planes, rows, skip, stiff_x, stiff_y, cases
):
    columns = rows + 1
    acc_columns = columns - 2 * skip
    tiles = cases // 8

    def step(index, _):
        plane, tile = index // tiles, index % tiles

        def emit(row, total):
            if not skip <= row < columns - skip:
                return
            for c, acc in enumerate((acc_s, acc_d)):
                for k in range(3):
                    lines = pl.ds(pl.multiple_of(k * cases + tile * 8, 8), 8)
                    low = plane * acc_columns + row - skip
                    acc[low, lines, :] += total[0][c][k] - total[1][c][k]
                    acc[low + acc_columns, lines, :] = total[0][c][k] + total[1][c][k]

        lower = x_modes(sums, diffs, plane, 0, tile, cases, columns)
        carry = None
        for row in range(rows):
            upper = x_modes(sums, diffs, plane, row + 1, tile, cases, columns)
            stiff = jnp.broadcast_to(
                stiff_ref[plane + stiff_x, pl.ds(row + stiff_y, 1), :], (8, LANES)
            )
            forces = mode_forces(modes_of(lower, upper), stiff)
            here = [[[None] * 3 for _ in range(2)] for _ in range(2)]
            following = [[[None] * 3 for _ in range(2)] for _ in range(2)]
            for a in range(2):
                for c in range(2):
                    for k in range(3):
                        one, two = forces[a][0][c][k], forces[a][1][c][k]
                        low = -two if one is None else one - two
                        high = two if one is None else one + two
                        here[a][c][k] = low if carry is None else carry[a][c][k] + low
                        following[a][c][k] = high
            emit(row, here)
            carry, lower = following, upper
        emit(rows, carry)
        return 0

    lax.fori_loop(0, planes * tiles, step, 0)


def fill(source, base, sizes, ref, xs, ys, code_xs, code_ys):
    planes, rows, cases = sizes
    block = 3 * cases
    line = 0
    for x in xs:
        start = (x * rows + ys[0]) * block
        count = len(ys) * block
        ref[line : line + count, :] = source[start : start + count, :]
        line += count
    for x in code_xs:
        start = base + x * rows + code_ys[0]
        ref[line : line + len(code_ys), :] = source[start : start + len(code_ys), :]
        line += len(code_ys)
    if line < ref.shape[0]:
        ref[line:, :] = jnp.zeros((ref.shape[0] - line, LANES), f32)


def pack_kernel(sizes, forces, codes, own, up, *down):
    planes, rows, cases = sizes
    block = 3 * cases
    base = planes * rows * block
    for x in range(planes):
        own[base + x * rows : base + (x + 1) * rows, :] = codes[x]
        scale = jnp.where(codes[x] > 0.0, LOAD, 0.0)
        for k in range(3):
            for c in range(cases):
                start = x * rows * block + k * cases + c
                own[pl.ds(start, rows, stride=block), :] = forces[k, c, x] * scale

    every_y, last = range(rows), (planes - 2, planes - 1)
    fill(own, base, sizes, up, last[1:], every_y, last, every_y)
    for ref in down:
        fill(own, base, sizes, ref, (0, 1), every_y, (0, 1), every_y)


def rows_kernel(sizes, own, ym, yp):
    planes, rows, cases = sizes
    base = planes * rows * 3 * cases
    every_x = range(planes)
    fill(own, base, sizes, ym, every_x, (0, 1), every_x, (0, 1))
    fill(own, base, sizes, yp, every_x, (rows - 1,), every_x, (rows - 2, rows - 1))


def corner_kernel(sizes, start, lower, upper, ym, yp):
    planes, rows, cases = sizes
    block = 3 * cases
    even = start[0] // planes % 2 == 0
    for ref, edges, code in ((ym, (0, 1), 0), (yp, (rows - 1,), rows - 2)):
        line = 0
        for slot in range(2):
            for edge in edges:
                at = slot * rows + edge
                above = upper[at * block : (at + 1) * block, :]
                below = lower[edge * block : (edge + 1) * block, :] if slot == 1 else 0.0
                ref[line : line + block, :] = jnp.where(even, below, above)
                line += block
        for slot in range(2):
            at = slot * rows + code
            above = upper[2 * rows * block + at : 2 * rows * block + at + 2, :]
            below = lower[rows * block + at : rows * block + at + 2, :]
            ref[line : line + 2, :] = jnp.where(even, below, above)
            line += 2
        if line < ref.shape[0]:
            ref[line:, :] = jnp.zeros((ref.shape[0] - line, LANES), f32)


def readers(sizes, first, own, pair, lower, upper, y_own, y_pair, y_corner):
    planes, rows, cases = sizes
    block = 3 * cases
    even = first // planes % 2 == 0

    def lines(ref, start, count):
        return ref[start : start + count, :]

    def inside(ref, x, y):
        return lines(ref, (x * rows + y) * block, block)

    def beyond(refs, slot, y):
        below, above = refs
        if y < 0:
            return lines(below, slot * block, block)
        return lines(above, (slot * 2 + y - rows) * block, block)

    def load(x, y):
        in_y = 0 <= y < rows
        if 0 <= x < planes:
            return inside(own, x, y) if in_y else beyond(y_own, x, y)
        if x < 0:
            if in_y:
                return jnp.where(even, inside(lower, 0, y), inside(pair, planes - 1, y))
            return jnp.where(even, beyond(y_corner, 1, y), beyond(y_pair, planes - 1, y))
        if in_y:
            return jnp.where(even, inside(pair, x - planes, y), inside(upper, x - planes, y))
        return jnp.where(even, beyond(y_pair, x - planes, y), beyond(y_corner, x - planes, y))

    def inside_codes(ref, x):
        return lines(ref, planes * rows * block + x * rows, rows)

    def beyond_codes(refs, slots, slot, y):
        below, above = refs
        if y < 0:
            return lines(below, slots * block + slot * 2, 2)
        return lines(above, slots * 2 * block + slot * 2, 2)

    def codes(x, y):
        if 0 <= x < planes:
            return inside_codes(own, x) if y == 0 else beyond_codes(y_own, planes, x, y)
        if x < 0:
            slot = x + 2
            if y == 0:
                other = inside_codes(pair, planes + x)
                return jnp.where(even, lines(lower, (block + slot) * rows, rows), other)
            other = beyond_codes(y_pair, planes, planes + x, y)
            return jnp.where(even, beyond_codes(y_corner, 2, slot, y), other)
        slot = x - planes
        if y == 0:
            other = lines(upper, (2 * block + slot) * rows, rows)
            return jnp.where(even, inside_codes(pair, slot), other)
        other = beyond_codes(y_corner, 2, slot, y)
        return jnp.where(even, beyond_codes(y_pair, planes, slot, y), other)

    return load, codes


def main_kernel(
    sizes, first, own, pair, lower, upper, ym, yp, ym_pair, yp_pair, ym_corner, yp_corner,
    both_out, system_out, stiff_ref, inverse,
    start, sums, diffs, acc_s, acc_d, w_sums, w_diffs, acc2_s, acc2_d, right, table,
):
    planes, rows, cases = sizes
    block = 3 * cases
    xs, ys = planes + 3, rows + 3
    load, signed = readers(
        sizes, first[0], own, pair, lower, upper,
        (ym, yp), (ym_pair, yp_pair), (ym_corner, yp_corner),
    )
    for x in range(-2, planes + 2):
        for y, count in ((-2, 2), (0, rows), (rows, 2)):
            stiff_ref[x + 2, y + 2 : y + 2 + count, :] = signed(x, y)
    for x in range(-1, planes + 2):
        codes = stiff_ref[x + 2, 0 : ys + 1, :]
        total = jnp.abs(stiff_ref[x + 1, 0 : ys + 1, :]) + jnp.abs(codes)
        total = total[:-1] + total[1:]
        total = total + shift_up(total)
        free = codes[1:] > 0.0
        value = 1.0 / (DIAGONAL * jnp.where(free, total, 1.0))
        inverse[x + 1, 0:ys, :] = jnp.where(free, value, 0.0)
    for x in range(planes + 4):
        stiff_ref[x] = jnp.abs(stiff_ref[x])

    for x in range(-1, planes + 2):
        for y in range(-1, rows + 2):
            value = load(x, y) * inverse[x + 1, y + 1 : y + 2, :]
            column = (x + 1) * ys + y + 1
            start[column] = value
            moved = shift_down(value)
            sums[column] = value + moved
            diffs[column] = moved - value

    nodes_y = rows + 1
    apply_elements(
        sums, diffs, stiff_ref, acc_s, acc_d, planes + 2, rows + 2, 1, 1, 1, cases
    )

    def image(x, y, place):
        column = (x + 1) * nodes_y + y
        s, d = acc_s[column], acc_d[column]
        force = s - d + shift_up(s + d)
        scaled = force * inverse[x + 1, pl.ds(y + 1, 1), :]
        moved = shift_down(scaled)
        w_sums[x * nodes_y + y] = scaled + moved
        w_diffs[x * nodes_y + y] = moved - scaled
        value = start[(x + 1) * ys + y + 1]
        for k in range(3):
            lines = slice(k * cases, (k + 1) * cases)
            pair = jnp.concatenate([value[lines], scaled[lines]], 0)
            lane = pl.ds(pl.multiple_of((place * 3 + k) * LANES, LANES), LANES)
            high, rest = split(pair)
            both_out[0 : 2 * cases, lane] = high
            both_out[2 * cases : 4 * cases, lane] = rest
        return force

    two = 2 * cases
    count = planes * rows

    def inside(index):
        force = image(index // rows, index % rows, index)
        given = own[pl.ds(pl.multiple_of(index * block, 8), block), :]
        for k in range(3):
            lines = slice(k * cases, (k + 1) * cases)
            pair = jnp.concatenate([given[lines], force[lines]], 0)
            lane = pl.ds(pl.multiple_of((index * 3 + k) * LANES, LANES), LANES)
            high, rest = split(pair)
            right[0:two, lane] = high
            right[two : 2 * two, lane] = rest

    unrolled(count, 4, inside)
    unrolled(planes, 2, lambda x: image(x, rows, count + x))
    unrolled(nodes_y, 3, lambda y: image(planes, y, count + planes + y))
    beyond = right.shape[1] - count * 3 * LANES
    right[0 : 2 * two, count * 3 * LANES :] = jnp.zeros((2 * two, beyond), bf16)

    for column in range(nodes_y):
        acc2_s[column] = jnp.zeros((block, LANES), f32)
        acc2_d[column] = jnp.zeros((block, LANES), f32)
    apply_elements(w_sums, w_diffs, stiff_ref, acc2_s, acc2_d, planes, rows, 0, 2, 2, cases)

    def second_force(x, y, place):
        column = x * nodes_y + y
        s, d = acc2_s[column], acc2_d[column]
        force = s - d + shift_up(s + d)
        for k in range(3):
            value = force[k * cases : (k + 1) * cases]
            high = value.astype(bf16).astype(f32)
            lane = pl.ds(pl.multiple_of((place * 3 + k) * LANES, LANES), LANES)
            right[2 * two :, lane] = jnp.concatenate([high, value - high], 0).astype(bf16)

    unrolled(count, 4, lambda index: second_force(index // rows, index % rows, index))
    unrolled(planes, 2, lambda x: second_force(x, rows, count + x))
    unrolled(nodes_y, 3, lambda y: second_force(planes, y, count + planes + y))

    contract = (((1,), (1,)), ((), ()))
    product = lax.dot_general(both_out[...], right[...], contract, preferred_element_type=f32)
    product = product[:two] + product[two:]
    gram = product[:, :two] + product[:, two : 2 * two]
    other = product[:, 2 * two : 2 * two + cases] + product[:, 2 * two + cases :]
    row = lax.broadcasted_iota(jnp.int32, (cases, cases), 0)
    column = lax.broadcasted_iota(jnp.int32, (cases, cases), 1)
    load_load, load_image = gram[:cases, :cases], gram[:cases, cases:]
    mixed, image_image = other[:cases], other[cases:]
    table[...] = jnp.zeros(table.shape, f32)
    table[:, 0:cases] = jnp.where(row <= column, load_load, load_image)
    table[:, cases:two] = jnp.where(row <= column, mixed, image_image)
    for lane, value in ((two, load_image), (two + 1, image_image)):
        own_entries = jnp.where(row == column, value, 0.0)
        table[:, lane : lane + 1] = jnp.sum(own_entries, axis=1, keepdims=True)
    half = cases // 2
    folded = table[:half, :] + pltpu.roll(table[half:, :], LANES // 2, 1)
    depth = system_out.shape[2]
    for index in range(system_out.shape[0]):
        for part in range(half // depth):
            system_out[index, part] = folded[part * depth : (part + 1) * depth]


def solve_kernel(
    sizes, system, both, codes, out, mixing, sums, diffs, energy, square, full
):
    planes, rows, cases = sizes
    two = 2 * cases
    nodes_y = rows + 1
    count = planes * rows
    total = jnp.sum(system[...], axis=0)
    half, depth = cases // 2, system.shape[2]
    square[...] = jnp.zeros(square.shape, f32)
    for part in range(half // depth):
        value = total[part]
        square[part * depth : (part + 1) * depth, :] = value
        lines = slice(half + part * depth, half + (part + 1) * depth)
        square[lines, :] = pltpu.roll(value, LANES // 2, 1)
    value, turned = square[0:cases, :], jnp.transpose(square[...])
    line = lax.broadcasted_iota(jnp.int32, (cases, cases), 0)
    place = lax.broadcasted_iota(jnp.int32, (cases, cases), 1)

    def mended(start, diagonal=None):
        kept, other = value[:, start : start + cases], turned[start : start + cases, :cases]
        if diagonal is None:
            return jnp.where(line <= place, kept, other)
        inner = jnp.where(line < place, other, value[:, diagonal : diagonal + 1])
        return jnp.where(line > place, kept, inner)

    load_image, mixed = mended(0, two), mended(cases)
    parts = ((load_image, mixed), (mixed, mended(cases, two + 1)), (mended(0), load_image))
    full[...] = jnp.zeros(full.shape, f32)
    for index, (left, right) in enumerate(parts):
        full[index * cases : (index + 1) * cases, 0:cases] = left
        full[index * cases : (index + 1) * cases, cases:two] = right
    table = full[...]
    lane = lax.broadcasted_iota(jnp.int32, (1, LANES), 1)
    gone, wide = 0, 4
    for pivot in range(0, two, wide):
        drop = pivot // 8 * 8 - gone
        table = table[drop:]
        gone += drop
        line = pivot - gone
        inner = (lane >= pivot) & (lane < pivot + wide)
        found = [table[line + p : line + p + 1, :] for p in range(wide)]
        block = [
            [jnp.broadcast_to(row[:, pivot + q : pivot + q + 1], row.shape) for q in range(wide)]
            for row in found
        ]
        solved = [
            jnp.where(lane == pivot + p, -1.0, jnp.where(inner, 0.0, found[p]))
            for p in range(wide)
        ]
        for p in range(wide):
            inverse = 1.0 / block[p][p]
            solved[p] = solved[p] * inverse
            block[p] = [value * inverse for value in block[p]]
            for q in range(wide):
                if q != p:
                    factor = block[q][p]
                    solved[q] = solved[q] - factor * solved[p]
                    for r in range(p + 1, wide):
                        block[q][r] = block[q][r] - factor * block[p][r]
        update = None
        for q in range(wide):
            term = table[:, pivot + q : pivot + q + 1] * solved[q]
            update = term if update is None else update + term
        table = jnp.where(inner, 0.0, table) - update
    answer = table[two - gone :, :two]
    high = answer.astype(bf16).astype(f32)
    mixing[...] = jnp.zeros(mixing.shape, f32)
    mixing[0:cases, 0:two] = high
    mixing[0:cases, two : 2 * two] = high
    mixing[cases:two, 0:two] = answer - high
    mix = mixing[...][:, : 2 * two].astype(bf16)

    def combined(place, width):
        lanes = pl.ds(pl.multiple_of(place * 3 * LANES, LANES), width * 3 * LANES)
        value = jnp.dot(mix, both[:, lanes], preferred_element_type=f32)
        return value[:cases] + value[cases:]

    def keep(value, index, column):
        for k in range(3):
            part = value[:, (index * 3 + k) * LANES : (index * 3 + k + 1) * LANES]
            moved = shift_down(part)
            sums[column, k * cases : (k + 1) * cases, :] = part + moved
            diffs[column, k * cases : (k + 1) * cases, :] = moved - part

    def inside(x, _):
        value = combined(x * rows, rows)
        for y in range(rows):
            keep(value, y, x * nodes_y + y)
        return 0

    lax.fori_loop(0, planes, inside, 0)
    value = combined(count, planes + nodes_y)
    for x in range(planes):
        keep(value, x, x * nodes_y + rows)
    for y in range(nodes_y):
        keep(value, planes + y, planes * nodes_y + y)

    tiles = cases // 8

    def step(plane, _):
        for tile in range(tiles):
            lower = x_modes(sums, diffs, plane, 0, tile, cases, nodes_y)
            for row in range(rows):
                upper = x_modes(sums, diffs, plane, row + 1, tile, cases, nodes_y)
                part = mode_energy(modes_of(lower, upper))
                if tile == 0:
                    energy[row] = part
                else:
                    energy[row] += part
                lower = upper
        total = jnp.sum(energy[...], axis=1)
        total = (-3.0 / cases) * jnp.abs(codes[plane]) * total
        for index in range(out.shape[0]):
            out[index, plane] = total
        return 0

    lax.fori_loop(0, planes, step, 0)


def smooth(ref, x, rows):
    weight = [2.5 - math.sqrt(q) for q in range(7)]
    near = {}
    for dx in range(-2, 3):
        for dy in range(-2, 3):
            q = dx * dx + dy * dy
            if q <= 5:
                value = ref[x + 2 + dx, 2 + dy : 2 + dy + rows, :]
                near[q] = value if q not in near else near[q] + value
    result = None
    for dz in range(3):
        part = None
        for q, value in near.items():
            if q + dz * dz <= 6:
                term = weight[q + dz * dz] * value
                part = term if part is None else part + term
        if dz == 0:
            result = part
        else:
            place = lax.broadcasted_iota(jnp.int32, part.shape, 1)
            forward = jnp.where(place >= LANES - dz, 0.0, pltpu.roll(part, LANES - dz, 1))
            backward = jnp.where(place < dz, 0.0, pltpu.roll(part, dz, 1))
            result = result + (forward + backward)
    return result


def scale_kernel(sizes, counts, start, levels, out, there):
    planes, rows, _ = sizes
    y = lax.broadcasted_iota(jnp.int32, (rows + 4, LANES), 0) + (start[1] - 2)
    in_y = (y >= 0) & (y < counts[1] * rows)
    for x in range(planes + 4):
        global_x = start[0] + (x - 2)
        in_x = (global_x >= 0) & (global_x < counts[0] * planes)
        there[x] = jnp.where(in_y & in_x, 1.0, 0.0)
    for x in range(planes):
        density = 0.3 + 0.7 * levels[x].astype(f32) / (LEVELS - 1)
        out[x] = 1.0 / (density * smooth(there, x, rows))


def filter_kernel(sizes, counts, start, blocks, scale, out, wide):
    planes, rows, _ = sizes
    sides_x = ((-1, planes - 2, planes, 0), (0, 0, planes, 2), (1, 0, 2, 2 + planes))
    sides_y = ((-1, rows - 2, rows, 0), (0, 0, rows, 2), (1, 0, 2, 2 + rows))
    for step_x, x0, x1, to_x in sides_x:
        for step_y, y0, y1, to_y in sides_y:
            at_x = start[0] // planes + step_x
            at_y = start[1] // rows + step_y
            inside = (at_x >= 0) & (at_x < counts[0]) & (at_y >= 0) & (at_y < counts[1])
            index = jnp.where(inside, at_x * counts[1] + at_y, 0)
            value = blocks[index, x0:x1, y0:y1, :]
            wide[to_x : to_x + x1 - x0, to_y : to_y + y1 - y0, :] = jnp.where(inside, value, 0.0)
    for x in range(planes):
        out[x] = smooth(wide, x, rows) * scale[x]


def local(forces, levels, supports):
    _, cases, planes, rows, _ = forces.shape
    sizes = (planes, rows, cases)
    block = 3 * cases
    count_x, count_y = lax.axis_size("gx"), lax.axis_size("gy")

    def shape(blocks, codes):
        return jax.ShapeDtypeStruct((blocks * block + up8(codes), LANES), f32)

    density = 0.3 + 0.7 * levels.astype(f32) / (LEVELS - 1)
    codes = density * density * density
    codes = jnp.where(supports == 0, codes, -codes)
    whole = shape(planes * rows, planes * rows)
    down = [] if planes == 2 else [shape(2 * rows, 2 * rows)]
    own, up, *down = pl.pallas_call(
        functools.partial(pack_kernel, sizes),
        out_shape=[whole, shape(rows, 2 * rows), *down],
        in_specs=[VMEM] * 2,
        out_specs=[VMEM] * (2 + len(down)),
        compiler_params=PARAMS,
        name="pack",
    )(forces, codes)

    start = jnp.stack([lax.axis_index("gx") * planes, lax.axis_index("gy") * rows])
    start = start.astype(jnp.int32)
    counts = (count_x, count_y)
    scalars = pl.BlockSpec(memory_space=pltpu.SMEM)
    scale = pl.pallas_call(
        functools.partial(scale_kernel, sizes, counts),
        out_shape=jax.ShapeDtypeStruct((planes, rows, LANES), f32),
        in_specs=[scalars, VMEM],
        out_specs=VMEM,
        scratch_shapes=[pltpu.VMEM((planes + 4, rows + 4, LANES), f32)],
        compiler_params=PARAMS,
        name="scale",
    )(start, levels)

    def moved(value, axis, step):
        count = lax.axis_size(axis)
        pairs = [(i, i + step) for i in range(count) if 0 <= i + step < count]
        return lax.ppermute(value, axis, pairs)

    def links(first, step):
        return [(i, i + step) for i in range(first, count_x, 2) if 0 <= i + step < count_x]

    def swapped(value):
        return lax.ppermute(value, "gx", links(0, 1) + links(1, -1))

    upper = lax.ppermute(down[0] if down else own, "gx", links(2, -1))
    lower = lax.ppermute(up, "gx", links(1, 1))
    pair = swapped(own)
    own, pair = lax.optimization_barrier((own, pair))
    ym, yp = pl.pallas_call(
        functools.partial(rows_kernel, sizes),
        out_shape=[shape(2 * planes, 2 * planes), shape(planes, 2 * planes)],
        in_specs=[VMEM],
        out_specs=[VMEM] * 2,
        compiler_params=PARAMS,
        name="rows",
    )(own)
    from_yp, from_ym = moved(ym, "gy", -1), moved(yp, "gy", 1)
    corner_m, corner_p = pl.pallas_call(
        functools.partial(corner_kernel, sizes),
        out_shape=[shape(4, 4), shape(2, 4)],
        in_specs=[scalars] + [VMEM] * 2,
        out_specs=[VMEM] * 2,
        compiler_params=PARAMS,
        name="corners",
    )(start, lower, upper)
    corner_yp, corner_ym = moved(corner_m, "gy", -1), moved(corner_p, "gy", 1)
    pair_yp, pair_ym = swapped(from_yp), swapped(from_ym)

    devices = count_x * count_y
    nodes = (planes + 1) * (rows + 1)
    wide = (planes + 3) * (rows + 3)
    acc = pltpu.VMEM(((planes + 3) * (rows + 1), block, LANES), f32)
    field = pltpu.VMEM((nodes, block, LANES), f32)
    both, system = pl.pallas_call(
        functools.partial(main_kernel, sizes),
        out_shape=[
            jax.ShapeDtypeStruct((4 * cases, nodes * 3 * LANES), bf16),
            jax.ShapeDtypeStruct((devices, cases // 8, 4, LANES), f32),
        ],
        in_specs=[scalars] + [VMEM] * 10,
        out_specs=[VMEM] * 2,
        scratch_shapes=[
            pltpu.VMEM((planes + 4, up8(rows + 4), LANES), f32),
            pltpu.VMEM((planes + 3, up8(rows + 3), LANES), f32),
            pltpu.VMEM((wide, block, LANES), f32),
            pltpu.VMEM((wide, block, LANES), f32),
            pltpu.VMEM((wide, block, LANES), f32),
            acc, acc, field, field, field, field,
            pltpu.VMEM((6 * cases, nodes * 3 * LANES), bf16),
            pltpu.VMEM((cases, LANES), f32),
        ],
        compiler_params=PARAMS,
        name="operator",
    )(
        start, own, pair, lower, upper, from_ym, from_yp,
        pair_ym, pair_yp, corner_ym, corner_yp,
    )

    def gathered(copies):
        return lax.all_to_all(copies, ("gx", "gy"), 0, 0)

    system = gathered(system)

    weighted = pl.pallas_call(
        functools.partial(solve_kernel, sizes),
        out_shape=jax.ShapeDtypeStruct((devices, planes, rows, LANES), f32),
        in_specs=[VMEM] * 3,
        out_specs=VMEM,
        scratch_shapes=[
            pltpu.VMEM((2 * cases, LANES), f32),
            field,
            field,
            pltpu.VMEM((rows, 8, LANES), f32),
            pltpu.VMEM((LANES, LANES), f32),
            pltpu.VMEM((3 * cases, LANES), f32),
        ],
        compiler_params=PARAMS,
        name="solve",
    )(system, both, codes)

    blocks = gathered(weighted)
    return pl.pallas_call(
        functools.partial(filter_kernel, sizes, counts),
        out_shape=jax.ShapeDtypeStruct((planes, rows, LANES), f32),
        in_specs=[scalars] + [VMEM] * 2,
        out_specs=VMEM,
        scratch_shapes=[pltpu.VMEM((planes + 4, rows + 4, LANES), f32)],
        compiler_params=PARAMS,
        name="cone",
    )(start, blocks, scale)


def solution(mesh):
    return jax.shard_map(
        local,
        mesh=mesh,
        in_specs=(P(None, None, "gx", "gy", None), P("gx", "gy", None), P("gx", "gy", None)),
        out_specs=P("gx", "gy", None),
        check_vma=False,
    )
```

```python
import functools
import math

import jax
import jax.numpy as jnp
from jax import lax
from jax.experimental import pallas as pl
from jax.experimental.pallas import tpu as pltpu
from jax.sharding import PartitionSpec as P

LEVELS = 16
LOAD = 0.2
LANES = 128
POISSON = 0.3
LAME = POISSON / ((1.0 + POISSON) * (1.0 - 2.0 * POISSON))
SHEAR = 1.0 / (2.0 * (1.0 + POISSON))
DIAGONAL = (LAME + 2.0 * SHEAR) / 9.0 + 2.0 * SHEAR / 9.0
VMEM = pl.BlockSpec(memory_space=pltpu.VMEM)
PARAMS = pltpu.CompilerParams(vmem_limit_bytes=30 * 2**20)
f32 = jnp.float32
bf16 = jnp.bfloat16


def up8(count):
    return -(-count // 8) * 8


def shift_down(value):
    lane = lax.broadcasted_iota(jnp.int32, value.shape, value.ndim - 1)
    rolled = pltpu.roll(value, LANES - 1, value.ndim - 1)
    return jnp.where(lane == LANES - 1, 0.0, rolled)


def shift_up(value):
    lane = lax.broadcasted_iota(jnp.int32, value.shape, value.ndim - 1)
    return jnp.where(lane == 0, 0.0, pltpu.roll(value, 1, value.ndim - 1))


def unrolled(count, factor, body):
    def turn(step, _):
        for offset in range(factor):
            body(step * factor + offset)
        return 0

    turns = count // factor
    if turns:
        lax.fori_loop(0, turns, turn, 0)
    for index in range(turns * factor, count):
        body(index)


def split(value):
    high = value.astype(bf16)
    return high, (value - high.astype(f32)).astype(bf16)


def modes_of(lower, upper):
    out = [[[[None] * 3 for _ in range(2)] for _ in range(2)] for _ in range(2)]
    for a in range(2):
        for c in range(2):
            for k in range(3):
                if a or c:
                    out[a][0][c][k] = lower[a][c][k] + upper[a][c][k]
                out[a][1][c][k] = upper[a][c][k] - lower[a][c][k]
    return out


PAIRS = (((1, 1, 0, 0), (0, 1, 1, 2)), ((1, 0, 1, 0), (0, 1, 1, 1)), ((1, 1, 0, 1), (1, 0, 1, 2)))
TRIPLE = ((0, 1, 1, 0), (1, 0, 1, 1), (1, 1, 0, 2))
SHEARS = (((0, 1, 0, 0), (1, 0, 0, 1)), ((0, 0, 1, 0), (1, 0, 0, 2)), ((0, 0, 1, 1), (0, 1, 0, 2)))
AXIAL = ((1, 0, 0, 0), (0, 1, 0, 1), (0, 0, 1, 2))


def at(modes, place):
    a, b, c, k = place
    return modes[a][b][c][k]


def mode_forces(modes, stiff):
    out = [[[[None] * 3 for _ in range(2)] for _ in range(2)] for _ in range(2)]

    def put(place, value):
        a, b, c, k = place
        out[a][b][c][k] = value

    shear = stiff * (SHEAR / 16)
    for first, second in SHEARS:
        force = shear * (at(modes, first) + at(modes, second))
        put(first, force)
        put(second, force)
    one, two, three = (at(modes, place) for place in AXIAL)
    volume = (stiff * (LAME / 16)) * (one + two + three)
    axial = stiff * (SHEAR / 8)
    for place in AXIAL:
        put(place, volume + axial * at(modes, place))
    own, cross = stiff * ((LAME + 3 * SHEAR) / 48), stiff * (LAME / 48)
    for first, second in PAIRS:
        one, two = at(modes, first), at(modes, second)
        put(first, own * one + cross * two)
        put(second, own * two + cross * one)
    twist = stiff * (SHEAR / 48)
    one, two, three = (at(modes, place) for place in TRIPLE)
    total = one + two + three
    for place in TRIPLE:
        put(place, twist * (total + at(modes, place)))
    last = stiff * ((LAME + 4 * SHEAR) / 144)
    for k in range(3):
        put((1, 1, 1, k), last * modes[1][1][1][k])
    return out


def mode_energy(modes):
    def square(value):
        return value * value

    shear = None
    for first, second in SHEARS:
        term = square(at(modes, first) + at(modes, second))
        shear = term if shear is None else shear + term
    one, two, three = (at(modes, place) for place in AXIAL)
    energy = (SHEAR / 16) * shear + (LAME / 16) * square(one + two + three)
    energy = energy + (SHEAR / 8) * (square(one) + square(two) + square(three))
    squares, products = None, None
    for first, second in PAIRS:
        one, two = at(modes, first), at(modes, second)
        term, product = square(one) + square(two), one * two
        squares = term if squares is None else squares + term
        products = product if products is None else products + product
    energy = energy + ((LAME + 3 * SHEAR) / 48) * squares + (LAME / 24) * products
    one, two, three = (at(modes, place) for place in TRIPLE)
    twist = square(one + two + three) + square(one) + square(two) + square(three)
    energy = energy + (SHEAR / 48) * twist
    last = square(modes[1][1][1][0]) + square(modes[1][1][1][1]) + square(modes[1][1][1][2])
    return energy + ((LAME + 4 * SHEAR) / 144) * last


def x_modes(sums, diffs, plane, row, tile, cases, columns):
    out = [[[None] * 3 for _ in range(2)] for _ in range(2)]
    for c, ref in enumerate((sums, diffs)):
        for k in range(3):
            rows = pl.ds(pl.multiple_of(k * cases + tile * 8, 8), 8)
            one = ref[plane * columns + row, rows, :]
            two = ref[(plane + 1) * columns + row, rows, :]
            out[0][c][k] = one + two
            out[1][c][k] = two - one
    return out


def apply_elements(
    sums, diffs, stiff_ref, acc_s, acc_d, planes, rows, skip, stiff_x, stiff_y, cases
):
    columns = rows + 1
    acc_columns = columns - 2 * skip
    tiles = cases // 8

    def step(index, _):
        plane, tile = index // tiles, index % tiles

        def emit(row, total):
            if not skip <= row < columns - skip:
                return
            for c, acc in enumerate((acc_s, acc_d)):
                for k in range(3):
                    lines = pl.ds(pl.multiple_of(k * cases + tile * 8, 8), 8)
                    low = plane * acc_columns + row - skip
                    acc[low, lines, :] += total[0][c][k] - total[1][c][k]
                    acc[low + acc_columns, lines, :] = total[0][c][k] + total[1][c][k]

        lower = x_modes(sums, diffs, plane, 0, tile, cases, columns)
        carry = None
        for row in range(rows):
            upper = x_modes(sums, diffs, plane, row + 1, tile, cases, columns)
            stiff = jnp.broadcast_to(
                stiff_ref[plane + stiff_x, pl.ds(row + stiff_y, 1), :], (8, LANES)
            )
            forces = mode_forces(modes_of(lower, upper), stiff)
            here = [[[None] * 3 for _ in range(2)] for _ in range(2)]
            following = [[[None] * 3 for _ in range(2)] for _ in range(2)]
            for a in range(2):
                for c in range(2):
                    for k in range(3):
                        one, two = forces[a][0][c][k], forces[a][1][c][k]
                        low = -two if one is None else one - two
                        high = two if one is None else one + two
                        here[a][c][k] = low if carry is None else carry[a][c][k] + low
                        following[a][c][k] = high
            emit(row, here)
            carry, lower = following, upper
        emit(rows, carry)
        return 0

    lax.fori_loop(0, planes * tiles, step, 0)


def fill(source, base, sizes, ref, xs, ys, code_xs, code_ys):
    planes, rows, cases = sizes
    block = 3 * cases
    line = 0
    for x in xs:
        start = (x * rows + ys[0]) * block
        count = len(ys) * block
        ref[line : line + count, :] = source[start : start + count, :]
        line += count
    for x in code_xs:
        start = base + x * rows + code_ys[0]
        ref[line : line + len(code_ys), :] = source[start : start + len(code_ys), :]
        line += len(code_ys)
    if line < ref.shape[0]:
        ref[line:, :] = jnp.zeros((ref.shape[0] - line, LANES), f32)


def pack_kernel(sizes, forces, codes, own, up, *down):
    planes, rows, cases = sizes
    block = 3 * cases
    base = planes * rows * block
    for x in range(planes):
        own[base + x * rows : base + (x + 1) * rows, :] = codes[x]
        scale = jnp.where(codes[x] > 0.0, LOAD, 0.0)
        for k in range(3):
            for c in range(cases):
                start = x * rows * block + k * cases + c
                own[pl.ds(start, rows, stride=block), :] = forces[k, c, x] * scale

    every_y, last = range(rows), (planes - 2, planes - 1)
    fill(own, base, sizes, up, last[1:], every_y, last, every_y)
    for ref in down:
        fill(own, base, sizes, ref, (0, 1), every_y, (0, 1), every_y)


def rows_kernel(sizes, own, ym, yp):
    planes, rows, cases = sizes
    base = planes * rows * 3 * cases
    every_x = range(planes)
    fill(own, base, sizes, ym, every_x, (0, 1), every_x, (0, 1))
    fill(own, base, sizes, yp, every_x, (rows - 1,), every_x, (rows - 2, rows - 1))


def corner_kernel(sizes, ym, yp, down, up):
    planes, rows, cases = sizes
    block = 3 * cases
    for ref, first, count in ((down, 0, 2), (up, planes - 1, 1)):
        line = 0
        for source, width in ((ym, 1), (yp, 2)):
            size = width * block
            ref[line : line + count * size, :] = source[first * size : (first + count) * size, :]
            line += count * size
            codes = planes * size + (first + count - 2) * 2
            ref[line : line + 4, :] = source[codes : codes + 4, :]
            ref[line + 4 : line + 8, :] = jnp.zeros((4, LANES), f32)
            line += 8


def readers(sizes, first, own, pair, lower, upper, y_own, y_pair, corner_low, corner_high):
    planes, rows, cases = sizes
    block = 3 * cases
    even = first // planes % 2 == 0

    def lines(ref, start, count):
        return ref[start : start + count, :]

    def inside(ref, x, y):
        return lines(ref, (x * rows + y) * block, block)

    def beyond(refs, slot, y):
        below, above = refs
        if y < 0:
            return lines(below, slot * block, block)
        return lines(above, (slot * 2 + y - rows) * block, block)

    def corner(ref, count, slot, y):
        if y < 0:
            return lines(ref, slot * block, block)
        return lines(ref, count * block + 8 + (slot * 2 + y - rows) * block, block)

    def corner_codes(ref, count, slot, y):
        start = count * block if y < 0 else 3 * count * block + 8
        return lines(ref, start + slot * 2, 2)

    def load(x, y):
        in_y = 0 <= y < rows
        if 0 <= x < planes:
            return inside(own, x, y) if in_y else beyond(y_own, x, y)
        if x < 0:
            if in_y:
                return jnp.where(even, inside(lower, 0, y), inside(pair, planes - 1, y))
            return jnp.where(even, corner(corner_low, 1, 0, y), beyond(y_pair, planes - 1, y))
        if in_y:
            return jnp.where(even, inside(pair, x - planes, y), inside(upper, x - planes, y))
        other = corner(corner_high, 2, x - planes, y)
        return jnp.where(even, beyond(y_pair, x - planes, y), other)

    def inside_codes(ref, x):
        return lines(ref, planes * rows * block + x * rows, rows)

    def beyond_codes(refs, slots, slot, y):
        below, above = refs
        if y < 0:
            return lines(below, slots * block + slot * 2, 2)
        return lines(above, slots * 2 * block + slot * 2, 2)

    def codes(x, y):
        if 0 <= x < planes:
            return inside_codes(own, x) if y == 0 else beyond_codes(y_own, planes, x, y)
        if x < 0:
            slot = x + 2
            if y == 0:
                other = inside_codes(pair, planes + x)
                return jnp.where(even, lines(lower, (block + slot) * rows, rows), other)
            other = beyond_codes(y_pair, planes, planes + x, y)
            return jnp.where(even, corner_codes(corner_low, 1, slot, y), other)
        slot = x - planes
        if y == 0:
            other = lines(upper, (2 * block + slot) * rows, rows)
            return jnp.where(even, inside_codes(pair, slot), other)
        other = corner_codes(corner_high, 2, slot, y)
        return jnp.where(even, beyond_codes(y_pair, planes, slot, y), other)

    return load, codes


def main_kernel(
    sizes, first, own, pair, lower, upper, ym, yp, ym_pair, yp_pair, corner_low, corner_high,
    both_out, system_out, stiff_ref, inverse,
    start, sums, diffs, acc_s, acc_d, w_sums, w_diffs, acc2_s, acc2_d, right, table,
):
    planes, rows, cases = sizes
    block = 3 * cases
    xs, ys = planes + 3, rows + 3
    load, signed = readers(
        sizes, first[0], own, pair, lower, upper,
        (ym, yp), (ym_pair, yp_pair), corner_low, corner_high,
    )
    for x in range(-2, planes + 2):
        for y, count in ((-2, 2), (0, rows), (rows, 2)):
            stiff_ref[x + 2, y + 2 : y + 2 + count, :] = signed(x, y)
    for x in range(-1, planes + 2):
        codes = stiff_ref[x + 2, 0 : ys + 1, :]
        total = jnp.abs(stiff_ref[x + 1, 0 : ys + 1, :]) + jnp.abs(codes)
        total = total[:-1] + total[1:]
        total = total + shift_up(total)
        free = codes[1:] > 0.0
        value = 1.0 / (DIAGONAL * jnp.where(free, total, 1.0))
        inverse[x + 1, 0:ys, :] = jnp.where(free, value, 0.0)
    for x in range(planes + 4):
        stiff_ref[x] = jnp.abs(stiff_ref[x])

    for x in range(-1, planes + 2):
        for y in range(-1, rows + 2):
            value = load(x, y) * inverse[x + 1, y + 1 : y + 2, :]
            column = (x + 1) * ys + y + 1
            start[column] = value
            moved = shift_down(value)
            sums[column] = value + moved
            diffs[column] = moved - value

    nodes_y = rows + 1
    apply_elements(
        sums, diffs, stiff_ref, acc_s, acc_d, planes + 2, rows + 2, 1, 1, 1, cases
    )

    def image(x, y, place):
        column = (x + 1) * nodes_y + y
        s, d = acc_s[column], acc_d[column]
        force = s - d + shift_up(s + d)
        scaled = force * inverse[x + 1, pl.ds(y + 1, 1), :]
        moved = shift_down(scaled)
        w_sums[x * nodes_y + y] = scaled + moved
        w_diffs[x * nodes_y + y] = moved - scaled
        value = start[(x + 1) * ys + y + 1]
        for k in range(3):
            lines = slice(k * cases, (k + 1) * cases)
            pair = jnp.concatenate([value[lines], scaled[lines]], 0)
            lane = pl.ds(pl.multiple_of((place * 3 + k) * LANES, LANES), LANES)
            high, rest = split(pair)
            both_out[0 : 2 * cases, lane] = high
            both_out[2 * cases : 4 * cases, lane] = rest
        return force

    two = 2 * cases
    count = planes * rows

    def inside(index):
        force = image(index // rows, index % rows, index)
        given = own[pl.ds(pl.multiple_of(index * block, 8), block), :]
        for k in range(3):
            lines = slice(k * cases, (k + 1) * cases)
            pair = jnp.concatenate([given[lines], force[lines]], 0)
            lane = pl.ds(pl.multiple_of((index * 3 + k) * LANES, LANES), LANES)
            high, rest = split(pair)
            right[0:two, lane] = high
            right[two : 2 * two, lane] = rest

    unrolled(count, 4, inside)
    unrolled(planes, 2, lambda x: image(x, rows, count + x))
    unrolled(nodes_y, 3, lambda y: image(planes, y, count + planes + y))
    beyond = right.shape[1] - count * 3 * LANES
    right[0 : 2 * two, count * 3 * LANES :] = jnp.zeros((2 * two, beyond), bf16)

    for column in range(nodes_y):
        acc2_s[column] = jnp.zeros((block, LANES), f32)
        acc2_d[column] = jnp.zeros((block, LANES), f32)
    apply_elements(w_sums, w_diffs, stiff_ref, acc2_s, acc2_d, planes, rows, 0, 2, 2, cases)

    def second_force(x, y, place):
        column = x * nodes_y + y
        s, d = acc2_s[column], acc2_d[column]
        force = s - d + shift_up(s + d)
        for k in range(3):
            value = force[k * cases : (k + 1) * cases]
            high = value.astype(bf16).astype(f32)
            lane = pl.ds(pl.multiple_of((place * 3 + k) * LANES, LANES), LANES)
            right[2 * two :, lane] = jnp.concatenate([high, value - high], 0).astype(bf16)

    unrolled(count, 4, lambda index: second_force(index // rows, index % rows, index))
    unrolled(planes, 2, lambda x: second_force(x, rows, count + x))
    unrolled(nodes_y, 3, lambda y: second_force(planes, y, count + planes + y))

    contract = (((1,), (1,)), ((), ()))
    product = lax.dot_general(both_out[...], right[...], contract, preferred_element_type=f32)
    product = product[:two] + product[two:]
    gram = product[:, :two] + product[:, two : 2 * two]
    other = product[:, 2 * two : 2 * two + cases] + product[:, 2 * two + cases :]
    row = lax.broadcasted_iota(jnp.int32, (cases, cases), 0)
    column = lax.broadcasted_iota(jnp.int32, (cases, cases), 1)
    load_load, load_image = gram[:cases, :cases], gram[:cases, cases:]
    mixed, image_image = other[:cases], other[cases:]
    table[...] = jnp.zeros(table.shape, f32)
    table[:, 0:cases] = jnp.where(row <= column, load_load, load_image)
    table[:, cases:two] = jnp.where(row <= column, mixed, image_image)
    for lane, value in ((two, load_image), (two + 1, image_image)):
        own_entries = jnp.where(row == column, value, 0.0)
        table[:, lane : lane + 1] = jnp.sum(own_entries, axis=1, keepdims=True)
    half = cases // 2
    folded = table[:half, :] + pltpu.roll(table[half:, :], LANES // 2, 1)
    depth = system_out.shape[2]
    for index in range(system_out.shape[0]):
        for part in range(half // depth):
            system_out[index, part] = folded[part * depth : (part + 1) * depth]


def solve_kernel(
    sizes, system, both, codes, out, mixing, sums, diffs, energy, square, full
):
    planes, rows, cases = sizes
    two = 2 * cases
    nodes_y = rows + 1
    count = planes * rows
    total = jnp.sum(system[...], axis=0)
    half, depth = cases // 2, system.shape[2]
    square[...] = jnp.zeros(square.shape, f32)
    for part in range(half // depth):
        value = total[part]
        square[part * depth : (part + 1) * depth, :] = value
        lines = slice(half + part * depth, half + (part + 1) * depth)
        square[lines, :] = pltpu.roll(value, LANES // 2, 1)
    value, turned = square[0:cases, :], jnp.transpose(square[...])
    line = lax.broadcasted_iota(jnp.int32, (cases, cases), 0)
    place = lax.broadcasted_iota(jnp.int32, (cases, cases), 1)

    def mended(start, diagonal=None):
        kept, other = value[:, start : start + cases], turned[start : start + cases, :cases]
        if diagonal is None:
            return jnp.where(line <= place, kept, other)
        inner = jnp.where(line < place, other, value[:, diagonal : diagonal + 1])
        return jnp.where(line > place, kept, inner)

    load_image, mixed = mended(0, two), mended(cases)
    parts = ((load_image, mixed), (mixed, mended(cases, two + 1)), (mended(0), load_image))
    full[...] = jnp.zeros(full.shape, f32)
    for index, (left, right) in enumerate(parts):
        full[index * cases : (index + 1) * cases, 0:cases] = left
        full[index * cases : (index + 1) * cases, cases:two] = right
    table = full[...]
    lane = lax.broadcasted_iota(jnp.int32, (1, LANES), 1)
    gone, wide = 0, 4
    for pivot in range(0, two, wide):
        drop = pivot // 8 * 8 - gone
        table = table[drop:]
        gone += drop
        line = pivot - gone
        inner = (lane >= pivot) & (lane < pivot + wide)
        found = [table[line + p : line + p + 1, :] for p in range(wide)]
        block = [
            [jnp.broadcast_to(row[:, pivot + q : pivot + q + 1], row.shape) for q in range(wide)]
            for row in found
        ]
        solved = [
            jnp.where(lane == pivot + p, -1.0, jnp.where(inner, 0.0, found[p]))
            for p in range(wide)
        ]
        for p in range(wide):
            inverse = 1.0 / block[p][p]
            solved[p] = solved[p] * inverse
            block[p] = [value * inverse for value in block[p]]
            for q in range(wide):
                if q != p:
                    factor = block[q][p]
                    solved[q] = solved[q] - factor * solved[p]
                    for r in range(p + 1, wide):
                        block[q][r] = block[q][r] - factor * block[p][r]
        update = None
        for q in range(wide):
            term = table[:, pivot + q : pivot + q + 1] * solved[q]
            update = term if update is None else update + term
        table = jnp.where(inner, 0.0, table) - update
    answer = table[two - gone :, :two]
    high = answer.astype(bf16).astype(f32)
    mixing[...] = jnp.zeros(mixing.shape, f32)
    mixing[0:cases, 0:two] = high
    mixing[0:cases, two : 2 * two] = high
    mixing[cases:two, 0:two] = answer - high
    mix = mixing[...][:, : 2 * two].astype(bf16)

    def combined(place, width):
        lanes = pl.ds(pl.multiple_of(place * 3 * LANES, LANES), width * 3 * LANES)
        value = jnp.dot(mix, both[:, lanes], preferred_element_type=f32)
        return value[:cases] + value[cases:]

    def keep(value, index, column):
        for k in range(3):
            part = value[:, (index * 3 + k) * LANES : (index * 3 + k + 1) * LANES]
            moved = shift_down(part)
            sums[column, k * cases : (k + 1) * cases, :] = part + moved
            diffs[column, k * cases : (k + 1) * cases, :] = moved - part

    def inside(x, _):
        value = combined(x * rows, rows)
        for y in range(rows):
            keep(value, y, x * nodes_y + y)
        return 0

    lax.fori_loop(0, planes, inside, 0)
    value = combined(count, planes + nodes_y)
    for x in range(planes):
        keep(value, x, x * nodes_y + rows)
    for y in range(nodes_y):
        keep(value, planes + y, planes * nodes_y + y)

    tiles = cases // 8

    def step(plane, _):
        for tile in range(tiles):
            lower = x_modes(sums, diffs, plane, 0, tile, cases, nodes_y)
            for row in range(rows):
                upper = x_modes(sums, diffs, plane, row + 1, tile, cases, nodes_y)
                part = mode_energy(modes_of(lower, upper))
                if tile == 0:
                    energy[row] = part
                else:
                    energy[row] += part
                lower = upper
        total = jnp.sum(energy[...], axis=1)
        total = (-3.0 / cases) * jnp.abs(codes[plane]) * total
        for index in range(out.shape[0]):
            out[index, plane] = total
        return 0

    lax.fori_loop(0, planes, step, 0)


def smooth(ref, x, rows):
    weight = [2.5 - math.sqrt(q) for q in range(7)]
    near = {}
    for dx in range(-2, 3):
        for dy in range(-2, 3):
            q = dx * dx + dy * dy
            if q <= 5:
                value = ref[x + 2 + dx, 2 + dy : 2 + dy + rows, :]
                near[q] = value if q not in near else near[q] + value
    result = None
    for dz in range(3):
        part = None
        for q, value in near.items():
            if q + dz * dz <= 6:
                term = weight[q + dz * dz] * value
                part = term if part is None else part + term
        if dz == 0:
            result = part
        else:
            place = lax.broadcasted_iota(jnp.int32, part.shape, 1)
            forward = jnp.where(place >= LANES - dz, 0.0, pltpu.roll(part, LANES - dz, 1))
            backward = jnp.where(place < dz, 0.0, pltpu.roll(part, dz, 1))
            result = result + (forward + backward)
    return result


def scale_kernel(sizes, counts, start, levels, out, there):
    planes, rows, _ = sizes
    y = lax.broadcasted_iota(jnp.int32, (rows + 4, LANES), 0) + (start[1] - 2)
    in_y = (y >= 0) & (y < counts[1] * rows)
    for x in range(planes + 4):
        global_x = start[0] + (x - 2)
        in_x = (global_x >= 0) & (global_x < counts[0] * planes)
        there[x] = jnp.where(in_y & in_x, 1.0, 0.0)
    for x in range(planes):
        density = 0.3 + 0.7 * levels[x].astype(f32) / (LEVELS - 1)
        out[x] = 1.0 / (density * smooth(there, x, rows))


def filter_kernel(sizes, counts, start, blocks, scale, out, wide):
    planes, rows, _ = sizes
    sides_x = ((-1, planes - 2, planes, 0), (0, 0, planes, 2), (1, 0, 2, 2 + planes))
    sides_y = ((-1, rows - 2, rows, 0), (0, 0, rows, 2), (1, 0, 2, 2 + rows))
    for step_x, x0, x1, to_x in sides_x:
        for step_y, y0, y1, to_y in sides_y:
            at_x = start[0] // planes + step_x
            at_y = start[1] // rows + step_y
            inside = (at_x >= 0) & (at_x < counts[0]) & (at_y >= 0) & (at_y < counts[1])
            index = jnp.where(inside, at_x * counts[1] + at_y, 0)
            value = blocks[index, x0:x1, y0:y1, :]
            wide[to_x : to_x + x1 - x0, to_y : to_y + y1 - y0, :] = jnp.where(inside, value, 0.0)
    for x in range(planes):
        out[x] = smooth(wide, x, rows) * scale[x]


def local(forces, levels, supports):
    _, cases, planes, rows, _ = forces.shape
    sizes = (planes, rows, cases)
    block = 3 * cases
    count_x, count_y = lax.axis_size("gx"), lax.axis_size("gy")

    def shape(blocks, codes):
        return jax.ShapeDtypeStruct((blocks * block + up8(codes), LANES), f32)

    density = 0.3 + 0.7 * levels.astype(f32) / (LEVELS - 1)
    codes = density * density * density
    codes = jnp.where(supports == 0, codes, -codes)
    whole = shape(planes * rows, planes * rows)
    down = [] if planes == 2 else [shape(2 * rows, 2 * rows)]
    own, up, *down = pl.pallas_call(
        functools.partial(pack_kernel, sizes),
        out_shape=[whole, shape(rows, 2 * rows), *down],
        in_specs=[VMEM] * 2,
        out_specs=[VMEM] * (2 + len(down)),
        compiler_params=PARAMS,
        name="pack",
    )(forces, codes)

    start = jnp.stack([lax.axis_index("gx") * planes, lax.axis_index("gy") * rows])
    start = start.astype(jnp.int32)
    counts = (count_x, count_y)
    scalars = pl.BlockSpec(memory_space=pltpu.SMEM)
    scale = pl.pallas_call(
        functools.partial(scale_kernel, sizes, counts),
        out_shape=jax.ShapeDtypeStruct((planes, rows, LANES), f32),
        in_specs=[scalars, VMEM],
        out_specs=VMEM,
        scratch_shapes=[pltpu.VMEM((planes + 4, rows + 4, LANES), f32)],
        compiler_params=PARAMS,
        name="scale",
    )(start, levels)

    def moved(value, axis, step):
        count = lax.axis_size(axis)
        pairs = [(i, i + step) for i in range(count) if 0 <= i + step < count]
        return lax.ppermute(value, axis, pairs)

    def links(first, step):
        return [(i, i + step) for i in range(first, count_x, 2) if 0 <= i + step < count_x]

    def swapped(value):
        return lax.ppermute(value, "gx", links(0, 1) + links(1, -1))

    upper = lax.ppermute(down[0] if down else own, "gx", links(2, -1))
    lower = lax.ppermute(up, "gx", links(1, 1))
    pair = swapped(own)
    own, pair = lax.optimization_barrier((own, pair))
    ym, yp = pl.pallas_call(
        functools.partial(rows_kernel, sizes),
        out_shape=[shape(2 * planes, 2 * planes), shape(planes, 2 * planes)],
        in_specs=[VMEM],
        out_specs=[VMEM] * 2,
        compiler_params=PARAMS,
        name="rows",
    )(own)
    from_yp, from_ym = moved(ym, "gy", -1), moved(yp, "gy", 1)
    pair_yp, pair_ym = swapped(from_yp), swapped(from_ym)
    corner_down, corner_up = pl.pallas_call(
        functools.partial(corner_kernel, sizes),
        out_shape=[
            jax.ShapeDtypeStruct((6 * block + 16, LANES), f32),
            jax.ShapeDtypeStruct((3 * block + 16, LANES), f32),
        ],
        in_specs=[VMEM] * 2,
        out_specs=[VMEM] * 2,
        compiler_params=PARAMS,
        name="corners",
    )(from_ym, from_yp)
    corner_high = lax.ppermute(corner_down, "gx", links(2, -1))
    corner_low = lax.ppermute(corner_up, "gx", links(1, 1))

    devices = count_x * count_y
    nodes = (planes + 1) * (rows + 1)
    wide = (planes + 3) * (rows + 3)
    acc = pltpu.VMEM(((planes + 3) * (rows + 1), block, LANES), f32)
    field = pltpu.VMEM((nodes, block, LANES), f32)
    both, system = pl.pallas_call(
        functools.partial(main_kernel, sizes),
        out_shape=[
            jax.ShapeDtypeStruct((4 * cases, nodes * 3 * LANES), bf16),
            jax.ShapeDtypeStruct((devices, cases // 8, 4, LANES), f32),
        ],
        in_specs=[scalars] + [VMEM] * 10,
        out_specs=[VMEM] * 2,
        scratch_shapes=[
            pltpu.VMEM((planes + 4, up8(rows + 4), LANES), f32),
            pltpu.VMEM((planes + 3, up8(rows + 3), LANES), f32),
            pltpu.VMEM((wide, block, LANES), f32),
            pltpu.VMEM((wide, block, LANES), f32),
            pltpu.VMEM((wide, block, LANES), f32),
            acc, acc, field, field, field, field,
            pltpu.VMEM((6 * cases, nodes * 3 * LANES), bf16),
            pltpu.VMEM((cases, LANES), f32),
        ],
        compiler_params=PARAMS,
        name="operator",
    )(
        start, own, pair, lower, upper, from_ym, from_yp,
        pair_ym, pair_yp, corner_low, corner_high,
    )

    def gathered(copies):
        return lax.all_to_all(copies, ("gx", "gy"), 0, 0)

    system = gathered(system)

    weighted = pl.pallas_call(
        functools.partial(solve_kernel, sizes),
        out_shape=jax.ShapeDtypeStruct((devices, planes, rows, LANES), f32),
        in_specs=[VMEM] * 3,
        out_specs=VMEM,
        scratch_shapes=[
            pltpu.VMEM((2 * cases, LANES), f32),
            field,
            field,
            pltpu.VMEM((rows, 8, LANES), f32),
            pltpu.VMEM((LANES, LANES), f32),
            pltpu.VMEM((3 * cases, LANES), f32),
        ],
        compiler_params=PARAMS,
        name="solve",
    )(system, both, codes)

    blocks = gathered(weighted)
    return pl.pallas_call(
        functools.partial(filter_kernel, sizes, counts),
        out_shape=jax.ShapeDtypeStruct((planes, rows, LANES), f32),
        in_specs=[scalars] + [VMEM] * 2,
        out_specs=VMEM,
        scratch_shapes=[pltpu.VMEM((planes + 4, rows + 4, LANES), f32)],
        compiler_params=PARAMS,
        name="cone",
    )(start, blocks, scale)


def solution(mesh):
    return jax.shard_map(
        local,
        mesh=mesh,
        in_specs=(P(None, None, "gx", "gy", None), P("gx", "gy", None), P("gx", "gy", None)),
        out_specs=P("gx", "gy", None),
        check_vma=False,
    )
```

```python
import functools
import math

import jax
import jax.numpy as jnp
from jax import lax
from jax.experimental import pallas as pl
from jax.experimental.pallas import tpu as pltpu
from jax.sharding import PartitionSpec as P

LEVELS = 16
LOAD = 0.2
LANES = 128
POISSON = 0.3
LAME = POISSON / ((1.0 + POISSON) * (1.0 - 2.0 * POISSON))
SHEAR = 1.0 / (2.0 * (1.0 + POISSON))
DIAGONAL = (LAME + 2.0 * SHEAR) / 9.0 + 2.0 * SHEAR / 9.0
VMEM = pl.BlockSpec(memory_space=pltpu.VMEM)
PARAMS = pltpu.CompilerParams(vmem_limit_bytes=30 * 2**20)
f32 = jnp.float32
bf16 = jnp.bfloat16


def up8(count):
    return -(-count // 8) * 8


def shift_down(value):
    lane = lax.broadcasted_iota(jnp.int32, value.shape, value.ndim - 1)
    rolled = pltpu.roll(value, LANES - 1, value.ndim - 1)
    return jnp.where(lane == LANES - 1, 0.0, rolled)


def shift_up(value):
    lane = lax.broadcasted_iota(jnp.int32, value.shape, value.ndim - 1)
    return jnp.where(lane == 0, 0.0, pltpu.roll(value, 1, value.ndim - 1))


def unrolled(count, factor, body):
    def turn(step, _):
        for offset in range(factor):
            body(step * factor + offset)
        return 0

    turns = count // factor
    if turns:
        lax.fori_loop(0, turns, turn, 0)
    for index in range(turns * factor, count):
        body(index)


def split(value):
    high = value.astype(bf16)
    return high, (value - high.astype(f32)).astype(bf16)


def modes_of(lower, upper):
    out = [[[[None] * 3 for _ in range(2)] for _ in range(2)] for _ in range(2)]
    for a in range(2):
        for c in range(2):
            for k in range(3):
                if a or c:
                    out[a][0][c][k] = lower[a][c][k] + upper[a][c][k]
                out[a][1][c][k] = upper[a][c][k] - lower[a][c][k]
    return out


PAIRS = (((1, 1, 0, 0), (0, 1, 1, 2)), ((1, 0, 1, 0), (0, 1, 1, 1)), ((1, 1, 0, 1), (1, 0, 1, 2)))
TRIPLE = ((0, 1, 1, 0), (1, 0, 1, 1), (1, 1, 0, 2))
SHEARS = (((0, 1, 0, 0), (1, 0, 0, 1)), ((0, 0, 1, 0), (1, 0, 0, 2)), ((0, 0, 1, 1), (0, 1, 0, 2)))
AXIAL = ((1, 0, 0, 0), (0, 1, 0, 1), (0, 0, 1, 2))


def at(modes, place):
    a, b, c, k = place
    return modes[a][b][c][k]


def mode_forces(modes, stiff):
    out = [[[[None] * 3 for _ in range(2)] for _ in range(2)] for _ in range(2)]

    def put(place, value):
        a, b, c, k = place
        out[a][b][c][k] = value

    shear = stiff * (SHEAR / 16)
    for first, second in SHEARS:
        force = shear * (at(modes, first) + at(modes, second))
        put(first, force)
        put(second, force)
    one, two, three = (at(modes, place) for place in AXIAL)
    volume = (stiff * (LAME / 16)) * (one + two + three)
    axial = stiff * (SHEAR / 8)
    for place in AXIAL:
        put(place, volume + axial * at(modes, place))
    own, cross = stiff * ((LAME + 3 * SHEAR) / 48), stiff * (LAME / 48)
    for first, second in PAIRS:
        one, two = at(modes, first), at(modes, second)
        put(first, own * one + cross * two)
        put(second, own * two + cross * one)
    twist = stiff * (SHEAR / 48)
    one, two, three = (at(modes, place) for place in TRIPLE)
    total = one + two + three
    for place in TRIPLE:
        put(place, twist * (total + at(modes, place)))
    last = stiff * ((LAME + 4 * SHEAR) / 144)
    for k in range(3):
        put((1, 1, 1, k), last * modes[1][1][1][k])
    return out


def mode_energy(modes):
    def square(value):
        return value * value

    shear = None
    for first, second in SHEARS:
        term = square(at(modes, first) + at(modes, second))
        shear = term if shear is None else shear + term
    one, two, three = (at(modes, place) for place in AXIAL)
    energy = (SHEAR / 16) * shear + (LAME / 16) * square(one + two + three)
    energy = energy + (SHEAR / 8) * (square(one) + square(two) + square(three))
    squares, products = None, None
    for first, second in PAIRS:
        one, two = at(modes, first), at(modes, second)
        term, product = square(one) + square(two), one * two
        squares = term if squares is None else squares + term
        products = product if products is None else products + product
    energy = energy + ((LAME + 3 * SHEAR) / 48) * squares + (LAME / 24) * products
    one, two, three = (at(modes, place) for place in TRIPLE)
    twist = square(one + two + three) + square(one) + square(two) + square(three)
    energy = energy + (SHEAR / 48) * twist
    last = square(modes[1][1][1][0]) + square(modes[1][1][1][1]) + square(modes[1][1][1][2])
    return energy + ((LAME + 4 * SHEAR) / 144) * last


def x_modes(sums, diffs, plane, row, tile, cases, columns):
    out = [[[None] * 3 for _ in range(2)] for _ in range(2)]
    for c, ref in enumerate((sums, diffs)):
        for k in range(3):
            rows = pl.ds(pl.multiple_of(k * cases + tile * 8, 8), 8)
            one = ref[plane * columns + row, rows, :]
            two = ref[(plane + 1) * columns + row, rows, :]
            out[0][c][k] = one + two
            out[1][c][k] = two - one
    return out


def apply_elements(
    sums, diffs, stiff_ref, acc_s, acc_d, planes, rows, skip, stiff_x, stiff_y, cases
):
    columns = rows + 1
    acc_columns = columns - 2 * skip
    tiles = cases // 8

    def step(index, _):
        plane, tile = index // tiles, index % tiles

        def emit(row, total):
            if not skip <= row < columns - skip:
                return
            for c, acc in enumerate((acc_s, acc_d)):
                for k in range(3):
                    lines = pl.ds(pl.multiple_of(k * cases + tile * 8, 8), 8)
                    low = plane * acc_columns + row - skip
                    acc[low, lines, :] += total[0][c][k] - total[1][c][k]
                    acc[low + acc_columns, lines, :] = total[0][c][k] + total[1][c][k]

        lower = x_modes(sums, diffs, plane, 0, tile, cases, columns)
        carry = None
        for row in range(rows):
            upper = x_modes(sums, diffs, plane, row + 1, tile, cases, columns)
            stiff = jnp.broadcast_to(
                stiff_ref[plane + stiff_x, pl.ds(row + stiff_y, 1), :], (8, LANES)
            )
            forces = mode_forces(modes_of(lower, upper), stiff)
            here = [[[None] * 3 for _ in range(2)] for _ in range(2)]
            following = [[[None] * 3 for _ in range(2)] for _ in range(2)]
            for a in range(2):
                for c in range(2):
                    for k in range(3):
                        one, two = forces[a][0][c][k], forces[a][1][c][k]
                        low = -two if one is None else one - two
                        high = two if one is None else one + two
                        here[a][c][k] = low if carry is None else carry[a][c][k] + low
                        following[a][c][k] = high
            emit(row, here)
            carry, lower = following, upper
        emit(rows, carry)
        return 0

    lax.fori_loop(0, planes * tiles, step, 0)


def fill(source, base, sizes, ref, xs, ys, code_xs, code_ys):
    planes, rows, cases = sizes
    block = 3 * cases
    line = 0
    for x in xs:
        start = (x * rows + ys[0]) * block
        count = len(ys) * block
        ref[line : line + count, :] = source[start : start + count, :]
        line += count
    for x in code_xs:
        start = base + x * rows + code_ys[0]
        ref[line : line + len(code_ys), :] = source[start : start + len(code_ys), :]
        line += len(code_ys)
    if line < ref.shape[0]:
        ref[line:, :] = jnp.zeros((ref.shape[0] - line, LANES), f32)


def pack_kernel(sizes, forces, codes, own, up, *down):
    planes, rows, cases = sizes
    block = 3 * cases
    base = planes * rows * block
    for x in range(planes):
        own[base + x * rows : base + (x + 1) * rows, :] = codes[x]
        scale = jnp.where(codes[x] > 0.0, LOAD, 0.0)
        for k in range(3):
            for c in range(cases):
                start = x * rows * block + k * cases + c
                own[pl.ds(start, rows, stride=block), :] = forces[k, c, x] * scale

    every_y, last = range(rows), (planes - 2, planes - 1)
    fill(own, base, sizes, up, last[1:], every_y, last, every_y)
    for ref in down:
        fill(own, base, sizes, ref, (0, 1), every_y, (0, 1), every_y)


def rows_kernel(sizes, own, ym, yp):
    planes, rows, cases = sizes
    base = planes * rows * 3 * cases
    every_x = range(planes)
    fill(own, base, sizes, ym, every_x, (0, 1), every_x, (0, 1))
    fill(own, base, sizes, yp, every_x, (rows - 1,), every_x, (rows - 2, rows - 1))


def corner_kernel(sizes, ym, yp, down, up):
    planes, rows, cases = sizes
    block = 3 * cases
    for ref, first, count in ((down, 0, 2), (up, planes - 1, 1)):
        line = 0
        for source, width in ((ym, 1), (yp, 2)):
            size = width * block
            ref[line : line + count * size, :] = source[first * size : (first + count) * size, :]
            line += count * size
            codes = planes * size + (first + count - 2) * 2
            ref[line : line + 4, :] = source[codes : codes + 4, :]
            ref[line + 4 : line + 8, :] = jnp.zeros((4, LANES), f32)
            line += 8


def readers(sizes, first, own, pair, lower, upper, y_own, y_pair, corner_low, corner_high):
    planes, rows, cases = sizes
    block = 3 * cases
    even = first // planes % 2 == 0

    def lines(ref, start, count):
        return ref[start : start + count, :]

    def inside(ref, x, y):
        return lines(ref, (x * rows + y) * block, block)

    def beyond(refs, slot, y):
        below, above = refs
        if y < 0:
            return lines(below, slot * block, block)
        return lines(above, (slot * 2 + y - rows) * block, block)

    def corner(ref, count, slot, y):
        if y < 0:
            return lines(ref, slot * block, block)
        return lines(ref, count * block + 8 + (slot * 2 + y - rows) * block, block)

    def corner_codes(ref, count, slot, y):
        start = count * block if y < 0 else 3 * count * block + 8
        return lines(ref, start + slot * 2, 2)

    def load(x, y):
        in_y = 0 <= y < rows
        if 0 <= x < planes:
            return inside(own, x, y) if in_y else beyond(y_own, x, y)
        if x < 0:
            if in_y:
                return jnp.where(even, inside(lower, 0, y), inside(pair, planes - 1, y))
            return jnp.where(even, corner(corner_low, 1, 0, y), beyond(y_pair, planes - 1, y))
        if in_y:
            return jnp.where(even, inside(pair, x - planes, y), inside(upper, x - planes, y))
        other = corner(corner_high, 2, x - planes, y)
        return jnp.where(even, beyond(y_pair, x - planes, y), other)

    def inside_codes(ref, x):
        return lines(ref, planes * rows * block + x * rows, rows)

    def beyond_codes(refs, slots, slot, y):
        below, above = refs
        if y < 0:
            return lines(below, slots * block + slot * 2, 2)
        return lines(above, slots * 2 * block + slot * 2, 2)

    def codes(x, y):
        if 0 <= x < planes:
            return inside_codes(own, x) if y == 0 else beyond_codes(y_own, planes, x, y)
        if x < 0:
            slot = x + 2
            if y == 0:
                other = inside_codes(pair, planes + x)
                return jnp.where(even, lines(lower, (block + slot) * rows, rows), other)
            other = beyond_codes(y_pair, planes, planes + x, y)
            return jnp.where(even, corner_codes(corner_low, 1, slot, y), other)
        slot = x - planes
        if y == 0:
            other = lines(upper, (2 * block + slot) * rows, rows)
            return jnp.where(even, inside_codes(pair, slot), other)
        other = corner_codes(corner_high, 2, slot, y)
        return jnp.where(even, beyond_codes(y_pair, planes, slot, y), other)

    return load, codes


def main_kernel(
    sizes, first, own, pair, lower, upper, ym, yp, ym_pair, yp_pair, corner_low, corner_high,
    both_out, system_out, stiff_ref, inverse,
    start, sums, diffs, acc_s, acc_d, w_sums, w_diffs, acc2_s, acc2_d, right, table,
):
    planes, rows, cases = sizes
    block = 3 * cases
    xs, ys = planes + 3, rows + 3
    load, signed = readers(
        sizes, first[0], own, pair, lower, upper,
        (ym, yp), (ym_pair, yp_pair), corner_low, corner_high,
    )
    for x in range(-2, planes + 2):
        for y, count in ((-2, 2), (0, rows), (rows, 2)):
            stiff_ref[x + 2, y + 2 : y + 2 + count, :] = signed(x, y)
    for x in range(-1, planes + 2):
        codes = stiff_ref[x + 2, 0 : ys + 1, :]
        total = jnp.abs(stiff_ref[x + 1, 0 : ys + 1, :]) + jnp.abs(codes)
        total = total[:-1] + total[1:]
        total = total + shift_up(total)
        free = codes[1:] > 0.0
        value = 1.0 / (DIAGONAL * jnp.where(free, total, 1.0))
        inverse[x + 1, 0:ys, :] = jnp.where(free, value, 0.0)
    for x in range(planes + 4):
        stiff_ref[x] = jnp.abs(stiff_ref[x])

    for x in range(-1, planes + 2):
        for y in range(-1, rows + 2):
            value = load(x, y) * inverse[x + 1, y + 1 : y + 2, :]
            column = (x + 1) * ys + y + 1
            start[column] = value
            moved = shift_down(value)
            sums[column] = value + moved
            diffs[column] = moved - value

    nodes_y = rows + 1
    apply_elements(
        sums, diffs, stiff_ref, acc_s, acc_d, planes + 2, rows + 2, 1, 1, 1, cases
    )

    def image(x, y, place):
        column = (x + 1) * nodes_y + y
        s, d = acc_s[column], acc_d[column]
        force = s - d + shift_up(s + d)
        scaled = force * inverse[x + 1, pl.ds(y + 1, 1), :]
        moved = shift_down(scaled)
        w_sums[x * nodes_y + y] = scaled + moved
        w_diffs[x * nodes_y + y] = moved - scaled
        value = start[(x + 1) * ys + y + 1]
        for k in range(3):
            lines = slice(k * cases, (k + 1) * cases)
            pair = jnp.concatenate([value[lines], scaled[lines]], 0)
            lane = pl.ds(pl.multiple_of((place * 3 + k) * LANES, LANES), LANES)
            high, rest = split(pair)
            both_out[0 : 2 * cases, lane] = high
            both_out[2 * cases : 4 * cases, lane] = rest
        return force

    two = 2 * cases
    count = planes * rows

    def inside(index):
        force = image(index // rows, index % rows, index)
        given = own[pl.ds(pl.multiple_of(index * block, 8), block), :]
        for k in range(3):
            lines = slice(k * cases, (k + 1) * cases)
            pair = jnp.concatenate([given[lines], force[lines]], 0)
            lane = pl.ds(pl.multiple_of((index * 3 + k) * LANES, LANES), LANES)
            high, rest = split(pair)
            right[0:two, lane] = high
            right[two : 2 * two, lane] = rest

    unrolled(count, 4, inside)
    unrolled(planes, 2, lambda x: image(x, rows, count + x))
    unrolled(nodes_y, 3, lambda y: image(planes, y, count + planes + y))
    beyond = right.shape[1] - count * 3 * LANES
    right[0 : 2 * two, count * 3 * LANES :] = jnp.zeros((2 * two, beyond), bf16)

    for column in range(nodes_y):
        acc2_s[column] = jnp.zeros((block, LANES), f32)
        acc2_d[column] = jnp.zeros((block, LANES), f32)
    apply_elements(w_sums, w_diffs, stiff_ref, acc2_s, acc2_d, planes, rows, 0, 2, 2, cases)

    def second_force(x, y, place):
        column = x * nodes_y + y
        s, d = acc2_s[column], acc2_d[column]
        force = s - d + shift_up(s + d)
        for k in range(3):
            value = force[k * cases : (k + 1) * cases]
            high = value.astype(bf16).astype(f32)
            lane = pl.ds(pl.multiple_of((place * 3 + k) * LANES, LANES), LANES)
            right[2 * two :, lane] = jnp.concatenate([high, value - high], 0).astype(bf16)

    unrolled(count, 4, lambda index: second_force(index // rows, index % rows, index))
    unrolled(planes, 2, lambda x: second_force(x, rows, count + x))
    unrolled(nodes_y, 3, lambda y: second_force(planes, y, count + planes + y))

    contract = (((1,), (1,)), ((), ()))
    product = lax.dot_general(both_out[...], right[...], contract, preferred_element_type=f32)
    product = product[:two] + product[two:]
    gram = product[:, :two] + product[:, two : 2 * two]
    other = product[:, 2 * two : 2 * two + cases] + product[:, 2 * two + cases :]
    row = lax.broadcasted_iota(jnp.int32, (cases, cases), 0)
    column = lax.broadcasted_iota(jnp.int32, (cases, cases), 1)
    load_load, load_image = gram[:cases, :cases], gram[:cases, cases:]
    mixed, image_image = other[:cases], other[cases:]
    table[...] = jnp.zeros(table.shape, f32)
    table[:, 0:cases] = jnp.where(row <= column, load_load, load_image)
    table[:, cases:two] = jnp.where(row <= column, mixed, image_image)
    for lane, value in ((two, load_image), (two + 1, image_image)):
        own_entries = jnp.where(row == column, value, 0.0)
        table[:, lane : lane + 1] = jnp.sum(own_entries, axis=1, keepdims=True)
    half = cases // 2
    folded = table[:half, :] + pltpu.roll(table[half:, :], LANES // 2, 1)
    depth = system_out.shape[2]
    for index in range(system_out.shape[0]):
        for part in range(half // depth):
            system_out[index, part] = folded[part * depth : (part + 1) * depth]


def solve_kernel(
    sizes, system, system_pair, both, codes, out, mixing, sums, diffs, energy, square, full
):
    planes, rows, cases = sizes
    two = 2 * cases
    nodes_y = rows + 1
    count = planes * rows
    total = jnp.sum(system[...], axis=0) + jnp.sum(system_pair[...], axis=0)
    half, depth = cases // 2, system.shape[2]
    square[...] = jnp.zeros(square.shape, f32)
    for part in range(half // depth):
        value = total[part]
        square[part * depth : (part + 1) * depth, :] = value
        lines = slice(half + part * depth, half + (part + 1) * depth)
        square[lines, :] = pltpu.roll(value, LANES // 2, 1)
    value, turned = square[0:cases, :], jnp.transpose(square[...])
    line = lax.broadcasted_iota(jnp.int32, (cases, cases), 0)
    place = lax.broadcasted_iota(jnp.int32, (cases, cases), 1)

    def mended(start, diagonal=None):
        kept, other = value[:, start : start + cases], turned[start : start + cases, :cases]
        if diagonal is None:
            return jnp.where(line <= place, kept, other)
        inner = jnp.where(line < place, other, value[:, diagonal : diagonal + 1])
        return jnp.where(line > place, kept, inner)

    load_image, mixed = mended(0, two), mended(cases)
    parts = ((load_image, mixed), (mixed, mended(cases, two + 1)), (mended(0), load_image))
    full[...] = jnp.zeros(full.shape, f32)
    for index, (left, right) in enumerate(parts):
        full[index * cases : (index + 1) * cases, 0:cases] = left
        full[index * cases : (index + 1) * cases, cases:two] = right
    table = full[...]
    lane = lax.broadcasted_iota(jnp.int32, (1, LANES), 1)
    gone, wide = 0, 4
    for pivot in range(0, two, wide):
        drop = pivot // 8 * 8 - gone
        table = table[drop:]
        gone += drop
        line = pivot - gone
        inner = (lane >= pivot) & (lane < pivot + wide)
        found = [table[line + p : line + p + 1, :] for p in range(wide)]
        block = [
            [jnp.broadcast_to(row[:, pivot + q : pivot + q + 1], row.shape) for q in range(wide)]
            for row in found
        ]
        solved = [
            jnp.where(lane == pivot + p, -1.0, jnp.where(inner, 0.0, found[p]))
            for p in range(wide)
        ]
        for p in range(wide):
            inverse = 1.0 / block[p][p]
            solved[p] = solved[p] * inverse
            block[p] = [value * inverse for value in block[p]]
            for q in range(wide):
                if q != p:
                    factor = block[q][p]
                    solved[q] = solved[q] - factor * solved[p]
                    for r in range(p + 1, wide):
                        block[q][r] = block[q][r] - factor * block[p][r]
        update = None
        for q in range(wide):
            term = table[:, pivot + q : pivot + q + 1] * solved[q]
            update = term if update is None else update + term
        table = jnp.where(inner, 0.0, table) - update
    answer = table[two - gone :, :two]
    high = answer.astype(bf16).astype(f32)
    mixing[...] = jnp.zeros(mixing.shape, f32)
    mixing[0:cases, 0:two] = high
    mixing[0:cases, two : 2 * two] = high
    mixing[cases:two, 0:two] = answer - high
    mix = mixing[...][:, : 2 * two].astype(bf16)

    def combined(place, width):
        lanes = pl.ds(pl.multiple_of(place * 3 * LANES, LANES), width * 3 * LANES)
        value = jnp.dot(mix, both[:, lanes], preferred_element_type=f32)
        return value[:cases] + value[cases:]

    def keep(value, index, column):
        for k in range(3):
            part = value[:, (index * 3 + k) * LANES : (index * 3 + k + 1) * LANES]
            moved = shift_down(part)
            sums[column, k * cases : (k + 1) * cases, :] = part + moved
            diffs[column, k * cases : (k + 1) * cases, :] = moved - part

    def inside(x, _):
        value = combined(x * rows, rows)
        for y in range(rows):
            keep(value, y, x * nodes_y + y)
        return 0

    lax.fori_loop(0, planes, inside, 0)
    value = combined(count, planes + nodes_y)
    for x in range(planes):
        keep(value, x, x * nodes_y + rows)
    for y in range(nodes_y):
        keep(value, planes + y, planes * nodes_y + y)

    tiles = cases // 8

    def step(plane, _):
        for tile in range(tiles):
            lower = x_modes(sums, diffs, plane, 0, tile, cases, nodes_y)
            for row in range(rows):
                upper = x_modes(sums, diffs, plane, row + 1, tile, cases, nodes_y)
                part = mode_energy(modes_of(lower, upper))
                if tile == 0:
                    energy[row] = part
                else:
                    energy[row] += part
                lower = upper
        total = jnp.sum(energy[...], axis=1)
        total = (-3.0 / cases) * jnp.abs(codes[plane]) * total
        for index in range(out.shape[0]):
            out[index, plane] = total
        return 0

    lax.fori_loop(0, planes, step, 0)


def smooth(ref, x, rows):
    weight = [2.5 - math.sqrt(q) for q in range(7)]
    near = {}
    for dx in range(-2, 3):
        for dy in range(-2, 3):
            q = dx * dx + dy * dy
            if q <= 5:
                value = ref[x + 2 + dx, 2 + dy : 2 + dy + rows, :]
                near[q] = value if q not in near else near[q] + value
    result = None
    for dz in range(3):
        part = None
        for q, value in near.items():
            if q + dz * dz <= 6:
                term = weight[q + dz * dz] * value
                part = term if part is None else part + term
        if dz == 0:
            result = part
        else:
            place = lax.broadcasted_iota(jnp.int32, part.shape, 1)
            forward = jnp.where(place >= LANES - dz, 0.0, pltpu.roll(part, LANES - dz, 1))
            backward = jnp.where(place < dz, 0.0, pltpu.roll(part, dz, 1))
            result = result + (forward + backward)
    return result


def scale_kernel(sizes, counts, start, levels, out, there):
    planes, rows, _ = sizes
    y = lax.broadcasted_iota(jnp.int32, (rows + 4, LANES), 0) + (start[1] - 2)
    in_y = (y >= 0) & (y < counts[1] * rows)
    for x in range(planes + 4):
        global_x = start[0] + (x - 2)
        in_x = (global_x >= 0) & (global_x < counts[0] * planes)
        there[x] = jnp.where(in_y & in_x, 1.0, 0.0)
    for x in range(planes):
        density = 0.3 + 0.7 * levels[x].astype(f32) / (LEVELS - 1)
        out[x] = 1.0 / (density * smooth(there, x, rows))


def filter_kernel(sizes, counts, start, blocks, blocks_pair, scale, out, wide):
    planes, rows, _ = sizes
    sides_x = ((-1, planes - 2, planes, 0), (0, 0, planes, 2), (1, 0, 2, 2 + planes))
    sides_y = ((-1, rows - 2, rows, 0), (0, 0, rows, 2), (1, 0, 2, 2 + rows))
    for step_x, x0, x1, to_x in sides_x:
        for step_y, y0, y1, to_y in sides_y:
            at_x = start[0] // planes + step_x
            at_y = start[1] // rows + step_y
            inside = (at_x >= 0) & (at_x < counts[0]) & (at_y >= 0) & (at_y < counts[1])
            index = jnp.where(inside, at_x // 2 * counts[1] + at_y, 0)
            value = (blocks_pair if step_x else blocks)[index, x0:x1, y0:y1, :]
            wide[to_x : to_x + x1 - x0, to_y : to_y + y1 - y0, :] = jnp.where(inside, value, 0.0)
    for x in range(planes):
        out[x] = smooth(wide, x, rows) * scale[x]


def local(forces, levels, supports):
    _, cases, planes, rows, _ = forces.shape
    sizes = (planes, rows, cases)
    block = 3 * cases
    count_x, count_y = lax.axis_size("gx"), lax.axis_size("gy")

    def shape(blocks, codes):
        return jax.ShapeDtypeStruct((blocks * block + up8(codes), LANES), f32)

    density = 0.3 + 0.7 * levels.astype(f32) / (LEVELS - 1)
    codes = density * density * density
    codes = jnp.where(supports == 0, codes, -codes)
    whole = shape(planes * rows, planes * rows)
    down = [] if planes == 2 else [shape(2 * rows, 2 * rows)]
    own, up, *down = pl.pallas_call(
        functools.partial(pack_kernel, sizes),
        out_shape=[whole, shape(rows, 2 * rows), *down],
        in_specs=[VMEM] * 2,
        out_specs=[VMEM] * (2 + len(down)),
        compiler_params=PARAMS,
        name="pack",
    )(forces, codes)

    start = jnp.stack([lax.axis_index("gx") * planes, lax.axis_index("gy") * rows])
    start = start.astype(jnp.int32)
    counts = (count_x, count_y)
    scalars = pl.BlockSpec(memory_space=pltpu.SMEM)
    scale = pl.pallas_call(
        functools.partial(scale_kernel, sizes, counts),
        out_shape=jax.ShapeDtypeStruct((planes, rows, LANES), f32),
        in_specs=[scalars, VMEM],
        out_specs=VMEM,
        scratch_shapes=[pltpu.VMEM((planes + 4, rows + 4, LANES), f32)],
        compiler_params=PARAMS,
        name="scale",
    )(start, levels)

    def moved(value, axis, step):
        count = lax.axis_size(axis)
        pairs = [(i, i + step) for i in range(count) if 0 <= i + step < count]
        return lax.ppermute(value, axis, pairs)

    def links(first, step):
        return [(i, i + step) for i in range(first, count_x, 2) if 0 <= i + step < count_x]

    def swapped(value):
        return lax.ppermute(value, "gx", links(0, 1) + links(1, -1))

    upper = lax.ppermute(down[0] if down else own, "gx", links(2, -1))
    lower = lax.ppermute(up, "gx", links(1, 1))
    pair = swapped(own)
    own, pair = lax.optimization_barrier((own, pair))
    ym, yp = pl.pallas_call(
        functools.partial(rows_kernel, sizes),
        out_shape=[shape(2 * planes, 2 * planes), shape(planes, 2 * planes)],
        in_specs=[VMEM],
        out_specs=[VMEM] * 2,
        compiler_params=PARAMS,
        name="rows",
    )(own)
    from_yp, from_ym = moved(ym, "gy", -1), moved(yp, "gy", 1)
    pair_yp, pair_ym = swapped(from_yp), swapped(from_ym)
    corner_down, corner_up = pl.pallas_call(
        functools.partial(corner_kernel, sizes),
        out_shape=[
            jax.ShapeDtypeStruct((6 * block + 16, LANES), f32),
            jax.ShapeDtypeStruct((3 * block + 16, LANES), f32),
        ],
        in_specs=[VMEM] * 2,
        out_specs=[VMEM] * 2,
        compiler_params=PARAMS,
        name="corners",
    )(from_ym, from_yp)
    corner_high = lax.ppermute(corner_down, "gx", links(2, -1))
    corner_low = lax.ppermute(corner_up, "gx", links(1, 1))

    devices = count_x * count_y
    nodes = (planes + 1) * (rows + 1)
    wide = (planes + 3) * (rows + 3)
    acc = pltpu.VMEM(((planes + 3) * (rows + 1), block, LANES), f32)
    field = pltpu.VMEM((nodes, block, LANES), f32)
    both, system = pl.pallas_call(
        functools.partial(main_kernel, sizes),
        out_shape=[
            jax.ShapeDtypeStruct((4 * cases, nodes * 3 * LANES), bf16),
            jax.ShapeDtypeStruct((devices // 2, cases // 8, 4, LANES), f32),
        ],
        in_specs=[scalars] + [VMEM] * 10,
        out_specs=[VMEM] * 2,
        scratch_shapes=[
            pltpu.VMEM((planes + 4, up8(rows + 4), LANES), f32),
            pltpu.VMEM((planes + 3, up8(rows + 3), LANES), f32),
            pltpu.VMEM((wide, block, LANES), f32),
            pltpu.VMEM((wide, block, LANES), f32),
            pltpu.VMEM((wide, block, LANES), f32),
            acc, acc, field, field, field, field,
            pltpu.VMEM((6 * cases, nodes * 3 * LANES), bf16),
            pltpu.VMEM((cases, LANES), f32),
        ],
        compiler_params=PARAMS,
        name="operator",
    )(
        start, own, pair, lower, upper, from_ym, from_yp,
        pair_ym, pair_yp, corner_low, corner_high,
    )

    groups = [
        [x * count_y + y for x in range(side, count_x, 2) for y in range(count_y)]
        for side in range(2)
    ]

    def gathered(copies):
        mine = lax.all_to_all(copies, ("gx", "gy"), 0, 0, axis_index_groups=groups)
        return mine, swapped(mine)

    system = gathered(system)

    weighted = pl.pallas_call(
        functools.partial(solve_kernel, sizes),
        out_shape=jax.ShapeDtypeStruct((devices // 2, planes, rows, LANES), f32),
        in_specs=[VMEM] * 4,
        out_specs=VMEM,
        scratch_shapes=[
            pltpu.VMEM((2 * cases, LANES), f32),
            field,
            field,
            pltpu.VMEM((rows, 8, LANES), f32),
            pltpu.VMEM((LANES, LANES), f32),
            pltpu.VMEM((3 * cases, LANES), f32),
        ],
        compiler_params=PARAMS,
        name="solve",
    )(*system, both, codes)

    blocks = gathered(weighted)
    return pl.pallas_call(
        functools.partial(filter_kernel, sizes, counts),
        out_shape=jax.ShapeDtypeStruct((planes, rows, LANES), f32),
        in_specs=[scalars] + [VMEM] * 3,
        out_specs=VMEM,
        scratch_shapes=[pltpu.VMEM((planes + 4, rows + 4, LANES), f32)],
        compiler_params=PARAMS,
        name="cone",
    )(start, *blocks, scale)


def solution(mesh):
    return jax.shard_map(
        local,
        mesh=mesh,
        in_specs=(P(None, None, "gx", "gy", None), P("gx", "gy", None), P("gx", "gy", None)),
        out_specs=P("gx", "gy", None),
        check_vma=False,
    )
```

```python
import functools
import math

import jax
import jax.numpy as jnp
from jax import lax
from jax.experimental import pallas as pl
from jax.experimental.pallas import tpu as pltpu
from jax.sharding import PartitionSpec as P

LEVELS = 16
LOAD = 0.2
LANES = 128
POISSON = 0.3
LAME = POISSON / ((1.0 + POISSON) * (1.0 - 2.0 * POISSON))
SHEAR = 1.0 / (2.0 * (1.0 + POISSON))
DIAGONAL = (LAME + 2.0 * SHEAR) / 9.0 + 2.0 * SHEAR / 9.0
VMEM = pl.BlockSpec(memory_space=pltpu.VMEM)
PARAMS = pltpu.CompilerParams(vmem_limit_bytes=30 * 2**20)
f32 = jnp.float32
bf16 = jnp.bfloat16


def up8(count):
    return -(-count // 8) * 8


def shift_down(value):
    lane = lax.broadcasted_iota(jnp.int32, value.shape, value.ndim - 1)
    rolled = pltpu.roll(value, LANES - 1, value.ndim - 1)
    return jnp.where(lane == LANES - 1, 0.0, rolled)


def shift_up(value):
    lane = lax.broadcasted_iota(jnp.int32, value.shape, value.ndim - 1)
    return jnp.where(lane == 0, 0.0, pltpu.roll(value, 1, value.ndim - 1))


def unrolled(count, factor, body):
    def turn(step, _):
        for offset in range(factor):
            body(step * factor + offset)
        return 0

    turns = count // factor
    if turns:
        lax.fori_loop(0, turns, turn, 0)
    for index in range(turns * factor, count):
        body(index)


def split(value):
    high = value.astype(bf16)
    return high, (value - high.astype(f32)).astype(bf16)


def modes_of(lower, upper):
    out = [[[[None] * 3 for _ in range(2)] for _ in range(2)] for _ in range(2)]
    for a in range(2):
        for c in range(2):
            for k in range(3):
                if a or c:
                    out[a][0][c][k] = lower[a][c][k] + upper[a][c][k]
                out[a][1][c][k] = upper[a][c][k] - lower[a][c][k]
    return out


PAIRS = (((1, 1, 0, 0), (0, 1, 1, 2)), ((1, 0, 1, 0), (0, 1, 1, 1)), ((1, 1, 0, 1), (1, 0, 1, 2)))
TRIPLE = ((0, 1, 1, 0), (1, 0, 1, 1), (1, 1, 0, 2))
SHEARS = (((0, 1, 0, 0), (1, 0, 0, 1)), ((0, 0, 1, 0), (1, 0, 0, 2)), ((0, 0, 1, 1), (0, 1, 0, 2)))
AXIAL = ((1, 0, 0, 0), (0, 1, 0, 1), (0, 0, 1, 2))


def at(modes, place):
    a, b, c, k = place
    return modes[a][b][c][k]


def mode_forces(modes, stiff):
    out = [[[[None] * 3 for _ in range(2)] for _ in range(2)] for _ in range(2)]

    def put(place, value):
        a, b, c, k = place
        out[a][b][c][k] = value

    shear = stiff * (SHEAR / 16)
    for first, second in SHEARS:
        force = shear * (at(modes, first) + at(modes, second))
        put(first, force)
        put(second, force)
    one, two, three = (at(modes, place) for place in AXIAL)
    volume = (stiff * (LAME / 16)) * (one + two + three)
    axial = stiff * (SHEAR / 8)
    for place in AXIAL:
        put(place, volume + axial * at(modes, place))
    own, cross = stiff * ((LAME + 3 * SHEAR) / 48), stiff * (LAME / 48)
    for first, second in PAIRS:
        one, two = at(modes, first), at(modes, second)
        put(first, own * one + cross * two)
        put(second, own * two + cross * one)
    twist = stiff * (SHEAR / 48)
    one, two, three = (at(modes, place) for place in TRIPLE)
    total = one + two + three
    for place in TRIPLE:
        put(place, twist * (total + at(modes, place)))
    last = stiff * ((LAME + 4 * SHEAR) / 144)
    for k in range(3):
        put((1, 1, 1, k), last * modes[1][1][1][k])
    return out


def mode_energy(modes):
    def square(value):
        return value * value

    shear = None
    for first, second in SHEARS:
        term = square(at(modes, first) + at(modes, second))
        shear = term if shear is None else shear + term
    one, two, three = (at(modes, place) for place in AXIAL)
    energy = (SHEAR / 16) * shear + (LAME / 16) * square(one + two + three)
    energy = energy + (SHEAR / 8) * (square(one) + square(two) + square(three))
    squares, products = None, None
    for first, second in PAIRS:
        one, two = at(modes, first), at(modes, second)
        term, product = square(one) + square(two), one * two
        squares = term if squares is None else squares + term
        products = product if products is None else products + product
    energy = energy + ((LAME + 3 * SHEAR) / 48) * squares + (LAME / 24) * products
    one, two, three = (at(modes, place) for place in TRIPLE)
    twist = square(one + two + three) + square(one) + square(two) + square(three)
    energy = energy + (SHEAR / 48) * twist
    last = square(modes[1][1][1][0]) + square(modes[1][1][1][1]) + square(modes[1][1][1][2])
    return energy + ((LAME + 4 * SHEAR) / 144) * last


def x_modes(sums, diffs, plane, row, tile, cases, columns):
    out = [[[None] * 3 for _ in range(2)] for _ in range(2)]
    for c, ref in enumerate((sums, diffs)):
        for k in range(3):
            rows = pl.ds(pl.multiple_of(k * cases + tile * 8, 8), 8)
            one = ref[plane * columns + row, rows, :]
            two = ref[(plane + 1) * columns + row, rows, :]
            out[0][c][k] = one + two
            out[1][c][k] = two - one
    return out


def apply_elements(
    sums, diffs, stiff_ref, acc_s, acc_d, planes, rows, skip, stiff_x, stiff_y, cases
):
    columns = rows + 1
    acc_columns = columns - 2 * skip
    tiles = cases // 8

    def step(index, _):
        plane, tile = index // tiles, index % tiles

        def emit(row, total):
            if not skip <= row < columns - skip:
                return
            for c, acc in enumerate((acc_s, acc_d)):
                for k in range(3):
                    lines = pl.ds(pl.multiple_of(k * cases + tile * 8, 8), 8)
                    low = plane * acc_columns + row - skip
                    acc[low, lines, :] += total[0][c][k] - total[1][c][k]
                    acc[low + acc_columns, lines, :] = total[0][c][k] + total[1][c][k]

        lower = x_modes(sums, diffs, plane, 0, tile, cases, columns)
        carry = None
        for row in range(rows):
            upper = x_modes(sums, diffs, plane, row + 1, tile, cases, columns)
            stiff = jnp.broadcast_to(
                stiff_ref[plane + stiff_x, pl.ds(row + stiff_y, 1), :], (8, LANES)
            )
            forces = mode_forces(modes_of(lower, upper), stiff)
            here = [[[None] * 3 for _ in range(2)] for _ in range(2)]
            following = [[[None] * 3 for _ in range(2)] for _ in range(2)]
            for a in range(2):
                for c in range(2):
                    for k in range(3):
                        one, two = forces[a][0][c][k], forces[a][1][c][k]
                        low = -two if one is None else one - two
                        high = two if one is None else one + two
                        here[a][c][k] = low if carry is None else carry[a][c][k] + low
                        following[a][c][k] = high
            emit(row, here)
            carry, lower = following, upper
        emit(rows, carry)
        return 0

    lax.fori_loop(0, planes * tiles, step, 0)


def fill(source, base, sizes, ref, xs, ys, code_xs, code_ys):
    planes, rows, cases = sizes
    block = 3 * cases
    line = 0
    for x in xs:
        start = (x * rows + ys[0]) * block
        count = len(ys) * block
        ref[line : line + count, :] = source[start : start + count, :]
        line += count
    for x in code_xs:
        start = base + x * rows + code_ys[0]
        ref[line : line + len(code_ys), :] = source[start : start + len(code_ys), :]
        line += len(code_ys)
    if line < ref.shape[0]:
        ref[line:, :] = jnp.zeros((ref.shape[0] - line, LANES), f32)


def pack_kernel(sizes, forces, codes, own, up, *down):
    planes, rows, cases = sizes
    block = 3 * cases
    base = planes * rows * block
    for x in range(planes):
        own[base + x * rows : base + (x + 1) * rows, :] = codes[x]
        scale = jnp.where(codes[x] > 0.0, LOAD, 0.0)
        for k in range(3):
            for c in range(cases):
                start = x * rows * block + k * cases + c
                own[pl.ds(start, rows, stride=block), :] = forces[k, c, x] * scale

    every_y, last = range(rows), (planes - 2, planes - 1)
    fill(own, base, sizes, up, last[1:], every_y, last, every_y)
    for ref in down:
        fill(own, base, sizes, ref, (0, 1), every_y, (0, 1), every_y)


def rows_kernel(sizes, own, ym, yp):
    planes, rows, cases = sizes
    base = planes * rows * 3 * cases
    every_x = range(planes)
    fill(own, base, sizes, ym, every_x, (0, 1), every_x, (0, 1))
    fill(own, base, sizes, yp, every_x, (rows - 1,), every_x, (rows - 2, rows - 1))


def corner_kernel(sizes, ym, yp, down, up):
    planes, rows, cases = sizes
    block = 3 * cases
    for ref, first, count in ((down, 0, 2), (up, planes - 1, 1)):
        line = 0
        for source, width in ((ym, 1), (yp, 2)):
            size = width * block
            ref[line : line + count * size, :] = source[first * size : (first + count) * size, :]
            line += count * size
            codes = planes * size + (first + count - 2) * 2
            ref[line : line + 4, :] = source[codes : codes + 4, :]
            ref[line + 4 : line + 8, :] = jnp.zeros((4, LANES), f32)
            line += 8


def lines(ref, start, count):
    return ref[start : start + count, :]


def inside(ref, x, y, rows, block):
    return lines(ref, (x * rows + y) * block, block)


def beyond(refs, slot, y, rows, block):
    below, above = refs
    if y < 0:
        return lines(below, slot * block, block)
    return lines(above, (slot * 2 + y - rows) * block, block)


def beyond_codes(refs, slots, slot, y, block):
    below, above = refs
    if y < 0:
        return lines(below, slots * block + slot * 2, 2)
    return lines(above, slots * 2 * block + slot * 2, 2)


def corner(ref, count, slot, y, rows, block):
    if y < 0:
        return lines(ref, slot * block, block)
    return lines(ref, count * block + 8 + (slot * 2 + y - rows) * block, block)


def corner_codes(ref, count, slot, y, block):
    start = count * block if y < 0 else 3 * count * block + 8
    return lines(ref, start + slot * 2, 2)


def node_inverse(signed, count, out):
    planes = signed.shape[0]
    for x in range(1, planes):
        codes = signed[x, 0 : count + 1, :]
        total = jnp.abs(signed[x - 1, 0 : count + 1, :]) + jnp.abs(codes)
        total = total[:-1] + total[1:]
        total = total + shift_up(total)
        free = codes[1:] > 0.0
        value = 1.0 / (DIAGONAL * jnp.where(free, total, 1.0))
        out[x - 1, 0:count, :] = jnp.where(free, value, 0.0)
    for x in range(planes):
        signed[x] = jnp.abs(signed[x])


def place_column(sums, diffs, column, value):
    moved = shift_down(value)
    sums[column] = value + moved
    diffs[column] = moved - value


def early_kernel(
    sizes, first, own, pair, ym, yp, ym_pair, yp_pair, start, sums, diffs, acc_s, acc_d,
    stiff_ref, inverse,
):
    planes, rows, cases = sizes
    block = 3 * cases
    ys = rows + 3
    even = first[0] // planes % 2 == 0
    y_own, y_pair = (ym, yp), (ym_pair, yp_pair)

    def both_ways(w, read):
        low = read(True, w + 1) if w + 1 < planes else read(False, w + 1 - planes)
        high = read(False, planes + w - 1) if w < 1 else read(True, w - 1)
        return jnp.where(even, low, high)

    def codes(w, y):
        def read(mine, x):
            if y == 0:
                return lines(own if mine else pair, (planes * block + x) * rows, rows)
            return beyond_codes(y_own if mine else y_pair, planes, x, y, block)

        return both_ways(w, read)

    for w in range(-1, planes + 1):
        for y, count in ((-2, 2), (0, rows), (rows, 2)):
            stiff_ref[w + 1, y + 2 : y + 2 + count, :] = codes(w, y)
    node_inverse(stiff_ref, ys, inverse)
    for w in range(planes + 1):
        for y in range(-1, rows + 2):

            def read(mine, x):
                if 0 <= y < rows:
                    return inside(own if mine else pair, x, y, rows, block)
                return beyond(y_own if mine else y_pair, x, y, rows, block)

            value = both_ways(w, read) * inverse[w, y + 1 : y + 2, :]
            column = w * ys + y + 1
            start[column] = value
            place_column(sums, diffs, column, value)
    for column in range(rows + 1):
        acc_s[column] = jnp.zeros((block, LANES), f32)
        acc_d[column] = jnp.zeros((block, LANES), f32)
    apply_elements(sums, diffs, stiff_ref, acc_s, acc_d, planes, rows + 2, 1, 1, 1, cases)


def main_kernel(
    sizes, first, own, pair, lower, upper, ym, yp, ym_pair, yp_pair, corner_low, corner_high,
    start, sums_e, diffs_e, acc_se, acc_de,
    both_out, system_out, stiff_ref, inverse,
    middle, sums, diffs, acc_s, acc_d, w_sums, w_diffs, acc2_s, acc2_d, right, table,
):
    planes, rows, cases = sizes
    block = 3 * cases
    ys = rows + 3
    even = first[0] // planes % 2 == 0
    y_own, y_pair = (ym, yp), (ym_pair, yp_pair)

    def codes(x, y):
        def read(mine, plane):
            if y == 0:
                return lines(own if mine else pair, (planes * block + plane) * rows, rows)
            return beyond_codes(y_own if mine else y_pair, planes, plane, y, block)

        if 0 <= x < planes:
            return read(True, x)
        ref, count, slot = (lower, 1, x + 2) if x < 0 else (upper, 2, x - planes)
        if y == 0:
            outer = lines(ref, (count * block + slot) * rows, rows)
        else:
            outer = corner_codes(corner_low if x < 0 else corner_high, count, slot, y, block)
        inner = read(False, planes + x if x < 0 else x - planes)
        return jnp.where(even, outer, inner) if x < 0 else jnp.where(even, inner, outer)

    for x in range(-2, planes + 2):
        for y, count in ((-2, 2), (0, rows), (rows, 2)):
            stiff_ref[x + 2, y + 2 : y + 2 + count, :] = codes(x, y)
    node_inverse(stiff_ref, ys, inverse)

    def place(v, x, read):
        for y in range(-1, rows + 2):
            value = read(y) * inverse[x + 1, y + 1 : y + 2, :]
            if v == 1:
                middle[y + 1] = value
            place_column(sums, diffs, v * ys + y + 1, value)

    def copy(v, w):
        for y in range(ys):
            sums[v * ys + y] = sums_e[w * ys + y]
            diffs[v * ys + y] = diffs_e[w * ys + y]

    @pl.when(even)
    def _():
        def outer(y):
            if 0 <= y < rows:
                return inside(lower, 0, y, rows, block)
            return corner(corner_low, 1, 0, y, rows, block)

        def inner(y):
            if 0 <= y < rows:
                return inside(own, 0, y, rows, block)
            return beyond(y_own, 0, y, rows, block)

        place(0, -1, outer)
        place(1, 0, inner)
        copy(2, 0)

    @pl.when(jnp.logical_not(even))
    def _():
        def outer(slot):
            def read(y):
                if 0 <= y < rows:
                    return inside(upper, slot, y, rows, block)
                return corner(corner_high, 2, slot, y, rows, block)

            return read

        copy(0, planes)
        place(1, planes, outer(0))
        place(2, planes + 1, outer(1))

    nodes_y = rows + 1
    for column in range(nodes_y):
        acc_s[column] = jnp.zeros((block, LANES), f32)
        acc_d[column] = jnp.zeros((block, LANES), f32)
    layer = jnp.where(even, 1, planes + 1)
    apply_elements(sums, diffs, stiff_ref, acc_s, acc_d, 2, rows + 2, 1, layer, 1, cases)

    def total(x, y, early, main):
        low = ([x - 1] if x >= 1 else [], [x + 1] if x <= 1 else [])
        high = ([x + 1] if x < planes else [], [x - planes + 1] if x >= planes - 1 else [])
        if low[0] and low[1] and high[0] and high[1]:
            one = early[jnp.where(even, low[0][0], high[0][0]) * nodes_y + y]
            return one + main[jnp.where(even, low[1][0], high[1][0]) * nodes_y + y]

        def read(places):
            found = [early[w * nodes_y + y] for w in places[0]]
            found += [main[v * nodes_y + y] for v in places[1]]
            return found[0] if len(found) == 1 else found[0] + found[1]

        return jnp.where(even, read(low), read(high))

    def image(x, y, place):
        s, d = total(x, y, acc_se, acc_s), total(x, y, acc_de, acc_d)
        force = s - d + shift_up(s + d)
        scaled = force * inverse[x + 1, pl.ds(y + 1, 1), :]
        place_column(w_sums, w_diffs, x * nodes_y + y, scaled)
        if x == 0:
            value = jnp.where(even, middle[y + 1], start[ys + y + 1])
        elif x == planes:
            value = jnp.where(even, start[(planes - 1) * ys + y + 1], middle[y + 1])
        else:
            value = start[jnp.where(even, x - 1, x + 1) * ys + y + 1]
        for k in range(3):
            lines = slice(k * cases, (k + 1) * cases)
            both = jnp.concatenate([value[lines], scaled[lines]], 0)
            lane = pl.ds(pl.multiple_of((place * 3 + k) * LANES, LANES), LANES)
            high, rest = split(both)
            both_out[0 : 2 * cases, lane] = high
            both_out[2 * cases : 4 * cases, lane] = rest
        return force

    two = 2 * cases
    count = planes * rows

    def within(x, y):
        index = x * rows + y
        force = image(x, y, index)
        given = own[pl.ds(pl.multiple_of(index * block, 8), block), :]
        for k in range(3):
            lines = slice(k * cases, (k + 1) * cases)
            both = jnp.concatenate([given[lines], force[lines]], 0)
            lane = pl.ds(pl.multiple_of((index * 3 + k) * LANES, LANES), LANES)
            high, rest = split(both)
            right[0:two, lane] = high
            right[two : 2 * two, lane] = rest

    for x in range(planes):
        unrolled(rows, 4, functools.partial(within, x))
        image(x, rows, count + x)
    unrolled(nodes_y, 3, lambda y: image(planes, y, count + planes + y))
    rest = right.shape[1] - count * 3 * LANES
    right[0 : 2 * two, count * 3 * LANES :] = jnp.zeros((2 * two, rest), bf16)

    for column in range(nodes_y):
        acc2_s[column] = jnp.zeros((block, LANES), f32)
        acc2_d[column] = jnp.zeros((block, LANES), f32)
    apply_elements(w_sums, w_diffs, stiff_ref, acc2_s, acc2_d, planes, rows, 0, 2, 2, cases)

    def second_force(x, y, place):
        column = x * nodes_y + y
        s, d = acc2_s[column], acc2_d[column]
        force = s - d + shift_up(s + d)
        for k in range(3):
            value = force[k * cases : (k + 1) * cases]
            high = value.astype(bf16).astype(f32)
            lane = pl.ds(pl.multiple_of((place * 3 + k) * LANES, LANES), LANES)
            right[2 * two :, lane] = jnp.concatenate([high, value - high], 0).astype(bf16)

    unrolled(count, 4, lambda index: second_force(index // rows, index % rows, index))
    unrolled(planes, 2, lambda x: second_force(x, rows, count + x))
    unrolled(nodes_y, 3, lambda y: second_force(planes, y, count + planes + y))

    contract = (((1,), (1,)), ((), ()))
    product = lax.dot_general(both_out[...], right[...], contract, preferred_element_type=f32)
    product = product[:two] + product[two:]
    gram = product[:, :two] + product[:, two : 2 * two]
    other = product[:, 2 * two : 2 * two + cases] + product[:, 2 * two + cases :]
    row = lax.broadcasted_iota(jnp.int32, (cases, cases), 0)
    column = lax.broadcasted_iota(jnp.int32, (cases, cases), 1)
    load_load, load_image = gram[:cases, :cases], gram[:cases, cases:]
    mixed, image_image = other[:cases], other[cases:]
    table[...] = jnp.zeros(table.shape, f32)
    table[:, 0:cases] = jnp.where(row <= column, load_load, load_image)
    table[:, cases:two] = jnp.where(row <= column, mixed, image_image)
    for lane, value in ((two, load_image), (two + 1, image_image)):
        own_entries = jnp.where(row == column, value, 0.0)
        table[:, lane : lane + 1] = jnp.sum(own_entries, axis=1, keepdims=True)
    half = cases // 2
    folded = table[:half, :] + pltpu.roll(table[half:, :], LANES // 2, 1)
    depth = system_out.shape[2]
    for index in range(system_out.shape[0]):
        for part in range(half // depth):
            system_out[index, part] = folded[part * depth : (part + 1) * depth]


def solve_kernel(
    sizes, system, system_pair, both, codes, out, mixing, sums, diffs, energy, square, full
):
    planes, rows, cases = sizes
    two = 2 * cases
    nodes_y = rows + 1
    count = planes * rows
    total = jnp.sum(system[...], axis=0) + jnp.sum(system_pair[...], axis=0)
    half, depth = cases // 2, system.shape[2]
    square[...] = jnp.zeros(square.shape, f32)
    for part in range(half // depth):
        value = total[part]
        square[part * depth : (part + 1) * depth, :] = value
        lines = slice(half + part * depth, half + (part + 1) * depth)
        square[lines, :] = pltpu.roll(value, LANES // 2, 1)
    value, turned = square[0:cases, :], jnp.transpose(square[...])
    line = lax.broadcasted_iota(jnp.int32, (cases, cases), 0)
    place = lax.broadcasted_iota(jnp.int32, (cases, cases), 1)

    def mended(start, diagonal=None):
        kept, other = value[:, start : start + cases], turned[start : start + cases, :cases]
        if diagonal is None:
            return jnp.where(line <= place, kept, other)
        inner = jnp.where(line < place, other, value[:, diagonal : diagonal + 1])
        return jnp.where(line > place, kept, inner)

    load_image, mixed = mended(0, two), mended(cases)
    parts = ((load_image, mixed), (mixed, mended(cases, two + 1)), (mended(0), load_image))
    full[...] = jnp.zeros(full.shape, f32)
    for index, (left, right) in enumerate(parts):
        full[index * cases : (index + 1) * cases, 0:cases] = left
        full[index * cases : (index + 1) * cases, cases:two] = right
    table = full[...]
    lane = lax.broadcasted_iota(jnp.int32, (1, LANES), 1)
    gone, wide = 0, 4
    for pivot in range(0, two, wide):
        drop = pivot // 8 * 8 - gone
        table = table[drop:]
        gone += drop
        line = pivot - gone
        inner = (lane >= pivot) & (lane < pivot + wide)
        found = [table[line + p : line + p + 1, :] for p in range(wide)]
        block = [
            [jnp.broadcast_to(row[:, pivot + q : pivot + q + 1], row.shape) for q in range(wide)]
            for row in found
        ]
        solved = [
            jnp.where(lane == pivot + p, -1.0, jnp.where(inner, 0.0, found[p]))
            for p in range(wide)
        ]
        for p in range(wide):
            inverse = 1.0 / block[p][p]
            solved[p] = solved[p] * inverse
            block[p] = [value * inverse for value in block[p]]
            for q in range(wide):
                if q != p:
                    factor = block[q][p]
                    solved[q] = solved[q] - factor * solved[p]
                    for r in range(p + 1, wide):
                        block[q][r] = block[q][r] - factor * block[p][r]
        update = None
        for q in range(wide):
            term = table[:, pivot + q : pivot + q + 1] * solved[q]
            update = term if update is None else update + term
        table = jnp.where(inner, 0.0, table) - update
    answer = table[two - gone :, :two]
    high = answer.astype(bf16).astype(f32)
    mixing[...] = jnp.zeros(mixing.shape, f32)
    mixing[0:cases, 0:two] = high
    mixing[0:cases, two : 2 * two] = high
    mixing[cases:two, 0:two] = answer - high
    mix = mixing[...][:, : 2 * two].astype(bf16)

    def combined(place, width):
        lanes = pl.ds(pl.multiple_of(place * 3 * LANES, LANES), width * 3 * LANES)
        value = jnp.dot(mix, both[:, lanes], preferred_element_type=f32)
        return value[:cases] + value[cases:]

    def keep(value, index, column):
        for k in range(3):
            part = value[:, (index * 3 + k) * LANES : (index * 3 + k + 1) * LANES]
            moved = shift_down(part)
            sums[column, k * cases : (k + 1) * cases, :] = part + moved
            diffs[column, k * cases : (k + 1) * cases, :] = moved - part

    def inside(x, _):
        value = combined(x * rows, rows)
        for y in range(rows):
            keep(value, y, x * nodes_y + y)
        return 0

    lax.fori_loop(0, planes, inside, 0)
    value = combined(count, planes + nodes_y)
    for x in range(planes):
        keep(value, x, x * nodes_y + rows)
    for y in range(nodes_y):
        keep(value, planes + y, planes * nodes_y + y)

    tiles = cases // 8

    def step(plane, _):
        for tile in range(tiles):
            lower = x_modes(sums, diffs, plane, 0, tile, cases, nodes_y)
            for row in range(rows):
                upper = x_modes(sums, diffs, plane, row + 1, tile, cases, nodes_y)
                part = mode_energy(modes_of(lower, upper))
                if tile == 0:
                    energy[row] = part
                else:
                    energy[row] += part
                lower = upper
        total = jnp.sum(energy[...], axis=1)
        total = (-3.0 / cases) * jnp.abs(codes[plane]) * total
        for index in range(out.shape[0]):
            out[index, plane] = total
        return 0

    lax.fori_loop(0, planes, step, 0)


def smooth(ref, x, rows):
    weight = [2.5 - math.sqrt(q) for q in range(7)]
    near = {}
    for dx in range(-2, 3):
        for dy in range(-2, 3):
            q = dx * dx + dy * dy
            if q <= 5:
                value = ref[x + 2 + dx, 2 + dy : 2 + dy + rows, :]
                near[q] = value if q not in near else near[q] + value
    result = None
    for dz in range(3):
        part = None
        for q, value in near.items():
            if q + dz * dz <= 6:
                term = weight[q + dz * dz] * value
                part = term if part is None else part + term
        if dz == 0:
            result = part
        else:
            place = lax.broadcasted_iota(jnp.int32, part.shape, 1)
            forward = jnp.where(place >= LANES - dz, 0.0, pltpu.roll(part, LANES - dz, 1))
            backward = jnp.where(place < dz, 0.0, pltpu.roll(part, dz, 1))
            result = result + (forward + backward)
    return result


def scale_kernel(sizes, counts, start, levels, out, there):
    planes, rows, _ = sizes
    y = lax.broadcasted_iota(jnp.int32, (rows + 4, LANES), 0) + (start[1] - 2)
    in_y = (y >= 0) & (y < counts[1] * rows)
    for x in range(planes + 4):
        global_x = start[0] + (x - 2)
        in_x = (global_x >= 0) & (global_x < counts[0] * planes)
        there[x] = jnp.where(in_y & in_x, 1.0, 0.0)
    for x in range(planes):
        density = 0.3 + 0.7 * levels[x].astype(f32) / (LEVELS - 1)
        out[x] = 1.0 / (density * smooth(there, x, rows))


def filter_kernel(sizes, counts, start, blocks, blocks_pair, scale, out, wide):
    planes, rows, _ = sizes
    sides_x = ((-1, planes - 2, planes, 0), (0, 0, planes, 2), (1, 0, 2, 2 + planes))
    sides_y = ((-1, rows - 2, rows, 0), (0, 0, rows, 2), (1, 0, 2, 2 + rows))
    for step_x, x0, x1, to_x in sides_x:
        for step_y, y0, y1, to_y in sides_y:
            at_x = start[0] // planes + step_x
            at_y = start[1] // rows + step_y
            inside = (at_x >= 0) & (at_x < counts[0]) & (at_y >= 0) & (at_y < counts[1])
            index = jnp.where(inside, at_x // 2 * counts[1] + at_y, 0)
            value = (blocks_pair if step_x else blocks)[index, x0:x1, y0:y1, :]
            wide[to_x : to_x + x1 - x0, to_y : to_y + y1 - y0, :] = jnp.where(inside, value, 0.0)
    for x in range(planes):
        out[x] = smooth(wide, x, rows) * scale[x]


def local(forces, levels, supports):
    _, cases, planes, rows, _ = forces.shape
    sizes = (planes, rows, cases)
    block = 3 * cases
    count_x, count_y = lax.axis_size("gx"), lax.axis_size("gy")

    def shape(blocks, codes):
        return jax.ShapeDtypeStruct((blocks * block + up8(codes), LANES), f32)

    density = 0.3 + 0.7 * levels.astype(f32) / (LEVELS - 1)
    codes = density * density * density
    codes = jnp.where(supports == 0, codes, -codes)
    whole = shape(planes * rows, planes * rows)
    down = [] if planes == 2 else [shape(2 * rows, 2 * rows)]
    own, up, *down = pl.pallas_call(
        functools.partial(pack_kernel, sizes),
        out_shape=[whole, shape(rows, 2 * rows), *down],
        in_specs=[VMEM] * 2,
        out_specs=[VMEM] * (2 + len(down)),
        compiler_params=PARAMS,
        name="pack",
    )(forces, codes)

    start = jnp.stack([lax.axis_index("gx") * planes, lax.axis_index("gy") * rows])
    start = start.astype(jnp.int32)
    counts = (count_x, count_y)
    scalars = pl.BlockSpec(memory_space=pltpu.SMEM)
    scale = pl.pallas_call(
        functools.partial(scale_kernel, sizes, counts),
        out_shape=jax.ShapeDtypeStruct((planes, rows, LANES), f32),
        in_specs=[scalars, VMEM],
        out_specs=VMEM,
        scratch_shapes=[pltpu.VMEM((planes + 4, rows + 4, LANES), f32)],
        compiler_params=PARAMS,
        name="scale",
    )(start, levels)

    def moved(value, axis, step):
        count = lax.axis_size(axis)
        pairs = [(i, i + step) for i in range(count) if 0 <= i + step < count]
        return lax.ppermute(value, axis, pairs)

    def links(first, step):
        return [(i, i + step) for i in range(first, count_x, 2) if 0 <= i + step < count_x]

    def swapped(value):
        return lax.ppermute(value, "gx", links(0, 1) + links(1, -1))

    upper = lax.ppermute(down[0] if down else own, "gx", links(2, -1))
    lower = lax.ppermute(up, "gx", links(1, 1))
    pair = swapped(own)
    own, pair = lax.optimization_barrier((own, pair))
    ym, yp = pl.pallas_call(
        functools.partial(rows_kernel, sizes),
        out_shape=[shape(2 * planes, 2 * planes), shape(planes, 2 * planes)],
        in_specs=[VMEM],
        out_specs=[VMEM] * 2,
        compiler_params=PARAMS,
        name="rows",
    )(own)
    from_yp, from_ym = moved(ym, "gy", -1), moved(yp, "gy", 1)
    pair_yp, pair_ym = swapped(from_yp), swapped(from_ym)
    corner_down, corner_up = pl.pallas_call(
        functools.partial(corner_kernel, sizes),
        out_shape=[
            jax.ShapeDtypeStruct((6 * block + 16, LANES), f32),
            jax.ShapeDtypeStruct((3 * block + 16, LANES), f32),
        ],
        in_specs=[VMEM] * 2,
        out_specs=[VMEM] * 2,
        compiler_params=PARAMS,
        name="corners",
    )(from_ym, from_yp)
    corner_high = lax.ppermute(corner_down, "gx", links(2, -1))
    corner_low = lax.ppermute(corner_up, "gx", links(1, 1))

    devices = count_x * count_y
    nodes = (planes + 1) * (rows + 1)
    window = jax.ShapeDtypeStruct(((planes + 1) * (rows + 3), block, LANES), f32)
    partial_forces = jax.ShapeDtypeStruct((nodes, block, LANES), f32)
    early = pl.pallas_call(
        functools.partial(early_kernel, sizes),
        out_shape=[window] * 3 + [partial_forces] * 2,
        in_specs=[scalars] + [VMEM] * 6,
        out_specs=[VMEM] * 5,
        scratch_shapes=[
            pltpu.VMEM((planes + 2, up8(rows + 4), LANES), f32),
            pltpu.VMEM((planes + 1, up8(rows + 3), LANES), f32),
        ],
        compiler_params=PARAMS,
        cost_estimate=pl.CostEstimate(
            flops=200 * planes * rows * block * LANES, bytes_accessed=2**23, transcendentals=0
        ),
        name="early",
    )(start, own, pair, from_ym, from_yp, pair_ym, pair_yp)

    side = pltpu.VMEM((3 * (rows + 3), block, LANES), f32)
    acc = pltpu.VMEM((3 * (rows + 1), block, LANES), f32)
    field = pltpu.VMEM((nodes, block, LANES), f32)
    both, system = pl.pallas_call(
        functools.partial(main_kernel, sizes),
        out_shape=[
            jax.ShapeDtypeStruct((4 * cases, nodes * 3 * LANES), bf16),
            jax.ShapeDtypeStruct((devices // 2, cases // 8, 4, LANES), f32),
        ],
        in_specs=[scalars] + [VMEM] * 15,
        out_specs=[VMEM] * 2,
        scratch_shapes=[
            pltpu.VMEM((planes + 4, up8(rows + 4), LANES), f32),
            pltpu.VMEM((planes + 3, up8(rows + 3), LANES), f32),
            pltpu.VMEM((rows + 3, block, LANES), f32),
            side, side, acc, acc, field, field, field, field,
            pltpu.VMEM((6 * cases, nodes * 3 * LANES), bf16),
            pltpu.VMEM((cases, LANES), f32),
        ],
        compiler_params=PARAMS,
        name="operator",
    )(
        start, own, pair, lower, upper, from_ym, from_yp, pair_ym, pair_yp,
        corner_low, corner_high, *early,
    )

    groups = [
        [x * count_y + y for x in range(side, count_x, 2) for y in range(count_y)]
        for side in range(2)
    ]

    def gathered(copies):
        mine = lax.all_to_all(copies, ("gx", "gy"), 0, 0, axis_index_groups=groups)
        return mine, swapped(mine)

    system = gathered(system)

    weighted = pl.pallas_call(
        functools.partial(solve_kernel, sizes),
        out_shape=jax.ShapeDtypeStruct((devices // 2, planes, rows, LANES), f32),
        in_specs=[VMEM] * 4,
        out_specs=VMEM,
        scratch_shapes=[
            pltpu.VMEM((2 * cases, LANES), f32),
            field,
            field,
            pltpu.VMEM((rows, 8, LANES), f32),
            pltpu.VMEM((LANES, LANES), f32),
            pltpu.VMEM((3 * cases, LANES), f32),
        ],
        compiler_params=PARAMS,
        name="solve",
    )(*system, both, codes)

    blocks = gathered(weighted)
    return pl.pallas_call(
        functools.partial(filter_kernel, sizes, counts),
        out_shape=jax.ShapeDtypeStruct((planes, rows, LANES), f32),
        in_specs=[scalars] + [VMEM] * 3,
        out_specs=VMEM,
        scratch_shapes=[pltpu.VMEM((planes + 4, rows + 4, LANES), f32)],
        compiler_params=PARAMS,
        name="cone",
    )(start, *blocks, scale)


def solution(mesh):
    return jax.shard_map(
        local,
        mesh=mesh,
        in_specs=(P(None, None, "gx", "gy", None), P("gx", "gy", None), P("gx", "gy", None)),
        out_specs=P("gx", "gy", None),
        check_vma=False,
    )
```

```python
import functools
import math

import jax
import jax.numpy as jnp
from jax import lax
from jax.experimental import pallas as pl
from jax.experimental.pallas import tpu as pltpu
from jax.sharding import PartitionSpec as P

LEVELS = 16
LOAD = 0.2
LANES = 128
POISSON = 0.3
LAME = POISSON / ((1.0 + POISSON) * (1.0 - 2.0 * POISSON))
SHEAR = 1.0 / (2.0 * (1.0 + POISSON))
DIAGONAL = (LAME + 2.0 * SHEAR) / 9.0 + 2.0 * SHEAR / 9.0
VMEM = pl.BlockSpec(memory_space=pltpu.VMEM)
PARAMS = pltpu.CompilerParams(vmem_limit_bytes=30 * 2**20)
f32 = jnp.float32
bf16 = jnp.bfloat16


def up8(count):
    return -(-count // 8) * 8


def shift_down(value):
    lane = lax.broadcasted_iota(jnp.int32, value.shape, value.ndim - 1)
    rolled = pltpu.roll(value, LANES - 1, value.ndim - 1)
    return jnp.where(lane == LANES - 1, 0.0, rolled)


def shift_up(value):
    lane = lax.broadcasted_iota(jnp.int32, value.shape, value.ndim - 1)
    return jnp.where(lane == 0, 0.0, pltpu.roll(value, 1, value.ndim - 1))


def unrolled(count, factor, body):
    def turn(step, _):
        for offset in range(factor):
            body(step * factor + offset)
        return 0

    turns = count // factor
    if turns:
        lax.fori_loop(0, turns, turn, 0)
    for index in range(turns * factor, count):
        body(index)


def split(value):
    high = value.astype(bf16)
    return high, (value - high.astype(f32)).astype(bf16)


def modes_of(lower, upper):
    out = [[[[None] * 3 for _ in range(2)] for _ in range(2)] for _ in range(2)]
    for a in range(2):
        for c in range(2):
            for k in range(3):
                if a or c:
                    out[a][0][c][k] = lower[a][c][k] + upper[a][c][k]
                out[a][1][c][k] = upper[a][c][k] - lower[a][c][k]
    return out


PAIRS = (((1, 1, 0, 0), (0, 1, 1, 2)), ((1, 0, 1, 0), (0, 1, 1, 1)), ((1, 1, 0, 1), (1, 0, 1, 2)))
TRIPLE = ((0, 1, 1, 0), (1, 0, 1, 1), (1, 1, 0, 2))
SHEARS = (((0, 1, 0, 0), (1, 0, 0, 1)), ((0, 0, 1, 0), (1, 0, 0, 2)), ((0, 0, 1, 1), (0, 1, 0, 2)))
AXIAL = ((1, 0, 0, 0), (0, 1, 0, 1), (0, 0, 1, 2))


def at(modes, place):
    a, b, c, k = place
    return modes[a][b][c][k]


def mode_forces(modes, stiff):
    out = [[[[None] * 3 for _ in range(2)] for _ in range(2)] for _ in range(2)]

    def put(place, value):
        a, b, c, k = place
        out[a][b][c][k] = value

    shear = stiff * (SHEAR / 16)
    for first, second in SHEARS:
        force = shear * (at(modes, first) + at(modes, second))
        put(first, force)
        put(second, force)
    one, two, three = (at(modes, place) for place in AXIAL)
    volume = (stiff * (LAME / 16)) * (one + two + three)
    axial = stiff * (SHEAR / 8)
    for place in AXIAL:
        put(place, volume + axial * at(modes, place))
    own, cross = stiff * ((LAME + 3 * SHEAR) / 48), stiff * (LAME / 48)
    for first, second in PAIRS:
        one, two = at(modes, first), at(modes, second)
        put(first, own * one + cross * two)
        put(second, own * two + cross * one)
    twist = stiff * (SHEAR / 48)
    one, two, three = (at(modes, place) for place in TRIPLE)
    total = one + two + three
    for place in TRIPLE:
        put(place, twist * (total + at(modes, place)))
    last = stiff * ((LAME + 4 * SHEAR) / 144)
    for k in range(3):
        put((1, 1, 1, k), last * modes[1][1][1][k])
    return out


def mode_energy(modes):
    def square(value):
        return value * value

    shear = None
    for first, second in SHEARS:
        term = square(at(modes, first) + at(modes, second))
        shear = term if shear is None else shear + term
    one, two, three = (at(modes, place) for place in AXIAL)
    energy = (SHEAR / 16) * shear + (LAME / 16) * square(one + two + three)
    energy = energy + (SHEAR / 8) * (square(one) + square(two) + square(three))
    squares, products = None, None
    for first, second in PAIRS:
        one, two = at(modes, first), at(modes, second)
        term, product = square(one) + square(two), one * two
        squares = term if squares is None else squares + term
        products = product if products is None else products + product
    energy = energy + ((LAME + 3 * SHEAR) / 48) * squares + (LAME / 24) * products
    one, two, three = (at(modes, place) for place in TRIPLE)
    twist = square(one + two + three) + square(one) + square(two) + square(three)
    energy = energy + (SHEAR / 48) * twist
    last = square(modes[1][1][1][0]) + square(modes[1][1][1][1]) + square(modes[1][1][1][2])
    return energy + ((LAME + 4 * SHEAR) / 144) * last


def x_modes(sums, diffs, plane, row, tile, cases, columns):
    out = [[[None] * 3 for _ in range(2)] for _ in range(2)]
    for c, ref in enumerate((sums, diffs)):
        for k in range(3):
            rows = pl.ds(pl.multiple_of(k * cases + tile * 8, 8), 8)
            one = ref[plane * columns + row, rows, :]
            two = ref[(plane + 1) * columns + row, rows, :]
            out[0][c][k] = one + two
            out[1][c][k] = two - one
    return out


def apply_elements(
    sums, diffs, stiff_ref, acc_s, acc_d, planes, rows, skip, stiff_x, stiff_y, cases
):
    columns = rows + 1
    acc_columns = columns - 2 * skip
    tiles = cases // 8

    def step(index, _):
        plane, tile = index // tiles, index % tiles

        def emit(row, total):
            if not skip <= row < columns - skip:
                return
            for c, acc in enumerate((acc_s, acc_d)):
                for k in range(3):
                    lines = pl.ds(pl.multiple_of(k * cases + tile * 8, 8), 8)
                    low = plane * acc_columns + row - skip
                    acc[low, lines, :] += total[0][c][k] - total[1][c][k]
                    acc[low + acc_columns, lines, :] = total[0][c][k] + total[1][c][k]

        lower = x_modes(sums, diffs, plane, 0, tile, cases, columns)
        carry = None
        for row in range(rows):
            upper = x_modes(sums, diffs, plane, row + 1, tile, cases, columns)
            stiff = jnp.broadcast_to(
                stiff_ref[plane + stiff_x, pl.ds(row + stiff_y, 1), :], (8, LANES)
            )
            forces = mode_forces(modes_of(lower, upper), stiff)
            here = [[[None] * 3 for _ in range(2)] for _ in range(2)]
            following = [[[None] * 3 for _ in range(2)] for _ in range(2)]
            for a in range(2):
                for c in range(2):
                    for k in range(3):
                        one, two = forces[a][0][c][k], forces[a][1][c][k]
                        low = -two if one is None else one - two
                        high = two if one is None else one + two
                        here[a][c][k] = low if carry is None else carry[a][c][k] + low
                        following[a][c][k] = high
            emit(row, here)
            carry, lower = following, upper
        emit(rows, carry)
        return 0

    lax.fori_loop(0, planes * tiles, step, 0)


def fill(source, base, sizes, ref, xs, ys, code_xs, code_ys):
    planes, rows, cases = sizes
    block = 3 * cases
    line = 0
    for x in xs:
        start = (x * rows + ys[0]) * block
        count = len(ys) * block
        ref[line : line + count, :] = source[start : start + count, :]
        line += count
    for x in code_xs:
        start = base + x * rows + code_ys[0]
        ref[line : line + len(code_ys), :] = source[start : start + len(code_ys), :]
        line += len(code_ys)
    if line < ref.shape[0]:
        ref[line:, :] = jnp.zeros((ref.shape[0] - line, LANES), f32)


def pack_kernel(sizes, forces, codes, own, up, *down):
    planes, rows, cases = sizes
    block = 3 * cases
    base = planes * rows * block
    for x in range(planes):
        own[base + x * rows : base + (x + 1) * rows, :] = codes[x]
        scale = jnp.where(codes[x] > 0.0, LOAD, 0.0)
        for k in range(3):
            for c in range(cases):
                start = x * rows * block + k * cases + c
                own[pl.ds(start, rows, stride=block), :] = forces[k, c, x] * scale

    every_y, last = range(rows), (planes - 2, planes - 1)
    fill(own, base, sizes, up, last[1:], every_y, last, every_y)
    for ref in down:
        fill(own, base, sizes, ref, (0, 1), every_y, (0, 1), every_y)


def rows_kernel(sizes, own, ym, yp):
    planes, rows, cases = sizes
    base = planes * rows * 3 * cases
    every_x = range(planes)
    fill(own, base, sizes, ym, every_x, (0, 1), every_x, (0, 1))
    fill(own, base, sizes, yp, every_x, (rows - 1,), every_x, (rows - 2, rows - 1))


def corner_kernel(sizes, first, ym, yp, edge, second):
    planes, rows, cases = sizes
    block = 3 * cases
    even = first[0] // planes % 2 == 0
    line = at = 0
    for source, width in ((ym, 1), (yp, 2)):
        size = width * block
        for start in range(0, size, block):
            last = (planes - 1) * size + start
            edge[line : line + block, :] = jnp.where(
                even, source[start : start + block, :], source[last : last + block, :]
            )
            line += block
        low, high = planes * size, planes * size + (planes - 2) * 2
        edge[line : line + 4, :] = jnp.where(
            even, source[low : low + 4, :], source[high : high + 4, :]
        )
        edge[line + 4 : line + 8, :] = jnp.zeros((4, LANES), f32)
        line += 8
        second[at : at + size, :] = source[size : 2 * size, :]
        at += size


def lines(ref, start, count):
    return ref[start : start + count, :]


def inside(ref, x, y, rows, block):
    return lines(ref, (x * rows + y) * block, block)


def beyond(refs, slot, y, rows, block):
    below, above = refs
    if y < 0:
        return lines(below, slot * block, block)
    return lines(above, (slot * 2 + y - rows) * block, block)


def beyond_codes(refs, slots, slot, y, block):
    below, above = refs
    if y < 0:
        return lines(below, slots * block + slot * 2, 2)
    return lines(above, slots * 2 * block + slot * 2, 2)


def corner(ref, y, rows, block, gap):
    start = 0 if y < 0 else block + gap + (y - rows) * block
    return lines(ref, start, block)


def corner_codes(ref, slot, y, block):
    return lines(ref, (block if y < 0 else 3 * block + 8) + slot * 2, 2)


def node_inverse(signed, count, out):
    planes = signed.shape[0]
    for x in range(1, planes):
        codes = signed[x, 0 : count + 1, :]
        total = jnp.abs(signed[x - 1, 0 : count + 1, :]) + jnp.abs(codes)
        total = total[:-1] + total[1:]
        total = total + shift_up(total)
        free = codes[1:] > 0.0
        value = 1.0 / (DIAGONAL * jnp.where(free, total, 1.0))
        out[x - 1, 0:count, :] = jnp.where(free, value, 0.0)
    for x in range(planes):
        signed[x] = jnp.abs(signed[x])


def place_column(sums, diffs, column, value):
    moved = shift_down(value)
    sums[column] = value + moved
    diffs[column] = moved - value


def early_kernel(
    sizes, first, own, pair, ym, yp, ym_pair, yp_pair, start, sums, diffs, acc_s, acc_d,
    stiff_ref, inverse,
):
    planes, rows, cases = sizes
    block = 3 * cases
    ys = rows + 3
    even = first[0] // planes % 2 == 0
    y_own, y_pair = (ym, yp), (ym_pair, yp_pair)

    def both_ways(w, read):
        low = read(True, w + 1) if w + 1 < planes else read(False, w + 1 - planes)
        high = read(False, planes + w - 1) if w < 1 else read(True, w - 1)
        return jnp.where(even, low, high)

    def codes(w, y):
        def read(mine, x):
            if y == 0:
                return lines(own if mine else pair, (planes * block + x) * rows, rows)
            return beyond_codes(y_own if mine else y_pair, planes, x, y, block)

        return both_ways(w, read)

    for w in range(-1, planes + 1):
        for y, count in ((-2, 2), (0, rows), (rows, 2)):
            stiff_ref[w + 1, y + 2 : y + 2 + count, :] = codes(w, y)
    node_inverse(stiff_ref, ys, inverse)
    for w in range(planes + 1):
        for y in range(-1, rows + 2):

            def read(mine, x):
                if 0 <= y < rows:
                    return inside(own if mine else pair, x, y, rows, block)
                return beyond(y_own if mine else y_pair, x, y, rows, block)

            value = both_ways(w, read) * inverse[w, y + 1 : y + 2, :]
            column = w * ys + y + 1
            start[column] = value
            place_column(sums, diffs, column, value)
    for column in range(rows + 1):
        acc_s[column] = jnp.zeros((block, LANES), f32)
        acc_d[column] = jnp.zeros((block, LANES), f32)
    apply_elements(sums, diffs, stiff_ref, acc_s, acc_d, planes, rows + 2, 1, 1, 1, cases)


def main_kernel(
    sizes, first, own, pair, lower, upper, ym, yp, ym_pair, yp_pair, corner_edge, corner_second,
    start, sums_e, diffs_e, acc_se, acc_de,
    both_out, system_out, stiff_ref, inverse,
    middle, sums, diffs, acc_s, acc_d, w_sums, w_diffs, acc2_s, acc2_d, right, table,
):
    planes, rows, cases = sizes
    block = 3 * cases
    ys = rows + 3
    even = first[0] // planes % 2 == 0
    y_own, y_pair = (ym, yp), (ym_pair, yp_pair)

    def codes(x, y):
        def read(mine, plane):
            if y == 0:
                return lines(own if mine else pair, (planes * block + plane) * rows, rows)
            return beyond_codes(y_own if mine else y_pair, planes, plane, y, block)

        if 0 <= x < planes:
            return read(True, x)
        ref, count, slot = (lower, 1, x + 2) if x < 0 else (upper, 2, x - planes)
        if y == 0:
            outer = lines(ref, (count * block + slot) * rows, rows)
        else:
            outer = corner_codes(corner_edge, slot, y, block)
        inner = read(False, planes + x if x < 0 else x - planes)
        return jnp.where(even, outer, inner) if x < 0 else jnp.where(even, inner, outer)

    for x in range(-2, planes + 2):
        for y, count in ((-2, 2), (0, rows), (rows, 2)):
            stiff_ref[x + 2, y + 2 : y + 2 + count, :] = codes(x, y)
    node_inverse(stiff_ref, ys, inverse)

    def place(v, x, read):
        for y in range(-1, rows + 2):
            value = read(y) * inverse[x + 1, y + 1 : y + 2, :]
            if v == 1:
                middle[y + 1] = value
            place_column(sums, diffs, v * ys + y + 1, value)

    def copy(v, w):
        for y in range(ys):
            sums[v * ys + y] = sums_e[w * ys + y]
            diffs[v * ys + y] = diffs_e[w * ys + y]

    @pl.when(even)
    def _():
        def outer(y):
            if 0 <= y < rows:
                return inside(lower, 0, y, rows, block)
            return corner(corner_edge, y, rows, block, 8)

        def inner(y):
            if 0 <= y < rows:
                return inside(own, 0, y, rows, block)
            return beyond(y_own, 0, y, rows, block)

        place(0, -1, outer)
        place(1, 0, inner)
        copy(2, 0)

    @pl.when(jnp.logical_not(even))
    def _():
        def outer(slot, corner_ref, gap):
            def read(y):
                if 0 <= y < rows:
                    return inside(upper, slot, y, rows, block)
                return corner(corner_ref, y, rows, block, gap)

            return read

        copy(0, planes)
        place(1, planes, outer(0, corner_edge, 8))
        place(2, planes + 1, outer(1, corner_second, 0))

    nodes_y = rows + 1
    for column in range(nodes_y):
        acc_s[column] = jnp.zeros((block, LANES), f32)
        acc_d[column] = jnp.zeros((block, LANES), f32)
    layer = jnp.where(even, 1, planes + 1)
    apply_elements(sums, diffs, stiff_ref, acc_s, acc_d, 2, rows + 2, 1, layer, 1, cases)

    def total(x, y, early, main):
        low = ([x - 1] if x >= 1 else [], [x + 1] if x <= 1 else [])
        high = ([x + 1] if x < planes else [], [x - planes + 1] if x >= planes - 1 else [])
        if low[0] and low[1] and high[0] and high[1]:
            one = early[jnp.where(even, low[0][0], high[0][0]) * nodes_y + y]
            return one + main[jnp.where(even, low[1][0], high[1][0]) * nodes_y + y]

        def read(places):
            found = [early[w * nodes_y + y] for w in places[0]]
            found += [main[v * nodes_y + y] for v in places[1]]
            return found[0] if len(found) == 1 else found[0] + found[1]

        return jnp.where(even, read(low), read(high))

    def image(x, y, place):
        s, d = total(x, y, acc_se, acc_s), total(x, y, acc_de, acc_d)
        force = s - d + shift_up(s + d)
        scaled = force * inverse[x + 1, pl.ds(y + 1, 1), :]
        place_column(w_sums, w_diffs, x * nodes_y + y, scaled)
        if x == 0:
            value = jnp.where(even, middle[y + 1], start[ys + y + 1])
        elif x == planes:
            value = jnp.where(even, start[(planes - 1) * ys + y + 1], middle[y + 1])
        else:
            value = start[jnp.where(even, x - 1, x + 1) * ys + y + 1]
        for k in range(3):
            lines = slice(k * cases, (k + 1) * cases)
            both = jnp.concatenate([value[lines], scaled[lines]], 0)
            lane = pl.ds(pl.multiple_of((place * 3 + k) * LANES, LANES), LANES)
            high, rest = split(both)
            both_out[0 : 2 * cases, lane] = high
            both_out[2 * cases : 4 * cases, lane] = rest
        return force

    two = 2 * cases
    count = planes * rows

    def within(x, y):
        index = x * rows + y
        force = image(x, y, index)
        given = own[pl.ds(pl.multiple_of(index * block, 8), block), :]
        for k in range(3):
            lines = slice(k * cases, (k + 1) * cases)
            both = jnp.concatenate([given[lines], force[lines]], 0)
            lane = pl.ds(pl.multiple_of((index * 3 + k) * LANES, LANES), LANES)
            high, rest = split(both)
            right[0:two, lane] = high
            right[two : 2 * two, lane] = rest

    for x in range(planes):
        unrolled(rows, 4, functools.partial(within, x))
        image(x, rows, count + x)
    unrolled(nodes_y, 3, lambda y: image(planes, y, count + planes + y))
    rest = right.shape[1] - count * 3 * LANES
    right[0 : 2 * two, count * 3 * LANES :] = jnp.zeros((2 * two, rest), bf16)

    for column in range(nodes_y):
        acc2_s[column] = jnp.zeros((block, LANES), f32)
        acc2_d[column] = jnp.zeros((block, LANES), f32)
    apply_elements(w_sums, w_diffs, stiff_ref, acc2_s, acc2_d, planes, rows, 0, 2, 2, cases)

    def second_force(x, y, place):
        column = x * nodes_y + y
        s, d = acc2_s[column], acc2_d[column]
        force = s - d + shift_up(s + d)
        for k in range(3):
            value = force[k * cases : (k + 1) * cases]
            high = value.astype(bf16).astype(f32)
            lane = pl.ds(pl.multiple_of((place * 3 + k) * LANES, LANES), LANES)
            right[2 * two :, lane] = jnp.concatenate([high, value - high], 0).astype(bf16)

    unrolled(count, 4, lambda index: second_force(index // rows, index % rows, index))
    unrolled(planes, 2, lambda x: second_force(x, rows, count + x))
    unrolled(nodes_y, 3, lambda y: second_force(planes, y, count + planes + y))

    contract = (((1,), (1,)), ((), ()))
    product = lax.dot_general(right[...], both_out[...], contract, preferred_element_type=f32)
    product = product[:, :two] + product[:, two:]
    gram = product[:two] + product[two : 2 * two]
    other = product[2 * two : 2 * two + cases] + product[2 * two + cases :]
    row = lax.broadcasted_iota(jnp.int32, (cases, cases), 0)
    column = lax.broadcasted_iota(jnp.int32, (cases, cases), 1)
    load_load, load_image = gram[:cases, :cases], gram[cases:, :cases]
    mixed, image_image = other[:, :cases], other[:, cases:]
    table[...] = jnp.zeros(table.shape, f32)
    table[:, 0:cases] = jnp.where(row <= column, load_load, load_image)
    table[:, cases:two] = jnp.where(row <= column, mixed, image_image)
    for lane, value in ((two, load_image), (two + 1, image_image)):
        own_entries = jnp.where(row == column, value, 0.0)
        table[:, lane : lane + 1] = jnp.sum(own_entries, axis=1, keepdims=True)
    half = cases // 2
    folded = table[:half, :] + pltpu.roll(table[half:, :], LANES // 2, 1)
    depth = system_out.shape[2]
    for index in range(system_out.shape[0]):
        for part in range(half // depth):
            system_out[index, part] = folded[part * depth : (part + 1) * depth]


def solve_kernel(
    sizes, system, system_pair, both, codes, out, mixing, sums, diffs, energy, square, full
):
    planes, rows, cases = sizes
    two = 2 * cases
    nodes_y = rows + 1
    count = planes * rows
    total = jnp.sum(system[...], axis=0) + jnp.sum(system_pair[...], axis=0)
    half, depth = cases // 2, system.shape[2]
    square[...] = jnp.zeros(square.shape, f32)
    for part in range(half // depth):
        value = total[part]
        square[part * depth : (part + 1) * depth, :] = value
        lines = slice(half + part * depth, half + (part + 1) * depth)
        square[lines, :] = pltpu.roll(value, LANES // 2, 1)
    value, turned = square[0:cases, :], jnp.transpose(square[...])
    line = lax.broadcasted_iota(jnp.int32, (cases, cases), 0)
    place = lax.broadcasted_iota(jnp.int32, (cases, cases), 1)

    def mended(start, diagonal=None):
        kept, other = value[:, start : start + cases], turned[start : start + cases, :cases]
        if diagonal is None:
            return jnp.where(line <= place, kept, other)
        inner = jnp.where(line < place, other, value[:, diagonal : diagonal + 1])
        return jnp.where(line > place, kept, inner)

    load_image, mixed = mended(0, two), mended(cases)
    parts = ((load_image, mixed), (mixed, mended(cases, two + 1)), (mended(0), load_image))
    full[...] = jnp.zeros(full.shape, f32)
    for index, (left, right) in enumerate(parts):
        full[index * cases : (index + 1) * cases, 0:cases] = left
        full[index * cases : (index + 1) * cases, cases:two] = right
    table = full[...]
    lane = lax.broadcasted_iota(jnp.int32, (1, LANES), 1)
    gone, wide = 0, 4
    for pivot in range(0, two, wide):
        drop = pivot // 8 * 8 - gone
        table = table[drop:]
        gone += drop
        line = pivot - gone
        inner = (lane >= pivot) & (lane < pivot + wide)
        found = [table[line + p : line + p + 1, :] for p in range(wide)]
        block = [
            [jnp.broadcast_to(row[:, pivot + q : pivot + q + 1], row.shape) for q in range(wide)]
            for row in found
        ]
        solved = [
            jnp.where(lane == pivot + p, -1.0, jnp.where(inner, 0.0, found[p]))
            for p in range(wide)
        ]
        for p in range(wide):
            inverse = 1.0 / block[p][p]
            solved[p] = solved[p] * inverse
            block[p] = [value * inverse for value in block[p]]
            for q in range(wide):
                if q != p:
                    factor = block[q][p]
                    solved[q] = solved[q] - factor * solved[p]
                    for r in range(p + 1, wide):
                        block[q][r] = block[q][r] - factor * block[p][r]
        update = None
        for q in range(wide):
            term = table[:, pivot + q : pivot + q + 1] * solved[q]
            update = term if update is None else update + term
        table = jnp.where(inner, 0.0, table) - update
    answer = table[two - gone :, :two]
    high = answer.astype(bf16).astype(f32)
    mixing[...] = jnp.zeros(mixing.shape, f32)
    mixing[0:cases, 0:two] = high
    mixing[0:cases, two : 2 * two] = high
    mixing[cases:two, 0:two] = answer - high
    mix = mixing[...][:, : 2 * two].astype(bf16)

    def combined(place, width):
        lanes = pl.ds(pl.multiple_of(place * 3 * LANES, LANES), width * 3 * LANES)
        value = jnp.dot(mix, both[:, lanes], preferred_element_type=f32)
        return value[:cases] + value[cases:]

    def keep(value, index, column):
        for k in range(3):
            part = value[:, (index * 3 + k) * LANES : (index * 3 + k + 1) * LANES]
            moved = shift_down(part)
            sums[column, k * cases : (k + 1) * cases, :] = part + moved
            diffs[column, k * cases : (k + 1) * cases, :] = moved - part

    def inside(x, _):
        value = combined(x * rows, rows)
        for y in range(rows):
            keep(value, y, x * nodes_y + y)
        return 0

    lax.fori_loop(0, planes, inside, 0)
    value = combined(count, planes + nodes_y)
    for x in range(planes):
        keep(value, x, x * nodes_y + rows)
    for y in range(nodes_y):
        keep(value, planes + y, planes * nodes_y + y)

    tiles = cases // 8

    def step(plane, _):
        for tile in range(tiles):
            lower = x_modes(sums, diffs, plane, 0, tile, cases, nodes_y)
            for row in range(rows):
                upper = x_modes(sums, diffs, plane, row + 1, tile, cases, nodes_y)
                part = mode_energy(modes_of(lower, upper))
                if tile == 0:
                    energy[row] = part
                else:
                    energy[row] += part
                lower = upper
        total = jnp.sum(energy[...], axis=1)
        total = (-3.0 / cases) * jnp.abs(codes[plane]) * total
        for index in range(out.shape[0]):
            out[index, plane] = total
        return 0

    lax.fori_loop(0, planes, step, 0)


def smooth(ref, x, rows):
    weight = [2.5 - math.sqrt(q) for q in range(7)]
    near = {}
    for dx in range(-2, 3):
        for dy in range(-2, 3):
            q = dx * dx + dy * dy
            if q <= 5:
                value = ref[x + 2 + dx, 2 + dy : 2 + dy + rows, :]
                near[q] = value if q not in near else near[q] + value
    result = None
    for dz in range(3):
        part = None
        for q, value in near.items():
            if q + dz * dz <= 6:
                term = weight[q + dz * dz] * value
                part = term if part is None else part + term
        if dz == 0:
            result = part
        else:
            place = lax.broadcasted_iota(jnp.int32, part.shape, 1)
            forward = jnp.where(place >= LANES - dz, 0.0, pltpu.roll(part, LANES - dz, 1))
            backward = jnp.where(place < dz, 0.0, pltpu.roll(part, dz, 1))
            result = result + (forward + backward)
    return result


def scale_kernel(sizes, counts, start, levels, out, there):
    planes, rows, _ = sizes
    y = lax.broadcasted_iota(jnp.int32, (rows + 4, LANES), 0) + (start[1] - 2)
    in_y = (y >= 0) & (y < counts[1] * rows)
    for x in range(planes + 4):
        global_x = start[0] + (x - 2)
        in_x = (global_x >= 0) & (global_x < counts[0] * planes)
        there[x] = jnp.where(in_y & in_x, 1.0, 0.0)
    for x in range(planes):
        density = 0.3 + 0.7 * levels[x].astype(f32) / (LEVELS - 1)
        out[x] = 1.0 / (density * smooth(there, x, rows))


def filter_kernel(sizes, counts, start, blocks, blocks_pair, scale, out, wide):
    planes, rows, _ = sizes
    sides_x = ((-1, planes - 2, planes, 0), (0, 0, planes, 2), (1, 0, 2, 2 + planes))
    sides_y = ((-1, rows - 2, rows, 0), (0, 0, rows, 2), (1, 0, 2, 2 + rows))
    for step_x, x0, x1, to_x in sides_x:
        for step_y, y0, y1, to_y in sides_y:
            at_x = start[0] // planes + step_x
            at_y = start[1] // rows + step_y
            inside = (at_x >= 0) & (at_x < counts[0]) & (at_y >= 0) & (at_y < counts[1])
            index = jnp.where(inside, at_x // 2 * counts[1] + at_y, 0)
            value = (blocks_pair if step_x else blocks)[index, x0:x1, y0:y1, :]
            wide[to_x : to_x + x1 - x0, to_y : to_y + y1 - y0, :] = jnp.where(inside, value, 0.0)
    for x in range(planes):
        out[x] = smooth(wide, x, rows) * scale[x]


def local(forces, levels, supports):
    _, cases, planes, rows, _ = forces.shape
    sizes = (planes, rows, cases)
    block = 3 * cases
    count_x, count_y = lax.axis_size("gx"), lax.axis_size("gy")

    def shape(blocks, codes):
        return jax.ShapeDtypeStruct((blocks * block + up8(codes), LANES), f32)

    density = 0.3 + 0.7 * levels.astype(f32) / (LEVELS - 1)
    codes = density * density * density
    codes = jnp.where(supports == 0, codes, -codes)
    start = jnp.stack([lax.axis_index("gx") * planes, lax.axis_index("gy") * rows])
    start = start.astype(jnp.int32)
    counts = (count_x, count_y)
    scalars = pl.BlockSpec(memory_space=pltpu.SMEM)
    whole = shape(planes * rows, planes * rows)
    down = [] if planes == 2 else [shape(2 * rows, 2 * rows)]
    own, up, *down = pl.pallas_call(
        functools.partial(pack_kernel, sizes),
        out_shape=[whole, shape(rows, 2 * rows), *down],
        in_specs=[VMEM] * 2,
        out_specs=[VMEM] * (2 + len(down)),
        compiler_params=PARAMS,
        name="pack",
    )(forces, codes)
    scale = pl.pallas_call(
        functools.partial(scale_kernel, sizes, counts),
        out_shape=jax.ShapeDtypeStruct((planes, rows, LANES), f32),
        in_specs=[scalars, VMEM],
        out_specs=VMEM,
        scratch_shapes=[pltpu.VMEM((planes + 4, rows + 4, LANES), f32)],
        compiler_params=PARAMS,
        name="scale",
    )(start, levels)

    def moved(value, axis, step):
        count = lax.axis_size(axis)
        pairs = [(i, i + step) for i in range(count) if 0 <= i + step < count]
        return lax.ppermute(value, axis, pairs)

    def links(first, step):
        return [(i, i + step) for i in range(first, count_x, 2) if 0 <= i + step < count_x]

    def swapped(value):
        return lax.ppermute(value, "gx", links(0, 1) + links(1, -1))

    def across(value):
        return lax.ppermute(value, "gx", links(1, 1) + links(2, -1))

    upper = lax.ppermute(down[0] if down else own, "gx", links(2, -1))
    lower = lax.ppermute(up, "gx", links(1, 1))
    pair = swapped(own)
    own, pair = lax.optimization_barrier((own, pair))
    ym, yp = pl.pallas_call(
        functools.partial(rows_kernel, sizes),
        out_shape=[shape(2 * planes, 2 * planes), shape(planes, 2 * planes)],
        in_specs=[VMEM],
        out_specs=[VMEM] * 2,
        compiler_params=PARAMS,
        name="rows",
    )(own)
    from_yp, from_ym = moved(ym, "gy", -1), moved(yp, "gy", 1)
    pair_yp, pair_ym = swapped(from_yp), swapped(from_ym)
    corner_edge, corner_second = pl.pallas_call(
        functools.partial(corner_kernel, sizes),
        out_shape=[
            jax.ShapeDtypeStruct((3 * block + 16, LANES), f32),
            jax.ShapeDtypeStruct((3 * block, LANES), f32),
        ],
        in_specs=[scalars] + [VMEM] * 2,
        out_specs=[VMEM] * 2,
        compiler_params=PARAMS,
        name="corners",
    )(start, from_ym, from_yp)
    corner_edge = across(corner_edge)
    corner_second = lax.ppermute(corner_second, "gx", links(2, -1))

    devices = count_x * count_y
    nodes = (planes + 1) * (rows + 1)
    window = jax.ShapeDtypeStruct(((planes + 1) * (rows + 3), block, LANES), f32)
    partial_forces = jax.ShapeDtypeStruct((nodes, block, LANES), f32)
    early = pl.pallas_call(
        functools.partial(early_kernel, sizes),
        out_shape=[window] * 3 + [partial_forces] * 2,
        in_specs=[scalars] + [VMEM] * 6,
        out_specs=[VMEM] * 5,
        scratch_shapes=[
            pltpu.VMEM((planes + 2, up8(rows + 4), LANES), f32),
            pltpu.VMEM((planes + 1, up8(rows + 3), LANES), f32),
        ],
        compiler_params=PARAMS,
        cost_estimate=pl.CostEstimate(
            flops=200 * planes * rows * block * LANES, bytes_accessed=2**23, transcendentals=0
        ),
        name="early",
    )(start, own, pair, from_ym, from_yp, pair_ym, pair_yp)

    side = pltpu.VMEM((3 * (rows + 3), block, LANES), f32)
    acc = pltpu.VMEM((3 * (rows + 1), block, LANES), f32)
    field = pltpu.VMEM((nodes, block, LANES), f32)
    both, system = pl.pallas_call(
        functools.partial(main_kernel, sizes),
        out_shape=[
            jax.ShapeDtypeStruct((4 * cases, nodes * 3 * LANES), bf16),
            jax.ShapeDtypeStruct((devices // 2, cases // 8, 4, LANES), f32),
        ],
        in_specs=[scalars] + [VMEM] * 15,
        out_specs=[VMEM] * 2,
        scratch_shapes=[
            pltpu.VMEM((planes + 4, up8(rows + 4), LANES), f32),
            pltpu.VMEM((planes + 3, up8(rows + 3), LANES), f32),
            pltpu.VMEM((rows + 3, block, LANES), f32),
            side, side, acc, acc, field, field, field, field,
            pltpu.VMEM((6 * cases, nodes * 3 * LANES), bf16),
            pltpu.VMEM((cases, LANES), f32),
        ],
        compiler_params=PARAMS,
        name="operator",
    )(
        start, own, pair, lower, upper, from_ym, from_yp, pair_ym, pair_yp,
        corner_edge, corner_second, *early,
    )

    groups = [
        [x * count_y + y for x in range(side, count_x, 2) for y in range(count_y)]
        for side in range(2)
    ]

    def gathered(copies):
        mine = lax.all_to_all(copies, ("gx", "gy"), 0, 0, axis_index_groups=groups)
        return mine, swapped(mine)

    system = gathered(system)

    weighted = pl.pallas_call(
        functools.partial(solve_kernel, sizes),
        out_shape=jax.ShapeDtypeStruct((devices // 2, planes, rows, LANES), f32),
        in_specs=[VMEM] * 4,
        out_specs=VMEM,
        scratch_shapes=[
            pltpu.VMEM((2 * cases, LANES), f32),
            field,
            field,
            pltpu.VMEM((rows, 8, LANES), f32),
            pltpu.VMEM((LANES, LANES), f32),
            pltpu.VMEM((3 * cases, LANES), f32),
        ],
        compiler_params=PARAMS,
        name="solve",
    )(*system, both, codes)

    blocks = gathered(weighted)
    return pl.pallas_call(
        functools.partial(filter_kernel, sizes, counts),
        out_shape=jax.ShapeDtypeStruct((planes, rows, LANES), f32),
        in_specs=[scalars] + [VMEM] * 3,
        out_specs=VMEM,
        scratch_shapes=[pltpu.VMEM((planes + 4, rows + 4, LANES), f32)],
        compiler_params=PARAMS,
        name="cone",
    )(start, *blocks, scale)


def solution(mesh):
    return jax.shard_map(
        local,
        mesh=mesh,
        in_specs=(P(None, None, "gx", "gy", None), P("gx", "gy", None), P("gx", "gy", None)),
        out_specs=P("gx", "gy", None),
        check_vma=False,
    )
```

```python
import functools
import math

import jax
import jax.numpy as jnp
from jax import lax
from jax.experimental import pallas as pl
from jax.experimental.pallas import tpu as pltpu
from jax.sharding import PartitionSpec as P

LEVELS = 16
LOAD = 0.2
LANES = 128
POISSON = 0.3
LAME = POISSON / ((1.0 + POISSON) * (1.0 - 2.0 * POISSON))
SHEAR = 1.0 / (2.0 * (1.0 + POISSON))
DIAGONAL = (LAME + 2.0 * SHEAR) / 9.0 + 2.0 * SHEAR / 9.0
VMEM = pl.BlockSpec(memory_space=pltpu.VMEM)
PARAMS = pltpu.CompilerParams(vmem_limit_bytes=30 * 2**20)
f32 = jnp.float32
bf16 = jnp.bfloat16


def up8(count):
    return -(-count // 8) * 8


def shift_down(value):
    lane = lax.broadcasted_iota(jnp.int32, value.shape, value.ndim - 1)
    rolled = pltpu.roll(value, LANES - 1, value.ndim - 1)
    return jnp.where(lane == LANES - 1, 0.0, rolled)


def shift_up(value):
    lane = lax.broadcasted_iota(jnp.int32, value.shape, value.ndim - 1)
    return jnp.where(lane == 0, 0.0, pltpu.roll(value, 1, value.ndim - 1))


def unrolled(count, factor, body):
    def turn(step, _):
        for offset in range(factor):
            body(step * factor + offset)
        return 0

    turns = count // factor
    if turns:
        lax.fori_loop(0, turns, turn, 0)
    for index in range(turns * factor, count):
        body(index)


def split(value):
    high = value.astype(bf16)
    return high, (value - high.astype(f32)).astype(bf16)


def modes_of(lower, upper):
    out = [[[[None] * 3 for _ in range(2)] for _ in range(2)] for _ in range(2)]
    for a in range(2):
        for c in range(2):
            for k in range(3):
                if a or c:
                    out[a][0][c][k] = lower[a][c][k] + upper[a][c][k]
                out[a][1][c][k] = upper[a][c][k] - lower[a][c][k]
    return out


PAIRS = (((1, 1, 0, 0), (0, 1, 1, 2)), ((1, 0, 1, 0), (0, 1, 1, 1)), ((1, 1, 0, 1), (1, 0, 1, 2)))
TRIPLE = ((0, 1, 1, 0), (1, 0, 1, 1), (1, 1, 0, 2))
SHEARS = (((0, 1, 0, 0), (1, 0, 0, 1)), ((0, 0, 1, 0), (1, 0, 0, 2)), ((0, 0, 1, 1), (0, 1, 0, 2)))
AXIAL = ((1, 0, 0, 0), (0, 1, 0, 1), (0, 0, 1, 2))


def at(modes, place):
    a, b, c, k = place
    return modes[a][b][c][k]


def mode_forces(modes, stiff):
    out = [[[[None] * 3 for _ in range(2)] for _ in range(2)] for _ in range(2)]

    def put(place, value):
        a, b, c, k = place
        out[a][b][c][k] = value

    shear = stiff * (SHEAR / 16)
    for first, second in SHEARS:
        force = shear * (at(modes, first) + at(modes, second))
        put(first, force)
        put(second, force)
    one, two, three = (at(modes, place) for place in AXIAL)
    volume = (stiff * (LAME / 16)) * (one + two + three)
    axial = stiff * (SHEAR / 8)
    for place in AXIAL:
        put(place, volume + axial * at(modes, place))
    own, cross = stiff * ((LAME + 3 * SHEAR) / 48), stiff * (LAME / 48)
    for first, second in PAIRS:
        one, two = at(modes, first), at(modes, second)
        put(first, own * one + cross * two)
        put(second, own * two + cross * one)
    twist = stiff * (SHEAR / 48)
    one, two, three = (at(modes, place) for place in TRIPLE)
    total = one + two + three
    for place in TRIPLE:
        put(place, twist * (total + at(modes, place)))
    last = stiff * ((LAME + 4 * SHEAR) / 144)
    for k in range(3):
        put((1, 1, 1, k), last * modes[1][1][1][k])
    return out


def mode_energy(modes):
    def square(value):
        return value * value

    shear = None
    for first, second in SHEARS:
        term = square(at(modes, first) + at(modes, second))
        shear = term if shear is None else shear + term
    one, two, three = (at(modes, place) for place in AXIAL)
    energy = (SHEAR / 16) * shear + (LAME / 16) * square(one + two + three)
    energy = energy + (SHEAR / 8) * (square(one) + square(two) + square(three))
    squares, products = None, None
    for first, second in PAIRS:
        one, two = at(modes, first), at(modes, second)
        term, product = square(one) + square(two), one * two
        squares = term if squares is None else squares + term
        products = product if products is None else products + product
    energy = energy + ((LAME + 3 * SHEAR) / 48) * squares + (LAME / 24) * products
    one, two, three = (at(modes, place) for place in TRIPLE)
    twist = square(one + two + three) + square(one) + square(two) + square(three)
    energy = energy + (SHEAR / 48) * twist
    last = square(modes[1][1][1][0]) + square(modes[1][1][1][1]) + square(modes[1][1][1][2])
    return energy + ((LAME + 4 * SHEAR) / 144) * last


def x_modes(find, plane, row, tile, cases):
    sums, diffs, columns, column = find(row)
    out = [[[None] * 3 for _ in range(2)] for _ in range(2)]
    for c, ref in enumerate((sums, diffs)):
        for k in range(3):
            rows = pl.ds(pl.multiple_of(k * cases + tile * 8, 8), 8)
            one = ref[plane * columns + column, rows, :]
            two = ref[(plane + 1) * columns + column, rows, :]
            out[0][c][k] = one + two
            out[1][c][k] = two - one
    return out


def whole(sums, diffs, columns):
    return lambda row: (sums, diffs, columns, row)


def apply_elements(find, stiff_ref, acc_s, acc_d, planes, rows, kept, stiff_x, stiff_y, cases):
    columns = len(kept)
    tiles = cases // 8
    for column in range(columns):
        acc_s[column] = jnp.zeros(acc_s.shape[1:], f32)
        acc_d[column] = jnp.zeros(acc_d.shape[1:], f32)

    def step(index, _):
        plane, tile = index // tiles, index % tiles

        def emit(row, total):
            if row not in kept:
                return
            for c, acc in enumerate((acc_s, acc_d)):
                for k in range(3):
                    lines = pl.ds(pl.multiple_of(k * cases + tile * 8, 8), 8)
                    low = plane * columns + row - kept[0]
                    acc[low, lines, :] += total[0][c][k] - total[1][c][k]
                    acc[low + columns, lines, :] = total[0][c][k] + total[1][c][k]

        lower = x_modes(find, plane, 0, tile, cases)
        carry = None
        for row in range(rows):
            upper = x_modes(find, plane, row + 1, tile, cases)
            stiff = jnp.broadcast_to(
                stiff_ref[plane + stiff_x, pl.ds(row + stiff_y, 1), :], (8, LANES)
            )
            forces = mode_forces(modes_of(lower, upper), stiff)
            here = [[[None] * 3 for _ in range(2)] for _ in range(2)]
            following = [[[None] * 3 for _ in range(2)] for _ in range(2)]
            for a in range(2):
                for c in range(2):
                    for k in range(3):
                        one, two = forces[a][0][c][k], forces[a][1][c][k]
                        low = -two if one is None else one - two
                        high = two if one is None else one + two
                        here[a][c][k] = low if carry is None else carry[a][c][k] + low
                        following[a][c][k] = high
            emit(row, here)
            carry, lower = following, upper
        emit(rows, carry)
        return 0

    lax.fori_loop(0, planes * tiles, step, 0)


def fill(source, base, sizes, ref, xs, ys, code_xs, code_ys):
    planes, rows, cases = sizes
    block = 3 * cases
    line = 0
    for x in xs:
        start = (x * rows + ys[0]) * block
        count = len(ys) * block
        ref[line : line + count, :] = source[start : start + count, :]
        line += count
    for x in code_xs:
        start = base + x * rows + code_ys[0]
        ref[line : line + len(code_ys), :] = source[start : start + len(code_ys), :]
        line += len(code_ys)
    if line < ref.shape[0]:
        ref[line:, :] = jnp.zeros((ref.shape[0] - line, LANES), f32)


def pack_kernel(sizes, forces, codes, own, up, *down):
    planes, rows, cases = sizes
    block = 3 * cases
    base = planes * rows * block
    for x in range(planes):
        own[base + x * rows : base + (x + 1) * rows, :] = codes[x]
        scale = jnp.where(codes[x] > 0.0, LOAD, 0.0)
        for k in range(3):
            for c in range(cases):
                start = x * rows * block + k * cases + c
                own[pl.ds(start, rows, stride=block), :] = forces[k, c, x] * scale

    every_y, last = range(rows), (planes - 2, planes - 1)
    fill(own, base, sizes, up, last[1:], every_y, last, every_y)
    for ref in down:
        fill(own, base, sizes, ref, (0, 1), every_y, (0, 1), every_y)


def rows_kernel(sizes, own, ym, yp):
    planes, rows, cases = sizes
    base = planes * rows * 3 * cases
    every_x = range(planes)
    fill(own, base, sizes, ym, every_x, (0, 1), every_x, (0, 1))
    fill(own, base, sizes, yp, every_x, (rows - 1,), every_x, (rows - 2, rows - 1))


def corner_kernel(sizes, first, ym, yp, out):
    planes, rows, cases = sizes
    block = 3 * cases
    even = first[0] // planes % 2 == 0
    line = 0
    for source, width in ((ym, 1), (yp, 2)):
        size = width * block
        parts = [(at, (planes - 2) * size + at, block) for at in range(0, 2 * size, block)]
        parts.append((planes * size, planes * size + (planes - 2) * 2, 4))
        for low, high, count in parts:
            value = lines(source, low, count)
            if low != high:
                value = jnp.where(even, value, lines(source, high, count))
            out[line : line + count, :] = value
            line += count
        out[line : line + 4, :] = jnp.zeros((4, LANES), f32)
        line += 4


def lines(ref, start, count):
    return ref[start : start + count, :]


def inside(ref, x, y, rows, block):
    return lines(ref, (x * rows + y) * block, block)


def beyond(refs, slot, y, rows, block):
    below, above = refs
    if y < 0:
        return lines(below, slot * block, block)
    return lines(above, (slot * 2 + y - rows) * block, block)


def beyond_codes(refs, slots, slot, y, block):
    below, above = refs
    if y < 0:
        return lines(below, slots * block + slot * 2, 2)
    return lines(above, slots * 2 * block + slot * 2, 2)


def corner(ref, slot, y, rows, block):
    start = slot * block if y < 0 else 2 * block + 8 + (slot * 2 + y - rows) * block
    return lines(ref, start, block)


def corner_codes(ref, slot, y, block):
    return lines(ref, (2 * block if y < 0 else 6 * block + 8) + slot * 2, 2)


def node_inverse(signed, count, out):
    planes = signed.shape[0]
    for x in range(1, planes):
        codes = signed[x, 0 : count + 1, :]
        total = jnp.abs(signed[x - 1, 0 : count + 1, :]) + jnp.abs(codes)
        total = total[:-1] + total[1:]
        total = total + shift_up(total)
        free = codes[1:] > 0.0
        value = 1.0 / (DIAGONAL * jnp.where(free, total, 1.0))
        out[x - 1, 0:count, :] = jnp.where(free, value, 0.0)
    for x in range(planes):
        signed[x] = jnp.abs(signed[x])


def place_column(sums, diffs, column, value):
    moved = shift_down(value)
    sums[column] = value + moved
    diffs[column] = moved - value


def early_kernel(
    sizes, first, own, pair, ym, yp, ym_pair, yp_pair, start, sums, diffs, acc_s, acc_d,
    stiff_ref, inverse,
):
    planes, rows, cases = sizes
    block = 3 * cases
    ys = rows + 3
    even = first[0] // planes % 2 == 0
    y_own, y_pair = (ym, yp), (ym_pair, yp_pair)

    def both_ways(w, read):
        low = read(True, w + 1) if w + 1 < planes else read(False, w + 1 - planes)
        high = read(False, planes + w - 1) if w < 1 else read(True, w - 1)
        return jnp.where(even, low, high)

    def codes(w, y):
        def read(mine, x):
            if y == 0:
                return lines(own if mine else pair, (planes * block + x) * rows, rows)
            return beyond_codes(y_own if mine else y_pair, planes, x, y, block)

        return both_ways(w, read)

    for w in range(-1, planes + 1):
        for y, count in ((-2, 2), (0, rows), (rows, 2)):
            stiff_ref[w + 1, y + 2 : y + 2 + count, :] = codes(w, y)
    node_inverse(stiff_ref, ys, inverse)
    for w in range(planes + 1):
        for y in range(-1, rows + 2):

            def read(mine, x):
                if 0 <= y < rows:
                    return inside(own if mine else pair, x, y, rows, block)
                return beyond(y_own if mine else y_pair, x, y, rows, block)

            value = both_ways(w, read) * inverse[w, y + 1 : y + 2, :]
            column = w * ys + y + 1
            start[column] = value
            place_column(sums, diffs, column, value)
    kept = range(1, rows + 2)
    find = whole(sums, diffs, ys)
    apply_elements(find, stiff_ref, acc_s, acc_d, planes, rows + 2, kept, 1, 1, cases)


def core_rows(rows):
    return range(2, rows - 1)


def rim_rows(rows):
    return (0, 1, rows - 1, rows)


def rim_columns(planes, rows):
    own = [(x, y) for x in range(planes) for y in rim_rows(rows) if y < rows]
    beyond_own = [(x, rows) for x in range(planes)] + [(planes, y) for y in rim_rows(rows)]
    return own + beyond_own, len(own)


def merged(x, planes, even, early, near):
    low = ([x - 1] if x >= 1 else [], [x + 1] if x <= 1 else [])
    high = ([x + 1] if x < planes else [], [x - planes + 1] if x >= planes - 1 else [])
    if low[0] and low[1] and high[0] and high[1]:
        one = early(jnp.where(even, low[0][0], high[0][0]))
        return one + near(jnp.where(even, low[1][0], high[1][0]))

    def read(places):
        found = [early(w) for w in places[0]] + [near(v) for v in places[1]]
        return found[0] if len(found) == 1 else found[0] + found[1]

    return jnp.where(even, read(low), read(high))


def direction_at(x, planes, even, early, middle):
    if x == 0:
        return jnp.where(even, middle, early(1))
    if x == planes:
        return jnp.where(even, early(planes - 1), middle)
    return early(jnp.where(even, x - 1, x + 1))


def keep_pair(ref, place, one, two, cases):
    for k in range(3):
        part = slice(k * cases, (k + 1) * cases)
        high, rest = split(jnp.concatenate([one[part], two[part]], 0))
        lane = pl.ds(pl.multiple_of((place * 3 + k) * LANES, LANES), LANES)
        ref[0 : 2 * cases, lane] = high
        ref[2 * cases : 4 * cases, lane] = rest


def products(first, second):
    contract = (((1,), (1,)), ((), ()))
    out = lax.dot_general(first, second, contract, preferred_element_type=f32)
    left, right = out.shape[0] // 2, out.shape[1] // 2
    out = out[:, :right] + out[:, right:]
    return out[:left] + out[left:]


def middle_kernel(
    sizes, first, own, pair, lower, upper, start, sums_e, diffs_e, acc_se, acc_de,
    sums, diffs, middle, acc_s, acc_d, w_sums, w_diffs, both_out, gram_out,
    stiff_ref, inverse, right,
):
    planes, rows, cases = sizes
    block = 3 * cases
    ys, nodes_y, inner = rows + 3, rows + 1, rows - 1
    core = core_rows(rows)
    even = first[0] // planes % 2 == 0

    def codes(x):
        if 0 <= x < planes:
            return lines(own, (planes * block + x) * rows, rows)
        if x < 0:
            outer = lines(lower, (block + x + 2) * rows, rows)
            return jnp.where(even, outer, lines(pair, (planes * block + planes + x) * rows, rows))
        slot = x - planes
        outer = lines(upper, (2 * block + slot) * rows, rows)
        return jnp.where(even, lines(pair, (planes * block + slot) * rows, rows), outer)

    for x in range(-2, planes + 2):
        stiff_ref[x + 2, 0:rows, :] = codes(x)
    node_inverse(stiff_ref, inner, inverse)

    def place(v, x, ref, slot):
        for y in range(1, rows):
            value = inside(ref, slot, y, rows, block) * inverse[x + 1, y - 1 : y, :]
            if v == 1:
                middle[y - 1] = value
            place_column(sums, diffs, v * inner + y - 1, value)

    def copy(v, w):
        for y in range(1, rows):
            sums[v * inner + y - 1] = sums_e[w * ys + y + 1]
            diffs[v * inner + y - 1] = diffs_e[w * ys + y + 1]

    @pl.when(even)
    def _():
        place(0, -1, lower, 0)
        place(1, 0, own, 0)
        copy(2, 0)

    @pl.when(jnp.logical_not(even))
    def _():
        copy(0, planes)
        place(1, planes, upper, 0)
        place(2, planes + 1, upper, 1)

    layer = jnp.where(even, 1, planes + 1)
    find = whole(sums, diffs, inner)
    apply_elements(find, stiff_ref, acc_s, acc_d, 2, rows - 2, range(inner), layer, 1, cases)

    def image(x, y, place):
        def total(early, near):
            return merged(
                x, planes, even, lambda w: early[w * nodes_y + y],
                lambda v: near[v * inner + y - 1],
            )

        s, d = total(acc_se, acc_s), total(acc_de, acc_d)
        force = s - d + shift_up(s + d)
        scaled = force * inverse[x + 1, pl.ds(y - 1, 1), :]
        place_column(w_sums, w_diffs, place, scaled)
        value = direction_at(x, planes, even, lambda w: start[w * ys + y + 1], middle[y - 1])
        keep_pair(both_out, place, value, scaled, cases)
        return force

    def within(x, index):
        y, place = core[0] + index, x * len(core) + index
        force = image(x, y, place)
        given = own[pl.ds(pl.multiple_of((x * rows + y) * block, 8), block), :]
        keep_pair(right, place, given, force, cases)

    for x in range(planes):
        unrolled(len(core), len(core), functools.partial(within, x))
    last = planes * len(core)
    unrolled(len(core), len(core), lambda index: image(planes, core[0] + index, last + index))
    gram_out[...] = products(right[...], both_out[:, : last * 3 * LANES])


def main_kernel(
    sizes, first, own, pair, lower, upper, ym, yp, ym_pair, yp_pair, corners,
    start, sums_e, diffs_e, acc_se, acc_de,
    sums_m, diffs_m, middle_m, acc_sm, acc_dm, w_sm, w_dm, both_m, gram_m,
    both_out, system_out, stiff_ref, inverse,
    middle, sums, diffs, acc_s0, acc_d0, acc_s1, acc_d1, w_sums, w_diffs,
    acc2_s, acc2_d, right, second_m, second_r, table,
):
    planes, rows, cases = sizes
    block = 3 * cases
    ys, nodes_y, inner = rows + 3, rows + 1, rows - 1
    core, rim = core_rows(rows), rim_rows(rows)
    columns, own_count = rim_columns(planes, rows)
    even = first[0] // planes % 2 == 0
    y_own, y_pair = (ym, yp), (ym_pair, yp_pair)

    def codes(x, y):
        def read(mine, plane):
            if y == 0:
                return lines(own if mine else pair, (planes * block + plane) * rows, rows)
            return beyond_codes(y_own if mine else y_pair, planes, plane, y, block)

        if 0 <= x < planes:
            return read(True, x)
        ref, count, slot = (lower, 1, x + 2) if x < 0 else (upper, 2, x - planes)
        if y == 0:
            outer = lines(ref, (count * block + slot) * rows, rows)
        else:
            outer = corner_codes(corners, slot, y, block)
        within = read(False, planes + x if x < 0 else x - planes)
        return jnp.where(even, outer, within) if x < 0 else jnp.where(even, within, outer)

    for x in range(-2, planes + 2):
        for y, count in ((-2, 2), (0, rows), (rows, 2)):
            stiff_ref[x + 2, y + 2 : y + 2 + count, :] = codes(x, y)
    node_inverse(stiff_ref, ys, inverse)

    sides = (-1, 0, rows, rows + 1)

    def place(v, x, ref, slot, beyond_at):
        for i, y in enumerate(sides):
            value = inside(ref, slot, y, rows, block) if y == 0 else beyond_at(y)
            value = value * inverse[x + 1, y + 1 : y + 2, :]
            if v == 1 and y in (0, rows):
                middle[y // rows] = value
            place_column(sums, diffs, v * 4 + i, value)

    def copy(v, w):
        for i, y in enumerate(sides):
            sums[v * 4 + i] = sums_e[w * ys + y + 1]
            diffs[v * 4 + i] = diffs_e[w * ys + y + 1]

    @pl.when(even)
    def _():
        place(0, -1, lower, 0, lambda y: corner(corners, 1, y, rows, block))
        place(1, 0, own, 0, lambda y: beyond(y_own, 0, y, rows, block))
        copy(2, 0)

    @pl.when(jnp.logical_not(even))
    def _():
        copy(0, planes)
        place(1, planes, upper, 0, lambda y: corner(corners, 0, y, rows, block))
        place(2, planes + 1, upper, 1, lambda y: corner(corners, 1, y, rows, block))

    def find_low(row):
        return (sums, diffs, 4, row) if row < 2 else (sums_m, diffs_m, inner, 0)

    def find_high(row):
        return (sums, diffs, 4, row + 1) if row else (sums_m, diffs_m, inner, inner - 1)

    layer = jnp.where(even, 1, planes + 1)
    apply_elements(find_low, stiff_ref, acc_s0, acc_d0, 2, 2, range(1, 3), layer, 1, cases)
    apply_elements(find_high, stiff_ref, acc_s1, acc_d1, 2, 2, range(2), layer, rows + 1, cases)

    def image(x, y, place):
        def total(early, near, low, high):
            def outer(v):
                value = low[v * 2 + y] if y < 2 else high[v * 2 + y - inner]
                return value + near[v * inner + y - 1] if y in (1, inner) else value

            return merged(x, planes, even, lambda w: early[w * nodes_y + y], outer)

        s = total(acc_se, acc_sm, acc_s0, acc_s1)
        d = total(acc_de, acc_dm, acc_d0, acc_d1)
        force = s - d + shift_up(s + d)
        scaled = force * inverse[x + 1, y + 1 : y + 2, :]
        place_column(w_sums, w_diffs, x * len(rim) + rim.index(y), scaled)
        inner_middle = middle_m[y - 1] if y in (1, inner) else middle[y // rows]
        value = direction_at(x, planes, even, lambda w: start[w * ys + y + 1], inner_middle)
        keep_pair(both_out, place, value, scaled, cases)
        return force

    for index, (x, y) in enumerate(columns):
        force = image(x, y, index)
        if index < own_count:
            keep_pair(right, index, inside(own, x, y, rows, block), force, cases)

    def find(row):
        if row in rim:
            return w_sums, w_diffs, len(rim), rim.index(row)
        return w_sm, w_dm, len(core), row - core[0]

    apply_elements(find, stiff_ref, acc2_s, acc2_d, planes, rows, range(nodes_y), 2, 2, cases)

    def second_force(ref, x, y, place):
        column = x * nodes_y + y
        s, d = acc2_s[column], acc2_d[column]
        force = s - d + shift_up(s + d)
        for k in range(3):
            value = force[k * cases : (k + 1) * cases]
            high = value.astype(bf16).astype(f32)
            lane = pl.ds(pl.multiple_of((place * 3 + k) * LANES, LANES), LANES)
            ref[:, lane] = jnp.concatenate([high, value - high], 0).astype(bf16)

    unrolled(
        (planes + 1) * len(core), len(core),
        lambda index: second_force(
            second_m, index // len(core), core[0] + index % len(core), index
        ),
    )
    for index, (x, y) in enumerate(columns):
        second_force(second_r, x, y, index)

    two = 2 * cases
    gram = products(right[...], both_out[:, : own_count * 3 * LANES]) + gram_m[...]
    other = products(second_m[...], both_m[...]) + products(second_r[...], both_out[...])
    row = lax.broadcasted_iota(jnp.int32, (cases, cases), 0)
    column = lax.broadcasted_iota(jnp.int32, (cases, cases), 1)
    load_load, load_image = gram[:cases, :cases], gram[cases:, :cases]
    mixed, image_image = other[:, :cases], other[:, cases:]
    table[...] = jnp.zeros(table.shape, f32)
    table[:, 0:cases] = jnp.where(row <= column, load_load, load_image)
    table[:, cases:two] = jnp.where(row <= column, mixed, image_image)
    for lane, value in ((two, load_image), (two + 1, image_image)):
        own_entries = jnp.where(row == column, value, 0.0)
        table[:, lane : lane + 1] = jnp.sum(own_entries, axis=1, keepdims=True)
    half = cases // 2
    folded = table[:half, :] + pltpu.roll(table[half:, :], LANES // 2, 1)
    depth = system_out.shape[2]
    for index in range(system_out.shape[0]):
        for part in range(half // depth):
            system_out[index, part] = folded[part * depth : (part + 1) * depth]


def solve_kernel(
    sizes, system, system_pair, both_m, both_r, codes, out, mixing, sums, diffs, energy, square, full
):
    planes, rows, cases = sizes
    two = 2 * cases
    nodes_y = rows + 1
    count = planes * rows
    total = jnp.sum(system[...], axis=0) + jnp.sum(system_pair[...], axis=0)
    half, depth = cases // 2, system.shape[2]
    square[...] = jnp.zeros(square.shape, f32)
    for part in range(half // depth):
        value = total[part]
        square[part * depth : (part + 1) * depth, :] = value
        lines = slice(half + part * depth, half + (part + 1) * depth)
        square[lines, :] = pltpu.roll(value, LANES // 2, 1)
    value, turned = square[0:cases, :], jnp.transpose(square[...])
    line = lax.broadcasted_iota(jnp.int32, (cases, cases), 0)
    place = lax.broadcasted_iota(jnp.int32, (cases, cases), 1)

    def mended(start, diagonal=None):
        kept, other = value[:, start : start + cases], turned[start : start + cases, :cases]
        if diagonal is None:
            return jnp.where(line <= place, kept, other)
        inner = jnp.where(line < place, other, value[:, diagonal : diagonal + 1])
        return jnp.where(line > place, kept, inner)

    load_image, mixed = mended(0, two), mended(cases)
    parts = ((load_image, mixed), (mixed, mended(cases, two + 1)), (mended(0), load_image))
    full[...] = jnp.zeros(full.shape, f32)
    for index, (left, right) in enumerate(parts):
        full[index * cases : (index + 1) * cases, 0:cases] = left
        full[index * cases : (index + 1) * cases, cases:two] = right
    table = full[...]
    lane = lax.broadcasted_iota(jnp.int32, (1, LANES), 1)
    gone, wide = 0, 4
    for pivot in range(0, two, wide):
        drop = pivot // 8 * 8 - gone
        table = table[drop:]
        gone += drop
        line = pivot - gone
        inner = (lane >= pivot) & (lane < pivot + wide)
        found = [table[line + p : line + p + 1, :] for p in range(wide)]
        block = [
            [jnp.broadcast_to(row[:, pivot + q : pivot + q + 1], row.shape) for q in range(wide)]
            for row in found
        ]
        solved = [
            jnp.where(lane == pivot + p, -1.0, jnp.where(inner, 0.0, found[p]))
            for p in range(wide)
        ]
        for p in range(wide):
            inverse = 1.0 / block[p][p]
            solved[p] = solved[p] * inverse
            block[p] = [value * inverse for value in block[p]]
            for q in range(wide):
                if q != p:
                    factor = block[q][p]
                    solved[q] = solved[q] - factor * solved[p]
                    for r in range(p + 1, wide):
                        block[q][r] = block[q][r] - factor * block[p][r]
        update = None
        for q in range(wide):
            term = table[:, pivot + q : pivot + q + 1] * solved[q]
            update = term if update is None else update + term
        table = jnp.where(inner, 0.0, table) - update
    answer = table[two - gone :, :two]
    high = answer.astype(bf16).astype(f32)
    mixing[...] = jnp.zeros(mixing.shape, f32)
    mixing[0:cases, 0:two] = high
    mixing[0:cases, two : 2 * two] = high
    mixing[cases:two, 0:two] = answer - high
    mix = mixing[...][:, : 2 * two].astype(bf16)

    def combined(ref, place, width):
        value = jnp.dot(
            mix, ref[:, place * 3 * LANES : (place + width) * 3 * LANES], preferred_element_type=f32
        )
        return value[:cases] + value[cases:]

    def keep(value, index, column):
        for k in range(3):
            part = value[:, (index * 3 + k) * LANES : (index * 3 + k + 1) * LANES]
            moved = shift_down(part)
            sums[column, k * cases : (k + 1) * cases, :] = part + moved
            diffs[column, k * cases : (k + 1) * cases, :] = moved - part

    core = core_rows(rows)
    for x in range(planes + 1):
        value = combined(both_m, x * len(core), len(core))
        for index, y in enumerate(core):
            keep(value, index, x * nodes_y + y)
    columns, _ = rim_columns(planes, rows)
    for start in range(0, len(columns), 6):
        some = columns[start : start + 6]
        value = combined(both_r, start, len(some))
        for index, (x, y) in enumerate(some):
            keep(value, index, x * nodes_y + y)

    find = whole(sums, diffs, nodes_y)
    tiles = cases // 8

    def step(plane, _):
        for tile in range(tiles):
            lower = x_modes(find, plane, 0, tile, cases)
            for row in range(rows):
                upper = x_modes(find, plane, row + 1, tile, cases)
                part = mode_energy(modes_of(lower, upper))
                if tile == 0:
                    energy[row] = part
                else:
                    energy[row] += part
                lower = upper
        total = jnp.sum(energy[...], axis=1)
        total = (-3.0 / cases) * jnp.abs(codes[plane]) * total
        for index in range(out.shape[0]):
            out[index, plane] = total
        return 0

    lax.fori_loop(0, planes, step, 0)


def smooth(ref, x, rows):
    weight = [2.5 - math.sqrt(q) for q in range(7)]
    near = {}
    for dx in range(-2, 3):
        for dy in range(-2, 3):
            q = dx * dx + dy * dy
            if q <= 5:
                value = ref[x + 2 + dx, 2 + dy : 2 + dy + rows, :]
                near[q] = value if q not in near else near[q] + value
    result = None
    for dz in range(3):
        part = None
        for q, value in near.items():
            if q + dz * dz <= 6:
                term = weight[q + dz * dz] * value
                part = term if part is None else part + term
        if dz == 0:
            result = part
        else:
            place = lax.broadcasted_iota(jnp.int32, part.shape, 1)
            forward = jnp.where(place >= LANES - dz, 0.0, pltpu.roll(part, LANES - dz, 1))
            backward = jnp.where(place < dz, 0.0, pltpu.roll(part, dz, 1))
            result = result + (forward + backward)
    return result


def scale_kernel(sizes, counts, start, levels, out, there):
    planes, rows, _ = sizes
    y = lax.broadcasted_iota(jnp.int32, (rows + 4, LANES), 0) + (start[1] - 2)
    in_y = (y >= 0) & (y < counts[1] * rows)
    for x in range(planes + 4):
        global_x = start[0] + (x - 2)
        in_x = (global_x >= 0) & (global_x < counts[0] * planes)
        there[x] = jnp.where(in_y & in_x, 1.0, 0.0)
    for x in range(planes):
        density = 0.3 + 0.7 * levels[x].astype(f32) / (LEVELS - 1)
        out[x] = 1.0 / (density * smooth(there, x, rows))


def filter_kernel(sizes, counts, start, blocks, blocks_pair, scale, out, wide):
    planes, rows, _ = sizes
    sides_x = ((-1, planes - 2, planes, 0), (0, 0, planes, 2), (1, 0, 2, 2 + planes))
    sides_y = ((-1, rows - 2, rows, 0), (0, 0, rows, 2), (1, 0, 2, 2 + rows))
    for step_x, x0, x1, to_x in sides_x:
        for step_y, y0, y1, to_y in sides_y:
            at_x = start[0] // planes + step_x
            at_y = start[1] // rows + step_y
            inside = (at_x >= 0) & (at_x < counts[0]) & (at_y >= 0) & (at_y < counts[1])
            index = jnp.where(inside, at_x // 2 * counts[1] + at_y, 0)
            value = (blocks_pair if step_x else blocks)[index, x0:x1, y0:y1, :]
            wide[to_x : to_x + x1 - x0, to_y : to_y + y1 - y0, :] = jnp.where(inside, value, 0.0)
    for x in range(planes):
        out[x] = smooth(wide, x, rows) * scale[x]


def local(forces, levels, supports):
    _, cases, planes, rows, _ = forces.shape
    sizes = (planes, rows, cases)
    block = 3 * cases
    count_x, count_y = lax.axis_size("gx"), lax.axis_size("gy")

    def shape(blocks, codes):
        return jax.ShapeDtypeStruct((blocks * block + up8(codes), LANES), f32)

    density = 0.3 + 0.7 * levels.astype(f32) / (LEVELS - 1)
    codes = density * density * density
    codes = jnp.where(supports == 0, codes, -codes)
    start = jnp.stack([lax.axis_index("gx") * planes, lax.axis_index("gy") * rows])
    start = start.astype(jnp.int32)
    counts = (count_x, count_y)
    scalars = pl.BlockSpec(memory_space=pltpu.SMEM)
    whole = shape(planes * rows, planes * rows)
    down = [] if planes == 2 else [shape(2 * rows, 2 * rows)]
    own, up, *down = pl.pallas_call(
        functools.partial(pack_kernel, sizes),
        out_shape=[whole, shape(rows, 2 * rows), *down],
        in_specs=[VMEM] * 2,
        out_specs=[VMEM] * (2 + len(down)),
        compiler_params=PARAMS,
        name="pack",
    )(forces, codes)
    scale = pl.pallas_call(
        functools.partial(scale_kernel, sizes, counts),
        out_shape=jax.ShapeDtypeStruct((planes, rows, LANES), f32),
        in_specs=[scalars, VMEM],
        out_specs=VMEM,
        scratch_shapes=[pltpu.VMEM((planes + 4, rows + 4, LANES), f32)],
        compiler_params=PARAMS,
        name="scale",
    )(start, levels)

    def moved(value, axis, step):
        count = lax.axis_size(axis)
        pairs = [(i, i + step) for i in range(count) if 0 <= i + step < count]
        return lax.ppermute(value, axis, pairs)

    def links(first, step):
        return [(i, i + step) for i in range(first, count_x, 2) if 0 <= i + step < count_x]

    def swapped(value):
        return lax.ppermute(value, "gx", links(0, 1) + links(1, -1))

    def across(value):
        return lax.ppermute(value, "gx", links(1, 1) + links(2, -1))

    upper = lax.ppermute(down[0] if down else own, "gx", links(2, -1))
    lower = lax.ppermute(up, "gx", links(1, 1))
    pair = swapped(own)
    own, pair = lax.optimization_barrier((own, pair))
    ym, yp = pl.pallas_call(
        functools.partial(rows_kernel, sizes),
        out_shape=[shape(2 * planes, 2 * planes), shape(planes, 2 * planes)],
        in_specs=[VMEM],
        out_specs=[VMEM] * 2,
        compiler_params=PARAMS,
        name="rows",
    )(own)
    from_yp, from_ym = moved(ym, "gy", -1), moved(yp, "gy", 1)
    pair_yp, pair_ym = swapped(from_yp), swapped(from_ym)
    corners = across(
        pl.pallas_call(
            functools.partial(corner_kernel, sizes),
            out_shape=jax.ShapeDtypeStruct((6 * block + 16, LANES), f32),
            in_specs=[scalars] + [VMEM] * 2,
            out_specs=VMEM,
            compiler_params=PARAMS,
            name="corners",
        )(start, from_ym, from_yp)
    )

    devices = count_x * count_y
    nodes = (planes + 1) * (rows + 1)
    window = jax.ShapeDtypeStruct(((planes + 1) * (rows + 3), block, LANES), f32)
    partial_forces = jax.ShapeDtypeStruct((nodes, block, LANES), f32)
    early = pl.pallas_call(
        functools.partial(early_kernel, sizes),
        out_shape=[window] * 3 + [partial_forces] * 2,
        in_specs=[scalars] + [VMEM] * 6,
        out_specs=[VMEM] * 5,
        scratch_shapes=[
            pltpu.VMEM((planes + 2, up8(rows + 4), LANES), f32),
            pltpu.VMEM((planes + 1, up8(rows + 3), LANES), f32),
        ],
        compiler_params=PARAMS,
        cost_estimate=pl.CostEstimate(
            flops=200 * planes * rows * block * LANES, bytes_accessed=2**23, transcendentals=0
        ),
        name="early",
    )(start, own, pair, from_ym, from_yp, pair_ym, pair_yp)

    def columns(count):
        return jax.ShapeDtypeStruct((count, block, LANES), f32)

    def fields(lines, count):
        return jax.ShapeDtypeStruct((lines * cases, count * 3 * LANES), bf16)

    def scratch(value):
        return pltpu.VMEM(value.shape, value.dtype)

    core = len(core_rows(rows))
    middle = pl.pallas_call(
        functools.partial(middle_kernel, sizes),
        out_shape=[columns(3 * (rows - 1))] * 2
        + [columns(rows - 1)]
        + [columns(3 * (rows - 1))] * 2
        + [columns((planes + 1) * core)] * 2
        + [fields(4, (planes + 1) * core), jax.ShapeDtypeStruct((2 * cases, 2 * cases), f32)],
        in_specs=[scalars] + [VMEM] * 9,
        out_specs=[VMEM] * 9,
        scratch_shapes=[
            pltpu.VMEM((planes + 4, up8(rows), LANES), f32),
            pltpu.VMEM((planes + 3, up8(rows), LANES), f32),
            scratch(fields(4, planes * core)),
        ],
        compiler_params=PARAMS,
        name="middle",
    )(start, own, pair, lower, upper, *early)

    rim, rim_own = rim_columns(planes, rows)
    field = scratch(columns(nodes))
    both, system = pl.pallas_call(
        functools.partial(main_kernel, sizes),
        out_shape=[
            fields(4, len(rim)),
            jax.ShapeDtypeStruct((devices // 2, cases // 8, 4, LANES), f32),
        ],
        in_specs=[scalars] + [VMEM] * 23,
        out_specs=[VMEM] * 2,
        scratch_shapes=[
            pltpu.VMEM((planes + 4, up8(rows + 4), LANES), f32),
            pltpu.VMEM((planes + 3, up8(rows + 3), LANES), f32),
            scratch(columns(2)),
            *[scratch(columns(12))] * 2,
            *[scratch(columns(6))] * 4,
            *[scratch(columns((planes + 1) * 4))] * 2,
            field, field,
            scratch(fields(4, rim_own)),
            scratch(fields(2, (planes + 1) * core)),
            scratch(fields(2, len(rim))),
            pltpu.VMEM((cases, LANES), f32),
        ],
        compiler_params=PARAMS,
        name="operator",
    )(
        start, own, pair, lower, upper, from_ym, from_yp, pair_ym, pair_yp, corners,
        *early, *middle,
    )

    groups = [
        [x * count_y + y for x in range(side, count_x, 2) for y in range(count_y)]
        for side in range(2)
    ]

    def gathered(copies):
        mine = lax.all_to_all(copies, ("gx", "gy"), 0, 0, axis_index_groups=groups)
        return mine, swapped(mine)

    system = gathered(system)

    weighted = pl.pallas_call(
        functools.partial(solve_kernel, sizes),
        out_shape=jax.ShapeDtypeStruct((devices // 2, planes, rows, LANES), f32),
        in_specs=[VMEM] * 5,
        out_specs=VMEM,
        scratch_shapes=[
            pltpu.VMEM((2 * cases, LANES), f32),
            field,
            field,
            pltpu.VMEM((rows, 8, LANES), f32),
            pltpu.VMEM((LANES, LANES), f32),
            pltpu.VMEM((3 * cases, LANES), f32),
        ],
        compiler_params=PARAMS,
        name="solve",
    )(*system, middle[7], both, codes)

    blocks = gathered(weighted)
    return pl.pallas_call(
        functools.partial(filter_kernel, sizes, counts),
        out_shape=jax.ShapeDtypeStruct((planes, rows, LANES), f32),
        in_specs=[scalars] + [VMEM] * 3,
        out_specs=VMEM,
        scratch_shapes=[pltpu.VMEM((planes + 4, rows + 4, LANES), f32)],
        compiler_params=PARAMS,
        name="cone",
    )(start, *blocks, scale)


def solution(mesh):
    return jax.shard_map(
        local,
        mesh=mesh,
        in_specs=(P(None, None, "gx", "gy", None), P("gx", "gy", None), P("gx", "gy", None)),
        out_specs=P("gx", "gy", None),
        check_vma=False,
    )
```

```python
import functools
import math

import jax
import jax.numpy as jnp
from jax import lax
from jax.experimental import pallas as pl
from jax.experimental.pallas import tpu as pltpu
from jax.sharding import PartitionSpec as P

LEVELS = 16
LOAD = 0.2
LANES = 128
POISSON = 0.3
LAME = POISSON / ((1.0 + POISSON) * (1.0 - 2.0 * POISSON))
SHEAR = 1.0 / (2.0 * (1.0 + POISSON))
DIAGONAL = (LAME + 2.0 * SHEAR) / 9.0 + 2.0 * SHEAR / 9.0
VMEM = pl.BlockSpec(memory_space=pltpu.VMEM)
PARAMS = pltpu.CompilerParams(vmem_limit_bytes=30 * 2**20)
f32 = jnp.float32
bf16 = jnp.bfloat16


def up8(count):
    return -(-count // 8) * 8


def shift_down(value):
    lane = lax.broadcasted_iota(jnp.int32, value.shape, value.ndim - 1)
    rolled = pltpu.roll(value, LANES - 1, value.ndim - 1)
    return jnp.where(lane == LANES - 1, 0.0, rolled)


def shift_up(value):
    lane = lax.broadcasted_iota(jnp.int32, value.shape, value.ndim - 1)
    return jnp.where(lane == 0, 0.0, pltpu.roll(value, 1, value.ndim - 1))


def unrolled(count, factor, body):
    def turn(step, _):
        for offset in range(factor):
            body(step * factor + offset)
        return 0

    turns = count // factor
    if turns:
        lax.fori_loop(0, turns, turn, 0)
    for index in range(turns * factor, count):
        body(index)


def split(value):
    high = value.astype(bf16)
    return high, (value - high.astype(f32)).astype(bf16)


def modes_of(lower, upper):
    out = [[[[None] * 3 for _ in range(2)] for _ in range(2)] for _ in range(2)]
    for a in range(2):
        for c in range(2):
            for k in range(3):
                if a or c:
                    out[a][0][c][k] = lower[a][c][k] + upper[a][c][k]
                out[a][1][c][k] = upper[a][c][k] - lower[a][c][k]
    return out


PAIRS = (((1, 1, 0, 0), (0, 1, 1, 2)), ((1, 0, 1, 0), (0, 1, 1, 1)), ((1, 1, 0, 1), (1, 0, 1, 2)))
TRIPLE = ((0, 1, 1, 0), (1, 0, 1, 1), (1, 1, 0, 2))
SHEARS = (((0, 1, 0, 0), (1, 0, 0, 1)), ((0, 0, 1, 0), (1, 0, 0, 2)), ((0, 0, 1, 1), (0, 1, 0, 2)))
AXIAL = ((1, 0, 0, 0), (0, 1, 0, 1), (0, 0, 1, 2))


def at(modes, place):
    a, b, c, k = place
    return modes[a][b][c][k]


def mode_forces(modes, stiff):
    out = [[[[None] * 3 for _ in range(2)] for _ in range(2)] for _ in range(2)]

    def put(place, value):
        a, b, c, k = place
        out[a][b][c][k] = value

    shear = stiff * (SHEAR / 16)
    for first, second in SHEARS:
        force = shear * (at(modes, first) + at(modes, second))
        put(first, force)
        put(second, force)
    one, two, three = (at(modes, place) for place in AXIAL)
    volume = (stiff * (LAME / 16)) * (one + two + three)
    axial = stiff * (SHEAR / 8)
    for place in AXIAL:
        put(place, volume + axial * at(modes, place))
    own, cross = stiff * ((LAME + 3 * SHEAR) / 48), stiff * (LAME / 48)
    for first, second in PAIRS:
        one, two = at(modes, first), at(modes, second)
        put(first, own * one + cross * two)
        put(second, own * two + cross * one)
    twist = stiff * (SHEAR / 48)
    one, two, three = (at(modes, place) for place in TRIPLE)
    total = one + two + three
    for place in TRIPLE:
        put(place, twist * (total + at(modes, place)))
    last = stiff * ((LAME + 4 * SHEAR) / 144)
    for k in range(3):
        put((1, 1, 1, k), last * modes[1][1][1][k])
    return out


def mode_energy(modes):
    def square(value):
        return value * value

    shear = None
    for first, second in SHEARS:
        term = square(at(modes, first) + at(modes, second))
        shear = term if shear is None else shear + term
    one, two, three = (at(modes, place) for place in AXIAL)
    energy = (SHEAR / 16) * shear + (LAME / 16) * square(one + two + three)
    energy = energy + (SHEAR / 8) * (square(one) + square(two) + square(three))
    squares, products = None, None
    for first, second in PAIRS:
        one, two = at(modes, first), at(modes, second)
        term, product = square(one) + square(two), one * two
        squares = term if squares is None else squares + term
        products = product if products is None else products + product
    energy = energy + ((LAME + 3 * SHEAR) / 48) * squares + (LAME / 24) * products
    one, two, three = (at(modes, place) for place in TRIPLE)
    twist = square(one + two + three) + square(one) + square(two) + square(three)
    energy = energy + (SHEAR / 48) * twist
    last = square(modes[1][1][1][0]) + square(modes[1][1][1][1]) + square(modes[1][1][1][2])
    return energy + ((LAME + 4 * SHEAR) / 144) * last


def x_modes(find, plane, row, tile, cases):
    sums, diffs, columns, column = find(row)
    out = [[[None] * 3 for _ in range(2)] for _ in range(2)]
    for c, ref in enumerate((sums, diffs)):
        for k in range(3):
            rows = pl.ds(pl.multiple_of(k * cases + tile * 8, 8), 8)
            one = ref[plane * columns + column, rows, :]
            two = ref[(plane + 1) * columns + column, rows, :]
            out[0][c][k] = one + two
            out[1][c][k] = two - one
    return out


def whole(sums, diffs, columns):
    return lambda row: (sums, diffs, columns, row)


def apply_elements(find, stiff_ref, acc_s, acc_d, planes, rows, kept, stiff_x, stiff_y, cases):
    columns = len(kept)
    tiles = cases // 8
    for column in range(columns):
        acc_s[column] = jnp.zeros(acc_s.shape[1:], f32)
        acc_d[column] = jnp.zeros(acc_d.shape[1:], f32)

    def step(index, _):
        plane, tile = index // tiles, index % tiles

        def emit(row, total):
            if row not in kept:
                return
            for c, acc in enumerate((acc_s, acc_d)):
                for k in range(3):
                    lines = pl.ds(pl.multiple_of(k * cases + tile * 8, 8), 8)
                    low = plane * columns + row - kept[0]
                    acc[low, lines, :] += total[0][c][k] - total[1][c][k]
                    acc[low + columns, lines, :] = total[0][c][k] + total[1][c][k]

        lower = x_modes(find, plane, 0, tile, cases)
        carry = None
        for row in range(rows):
            upper = x_modes(find, plane, row + 1, tile, cases)
            stiff = jnp.broadcast_to(
                stiff_ref[plane + stiff_x, pl.ds(row + stiff_y, 1), :], (8, LANES)
            )
            forces = mode_forces(modes_of(lower, upper), stiff)
            here = [[[None] * 3 for _ in range(2)] for _ in range(2)]
            following = [[[None] * 3 for _ in range(2)] for _ in range(2)]
            for a in range(2):
                for c in range(2):
                    for k in range(3):
                        one, two = forces[a][0][c][k], forces[a][1][c][k]
                        low = -two if one is None else one - two
                        high = two if one is None else one + two
                        here[a][c][k] = low if carry is None else carry[a][c][k] + low
                        following[a][c][k] = high
            emit(row, here)
            carry, lower = following, upper
        emit(rows, carry)
        return 0

    lax.fori_loop(0, planes * tiles, step, 0)


def fill(source, base, sizes, ref, xs, ys, code_xs, code_ys):
    planes, rows, cases = sizes
    block = 3 * cases
    line = 0
    for x in xs:
        start = (x * rows + ys[0]) * block
        count = len(ys) * block
        ref[line : line + count, :] = source[start : start + count, :]
        line += count
    for x in code_xs:
        start = base + x * rows + code_ys[0]
        ref[line : line + len(code_ys), :] = source[start : start + len(code_ys), :]
        line += len(code_ys)
    if line < ref.shape[0]:
        ref[line:, :] = jnp.zeros((ref.shape[0] - line, LANES), f32)


def pack_kernel(sizes, forces, codes, own, *down):
    planes, rows, cases = sizes
    block = 3 * cases
    base = planes * rows * block
    for x in range(planes):
        own[base + x * rows : base + (x + 1) * rows, :] = codes[x]
        scale = jnp.where(codes[x] > 0.0, LOAD, 0.0)
        for k in range(3):
            for c in range(cases):
                start = x * rows * block + k * cases + c
                own[pl.ds(start, rows, stride=block), :] = forces[k, c, x] * scale

    every_y = range(rows)
    for ref in down:
        fill(own, base, sizes, ref, (0, 1), every_y, (0, 1), every_y)


def up_kernel(sizes, begun, own, up):
    planes, rows, cases = sizes
    last, every_y = (planes - 2, planes - 1), range(rows)
    fill(own, planes * rows * 3 * cases, sizes, up, last[1:], every_y, last, every_y)


def rows_kernel(sizes, own, ym, yp):
    planes, rows, cases = sizes
    base = planes * rows * 3 * cases
    every_x = range(planes)
    fill(own, base, sizes, ym, every_x, (0, 1), every_x, (0, 1))
    fill(own, base, sizes, yp, every_x, (rows - 1,), every_x, (rows - 2, rows - 1))


def corner_kernel(sizes, first, ym, yp, out):
    planes, rows, cases = sizes
    block = 3 * cases
    even = first[0] // planes % 2 == 0
    line = 0
    for source, width in ((ym, 1), (yp, 2)):
        size = width * block
        parts = [(at, (planes - 2) * size + at, block) for at in range(0, 2 * size, block)]
        parts.append((planes * size, planes * size + (planes - 2) * 2, 4))
        for low, high, count in parts:
            value = lines(source, low, count)
            if low != high:
                value = jnp.where(even, value, lines(source, high, count))
            out[line : line + count, :] = value
            line += count
        out[line : line + 4, :] = jnp.zeros((4, LANES), f32)
        line += 4


def lines(ref, start, count):
    return ref[start : start + count, :]


def inside(ref, x, y, rows, block):
    return lines(ref, (x * rows + y) * block, block)


def beyond(refs, slot, y, rows, block):
    below, above = refs
    if y < 0:
        return lines(below, slot * block, block)
    return lines(above, (slot * 2 + y - rows) * block, block)


def beyond_codes(refs, slots, slot, y, block):
    below, above = refs
    if y < 0:
        return lines(below, slots * block + slot * 2, 2)
    return lines(above, slots * 2 * block + slot * 2, 2)


def corner(ref, slot, y, rows, block):
    start = slot * block if y < 0 else 2 * block + 8 + (slot * 2 + y - rows) * block
    return lines(ref, start, block)


def corner_codes(ref, slot, y, block):
    return lines(ref, (2 * block if y < 0 else 6 * block + 8) + slot * 2, 2)


def node_inverse(signed, count, out):
    planes = signed.shape[0]
    for x in range(1, planes):
        codes = signed[x, 0 : count + 1, :]
        total = jnp.abs(signed[x - 1, 0 : count + 1, :]) + jnp.abs(codes)
        total = total[:-1] + total[1:]
        total = total + shift_up(total)
        free = codes[1:] > 0.0
        value = 1.0 / (DIAGONAL * jnp.where(free, total, 1.0))
        out[x - 1, 0:count, :] = jnp.where(free, value, 0.0)
    for x in range(planes):
        signed[x] = jnp.abs(signed[x])


def place_column(sums, diffs, column, value):
    moved = shift_down(value)
    sums[column] = value + moved
    diffs[column] = moved - value


def early_kernel(
    sizes, first, own, pair, ym, yp, ym_pair, yp_pair, start, sums, diffs, acc_s, acc_d,
    stiff_ref, inverse,
):
    planes, rows, cases = sizes
    block = 3 * cases
    ys = rows + 3
    even = first[0] // planes % 2 == 0
    y_own, y_pair = (ym, yp), (ym_pair, yp_pair)

    def both_ways(w, read):
        low = read(True, w + 1) if w + 1 < planes else read(False, w + 1 - planes)
        high = read(False, planes + w - 1) if w < 1 else read(True, w - 1)
        return jnp.where(even, low, high)

    def codes(w, y):
        def read(mine, x):
            if y == 0:
                return lines(own if mine else pair, (planes * block + x) * rows, rows)
            return beyond_codes(y_own if mine else y_pair, planes, x, y, block)

        return both_ways(w, read)

    for w in range(-1, planes + 1):
        for y, count in ((-2, 2), (0, rows), (rows, 2)):
            stiff_ref[w + 1, y + 2 : y + 2 + count, :] = codes(w, y)
    node_inverse(stiff_ref, ys, inverse)
    for w in range(planes + 1):
        for y in range(-1, rows + 2):

            def read(mine, x):
                if 0 <= y < rows:
                    return inside(own if mine else pair, x, y, rows, block)
                return beyond(y_own if mine else y_pair, x, y, rows, block)

            value = both_ways(w, read) * inverse[w, y + 1 : y + 2, :]
            column = w * ys + y + 1
            start[column] = value
            place_column(sums, diffs, column, value)
    kept = range(1, rows + 2)
    find = whole(sums, diffs, ys)
    apply_elements(find, stiff_ref, acc_s, acc_d, planes, rows + 2, kept, 1, 1, cases)


def core_rows(rows):
    return range(2, rows - 1)


def rim_rows(rows):
    return (0, 1, rows - 1, rows)


def rim_columns(planes, rows):
    own = [(x, y) for x in range(planes) for y in rim_rows(rows) if y < rows]
    beyond_own = [(x, rows) for x in range(planes)] + [(planes, y) for y in rim_rows(rows)]
    return own + beyond_own, len(own)


def merged(x, planes, even, early, near):
    low = ([x - 1] if x >= 1 else [], [x + 1] if x <= 1 else [])
    high = ([x + 1] if x < planes else [], [x - planes + 1] if x >= planes - 1 else [])
    if low[0] and low[1] and high[0] and high[1]:
        one = early(jnp.where(even, low[0][0], high[0][0]))
        return one + near(jnp.where(even, low[1][0], high[1][0]))

    def read(places):
        found = [early(w) for w in places[0]] + [near(v) for v in places[1]]
        return found[0] if len(found) == 1 else found[0] + found[1]

    return jnp.where(even, read(low), read(high))


def direction_at(x, planes, even, early, middle):
    if x == 0:
        return jnp.where(even, middle, early(1))
    if x == planes:
        return jnp.where(even, early(planes - 1), middle)
    return early(jnp.where(even, x - 1, x + 1))


def keep_pair(ref, place, one, two, cases):
    for k in range(3):
        part = slice(k * cases, (k + 1) * cases)
        high, rest = split(jnp.concatenate([one[part], two[part]], 0))
        lane = pl.ds(pl.multiple_of((place * 3 + k) * LANES, LANES), LANES)
        ref[0 : 2 * cases, lane] = high
        ref[2 * cases : 4 * cases, lane] = rest


def products(first, second):
    contract = (((1,), (1,)), ((), ()))
    out = lax.dot_general(first, second, contract, preferred_element_type=f32)
    left, right = out.shape[0] // 2, out.shape[1] // 2
    out = out[:, :right] + out[:, right:]
    return out[:left] + out[left:]


def middle_kernel(
    sizes, first, own, pair, lower, upper, start, sums_e, diffs_e, acc_se, acc_de,
    sums, diffs, middle, acc_s, acc_d, w_sums, w_diffs, both_out, gram_out,
    stiff_ref, inverse, right,
):
    planes, rows, cases = sizes
    block = 3 * cases
    ys, nodes_y, inner = rows + 3, rows + 1, rows - 1
    core = core_rows(rows)
    even = first[0] // planes % 2 == 0

    def codes(x):
        if 0 <= x < planes:
            return lines(own, (planes * block + x) * rows, rows)
        if x < 0:
            outer = lines(lower, (block + x + 2) * rows, rows)
            return jnp.where(even, outer, lines(pair, (planes * block + planes + x) * rows, rows))
        slot = x - planes
        outer = lines(upper, (2 * block + slot) * rows, rows)
        return jnp.where(even, lines(pair, (planes * block + slot) * rows, rows), outer)

    for x in range(-2, planes + 2):
        stiff_ref[x + 2, 0:rows, :] = codes(x)
    node_inverse(stiff_ref, inner, inverse)

    def place(v, x, ref, slot):
        for y in range(1, rows):
            value = inside(ref, slot, y, rows, block) * inverse[x + 1, y - 1 : y, :]
            if v == 1:
                middle[y - 1] = value
            place_column(sums, diffs, v * inner + y - 1, value)

    def copy(v, w):
        for y in range(1, rows):
            sums[v * inner + y - 1] = sums_e[w * ys + y + 1]
            diffs[v * inner + y - 1] = diffs_e[w * ys + y + 1]

    @pl.when(even)
    def _():
        place(0, -1, lower, 0)
        place(1, 0, own, 0)
        copy(2, 0)

    @pl.when(jnp.logical_not(even))
    def _():
        copy(0, planes)
        place(1, planes, upper, 0)
        place(2, planes + 1, upper, 1)

    layer = jnp.where(even, 1, planes + 1)
    find = whole(sums, diffs, inner)
    apply_elements(find, stiff_ref, acc_s, acc_d, 2, rows - 2, range(inner), layer, 1, cases)

    def image(x, y, place):
        def total(early, near):
            return merged(
                x, planes, even, lambda w: early[w * nodes_y + y],
                lambda v: near[v * inner + y - 1],
            )

        s, d = total(acc_se, acc_s), total(acc_de, acc_d)
        force = s - d + shift_up(s + d)
        scaled = force * inverse[x + 1, pl.ds(y - 1, 1), :]
        place_column(w_sums, w_diffs, place, scaled)
        value = direction_at(x, planes, even, lambda w: start[w * ys + y + 1], middle[y - 1])
        keep_pair(both_out, place, value, scaled, cases)
        return force

    def within(x, index):
        y, place = core[0] + index, x * len(core) + index
        force = image(x, y, place)
        given = own[pl.ds(pl.multiple_of((x * rows + y) * block, 8), block), :]
        keep_pair(right, place, given, force, cases)

    for x in range(planes):
        unrolled(len(core), len(core), functools.partial(within, x))
    last = planes * len(core)
    unrolled(len(core), len(core), lambda index: image(planes, core[0] + index, last + index))
    gram_out[...] = products(right[...], both_out[:, : last * 3 * LANES])


def main_kernel(
    sizes, first, own, pair, lower, upper, ym, yp, ym_pair, yp_pair, corners,
    start, sums_e, diffs_e, acc_se, acc_de,
    sums_m, diffs_m, middle_m, acc_sm, acc_dm, w_sm, w_dm, both_m, gram_m,
    both_out, system_out, stiff_ref, inverse,
    middle, sums, diffs, acc_s0, acc_d0, acc_s1, acc_d1, w_sums, w_diffs,
    acc2_s, acc2_d, right, second_m, second_r, table,
):
    planes, rows, cases = sizes
    block = 3 * cases
    ys, nodes_y, inner = rows + 3, rows + 1, rows - 1
    core, rim = core_rows(rows), rim_rows(rows)
    columns, own_count = rim_columns(planes, rows)
    even = first[0] // planes % 2 == 0
    y_own, y_pair = (ym, yp), (ym_pair, yp_pair)

    def codes(x, y):
        def read(mine, plane):
            if y == 0:
                return lines(own if mine else pair, (planes * block + plane) * rows, rows)
            return beyond_codes(y_own if mine else y_pair, planes, plane, y, block)

        if 0 <= x < planes:
            return read(True, x)
        ref, count, slot = (lower, 1, x + 2) if x < 0 else (upper, 2, x - planes)
        if y == 0:
            outer = lines(ref, (count * block + slot) * rows, rows)
        else:
            outer = corner_codes(corners, slot, y, block)
        within = read(False, planes + x if x < 0 else x - planes)
        return jnp.where(even, outer, within) if x < 0 else jnp.where(even, within, outer)

    for x in range(-2, planes + 2):
        for y, count in ((-2, 2), (0, rows), (rows, 2)):
            stiff_ref[x + 2, y + 2 : y + 2 + count, :] = codes(x, y)
    node_inverse(stiff_ref, ys, inverse)

    sides = (-1, 0, rows, rows + 1)

    def place(v, x, ref, slot, beyond_at):
        for i, y in enumerate(sides):
            value = inside(ref, slot, y, rows, block) if y == 0 else beyond_at(y)
            value = value * inverse[x + 1, y + 1 : y + 2, :]
            if v == 1 and y in (0, rows):
                middle[y // rows] = value
            place_column(sums, diffs, v * 4 + i, value)

    def copy(v, w):
        for i, y in enumerate(sides):
            sums[v * 4 + i] = sums_e[w * ys + y + 1]
            diffs[v * 4 + i] = diffs_e[w * ys + y + 1]

    @pl.when(even)
    def _():
        place(0, -1, lower, 0, lambda y: corner(corners, 1, y, rows, block))
        place(1, 0, own, 0, lambda y: beyond(y_own, 0, y, rows, block))
        copy(2, 0)

    @pl.when(jnp.logical_not(even))
    def _():
        copy(0, planes)
        place(1, planes, upper, 0, lambda y: corner(corners, 0, y, rows, block))
        place(2, planes + 1, upper, 1, lambda y: corner(corners, 1, y, rows, block))

    def find_low(row):
        return (sums, diffs, 4, row) if row < 2 else (sums_m, diffs_m, inner, 0)

    def find_high(row):
        return (sums, diffs, 4, row + 1) if row else (sums_m, diffs_m, inner, inner - 1)

    layer = jnp.where(even, 1, planes + 1)
    apply_elements(find_low, stiff_ref, acc_s0, acc_d0, 2, 2, range(1, 3), layer, 1, cases)
    apply_elements(find_high, stiff_ref, acc_s1, acc_d1, 2, 2, range(2), layer, rows + 1, cases)

    def image(x, y, place):
        def total(early, near, low, high):
            def outer(v):
                value = low[v * 2 + y] if y < 2 else high[v * 2 + y - inner]
                return value + near[v * inner + y - 1] if y in (1, inner) else value

            return merged(x, planes, even, lambda w: early[w * nodes_y + y], outer)

        s = total(acc_se, acc_sm, acc_s0, acc_s1)
        d = total(acc_de, acc_dm, acc_d0, acc_d1)
        force = s - d + shift_up(s + d)
        scaled = force * inverse[x + 1, y + 1 : y + 2, :]
        place_column(w_sums, w_diffs, x * len(rim) + rim.index(y), scaled)
        inner_middle = middle_m[y - 1] if y in (1, inner) else middle[y // rows]
        value = direction_at(x, planes, even, lambda w: start[w * ys + y + 1], inner_middle)
        keep_pair(both_out, place, value, scaled, cases)
        return force

    for index, (x, y) in enumerate(columns):
        force = image(x, y, index)
        if index < own_count:
            keep_pair(right, index, inside(own, x, y, rows, block), force, cases)

    def find(row):
        if row in rim:
            return w_sums, w_diffs, len(rim), rim.index(row)
        return w_sm, w_dm, len(core), row - core[0]

    apply_elements(find, stiff_ref, acc2_s, acc2_d, planes, rows, range(nodes_y), 2, 2, cases)

    def second_force(ref, x, y, place):
        column = x * nodes_y + y
        s, d = acc2_s[column], acc2_d[column]
        force = s - d + shift_up(s + d)
        for k in range(3):
            value = force[k * cases : (k + 1) * cases]
            high = value.astype(bf16).astype(f32)
            lane = pl.ds(pl.multiple_of((place * 3 + k) * LANES, LANES), LANES)
            ref[:, lane] = jnp.concatenate([high, value - high], 0).astype(bf16)

    unrolled(
        (planes + 1) * len(core), len(core),
        lambda index: second_force(
            second_m, index // len(core), core[0] + index % len(core), index
        ),
    )
    for index, (x, y) in enumerate(columns):
        second_force(second_r, x, y, index)

    two = 2 * cases
    gram = products(right[...], both_out[:, : own_count * 3 * LANES]) + gram_m[...]
    other = products(second_m[...], both_m[...]) + products(second_r[...], both_out[...])
    row = lax.broadcasted_iota(jnp.int32, (cases, cases), 0)
    column = lax.broadcasted_iota(jnp.int32, (cases, cases), 1)
    load_load, load_image = gram[:cases, :cases], gram[cases:, :cases]
    mixed, image_image = other[:, :cases], other[:, cases:]
    table[...] = jnp.zeros(table.shape, f32)
    table[:, 0:cases] = jnp.where(row <= column, load_load, load_image)
    table[:, cases:two] = jnp.where(row <= column, mixed, image_image)
    for lane, value in ((two, load_image), (two + 1, image_image)):
        own_entries = jnp.where(row == column, value, 0.0)
        table[:, lane : lane + 1] = jnp.sum(own_entries, axis=1, keepdims=True)
    half = cases // 2
    folded = table[:half, :] + pltpu.roll(table[half:, :], LANES // 2, 1)
    depth = system_out.shape[2]
    for index in range(system_out.shape[0]):
        for part in range(half // depth):
            system_out[index, part] = folded[part * depth : (part + 1) * depth]


def solve_kernel(
    sizes, system, system_pair, both_m, both_r, codes, out, mixing, sums, diffs, energy, square, full
):
    planes, rows, cases = sizes
    two = 2 * cases
    nodes_y = rows + 1
    count = planes * rows
    total = jnp.sum(system[...], axis=0) + jnp.sum(system_pair[...], axis=0)
    half, depth = cases // 2, system.shape[2]
    square[...] = jnp.zeros(square.shape, f32)
    for part in range(half // depth):
        value = total[part]
        square[part * depth : (part + 1) * depth, :] = value
        lines = slice(half + part * depth, half + (part + 1) * depth)
        square[lines, :] = pltpu.roll(value, LANES // 2, 1)
    value, turned = square[0:cases, :], jnp.transpose(square[...])
    line = lax.broadcasted_iota(jnp.int32, (cases, cases), 0)
    place = lax.broadcasted_iota(jnp.int32, (cases, cases), 1)

    def mended(start, diagonal=None):
        kept, other = value[:, start : start + cases], turned[start : start + cases, :cases]
        if diagonal is None:
            return jnp.where(line <= place, kept, other)
        inner = jnp.where(line < place, other, value[:, diagonal : diagonal + 1])
        return jnp.where(line > place, kept, inner)

    load_image, mixed = mended(0, two), mended(cases)
    parts = ((load_image, mixed), (mixed, mended(cases, two + 1)), (mended(0), load_image))
    full[...] = jnp.zeros(full.shape, f32)
    for index, (left, right) in enumerate(parts):
        full[index * cases : (index + 1) * cases, 0:cases] = left
        full[index * cases : (index + 1) * cases, cases:two] = right
    table = full[...]
    lane = lax.broadcasted_iota(jnp.int32, (1, LANES), 1)
    gone, wide = 0, 4
    for pivot in range(0, two, wide):
        drop = pivot // 8 * 8 - gone
        table = table[drop:]
        gone += drop
        line = pivot - gone
        inner = (lane >= pivot) & (lane < pivot + wide)
        found = [table[line + p : line + p + 1, :] for p in range(wide)]
        block = [
            [jnp.broadcast_to(row[:, pivot + q : pivot + q + 1], row.shape) for q in range(wide)]
            for row in found
        ]
        solved = [
            jnp.where(lane == pivot + p, -1.0, jnp.where(inner, 0.0, found[p]))
            for p in range(wide)
        ]
        for p in range(wide):
            inverse = 1.0 / block[p][p]
            solved[p] = solved[p] * inverse
            block[p] = [value * inverse for value in block[p]]
            for q in range(wide):
                if q != p:
                    factor = block[q][p]
                    solved[q] = solved[q] - factor * solved[p]
                    for r in range(p + 1, wide):
                        block[q][r] = block[q][r] - factor * block[p][r]
        update = None
        for q in range(wide):
            term = table[:, pivot + q : pivot + q + 1] * solved[q]
            update = term if update is None else update + term
        table = jnp.where(inner, 0.0, table) - update
    answer = table[two - gone :, :two]
    high = answer.astype(bf16).astype(f32)
    mixing[...] = jnp.zeros(mixing.shape, f32)
    mixing[0:cases, 0:two] = high
    mixing[0:cases, two : 2 * two] = high
    mixing[cases:two, 0:two] = answer - high
    mix = mixing[...][:, : 2 * two].astype(bf16)

    def combined(ref, place, width):
        value = jnp.dot(
            mix, ref[:, place * 3 * LANES : (place + width) * 3 * LANES], preferred_element_type=f32
        )
        return value[:cases] + value[cases:]

    def keep(value, index, column):
        for k in range(3):
            part = value[:, (index * 3 + k) * LANES : (index * 3 + k + 1) * LANES]
            moved = shift_down(part)
            sums[column, k * cases : (k + 1) * cases, :] = part + moved
            diffs[column, k * cases : (k + 1) * cases, :] = moved - part

    core = core_rows(rows)
    for x in range(planes + 1):
        value = combined(both_m, x * len(core), len(core))
        for index, y in enumerate(core):
            keep(value, index, x * nodes_y + y)
    columns, _ = rim_columns(planes, rows)
    for start in range(0, len(columns), 6):
        some = columns[start : start + 6]
        value = combined(both_r, start, len(some))
        for index, (x, y) in enumerate(some):
            keep(value, index, x * nodes_y + y)

    find = whole(sums, diffs, nodes_y)
    tiles = cases // 8

    def step(plane, _):
        for tile in range(tiles):
            lower = x_modes(find, plane, 0, tile, cases)
            for row in range(rows):
                upper = x_modes(find, plane, row + 1, tile, cases)
                part = mode_energy(modes_of(lower, upper))
                if tile == 0:
                    energy[row] = part
                else:
                    energy[row] += part
                lower = upper
        total = jnp.sum(energy[...], axis=1)
        total = (-3.0 / cases) * jnp.abs(codes[plane]) * total
        for index in range(out.shape[0]):
            out[index, plane] = total
        return 0

    lax.fori_loop(0, planes, step, 0)


def smooth(ref, x, rows):
    weight = [2.5 - math.sqrt(q) for q in range(7)]
    near = {}
    for dx in range(-2, 3):
        for dy in range(-2, 3):
            q = dx * dx + dy * dy
            if q <= 5:
                value = ref[x + 2 + dx, 2 + dy : 2 + dy + rows, :]
                near[q] = value if q not in near else near[q] + value
    result = None
    for dz in range(3):
        part = None
        for q, value in near.items():
            if q + dz * dz <= 6:
                term = weight[q + dz * dz] * value
                part = term if part is None else part + term
        if dz == 0:
            result = part
        else:
            place = lax.broadcasted_iota(jnp.int32, part.shape, 1)
            forward = jnp.where(place >= LANES - dz, 0.0, pltpu.roll(part, LANES - dz, 1))
            backward = jnp.where(place < dz, 0.0, pltpu.roll(part, dz, 1))
            result = result + (forward + backward)
    return result


def scale_kernel(sizes, counts, start, levels, out, there):
    planes, rows, _ = sizes
    y = lax.broadcasted_iota(jnp.int32, (rows + 4, LANES), 0) + (start[1] - 2)
    in_y = (y >= 0) & (y < counts[1] * rows)
    for x in range(planes + 4):
        global_x = start[0] + (x - 2)
        in_x = (global_x >= 0) & (global_x < counts[0] * planes)
        there[x] = jnp.where(in_y & in_x, 1.0, 0.0)
    for x in range(planes):
        density = 0.3 + 0.7 * levels[x].astype(f32) / (LEVELS - 1)
        out[x] = 1.0 / (density * smooth(there, x, rows))


def filter_kernel(sizes, counts, start, blocks, blocks_pair, scale, out, wide):
    planes, rows, _ = sizes
    sides_x = ((-1, planes - 2, planes, 0), (0, 0, planes, 2), (1, 0, 2, 2 + planes))
    sides_y = ((-1, rows - 2, rows, 0), (0, 0, rows, 2), (1, 0, 2, 2 + rows))
    for step_x, x0, x1, to_x in sides_x:
        for step_y, y0, y1, to_y in sides_y:
            at_x = start[0] // planes + step_x
            at_y = start[1] // rows + step_y
            inside = (at_x >= 0) & (at_x < counts[0]) & (at_y >= 0) & (at_y < counts[1])
            index = jnp.where(inside, at_x // 2 * counts[1] + at_y, 0)
            value = (blocks_pair if step_x else blocks)[index, x0:x1, y0:y1, :]
            wide[to_x : to_x + x1 - x0, to_y : to_y + y1 - y0, :] = jnp.where(inside, value, 0.0)
    for x in range(planes):
        out[x] = smooth(wide, x, rows) * scale[x]


def local(forces, levels, supports):
    _, cases, planes, rows, _ = forces.shape
    sizes = (planes, rows, cases)
    block = 3 * cases
    count_x, count_y = lax.axis_size("gx"), lax.axis_size("gy")

    def shape(blocks, codes):
        return jax.ShapeDtypeStruct((blocks * block + up8(codes), LANES), f32)

    density = 0.3 + 0.7 * levels.astype(f32) / (LEVELS - 1)
    codes = density * density * density
    codes = jnp.where(supports == 0, codes, -codes)
    start = jnp.stack([lax.axis_index("gx") * planes, lax.axis_index("gy") * rows])
    start = start.astype(jnp.int32)
    counts = (count_x, count_y)
    scalars = pl.BlockSpec(memory_space=pltpu.SMEM)
    whole = shape(planes * rows, planes * rows)
    down = [] if planes == 2 else [shape(2 * rows, 2 * rows)]
    own, *down = pl.pallas_call(
        functools.partial(pack_kernel, sizes),
        out_shape=[whole, *down],
        in_specs=[VMEM] * 2,
        out_specs=[VMEM] * (1 + len(down)),
        compiler_params=PARAMS,
        name="pack",
    )(forces, codes)
    scale = pl.pallas_call(
        functools.partial(scale_kernel, sizes, counts),
        out_shape=jax.ShapeDtypeStruct((planes, rows, LANES), f32),
        in_specs=[scalars, VMEM],
        out_specs=VMEM,
        scratch_shapes=[pltpu.VMEM((planes + 4, rows + 4, LANES), f32)],
        compiler_params=PARAMS,
        name="scale",
    )(start, levels)

    def moved(value, axis, step):
        count = lax.axis_size(axis)
        pairs = [(i, i + step) for i in range(count) if 0 <= i + step < count]
        return lax.ppermute(value, axis, pairs)

    def links(first, step):
        return [(i, i + step) for i in range(first, count_x, 2) if 0 <= i + step < count_x]

    def swapped(value):
        return lax.ppermute(value, "gx", links(0, 1) + links(1, -1))

    def across(value):
        return lax.ppermute(value, "gx", links(1, 1) + links(2, -1))

    upper = lax.ppermute(down[0] if down else own, "gx", links(2, -1))
    pair = swapped(own)
    own, pair = lax.optimization_barrier((own, pair))
    ym, yp = pl.pallas_call(
        functools.partial(rows_kernel, sizes),
        out_shape=[shape(2 * planes, 2 * planes), shape(planes, 2 * planes)],
        in_specs=[VMEM],
        out_specs=[VMEM] * 2,
        compiler_params=PARAMS,
        name="rows",
    )(own)
    from_yp, from_ym = moved(ym, "gy", -1), moved(yp, "gy", 1)
    up = pl.pallas_call(
        functools.partial(up_kernel, sizes),
        out_shape=shape(rows, 2 * rows),
        in_specs=[VMEM] * 2,
        out_specs=VMEM,
        compiler_params=PARAMS,
        name="up",
    )(swapped(codes), own)
    lower = lax.ppermute(up, "gx", links(1, 1))
    pair_yp, pair_ym = swapped(from_yp), swapped(from_ym)
    corners = across(
        pl.pallas_call(
            functools.partial(corner_kernel, sizes),
            out_shape=jax.ShapeDtypeStruct((6 * block + 16, LANES), f32),
            in_specs=[scalars] + [VMEM] * 2,
            out_specs=VMEM,
            compiler_params=PARAMS,
            name="corners",
        )(start, from_ym, from_yp)
    )

    devices = count_x * count_y
    nodes = (planes + 1) * (rows + 1)
    window = jax.ShapeDtypeStruct(((planes + 1) * (rows + 3), block, LANES), f32)
    partial_forces = jax.ShapeDtypeStruct((nodes, block, LANES), f32)
    early = pl.pallas_call(
        functools.partial(early_kernel, sizes),
        out_shape=[window] * 3 + [partial_forces] * 2,
        in_specs=[scalars] + [VMEM] * 6,
        out_specs=[VMEM] * 5,
        scratch_shapes=[
            pltpu.VMEM((planes + 2, up8(rows + 4), LANES), f32),
            pltpu.VMEM((planes + 1, up8(rows + 3), LANES), f32),
        ],
        compiler_params=PARAMS,
        cost_estimate=pl.CostEstimate(
            flops=200 * planes * rows * block * LANES, bytes_accessed=2**23, transcendentals=0
        ),
        name="early",
    )(start, own, pair, from_ym, from_yp, pair_ym, pair_yp)

    def columns(count):
        return jax.ShapeDtypeStruct((count, block, LANES), f32)

    def fields(lines, count):
        return jax.ShapeDtypeStruct((lines * cases, count * 3 * LANES), bf16)

    def scratch(value):
        return pltpu.VMEM(value.shape, value.dtype)

    core = len(core_rows(rows))
    middle = pl.pallas_call(
        functools.partial(middle_kernel, sizes),
        out_shape=[columns(3 * (rows - 1))] * 2
        + [columns(rows - 1)]
        + [columns(3 * (rows - 1))] * 2
        + [columns((planes + 1) * core)] * 2
        + [fields(4, (planes + 1) * core), jax.ShapeDtypeStruct((2 * cases, 2 * cases), f32)],
        in_specs=[scalars] + [VMEM] * 9,
        out_specs=[VMEM] * 9,
        scratch_shapes=[
            pltpu.VMEM((planes + 4, up8(rows), LANES), f32),
            pltpu.VMEM((planes + 3, up8(rows), LANES), f32),
            scratch(fields(4, planes * core)),
        ],
        compiler_params=PARAMS,
        name="middle",
    )(start, own, pair, lower, upper, *early)

    rim, rim_own = rim_columns(planes, rows)
    field = scratch(columns(nodes))
    both, system = pl.pallas_call(
        functools.partial(main_kernel, sizes),
        out_shape=[
            fields(4, len(rim)),
            jax.ShapeDtypeStruct((devices // 2, cases // 8, 4, LANES), f32),
        ],
        in_specs=[scalars] + [VMEM] * 23,
        out_specs=[VMEM] * 2,
        scratch_shapes=[
            pltpu.VMEM((planes + 4, up8(rows + 4), LANES), f32),
            pltpu.VMEM((planes + 3, up8(rows + 3), LANES), f32),
            scratch(columns(2)),
            *[scratch(columns(12))] * 2,
            *[scratch(columns(6))] * 4,
            *[scratch(columns((planes + 1) * 4))] * 2,
            field, field,
            scratch(fields(4, rim_own)),
            scratch(fields(2, (planes + 1) * core)),
            scratch(fields(2, len(rim))),
            pltpu.VMEM((cases, LANES), f32),
        ],
        compiler_params=PARAMS,
        name="operator",
    )(
        start, own, pair, lower, upper, from_ym, from_yp, pair_ym, pair_yp, corners,
        *early, *middle,
    )

    groups = [
        [x * count_y + y for x in range(side, count_x, 2) for y in range(count_y)]
        for side in range(2)
    ]

    def gathered(copies):
        mine = lax.all_to_all(copies, ("gx", "gy"), 0, 0, axis_index_groups=groups)
        return mine, swapped(mine)

    system = gathered(system)

    weighted = pl.pallas_call(
        functools.partial(solve_kernel, sizes),
        out_shape=jax.ShapeDtypeStruct((devices // 2, planes, rows, LANES), f32),
        in_specs=[VMEM] * 5,
        out_specs=VMEM,
        scratch_shapes=[
            pltpu.VMEM((2 * cases, LANES), f32),
            field,
            field,
            pltpu.VMEM((rows, 8, LANES), f32),
            pltpu.VMEM((LANES, LANES), f32),
            pltpu.VMEM((3 * cases, LANES), f32),
        ],
        compiler_params=PARAMS,
        name="solve",
    )(*system, middle[7], both, codes)

    blocks = gathered(weighted)
    return pl.pallas_call(
        functools.partial(filter_kernel, sizes, counts),
        out_shape=jax.ShapeDtypeStruct((planes, rows, LANES), f32),
        in_specs=[scalars] + [VMEM] * 3,
        out_specs=VMEM,
        scratch_shapes=[pltpu.VMEM((planes + 4, rows + 4, LANES), f32)],
        compiler_params=PARAMS,
        name="cone",
    )(start, *blocks, scale)


def solution(mesh):
    return jax.shard_map(
        local,
        mesh=mesh,
        in_specs=(P(None, None, "gx", "gy", None), P("gx", "gy", None), P("gx", "gy", None)),
        out_specs=P("gx", "gy", None),
        check_vma=False,
    )
```

```python
import functools
import math

import jax
import jax.numpy as jnp
from jax import lax
from jax.experimental import pallas as pl
from jax.experimental.pallas import tpu as pltpu
from jax.sharding import PartitionSpec as P

LEVELS = 16
LOAD = 0.2
LANES = 128
POISSON = 0.3
LAME = POISSON / ((1.0 + POISSON) * (1.0 - 2.0 * POISSON))
SHEAR = 1.0 / (2.0 * (1.0 + POISSON))
DIAGONAL = (LAME + 2.0 * SHEAR) / 9.0 + 2.0 * SHEAR / 9.0
VMEM = pl.BlockSpec(memory_space=pltpu.VMEM)
PARAMS = pltpu.CompilerParams(vmem_limit_bytes=30 * 2**20)
f32 = jnp.float32
bf16 = jnp.bfloat16


def up8(count):
    return -(-count // 8) * 8


def shift_down(value):
    lane = lax.broadcasted_iota(jnp.int32, value.shape, value.ndim - 1)
    rolled = pltpu.roll(value, LANES - 1, value.ndim - 1)
    return jnp.where(lane == LANES - 1, 0.0, rolled)


def shift_up(value):
    lane = lax.broadcasted_iota(jnp.int32, value.shape, value.ndim - 1)
    return jnp.where(lane == 0, 0.0, pltpu.roll(value, 1, value.ndim - 1))


def unrolled(count, factor, body):
    def turn(step, _):
        for offset in range(factor):
            body(step * factor + offset)
        return 0

    turns = count // factor
    if turns:
        lax.fori_loop(0, turns, turn, 0)
    for index in range(turns * factor, count):
        body(index)


def split(value):
    high = value.astype(bf16)
    return high, (value - high.astype(f32)).astype(bf16)


def modes_of(lower, upper):
    out = [[[[None] * 3 for _ in range(2)] for _ in range(2)] for _ in range(2)]
    for a in range(2):
        for c in range(2):
            for k in range(3):
                if a or c:
                    out[a][0][c][k] = lower[a][c][k] + upper[a][c][k]
                out[a][1][c][k] = upper[a][c][k] - lower[a][c][k]
    return out


PAIRS = (((1, 1, 0, 0), (0, 1, 1, 2)), ((1, 0, 1, 0), (0, 1, 1, 1)), ((1, 1, 0, 1), (1, 0, 1, 2)))
TRIPLE = ((0, 1, 1, 0), (1, 0, 1, 1), (1, 1, 0, 2))
SHEARS = (((0, 1, 0, 0), (1, 0, 0, 1)), ((0, 0, 1, 0), (1, 0, 0, 2)), ((0, 0, 1, 1), (0, 1, 0, 2)))
AXIAL = ((1, 0, 0, 0), (0, 1, 0, 1), (0, 0, 1, 2))


def at(modes, place):
    a, b, c, k = place
    return modes[a][b][c][k]


def mode_forces(modes, stiff):
    out = [[[[None] * 3 for _ in range(2)] for _ in range(2)] for _ in range(2)]

    def put(place, value):
        a, b, c, k = place
        out[a][b][c][k] = value

    shear = stiff * (SHEAR / 16)
    for first, second in SHEARS:
        force = shear * (at(modes, first) + at(modes, second))
        put(first, force)
        put(second, force)
    one, two, three = (at(modes, place) for place in AXIAL)
    volume = (stiff * (LAME / 16)) * (one + two + three)
    axial = stiff * (SHEAR / 8)
    for place in AXIAL:
        put(place, volume + axial * at(modes, place))
    own, cross = stiff * ((LAME + 3 * SHEAR) / 48), stiff * (LAME / 48)
    for first, second in PAIRS:
        one, two = at(modes, first), at(modes, second)
        put(first, own * one + cross * two)
        put(second, own * two + cross * one)
    twist = stiff * (SHEAR / 48)
    one, two, three = (at(modes, place) for place in TRIPLE)
    total = one + two + three
    for place in TRIPLE:
        put(place, twist * (total + at(modes, place)))
    last = stiff * ((LAME + 4 * SHEAR) / 144)
    for k in range(3):
        put((1, 1, 1, k), last * modes[1][1][1][k])
    return out


def mode_energy(modes):
    def square(value):
        return value * value

    shear = None
    for first, second in SHEARS:
        term = square(at(modes, first) + at(modes, second))
        shear = term if shear is None else shear + term
    one, two, three = (at(modes, place) for place in AXIAL)
    energy = (SHEAR / 16) * shear + (LAME / 16) * square(one + two + three)
    energy = energy + (SHEAR / 8) * (square(one) + square(two) + square(three))
    squares, products = None, None
    for first, second in PAIRS:
        one, two = at(modes, first), at(modes, second)
        term, product = square(one) + square(two), one * two
        squares = term if squares is None else squares + term
        products = product if products is None else products + product
    energy = energy + ((LAME + 3 * SHEAR) / 48) * squares + (LAME / 24) * products
    one, two, three = (at(modes, place) for place in TRIPLE)
    twist = square(one + two + three) + square(one) + square(two) + square(three)
    energy = energy + (SHEAR / 48) * twist
    last = square(modes[1][1][1][0]) + square(modes[1][1][1][1]) + square(modes[1][1][1][2])
    return energy + ((LAME + 4 * SHEAR) / 144) * last


def x_modes(find, plane, row, tile, cases):
    sums, diffs, columns, column = find(row)
    out = [[[None] * 3 for _ in range(2)] for _ in range(2)]
    for c, ref in enumerate((sums, diffs)):
        for k in range(3):
            rows = pl.ds(pl.multiple_of(k * cases + tile * 8, 8), 8)
            one = ref[plane * columns + column, rows, :]
            two = ref[(plane + 1) * columns + column, rows, :]
            out[0][c][k] = one + two
            out[1][c][k] = two - one
    return out


def whole(sums, diffs, columns):
    return lambda row: (sums, diffs, columns, row)


def apply_elements(find, stiff_ref, acc_s, acc_d, planes, rows, kept, stiff_x, stiff_y, cases):
    columns = len(kept)
    tiles = cases // 8
    for column in range(columns):
        acc_s[column] = jnp.zeros(acc_s.shape[1:], f32)
        acc_d[column] = jnp.zeros(acc_d.shape[1:], f32)

    def step(index, _):
        plane, tile = index // tiles, index % tiles

        def emit(row, total):
            if row not in kept:
                return
            for c, acc in enumerate((acc_s, acc_d)):
                for k in range(3):
                    lines = pl.ds(pl.multiple_of(k * cases + tile * 8, 8), 8)
                    low = plane * columns + row - kept[0]
                    acc[low, lines, :] += total[0][c][k] - total[1][c][k]
                    acc[low + columns, lines, :] = total[0][c][k] + total[1][c][k]

        lower = x_modes(find, plane, 0, tile, cases)
        carry = None
        for row in range(rows):
            upper = x_modes(find, plane, row + 1, tile, cases)
            stiff = jnp.broadcast_to(
                stiff_ref[plane + stiff_x, pl.ds(row + stiff_y, 1), :], (8, LANES)
            )
            forces = mode_forces(modes_of(lower, upper), stiff)
            here = [[[None] * 3 for _ in range(2)] for _ in range(2)]
            following = [[[None] * 3 for _ in range(2)] for _ in range(2)]
            for a in range(2):
                for c in range(2):
                    for k in range(3):
                        one, two = forces[a][0][c][k], forces[a][1][c][k]
                        low = -two if one is None else one - two
                        high = two if one is None else one + two
                        here[a][c][k] = low if carry is None else carry[a][c][k] + low
                        following[a][c][k] = high
            emit(row, here)
            carry, lower = following, upper
        emit(rows, carry)
        return 0

    lax.fori_loop(0, planes * tiles, step, 0)


def fill(source, base, sizes, ref, xs, ys, code_xs, code_ys):
    planes, rows, cases = sizes
    block = 3 * cases
    line = 0
    for x in xs:
        start = (x * rows + ys[0]) * block
        count = len(ys) * block
        ref[line : line + count, :] = source[start : start + count, :]
        line += count
    for x in code_xs:
        start = base + x * rows + code_ys[0]
        ref[line : line + len(code_ys), :] = source[start : start + len(code_ys), :]
        line += len(code_ys)
    if line < ref.shape[0]:
        ref[line:, :] = jnp.zeros((ref.shape[0] - line, LANES), f32)


def pack_kernel(sizes, first, forces, codes, own, edge):
    planes, rows, cases = sizes
    block = 3 * cases
    base = planes * rows * block
    for x in range(planes):
        own[base + x * rows : base + (x + 1) * rows, :] = codes[x]
        scale = jnp.where(codes[x] > 0.0, LOAD, 0.0)
        for k in range(3):
            for c in range(cases):
                start = x * rows * block + k * cases + c
                own[pl.ds(start, rows, stride=block), :] = forces[k, c, x] * scale

    even = first[0] // planes % 2 == 0
    size = rows * block
    for line in range(0, size, block):
        high = lines(own, (planes - 1) * size + line, block)
        edge[line : line + block, :] = jnp.where(even, lines(own, line, block), high)
    high = lines(own, base + (planes - 2) * rows, 2 * rows)
    edge[size:, :] = jnp.where(even, lines(own, base, 2 * rows), high)


def second_kernel(sizes, begun, own, second):
    _, rows, cases = sizes
    size = rows * 3 * cases
    second[...] = lines(own, size, size)


def rows_kernel(sizes, own, ym, yp):
    planes, rows, cases = sizes
    base = planes * rows * 3 * cases
    every_x = range(planes)
    fill(own, base, sizes, ym, every_x, (0, 1), every_x, (0, 1))
    fill(own, base, sizes, yp, every_x, (rows - 1,), every_x, (rows - 2, rows - 1))


def corner_kernel(sizes, first, ym, yp, out):
    planes, rows, cases = sizes
    block = 3 * cases
    even = first[0] // planes % 2 == 0
    line = 0
    for source, width in ((ym, 1), (yp, 2)):
        size = width * block
        parts = [(at, (planes - 2) * size + at, block) for at in range(0, 2 * size, block)]
        parts.append((planes * size, planes * size + (planes - 2) * 2, 4))
        for low, high, count in parts:
            value = lines(source, low, count)
            if low != high:
                value = jnp.where(even, value, lines(source, high, count))
            out[line : line + count, :] = value
            line += count
        out[line : line + 4, :] = jnp.zeros((4, LANES), f32)
        line += 4


def lines(ref, start, count):
    return ref[start : start + count, :]


def inside(ref, x, y, rows, block):
    return lines(ref, (x * rows + y) * block, block)


def beyond(refs, slot, y, rows, block):
    below, above = refs
    if y < 0:
        return lines(below, slot * block, block)
    return lines(above, (slot * 2 + y - rows) * block, block)


def beyond_codes(refs, slots, slot, y, block):
    below, above = refs
    if y < 0:
        return lines(below, slots * block + slot * 2, 2)
    return lines(above, slots * 2 * block + slot * 2, 2)


def corner(ref, slot, y, rows, block):
    start = slot * block if y < 0 else 2 * block + 8 + (slot * 2 + y - rows) * block
    return lines(ref, start, block)


def corner_codes(ref, slot, y, block):
    return lines(ref, (2 * block if y < 0 else 6 * block + 8) + slot * 2, 2)


def node_inverse(signed, count, out):
    planes = signed.shape[0]
    for x in range(1, planes):
        codes = signed[x, 0 : count + 1, :]
        total = jnp.abs(signed[x - 1, 0 : count + 1, :]) + jnp.abs(codes)
        total = total[:-1] + total[1:]
        total = total + shift_up(total)
        free = codes[1:] > 0.0
        value = 1.0 / (DIAGONAL * jnp.where(free, total, 1.0))
        out[x - 1, 0:count, :] = jnp.where(free, value, 0.0)
    for x in range(planes):
        signed[x] = jnp.abs(signed[x])


def place_column(sums, diffs, column, value):
    moved = shift_down(value)
    sums[column] = value + moved
    diffs[column] = moved - value


def early_kernel(
    sizes, first, own, pair, ym, yp, ym_pair, yp_pair, start, sums, diffs, acc_s, acc_d,
    stiff_ref, inverse,
):
    planes, rows, cases = sizes
    block = 3 * cases
    ys = rows + 3
    even = first[0] // planes % 2 == 0
    y_own, y_pair = (ym, yp), (ym_pair, yp_pair)

    def both_ways(w, read):
        low = read(True, w + 1) if w + 1 < planes else read(False, w + 1 - planes)
        high = read(False, planes + w - 1) if w < 1 else read(True, w - 1)
        return jnp.where(even, low, high)

    def codes(w, y):
        def read(mine, x):
            if y == 0:
                return lines(own if mine else pair, (planes * block + x) * rows, rows)
            return beyond_codes(y_own if mine else y_pair, planes, x, y, block)

        return both_ways(w, read)

    for w in range(-1, planes + 1):
        for y, count in ((-2, 2), (0, rows), (rows, 2)):
            stiff_ref[w + 1, y + 2 : y + 2 + count, :] = codes(w, y)
    node_inverse(stiff_ref, ys, inverse)
    for w in range(planes + 1):
        for y in range(-1, rows + 2):

            def read(mine, x):
                if 0 <= y < rows:
                    return inside(own if mine else pair, x, y, rows, block)
                return beyond(y_own if mine else y_pair, x, y, rows, block)

            value = both_ways(w, read) * inverse[w, y + 1 : y + 2, :]
            column = w * ys + y + 1
            start[column] = value
            place_column(sums, diffs, column, value)
    kept = range(1, rows + 2)
    find = whole(sums, diffs, ys)
    apply_elements(find, stiff_ref, acc_s, acc_d, planes, rows + 2, kept, 1, 1, cases)


def core_rows(rows):
    return range(2, rows - 1)


def rim_rows(rows):
    return (0, 1, rows - 1, rows)


def rim_columns(planes, rows):
    own = [(x, y) for x in range(planes) for y in rim_rows(rows) if y < rows]
    beyond_own = [(x, rows) for x in range(planes)] + [(planes, y) for y in rim_rows(rows)]
    return own + beyond_own, len(own)


def merged(x, planes, even, early, near):
    low = ([x - 1] if x >= 1 else [], [x + 1] if x <= 1 else [])
    high = ([x + 1] if x < planes else [], [x - planes + 1] if x >= planes - 1 else [])
    if low[0] and low[1] and high[0] and high[1]:
        one = early(jnp.where(even, low[0][0], high[0][0]))
        return one + near(jnp.where(even, low[1][0], high[1][0]))

    def read(places):
        found = [early(w) for w in places[0]] + [near(v) for v in places[1]]
        return found[0] if len(found) == 1 else found[0] + found[1]

    return jnp.where(even, read(low), read(high))


def direction_at(x, planes, even, early, middle):
    if x == 0:
        return jnp.where(even, middle, early(1))
    if x == planes:
        return jnp.where(even, early(planes - 1), middle)
    return early(jnp.where(even, x - 1, x + 1))


def keep_pair(ref, place, one, two, cases):
    for k in range(3):
        part = slice(k * cases, (k + 1) * cases)
        high, rest = split(jnp.concatenate([one[part], two[part]], 0))
        lane = pl.ds(pl.multiple_of((place * 3 + k) * LANES, LANES), LANES)
        ref[0 : 2 * cases, lane] = high
        ref[2 * cases : 4 * cases, lane] = rest


def products(first, second):
    contract = (((1,), (1,)), ((), ()))
    out = lax.dot_general(first, second, contract, preferred_element_type=f32)
    left, right = out.shape[0] // 2, out.shape[1] // 2
    out = out[:, :right] + out[:, right:]
    return out[:left] + out[left:]


def middle_kernel(
    sizes, first, own, pair, edge, second, start, sums_e, diffs_e, acc_se, acc_de,
    sums, diffs, middle, acc_s, acc_d, w_sums, w_diffs, both_out, gram_out,
    stiff_ref, inverse, right,
):
    planes, rows, cases = sizes
    block = 3 * cases
    ys, nodes_y, inner = rows + 3, rows + 1, rows - 1
    core = core_rows(rows)
    even = first[0] // planes % 2 == 0

    def codes(x):
        if 0 <= x < planes:
            return lines(own, (planes * block + x) * rows, rows)
        slot = x + 2 if x < 0 else x - planes
        outer = lines(edge, (block + slot) * rows, rows)
        if x < 0:
            return jnp.where(even, outer, lines(pair, (planes * block + planes + x) * rows, rows))
        return jnp.where(even, lines(pair, (planes * block + slot) * rows, rows), outer)

    for x in range(-2, planes + 2):
        stiff_ref[x + 2, 0:rows, :] = codes(x)
    node_inverse(stiff_ref, inner, inverse)

    def place(v, x, ref, slot):
        for y in range(1, rows):
            value = inside(ref, slot, y, rows, block) * inverse[x + 1, y - 1 : y, :]
            if v == 1:
                middle[y - 1] = value
            place_column(sums, diffs, v * inner + y - 1, value)

    def copy(v, w):
        for y in range(1, rows):
            sums[v * inner + y - 1] = sums_e[w * ys + y + 1]
            diffs[v * inner + y - 1] = diffs_e[w * ys + y + 1]

    @pl.when(even)
    def _():
        place(0, -1, edge, 0)
        place(1, 0, own, 0)
        copy(2, 0)

    @pl.when(jnp.logical_not(even))
    def _():
        copy(0, planes)
        place(1, planes, edge, 0)
        place(2, planes + 1, second, 0)

    layer = jnp.where(even, 1, planes + 1)
    find = whole(sums, diffs, inner)
    apply_elements(find, stiff_ref, acc_s, acc_d, 2, rows - 2, range(inner), layer, 1, cases)

    def image(x, y, place):
        def total(early, near):
            return merged(
                x, planes, even, lambda w: early[w * nodes_y + y],
                lambda v: near[v * inner + y - 1],
            )

        s, d = total(acc_se, acc_s), total(acc_de, acc_d)
        force = s - d + shift_up(s + d)
        scaled = force * inverse[x + 1, pl.ds(y - 1, 1), :]
        place_column(w_sums, w_diffs, place, scaled)
        value = direction_at(x, planes, even, lambda w: start[w * ys + y + 1], middle[y - 1])
        keep_pair(both_out, place, value, scaled, cases)
        return force

    def within(x, index):
        y, place = core[0] + index, x * len(core) + index
        force = image(x, y, place)
        given = own[pl.ds(pl.multiple_of((x * rows + y) * block, 8), block), :]
        keep_pair(right, place, given, force, cases)

    for x in range(planes):
        unrolled(len(core), len(core), functools.partial(within, x))
    last = planes * len(core)
    unrolled(len(core), len(core), lambda index: image(planes, core[0] + index, last + index))
    gram_out[...] = products(right[...], both_out[:, : last * 3 * LANES])


def main_kernel(
    sizes, first, own, pair, edge, second, ym, yp, ym_pair, yp_pair, corners,
    start, sums_e, diffs_e, acc_se, acc_de,
    sums_m, diffs_m, middle_m, acc_sm, acc_dm, w_sm, w_dm, both_m, gram_m,
    both_out, system_out, stiff_ref, inverse,
    middle, sums, diffs, acc_s0, acc_d0, acc_s1, acc_d1, w_sums, w_diffs,
    acc2_s, acc2_d, right, second_m, second_r, table,
):
    planes, rows, cases = sizes
    block = 3 * cases
    ys, nodes_y, inner = rows + 3, rows + 1, rows - 1
    core, rim = core_rows(rows), rim_rows(rows)
    columns, own_count = rim_columns(planes, rows)
    even = first[0] // planes % 2 == 0
    y_own, y_pair = (ym, yp), (ym_pair, yp_pair)

    def codes(x, y):
        def read(mine, plane):
            if y == 0:
                return lines(own if mine else pair, (planes * block + plane) * rows, rows)
            return beyond_codes(y_own if mine else y_pair, planes, plane, y, block)

        if 0 <= x < planes:
            return read(True, x)
        slot = x + 2 if x < 0 else x - planes
        if y == 0:
            outer = lines(edge, (block + slot) * rows, rows)
        else:
            outer = corner_codes(corners, slot, y, block)
        within = read(False, planes + x if x < 0 else x - planes)
        return jnp.where(even, outer, within) if x < 0 else jnp.where(even, within, outer)

    for x in range(-2, planes + 2):
        for y, count in ((-2, 2), (0, rows), (rows, 2)):
            stiff_ref[x + 2, y + 2 : y + 2 + count, :] = codes(x, y)
    node_inverse(stiff_ref, ys, inverse)

    sides = (-1, 0, rows, rows + 1)

    def place(v, x, ref, slot, beyond_at):
        for i, y in enumerate(sides):
            value = inside(ref, slot, y, rows, block) if y == 0 else beyond_at(y)
            value = value * inverse[x + 1, y + 1 : y + 2, :]
            if v == 1 and y in (0, rows):
                middle[y // rows] = value
            place_column(sums, diffs, v * 4 + i, value)

    def copy(v, w):
        for i, y in enumerate(sides):
            sums[v * 4 + i] = sums_e[w * ys + y + 1]
            diffs[v * 4 + i] = diffs_e[w * ys + y + 1]

    @pl.when(even)
    def _():
        place(0, -1, edge, 0, lambda y: corner(corners, 1, y, rows, block))
        place(1, 0, own, 0, lambda y: beyond(y_own, 0, y, rows, block))
        copy(2, 0)

    @pl.when(jnp.logical_not(even))
    def _():
        copy(0, planes)
        place(1, planes, edge, 0, lambda y: corner(corners, 0, y, rows, block))
        place(2, planes + 1, second, 0, lambda y: corner(corners, 1, y, rows, block))

    def find_low(row):
        return (sums, diffs, 4, row) if row < 2 else (sums_m, diffs_m, inner, 0)

    def find_high(row):
        return (sums, diffs, 4, row + 1) if row else (sums_m, diffs_m, inner, inner - 1)

    layer = jnp.where(even, 1, planes + 1)
    apply_elements(find_low, stiff_ref, acc_s0, acc_d0, 2, 2, range(1, 3), layer, 1, cases)
    apply_elements(find_high, stiff_ref, acc_s1, acc_d1, 2, 2, range(2), layer, rows + 1, cases)

    def image(x, y, place):
        def total(early, near, low, high):
            def outer(v):
                value = low[v * 2 + y] if y < 2 else high[v * 2 + y - inner]
                return value + near[v * inner + y - 1] if y in (1, inner) else value

            return merged(x, planes, even, lambda w: early[w * nodes_y + y], outer)

        s = total(acc_se, acc_sm, acc_s0, acc_s1)
        d = total(acc_de, acc_dm, acc_d0, acc_d1)
        force = s - d + shift_up(s + d)
        scaled = force * inverse[x + 1, y + 1 : y + 2, :]
        place_column(w_sums, w_diffs, x * len(rim) + rim.index(y), scaled)
        inner_middle = middle_m[y - 1] if y in (1, inner) else middle[y // rows]
        value = direction_at(x, planes, even, lambda w: start[w * ys + y + 1], inner_middle)
        keep_pair(both_out, place, value, scaled, cases)
        return force

    for index, (x, y) in enumerate(columns):
        force = image(x, y, index)
        if index < own_count:
            keep_pair(right, index, inside(own, x, y, rows, block), force, cases)

    def find(row):
        if row in rim:
            return w_sums, w_diffs, len(rim), rim.index(row)
        return w_sm, w_dm, len(core), row - core[0]

    apply_elements(find, stiff_ref, acc2_s, acc2_d, planes, rows, range(nodes_y), 2, 2, cases)

    def second_force(ref, x, y, place):
        column = x * nodes_y + y
        s, d = acc2_s[column], acc2_d[column]
        force = s - d + shift_up(s + d)
        for k in range(3):
            value = force[k * cases : (k + 1) * cases]
            high = value.astype(bf16).astype(f32)
            lane = pl.ds(pl.multiple_of((place * 3 + k) * LANES, LANES), LANES)
            ref[:, lane] = jnp.concatenate([high, value - high], 0).astype(bf16)

    unrolled(
        (planes + 1) * len(core), len(core),
        lambda index: second_force(
            second_m, index // len(core), core[0] + index % len(core), index
        ),
    )
    for index, (x, y) in enumerate(columns):
        second_force(second_r, x, y, index)

    two = 2 * cases
    gram = products(right[...], both_out[:, : own_count * 3 * LANES]) + gram_m[...]
    other = products(second_m[...], both_m[...]) + products(second_r[...], both_out[...])
    row = lax.broadcasted_iota(jnp.int32, (cases, cases), 0)
    column = lax.broadcasted_iota(jnp.int32, (cases, cases), 1)
    load_load, load_image = gram[:cases, :cases], gram[cases:, :cases]
    mixed, image_image = other[:, :cases], other[:, cases:]
    table[...] = jnp.zeros(table.shape, f32)
    table[:, 0:cases] = jnp.where(row <= column, load_load, load_image)
    table[:, cases:two] = jnp.where(row <= column, mixed, image_image)
    for lane, value in ((two, load_image), (two + 1, image_image)):
        own_entries = jnp.where(row == column, value, 0.0)
        table[:, lane : lane + 1] = jnp.sum(own_entries, axis=1, keepdims=True)
    half = cases // 2
    folded = table[:half, :] + pltpu.roll(table[half:, :], LANES // 2, 1)
    depth = system_out.shape[2]
    for index in range(system_out.shape[0]):
        for part in range(half // depth):
            system_out[index, part] = folded[part * depth : (part + 1) * depth]


def solve_kernel(
    sizes, system, system_pair, both_m, both_r, codes, out, mixing, sums, diffs, energy, square, full
):
    planes, rows, cases = sizes
    two = 2 * cases
    nodes_y = rows + 1
    count = planes * rows
    total = jnp.sum(system[...], axis=0) + jnp.sum(system_pair[...], axis=0)
    half, depth = cases // 2, system.shape[2]
    square[...] = jnp.zeros(square.shape, f32)
    for part in range(half // depth):
        value = total[part]
        square[part * depth : (part + 1) * depth, :] = value
        lines = slice(half + part * depth, half + (part + 1) * depth)
        square[lines, :] = pltpu.roll(value, LANES // 2, 1)
    value, turned = square[0:cases, :], jnp.transpose(square[...])
    line = lax.broadcasted_iota(jnp.int32, (cases, cases), 0)
    place = lax.broadcasted_iota(jnp.int32, (cases, cases), 1)

    def mended(start, diagonal=None):
        kept, other = value[:, start : start + cases], turned[start : start + cases, :cases]
        if diagonal is None:
            return jnp.where(line <= place, kept, other)
        inner = jnp.where(line < place, other, value[:, diagonal : diagonal + 1])
        return jnp.where(line > place, kept, inner)

    load_image, mixed = mended(0, two), mended(cases)
    parts = ((load_image, mixed), (mixed, mended(cases, two + 1)), (mended(0), load_image))
    full[...] = jnp.zeros(full.shape, f32)
    for index, (left, right) in enumerate(parts):
        full[index * cases : (index + 1) * cases, 0:cases] = left
        full[index * cases : (index + 1) * cases, cases:two] = right
    table = full[...]
    lane = lax.broadcasted_iota(jnp.int32, (1, LANES), 1)
    gone, wide = 0, 4
    for pivot in range(0, two, wide):
        drop = pivot // 8 * 8 - gone
        table = table[drop:]
        gone += drop
        line = pivot - gone
        inner = (lane >= pivot) & (lane < pivot + wide)
        found = [table[line + p : line + p + 1, :] for p in range(wide)]
        block = [
            [jnp.broadcast_to(row[:, pivot + q : pivot + q + 1], row.shape) for q in range(wide)]
            for row in found
        ]
        solved = [
            jnp.where(lane == pivot + p, -1.0, jnp.where(inner, 0.0, found[p]))
            for p in range(wide)
        ]
        for p in range(wide):
            inverse = 1.0 / block[p][p]
            solved[p] = solved[p] * inverse
            block[p] = [value * inverse for value in block[p]]
            for q in range(wide):
                if q != p:
                    factor = block[q][p]
                    solved[q] = solved[q] - factor * solved[p]
                    for r in range(p + 1, wide):
                        block[q][r] = block[q][r] - factor * block[p][r]
        update = None
        for q in range(wide):
            term = table[:, pivot + q : pivot + q + 1] * solved[q]
            update = term if update is None else update + term
        table = jnp.where(inner, 0.0, table) - update
    answer = table[two - gone :, :two]
    high = answer.astype(bf16).astype(f32)
    mixing[...] = jnp.zeros(mixing.shape, f32)
    mixing[0:cases, 0:two] = high
    mixing[0:cases, two : 2 * two] = high
    mixing[cases:two, 0:two] = answer - high
    mix = mixing[...][:, : 2 * two].astype(bf16)

    def combined(ref, place, width):
        value = jnp.dot(
            mix, ref[:, place * 3 * LANES : (place + width) * 3 * LANES], preferred_element_type=f32
        )
        return value[:cases] + value[cases:]

    def keep(value, index, column):
        for k in range(3):
            part = value[:, (index * 3 + k) * LANES : (index * 3 + k + 1) * LANES]
            moved = shift_down(part)
            sums[column, k * cases : (k + 1) * cases, :] = part + moved
            diffs[column, k * cases : (k + 1) * cases, :] = moved - part

    core = core_rows(rows)
    for x in range(planes + 1):
        value = combined(both_m, x * len(core), len(core))
        for index, y in enumerate(core):
            keep(value, index, x * nodes_y + y)
    columns, _ = rim_columns(planes, rows)
    for start in range(0, len(columns), 6):
        some = columns[start : start + 6]
        value = combined(both_r, start, len(some))
        for index, (x, y) in enumerate(some):
            keep(value, index, x * nodes_y + y)

    find = whole(sums, diffs, nodes_y)
    tiles = cases // 8

    def step(plane, _):
        for tile in range(tiles):
            lower = x_modes(find, plane, 0, tile, cases)
            for row in range(rows):
                upper = x_modes(find, plane, row + 1, tile, cases)
                part = mode_energy(modes_of(lower, upper))
                if tile == 0:
                    energy[row] = part
                else:
                    energy[row] += part
                lower = upper
        total = jnp.sum(energy[...], axis=1)
        total = (-3.0 / cases) * jnp.abs(codes[plane]) * total
        for index in range(out.shape[0]):
            out[index, plane] = total
        return 0

    lax.fori_loop(0, planes, step, 0)


def smooth(ref, x, rows):
    weight = [2.5 - math.sqrt(q) for q in range(7)]
    near = {}
    for dx in range(-2, 3):
        for dy in range(-2, 3):
            q = dx * dx + dy * dy
            if q <= 5:
                value = ref[x + 2 + dx, 2 + dy : 2 + dy + rows, :]
                near[q] = value if q not in near else near[q] + value
    result = None
    for dz in range(3):
        part = None
        for q, value in near.items():
            if q + dz * dz <= 6:
                term = weight[q + dz * dz] * value
                part = term if part is None else part + term
        if dz == 0:
            result = part
        else:
            place = lax.broadcasted_iota(jnp.int32, part.shape, 1)
            forward = jnp.where(place >= LANES - dz, 0.0, pltpu.roll(part, LANES - dz, 1))
            backward = jnp.where(place < dz, 0.0, pltpu.roll(part, dz, 1))
            result = result + (forward + backward)
    return result


def scale_kernel(sizes, counts, start, levels, out, there):
    planes, rows, _ = sizes
    y = lax.broadcasted_iota(jnp.int32, (rows + 4, LANES), 0) + (start[1] - 2)
    in_y = (y >= 0) & (y < counts[1] * rows)
    for x in range(planes + 4):
        global_x = start[0] + (x - 2)
        in_x = (global_x >= 0) & (global_x < counts[0] * planes)
        there[x] = jnp.where(in_y & in_x, 1.0, 0.0)
    for x in range(planes):
        density = 0.3 + 0.7 * levels[x].astype(f32) / (LEVELS - 1)
        out[x] = 1.0 / (density * smooth(there, x, rows))


def filter_kernel(sizes, counts, start, blocks, blocks_pair, scale, out, wide):
    planes, rows, _ = sizes
    sides_x = ((-1, planes - 2, planes, 0), (0, 0, planes, 2), (1, 0, 2, 2 + planes))
    sides_y = ((-1, rows - 2, rows, 0), (0, 0, rows, 2), (1, 0, 2, 2 + rows))
    for step_x, x0, x1, to_x in sides_x:
        for step_y, y0, y1, to_y in sides_y:
            at_x = start[0] // planes + step_x
            at_y = start[1] // rows + step_y
            inside = (at_x >= 0) & (at_x < counts[0]) & (at_y >= 0) & (at_y < counts[1])
            index = jnp.where(inside, at_x // 2 * counts[1] + at_y, 0)
            value = (blocks_pair if step_x else blocks)[index, x0:x1, y0:y1, :]
            wide[to_x : to_x + x1 - x0, to_y : to_y + y1 - y0, :] = jnp.where(inside, value, 0.0)
    for x in range(planes):
        out[x] = smooth(wide, x, rows) * scale[x]


def local(forces, levels, supports):
    _, cases, planes, rows, _ = forces.shape
    sizes = (planes, rows, cases)
    block = 3 * cases
    count_x, count_y = lax.axis_size("gx"), lax.axis_size("gy")

    def shape(blocks, codes):
        return jax.ShapeDtypeStruct((blocks * block + up8(codes), LANES), f32)

    density = 0.3 + 0.7 * levels.astype(f32) / (LEVELS - 1)
    codes = density * density * density
    codes = jnp.where(supports == 0, codes, -codes)
    start = jnp.stack([lax.axis_index("gx") * planes, lax.axis_index("gy") * rows])
    start = start.astype(jnp.int32)
    counts = (count_x, count_y)
    scalars = pl.BlockSpec(memory_space=pltpu.SMEM)
    own, edge = pl.pallas_call(
        functools.partial(pack_kernel, sizes),
        out_shape=[shape(planes * rows, planes * rows), shape(rows, 2 * rows)],
        in_specs=[scalars] + [VMEM] * 2,
        out_specs=[VMEM] * 2,
        compiler_params=PARAMS,
        name="pack",
    )(start, forces, codes)
    scale = pl.pallas_call(
        functools.partial(scale_kernel, sizes, counts),
        out_shape=jax.ShapeDtypeStruct((planes, rows, LANES), f32),
        in_specs=[scalars, VMEM],
        out_specs=VMEM,
        scratch_shapes=[pltpu.VMEM((planes + 4, rows + 4, LANES), f32)],
        compiler_params=PARAMS,
        name="scale",
    )(start, levels)

    def moved(value, axis, step):
        count = lax.axis_size(axis)
        pairs = [(i, i + step) for i in range(count) if 0 <= i + step < count]
        return lax.ppermute(value, axis, pairs)

    def links(first, step):
        return [(i, i + step) for i in range(first, count_x, 2) if 0 <= i + step < count_x]

    def swapped(value):
        return lax.ppermute(value, "gx", links(0, 1) + links(1, -1))

    def across(value):
        return lax.ppermute(value, "gx", links(1, 1) + links(2, -1))

    edge = across(edge)
    pair = swapped(own)
    own, pair = lax.optimization_barrier((own, pair))
    ym, yp = pl.pallas_call(
        functools.partial(rows_kernel, sizes),
        out_shape=[shape(2 * planes, 2 * planes), shape(planes, 2 * planes)],
        in_specs=[VMEM],
        out_specs=[VMEM] * 2,
        compiler_params=PARAMS,
        name="rows",
    )(own)
    from_yp, from_ym = moved(ym, "gy", -1), moved(yp, "gy", 1)
    second = pl.pallas_call(
        functools.partial(second_kernel, sizes),
        out_shape=shape(rows, 0),
        in_specs=[VMEM] * 2,
        out_specs=VMEM,
        compiler_params=PARAMS,
        name="second",
    )(swapped(codes), own)
    second = lax.ppermute(second, "gx", links(2, -1))
    pair_yp, pair_ym = swapped(from_yp), swapped(from_ym)
    from_ym, from_yp, edge = lax.optimization_barrier((from_ym, from_yp, edge))
    corners = across(
        pl.pallas_call(
            functools.partial(corner_kernel, sizes),
            out_shape=jax.ShapeDtypeStruct((6 * block + 16, LANES), f32),
            in_specs=[scalars] + [VMEM] * 2,
            out_specs=VMEM,
            compiler_params=PARAMS,
            name="corners",
        )(start, from_ym, from_yp)
    )

    devices = count_x * count_y
    nodes = (planes + 1) * (rows + 1)
    window = jax.ShapeDtypeStruct(((planes + 1) * (rows + 3), block, LANES), f32)
    partial_forces = jax.ShapeDtypeStruct((nodes, block, LANES), f32)
    early = pl.pallas_call(
        functools.partial(early_kernel, sizes),
        out_shape=[window] * 3 + [partial_forces] * 2,
        in_specs=[scalars] + [VMEM] * 6,
        out_specs=[VMEM] * 5,
        scratch_shapes=[
            pltpu.VMEM((planes + 2, up8(rows + 4), LANES), f32),
            pltpu.VMEM((planes + 1, up8(rows + 3), LANES), f32),
        ],
        compiler_params=PARAMS,
        cost_estimate=pl.CostEstimate(
            flops=200 * planes * rows * block * LANES, bytes_accessed=2**23, transcendentals=0
        ),
        name="early",
    )(start, own, pair, from_ym, from_yp, pair_ym, pair_yp)

    def columns(count):
        return jax.ShapeDtypeStruct((count, block, LANES), f32)

    def fields(lines, count):
        return jax.ShapeDtypeStruct((lines * cases, count * 3 * LANES), bf16)

    def scratch(value):
        return pltpu.VMEM(value.shape, value.dtype)

    core = len(core_rows(rows))
    middle = pl.pallas_call(
        functools.partial(middle_kernel, sizes),
        out_shape=[columns(3 * (rows - 1))] * 2
        + [columns(rows - 1)]
        + [columns(3 * (rows - 1))] * 2
        + [columns((planes + 1) * core)] * 2
        + [fields(4, (planes + 1) * core), jax.ShapeDtypeStruct((2 * cases, 2 * cases), f32)],
        in_specs=[scalars] + [VMEM] * 9,
        out_specs=[VMEM] * 9,
        scratch_shapes=[
            pltpu.VMEM((planes + 4, up8(rows), LANES), f32),
            pltpu.VMEM((planes + 3, up8(rows), LANES), f32),
            scratch(fields(4, planes * core)),
        ],
        compiler_params=PARAMS,
        name="middle",
    )(start, own, pair, edge, second, *early)

    rim, rim_own = rim_columns(planes, rows)
    field = scratch(columns(nodes))
    both, system = pl.pallas_call(
        functools.partial(main_kernel, sizes),
        out_shape=[
            fields(4, len(rim)),
            jax.ShapeDtypeStruct((devices // 2, cases // 8, 4, LANES), f32),
        ],
        in_specs=[scalars] + [VMEM] * 23,
        out_specs=[VMEM] * 2,
        scratch_shapes=[
            pltpu.VMEM((planes + 4, up8(rows + 4), LANES), f32),
            pltpu.VMEM((planes + 3, up8(rows + 3), LANES), f32),
            scratch(columns(2)),
            *[scratch(columns(12))] * 2,
            *[scratch(columns(6))] * 4,
            *[scratch(columns((planes + 1) * 4))] * 2,
            field, field,
            scratch(fields(4, rim_own)),
            scratch(fields(2, (planes + 1) * core)),
            scratch(fields(2, len(rim))),
            pltpu.VMEM((cases, LANES), f32),
        ],
        compiler_params=PARAMS,
        name="operator",
    )(
        start, own, pair, edge, second, from_ym, from_yp, pair_ym, pair_yp, corners,
        *early, *middle,
    )

    groups = [
        [x * count_y + y for x in range(side, count_x, 2) for y in range(count_y)]
        for side in range(2)
    ]

    def gathered(copies):
        mine = lax.all_to_all(copies, ("gx", "gy"), 0, 0, axis_index_groups=groups)
        return mine, swapped(mine)

    system = gathered(system)

    weighted = pl.pallas_call(
        functools.partial(solve_kernel, sizes),
        out_shape=jax.ShapeDtypeStruct((devices // 2, planes, rows, LANES), f32),
        in_specs=[VMEM] * 5,
        out_specs=VMEM,
        scratch_shapes=[
            pltpu.VMEM((2 * cases, LANES), f32),
            field,
            field,
            pltpu.VMEM((rows, 8, LANES), f32),
            pltpu.VMEM((LANES, LANES), f32),
            pltpu.VMEM((3 * cases, LANES), f32),
        ],
        compiler_params=PARAMS,
        name="solve",
    )(*system, middle[7], both, codes)

    blocks = gathered(weighted)
    return pl.pallas_call(
        functools.partial(filter_kernel, sizes, counts),
        out_shape=jax.ShapeDtypeStruct((planes, rows, LANES), f32),
        in_specs=[scalars] + [VMEM] * 3,
        out_specs=VMEM,
        scratch_shapes=[pltpu.VMEM((planes + 4, rows + 4, LANES), f32)],
        compiler_params=PARAMS,
        name="cone",
    )(start, *blocks, scale)


def solution(mesh):
    return jax.shard_map(
        local,
        mesh=mesh,
        in_specs=(P(None, None, "gx", "gy", None), P("gx", "gy", None), P("gx", "gy", None)),
        out_specs=P("gx", "gy", None),
        check_vma=False,
    )
```

```python
import functools
import math

import jax
import jax.numpy as jnp
from jax import lax
from jax.experimental import pallas as pl
from jax.experimental.pallas import tpu as pltpu
from jax.sharding import PartitionSpec as P

LEVELS = 16
LOAD = 0.2
LANES = 128
POISSON = 0.3
LAME = POISSON / ((1.0 + POISSON) * (1.0 - 2.0 * POISSON))
SHEAR = 1.0 / (2.0 * (1.0 + POISSON))
DIAGONAL = (LAME + 2.0 * SHEAR) / 9.0 + 2.0 * SHEAR / 9.0
VMEM = pl.BlockSpec(memory_space=pltpu.VMEM)
PARAMS = pltpu.CompilerParams(vmem_limit_bytes=30 * 2**20)
f32 = jnp.float32
bf16 = jnp.bfloat16


def up8(count):
    return -(-count // 8) * 8


def shift_down(value):
    lane = lax.broadcasted_iota(jnp.int32, value.shape, value.ndim - 1)
    rolled = pltpu.roll(value, LANES - 1, value.ndim - 1)
    return jnp.where(lane == LANES - 1, 0.0, rolled)


def shift_up(value):
    lane = lax.broadcasted_iota(jnp.int32, value.shape, value.ndim - 1)
    return jnp.where(lane == 0, 0.0, pltpu.roll(value, 1, value.ndim - 1))


def unrolled(count, factor, body):
    def turn(step, _):
        for offset in range(factor):
            body(step * factor + offset)
        return 0

    turns = count // factor
    if turns:
        lax.fori_loop(0, turns, turn, 0)
    for index in range(turns * factor, count):
        body(index)


def split(value):
    high = value.astype(bf16)
    return high, (value - high.astype(f32)).astype(bf16)


def modes_of(lower, upper):
    out = [[[[None] * 3 for _ in range(2)] for _ in range(2)] for _ in range(2)]
    for a in range(2):
        for c in range(2):
            for k in range(3):
                if a or c:
                    out[a][0][c][k] = lower[a][c][k] + upper[a][c][k]
                out[a][1][c][k] = upper[a][c][k] - lower[a][c][k]
    return out


PAIRS = (((1, 1, 0, 0), (0, 1, 1, 2)), ((1, 0, 1, 0), (0, 1, 1, 1)), ((1, 1, 0, 1), (1, 0, 1, 2)))
TRIPLE = ((0, 1, 1, 0), (1, 0, 1, 1), (1, 1, 0, 2))
SHEARS = (((0, 1, 0, 0), (1, 0, 0, 1)), ((0, 0, 1, 0), (1, 0, 0, 2)), ((0, 0, 1, 1), (0, 1, 0, 2)))
AXIAL = ((1, 0, 0, 0), (0, 1, 0, 1), (0, 0, 1, 2))


def at(modes, place):
    a, b, c, k = place
    return modes[a][b][c][k]


def mode_forces(modes, stiff):
    out = [[[[None] * 3 for _ in range(2)] for _ in range(2)] for _ in range(2)]

    def put(place, value):
        a, b, c, k = place
        out[a][b][c][k] = value

    shear = stiff * (SHEAR / 16)
    for first, second in SHEARS:
        force = shear * (at(modes, first) + at(modes, second))
        put(first, force)
        put(second, force)
    one, two, three = (at(modes, place) for place in AXIAL)
    volume = (stiff * (LAME / 16)) * (one + two + three)
    axial = stiff * (SHEAR / 8)
    for place in AXIAL:
        put(place, volume + axial * at(modes, place))
    own, cross = stiff * ((LAME + 3 * SHEAR) / 48), stiff * (LAME / 48)
    for first, second in PAIRS:
        one, two = at(modes, first), at(modes, second)
        put(first, own * one + cross * two)
        put(second, own * two + cross * one)
    twist = stiff * (SHEAR / 48)
    one, two, three = (at(modes, place) for place in TRIPLE)
    total = one + two + three
    for place in TRIPLE:
        put(place, twist * (total + at(modes, place)))
    last = stiff * ((LAME + 4 * SHEAR) / 144)
    for k in range(3):
        put((1, 1, 1, k), last * modes[1][1][1][k])
    return out


def mode_energy(modes):
    def square(value):
        return value * value

    shear = None
    for first, second in SHEARS:
        term = square(at(modes, first) + at(modes, second))
        shear = term if shear is None else shear + term
    one, two, three = (at(modes, place) for place in AXIAL)
    energy = (SHEAR / 16) * shear + (LAME / 16) * square(one + two + three)
    energy = energy + (SHEAR / 8) * (square(one) + square(two) + square(three))
    squares, products = None, None
    for first, second in PAIRS:
        one, two = at(modes, first), at(modes, second)
        term, product = square(one) + square(two), one * two
        squares = term if squares is None else squares + term
        products = product if products is None else products + product
    energy = energy + ((LAME + 3 * SHEAR) / 48) * squares + (LAME / 24) * products
    one, two, three = (at(modes, place) for place in TRIPLE)
    twist = square(one + two + three) + square(one) + square(two) + square(three)
    energy = energy + (SHEAR / 48) * twist
    last = square(modes[1][1][1][0]) + square(modes[1][1][1][1]) + square(modes[1][1][1][2])
    return energy + ((LAME + 4 * SHEAR) / 144) * last


def x_modes(find, plane, row, tile, cases):
    sums, diffs, columns, column = find(row)
    out = [[[None] * 3 for _ in range(2)] for _ in range(2)]
    for c, ref in enumerate((sums, diffs)):
        for k in range(3):
            rows = pl.ds(pl.multiple_of(k * cases + tile * 8, 8), 8)
            one = ref[plane * columns + column, rows, :]
            two = ref[(plane + 1) * columns + column, rows, :]
            out[0][c][k] = one + two
            out[1][c][k] = two - one
    return out


def whole(sums, diffs, columns):
    return lambda row: (sums, diffs, columns, row)


def apply_elements(find, stiff_ref, acc_s, acc_d, planes, rows, kept, stiff_x, stiff_y, cases):
    columns = len(kept)
    tiles = cases // 8
    for column in range(columns):
        acc_s[column] = jnp.zeros(acc_s.shape[1:], f32)
        acc_d[column] = jnp.zeros(acc_d.shape[1:], f32)

    def step(index, _):
        plane, tile = index // tiles, index % tiles

        def emit(row, total):
            if row not in kept:
                return
            for c, acc in enumerate((acc_s, acc_d)):
                for k in range(3):
                    lines = pl.ds(pl.multiple_of(k * cases + tile * 8, 8), 8)
                    low = plane * columns + row - kept[0]
                    acc[low, lines, :] += total[0][c][k] - total[1][c][k]
                    acc[low + columns, lines, :] = total[0][c][k] + total[1][c][k]

        lower = x_modes(find, plane, 0, tile, cases)
        carry = None
        for row in range(rows):
            upper = x_modes(find, plane, row + 1, tile, cases)
            stiff = jnp.broadcast_to(
                stiff_ref[plane + stiff_x, pl.ds(row + stiff_y, 1), :], (8, LANES)
            )
            forces = mode_forces(modes_of(lower, upper), stiff)
            here = [[[None] * 3 for _ in range(2)] for _ in range(2)]
            following = [[[None] * 3 for _ in range(2)] for _ in range(2)]
            for a in range(2):
                for c in range(2):
                    for k in range(3):
                        one, two = forces[a][0][c][k], forces[a][1][c][k]
                        low = -two if one is None else one - two
                        high = two if one is None else one + two
                        here[a][c][k] = low if carry is None else carry[a][c][k] + low
                        following[a][c][k] = high
            emit(row, here)
            carry, lower = following, upper
        emit(rows, carry)
        return 0

    lax.fori_loop(0, planes * tiles, step, 0)


def fill(source, base, sizes, ref, xs, ys, code_xs, code_ys):
    planes, rows, cases = sizes
    block = 3 * cases
    line = 0
    for x in xs:
        start = (x * rows + ys[0]) * block
        count = len(ys) * block
        ref[line : line + count, :] = source[start : start + count, :]
        line += count
    for x in code_xs:
        start = base + x * rows + code_ys[0]
        ref[line : line + len(code_ys), :] = source[start : start + len(code_ys), :]
        line += len(code_ys)
    if line < ref.shape[0]:
        ref[line:, :] = jnp.zeros((ref.shape[0] - line, LANES), f32)


def pack_kernel(sizes, forces, codes, own, edge):
    planes, rows, cases = sizes
    block = 3 * cases
    base = planes * rows * block
    for x in range(planes):
        own[base + x * rows : base + (x + 1) * rows, :] = codes[x]
        scale = jnp.where(codes[x] > 0.0, LOAD, 0.0)
        for k in range(3):
            for c in range(cases):
                start = x * rows * block + k * cases + c
                own[pl.ds(start, rows, stride=block), :] = forces[k, c, x] * scale

    even = lax.axis_index("gx") % 2 == 0
    size = rows * block
    for line in range(0, size, block):
        high = lines(own, (planes - 1) * size + line, block)
        edge[line : line + block, :] = jnp.where(even, lines(own, line, block), high)
    high = lines(own, base + (planes - 2) * rows, 2 * rows)
    edge[size:, :] = jnp.where(even, lines(own, base, 2 * rows), high)


def second_kernel(sizes, begun, own, second):
    _, rows, cases = sizes
    size = rows * 3 * cases
    second[...] = lines(own, size, size)


def rows_kernel(sizes, own, ym, yp):
    planes, rows, cases = sizes
    base = planes * rows * 3 * cases
    every_x = range(planes)
    fill(own, base, sizes, ym, every_x, (0, 1), every_x, (0, 1))
    fill(own, base, sizes, yp, every_x, (rows - 1,), every_x, (rows - 2, rows - 1))


def corner_kernel(sizes, ym, yp, out):
    planes, rows, cases = sizes
    block = 3 * cases
    even = lax.axis_index("gx") % 2 == 0
    line = 0
    for source, width in ((ym, 1), (yp, 2)):
        size = width * block
        parts = [(at, (planes - 2) * size + at, block) for at in range(0, 2 * size, block)]
        parts.append((planes * size, planes * size + (planes - 2) * 2, 4))
        for low, high, count in parts:
            value = lines(source, low, count)
            if low != high:
                value = jnp.where(even, value, lines(source, high, count))
            out[line : line + count, :] = value
            line += count
        out[line : line + 4, :] = jnp.zeros((4, LANES), f32)
        line += 4


def lines(ref, start, count):
    return ref[start : start + count, :]


def inside(ref, x, y, rows, block):
    return lines(ref, (x * rows + y) * block, block)


def beyond(refs, slot, y, rows, block):
    below, above = refs
    if y < 0:
        return lines(below, slot * block, block)
    return lines(above, (slot * 2 + y - rows) * block, block)


def beyond_codes(refs, slots, slot, y, block):
    below, above = refs
    if y < 0:
        return lines(below, slots * block + slot * 2, 2)
    return lines(above, slots * 2 * block + slot * 2, 2)


def corner(ref, slot, y, rows, block):
    start = slot * block if y < 0 else 2 * block + 8 + (slot * 2 + y - rows) * block
    return lines(ref, start, block)


def corner_codes(ref, slot, y, block):
    return lines(ref, (2 * block if y < 0 else 6 * block + 8) + slot * 2, 2)


def node_inverse(signed, count, out):
    planes = signed.shape[0]
    for x in range(1, planes):
        codes = signed[x, 0 : count + 1, :]
        total = jnp.abs(signed[x - 1, 0 : count + 1, :]) + jnp.abs(codes)
        total = total[:-1] + total[1:]
        total = total + shift_up(total)
        free = codes[1:] > 0.0
        value = 1.0 / (DIAGONAL * jnp.where(free, total, 1.0))
        out[x - 1, 0:count, :] = jnp.where(free, value, 0.0)
    for x in range(planes):
        signed[x] = jnp.abs(signed[x])


def place_column(sums, diffs, column, value):
    moved = shift_down(value)
    sums[column] = value + moved
    diffs[column] = moved - value


def early_kernel(
    sizes, own, pair, ym, yp, ym_pair, yp_pair, start, sums, diffs, acc_s, acc_d,
    stiff_ref, inverse,
):
    planes, rows, cases = sizes
    block = 3 * cases
    ys = rows + 3
    even = lax.axis_index("gx") % 2 == 0
    y_own, y_pair = (ym, yp), (ym_pair, yp_pair)

    def both_ways(w, read):
        low = read(True, w + 1) if w + 1 < planes else read(False, w + 1 - planes)
        high = read(False, planes + w - 1) if w < 1 else read(True, w - 1)
        return jnp.where(even, low, high)

    def codes(w, y):
        def read(mine, x):
            if y == 0:
                return lines(own if mine else pair, (planes * block + x) * rows, rows)
            return beyond_codes(y_own if mine else y_pair, planes, x, y, block)

        return both_ways(w, read)

    for w in range(-1, planes + 1):
        for y, count in ((-2, 2), (0, rows), (rows, 2)):
            stiff_ref[w + 1, y + 2 : y + 2 + count, :] = codes(w, y)
    node_inverse(stiff_ref, ys, inverse)
    for w in range(planes + 1):
        for y in range(-1, rows + 2):

            def read(mine, x):
                if 0 <= y < rows:
                    return inside(own if mine else pair, x, y, rows, block)
                return beyond(y_own if mine else y_pair, x, y, rows, block)

            value = both_ways(w, read) * inverse[w, y + 1 : y + 2, :]
            column = w * ys + y + 1
            start[column] = value
            place_column(sums, diffs, column, value)
    kept = range(1, rows + 2)
    find = whole(sums, diffs, ys)
    apply_elements(find, stiff_ref, acc_s, acc_d, planes, rows + 2, kept, 1, 1, cases)


def core_rows(rows):
    return range(2, rows - 1)


def rim_rows(rows):
    return (0, 1, rows - 1, rows)


def rim_columns(planes, rows):
    own = [(x, y) for x in range(planes) for y in rim_rows(rows) if y < rows]
    beyond_own = [(x, rows) for x in range(planes)] + [(planes, y) for y in rim_rows(rows)]
    return own + beyond_own, len(own)


def merged(x, planes, even, early, near):
    low = ([x - 1] if x >= 1 else [], [x + 1] if x <= 1 else [])
    high = ([x + 1] if x < planes else [], [x - planes + 1] if x >= planes - 1 else [])
    if low[0] and low[1] and high[0] and high[1]:
        one = early(jnp.where(even, low[0][0], high[0][0]))
        return one + near(jnp.where(even, low[1][0], high[1][0]))

    def read(places):
        found = [early(w) for w in places[0]] + [near(v) for v in places[1]]
        return found[0] if len(found) == 1 else found[0] + found[1]

    return jnp.where(even, read(low), read(high))


def direction_at(x, planes, even, early, middle):
    if x == 0:
        return jnp.where(even, middle, early(1))
    if x == planes:
        return jnp.where(even, early(planes - 1), middle)
    return early(jnp.where(even, x - 1, x + 1))


def keep_pair(ref, place, one, two, cases):
    for k in range(3):
        part = slice(k * cases, (k + 1) * cases)
        high, rest = split(jnp.concatenate([one[part], two[part]], 0))
        lane = pl.ds(pl.multiple_of((place * 3 + k) * LANES, LANES), LANES)
        ref[0 : 2 * cases, lane] = high
        ref[2 * cases : 4 * cases, lane] = rest


def products(first, second):
    contract = (((1,), (1,)), ((), ()))
    out = lax.dot_general(first, second, contract, preferred_element_type=f32)
    left, right = out.shape[0] // 2, out.shape[1] // 2
    out = out[:, :right] + out[:, right:]
    return out[:left] + out[left:]


def middle_kernel(
    sizes, own, pair, edge, second, start, sums_e, diffs_e, acc_se, acc_de,
    sums, diffs, middle, acc_s, acc_d, w_sums, w_diffs, both_out, gram_out,
    stiff_ref, inverse, right,
):
    planes, rows, cases = sizes
    block = 3 * cases
    ys, nodes_y, inner = rows + 3, rows + 1, rows - 1
    core = core_rows(rows)
    even = lax.axis_index("gx") % 2 == 0

    def codes(x):
        if 0 <= x < planes:
            return lines(own, (planes * block + x) * rows, rows)
        slot = x + 2 if x < 0 else x - planes
        outer = lines(edge, (block + slot) * rows, rows)
        if x < 0:
            return jnp.where(even, outer, lines(pair, (planes * block + planes + x) * rows, rows))
        return jnp.where(even, lines(pair, (planes * block + slot) * rows, rows), outer)

    for x in range(-2, planes + 2):
        stiff_ref[x + 2, 0:rows, :] = codes(x)
    node_inverse(stiff_ref, inner, inverse)

    def place(v, x, ref, slot):
        for y in range(1, rows):
            value = inside(ref, slot, y, rows, block) * inverse[x + 1, y - 1 : y, :]
            if v == 1:
                middle[y - 1] = value
            place_column(sums, diffs, v * inner + y - 1, value)

    def copy(v, w):
        for y in range(1, rows):
            sums[v * inner + y - 1] = sums_e[w * ys + y + 1]
            diffs[v * inner + y - 1] = diffs_e[w * ys + y + 1]

    @pl.when(even)
    def _():
        place(0, -1, edge, 0)
        place(1, 0, own, 0)
        copy(2, 0)

    @pl.when(jnp.logical_not(even))
    def _():
        copy(0, planes)
        place(1, planes, edge, 0)
        place(2, planes + 1, second, 0)

    layer = jnp.where(even, 1, planes + 1)
    find = whole(sums, diffs, inner)
    apply_elements(find, stiff_ref, acc_s, acc_d, 2, rows - 2, range(inner), layer, 1, cases)

    def image(x, y, place):
        def total(early, near):
            return merged(
                x, planes, even, lambda w: early[w * nodes_y + y],
                lambda v: near[v * inner + y - 1],
            )

        s, d = total(acc_se, acc_s), total(acc_de, acc_d)
        force = s - d + shift_up(s + d)
        scaled = force * inverse[x + 1, pl.ds(y - 1, 1), :]
        place_column(w_sums, w_diffs, place, scaled)
        value = direction_at(x, planes, even, lambda w: start[w * ys + y + 1], middle[y - 1])
        keep_pair(both_out, place, value, scaled, cases)
        return force

    def within(x, index):
        y, place = core[0] + index, x * len(core) + index
        force = image(x, y, place)
        given = own[pl.ds(pl.multiple_of((x * rows + y) * block, 8), block), :]
        keep_pair(right, place, given, force, cases)

    for x in range(planes):
        unrolled(len(core), len(core), functools.partial(within, x))
    last = planes * len(core)
    unrolled(len(core), len(core), lambda index: image(planes, core[0] + index, last + index))
    gram_out[...] = products(right[...], both_out[:, : last * 3 * LANES])


def main_kernel(
    sizes, own, pair, edge, second, ym, yp, ym_pair, yp_pair, corners,
    start, sums_e, diffs_e, acc_se, acc_de,
    sums_m, diffs_m, middle_m, acc_sm, acc_dm, w_sm, w_dm, both_m, gram_m,
    both_out, system_out, stiff_ref, inverse,
    middle, sums, diffs, acc_s0, acc_d0, acc_s1, acc_d1, w_sums, w_diffs,
    acc2_s, acc2_d, right, second_m, second_r, table,
):
    planes, rows, cases = sizes
    block = 3 * cases
    ys, nodes_y, inner = rows + 3, rows + 1, rows - 1
    core, rim = core_rows(rows), rim_rows(rows)
    columns, own_count = rim_columns(planes, rows)
    even = lax.axis_index("gx") % 2 == 0
    y_own, y_pair = (ym, yp), (ym_pair, yp_pair)

    def codes(x, y):
        def read(mine, plane):
            if y == 0:
                return lines(own if mine else pair, (planes * block + plane) * rows, rows)
            return beyond_codes(y_own if mine else y_pair, planes, plane, y, block)

        if 0 <= x < planes:
            return read(True, x)
        slot = x + 2 if x < 0 else x - planes
        if y == 0:
            outer = lines(edge, (block + slot) * rows, rows)
        else:
            outer = corner_codes(corners, slot, y, block)
        within = read(False, planes + x if x < 0 else x - planes)
        return jnp.where(even, outer, within) if x < 0 else jnp.where(even, within, outer)

    for x in range(-2, planes + 2):
        for y, count in ((-2, 2), (0, rows), (rows, 2)):
            stiff_ref[x + 2, y + 2 : y + 2 + count, :] = codes(x, y)
    node_inverse(stiff_ref, ys, inverse)

    sides = (-1, 0, rows, rows + 1)

    def place(v, x, ref, slot, beyond_at):
        for i, y in enumerate(sides):
            value = inside(ref, slot, y, rows, block) if y == 0 else beyond_at(y)
            value = value * inverse[x + 1, y + 1 : y + 2, :]
            if v == 1 and y in (0, rows):
                middle[y // rows] = value
            place_column(sums, diffs, v * 4 + i, value)

    def copy(v, w):
        for i, y in enumerate(sides):
            sums[v * 4 + i] = sums_e[w * ys + y + 1]
            diffs[v * 4 + i] = diffs_e[w * ys + y + 1]

    @pl.when(even)
    def _():
        place(0, -1, edge, 0, lambda y: corner(corners, 1, y, rows, block))
        place(1, 0, own, 0, lambda y: beyond(y_own, 0, y, rows, block))
        copy(2, 0)

    @pl.when(jnp.logical_not(even))
    def _():
        copy(0, planes)
        place(1, planes, edge, 0, lambda y: corner(corners, 0, y, rows, block))
        place(2, planes + 1, second, 0, lambda y: corner(corners, 1, y, rows, block))

    def find_low(row):
        return (sums, diffs, 4, row) if row < 2 else (sums_m, diffs_m, inner, 0)

    def find_high(row):
        return (sums, diffs, 4, row + 1) if row else (sums_m, diffs_m, inner, inner - 1)

    layer = jnp.where(even, 1, planes + 1)
    apply_elements(find_low, stiff_ref, acc_s0, acc_d0, 2, 2, range(1, 3), layer, 1, cases)
    apply_elements(find_high, stiff_ref, acc_s1, acc_d1, 2, 2, range(2), layer, rows + 1, cases)

    def image(x, y, place):
        def total(early, near, low, high):
            def outer(v):
                value = low[v * 2 + y] if y < 2 else high[v * 2 + y - inner]
                return value + near[v * inner + y - 1] if y in (1, inner) else value

            return merged(x, planes, even, lambda w: early[w * nodes_y + y], outer)

        s = total(acc_se, acc_sm, acc_s0, acc_s1)
        d = total(acc_de, acc_dm, acc_d0, acc_d1)
        force = s - d + shift_up(s + d)
        scaled = force * inverse[x + 1, y + 1 : y + 2, :]
        place_column(w_sums, w_diffs, x * len(rim) + rim.index(y), scaled)
        inner_middle = middle_m[y - 1] if y in (1, inner) else middle[y // rows]
        value = direction_at(x, planes, even, lambda w: start[w * ys + y + 1], inner_middle)
        keep_pair(both_out, place, value, scaled, cases)
        return force

    for index, (x, y) in enumerate(columns):
        force = image(x, y, index)
        if index < own_count:
            keep_pair(right, index, inside(own, x, y, rows, block), force, cases)

    def find(row):
        if row in rim:
            return w_sums, w_diffs, len(rim), rim.index(row)
        return w_sm, w_dm, len(core), row - core[0]

    apply_elements(find, stiff_ref, acc2_s, acc2_d, planes, rows, range(nodes_y), 2, 2, cases)

    def second_force(ref, x, y, place):
        column = x * nodes_y + y
        s, d = acc2_s[column], acc2_d[column]
        force = s - d + shift_up(s + d)
        for k in range(3):
            value = force[k * cases : (k + 1) * cases]
            high = value.astype(bf16).astype(f32)
            lane = pl.ds(pl.multiple_of((place * 3 + k) * LANES, LANES), LANES)
            ref[:, lane] = jnp.concatenate([high, value - high], 0).astype(bf16)

    unrolled(
        (planes + 1) * len(core), len(core),
        lambda index: second_force(
            second_m, index // len(core), core[0] + index % len(core), index
        ),
    )
    for index, (x, y) in enumerate(columns):
        second_force(second_r, x, y, index)

    two = 2 * cases
    gram = products(right[...], both_out[:, : own_count * 3 * LANES]) + gram_m[...]
    other = products(second_m[...], both_m[...]) + products(second_r[...], both_out[...])
    row = lax.broadcasted_iota(jnp.int32, (cases, cases), 0)
    column = lax.broadcasted_iota(jnp.int32, (cases, cases), 1)
    load_load, load_image = gram[:cases, :cases], gram[cases:, :cases]
    mixed, image_image = other[:, :cases], other[:, cases:]
    table[...] = jnp.zeros(table.shape, f32)
    table[:, 0:cases] = jnp.where(row <= column, load_load, load_image)
    table[:, cases:two] = jnp.where(row <= column, mixed, image_image)
    for lane, value in ((two, load_image), (two + 1, image_image)):
        own_entries = jnp.where(row == column, value, 0.0)
        table[:, lane : lane + 1] = jnp.sum(own_entries, axis=1, keepdims=True)
    half = cases // 2
    folded = table[:half, :] + pltpu.roll(table[half:, :], LANES // 2, 1)
    depth = system_out.shape[2]
    for index in range(system_out.shape[0]):
        for part in range(half // depth):
            system_out[index, part] = folded[part * depth : (part + 1) * depth]


def solve_kernel(
    sizes, system, system_pair, both_m, both_r, codes, out, mixing, sums, diffs, energy, square, full
):
    planes, rows, cases = sizes
    two = 2 * cases
    nodes_y = rows + 1
    count = planes * rows
    total = jnp.sum(system[...], axis=0) + jnp.sum(system_pair[...], axis=0)
    half, depth = cases // 2, system.shape[2]
    square[...] = jnp.zeros(square.shape, f32)
    for part in range(half // depth):
        value = total[part]
        square[part * depth : (part + 1) * depth, :] = value
        lines = slice(half + part * depth, half + (part + 1) * depth)
        square[lines, :] = pltpu.roll(value, LANES // 2, 1)
    value, turned = square[0:cases, :], jnp.transpose(square[...])
    line = lax.broadcasted_iota(jnp.int32, (cases, cases), 0)
    place = lax.broadcasted_iota(jnp.int32, (cases, cases), 1)

    def mended(start, diagonal=None):
        kept, other = value[:, start : start + cases], turned[start : start + cases, :cases]
        if diagonal is None:
            return jnp.where(line <= place, kept, other)
        inner = jnp.where(line < place, other, value[:, diagonal : diagonal + 1])
        return jnp.where(line > place, kept, inner)

    load_image, mixed = mended(0, two), mended(cases)
    parts = ((load_image, mixed), (mixed, mended(cases, two + 1)), (mended(0), load_image))
    full[...] = jnp.zeros(full.shape, f32)
    for index, (left, right) in enumerate(parts):
        full[index * cases : (index + 1) * cases, 0:cases] = left
        full[index * cases : (index + 1) * cases, cases:two] = right
    table = full[...]
    lane = lax.broadcasted_iota(jnp.int32, (1, LANES), 1)
    gone, wide = 0, 4
    for pivot in range(0, two, wide):
        drop = pivot // 8 * 8 - gone
        table = table[drop:]
        gone += drop
        line = pivot - gone
        inner = (lane >= pivot) & (lane < pivot + wide)
        found = [table[line + p : line + p + 1, :] for p in range(wide)]
        block = [
            [jnp.broadcast_to(row[:, pivot + q : pivot + q + 1], row.shape) for q in range(wide)]
            for row in found
        ]
        solved = [
            jnp.where(lane == pivot + p, -1.0, jnp.where(inner, 0.0, found[p]))
            for p in range(wide)
        ]
        for p in range(wide):
            inverse = 1.0 / block[p][p]
            solved[p] = solved[p] * inverse
            block[p] = [value * inverse for value in block[p]]
            for q in range(wide):
                if q != p:
                    factor = block[q][p]
                    solved[q] = solved[q] - factor * solved[p]
                    for r in range(p + 1, wide):
                        block[q][r] = block[q][r] - factor * block[p][r]
        update = None
        for q in range(wide):
            term = table[:, pivot + q : pivot + q + 1] * solved[q]
            update = term if update is None else update + term
        table = jnp.where(inner, 0.0, table) - update
    answer = table[two - gone :, :two]
    high = answer.astype(bf16).astype(f32)
    mixing[...] = jnp.zeros(mixing.shape, f32)
    mixing[0:cases, 0:two] = high
    mixing[0:cases, two : 2 * two] = high
    mixing[cases:two, 0:two] = answer - high
    mix = mixing[...][:, : 2 * two].astype(bf16)

    def combined(ref, place, width):
        value = jnp.dot(
            mix, ref[:, place * 3 * LANES : (place + width) * 3 * LANES], preferred_element_type=f32
        )
        return value[:cases] + value[cases:]

    def keep(value, index, column):
        for k in range(3):
            part = value[:, (index * 3 + k) * LANES : (index * 3 + k + 1) * LANES]
            moved = shift_down(part)
            sums[column, k * cases : (k + 1) * cases, :] = part + moved
            diffs[column, k * cases : (k + 1) * cases, :] = moved - part

    core = core_rows(rows)
    for x in range(planes + 1):
        value = combined(both_m, x * len(core), len(core))
        for index, y in enumerate(core):
            keep(value, index, x * nodes_y + y)
    columns, _ = rim_columns(planes, rows)
    for start in range(0, len(columns), 6):
        some = columns[start : start + 6]
        value = combined(both_r, start, len(some))
        for index, (x, y) in enumerate(some):
            keep(value, index, x * nodes_y + y)

    find = whole(sums, diffs, nodes_y)
    tiles = cases // 8

    def step(plane, _):
        for tile in range(tiles):
            lower = x_modes(find, plane, 0, tile, cases)
            for row in range(rows):
                upper = x_modes(find, plane, row + 1, tile, cases)
                part = mode_energy(modes_of(lower, upper))
                if tile == 0:
                    energy[row] = part
                else:
                    energy[row] += part
                lower = upper
        total = jnp.sum(energy[...], axis=1)
        total = (-3.0 / cases) * jnp.abs(codes[plane]) * total
        for index in range(out.shape[0]):
            out[index, plane] = total
        return 0

    lax.fori_loop(0, planes, step, 0)


def smooth(ref, x, rows):
    weight = [2.5 - math.sqrt(q) for q in range(7)]
    near = {}
    for dx in range(-2, 3):
        for dy in range(-2, 3):
            q = dx * dx + dy * dy
            if q <= 5:
                value = ref[x + 2 + dx, 2 + dy : 2 + dy + rows, :]
                near[q] = value if q not in near else near[q] + value
    result = None
    for dz in range(3):
        part = None
        for q, value in near.items():
            if q + dz * dz <= 6:
                term = weight[q + dz * dz] * value
                part = term if part is None else part + term
        if dz == 0:
            result = part
        else:
            place = lax.broadcasted_iota(jnp.int32, part.shape, 1)
            forward = jnp.where(place >= LANES - dz, 0.0, pltpu.roll(part, LANES - dz, 1))
            backward = jnp.where(place < dz, 0.0, pltpu.roll(part, dz, 1))
            result = result + (forward + backward)
    return result


def scale_kernel(sizes, counts, levels, out, there):
    planes, rows, _ = sizes
    y = lax.broadcasted_iota(jnp.int32, (rows + 4, LANES), 0)
    y = y + (lax.axis_index("gy") * rows - 2)
    in_y = (y >= 0) & (y < counts[1] * rows)
    for x in range(planes + 4):
        global_x = lax.axis_index("gx") * planes + (x - 2)
        in_x = (global_x >= 0) & (global_x < counts[0] * planes)
        there[x] = jnp.where(in_y & in_x, 1.0, 0.0)
    for x in range(planes):
        density = 0.3 + 0.7 * levels[x].astype(f32) / (LEVELS - 1)
        out[x] = 1.0 / (density * smooth(there, x, rows))


def filter_kernel(sizes, counts, blocks, blocks_pair, scale, out, wide):
    planes, rows, _ = sizes
    sides_x = ((-1, planes - 2, planes, 0), (0, 0, planes, 2), (1, 0, 2, 2 + planes))
    sides_y = ((-1, rows - 2, rows, 0), (0, 0, rows, 2), (1, 0, 2, 2 + rows))
    for step_x, x0, x1, to_x in sides_x:
        for step_y, y0, y1, to_y in sides_y:
            at_x = lax.axis_index("gx") + step_x
            at_y = lax.axis_index("gy") + step_y
            inside = (at_x >= 0) & (at_x < counts[0]) & (at_y >= 0) & (at_y < counts[1])
            index = jnp.where(inside, at_x // 2 * counts[1] + at_y, 0)
            value = (blocks_pair if step_x else blocks)[index, x0:x1, y0:y1, :]
            wide[to_x : to_x + x1 - x0, to_y : to_y + y1 - y0, :] = jnp.where(inside, value, 0.0)
    for x in range(planes):
        out[x] = smooth(wide, x, rows) * scale[x]


def local(forces, levels, supports):
    _, cases, planes, rows, _ = forces.shape
    sizes = (planes, rows, cases)
    block = 3 * cases
    count_x, count_y = lax.axis_size("gx"), lax.axis_size("gy")

    def shape(blocks, codes):
        return jax.ShapeDtypeStruct((blocks * block + up8(codes), LANES), f32)

    density = 0.3 + 0.7 * levels.astype(f32) / (LEVELS - 1)
    codes = density * density * density
    codes = jnp.where(supports == 0, codes, -codes)
    counts = (count_x, count_y)
    own, edge = pl.pallas_call(
        functools.partial(pack_kernel, sizes),
        out_shape=[shape(planes * rows, planes * rows), shape(rows, 2 * rows)],
        in_specs=[VMEM] * 2,
        out_specs=[VMEM] * 2,
        compiler_params=PARAMS,
        name="pack",
    )(forces, codes)
    scale = pl.pallas_call(
        functools.partial(scale_kernel, sizes, counts),
        out_shape=jax.ShapeDtypeStruct((planes, rows, LANES), f32),
        in_specs=[VMEM],
        out_specs=VMEM,
        scratch_shapes=[pltpu.VMEM((planes + 4, rows + 4, LANES), f32)],
        compiler_params=PARAMS,
        name="scale",
    )(levels)

    def moved(value, axis, step):
        count = lax.axis_size(axis)
        pairs = [(i, i + step) for i in range(count) if 0 <= i + step < count]
        return lax.ppermute(value, axis, pairs)

    def links(first, step):
        return [(i, i + step) for i in range(first, count_x, 2) if 0 <= i + step < count_x]

    def swapped(value):
        return lax.ppermute(value, "gx", links(0, 1) + links(1, -1))

    def across(value):
        return lax.ppermute(value, "gx", links(1, 1) + links(2, -1))

    edge = across(edge)
    pair = swapped(own)
    own, pair = lax.optimization_barrier((own, pair))
    ym, yp = pl.pallas_call(
        functools.partial(rows_kernel, sizes),
        out_shape=[shape(2 * planes, 2 * planes), shape(planes, 2 * planes)],
        in_specs=[VMEM],
        out_specs=[VMEM] * 2,
        compiler_params=PARAMS,
        name="rows",
    )(own)
    from_yp, from_ym = moved(ym, "gy", -1), moved(yp, "gy", 1)
    second = pl.pallas_call(
        functools.partial(second_kernel, sizes),
        out_shape=shape(rows, 0),
        in_specs=[VMEM] * 2,
        out_specs=VMEM,
        compiler_params=PARAMS,
        name="second",
    )(swapped(codes), own)
    second = lax.ppermute(second, "gx", links(2, -1))
    pair_yp, pair_ym = swapped(from_yp), swapped(from_ym)
    from_ym, from_yp, edge = lax.optimization_barrier((from_ym, from_yp, edge))
    corners = across(
        pl.pallas_call(
            functools.partial(corner_kernel, sizes),
            out_shape=jax.ShapeDtypeStruct((6 * block + 16, LANES), f32),
            in_specs=[VMEM] * 2,
            out_specs=VMEM,
            compiler_params=PARAMS,
            name="corners",
        )(from_ym, from_yp)
    )

    devices = count_x * count_y
    nodes = (planes + 1) * (rows + 1)
    window = jax.ShapeDtypeStruct(((planes + 1) * (rows + 3), block, LANES), f32)
    partial_forces = jax.ShapeDtypeStruct((nodes, block, LANES), f32)
    early = pl.pallas_call(
        functools.partial(early_kernel, sizes),
        out_shape=[window] * 3 + [partial_forces] * 2,
        in_specs=[VMEM] * 6,
        out_specs=[VMEM] * 5,
        scratch_shapes=[
            pltpu.VMEM((planes + 2, up8(rows + 4), LANES), f32),
            pltpu.VMEM((planes + 1, up8(rows + 3), LANES), f32),
        ],
        compiler_params=PARAMS,
        cost_estimate=pl.CostEstimate(
            flops=200 * planes * rows * block * LANES, bytes_accessed=2**23, transcendentals=0
        ),
        name="early",
    )(own, pair, from_ym, from_yp, pair_ym, pair_yp)

    def columns(count):
        return jax.ShapeDtypeStruct((count, block, LANES), f32)

    def fields(lines, count):
        return jax.ShapeDtypeStruct((lines * cases, count * 3 * LANES), bf16)

    def scratch(value):
        return pltpu.VMEM(value.shape, value.dtype)

    core = len(core_rows(rows))
    middle = pl.pallas_call(
        functools.partial(middle_kernel, sizes),
        out_shape=[columns(3 * (rows - 1))] * 2
        + [columns(rows - 1)]
        + [columns(3 * (rows - 1))] * 2
        + [columns((planes + 1) * core)] * 2
        + [fields(4, (planes + 1) * core), jax.ShapeDtypeStruct((2 * cases, 2 * cases), f32)],
        in_specs=[VMEM] * 9,
        out_specs=[VMEM] * 9,
        scratch_shapes=[
            pltpu.VMEM((planes + 4, up8(rows), LANES), f32),
            pltpu.VMEM((planes + 3, up8(rows), LANES), f32),
            scratch(fields(4, planes * core)),
        ],
        compiler_params=PARAMS,
        name="middle",
    )(own, pair, edge, second, *early)

    rim, rim_own = rim_columns(planes, rows)
    field = scratch(columns(nodes))
    both, system = pl.pallas_call(
        functools.partial(main_kernel, sizes),
        out_shape=[
            fields(4, len(rim)),
            jax.ShapeDtypeStruct((devices // 2, cases // 8, 4, LANES), f32),
        ],
        in_specs=[VMEM] * 23,
        out_specs=[VMEM] * 2,
        scratch_shapes=[
            pltpu.VMEM((planes + 4, up8(rows + 4), LANES), f32),
            pltpu.VMEM((planes + 3, up8(rows + 3), LANES), f32),
            scratch(columns(2)),
            *[scratch(columns(12))] * 2,
            *[scratch(columns(6))] * 4,
            *[scratch(columns((planes + 1) * 4))] * 2,
            field, field,
            scratch(fields(4, rim_own)),
            scratch(fields(2, (planes + 1) * core)),
            scratch(fields(2, len(rim))),
            pltpu.VMEM((cases, LANES), f32),
        ],
        compiler_params=PARAMS,
        name="operator",
    )(
        own, pair, edge, second, from_ym, from_yp, pair_ym, pair_yp, corners,
        *early, *middle,
    )

    groups = [
        [x * count_y + y for x in range(side, count_x, 2) for y in range(count_y)]
        for side in range(2)
    ]

    def gathered(copies):
        mine = lax.all_to_all(copies, ("gx", "gy"), 0, 0, axis_index_groups=groups)
        return mine, swapped(mine)

    system = gathered(system)

    weighted = pl.pallas_call(
        functools.partial(solve_kernel, sizes),
        out_shape=jax.ShapeDtypeStruct((devices // 2, planes, rows, LANES), f32),
        in_specs=[VMEM] * 5,
        out_specs=VMEM,
        scratch_shapes=[
            pltpu.VMEM((2 * cases, LANES), f32),
            field,
            field,
            pltpu.VMEM((rows, 8, LANES), f32),
            pltpu.VMEM((LANES, LANES), f32),
            pltpu.VMEM((3 * cases, LANES), f32),
        ],
        compiler_params=PARAMS,
        name="solve",
    )(*system, middle[7], both, codes)

    blocks = gathered(weighted)
    return pl.pallas_call(
        functools.partial(filter_kernel, sizes, counts),
        out_shape=jax.ShapeDtypeStruct((planes, rows, LANES), f32),
        in_specs=[VMEM] * 3,
        out_specs=VMEM,
        scratch_shapes=[pltpu.VMEM((planes + 4, rows + 4, LANES), f32)],
        compiler_params=PARAMS,
        name="cone",
    )(*blocks, scale)


def solution(mesh):
    return jax.shard_map(
        local,
        mesh=mesh,
        in_specs=(P(None, None, "gx", "gy", None), P("gx", "gy", None), P("gx", "gy", None)),
        out_specs=P("gx", "gy", None),
        check_vma=False,
    )
```

```python
import functools
import math

import jax
import jax.numpy as jnp
from jax import lax
from jax.experimental import pallas as pl
from jax.experimental.pallas import tpu as pltpu
from jax.sharding import PartitionSpec as P

LEVELS = 16
LOAD = 0.2
LANES = 128
POISSON = 0.3
LAME = POISSON / ((1.0 + POISSON) * (1.0 - 2.0 * POISSON))
SHEAR = 1.0 / (2.0 * (1.0 + POISSON))
DIAGONAL = (LAME + 2.0 * SHEAR) / 9.0 + 2.0 * SHEAR / 9.0
VMEM = pl.BlockSpec(memory_space=pltpu.VMEM)
PARAMS = pltpu.CompilerParams(vmem_limit_bytes=30 * 2**20)
f32 = jnp.float32
bf16 = jnp.bfloat16


def up8(count):
    return -(-count // 8) * 8


def shift_down(value):
    lane = lax.broadcasted_iota(jnp.int32, value.shape, value.ndim - 1)
    rolled = pltpu.roll(value, LANES - 1, value.ndim - 1)
    return jnp.where(lane == LANES - 1, 0.0, rolled)


def shift_up(value):
    lane = lax.broadcasted_iota(jnp.int32, value.shape, value.ndim - 1)
    return jnp.where(lane == 0, 0.0, pltpu.roll(value, 1, value.ndim - 1))


def unrolled(count, factor, body):
    def turn(step, _):
        for offset in range(factor):
            body(step * factor + offset)
        return 0

    turns = count // factor
    if turns:
        lax.fori_loop(0, turns, turn, 0)
    for index in range(turns * factor, count):
        body(index)


def split(value):
    high = value.astype(bf16)
    return high, (value - high.astype(f32)).astype(bf16)


def modes_of(lower, upper):
    out = [[[[None] * 3 for _ in range(2)] for _ in range(2)] for _ in range(2)]
    for a in range(2):
        for c in range(2):
            for k in range(3):
                if a or c:
                    out[a][0][c][k] = lower[a][c][k] + upper[a][c][k]
                out[a][1][c][k] = upper[a][c][k] - lower[a][c][k]
    return out


PAIRS = (((1, 1, 0, 0), (0, 1, 1, 2)), ((1, 0, 1, 0), (0, 1, 1, 1)), ((1, 1, 0, 1), (1, 0, 1, 2)))
TRIPLE = ((0, 1, 1, 0), (1, 0, 1, 1), (1, 1, 0, 2))
SHEARS = (((0, 1, 0, 0), (1, 0, 0, 1)), ((0, 0, 1, 0), (1, 0, 0, 2)), ((0, 0, 1, 1), (0, 1, 0, 2)))
AXIAL = ((1, 0, 0, 0), (0, 1, 0, 1), (0, 0, 1, 2))


def at(modes, place):
    a, b, c, k = place
    return modes[a][b][c][k]


def mode_forces(modes, stiff):
    out = [[[[None] * 3 for _ in range(2)] for _ in range(2)] for _ in range(2)]

    def put(place, value):
        a, b, c, k = place
        out[a][b][c][k] = value

    shear = stiff * (SHEAR / 16)
    for first, second in SHEARS:
        force = shear * (at(modes, first) + at(modes, second))
        put(first, force)
        put(second, force)
    one, two, three = (at(modes, place) for place in AXIAL)
    volume = (stiff * (LAME / 16)) * (one + two + three)
    axial = stiff * (SHEAR / 8)
    for place in AXIAL:
        put(place, volume + axial * at(modes, place))
    own, cross = stiff * ((LAME + 3 * SHEAR) / 48), stiff * (LAME / 48)
    for first, second in PAIRS:
        one, two = at(modes, first), at(modes, second)
        put(first, own * one + cross * two)
        put(second, own * two + cross * one)
    twist = stiff * (SHEAR / 48)
    one, two, three = (at(modes, place) for place in TRIPLE)
    total = one + two + three
    for place in TRIPLE:
        put(place, twist * (total + at(modes, place)))
    last = stiff * ((LAME + 4 * SHEAR) / 144)
    for k in range(3):
        put((1, 1, 1, k), last * modes[1][1][1][k])
    return out


def mode_energy(modes):
    def square(value):
        return value * value

    shear = None
    for first, second in SHEARS:
        term = square(at(modes, first) + at(modes, second))
        shear = term if shear is None else shear + term
    one, two, three = (at(modes, place) for place in AXIAL)
    energy = (SHEAR / 16) * shear + (LAME / 16) * square(one + two + three)
    energy = energy + (SHEAR / 8) * (square(one) + square(two) + square(three))
    squares, products = None, None
    for first, second in PAIRS:
        one, two = at(modes, first), at(modes, second)
        term, product = square(one) + square(two), one * two
        squares = term if squares is None else squares + term
        products = product if products is None else products + product
    energy = energy + ((LAME + 3 * SHEAR) / 48) * squares + (LAME / 24) * products
    one, two, three = (at(modes, place) for place in TRIPLE)
    twist = square(one + two + three) + square(one) + square(two) + square(three)
    energy = energy + (SHEAR / 48) * twist
    last = square(modes[1][1][1][0]) + square(modes[1][1][1][1]) + square(modes[1][1][1][2])
    return energy + ((LAME + 4 * SHEAR) / 144) * last


def x_modes(find, plane, row, tile, cases):
    sums, diffs, columns, column = find(row)
    out = [[[None] * 3 for _ in range(2)] for _ in range(2)]
    for c, ref in enumerate((sums, diffs)):
        for k in range(3):
            rows = pl.ds(pl.multiple_of(k * cases + tile * 8, 8), 8)
            one = ref[plane * columns + column, rows, :]
            two = ref[(plane + 1) * columns + column, rows, :]
            out[0][c][k] = one + two
            out[1][c][k] = two - one
    return out


def whole(sums, diffs, columns):
    return lambda row: (sums, diffs, columns, row)


def apply_elements(find, stiff_ref, acc_s, acc_d, planes, rows, kept, stiff_x, stiff_y, cases):
    columns = len(kept)
    tiles = cases // 8
    for column in range(columns):
        acc_s[column] = jnp.zeros(acc_s.shape[1:], f32)
        acc_d[column] = jnp.zeros(acc_d.shape[1:], f32)

    def step(index, _):
        plane, tile = index // tiles, index % tiles

        def emit(row, total):
            if row not in kept:
                return
            for c, acc in enumerate((acc_s, acc_d)):
                for k in range(3):
                    lines = pl.ds(pl.multiple_of(k * cases + tile * 8, 8), 8)
                    low = plane * columns + row - kept[0]
                    acc[low, lines, :] += total[0][c][k] - total[1][c][k]
                    acc[low + columns, lines, :] = total[0][c][k] + total[1][c][k]

        lower = x_modes(find, plane, 0, tile, cases)
        carry = None
        for row in range(rows):
            upper = x_modes(find, plane, row + 1, tile, cases)
            stiff = jnp.broadcast_to(
                stiff_ref[plane + stiff_x, pl.ds(row + stiff_y, 1), :], (8, LANES)
            )
            forces = mode_forces(modes_of(lower, upper), stiff)
            here = [[[None] * 3 for _ in range(2)] for _ in range(2)]
            following = [[[None] * 3 for _ in range(2)] for _ in range(2)]
            for a in range(2):
                for c in range(2):
                    for k in range(3):
                        one, two = forces[a][0][c][k], forces[a][1][c][k]
                        low = -two if one is None else one - two
                        high = two if one is None else one + two
                        here[a][c][k] = low if carry is None else carry[a][c][k] + low
                        following[a][c][k] = high
            emit(row, here)
            carry, lower = following, upper
        emit(rows, carry)
        return 0

    lax.fori_loop(0, planes * tiles, step, 0)


def fill(source, base, sizes, ref, xs, ys, code_xs, code_ys):
    planes, rows, cases = sizes
    block = 3 * cases
    line = 0
    for x in xs:
        start = (x * rows + ys[0]) * block
        count = len(ys) * block
        ref[line : line + count, :] = source[start : start + count, :]
        line += count
    for x in code_xs:
        start = base + x * rows + code_ys[0]
        ref[line : line + len(code_ys), :] = source[start : start + len(code_ys), :]
        line += len(code_ys)
    if line < ref.shape[0]:
        ref[line:, :] = jnp.zeros((ref.shape[0] - line, LANES), f32)


def pack_kernel(sizes, forces, codes, own, edge):
    planes, rows, cases = sizes
    block = 3 * cases
    base = planes * rows * block
    for x in range(planes):
        own[base + x * rows : base + (x + 1) * rows, :] = codes[x]
        scale = jnp.where(codes[x] > 0.0, LOAD, 0.0)
        for k in range(3):
            for c in range(cases):
                start = x * rows * block + k * cases + c
                own[pl.ds(start, rows, stride=block), :] = forces[k, c, x] * scale

    even = lax.axis_index("gx") % 2 == 0
    size = rows * block
    for line in range(0, size, block):
        high = lines(own, (planes - 1) * size + line, block)
        edge[line : line + block, :] = jnp.where(even, lines(own, line, block), high)
    high = lines(own, base + (planes - 2) * rows, 2 * rows)
    edge[size:, :] = jnp.where(even, lines(own, base, 2 * rows), high)


def second_kernel(sizes, begun, own, second):
    _, rows, cases = sizes
    size = rows * 3 * cases
    second[...] = lines(own, size, size)


def rows_kernel(sizes, own, ym, yp):
    planes, rows, cases = sizes
    base = planes * rows * 3 * cases
    every_x = range(planes)
    fill(own, base, sizes, ym, every_x, (0, 1), every_x, (0, 1))
    fill(own, base, sizes, yp, every_x, (rows - 1,), every_x, (rows - 2, rows - 1))


def corner_kernel(sizes, ym, yp, out):
    planes, rows, cases = sizes
    block = 3 * cases
    even = lax.axis_index("gx") % 2 == 0
    line = 0
    for source, width in ((ym, 1), (yp, 2)):
        size = width * block
        parts = [(at, (planes - 2) * size + at, block) for at in range(0, 2 * size, block)]
        parts.append((planes * size, planes * size + (planes - 2) * 2, 4))
        for low, high, count in parts:
            value = lines(source, low, count)
            if low != high:
                value = jnp.where(even, value, lines(source, high, count))
            out[line : line + count, :] = value
            line += count
        out[line : line + 4, :] = jnp.zeros((4, LANES), f32)
        line += 4


def lines(ref, start, count):
    return ref[start : start + count, :]


def inside(ref, x, y, rows, block):
    return lines(ref, (x * rows + y) * block, block)


def beyond(refs, slot, y, rows, block):
    below, above = refs
    if y < 0:
        return lines(below, slot * block, block)
    return lines(above, (slot * 2 + y - rows) * block, block)


def beyond_codes(refs, slots, slot, y, block):
    below, above = refs
    if y < 0:
        return lines(below, slots * block + slot * 2, 2)
    return lines(above, slots * 2 * block + slot * 2, 2)


def corner(ref, slot, y, rows, block):
    start = slot * block if y < 0 else 2 * block + 8 + (slot * 2 + y - rows) * block
    return lines(ref, start, block)


def corner_codes(ref, slot, y, block):
    return lines(ref, (2 * block if y < 0 else 6 * block + 8) + slot * 2, 2)


def node_inverse(signed, count, out):
    planes = signed.shape[0]
    for x in range(1, planes):
        codes = signed[x, 0 : count + 1, :]
        total = jnp.abs(signed[x - 1, 0 : count + 1, :]) + jnp.abs(codes)
        total = total[:-1] + total[1:]
        total = total + shift_up(total)
        free = codes[1:] > 0.0
        value = 1.0 / (DIAGONAL * jnp.where(free, total, 1.0))
        out[x - 1, 0:count, :] = jnp.where(free, value, 0.0)
    for x in range(planes):
        signed[x] = jnp.abs(signed[x])


def place_column(sums, diffs, column, value):
    moved = shift_down(value)
    sums[column] = value + moved
    diffs[column] = moved - value


def early_kernel(
    sizes, own, pair, ym, yp, ym_pair, yp_pair, start, sums, diffs, acc_s, acc_d,
    stiff_ref, inverse,
):
    planes, rows, cases = sizes
    block = 3 * cases
    ys = rows + 3
    even = lax.axis_index("gx") % 2 == 0
    y_own, y_pair = (ym, yp), (ym_pair, yp_pair)

    def both_ways(w, read):
        low = read(True, w + 1) if w + 1 < planes else read(False, w + 1 - planes)
        high = read(False, planes + w - 1) if w < 1 else read(True, w - 1)
        return jnp.where(even, low, high)

    def codes(w, y):
        def read(mine, x):
            if y == 0:
                return lines(own if mine else pair, (planes * block + x) * rows, rows)
            return beyond_codes(y_own if mine else y_pair, planes, x, y, block)

        return both_ways(w, read)

    for w in range(-1, planes + 1):
        for y, count in ((-2, 2), (0, rows), (rows, 2)):
            stiff_ref[w + 1, y + 2 : y + 2 + count, :] = codes(w, y)
    node_inverse(stiff_ref, ys, inverse)
    for w in range(planes + 1):
        for y in range(-1, rows + 2):

            def read(mine, x):
                if 0 <= y < rows:
                    return inside(own if mine else pair, x, y, rows, block)
                return beyond(y_own if mine else y_pair, x, y, rows, block)

            value = both_ways(w, read) * inverse[w, y + 1 : y + 2, :]
            column = w * ys + y + 1
            start[column] = value
            place_column(sums, diffs, column, value)
    kept = range(1, rows + 2)
    find = whole(sums, diffs, ys)
    apply_elements(find, stiff_ref, acc_s, acc_d, planes, rows + 2, kept, 1, 1, cases)


def core_rows(rows):
    return range(2, rows - 1)


def rim_rows(rows):
    return (0, 1, rows - 1, rows)


def rim_columns(planes, rows):
    own = [(x, y) for x in range(planes) for y in rim_rows(rows) if y < rows]
    beyond_own = [(x, rows) for x in range(planes)] + [(planes, y) for y in rim_rows(rows)]
    return own + beyond_own, len(own)


def merged(x, planes, even, early, near):
    low = ([x - 1] if x >= 1 else [], [x + 1] if x <= 1 else [])
    high = ([x + 1] if x < planes else [], [x - planes + 1] if x >= planes - 1 else [])
    if low[0] and low[1] and high[0] and high[1]:
        one = early(jnp.where(even, low[0][0], high[0][0]))
        return one + near(jnp.where(even, low[1][0], high[1][0]))

    def read(places):
        found = [early(w) for w in places[0]] + [near(v) for v in places[1]]
        return found[0] if len(found) == 1 else found[0] + found[1]

    return jnp.where(even, read(low), read(high))


def direction_at(x, planes, even, early, middle):
    if x == 0:
        return jnp.where(even, middle, early(1))
    if x == planes:
        return jnp.where(even, early(planes - 1), middle)
    return early(jnp.where(even, x - 1, x + 1))


def keep_pair(ref, place, one, two, cases):
    for k in range(3):
        part = slice(k * cases, (k + 1) * cases)
        high, rest = split(jnp.concatenate([one[part], two[part]], 0))
        lane = pl.ds(pl.multiple_of((place * 3 + k) * LANES, LANES), LANES)
        ref[0 : 2 * cases, lane] = high
        ref[2 * cases : 4 * cases, lane] = rest


def products(first, second):
    contract = (((1,), (1,)), ((), ()))
    out = lax.dot_general(first, second, contract, preferred_element_type=f32)
    left, right = out.shape[0] // 2, out.shape[1] // 2
    out = out[:, :right] + out[:, right:]
    return out[:left] + out[left:]


def middle_kernel(
    sizes, own, pair, edge, second, start, sums_e, diffs_e, acc_se, acc_de,
    sums, diffs, middle, acc_s, acc_d, w_sums, w_diffs, both_out, gram_out, acc2_s, acc2_d,
    stiff_ref, inverse, right,
):
    planes, rows, cases = sizes
    block = 3 * cases
    ys, nodes_y, inner = rows + 3, rows + 1, rows - 1
    core = core_rows(rows)
    even = lax.axis_index("gx") % 2 == 0

    def codes(x):
        if 0 <= x < planes:
            return lines(own, (planes * block + x) * rows, rows)
        slot = x + 2 if x < 0 else x - planes
        outer = lines(edge, (block + slot) * rows, rows)
        if x < 0:
            return jnp.where(even, outer, lines(pair, (planes * block + planes + x) * rows, rows))
        return jnp.where(even, lines(pair, (planes * block + slot) * rows, rows), outer)

    for x in range(-2, planes + 2):
        stiff_ref[x + 2, 0:rows, :] = codes(x)
    node_inverse(stiff_ref, inner, inverse)

    def place(v, x, ref, slot):
        for y in range(1, rows):
            value = inside(ref, slot, y, rows, block) * inverse[x + 1, y - 1 : y, :]
            if v == 1:
                middle[y - 1] = value
            place_column(sums, diffs, v * inner + y - 1, value)

    def copy(v, w):
        for y in range(1, rows):
            sums[v * inner + y - 1] = sums_e[w * ys + y + 1]
            diffs[v * inner + y - 1] = diffs_e[w * ys + y + 1]

    @pl.when(even)
    def _():
        place(0, -1, edge, 0)
        place(1, 0, own, 0)
        copy(2, 0)

    @pl.when(jnp.logical_not(even))
    def _():
        copy(0, planes)
        place(1, planes, edge, 0)
        place(2, planes + 1, second, 0)

    layer = jnp.where(even, 1, planes + 1)
    find = whole(sums, diffs, inner)
    apply_elements(find, stiff_ref, acc_s, acc_d, 2, rows - 2, range(inner), layer, 1, cases)

    def image(x, y, place):
        def total(early, near):
            return merged(
                x, planes, even, lambda w: early[w * nodes_y + y],
                lambda v: near[v * inner + y - 1],
            )

        s, d = total(acc_se, acc_s), total(acc_de, acc_d)
        force = s - d + shift_up(s + d)
        scaled = force * inverse[x + 1, pl.ds(y - 1, 1), :]
        place_column(w_sums, w_diffs, place, scaled)
        value = direction_at(x, planes, even, lambda w: start[w * ys + y + 1], middle[y - 1])
        keep_pair(both_out, place, value, scaled, cases)
        return force

    def within(x, index):
        y, place = core[0] + index, x * len(core) + index
        force = image(x, y, place)
        given = own[pl.ds(pl.multiple_of((x * rows + y) * block, 8), block), :]
        keep_pair(right, place, given, force, cases)

    for x in range(planes):
        unrolled(len(core), len(core), functools.partial(within, x))
    last = planes * len(core)
    unrolled(len(core), len(core), lambda index: image(planes, core[0] + index, last + index))
    gram_out[...] = products(right[...], both_out[:, : last * 3 * LANES])

    find = whole(w_sums, w_diffs, len(core))
    kept = range(len(core))
    apply_elements(
        find, stiff_ref, acc2_s, acc2_d, planes, len(core) - 1, kept, 2, core[0], cases
    )


def main_kernel(
    sizes, own, pair, edge, second, ym, yp, ym_pair, yp_pair, corners,
    start, sums_e, diffs_e, acc_se, acc_de,
    sums_m, diffs_m, middle_m, acc_sm, acc_dm, w_sm, w_dm, both_m, gram_m,
    acc2_sm, acc2_dm, both_out, system_out, stiff_ref, inverse,
    middle, sums, diffs, acc_s0, acc_d0, acc_s1, acc_d1, w_sums, w_diffs,
    acc2_s0, acc2_d0, acc2_s1, acc2_d1, right, second_m, second_r, table,
):
    planes, rows, cases = sizes
    block = 3 * cases
    ys, nodes_y, inner = rows + 3, rows + 1, rows - 1
    core, rim = core_rows(rows), rim_rows(rows)
    columns, own_count = rim_columns(planes, rows)
    even = lax.axis_index("gx") % 2 == 0
    y_own, y_pair = (ym, yp), (ym_pair, yp_pair)

    def codes(x, y):
        def read(mine, plane):
            if y == 0:
                return lines(own if mine else pair, (planes * block + plane) * rows, rows)
            return beyond_codes(y_own if mine else y_pair, planes, plane, y, block)

        if 0 <= x < planes:
            return read(True, x)
        slot = x + 2 if x < 0 else x - planes
        if y == 0:
            outer = lines(edge, (block + slot) * rows, rows)
        else:
            outer = corner_codes(corners, slot, y, block)
        within = read(False, planes + x if x < 0 else x - planes)
        return jnp.where(even, outer, within) if x < 0 else jnp.where(even, within, outer)

    for x in range(-2, planes + 2):
        for y, count in ((-2, 2), (0, rows), (rows, 2)):
            stiff_ref[x + 2, y + 2 : y + 2 + count, :] = codes(x, y)
    node_inverse(stiff_ref, ys, inverse)

    sides = (-1, 0, rows, rows + 1)

    def place(v, x, ref, slot, beyond_at):
        for i, y in enumerate(sides):
            value = inside(ref, slot, y, rows, block) if y == 0 else beyond_at(y)
            value = value * inverse[x + 1, y + 1 : y + 2, :]
            if v == 1 and y in (0, rows):
                middle[y // rows] = value
            place_column(sums, diffs, v * 4 + i, value)

    def copy(v, w):
        for i, y in enumerate(sides):
            sums[v * 4 + i] = sums_e[w * ys + y + 1]
            diffs[v * 4 + i] = diffs_e[w * ys + y + 1]

    @pl.when(even)
    def _():
        place(0, -1, edge, 0, lambda y: corner(corners, 1, y, rows, block))
        place(1, 0, own, 0, lambda y: beyond(y_own, 0, y, rows, block))
        copy(2, 0)

    @pl.when(jnp.logical_not(even))
    def _():
        copy(0, planes)
        place(1, planes, edge, 0, lambda y: corner(corners, 0, y, rows, block))
        place(2, planes + 1, second, 0, lambda y: corner(corners, 1, y, rows, block))

    def find_low(row):
        return (sums, diffs, 4, row) if row < 2 else (sums_m, diffs_m, inner, 0)

    def find_high(row):
        return (sums, diffs, 4, row + 1) if row else (sums_m, diffs_m, inner, inner - 1)

    layer = jnp.where(even, 1, planes + 1)
    apply_elements(find_low, stiff_ref, acc_s0, acc_d0, 2, 2, range(1, 3), layer, 1, cases)
    apply_elements(find_high, stiff_ref, acc_s1, acc_d1, 2, 2, range(2), layer, rows + 1, cases)

    def image(x, y, place):
        def total(early, near, low, high):
            def outer(v):
                value = low[v * 2 + y] if y < 2 else high[v * 2 + y - inner]
                return value + near[v * inner + y - 1] if y in (1, inner) else value

            return merged(x, planes, even, lambda w: early[w * nodes_y + y], outer)

        s = total(acc_se, acc_sm, acc_s0, acc_s1)
        d = total(acc_de, acc_dm, acc_d0, acc_d1)
        force = s - d + shift_up(s + d)
        scaled = force * inverse[x + 1, y + 1 : y + 2, :]
        place_column(w_sums, w_diffs, x * len(rim) + rim.index(y), scaled)
        inner_middle = middle_m[y - 1] if y in (1, inner) else middle[y // rows]
        value = direction_at(x, planes, even, lambda w: start[w * ys + y + 1], inner_middle)
        keep_pair(both_out, place, value, scaled, cases)
        return force

    for index, (x, y) in enumerate(columns):
        force = image(x, y, index)
        if index < own_count:
            keep_pair(right, index, inside(own, x, y, rows, block), force, cases)

    def find(row):
        if row in rim:
            return w_sums, w_diffs, len(rim), rim.index(row)
        return w_sm, w_dm, len(core), row - core[0]

    def find_last(row):
        return find(row + rows - 2)

    low, high = (acc2_s0, acc2_d0), (acc2_s1, acc2_d1)
    apply_elements(find, stiff_ref, *low, planes, 2, range(3), 2, 2, cases)
    apply_elements(find_last, stiff_ref, *high, planes, 2, range(3), 2, rows, cases)

    def second_force(ref, x, y, place):
        s, d = None, None
        for parts, width, first in (
            (low, 3, 0), ((acc2_sm, acc2_dm), len(core), core[0]), (high, 3, rows - 2)
        ):
            if first <= y < first + width:
                column = x * width + y - first
                more = parts[0][column], parts[1][column]
                s, d = more if s is None else (s + more[0], d + more[1])
        force = s - d + shift_up(s + d)
        for k in range(3):
            value = force[k * cases : (k + 1) * cases]
            top = value.astype(bf16).astype(f32)
            lane = pl.ds(pl.multiple_of((place * 3 + k) * LANES, LANES), LANES)
            ref[:, lane] = jnp.concatenate([top, value - top], 0).astype(bf16)

    for x in range(planes + 1):
        for index, y in enumerate(core):
            second_force(second_m, x, y, x * len(core) + index)
    for index, (x, y) in enumerate(columns):
        second_force(second_r, x, y, index)

    two = 2 * cases
    gram = products(right[...], both_out[:, : own_count * 3 * LANES]) + gram_m[...]
    other = products(second_m[...], both_m[...]) + products(second_r[...], both_out[...])
    row = lax.broadcasted_iota(jnp.int32, (cases, cases), 0)
    column = lax.broadcasted_iota(jnp.int32, (cases, cases), 1)
    load_load, load_image = gram[:cases, :cases], gram[cases:, :cases]
    mixed, image_image = other[:, :cases], other[:, cases:]
    table[...] = jnp.zeros(table.shape, f32)
    table[:, 0:cases] = jnp.where(row <= column, load_load, load_image)
    table[:, cases:two] = jnp.where(row <= column, mixed, image_image)
    for lane, value in ((two, load_image), (two + 1, image_image)):
        own_entries = jnp.where(row == column, value, 0.0)
        table[:, lane : lane + 1] = jnp.sum(own_entries, axis=1, keepdims=True)
    half = cases // 2
    folded = table[:half, :] + pltpu.roll(table[half:, :], LANES // 2, 1)
    depth = system_out.shape[2]
    for index in range(system_out.shape[0]):
        for part in range(half // depth):
            system_out[index, part] = folded[part * depth : (part + 1) * depth]


def solve_kernel(
    sizes, system, both_m, both_r, codes, out, mixing, sums, diffs, energy, square, full
):
    planes, rows, cases = sizes
    two = 2 * cases
    nodes_y = rows + 1
    count = planes * rows
    total = jnp.sum(system[...], axis=0)
    half, depth = cases // 2, system.shape[2]
    square[...] = jnp.zeros(square.shape, f32)
    for part in range(half // depth):
        value = total[part]
        square[part * depth : (part + 1) * depth, :] = value
        lines = slice(half + part * depth, half + (part + 1) * depth)
        square[lines, :] = pltpu.roll(value, LANES // 2, 1)
    value, turned = square[0:cases, :], jnp.transpose(square[...])
    line = lax.broadcasted_iota(jnp.int32, (cases, cases), 0)
    place = lax.broadcasted_iota(jnp.int32, (cases, cases), 1)

    def mended(start, diagonal=None):
        kept, other = value[:, start : start + cases], turned[start : start + cases, :cases]
        if diagonal is None:
            return jnp.where(line <= place, kept, other)
        inner = jnp.where(line < place, other, value[:, diagonal : diagonal + 1])
        return jnp.where(line > place, kept, inner)

    load_image, mixed = mended(0, two), mended(cases)
    parts = ((load_image, mixed), (mixed, mended(cases, two + 1)), (mended(0), load_image))
    full[...] = jnp.zeros(full.shape, f32)
    for index, (left, right) in enumerate(parts):
        full[index * cases : (index + 1) * cases, 0:cases] = left
        full[index * cases : (index + 1) * cases, cases:two] = right
    table = full[...]
    lane = lax.broadcasted_iota(jnp.int32, (1, LANES), 1)
    gone, wide = 0, 8
    for pivot in range(0, two, wide):
        drop = pivot // 8 * 8 - gone
        table = table[drop:]
        gone += drop
        line = pivot - gone
        inner = (lane >= pivot) & (lane < pivot + wide)
        found = [table[line + p : line + p + 1, :] for p in range(wide)]
        block = [
            [jnp.broadcast_to(row[:, pivot + q : pivot + q + 1], row.shape) for q in range(wide)]
            for row in found
        ]
        solved = [
            jnp.where(lane == pivot + p, -1.0, jnp.where(inner, 0.0, found[p]))
            for p in range(wide)
        ]
        for p in range(wide):
            inverse = 1.0 / block[p][p]
            solved[p] = solved[p] * inverse
            block[p] = [value * inverse for value in block[p]]
            for q in range(wide):
                if q != p:
                    factor = block[q][p]
                    solved[q] = solved[q] - factor * solved[p]
                    for r in range(p + 1, wide):
                        block[q][r] = block[q][r] - factor * block[p][r]
        update = None
        for q in range(wide):
            term = table[:, pivot + q : pivot + q + 1] * solved[q]
            update = term if update is None else update + term
        table = jnp.where(inner, 0.0, table) - update
    answer = table[two - gone :, :two]
    high = answer.astype(bf16).astype(f32)
    mixing[...] = jnp.zeros(mixing.shape, f32)
    mixing[0:cases, 0:two] = high
    mixing[0:cases, two : 2 * two] = high
    mixing[cases:two, 0:two] = answer - high
    mix = mixing[...][:, : 2 * two].astype(bf16)

    def combined(ref, place, width):
        value = jnp.dot(
            mix, ref[:, place * 3 * LANES : (place + width) * 3 * LANES], preferred_element_type=f32
        )
        return value[:cases] + value[cases:]

    def keep(value, index, column):
        for k in range(3):
            part = value[:, (index * 3 + k) * LANES : (index * 3 + k + 1) * LANES]
            moved = shift_down(part)
            sums[column, k * cases : (k + 1) * cases, :] = part + moved
            diffs[column, k * cases : (k + 1) * cases, :] = moved - part

    core = core_rows(rows)
    for x in range(planes + 1):
        value = combined(both_m, x * len(core), len(core))
        for index, y in enumerate(core):
            keep(value, index, x * nodes_y + y)
    columns, _ = rim_columns(planes, rows)
    for start in range(0, len(columns), 6):
        some = columns[start : start + 6]
        value = combined(both_r, start, len(some))
        for index, (x, y) in enumerate(some):
            keep(value, index, x * nodes_y + y)

    find = whole(sums, diffs, nodes_y)
    tiles = cases // 8

    def step(plane, _):
        for tile in range(tiles):
            lower = x_modes(find, plane, 0, tile, cases)
            for row in range(rows):
                upper = x_modes(find, plane, row + 1, tile, cases)
                part = mode_energy(modes_of(lower, upper))
                if tile == 0:
                    energy[row] = part
                else:
                    energy[row] += part
                lower = upper
        total = jnp.sum(energy[...], axis=1)
        total = (-3.0 / cases) * jnp.abs(codes[plane]) * total
        for index in range(out.shape[0]):
            out[index, plane] = total
        return 0

    lax.fori_loop(0, planes, step, 0)


def smooth(ref, x, rows):
    weight = [2.5 - math.sqrt(q) for q in range(7)]
    near = {}
    for dx in range(-2, 3):
        for dy in range(-2, 3):
            q = dx * dx + dy * dy
            if q <= 5:
                value = ref[x + 2 + dx, 2 + dy : 2 + dy + rows, :]
                near[q] = value if q not in near else near[q] + value
    result = None
    for dz in range(3):
        part = None
        for q, value in near.items():
            if q + dz * dz <= 6:
                term = weight[q + dz * dz] * value
                part = term if part is None else part + term
        if dz == 0:
            result = part
        else:
            place = lax.broadcasted_iota(jnp.int32, part.shape, 1)
            forward = jnp.where(place >= LANES - dz, 0.0, pltpu.roll(part, LANES - dz, 1))
            backward = jnp.where(place < dz, 0.0, pltpu.roll(part, dz, 1))
            result = result + (forward + backward)
    return result


def scale_kernel(sizes, counts, levels, out, there):
    planes, rows, _ = sizes
    y = lax.broadcasted_iota(jnp.int32, (rows + 4, LANES), 0)
    y = y + (lax.axis_index("gy") * rows - 2)
    in_y = (y >= 0) & (y < counts[1] * rows)
    for x in range(planes + 4):
        global_x = lax.axis_index("gx") * planes + (x - 2)
        in_x = (global_x >= 0) & (global_x < counts[0] * planes)
        there[x] = jnp.where(in_y & in_x, 1.0, 0.0)
    for x in range(planes):
        density = 0.3 + 0.7 * levels[x].astype(f32) / (LEVELS - 1)
        out[x] = 1.0 / (density * smooth(there, x, rows))


def filter_kernel(sizes, counts, blocks, blocks_pair, scale, out, wide):
    planes, rows, _ = sizes
    sides_x = ((-1, planes - 2, planes, 0), (0, 0, planes, 2), (1, 0, 2, 2 + planes))
    sides_y = ((-1, rows - 2, rows, 0), (0, 0, rows, 2), (1, 0, 2, 2 + rows))
    for step_x, x0, x1, to_x in sides_x:
        for step_y, y0, y1, to_y in sides_y:
            at_x = lax.axis_index("gx") + step_x
            at_y = lax.axis_index("gy") + step_y
            inside = (at_x >= 0) & (at_x < counts[0]) & (at_y >= 0) & (at_y < counts[1])
            index = jnp.where(inside, at_x // 2 * counts[1] + at_y, 0)
            value = (blocks_pair if step_x else blocks)[index, x0:x1, y0:y1, :]
            wide[to_x : to_x + x1 - x0, to_y : to_y + y1 - y0, :] = jnp.where(inside, value, 0.0)
    for x in range(planes):
        out[x] = smooth(wide, x, rows) * scale[x]


def local(forces, levels, supports):
    _, cases, planes, rows, _ = forces.shape
    sizes = (planes, rows, cases)
    block = 3 * cases
    count_x, count_y = lax.axis_size("gx"), lax.axis_size("gy")

    def shape(blocks, codes):
        return jax.ShapeDtypeStruct((blocks * block + up8(codes), LANES), f32)

    density = 0.3 + 0.7 * levels.astype(f32) / (LEVELS - 1)
    codes = density * density * density
    codes = jnp.where(supports == 0, codes, -codes)
    counts = (count_x, count_y)
    own, edge = pl.pallas_call(
        functools.partial(pack_kernel, sizes),
        out_shape=[shape(planes * rows, planes * rows), shape(rows, 2 * rows)],
        in_specs=[VMEM] * 2,
        out_specs=[VMEM] * 2,
        compiler_params=PARAMS,
        name="pack",
    )(forces, codes)
    scale = pl.pallas_call(
        functools.partial(scale_kernel, sizes, counts),
        out_shape=jax.ShapeDtypeStruct((planes, rows, LANES), f32),
        in_specs=[VMEM],
        out_specs=VMEM,
        scratch_shapes=[pltpu.VMEM((planes + 4, rows + 4, LANES), f32)],
        compiler_params=PARAMS,
        name="scale",
    )(levels)

    def moved(value, axis, step):
        count = lax.axis_size(axis)
        pairs = [(i, i + step) for i in range(count) if 0 <= i + step < count]
        return lax.ppermute(value, axis, pairs)

    def links(first, step):
        return [(i, i + step) for i in range(first, count_x, 2) if 0 <= i + step < count_x]

    def swapped(value):
        return lax.ppermute(value, "gx", links(0, 1) + links(1, -1))

    def across(value):
        return lax.ppermute(value, "gx", links(1, 1) + links(2, -1))

    edge = across(edge)
    pair = swapped(own)
    own, pair = lax.optimization_barrier((own, pair))
    ym, yp = pl.pallas_call(
        functools.partial(rows_kernel, sizes),
        out_shape=[shape(2 * planes, 2 * planes), shape(planes, 2 * planes)],
        in_specs=[VMEM],
        out_specs=[VMEM] * 2,
        compiler_params=PARAMS,
        name="rows",
    )(own)
    from_yp, from_ym = moved(ym, "gy", -1), moved(yp, "gy", 1)
    second = pl.pallas_call(
        functools.partial(second_kernel, sizes),
        out_shape=shape(rows, 0),
        in_specs=[VMEM] * 2,
        out_specs=VMEM,
        compiler_params=PARAMS,
        name="second",
    )(swapped(codes), own)
    second = lax.ppermute(second, "gx", links(2, -1))
    pair_yp, pair_ym = swapped(from_yp), swapped(from_ym)
    from_ym, from_yp, edge = lax.optimization_barrier((from_ym, from_yp, edge))
    corners = across(
        pl.pallas_call(
            functools.partial(corner_kernel, sizes),
            out_shape=jax.ShapeDtypeStruct((6 * block + 16, LANES), f32),
            in_specs=[VMEM] * 2,
            out_specs=VMEM,
            compiler_params=PARAMS,
            name="corners",
        )(from_ym, from_yp)
    )

    devices = count_x * count_y
    nodes = (planes + 1) * (rows + 1)
    window = jax.ShapeDtypeStruct(((planes + 1) * (rows + 3), block, LANES), f32)
    partial_forces = jax.ShapeDtypeStruct((nodes, block, LANES), f32)
    early = pl.pallas_call(
        functools.partial(early_kernel, sizes),
        out_shape=[window] * 3 + [partial_forces] * 2,
        in_specs=[VMEM] * 6,
        out_specs=[VMEM] * 5,
        scratch_shapes=[
            pltpu.VMEM((planes + 2, up8(rows + 4), LANES), f32),
            pltpu.VMEM((planes + 1, up8(rows + 3), LANES), f32),
        ],
        compiler_params=PARAMS,
        cost_estimate=pl.CostEstimate(
            flops=200 * planes * rows * block * LANES, bytes_accessed=2**23, transcendentals=0
        ),
        name="early",
    )(own, pair, from_ym, from_yp, pair_ym, pair_yp)

    def columns(count):
        return jax.ShapeDtypeStruct((count, block, LANES), f32)

    def fields(lines, count):
        return jax.ShapeDtypeStruct((lines * cases, count * 3 * LANES), bf16)

    def scratch(value):
        return pltpu.VMEM(value.shape, value.dtype)

    core = len(core_rows(rows))
    middle = pl.pallas_call(
        functools.partial(middle_kernel, sizes),
        out_shape=[columns(3 * (rows - 1))] * 2
        + [columns(rows - 1)]
        + [columns(3 * (rows - 1))] * 2
        + [columns((planes + 1) * core)] * 2
        + [fields(4, (planes + 1) * core), jax.ShapeDtypeStruct((2 * cases, 2 * cases), f32)]
        + [columns((planes + 1) * core)] * 2,
        in_specs=[VMEM] * 9,
        out_specs=[VMEM] * 11,
        scratch_shapes=[
            pltpu.VMEM((planes + 4, up8(rows), LANES), f32),
            pltpu.VMEM((planes + 3, up8(rows), LANES), f32),
            scratch(fields(4, planes * core)),
        ],
        compiler_params=PARAMS,
        name="middle",
    )(own, pair, edge, second, *early)

    rim, rim_own = rim_columns(planes, rows)
    both, system = pl.pallas_call(
        functools.partial(main_kernel, sizes),
        out_shape=[
            fields(4, len(rim)),
            jax.ShapeDtypeStruct((devices, cases // 8, 4, LANES), f32),
        ],
        in_specs=[VMEM] * 25,
        out_specs=[VMEM] * 2,
        scratch_shapes=[
            pltpu.VMEM((planes + 4, up8(rows + 4), LANES), f32),
            pltpu.VMEM((planes + 3, up8(rows + 3), LANES), f32),
            scratch(columns(2)),
            *[scratch(columns(12))] * 2,
            *[scratch(columns(6))] * 4,
            *[scratch(columns((planes + 1) * 4))] * 2,
            *[scratch(columns((planes + 1) * 3))] * 4,
            scratch(fields(4, rim_own)),
            scratch(fields(2, (planes + 1) * core)),
            scratch(fields(2, len(rim))),
            pltpu.VMEM((cases, LANES), f32),
        ],
        compiler_params=PARAMS,
        name="operator",
    )(
        own, pair, edge, second, from_ym, from_yp, pair_ym, pair_yp, corners,
        *early, *middle,
    )

    groups = [
        [x * count_y + y for x in range(side, count_x, 2) for y in range(count_y)]
        for side in range(2)
    ]

    def gathered(copies):
        mine = lax.all_to_all(copies, ("gx", "gy"), 0, 0, axis_index_groups=groups)
        return mine, swapped(mine)

    system = lax.all_to_all(system, ("gx", "gy"), 0, 0)

    weighted = pl.pallas_call(
        functools.partial(solve_kernel, sizes),
        out_shape=jax.ShapeDtypeStruct((devices // 2, planes, rows, LANES), f32),
        in_specs=[VMEM] * 4,
        out_specs=VMEM,
        scratch_shapes=[
            pltpu.VMEM((2 * cases, LANES), f32),
            scratch(columns(nodes)),
            scratch(columns(nodes)),
            pltpu.VMEM((rows, 8, LANES), f32),
            pltpu.VMEM((LANES, LANES), f32),
            pltpu.VMEM((3 * cases, LANES), f32),
        ],
        compiler_params=PARAMS,
        name="solve",
    )(system, middle[7], both, codes)

    blocks = gathered(weighted)
    return pl.pallas_call(
        functools.partial(filter_kernel, sizes, counts),
        out_shape=jax.ShapeDtypeStruct((planes, rows, LANES), f32),
        in_specs=[VMEM] * 3,
        out_specs=VMEM,
        scratch_shapes=[pltpu.VMEM((planes + 4, rows + 4, LANES), f32)],
        compiler_params=PARAMS,
        name="cone",
    )(*blocks, scale)


def solution(mesh):
    return jax.shard_map(
        local,
        mesh=mesh,
        in_specs=(P(None, None, "gx", "gy", None), P("gx", "gy", None), P("gx", "gy", None)),
        out_specs=P("gx", "gy", None),
        check_vma=False,
    )
```

```python
import functools
import math

import jax
import jax.numpy as jnp
from jax import lax
from jax.experimental import pallas as pl
from jax.experimental.pallas import tpu as pltpu
from jax.sharding import PartitionSpec as P

LEVELS = 16
LOAD = 0.2
LANES = 128
POISSON = 0.3
LAME = POISSON / ((1.0 + POISSON) * (1.0 - 2.0 * POISSON))
SHEAR = 1.0 / (2.0 * (1.0 + POISSON))
DIAGONAL = (LAME + 2.0 * SHEAR) / 9.0 + 2.0 * SHEAR / 9.0
VMEM = pl.BlockSpec(memory_space=pltpu.VMEM)
PARAMS = pltpu.CompilerParams(vmem_limit_bytes=30 * 2**20)
f32 = jnp.float32
bf16 = jnp.bfloat16


def up8(count):
    return -(-count // 8) * 8


def shift_down(value):
    lane = lax.broadcasted_iota(jnp.int32, value.shape, value.ndim - 1)
    rolled = pltpu.roll(value, LANES - 1, value.ndim - 1)
    return jnp.where(lane == LANES - 1, 0.0, rolled)


def shift_up(value):
    lane = lax.broadcasted_iota(jnp.int32, value.shape, value.ndim - 1)
    return jnp.where(lane == 0, 0.0, pltpu.roll(value, 1, value.ndim - 1))


def unrolled(count, factor, body):
    def turn(step, _):
        for offset in range(factor):
            body(step * factor + offset)
        return 0

    turns = count // factor
    if turns:
        lax.fori_loop(0, turns, turn, 0)
    for index in range(turns * factor, count):
        body(index)


def split(value):
    high = value.astype(bf16)
    return high, (value - high.astype(f32)).astype(bf16)


def modes_of(lower, upper):
    out = [[[[None] * 3 for _ in range(2)] for _ in range(2)] for _ in range(2)]
    for a in range(2):
        for c in range(2):
            for k in range(3):
                if a or c:
                    out[a][0][c][k] = lower[a][c][k] + upper[a][c][k]
                out[a][1][c][k] = upper[a][c][k] - lower[a][c][k]
    return out


PAIRS = (((1, 1, 0, 0), (0, 1, 1, 2)), ((1, 0, 1, 0), (0, 1, 1, 1)), ((1, 1, 0, 1), (1, 0, 1, 2)))
TRIPLE = ((0, 1, 1, 0), (1, 0, 1, 1), (1, 1, 0, 2))
SHEARS = (((0, 1, 0, 0), (1, 0, 0, 1)), ((0, 0, 1, 0), (1, 0, 0, 2)), ((0, 0, 1, 1), (0, 1, 0, 2)))
AXIAL = ((1, 0, 0, 0), (0, 1, 0, 1), (0, 0, 1, 2))


def at(modes, place):
    a, b, c, k = place
    return modes[a][b][c][k]


def mode_forces(modes, stiff):
    out = [[[[None] * 3 for _ in range(2)] for _ in range(2)] for _ in range(2)]

    def put(place, value):
        a, b, c, k = place
        out[a][b][c][k] = value

    shear = stiff * (SHEAR / 16)
    for first, second in SHEARS:
        force = shear * (at(modes, first) + at(modes, second))
        put(first, force)
        put(second, force)
    one, two, three = (at(modes, place) for place in AXIAL)
    volume = (stiff * (LAME / 16)) * (one + two + three)
    axial = stiff * (SHEAR / 8)
    for place in AXIAL:
        put(place, volume + axial * at(modes, place))
    own, cross = stiff * ((LAME + 3 * SHEAR) / 48), stiff * (LAME / 48)
    for first, second in PAIRS:
        one, two = at(modes, first), at(modes, second)
        put(first, own * one + cross * two)
        put(second, own * two + cross * one)
    twist = stiff * (SHEAR / 48)
    one, two, three = (at(modes, place) for place in TRIPLE)
    total = one + two + three
    for place in TRIPLE:
        put(place, twist * (total + at(modes, place)))
    last = stiff * ((LAME + 4 * SHEAR) / 144)
    for k in range(3):
        put((1, 1, 1, k), last * modes[1][1][1][k])
    return out


def mode_energy(modes):
    def square(value):
        return value * value

    shear = None
    for first, second in SHEARS:
        term = square(at(modes, first) + at(modes, second))
        shear = term if shear is None else shear + term
    one, two, three = (at(modes, place) for place in AXIAL)
    energy = (SHEAR / 16) * shear + (LAME / 16) * square(one + two + three)
    energy = energy + (SHEAR / 8) * (square(one) + square(two) + square(three))
    squares, products = None, None
    for first, second in PAIRS:
        one, two = at(modes, first), at(modes, second)
        term, product = square(one) + square(two), one * two
        squares = term if squares is None else squares + term
        products = product if products is None else products + product
    energy = energy + ((LAME + 3 * SHEAR) / 48) * squares + (LAME / 24) * products
    one, two, three = (at(modes, place) for place in TRIPLE)
    twist = square(one + two + three) + square(one) + square(two) + square(three)
    energy = energy + (SHEAR / 48) * twist
    last = square(modes[1][1][1][0]) + square(modes[1][1][1][1]) + square(modes[1][1][1][2])
    return energy + ((LAME + 4 * SHEAR) / 144) * last


def x_modes(find, plane, row, tile, cases):
    sums, diffs, columns, column = find(row)
    out = [[[None] * 3 for _ in range(2)] for _ in range(2)]
    for c, ref in enumerate((sums, diffs)):
        for k in range(3):
            rows = pl.ds(pl.multiple_of(k * cases + tile * 8, 8), 8)
            one = ref[plane * columns + column, rows, :]
            two = ref[(plane + 1) * columns + column, rows, :]
            out[0][c][k] = one + two
            out[1][c][k] = two - one
    return out


def whole(sums, diffs, columns):
    return lambda row: (sums, diffs, columns, row)


def apply_elements(find, stiff_ref, acc_s, acc_d, planes, rows, kept, stiff_x, stiff_y, cases):
    columns = len(kept)
    tiles = cases // 8
    for column in range(columns):
        acc_s[column] = jnp.zeros(acc_s.shape[1:], f32)
        acc_d[column] = jnp.zeros(acc_d.shape[1:], f32)

    def step(index, _):
        plane, tile = index // tiles, index % tiles

        def emit(row, total):
            if row not in kept:
                return
            for c, acc in enumerate((acc_s, acc_d)):
                for k in range(3):
                    lines = pl.ds(pl.multiple_of(k * cases + tile * 8, 8), 8)
                    low = plane * columns + row - kept[0]
                    acc[low, lines, :] += total[0][c][k] - total[1][c][k]
                    acc[low + columns, lines, :] = total[0][c][k] + total[1][c][k]

        lower = x_modes(find, plane, 0, tile, cases)
        carry = None
        for row in range(rows):
            upper = x_modes(find, plane, row + 1, tile, cases)
            stiff = jnp.broadcast_to(
                stiff_ref[plane + stiff_x, pl.ds(row + stiff_y, 1), :], (8, LANES)
            )
            forces = mode_forces(modes_of(lower, upper), stiff)
            here = [[[None] * 3 for _ in range(2)] for _ in range(2)]
            following = [[[None] * 3 for _ in range(2)] for _ in range(2)]
            for a in range(2):
                for c in range(2):
                    for k in range(3):
                        one, two = forces[a][0][c][k], forces[a][1][c][k]
                        if one is None:
                            here[a][c][k] = -two if carry is None else carry[a][c][k] - two
                            following[a][c][k] = two
                        else:
                            low = one - two
                            here[a][c][k] = low if carry is None else carry[a][c][k] + low
                            following[a][c][k] = one + two
            emit(row, here)
            carry, lower = following, upper
        emit(rows, carry)
        return 0

    lax.fori_loop(0, planes * tiles, step, 0)


def fill(source, base, sizes, ref, xs, ys, code_xs, code_ys):
    planes, rows, cases = sizes
    block = 3 * cases
    line = 0
    for x in xs:
        start = (x * rows + ys[0]) * block
        count = len(ys) * block
        ref[line : line + count, :] = source[start : start + count, :]
        line += count
    for x in code_xs:
        start = base + x * rows + code_ys[0]
        ref[line : line + len(code_ys), :] = source[start : start + len(code_ys), :]
        line += len(code_ys)
    if line < ref.shape[0]:
        ref[line:, :] = jnp.zeros((ref.shape[0] - line, LANES), f32)


def pack_kernel(sizes, forces, codes, own, edge):
    planes, rows, cases = sizes
    block = 3 * cases
    base = planes * rows * block
    for x in range(planes):
        own[base + x * rows : base + (x + 1) * rows, :] = codes[x]
        scale = jnp.where(codes[x] > 0.0, LOAD, 0.0)
        for k in range(3):
            for c in range(cases):
                start = x * rows * block + k * cases + c
                own[pl.ds(start, rows, stride=block), :] = forces[k, c, x] * scale

    even = lax.axis_index("gx") % 2 == 0
    size = rows * block
    for line in range(0, size, block):
        high = lines(own, (planes - 1) * size + line, block)
        edge[line : line + block, :] = jnp.where(even, lines(own, line, block), high)
    high = lines(own, base + (planes - 2) * rows, 2 * rows)
    edge[size:, :] = jnp.where(even, lines(own, base, 2 * rows), high)


def second_kernel(sizes, begun, own, second):
    _, rows, cases = sizes
    size = rows * 3 * cases
    second[...] = lines(own, size, size)


def rows_kernel(sizes, own, ym, yp):
    planes, rows, cases = sizes
    base = planes * rows * 3 * cases
    every_x = range(planes)
    fill(own, base, sizes, ym, every_x, (0, 1), every_x, (0, 1))
    fill(own, base, sizes, yp, every_x, (rows - 1,), every_x, (rows - 2, rows - 1))


def corner_kernel(sizes, ym, yp, out):
    planes, rows, cases = sizes
    block = 3 * cases
    even = lax.axis_index("gx") % 2 == 0
    line = 0
    for source, width in ((ym, 1), (yp, 2)):
        size = width * block
        parts = [(at, (planes - 2) * size + at, block) for at in range(0, 2 * size, block)]
        parts.append((planes * size, planes * size + (planes - 2) * 2, 4))
        for low, high, count in parts:
            value = lines(source, low, count)
            if low != high:
                value = jnp.where(even, value, lines(source, high, count))
            out[line : line + count, :] = value
            line += count
        out[line : line + 4, :] = jnp.zeros((4, LANES), f32)
        line += 4


def lines(ref, start, count):
    return ref[start : start + count, :]


def inside(ref, x, y, rows, block):
    return lines(ref, (x * rows + y) * block, block)


def beyond(refs, slot, y, rows, block):
    below, above = refs
    if y < 0:
        return lines(below, slot * block, block)
    return lines(above, (slot * 2 + y - rows) * block, block)


def beyond_codes(refs, slots, slot, y, block):
    below, above = refs
    if y < 0:
        return lines(below, slots * block + slot * 2, 2)
    return lines(above, slots * 2 * block + slot * 2, 2)


def corner(ref, slot, y, rows, block):
    start = slot * block if y < 0 else 2 * block + 8 + (slot * 2 + y - rows) * block
    return lines(ref, start, block)


def corner_codes(ref, slot, y, block):
    return lines(ref, (2 * block if y < 0 else 6 * block + 8) + slot * 2, 2)


def node_inverse(signed, count, out):
    planes = signed.shape[0]
    for x in range(1, planes):
        codes = signed[x, 0 : count + 1, :]
        total = jnp.abs(signed[x - 1, 0 : count + 1, :]) + jnp.abs(codes)
        total = total[:-1] + total[1:]
        total = total + shift_up(total)
        free = codes[1:] > 0.0
        value = 1.0 / (DIAGONAL * jnp.where(free, total, 1.0))
        out[x - 1, 0:count, :] = jnp.where(free, value, 0.0)
    for x in range(planes):
        signed[x] = jnp.abs(signed[x])


def place_column(sums, diffs, column, value):
    moved = shift_down(value)
    sums[column] = value + moved
    diffs[column] = moved - value


def early_kernel(
    sizes, own, pair, ym, yp, ym_pair, yp_pair, start, sums, diffs, acc_s, acc_d,
    stiff_ref, inverse,
):
    planes, rows, cases = sizes
    block = 3 * cases
    ys = rows + 3
    even = lax.axis_index("gx") % 2 == 0
    y_own, y_pair = (ym, yp), (ym_pair, yp_pair)

    def both_ways(w, read):
        low = read(True, w + 1) if w + 1 < planes else read(False, w + 1 - planes)
        high = read(False, planes + w - 1) if w < 1 else read(True, w - 1)
        return jnp.where(even, low, high)

    def codes(w, y):
        def read(mine, x):
            if y == 0:
                return lines(own if mine else pair, (planes * block + x) * rows, rows)
            return beyond_codes(y_own if mine else y_pair, planes, x, y, block)

        return both_ways(w, read)

    for w in range(-1, planes + 1):
        for y, count in ((-2, 2), (0, rows), (rows, 2)):
            stiff_ref[w + 1, y + 2 : y + 2 + count, :] = codes(w, y)
    node_inverse(stiff_ref, ys, inverse)
    for w in range(planes + 1):
        for y in range(-1, rows + 2):

            def read(mine, x):
                if 0 <= y < rows:
                    return inside(own if mine else pair, x, y, rows, block)
                return beyond(y_own if mine else y_pair, x, y, rows, block)

            value = both_ways(w, read) * inverse[w, y + 1 : y + 2, :]
            column = w * ys + y + 1
            start[column] = value
            place_column(sums, diffs, column, value)
    kept = range(1, rows + 2)
    find = whole(sums, diffs, ys)
    apply_elements(find, stiff_ref, acc_s, acc_d, planes, rows + 2, kept, 1, 1, cases)


def core_rows(rows):
    return range(2, rows - 1)


def rim_rows(rows):
    return (0, 1, rows - 1, rows)


def rim_columns(planes, rows):
    own = [(x, y) for x in range(planes) for y in rim_rows(rows) if y < rows]
    beyond_own = [(x, rows) for x in range(planes)] + [(planes, y) for y in rim_rows(rows)]
    return own + beyond_own, len(own)


def merged(x, planes, even, early, near):
    low = ([x - 1] if x >= 1 else [], [x + 1] if x <= 1 else [])
    high = ([x + 1] if x < planes else [], [x - planes + 1] if x >= planes - 1 else [])
    if low[0] and low[1] and high[0] and high[1]:
        one = early(jnp.where(even, low[0][0], high[0][0]))
        return one + near(jnp.where(even, low[1][0], high[1][0]))

    def read(places):
        found = [early(w) for w in places[0]] + [near(v) for v in places[1]]
        return found[0] if len(found) == 1 else found[0] + found[1]

    return jnp.where(even, read(low), read(high))


def direction_at(x, planes, even, early, middle):
    if x == 0:
        return jnp.where(even, middle, early(1))
    if x == planes:
        return jnp.where(even, early(planes - 1), middle)
    return early(jnp.where(even, x - 1, x + 1))


def keep_pair(ref, place, one, two, cases):
    for k in range(3):
        part = slice(k * cases, (k + 1) * cases)
        high, rest = split(jnp.concatenate([one[part], two[part]], 0))
        lane = pl.ds(pl.multiple_of((place * 3 + k) * LANES, LANES), LANES)
        ref[0 : 2 * cases, lane] = high
        ref[2 * cases : 4 * cases, lane] = rest


def products(first, second):
    contract = (((1,), (1,)), ((), ()))
    out = lax.dot_general(first, second, contract, preferred_element_type=f32)
    left, right = out.shape[0] // 2, out.shape[1] // 2
    out = out[:, :right] + out[:, right:]
    return out[:left] + out[left:]


def folds(cases):
    two, count, rest = 2 * cases, 5 * cases // 12, cases // 6
    first, part = 2 * two, LANES - 2 * two
    return (
        ((slice(0, count), slice(0, two)), (slice(0, count), slice(0, two))),
        ((slice(0, count), slice(two, first)), (slice(count, 2 * count), slice(0, two))),
        ((slice(0, rest), slice(first, LANES)), (slice(2 * count, cases), slice(0, part))),
        (
            (slice(rest, 2 * rest), slice(first, first + two - part)),
            (slice(2 * count, cases), slice(part, two)),
        ),
    )


def diagonal_place(cases, index):
    line = cases // 3 + index
    return slice(line, line + 1), slice(4 * cases, 5 * cases)


def middle_kernel(
    sizes, own, pair, edge, second, start, sums_e, diffs_e, acc_se, acc_de,
    sums, diffs, middle, acc_s, acc_d, w_sums, w_diffs, both_out, gram_out, acc2_s, acc2_d,
    stiff_ref, inverse, right,
):
    planes, rows, cases = sizes
    block = 3 * cases
    ys, nodes_y, inner = rows + 3, rows + 1, rows - 1
    core = core_rows(rows)
    even = lax.axis_index("gx") % 2 == 0

    def codes(x):
        if 0 <= x < planes:
            return lines(own, (planes * block + x) * rows, rows)
        slot = x + 2 if x < 0 else x - planes
        outer = lines(edge, (block + slot) * rows, rows)
        if x < 0:
            return jnp.where(even, outer, lines(pair, (planes * block + planes + x) * rows, rows))
        return jnp.where(even, lines(pair, (planes * block + slot) * rows, rows), outer)

    for x in range(-2, planes + 2):
        stiff_ref[x + 2, 0:rows, :] = codes(x)
    node_inverse(stiff_ref, inner, inverse)

    def place(v, x, ref, slot):
        for y in range(1, rows):
            value = inside(ref, slot, y, rows, block) * inverse[x + 1, y - 1 : y, :]
            if v == 1:
                middle[y - 1] = value
            place_column(sums, diffs, v * inner + y - 1, value)

    def copy(v, w):
        for y in range(1, rows):
            sums[v * inner + y - 1] = sums_e[w * ys + y + 1]
            diffs[v * inner + y - 1] = diffs_e[w * ys + y + 1]

    @pl.when(even)
    def _():
        place(0, -1, edge, 0)
        place(1, 0, own, 0)
        copy(2, 0)

    @pl.when(jnp.logical_not(even))
    def _():
        copy(0, planes)
        place(1, planes, edge, 0)
        place(2, planes + 1, second, 0)

    layer = jnp.where(even, 1, planes + 1)
    find = whole(sums, diffs, inner)
    apply_elements(find, stiff_ref, acc_s, acc_d, 2, rows - 2, range(inner), layer, 1, cases)

    def image(x, y, place):
        def total(early, near):
            return merged(
                x, planes, even, lambda w: early[w * nodes_y + y],
                lambda v: near[v * inner + y - 1],
            )

        s, d = total(acc_se, acc_s), total(acc_de, acc_d)
        force = s - d + shift_up(s + d)
        scaled = force * inverse[x + 1, pl.ds(y - 1, 1), :]
        place_column(w_sums, w_diffs, place, scaled)
        value = direction_at(x, planes, even, lambda w: start[w * ys + y + 1], middle[y - 1])
        keep_pair(both_out, place, value, scaled, cases)
        return force

    def within(x, index):
        y, place = core[0] + index, x * len(core) + index
        force = image(x, y, place)
        given = own[pl.ds(pl.multiple_of((x * rows + y) * block, 8), block), :]
        keep_pair(right, place, given, force, cases)

    for x in range(planes):
        unrolled(len(core), len(core), functools.partial(within, x))
    last = planes * len(core)
    unrolled(len(core), len(core), lambda index: image(planes, core[0] + index, last + index))
    gram_out[...] = products(right[...], both_out[:, : last * 3 * LANES])

    find = whole(w_sums, w_diffs, len(core))
    kept = range(len(core))
    apply_elements(
        find, stiff_ref, acc2_s, acc2_d, planes, len(core) - 1, kept, 2, core[0], cases
    )


def main_kernel(
    sizes, own, pair, edge, second, ym, yp, ym_pair, yp_pair, corners,
    start, sums_e, diffs_e, acc_se, acc_de,
    sums_m, diffs_m, middle_m, acc_sm, acc_dm, w_sm, w_dm, both_m, gram_m,
    acc2_sm, acc2_dm, both_out, system_out, stiff_ref, inverse,
    middle, sums, diffs, acc_s0, acc_d0, acc_s1, acc_d1, w_sums, w_diffs,
    acc2_s0, acc2_d0, acc2_s1, acc2_d1, right, second_m, second_r, table, dense,
):
    planes, rows, cases = sizes
    block = 3 * cases
    ys, nodes_y, inner = rows + 3, rows + 1, rows - 1
    core, rim = core_rows(rows), rim_rows(rows)
    columns, own_count = rim_columns(planes, rows)
    even = lax.axis_index("gx") % 2 == 0
    y_own, y_pair = (ym, yp), (ym_pair, yp_pair)

    def codes(x, y):
        def read(mine, plane):
            if y == 0:
                return lines(own if mine else pair, (planes * block + plane) * rows, rows)
            return beyond_codes(y_own if mine else y_pair, planes, plane, y, block)

        if 0 <= x < planes:
            return read(True, x)
        slot = x + 2 if x < 0 else x - planes
        if y == 0:
            outer = lines(edge, (block + slot) * rows, rows)
        else:
            outer = corner_codes(corners, slot, y, block)
        within = read(False, planes + x if x < 0 else x - planes)
        return jnp.where(even, outer, within) if x < 0 else jnp.where(even, within, outer)

    for x in range(-2, planes + 2):
        for y, count in ((-2, 2), (0, rows), (rows, 2)):
            stiff_ref[x + 2, y + 2 : y + 2 + count, :] = codes(x, y)
    node_inverse(stiff_ref, ys, inverse)

    sides = (-1, 0, rows, rows + 1)

    def place(v, x, ref, slot, beyond_at):
        for i, y in enumerate(sides):
            value = inside(ref, slot, y, rows, block) if y == 0 else beyond_at(y)
            value = value * inverse[x + 1, y + 1 : y + 2, :]
            if v == 1 and y in (0, rows):
                middle[y // rows] = value
            place_column(sums, diffs, v * 4 + i, value)

    def copy(v, w):
        for i, y in enumerate(sides):
            sums[v * 4 + i] = sums_e[w * ys + y + 1]
            diffs[v * 4 + i] = diffs_e[w * ys + y + 1]

    @pl.when(even)
    def _():
        place(0, -1, edge, 0, lambda y: corner(corners, 1, y, rows, block))
        place(1, 0, own, 0, lambda y: beyond(y_own, 0, y, rows, block))
        copy(2, 0)

    @pl.when(jnp.logical_not(even))
    def _():
        copy(0, planes)
        place(1, planes, edge, 0, lambda y: corner(corners, 0, y, rows, block))
        place(2, planes + 1, second, 0, lambda y: corner(corners, 1, y, rows, block))

    def find_low(row):
        return (sums, diffs, 4, row) if row < 2 else (sums_m, diffs_m, inner, 0)

    def find_high(row):
        return (sums, diffs, 4, row + 1) if row else (sums_m, diffs_m, inner, inner - 1)

    layer = jnp.where(even, 1, planes + 1)
    apply_elements(find_low, stiff_ref, acc_s0, acc_d0, 2, 2, range(1, 3), layer, 1, cases)
    apply_elements(find_high, stiff_ref, acc_s1, acc_d1, 2, 2, range(2), layer, rows + 1, cases)

    def image(x, y, place):
        def total(early, near, low, high):
            def outer(v):
                value = low[v * 2 + y] if y < 2 else high[v * 2 + y - inner]
                return value + near[v * inner + y - 1] if y in (1, inner) else value

            return merged(x, planes, even, lambda w: early[w * nodes_y + y], outer)

        s = total(acc_se, acc_sm, acc_s0, acc_s1)
        d = total(acc_de, acc_dm, acc_d0, acc_d1)
        force = s - d + shift_up(s + d)
        scaled = force * inverse[x + 1, y + 1 : y + 2, :]
        place_column(w_sums, w_diffs, x * len(rim) + rim.index(y), scaled)
        inner_middle = middle_m[y - 1] if y in (1, inner) else middle[y // rows]
        value = direction_at(x, planes, even, lambda w: start[w * ys + y + 1], inner_middle)
        keep_pair(both_out, place, value, scaled, cases)
        return force

    for index, (x, y) in enumerate(columns):
        force = image(x, y, index)
        if index < own_count:
            keep_pair(right, index, inside(own, x, y, rows, block), force, cases)

    def find(row):
        if row in rim:
            return w_sums, w_diffs, len(rim), rim.index(row)
        return w_sm, w_dm, len(core), row - core[0]

    def find_last(row):
        return find(row + rows - 2)

    low, high = (acc2_s0, acc2_d0), (acc2_s1, acc2_d1)
    apply_elements(find, stiff_ref, *low, planes, 2, range(3), 2, 2, cases)
    apply_elements(find_last, stiff_ref, *high, planes, 2, range(3), 2, rows, cases)

    def second_force(ref, x, y, place):
        s, d = None, None
        for parts, width, first in (
            (low, 3, 0), ((acc2_sm, acc2_dm), len(core), core[0]), (high, 3, rows - 2)
        ):
            if first <= y < first + width:
                column = x * width + y - first
                more = parts[0][column], parts[1][column]
                s, d = more if s is None else (s + more[0], d + more[1])
        force = s - d + shift_up(s + d)
        for k in range(3):
            value = force[k * cases : (k + 1) * cases]
            top = value.astype(bf16).astype(f32)
            lane = pl.ds(pl.multiple_of((place * 3 + k) * LANES, LANES), LANES)
            ref[:, lane] = jnp.concatenate([top, value - top], 0).astype(bf16)

    for x in range(planes + 1):
        for index, y in enumerate(core):
            second_force(second_m, x, y, x * len(core) + index)
    for index, (x, y) in enumerate(columns):
        second_force(second_r, x, y, index)

    two = 2 * cases
    gram = products(right[...], both_out[:, : own_count * 3 * LANES]) + gram_m[...]
    other = products(second_m[...], both_m[...]) + products(second_r[...], both_out[...])
    row = lax.broadcasted_iota(jnp.int32, (cases, cases), 0)
    column = lax.broadcasted_iota(jnp.int32, (cases, cases), 1)
    load_load, load_image = gram[:cases, :cases], gram[cases:, :cases]
    mixed, image_image = other[:, :cases], other[:, cases:]
    table[:, 0:cases] = jnp.where(row <= column, load_load, load_image)
    table[:, cases:two] = jnp.where(row <= column, mixed, image_image)
    dense[...] = jnp.zeros(dense.shape, f32)
    for target, source in folds(cases):
        dense[target] = table[source]
    for index, value in enumerate((load_image, image_image)):
        diagonal = jnp.sum(jnp.where(row == column, value, 0.0), axis=0, keepdims=True)
        dense[diagonal_place(cases, index)] = diagonal
    depth = system_out.shape[2]
    for index in range(system_out.shape[0]):
        for part in range(system_out.shape[1]):
            system_out[index, part] = dense[part * depth : (part + 1) * depth, :]


def solve_kernel(
    sizes, system, both_m, both_r, codes, out, mixing, sums, diffs, energy, square, full, dense
):
    planes, rows, cases = sizes
    two = 2 * cases
    nodes_y = rows + 1
    count = planes * rows
    total = jnp.sum(system[...], axis=0)
    depth = system.shape[2]
    for part in range(system.shape[1]):
        dense[part * depth : (part + 1) * depth, :] = total[part]
    square[...] = jnp.zeros(square.shape, f32)
    for source, target in folds(cases):
        square[target] = dense[source]
    value, turned = square[0:cases, :], jnp.transpose(square[...])
    line = lax.broadcasted_iota(jnp.int32, (cases, cases), 0)
    place = lax.broadcasted_iota(jnp.int32, (cases, cases), 1)

    def mended(start, diagonal=None):
        kept, other = value[:, start : start + cases], turned[start : start + cases, :cases]
        if diagonal is None:
            return jnp.where(line <= place, kept, other)
        inner = jnp.where(line < place, other, dense[diagonal_place(cases, diagonal)])
        return jnp.where(line > place, kept, inner)

    load_image, mixed = mended(0, 0), mended(cases)
    parts = ((load_image, mixed), (mixed, mended(cases, 1)), (mended(0), load_image))
    full[...] = jnp.zeros(full.shape, f32)
    for index, (left, right) in enumerate(parts):
        full[index * cases : (index + 1) * cases, 0:cases] = left
        full[index * cases : (index + 1) * cases, cases:two] = right
    table = full[...]
    lane = lax.broadcasted_iota(jnp.int32, (1, LANES), 1)
    gone, wide = 0, 8
    for pivot in range(0, two, wide):
        drop = pivot // 8 * 8 - gone
        table = table[drop:]
        gone += drop
        line = pivot - gone
        inner = (lane >= pivot) & (lane < pivot + wide)
        found = [table[line + p : line + p + 1, :] for p in range(wide)]
        block = [
            [jnp.broadcast_to(row[:, pivot + q : pivot + q + 1], row.shape) for q in range(wide)]
            for row in found
        ]
        solved = [
            jnp.where(lane == pivot + p, -1.0, jnp.where(inner, 0.0, found[p]))
            for p in range(wide)
        ]
        for p in range(wide):
            inverse = 1.0 / block[p][p]
            solved[p] = solved[p] * inverse
            block[p] = [value * inverse for value in block[p]]
            for q in range(wide):
                if q != p:
                    factor = block[q][p]
                    solved[q] = solved[q] - factor * solved[p]
                    for r in range(p + 1, wide):
                        block[q][r] = block[q][r] - factor * block[p][r]
        update = None
        for q in range(wide):
            term = table[:, pivot + q : pivot + q + 1] * solved[q]
            update = term if update is None else update + term
        table = jnp.where(inner, 0.0, table) - update
    answer = table[two - gone :, :two]
    high = answer.astype(bf16).astype(f32)
    mixing[...] = jnp.zeros(mixing.shape, f32)
    mixing[0:cases, 0:two] = high
    mixing[0:cases, two : 2 * two] = high
    mixing[cases:two, 0:two] = answer - high
    mix = mixing[...][:, : 2 * two].astype(bf16)

    def combined(ref, place, width):
        value = jnp.dot(
            mix, ref[:, place * 3 * LANES : (place + width) * 3 * LANES], preferred_element_type=f32
        )
        return value[:cases] + value[cases:]

    def keep(value, index, column):
        for k in range(3):
            part = value[:, (index * 3 + k) * LANES : (index * 3 + k + 1) * LANES]
            moved = shift_down(part)
            sums[column, k * cases : (k + 1) * cases, :] = part + moved
            diffs[column, k * cases : (k + 1) * cases, :] = moved - part

    core = core_rows(rows)
    for x in range(planes + 1):
        value = combined(both_m, x * len(core), len(core))
        for index, y in enumerate(core):
            keep(value, index, x * nodes_y + y)
    columns, _ = rim_columns(planes, rows)
    for start in range(0, len(columns), 6):
        some = columns[start : start + 6]
        value = combined(both_r, start, len(some))
        for index, (x, y) in enumerate(some):
            keep(value, index, x * nodes_y + y)

    find = whole(sums, diffs, nodes_y)
    tiles = cases // 8

    def step(plane, _):
        for tile in range(tiles):
            lower = x_modes(find, plane, 0, tile, cases)
            for row in range(rows):
                upper = x_modes(find, plane, row + 1, tile, cases)
                part = mode_energy(modes_of(lower, upper))
                if tile == 0:
                    energy[row] = part
                else:
                    energy[row] += part
                lower = upper
        total = jnp.sum(energy[...], axis=1)
        total = (-3.0 / cases) * jnp.abs(codes[plane]) * total
        for index in range(out.shape[0]):
            out[index, plane] = total
        return 0

    lax.fori_loop(0, planes, step, 0)


def smooth(ref, x, rows):
    weight = [2.5 - math.sqrt(q) for q in range(7)]
    near = {}
    for dx in range(-2, 3):
        for dy in range(-2, 3):
            q = dx * dx + dy * dy
            if q <= 5:
                value = ref[x + 2 + dx, 2 + dy : 2 + dy + rows, :]
                near[q] = value if q not in near else near[q] + value
    result = None
    for dz in range(3):
        part = None
        for q, value in near.items():
            if q + dz * dz <= 6:
                term = weight[q + dz * dz] * value
                part = term if part is None else part + term
        if dz == 0:
            result = part
        else:
            place = lax.broadcasted_iota(jnp.int32, part.shape, 1)
            forward = jnp.where(place >= LANES - dz, 0.0, pltpu.roll(part, LANES - dz, 1))
            backward = jnp.where(place < dz, 0.0, pltpu.roll(part, dz, 1))
            result = result + (forward + backward)
    return result


def scale_kernel(sizes, counts, levels, out, there):
    planes, rows, _ = sizes
    y = lax.broadcasted_iota(jnp.int32, (rows + 4, LANES), 0)
    y = y + (lax.axis_index("gy") * rows - 2)
    in_y = (y >= 0) & (y < counts[1] * rows)
    for x in range(planes + 4):
        global_x = lax.axis_index("gx") * planes + (x - 2)
        in_x = (global_x >= 0) & (global_x < counts[0] * planes)
        there[x] = jnp.where(in_y & in_x, 1.0, 0.0)
    for x in range(planes):
        density = 0.3 + 0.7 * levels[x].astype(f32) / (LEVELS - 1)
        out[x] = 1.0 / (density * smooth(there, x, rows))


def filter_kernel(sizes, counts, blocks, blocks_pair, scale, out, wide):
    planes, rows, _ = sizes
    sides_x = ((-1, planes - 2, planes, 0), (0, 0, planes, 2), (1, 0, 2, 2 + planes))
    sides_y = ((-1, rows - 2, rows, 0), (0, 0, rows, 2), (1, 0, 2, 2 + rows))
    for step_x, x0, x1, to_x in sides_x:
        for step_y, y0, y1, to_y in sides_y:
            at_x = lax.axis_index("gx") + step_x
            at_y = lax.axis_index("gy") + step_y
            inside = (at_x >= 0) & (at_x < counts[0]) & (at_y >= 0) & (at_y < counts[1])
            index = jnp.where(inside, at_x // 2 * counts[1] + at_y, 0)
            value = (blocks_pair if step_x else blocks)[index, x0:x1, y0:y1, :]
            wide[to_x : to_x + x1 - x0, to_y : to_y + y1 - y0, :] = jnp.where(inside, value, 0.0)
    for x in range(planes):
        out[x] = smooth(wide, x, rows) * scale[x]


def local(forces, levels, supports):
    _, cases, planes, rows, _ = forces.shape
    sizes = (planes, rows, cases)
    block = 3 * cases
    count_x, count_y = lax.axis_size("gx"), lax.axis_size("gy")

    def shape(blocks, codes):
        return jax.ShapeDtypeStruct((blocks * block + up8(codes), LANES), f32)

    density = 0.3 + 0.7 * levels.astype(f32) / (LEVELS - 1)
    codes = density * density * density
    codes = jnp.where(supports == 0, codes, -codes)
    counts = (count_x, count_y)
    own, edge = pl.pallas_call(
        functools.partial(pack_kernel, sizes),
        out_shape=[shape(planes * rows, planes * rows), shape(rows, 2 * rows)],
        in_specs=[VMEM] * 2,
        out_specs=[VMEM] * 2,
        compiler_params=PARAMS,
        name="pack",
    )(forces, codes)
    scale = pl.pallas_call(
        functools.partial(scale_kernel, sizes, counts),
        out_shape=jax.ShapeDtypeStruct((planes, rows, LANES), f32),
        in_specs=[VMEM],
        out_specs=VMEM,
        scratch_shapes=[pltpu.VMEM((planes + 4, rows + 4, LANES), f32)],
        compiler_params=PARAMS,
        name="scale",
    )(levels)

    def moved(value, axis, step):
        count = lax.axis_size(axis)
        pairs = [(i, i + step) for i in range(count) if 0 <= i + step < count]
        return lax.ppermute(value, axis, pairs)

    def links(first, step):
        return [(i, i + step) for i in range(first, count_x, 2) if 0 <= i + step < count_x]

    def swapped(value):
        return lax.ppermute(value, "gx", links(0, 1) + links(1, -1))

    def across(value):
        return lax.ppermute(value, "gx", links(1, 1) + links(2, -1))

    edge = across(edge)
    pair = swapped(own)
    own, pair = lax.optimization_barrier((own, pair))
    ym, yp = pl.pallas_call(
        functools.partial(rows_kernel, sizes),
        out_shape=[shape(2 * planes, 2 * planes), shape(planes, 2 * planes)],
        in_specs=[VMEM],
        out_specs=[VMEM] * 2,
        compiler_params=PARAMS,
        name="rows",
    )(own)
    from_yp, from_ym = moved(ym, "gy", -1), moved(yp, "gy", 1)
    second = pl.pallas_call(
        functools.partial(second_kernel, sizes),
        out_shape=shape(rows, 0),
        in_specs=[VMEM] * 2,
        out_specs=VMEM,
        compiler_params=PARAMS,
        name="second",
    )(swapped(codes), own)
    second = lax.ppermute(second, "gx", links(2, -1))
    pair_yp, pair_ym = swapped(from_yp), swapped(from_ym)
    from_ym, from_yp, edge = lax.optimization_barrier((from_ym, from_yp, edge))
    corners = across(
        pl.pallas_call(
            functools.partial(corner_kernel, sizes),
            out_shape=jax.ShapeDtypeStruct((6 * block + 16, LANES), f32),
            in_specs=[VMEM] * 2,
            out_specs=VMEM,
            compiler_params=PARAMS,
            name="corners",
        )(from_ym, from_yp)
    )

    devices = count_x * count_y
    nodes = (planes + 1) * (rows + 1)
    window = jax.ShapeDtypeStruct(((planes + 1) * (rows + 3), block, LANES), f32)
    partial_forces = jax.ShapeDtypeStruct((nodes, block, LANES), f32)
    early = pl.pallas_call(
        functools.partial(early_kernel, sizes),
        out_shape=[window] * 3 + [partial_forces] * 2,
        in_specs=[VMEM] * 6,
        out_specs=[VMEM] * 5,
        scratch_shapes=[
            pltpu.VMEM((planes + 2, up8(rows + 4), LANES), f32),
            pltpu.VMEM((planes + 1, up8(rows + 3), LANES), f32),
        ],
        compiler_params=PARAMS,
        cost_estimate=pl.CostEstimate(
            flops=200 * planes * rows * block * LANES, bytes_accessed=2**23, transcendentals=0
        ),
        name="early",
    )(own, pair, from_ym, from_yp, pair_ym, pair_yp)

    def columns(count):
        return jax.ShapeDtypeStruct((count, block, LANES), f32)

    def fields(lines, count):
        return jax.ShapeDtypeStruct((lines * cases, count * 3 * LANES), bf16)

    def scratch(value):
        return pltpu.VMEM(value.shape, value.dtype)

    core = len(core_rows(rows))
    middle = pl.pallas_call(
        functools.partial(middle_kernel, sizes),
        out_shape=[columns(3 * (rows - 1))] * 2
        + [columns(rows - 1)]
        + [columns(3 * (rows - 1))] * 2
        + [columns((planes + 1) * core)] * 2
        + [fields(4, (planes + 1) * core), jax.ShapeDtypeStruct((2 * cases, 2 * cases), f32)]
        + [columns((planes + 1) * core)] * 2,
        in_specs=[VMEM] * 9,
        out_specs=[VMEM] * 11,
        scratch_shapes=[
            pltpu.VMEM((planes + 4, up8(rows), LANES), f32),
            pltpu.VMEM((planes + 3, up8(rows), LANES), f32),
            scratch(fields(4, planes * core)),
        ],
        compiler_params=PARAMS,
        name="middle",
    )(own, pair, edge, second, *early)

    rim, rim_own = rim_columns(planes, rows)
    both, system = pl.pallas_call(
        functools.partial(main_kernel, sizes),
        out_shape=[
            fields(4, len(rim)),
            jax.ShapeDtypeStruct((devices, 5 * cases // 24, 2, LANES), f32),
        ],
        in_specs=[VMEM] * 25,
        out_specs=[VMEM] * 2,
        scratch_shapes=[
            pltpu.VMEM((planes + 4, up8(rows + 4), LANES), f32),
            pltpu.VMEM((planes + 3, up8(rows + 3), LANES), f32),
            scratch(columns(2)),
            *[scratch(columns(12))] * 2,
            *[scratch(columns(6))] * 4,
            *[scratch(columns((planes + 1) * 4))] * 2,
            *[scratch(columns((planes + 1) * 3))] * 4,
            scratch(fields(4, rim_own)),
            scratch(fields(2, (planes + 1) * core)),
            scratch(fields(2, len(rim))),
            pltpu.VMEM((cases, LANES), f32),
            pltpu.VMEM((5 * cases // 12, LANES), f32),
        ],
        compiler_params=PARAMS,
        name="operator",
    )(
        own, pair, edge, second, from_ym, from_yp, pair_ym, pair_yp, corners,
        *early, *middle,
    )

    groups = [
        [x * count_y + y for x in range(side, count_x, 2) for y in range(count_y)]
        for side in range(2)
    ]

    def gathered(copies):
        mine = lax.all_to_all(copies, ("gx", "gy"), 0, 0, axis_index_groups=groups)
        return mine, swapped(mine)

    system = lax.all_to_all(system, ("gx", "gy"), 0, 0)

    weighted = pl.pallas_call(
        functools.partial(solve_kernel, sizes),
        out_shape=jax.ShapeDtypeStruct((devices // 2, planes, rows, LANES), f32),
        in_specs=[VMEM] * 4,
        out_specs=VMEM,
        scratch_shapes=[
            pltpu.VMEM((2 * cases, LANES), f32),
            scratch(columns(nodes)),
            scratch(columns(nodes)),
            pltpu.VMEM((rows, 8, LANES), f32),
            pltpu.VMEM((LANES, LANES), f32),
            pltpu.VMEM((3 * cases, LANES), f32),
            pltpu.VMEM((5 * cases // 12, LANES), f32),
        ],
        compiler_params=PARAMS,
        name="solve",
    )(system, middle[7], both, codes)

    blocks = gathered(weighted)
    return pl.pallas_call(
        functools.partial(filter_kernel, sizes, counts),
        out_shape=jax.ShapeDtypeStruct((planes, rows, LANES), f32),
        in_specs=[VMEM] * 3,
        out_specs=VMEM,
        scratch_shapes=[pltpu.VMEM((planes + 4, rows + 4, LANES), f32)],
        compiler_params=PARAMS,
        name="cone",
    )(*blocks, scale)


def solution(mesh):
    return jax.shard_map(
        local,
        mesh=mesh,
        in_specs=(P(None, None, "gx", "gy", None), P("gx", "gy", None), P("gx", "gy", None)),
        out_specs=P("gx", "gy", None),
        check_vma=False,
    )
```

```python
import functools
import math

import jax
import jax.numpy as jnp
from jax import lax
from jax.experimental import pallas as pl
from jax.experimental.pallas import tpu as pltpu
from jax.sharding import PartitionSpec as P

LEVELS = 16
LOAD = 0.2
LANES = 128
POISSON = 0.3
LAME = POISSON / ((1.0 + POISSON) * (1.0 - 2.0 * POISSON))
SHEAR = 1.0 / (2.0 * (1.0 + POISSON))
DIAGONAL = (LAME + 2.0 * SHEAR) / 9.0 + 2.0 * SHEAR / 9.0
VMEM = pl.BlockSpec(memory_space=pltpu.VMEM)
PARAMS = pltpu.CompilerParams(vmem_limit_bytes=30 * 2**20)
f32 = jnp.float32
bf16 = jnp.bfloat16


def up8(count):
    return -(-count // 8) * 8


def shift_down(value):
    lane = lax.broadcasted_iota(jnp.int32, value.shape, value.ndim - 1)
    rolled = pltpu.roll(value, LANES - 1, value.ndim - 1)
    return jnp.where(lane == LANES - 1, 0.0, rolled)


def shift_up(value):
    lane = lax.broadcasted_iota(jnp.int32, value.shape, value.ndim - 1)
    return jnp.where(lane == 0, 0.0, pltpu.roll(value, 1, value.ndim - 1))


def unrolled(count, factor, body):
    def turn(step, _):
        for offset in range(factor):
            body(step * factor + offset)
        return 0

    turns = count // factor
    if turns:
        lax.fori_loop(0, turns, turn, 0)
    for index in range(turns * factor, count):
        body(index)


def split(value):
    high = value.astype(bf16)
    return high, (value - high.astype(f32)).astype(bf16)


def modes_of(lower, upper):
    out = [[[[None] * 3 for _ in range(2)] for _ in range(2)] for _ in range(2)]
    for a in range(2):
        for c in range(2):
            for k in range(3):
                if a or c:
                    out[a][0][c][k] = lower[a][c][k] + upper[a][c][k]
                out[a][1][c][k] = upper[a][c][k] - lower[a][c][k]
    return out


PAIRS = (((1, 1, 0, 0), (0, 1, 1, 2)), ((1, 0, 1, 0), (0, 1, 1, 1)), ((1, 1, 0, 1), (1, 0, 1, 2)))
TRIPLE = ((0, 1, 1, 0), (1, 0, 1, 1), (1, 1, 0, 2))
SHEARS = (((0, 1, 0, 0), (1, 0, 0, 1)), ((0, 0, 1, 0), (1, 0, 0, 2)), ((0, 0, 1, 1), (0, 1, 0, 2)))
AXIAL = ((1, 0, 0, 0), (0, 1, 0, 1), (0, 0, 1, 2))


def at(modes, place):
    a, b, c, k = place
    return modes[a][b][c][k]


def mode_forces(modes, stiff):
    out = [[[[None] * 3 for _ in range(2)] for _ in range(2)] for _ in range(2)]

    def put(place, value):
        a, b, c, k = place
        out[a][b][c][k] = value

    shear = stiff * (SHEAR / 16)
    for first, second in SHEARS:
        force = shear * (at(modes, first) + at(modes, second))
        put(first, force)
        put(second, force)
    one, two, three = (at(modes, place) for place in AXIAL)
    volume = (stiff * (LAME / 16)) * (one + two + three)
    axial = stiff * (SHEAR / 8)
    for place in AXIAL:
        put(place, volume + axial * at(modes, place))
    own, cross = stiff * ((LAME + 3 * SHEAR) / 48), stiff * (LAME / 48)
    for first, second in PAIRS:
        one, two = at(modes, first), at(modes, second)
        put(first, own * one + cross * two)
        put(second, own * two + cross * one)
    twist = stiff * (SHEAR / 48)
    one, two, three = (at(modes, place) for place in TRIPLE)
    total = one + two + three
    for place in TRIPLE:
        put(place, twist * (total + at(modes, place)))
    last = stiff * ((LAME + 4 * SHEAR) / 144)
    for k in range(3):
        put((1, 1, 1, k), last * modes[1][1][1][k])
    return out


def mode_energy(modes):
    def square(value):
        return value * value

    shear = None
    for first, second in SHEARS:
        term = square(at(modes, first) + at(modes, second))
        shear = term if shear is None else shear + term
    one, two, three = (at(modes, place) for place in AXIAL)
    energy = (SHEAR / 16) * shear + (LAME / 16) * square(one + two + three)
    energy = energy + (SHEAR / 8) * (square(one) + square(two) + square(three))
    squares, products = None, None
    for first, second in PAIRS:
        one, two = at(modes, first), at(modes, second)
        term, product = square(one) + square(two), one * two
        squares = term if squares is None else squares + term
        products = product if products is None else products + product
    energy = energy + ((LAME + 3 * SHEAR) / 48) * squares + (LAME / 24) * products
    one, two, three = (at(modes, place) for place in TRIPLE)
    twist = square(one + two + three) + square(one) + square(two) + square(three)
    energy = energy + (SHEAR / 48) * twist
    last = square(modes[1][1][1][0]) + square(modes[1][1][1][1]) + square(modes[1][1][1][2])
    return energy + ((LAME + 4 * SHEAR) / 144) * last


def x_modes(find, plane, row, tile, cases):
    sums, diffs, columns, column = find(row)
    out = [[[None] * 3 for _ in range(2)] for _ in range(2)]
    for c, ref in enumerate((sums, diffs)):
        for k in range(3):
            rows = pl.ds(pl.multiple_of(k * cases + tile * 8, 8), 8)
            one = ref[plane * columns + column, rows, :]
            two = ref[(plane + 1) * columns + column, rows, :]
            out[0][c][k] = one + two
            out[1][c][k] = two - one
    return out


def whole(sums, diffs, columns):
    return lambda row: (sums, diffs, columns, row)


def apply_elements(find, stiff_ref, acc_s, acc_d, planes, rows, kept, stiff_x, stiff_y, cases):
    columns = len(kept)
    tiles = cases // 8
    for column in range(columns):
        acc_s[column] = jnp.zeros(acc_s.shape[1:], f32)
        acc_d[column] = jnp.zeros(acc_d.shape[1:], f32)

    def step(index, _):
        plane, tile = index // tiles, index % tiles

        def emit(row, total):
            if row not in kept:
                return
            for c, acc in enumerate((acc_s, acc_d)):
                for k in range(3):
                    lines = pl.ds(pl.multiple_of(k * cases + tile * 8, 8), 8)
                    low = plane * columns + row - kept[0]
                    acc[low, lines, :] += total[0][c][k] - total[1][c][k]
                    acc[low + columns, lines, :] = total[0][c][k] + total[1][c][k]

        lower = x_modes(find, plane, 0, tile, cases)
        carry = None
        for row in range(rows):
            upper = x_modes(find, plane, row + 1, tile, cases)
            stiff = jnp.broadcast_to(
                stiff_ref[plane + stiff_x, pl.ds(row + stiff_y, 1), :], (8, LANES)
            )
            forces = mode_forces(modes_of(lower, upper), stiff)
            here = [[[None] * 3 for _ in range(2)] for _ in range(2)]
            following = [[[None] * 3 for _ in range(2)] for _ in range(2)]
            for a in range(2):
                for c in range(2):
                    for k in range(3):
                        one, two = forces[a][0][c][k], forces[a][1][c][k]
                        if one is None:
                            here[a][c][k] = -two if carry is None else carry[a][c][k] - two
                            following[a][c][k] = two
                        else:
                            low = one - two
                            here[a][c][k] = low if carry is None else carry[a][c][k] + low
                            following[a][c][k] = one + two
            emit(row, here)
            carry, lower = following, upper
        emit(rows, carry)
        return 0

    lax.fori_loop(0, planes * tiles, step, 0)


def fill(source, base, sizes, ref, xs, ys, code_xs, code_ys):
    planes, rows, cases = sizes
    block = 3 * cases
    line = 0
    for x in xs:
        start = (x * rows + ys[0]) * block
        count = len(ys) * block
        ref[line : line + count, :] = source[start : start + count, :]
        line += count
    for x in code_xs:
        start = base + x * rows + code_ys[0]
        ref[line : line + len(code_ys), :] = source[start : start + len(code_ys), :]
        line += len(code_ys)
    if line < ref.shape[0]:
        ref[line:, :] = jnp.zeros((ref.shape[0] - line, LANES), f32)


def pack_kernel(sizes, forces, codes, own, edge):
    planes, rows, cases = sizes
    block = 3 * cases
    base = planes * rows * block
    for x in range(planes):
        own[base + x * rows : base + (x + 1) * rows, :] = codes[x]
        scale = jnp.where(codes[x] > 0.0, LOAD, 0.0)
        for k in range(3):
            for c in range(cases):
                start = x * rows * block + k * cases + c
                own[pl.ds(start, rows, stride=block), :] = forces[k, c, x] * scale

    even = lax.axis_index("gx") % 2 == 0
    size = rows * block
    for line in range(0, size, block):
        high = lines(own, (planes - 1) * size + line, block)
        edge[line : line + block, :] = jnp.where(even, lines(own, line, block), high)
    high = lines(own, base + (planes - 2) * rows, 2 * rows)
    edge[size:, :] = jnp.where(even, lines(own, base, 2 * rows), high)


def second_kernel(sizes, begun, own, second):
    _, rows, cases = sizes
    size = rows * 3 * cases
    second[...] = lines(own, size, size)


def rows_kernel(sizes, own, ym, yp):
    planes, rows, cases = sizes
    base = planes * rows * 3 * cases
    every_x = range(planes)
    fill(own, base, sizes, ym, every_x, (0, 1), every_x, (0, 1))
    fill(own, base, sizes, yp, every_x, (rows - 1,), every_x, (rows - 2, rows - 1))


def corner_kernel(sizes, ym, yp, out):
    planes, rows, cases = sizes
    block = 3 * cases
    even = lax.axis_index("gx") % 2 == 0
    line = 0
    for source, width in ((ym, 1), (yp, 2)):
        size = width * block
        parts = [(at, (planes - 2) * size + at, block) for at in range(0, 2 * size, block)]
        parts.append((planes * size, planes * size + (planes - 2) * 2, 4))
        for low, high, count in parts:
            value = lines(source, low, count)
            if low != high:
                value = jnp.where(even, value, lines(source, high, count))
            out[line : line + count, :] = value
            line += count
        out[line : line + 4, :] = jnp.zeros((4, LANES), f32)
        line += 4


def lines(ref, start, count):
    return ref[start : start + count, :]


def inside(ref, x, y, rows, block):
    return lines(ref, (x * rows + y) * block, block)


def beyond(refs, slot, y, rows, block):
    below, above = refs
    if y < 0:
        return lines(below, slot * block, block)
    return lines(above, (slot * 2 + y - rows) * block, block)


def beyond_codes(refs, slots, slot, y, block):
    below, above = refs
    if y < 0:
        return lines(below, slots * block + slot * 2, 2)
    return lines(above, slots * 2 * block + slot * 2, 2)


def corner(ref, slot, y, rows, block):
    start = slot * block if y < 0 else 2 * block + 8 + (slot * 2 + y - rows) * block
    return lines(ref, start, block)


def corner_codes(ref, slot, y, block):
    return lines(ref, (2 * block if y < 0 else 6 * block + 8) + slot * 2, 2)


def node_inverse(signed, count, out):
    planes = signed.shape[0]
    for x in range(1, planes):
        codes = signed[x, 0 : count + 1, :]
        total = jnp.abs(signed[x - 1, 0 : count + 1, :]) + jnp.abs(codes)
        total = total[:-1] + total[1:]
        total = total + shift_up(total)
        free = codes[1:] > 0.0
        value = 1.0 / (DIAGONAL * jnp.where(free, total, 1.0))
        out[x - 1, 0:count, :] = jnp.where(free, value, 0.0)
    for x in range(planes):
        signed[x] = jnp.abs(signed[x])


def place_column(sums, diffs, column, value):
    moved = shift_down(value)
    sums[column] = value + moved
    diffs[column] = moved - value


def early_kernel(
    sizes, own, pair, ym, yp, ym_pair, yp_pair, start, sums, diffs, acc_s, acc_d,
    stiff_ref, inverse,
):
    planes, rows, cases = sizes
    block = 3 * cases
    ys = rows + 3
    even = lax.axis_index("gx") % 2 == 0
    y_own, y_pair = (ym, yp), (ym_pair, yp_pair)

    def both_ways(w, read):
        low = read(True, w + 1) if w + 1 < planes else read(False, w + 1 - planes)
        high = read(False, planes + w - 1) if w < 1 else read(True, w - 1)
        return jnp.where(even, low, high)

    def codes(w, y):
        def read(mine, x):
            if y == 0:
                return lines(own if mine else pair, (planes * block + x) * rows, rows)
            return beyond_codes(y_own if mine else y_pair, planes, x, y, block)

        return both_ways(w, read)

    for w in range(-1, planes + 1):
        for y, count in ((-2, 2), (0, rows), (rows, 2)):
            stiff_ref[w + 1, y + 2 : y + 2 + count, :] = codes(w, y)
    node_inverse(stiff_ref, ys, inverse)
    for w in range(planes + 1):
        for y in range(-1, rows + 2):

            def read(mine, x):
                if 0 <= y < rows:
                    return inside(own if mine else pair, x, y, rows, block)
                return beyond(y_own if mine else y_pair, x, y, rows, block)

            value = both_ways(w, read) * inverse[w, y + 1 : y + 2, :]
            column = w * ys + y + 1
            start[column] = value
            place_column(sums, diffs, column, value)
    kept = range(1, rows + 2)
    find = whole(sums, diffs, ys)
    apply_elements(find, stiff_ref, acc_s, acc_d, planes, rows + 2, kept, 1, 1, cases)


def core_rows(rows):
    return range(2, rows - 1)


def rim_rows(rows):
    return (0, 1, rows - 1, rows)


def core_columns(planes, rows):
    core = core_rows(rows)
    inner, outer = core[1:-1], (core[0], core[-1])
    first = [(x, y) for x in range(planes + 1) for y in inner]
    last = [(x, y) for x in range(planes + 1) for y in outer]
    return first, last, planes * len(inner), planes * len(outer)


def rim_columns(planes, rows):
    own = [(x, y) for x in range(planes) for y in rim_rows(rows) if y < rows]
    beyond_own = [(x, rows) for x in range(planes)] + [(planes, y) for y in rim_rows(rows)]
    return own + beyond_own, len(own)


def merged(x, planes, even, early, near):
    low = ([x - 1] if x >= 1 else [], [x + 1] if x <= 1 else [])
    high = ([x + 1] if x < planes else [], [x - planes + 1] if x >= planes - 1 else [])
    if low[0] and low[1] and high[0] and high[1]:
        one = early(jnp.where(even, low[0][0], high[0][0]))
        return one + near(jnp.where(even, low[1][0], high[1][0]))

    def read(places):
        found = [early(w) for w in places[0]] + [near(v) for v in places[1]]
        return found[0] if len(found) == 1 else found[0] + found[1]

    return jnp.where(even, read(low), read(high))


def direction_at(x, planes, even, early, middle):
    if x == 0:
        return jnp.where(even, middle, early(1))
    if x == planes:
        return jnp.where(even, early(planes - 1), middle)
    return early(jnp.where(even, x - 1, x + 1))


def keep_pair(ref, place, one, two, cases):
    for k in range(3):
        part = slice(k * cases, (k + 1) * cases)
        high, rest = split(jnp.concatenate([one[part], two[part]], 0))
        lane = pl.ds(pl.multiple_of((place * 3 + k) * LANES, LANES), LANES)
        ref[0 : 2 * cases, lane] = high
        ref[2 * cases : 4 * cases, lane] = rest


def keep_split(ref, place, value, cases):
    for k in range(3):
        part = value[k * cases : (k + 1) * cases]
        high = part.astype(bf16).astype(f32)
        ref[:, (place * 3 + k) * LANES : (place * 3 + k + 1) * LANES] = jnp.concatenate(
            [high, part - high], 0
        ).astype(bf16)


def products(first, second):
    contract = (((1,), (1,)), ((), ()))
    out = lax.dot_general(first, second, contract, preferred_element_type=f32)
    left, right = out.shape[0] // 2, out.shape[1] // 2
    out = out[:, :right] + out[:, right:]
    return out[:left] + out[left:]


def folds(cases):
    two, count, rest = 2 * cases, 5 * cases // 12, cases // 6
    first, part = 2 * two, LANES - 2 * two
    return (
        ((slice(0, count), slice(0, two)), (slice(0, count), slice(0, two))),
        ((slice(0, count), slice(two, first)), (slice(count, 2 * count), slice(0, two))),
        ((slice(0, rest), slice(first, LANES)), (slice(2 * count, cases), slice(0, part))),
        (
            (slice(rest, 2 * rest), slice(first, first + two - part)),
            (slice(2 * count, cases), slice(part, two)),
        ),
    )


def diagonal_place(cases, index):
    line = cases // 3 + index
    return slice(line, line + 1), slice(4 * cases, 5 * cases)


def middle_kernel(
    sizes, own, pair, edge, second, start, sums_e, diffs_e, acc_se, acc_de,
    sums, diffs, middle, acc_s, acc_d, w_sums, w_diffs, both_out, gram_out, other_out,
    acc2_s, acc2_d, stiff_ref, inverse, right, again,
):
    planes, rows, cases = sizes
    block = 3 * cases
    ys, nodes_y, inner = rows + 3, rows + 1, rows - 1
    core = core_rows(rows)
    even = lax.axis_index("gx") % 2 == 0

    def codes(x):
        if 0 <= x < planes:
            return lines(own, (planes * block + x) * rows, rows)
        slot = x + 2 if x < 0 else x - planes
        outer = lines(edge, (block + slot) * rows, rows)
        if x < 0:
            return jnp.where(even, outer, lines(pair, (planes * block + planes + x) * rows, rows))
        return jnp.where(even, lines(pair, (planes * block + slot) * rows, rows), outer)

    for x in range(-2, planes + 2):
        stiff_ref[x + 2, 0:rows, :] = codes(x)
    node_inverse(stiff_ref, inner, inverse)

    def place(v, x, ref, slot):
        for y in range(1, rows):
            value = inside(ref, slot, y, rows, block) * inverse[x + 1, y - 1 : y, :]
            if v == 1:
                middle[y - 1] = value
            place_column(sums, diffs, v * inner + y - 1, value)

    def copy(v, w):
        for y in range(1, rows):
            sums[v * inner + y - 1] = sums_e[w * ys + y + 1]
            diffs[v * inner + y - 1] = diffs_e[w * ys + y + 1]

    @pl.when(even)
    def _():
        place(0, -1, edge, 0)
        place(1, 0, own, 0)
        copy(2, 0)

    @pl.when(jnp.logical_not(even))
    def _():
        copy(0, planes)
        place(1, planes, edge, 0)
        place(2, planes + 1, second, 0)

    layer = jnp.where(even, 1, planes + 1)
    find = whole(sums, diffs, inner)
    apply_elements(find, stiff_ref, acc_s, acc_d, 2, rows - 2, range(inner), layer, 1, cases)

    def image(x, y, place):
        def total(early, near):
            return merged(
                x, planes, even, lambda w: early[w * nodes_y + y],
                lambda v: near[v * inner + y - 1],
            )

        s, d = total(acc_se, acc_s), total(acc_de, acc_d)
        force = s - d + shift_up(s + d)
        scaled = force * inverse[x + 1, pl.ds(y - 1, 1), :]
        place_column(w_sums, w_diffs, x * len(core) + y - core[0], scaled)
        value = direction_at(x, planes, even, lambda w: start[w * ys + y + 1], middle[y - 1])
        keep_pair(both_out, place, value, scaled, cases)
        return force

    inner_columns, outer_columns, inner_own, outer_own = core_columns(planes, rows)
    count = len(inner_columns)
    for index, (x, y) in enumerate(inner_columns + outer_columns):
        force = image(x, y, index)
        if x < planes:
            place = index if index < count else inner_own + index - count
            keep_pair(right, place, inside(own, x, y, rows, block), force, cases)
    width = 3 * LANES
    gram = products(right[:, : inner_own * width], both_out[:, : inner_own * width])
    outer_part = both_out[:, count * width : (count + outer_own) * width]
    gram_out[...] = gram + products(right[:, inner_own * width :], outer_part)

    find = whole(w_sums, w_diffs, len(core))
    kept = range(len(core))
    apply_elements(
        find, stiff_ref, acc2_s, acc2_d, planes, len(core) - 1, kept, 2, core[0], cases
    )
    for index, (x, y) in enumerate(inner_columns):
        column = x * len(core) + y - core[0]
        s, d = acc2_s[column], acc2_d[column]
        keep_split(again, index, s - d + shift_up(s + d), cases)
    other_out[...] = products(again[...], both_out[:, : count * width])


def main_kernel(
    sizes, own, pair, edge, second, ym, yp, ym_pair, yp_pair, corners,
    start, sums_e, diffs_e, acc_se, acc_de,
    sums_m, diffs_m, middle_m, acc_sm, acc_dm, w_sm, w_dm, both_m, gram_m,
    other_m, acc2_sm, acc2_dm, both_out, system_out, stiff_ref, inverse,
    middle, sums, diffs, acc_s0, acc_d0, acc_s1, acc_d1, w_sums, w_diffs,
    acc2_s0, acc2_d0, acc2_s1, acc2_d1, right, second_m, second_r, table, dense,
):
    planes, rows, cases = sizes
    block = 3 * cases
    ys, nodes_y, inner = rows + 3, rows + 1, rows - 1
    core, rim = core_rows(rows), rim_rows(rows)
    columns, own_count = rim_columns(planes, rows)
    even = lax.axis_index("gx") % 2 == 0
    y_own, y_pair = (ym, yp), (ym_pair, yp_pair)

    def codes(x, y):
        def read(mine, plane):
            if y == 0:
                return lines(own if mine else pair, (planes * block + plane) * rows, rows)
            return beyond_codes(y_own if mine else y_pair, planes, plane, y, block)

        if 0 <= x < planes:
            return read(True, x)
        slot = x + 2 if x < 0 else x - planes
        if y == 0:
            outer = lines(edge, (block + slot) * rows, rows)
        else:
            outer = corner_codes(corners, slot, y, block)
        within = read(False, planes + x if x < 0 else x - planes)
        return jnp.where(even, outer, within) if x < 0 else jnp.where(even, within, outer)

    for x in range(-2, planes + 2):
        for y, count in ((-2, 2), (0, rows), (rows, 2)):
            stiff_ref[x + 2, y + 2 : y + 2 + count, :] = codes(x, y)
    node_inverse(stiff_ref, ys, inverse)

    sides = (-1, 0, rows, rows + 1)

    def place(v, x, ref, slot, beyond_at):
        for i, y in enumerate(sides):
            value = inside(ref, slot, y, rows, block) if y == 0 else beyond_at(y)
            value = value * inverse[x + 1, y + 1 : y + 2, :]
            if v == 1 and y in (0, rows):
                middle[y // rows] = value
            place_column(sums, diffs, v * 4 + i, value)

    def copy(v, w):
        for i, y in enumerate(sides):
            sums[v * 4 + i] = sums_e[w * ys + y + 1]
            diffs[v * 4 + i] = diffs_e[w * ys + y + 1]

    @pl.when(even)
    def _():
        place(0, -1, edge, 0, lambda y: corner(corners, 1, y, rows, block))
        place(1, 0, own, 0, lambda y: beyond(y_own, 0, y, rows, block))
        copy(2, 0)

    @pl.when(jnp.logical_not(even))
    def _():
        copy(0, planes)
        place(1, planes, edge, 0, lambda y: corner(corners, 0, y, rows, block))
        place(2, planes + 1, second, 0, lambda y: corner(corners, 1, y, rows, block))

    def find_low(row):
        return (sums, diffs, 4, row) if row < 2 else (sums_m, diffs_m, inner, 0)

    def find_high(row):
        return (sums, diffs, 4, row + 1) if row else (sums_m, diffs_m, inner, inner - 1)

    layer = jnp.where(even, 1, planes + 1)
    apply_elements(find_low, stiff_ref, acc_s0, acc_d0, 2, 2, range(1, 3), layer, 1, cases)
    apply_elements(find_high, stiff_ref, acc_s1, acc_d1, 2, 2, range(2), layer, rows + 1, cases)

    def image(x, y, place):
        def total(early, near, low, high):
            def outer(v):
                value = low[v * 2 + y] if y < 2 else high[v * 2 + y - inner]
                return value + near[v * inner + y - 1] if y in (1, inner) else value

            return merged(x, planes, even, lambda w: early[w * nodes_y + y], outer)

        s = total(acc_se, acc_sm, acc_s0, acc_s1)
        d = total(acc_de, acc_dm, acc_d0, acc_d1)
        force = s - d + shift_up(s + d)
        scaled = force * inverse[x + 1, y + 1 : y + 2, :]
        place_column(w_sums, w_diffs, x * len(rim) + rim.index(y), scaled)
        inner_middle = middle_m[y - 1] if y in (1, inner) else middle[y // rows]
        value = direction_at(x, planes, even, lambda w: start[w * ys + y + 1], inner_middle)
        keep_pair(both_out, place, value, scaled, cases)
        return force

    for index, (x, y) in enumerate(columns):
        force = image(x, y, index)
        if index < own_count:
            keep_pair(right, index, inside(own, x, y, rows, block), force, cases)

    def find(row):
        if row in rim:
            return w_sums, w_diffs, len(rim), rim.index(row)
        return w_sm, w_dm, len(core), row - core[0]

    def find_last(row):
        return find(row + rows - 2)

    low, high = (acc2_s0, acc2_d0), (acc2_s1, acc2_d1)
    apply_elements(find, stiff_ref, *low, planes, 2, range(3), 2, 2, cases)
    apply_elements(find_last, stiff_ref, *high, planes, 2, range(3), 2, rows, cases)

    def second_force(x, y):
        s, d = None, None
        for parts, width, first in (
            (low, 3, 0), ((acc2_sm, acc2_dm), len(core), core[0]), (high, 3, rows - 2)
        ):
            if first <= y < first + width:
                column = x * width + y - first
                more = parts[0][column], parts[1][column]
                s, d = more if s is None else (s + more[0], d + more[1])
        return s - d + shift_up(s + d)

    inner_columns, outer_columns, _, _ = core_columns(planes, rows)
    for index, (x, y) in enumerate(outer_columns):
        keep_split(second_m, index, second_force(x, y), cases)
    for index, (x, y) in enumerate(columns):
        keep_split(second_r, index, second_force(x, y), cases)

    two = 2 * cases
    gram = products(right[...], both_out[:, : own_count * 3 * LANES]) + gram_m[...]
    other = products(second_m[...], both_m[:, len(inner_columns) * 3 * LANES :]) + other_m[...]
    other = other + products(second_r[...], both_out[...])
    row = lax.broadcasted_iota(jnp.int32, (cases, cases), 0)
    column = lax.broadcasted_iota(jnp.int32, (cases, cases), 1)
    load_load, load_image = gram[:cases, :cases], gram[cases:, :cases]
    mixed, image_image = other[:, :cases], other[:, cases:]
    table[:, 0:cases] = jnp.where(row <= column, load_load, load_image)
    table[:, cases:two] = jnp.where(row <= column, mixed, image_image)
    dense[...] = jnp.zeros(dense.shape, f32)
    for target, source in folds(cases):
        dense[target] = table[source]
    for index, value in enumerate((load_image, image_image)):
        diagonal = jnp.sum(jnp.where(row == column, value, 0.0), axis=0, keepdims=True)
        dense[diagonal_place(cases, index)] = diagonal
    depth = system_out.shape[2]
    for index in range(system_out.shape[0]):
        for part in range(system_out.shape[1]):
            system_out[index, part] = dense[part * depth : (part + 1) * depth, :]


def solve_kernel(
    sizes, system, both_m, both_r, codes, out, mixing, sums, diffs, energy, square, full, dense
):
    planes, rows, cases = sizes
    two = 2 * cases
    nodes_y = rows + 1
    count = planes * rows
    total = jnp.sum(system[...], axis=0)
    depth = system.shape[2]
    for part in range(system.shape[1]):
        dense[part * depth : (part + 1) * depth, :] = total[part]
    square[...] = jnp.zeros(square.shape, f32)
    for source, target in folds(cases):
        square[target] = dense[source]
    value, turned = square[0:cases, :], jnp.transpose(square[...])
    line = lax.broadcasted_iota(jnp.int32, (cases, cases), 0)
    place = lax.broadcasted_iota(jnp.int32, (cases, cases), 1)

    def mended(start, diagonal=None):
        kept, other = value[:, start : start + cases], turned[start : start + cases, :cases]
        if diagonal is None:
            return jnp.where(line <= place, kept, other)
        inner = jnp.where(line < place, other, dense[diagonal_place(cases, diagonal)])
        return jnp.where(line > place, kept, inner)

    load_image, mixed = mended(0, 0), mended(cases)
    parts = ((load_image, mixed), (mixed, mended(cases, 1)), (mended(0), load_image))
    full[...] = jnp.zeros(full.shape, f32)
    for index, (left, right) in enumerate(parts):
        full[index * cases : (index + 1) * cases, 0:cases] = left
        full[index * cases : (index + 1) * cases, cases:two] = right
    table = full[...]
    lane = lax.broadcasted_iota(jnp.int32, (1, LANES), 1)
    gone, wide = 0, 8
    for pivot in range(0, two, wide):
        drop = pivot // 8 * 8 - gone
        table = table[drop:]
        gone += drop
        line = pivot - gone
        inner = (lane >= pivot) & (lane < pivot + wide)
        found = [table[line + p : line + p + 1, :] for p in range(wide)]
        block = [
            [jnp.broadcast_to(row[:, pivot + q : pivot + q + 1], row.shape) for q in range(wide)]
            for row in found
        ]
        solved = [
            jnp.where(lane == pivot + p, -1.0, jnp.where(inner, 0.0, found[p]))
            for p in range(wide)
        ]
        for p in range(wide):
            inverse = 1.0 / block[p][p]
            solved[p] = solved[p] * inverse
            block[p] = [value * inverse for value in block[p]]
            for q in range(wide):
                if q != p:
                    factor = block[q][p]
                    solved[q] = solved[q] - factor * solved[p]
                    for r in range(p + 1, wide):
                        block[q][r] = block[q][r] - factor * block[p][r]
        update = None
        for q in range(wide):
            term = table[:, pivot + q : pivot + q + 1] * solved[q]
            update = term if update is None else update + term
        table = jnp.where(inner, 0.0, table) - update
    answer = table[two - gone :, :two]
    high = answer.astype(bf16).astype(f32)
    mixing[...] = jnp.zeros(mixing.shape, f32)
    mixing[0:cases, 0:two] = high
    mixing[0:cases, two : 2 * two] = high
    mixing[cases:two, 0:two] = answer - high
    mix = mixing[...][:, : 2 * two].astype(bf16)

    def combined(ref, place, width):
        value = jnp.dot(
            mix, ref[:, place * 3 * LANES : (place + width) * 3 * LANES], preferred_element_type=f32
        )
        return value[:cases] + value[cases:]

    def keep(value, index, column):
        for k in range(3):
            part = value[:, (index * 3 + k) * LANES : (index * 3 + k + 1) * LANES]
            moved = shift_down(part)
            sums[column, k * cases : (k + 1) * cases, :] = part + moved
            diffs[column, k * cases : (k + 1) * cases, :] = moved - part

    inner_columns, outer_columns, _, _ = core_columns(planes, rows)
    columns, _ = rim_columns(planes, rows)
    for ref, columns in ((both_m, inner_columns + outer_columns), (both_r, columns)):
        for start in range(0, len(columns), 6):
            some = columns[start : start + 6]
            value = combined(ref, start, len(some))
            for index, (x, y) in enumerate(some):
                keep(value, index, x * nodes_y + y)

    find = whole(sums, diffs, nodes_y)
    tiles = cases // 8

    def step(plane, _):
        for tile in range(tiles):
            lower = x_modes(find, plane, 0, tile, cases)
            for row in range(rows):
                upper = x_modes(find, plane, row + 1, tile, cases)
                part = mode_energy(modes_of(lower, upper))
                if tile == 0:
                    energy[row] = part
                else:
                    energy[row] += part
                lower = upper
        total = jnp.sum(energy[...], axis=1)
        total = (-3.0 / cases) * jnp.abs(codes[plane]) * total
        for index in range(out.shape[0]):
            out[index, plane] = total
        return 0

    lax.fori_loop(0, planes, step, 0)


def smooth(ref, x, rows):
    weight = [2.5 - math.sqrt(q) for q in range(7)]
    near = {}
    for dx in range(-2, 3):
        for dy in range(-2, 3):
            q = dx * dx + dy * dy
            if q <= 5:
                value = ref[x + 2 + dx, 2 + dy : 2 + dy + rows, :]
                near[q] = value if q not in near else near[q] + value
    result = None
    for dz in range(3):
        part = None
        for q, value in near.items():
            if q + dz * dz <= 6:
                term = weight[q + dz * dz] * value
                part = term if part is None else part + term
        if dz == 0:
            result = part
        else:
            place = lax.broadcasted_iota(jnp.int32, part.shape, 1)
            forward = jnp.where(place >= LANES - dz, 0.0, pltpu.roll(part, LANES - dz, 1))
            backward = jnp.where(place < dz, 0.0, pltpu.roll(part, dz, 1))
            result = result + (forward + backward)
    return result


def scale_kernel(sizes, counts, levels, out, there):
    planes, rows, _ = sizes
    y = lax.broadcasted_iota(jnp.int32, (rows + 4, LANES), 0)
    y = y + (lax.axis_index("gy") * rows - 2)
    in_y = (y >= 0) & (y < counts[1] * rows)
    for x in range(planes + 4):
        global_x = lax.axis_index("gx") * planes + (x - 2)
        in_x = (global_x >= 0) & (global_x < counts[0] * planes)
        there[x] = jnp.where(in_y & in_x, 1.0, 0.0)
    for x in range(planes):
        density = 0.3 + 0.7 * levels[x].astype(f32) / (LEVELS - 1)
        out[x] = 1.0 / (density * smooth(there, x, rows))


def filter_kernel(sizes, counts, blocks, blocks_pair, scale, out, wide):
    planes, rows, _ = sizes
    sides_x = ((-1, planes - 2, planes, 0), (0, 0, planes, 2), (1, 0, 2, 2 + planes))
    sides_y = ((-1, rows - 2, rows, 0), (0, 0, rows, 2), (1, 0, 2, 2 + rows))
    for step_x, x0, x1, to_x in sides_x:
        for step_y, y0, y1, to_y in sides_y:
            at_x = lax.axis_index("gx") + step_x
            at_y = lax.axis_index("gy") + step_y
            inside = (at_x >= 0) & (at_x < counts[0]) & (at_y >= 0) & (at_y < counts[1])
            index = jnp.where(inside, at_x // 2 * counts[1] + at_y, 0)
            value = (blocks_pair if step_x else blocks)[index, x0:x1, y0:y1, :]
            wide[to_x : to_x + x1 - x0, to_y : to_y + y1 - y0, :] = jnp.where(inside, value, 0.0)
    for x in range(planes):
        out[x] = smooth(wide, x, rows) * scale[x]


def local(forces, levels, supports):
    _, cases, planes, rows, _ = forces.shape
    sizes = (planes, rows, cases)
    block = 3 * cases
    count_x, count_y = lax.axis_size("gx"), lax.axis_size("gy")

    def shape(blocks, codes):
        return jax.ShapeDtypeStruct((blocks * block + up8(codes), LANES), f32)

    density = 0.3 + 0.7 * levels.astype(f32) / (LEVELS - 1)
    codes = density * density * density
    codes = jnp.where(supports == 0, codes, -codes)
    counts = (count_x, count_y)
    own, edge = pl.pallas_call(
        functools.partial(pack_kernel, sizes),
        out_shape=[shape(planes * rows, planes * rows), shape(rows, 2 * rows)],
        in_specs=[VMEM] * 2,
        out_specs=[VMEM] * 2,
        compiler_params=PARAMS,
        name="pack",
    )(forces, codes)
    scale = pl.pallas_call(
        functools.partial(scale_kernel, sizes, counts),
        out_shape=jax.ShapeDtypeStruct((planes, rows, LANES), f32),
        in_specs=[VMEM],
        out_specs=VMEM,
        scratch_shapes=[pltpu.VMEM((planes + 4, rows + 4, LANES), f32)],
        compiler_params=PARAMS,
        name="scale",
    )(levels)

    def moved(value, axis, step):
        count = lax.axis_size(axis)
        pairs = [(i, i + step) for i in range(count) if 0 <= i + step < count]
        return lax.ppermute(value, axis, pairs)

    def links(first, step):
        return [(i, i + step) for i in range(first, count_x, 2) if 0 <= i + step < count_x]

    def swapped(value):
        return lax.ppermute(value, "gx", links(0, 1) + links(1, -1))

    def across(value):
        return lax.ppermute(value, "gx", links(1, 1) + links(2, -1))

    edge = across(edge)
    pair = swapped(own)
    own, pair = lax.optimization_barrier((own, pair))
    ym, yp = pl.pallas_call(
        functools.partial(rows_kernel, sizes),
        out_shape=[shape(2 * planes, 2 * planes), shape(planes, 2 * planes)],
        in_specs=[VMEM],
        out_specs=[VMEM] * 2,
        compiler_params=PARAMS,
        name="rows",
    )(own)
    from_yp, from_ym = moved(ym, "gy", -1), moved(yp, "gy", 1)
    second = pl.pallas_call(
        functools.partial(second_kernel, sizes),
        out_shape=shape(rows, 0),
        in_specs=[VMEM] * 2,
        out_specs=VMEM,
        compiler_params=PARAMS,
        name="second",
    )(swapped(codes), own)
    second = lax.ppermute(second, "gx", links(2, -1))
    pair_yp, pair_ym = swapped(from_yp), swapped(from_ym)
    from_ym, from_yp, edge = lax.optimization_barrier((from_ym, from_yp, edge))
    corners = across(
        pl.pallas_call(
            functools.partial(corner_kernel, sizes),
            out_shape=jax.ShapeDtypeStruct((6 * block + 16, LANES), f32),
            in_specs=[VMEM] * 2,
            out_specs=VMEM,
            compiler_params=PARAMS,
            name="corners",
        )(from_ym, from_yp)
    )

    devices = count_x * count_y
    nodes = (planes + 1) * (rows + 1)
    window = jax.ShapeDtypeStruct(((planes + 1) * (rows + 3), block, LANES), f32)
    partial_forces = jax.ShapeDtypeStruct((nodes, block, LANES), f32)
    early = pl.pallas_call(
        functools.partial(early_kernel, sizes),
        out_shape=[window] * 3 + [partial_forces] * 2,
        in_specs=[VMEM] * 6,
        out_specs=[VMEM] * 5,
        scratch_shapes=[
            pltpu.VMEM((planes + 2, up8(rows + 4), LANES), f32),
            pltpu.VMEM((planes + 1, up8(rows + 3), LANES), f32),
        ],
        compiler_params=PARAMS,
        cost_estimate=pl.CostEstimate(
            flops=200 * planes * rows * block * LANES, bytes_accessed=2**23, transcendentals=0
        ),
        name="early",
    )(own, pair, from_ym, from_yp, pair_ym, pair_yp)

    def columns(count):
        return jax.ShapeDtypeStruct((count, block, LANES), f32)

    def fields(lines, count):
        return jax.ShapeDtypeStruct((lines * cases, count * 3 * LANES), bf16)

    def scratch(value):
        return pltpu.VMEM(value.shape, value.dtype)

    core = len(core_rows(rows))
    middle = pl.pallas_call(
        functools.partial(middle_kernel, sizes),
        out_shape=[columns(3 * (rows - 1))] * 2
        + [columns(rows - 1)]
        + [columns(3 * (rows - 1))] * 2
        + [columns((planes + 1) * core)] * 2
        + [fields(4, (planes + 1) * core), jax.ShapeDtypeStruct((2 * cases, 2 * cases), f32)]
        + [jax.ShapeDtypeStruct((cases, 2 * cases), f32)]
        + [columns((planes + 1) * core)] * 2,
        in_specs=[VMEM] * 9,
        out_specs=[VMEM] * 12,
        scratch_shapes=[
            pltpu.VMEM((planes + 4, up8(rows), LANES), f32),
            pltpu.VMEM((planes + 3, up8(rows), LANES), f32),
            scratch(fields(4, planes * core)),
            scratch(fields(2, (planes + 1) * (core - 2))),
        ],
        compiler_params=PARAMS,
        name="middle",
    )(own, pair, edge, second, *early)

    rim, rim_own = rim_columns(planes, rows)
    both, system = pl.pallas_call(
        functools.partial(main_kernel, sizes),
        out_shape=[
            fields(4, len(rim)),
            jax.ShapeDtypeStruct((devices, 5 * cases // 24, 2, LANES), f32),
        ],
        in_specs=[VMEM] * 26,
        out_specs=[VMEM] * 2,
        scratch_shapes=[
            pltpu.VMEM((planes + 4, up8(rows + 4), LANES), f32),
            pltpu.VMEM((planes + 3, up8(rows + 3), LANES), f32),
            scratch(columns(2)),
            *[scratch(columns(12))] * 2,
            *[scratch(columns(6))] * 4,
            *[scratch(columns((planes + 1) * 4))] * 2,
            *[scratch(columns((planes + 1) * 3))] * 4,
            scratch(fields(4, rim_own)),
            scratch(fields(2, (planes + 1) * 2)),
            scratch(fields(2, len(rim))),
            pltpu.VMEM((cases, LANES), f32),
            pltpu.VMEM((5 * cases // 12, LANES), f32),
        ],
        compiler_params=PARAMS,
        name="operator",
    )(
        own, pair, edge, second, from_ym, from_yp, pair_ym, pair_yp, corners,
        *early, *middle,
    )

    groups = [
        [x * count_y + y for x in range(side, count_x, 2) for y in range(count_y)]
        for side in range(2)
    ]

    def gathered(copies):
        mine = lax.all_to_all(copies, ("gx", "gy"), 0, 0, axis_index_groups=groups)
        return mine, swapped(mine)

    system = lax.all_to_all(system, ("gx", "gy"), 0, 0)

    weighted = pl.pallas_call(
        functools.partial(solve_kernel, sizes),
        out_shape=jax.ShapeDtypeStruct((devices // 2, planes, rows, LANES), f32),
        in_specs=[VMEM] * 4,
        out_specs=VMEM,
        scratch_shapes=[
            pltpu.VMEM((2 * cases, LANES), f32),
            scratch(columns(nodes)),
            scratch(columns(nodes)),
            pltpu.VMEM((rows, 8, LANES), f32),
            pltpu.VMEM((LANES, LANES), f32),
            pltpu.VMEM((3 * cases, LANES), f32),
            pltpu.VMEM((5 * cases // 12, LANES), f32),
        ],
        compiler_params=PARAMS,
        name="solve",
    )(system, middle[7], both, codes)

    blocks = gathered(weighted)
    return pl.pallas_call(
        functools.partial(filter_kernel, sizes, counts),
        out_shape=jax.ShapeDtypeStruct((planes, rows, LANES), f32),
        in_specs=[VMEM] * 3,
        out_specs=VMEM,
        scratch_shapes=[pltpu.VMEM((planes + 4, rows + 4, LANES), f32)],
        compiler_params=PARAMS,
        name="cone",
    )(*blocks, scale)


def solution(mesh):
    return jax.shard_map(
        local,
        mesh=mesh,
        in_specs=(P(None, None, "gx", "gy", None), P("gx", "gy", None), P("gx", "gy", None)),
        out_specs=P("gx", "gy", None),
        check_vma=False,
    )
```

```python
import functools
import math

import jax
import jax.numpy as jnp
from jax import lax
from jax.experimental import pallas as pl
from jax.experimental.pallas import tpu as pltpu
from jax.sharding import PartitionSpec as P

LEVELS = 16
LOAD = 0.2
LANES = 128
POISSON = 0.3
LAME = POISSON / ((1.0 + POISSON) * (1.0 - 2.0 * POISSON))
SHEAR = 1.0 / (2.0 * (1.0 + POISSON))
DIAGONAL = (LAME + 2.0 * SHEAR) / 9.0 + 2.0 * SHEAR / 9.0
VMEM = pl.BlockSpec(memory_space=pltpu.VMEM)
PARAMS = pltpu.CompilerParams(vmem_limit_bytes=30 * 2**20)
f32 = jnp.float32
bf16 = jnp.bfloat16


def up8(count):
    return -(-count // 8) * 8


def shift_down(value):
    lane = lax.broadcasted_iota(jnp.int32, value.shape, value.ndim - 1)
    rolled = pltpu.roll(value, LANES - 1, value.ndim - 1)
    return jnp.where(lane == LANES - 1, 0.0, rolled)


def shift_up(value):
    lane = lax.broadcasted_iota(jnp.int32, value.shape, value.ndim - 1)
    return jnp.where(lane == 0, 0.0, pltpu.roll(value, 1, value.ndim - 1))


def unrolled(count, factor, body):
    def turn(step, _):
        for offset in range(factor):
            body(step * factor + offset)
        return 0

    turns = count // factor
    if turns:
        lax.fori_loop(0, turns, turn, 0)
    for index in range(turns * factor, count):
        body(index)


def split(value):
    high = value.astype(bf16)
    return high, (value - high.astype(f32)).astype(bf16)


def modes_of(lower, upper):
    out = [[[[None] * 3 for _ in range(2)] for _ in range(2)] for _ in range(2)]
    for a in range(2):
        for c in range(2):
            for k in range(3):
                if a or c:
                    out[a][0][c][k] = lower[a][c][k] + upper[a][c][k]
                out[a][1][c][k] = upper[a][c][k] - lower[a][c][k]
    return out


PAIRS = (((1, 1, 0, 0), (0, 1, 1, 2)), ((1, 0, 1, 0), (0, 1, 1, 1)), ((1, 1, 0, 1), (1, 0, 1, 2)))
TRIPLE = ((0, 1, 1, 0), (1, 0, 1, 1), (1, 1, 0, 2))
SHEARS = (((0, 1, 0, 0), (1, 0, 0, 1)), ((0, 0, 1, 0), (1, 0, 0, 2)), ((0, 0, 1, 1), (0, 1, 0, 2)))
AXIAL = ((1, 0, 0, 0), (0, 1, 0, 1), (0, 0, 1, 2))


def at(modes, place):
    a, b, c, k = place
    return modes[a][b][c][k]


def mode_forces(modes, stiff):
    out = [[[[None] * 3 for _ in range(2)] for _ in range(2)] for _ in range(2)]

    def put(place, value):
        a, b, c, k = place
        out[a][b][c][k] = value

    shear = stiff * (SHEAR / 16)
    for first, second in SHEARS:
        force = shear * (at(modes, first) + at(modes, second))
        put(first, force)
        put(second, force)
    one, two, three = (at(modes, place) for place in AXIAL)
    volume = (stiff * (LAME / 16)) * (one + two + three)
    axial = stiff * (SHEAR / 8)
    for place in AXIAL:
        put(place, volume + axial * at(modes, place))
    own, cross = stiff * ((LAME + 3 * SHEAR) / 48), stiff * (LAME / 48)
    for first, second in PAIRS:
        one, two = at(modes, first), at(modes, second)
        put(first, own * one + cross * two)
        put(second, own * two + cross * one)
    twist = stiff * (SHEAR / 48)
    one, two, three = (at(modes, place) for place in TRIPLE)
    total = one + two + three
    for place in TRIPLE:
        put(place, twist * (total + at(modes, place)))
    last = stiff * ((LAME + 4 * SHEAR) / 144)
    for k in range(3):
        put((1, 1, 1, k), last * modes[1][1][1][k])
    return out


def mode_energy(modes):
    def square(value):
        return value * value

    shear = None
    for first, second in SHEARS:
        term = square(at(modes, first) + at(modes, second))
        shear = term if shear is None else shear + term
    one, two, three = (at(modes, place) for place in AXIAL)
    energy = (SHEAR / 16) * shear + (LAME / 16) * square(one + two + three)
    energy = energy + (SHEAR / 8) * (square(one) + square(two) + square(three))
    squares, products = None, None
    for first, second in PAIRS:
        one, two = at(modes, first), at(modes, second)
        term, product = square(one) + square(two), one * two
        squares = term if squares is None else squares + term
        products = product if products is None else products + product
    energy = energy + ((LAME + 3 * SHEAR) / 48) * squares + (LAME / 24) * products
    one, two, three = (at(modes, place) for place in TRIPLE)
    twist = square(one + two + three) + square(one) + square(two) + square(three)
    energy = energy + (SHEAR / 48) * twist
    last = square(modes[1][1][1][0]) + square(modes[1][1][1][1]) + square(modes[1][1][1][2])
    return energy + ((LAME + 4 * SHEAR) / 144) * last


def x_modes(find, plane, row, tile, cases):
    sums, diffs, columns, column = find(row)
    out = [[[None] * 3 for _ in range(2)] for _ in range(2)]
    for c, ref in enumerate((sums, diffs)):
        for k in range(3):
            rows = pl.ds(pl.multiple_of(k * cases + tile * 8, 8), 8)
            one = ref[plane * columns + column, rows, :]
            two = ref[(plane + 1) * columns + column, rows, :]
            out[0][c][k] = one + two
            out[1][c][k] = two - one
    return out


def whole(sums, diffs, columns):
    return lambda row: (sums, diffs, columns, row)


def apply_elements(find, stiff_ref, acc_s, acc_d, planes, rows, kept, stiff_x, stiff_y, cases):
    columns = len(kept)
    tiles = cases // 8
    for column in range(columns):
        acc_s[column] = jnp.zeros(acc_s.shape[1:], f32)
        acc_d[column] = jnp.zeros(acc_d.shape[1:], f32)

    def step(index, _):
        plane, tile = index // tiles, index % tiles

        def emit(row, total):
            if row not in kept:
                return
            for c, acc in enumerate((acc_s, acc_d)):
                for k in range(3):
                    lines = pl.ds(pl.multiple_of(k * cases + tile * 8, 8), 8)
                    low = plane * columns + row - kept[0]
                    acc[low, lines, :] += total[0][c][k] - total[1][c][k]
                    acc[low + columns, lines, :] = total[0][c][k] + total[1][c][k]

        lower = x_modes(find, plane, 0, tile, cases)
        carry = None
        for row in range(rows):
            upper = x_modes(find, plane, row + 1, tile, cases)
            stiff = jnp.broadcast_to(
                stiff_ref[plane + stiff_x, pl.ds(row + stiff_y, 1), :], (8, LANES)
            )
            forces = mode_forces(modes_of(lower, upper), stiff)
            here = [[[None] * 3 for _ in range(2)] for _ in range(2)]
            following = [[[None] * 3 for _ in range(2)] for _ in range(2)]
            for a in range(2):
                for c in range(2):
                    for k in range(3):
                        one, two = forces[a][0][c][k], forces[a][1][c][k]
                        if one is None:
                            here[a][c][k] = -two if carry is None else carry[a][c][k] - two
                            following[a][c][k] = two
                        else:
                            low = one - two
                            here[a][c][k] = low if carry is None else carry[a][c][k] + low
                            following[a][c][k] = one + two
            emit(row, here)
            carry, lower = following, upper
        emit(rows, carry)
        return 0

    lax.fori_loop(0, planes * tiles, step, 0)


def fill(source, base, sizes, ref, xs, ys, code_xs, code_ys):
    planes, rows, cases = sizes
    block = 3 * cases
    line = 0
    for x in xs:
        start = (x * rows + ys[0]) * block
        count = len(ys) * block
        ref[line : line + count, :] = source[start : start + count, :]
        line += count
    for x in code_xs:
        start = base + x * rows + code_ys[0]
        ref[line : line + len(code_ys), :] = source[start : start + len(code_ys), :]
        line += len(code_ys)
    if line < ref.shape[0]:
        ref[line:, :] = jnp.zeros((ref.shape[0] - line, LANES), f32)


def pack_kernel(sizes, forces, codes, own, edge):
    planes, rows, cases = sizes
    block = 3 * cases
    base = planes * rows * block
    for x in range(planes):
        own[base + x * rows : base + (x + 1) * rows, :] = codes[x]
        scale = jnp.where(codes[x] > 0.0, LOAD, 0.0)
        for k in range(3):
            for c in range(cases):
                start = x * rows * block + k * cases + c
                own[pl.ds(start, rows, stride=block), :] = forces[k, c, x] * scale

    even = lax.axis_index("gx") % 2 == 0
    size = rows * block
    for line in range(0, size, block):
        high = lines(own, (planes - 1) * size + line, block)
        edge[line : line + block, :] = jnp.where(even, lines(own, line, block), high)
    high = lines(own, base + (planes - 2) * rows, 2 * rows)
    edge[size:, :] = jnp.where(even, lines(own, base, 2 * rows), high)


def second_kernel(sizes, begun, own, second):
    _, rows, cases = sizes
    size = rows * 3 * cases
    second[...] = lines(own, size, size)


def rows_kernel(sizes, own, ym, yp):
    planes, rows, cases = sizes
    base = planes * rows * 3 * cases
    every_x = range(planes)
    fill(own, base, sizes, ym, every_x, (0, 1), every_x, (0, 1))
    fill(own, base, sizes, yp, every_x, (rows - 1,), every_x, (rows - 2, rows - 1))


def corner_kernel(sizes, ym, yp, out):
    planes, rows, cases = sizes
    block = 3 * cases
    even = lax.axis_index("gx") % 2 == 0
    line = 0
    for source, width in ((ym, 1), (yp, 2)):
        size = width * block
        parts = [(at, (planes - 2) * size + at, block) for at in range(0, 2 * size, block)]
        parts.append((planes * size, planes * size + (planes - 2) * 2, 4))
        for low, high, count in parts:
            value = lines(source, low, count)
            if low != high:
                value = jnp.where(even, value, lines(source, high, count))
            out[line : line + count, :] = value
            line += count
        out[line : line + 4, :] = jnp.zeros((4, LANES), f32)
        line += 4


def lines(ref, start, count):
    return ref[start : start + count, :]


def inside(ref, x, y, rows, block):
    return lines(ref, (x * rows + y) * block, block)


def beyond(refs, slot, y, rows, block):
    below, above = refs
    if y < 0:
        return lines(below, slot * block, block)
    return lines(above, (slot * 2 + y - rows) * block, block)


def beyond_codes(refs, slots, slot, y, block):
    below, above = refs
    if y < 0:
        return lines(below, slots * block + slot * 2, 2)
    return lines(above, slots * 2 * block + slot * 2, 2)


def corner(ref, slot, y, rows, block):
    start = slot * block if y < 0 else 2 * block + 8 + (slot * 2 + y - rows) * block
    return lines(ref, start, block)


def corner_codes(ref, slot, y, block):
    return lines(ref, (2 * block if y < 0 else 6 * block + 8) + slot * 2, 2)


def node_inverse(signed, count, out):
    planes = signed.shape[0]
    for x in range(1, planes):
        codes = signed[x, 0 : count + 1, :]
        total = jnp.abs(signed[x - 1, 0 : count + 1, :]) + jnp.abs(codes)
        total = total[:-1] + total[1:]
        total = total + shift_up(total)
        free = codes[1:] > 0.0
        value = 1.0 / (DIAGONAL * jnp.where(free, total, 1.0))
        out[x - 1, 0:count, :] = jnp.where(free, value, 0.0)
    for x in range(planes):
        signed[x] = jnp.abs(signed[x])


def place_column(sums, diffs, column, value):
    moved = shift_down(value)
    sums[column] = value + moved
    diffs[column] = moved - value


def early_kernel(
    sizes, own, pair, ym, yp, ym_pair, yp_pair, start, sums, diffs, acc_s, acc_d,
    stiff_ref, inverse,
):
    planes, rows, cases = sizes
    block = 3 * cases
    ys = rows + 3
    even = lax.axis_index("gx") % 2 == 0
    y_own, y_pair = (ym, yp), (ym_pair, yp_pair)

    def both_ways(w, read):
        low = read(True, w + 1) if w + 1 < planes else read(False, w + 1 - planes)
        high = read(False, planes + w - 1) if w < 1 else read(True, w - 1)
        return jnp.where(even, low, high)

    def codes(w, y):
        def read(mine, x):
            if y == 0:
                return lines(own if mine else pair, (planes * block + x) * rows, rows)
            return beyond_codes(y_own if mine else y_pair, planes, x, y, block)

        return both_ways(w, read)

    for w in range(-1, planes + 1):
        for y, count in ((-2, 2), (0, rows), (rows, 2)):
            stiff_ref[w + 1, y + 2 : y + 2 + count, :] = codes(w, y)
    node_inverse(stiff_ref, ys, inverse)
    for w in range(planes + 1):
        for y in range(-1, rows + 2):

            def read(mine, x):
                if 0 <= y < rows:
                    return inside(own if mine else pair, x, y, rows, block)
                return beyond(y_own if mine else y_pair, x, y, rows, block)

            value = both_ways(w, read) * inverse[w, y + 1 : y + 2, :]
            column = w * ys + y + 1
            start[column] = value
            place_column(sums, diffs, column, value)
    kept = range(1, rows + 2)
    find = whole(sums, diffs, ys)
    apply_elements(find, stiff_ref, acc_s, acc_d, planes, rows + 2, kept, 1, 1, cases)


def core_rows(rows):
    return range(2, rows - 1)


def rim_rows(rows):
    return (0, 1, rows - 1, rows)


def core_columns(planes, rows):
    core = core_rows(rows)
    inner, outer = core[1:-1], (core[0], core[-1])
    first = [(x, y) for x in range(planes + 1) for y in inner]
    last = [(x, y) for x in range(planes + 1) for y in outer]
    return first, last, planes * len(inner), planes * len(outer)


def rim_columns(planes, rows):
    own = [(x, y) for x in range(planes) for y in rim_rows(rows) if y < rows]
    beyond_own = [(x, rows) for x in range(planes)] + [(planes, y) for y in rim_rows(rows)]
    return own + beyond_own, len(own)


def merged(x, planes, even, early, near):
    low = ([x - 1] if x >= 1 else [], [x + 1] if x <= 1 else [])
    high = ([x + 1] if x < planes else [], [x - planes + 1] if x >= planes - 1 else [])
    if low[0] and low[1] and high[0] and high[1]:
        one = early(jnp.where(even, low[0][0], high[0][0]))
        return one + near(jnp.where(even, low[1][0], high[1][0]))

    def read(places):
        found = [early(w) for w in places[0]] + [near(v) for v in places[1]]
        return found[0] if len(found) == 1 else found[0] + found[1]

    return jnp.where(even, read(low), read(high))


def direction_at(x, planes, even, early, middle):
    if x == 0:
        return jnp.where(even, middle, early(1))
    if x == planes:
        return jnp.where(even, early(planes - 1), middle)
    return early(jnp.where(even, x - 1, x + 1))


def keep_pair(ref, place, one, two, cases):
    for k in range(3):
        part = slice(k * cases, (k + 1) * cases)
        high, rest = split(jnp.concatenate([one[part], two[part]], 0))
        lane = pl.ds(pl.multiple_of((place * 3 + k) * LANES, LANES), LANES)
        ref[0 : 2 * cases, lane] = high
        ref[2 * cases : 4 * cases, lane] = rest


def keep_split(ref, line, place, value, cases):
    for k in range(3):
        part = value[k * cases : (k + 1) * cases]
        high = part.astype(bf16).astype(f32)
        lane = slice((place * 3 + k) * LANES, (place * 3 + k + 1) * LANES)
        both = jnp.concatenate([high, part - high], 0).astype(bf16)
        ref[line : line + 2 * cases, lane] = both


def folded(value):
    half = value.shape[0] // 2
    return value[:half] + value[half:]


def products(first, second, cases):
    contract = (((1,), (1,)), ((), ()))
    out = lax.dot_general(first, second, contract, preferred_element_type=f32)
    return out[:, : 2 * cases] + out[:, 2 * cases :]


def folds(cases):
    two, count, rest = 2 * cases, 5 * cases // 12, cases // 6
    first, part = 2 * two, LANES - 2 * two
    return (
        ((slice(0, count), slice(0, two)), (slice(0, count), slice(0, two))),
        ((slice(0, count), slice(two, first)), (slice(count, 2 * count), slice(0, two))),
        ((slice(0, rest), slice(first, LANES)), (slice(2 * count, cases), slice(0, part))),
        (
            (slice(rest, 2 * rest), slice(first, first + two - part)),
            (slice(2 * count, cases), slice(part, two)),
        ),
    )


def diagonal_place(cases, index):
    line = cases // 3 + index
    return slice(line, line + 1), slice(4 * cases, 5 * cases)


def middle_kernel(
    sizes, own, pair, edge, second, start, sums_e, diffs_e, acc_se, acc_de,
    sums, diffs, middle, acc_s, acc_d, w_sums, w_diffs, both_out, gram_out, other_out,
    acc2_s, acc2_d, stiff_ref, inverse, right, again,
):
    planes, rows, cases = sizes
    block = 3 * cases
    ys, nodes_y, inner = rows + 3, rows + 1, rows - 1
    core = core_rows(rows)
    even = lax.axis_index("gx") % 2 == 0

    def codes(x):
        if 0 <= x < planes:
            return lines(own, (planes * block + x) * rows, rows)
        slot = x + 2 if x < 0 else x - planes
        outer = lines(edge, (block + slot) * rows, rows)
        if x < 0:
            return jnp.where(even, outer, lines(pair, (planes * block + planes + x) * rows, rows))
        return jnp.where(even, lines(pair, (planes * block + slot) * rows, rows), outer)

    for x in range(-2, planes + 2):
        stiff_ref[x + 2, 0:rows, :] = codes(x)
    node_inverse(stiff_ref, inner, inverse)

    def place(v, x, ref, slot):
        for y in range(1, rows):
            value = inside(ref, slot, y, rows, block) * inverse[x + 1, y - 1 : y, :]
            if v == 1:
                middle[y - 1] = value
            place_column(sums, diffs, v * inner + y - 1, value)

    def copy(v, w):
        for y in range(1, rows):
            sums[v * inner + y - 1] = sums_e[w * ys + y + 1]
            diffs[v * inner + y - 1] = diffs_e[w * ys + y + 1]

    @pl.when(even)
    def _():
        place(0, -1, edge, 0)
        place(1, 0, own, 0)
        copy(2, 0)

    @pl.when(jnp.logical_not(even))
    def _():
        copy(0, planes)
        place(1, planes, edge, 0)
        place(2, planes + 1, second, 0)

    layer = jnp.where(even, 1, planes + 1)
    find = whole(sums, diffs, inner)
    apply_elements(find, stiff_ref, acc_s, acc_d, 2, rows - 2, range(inner), layer, 1, cases)

    def image(x, y, place):
        def total(early, near):
            return merged(
                x, planes, even, lambda w: early[w * nodes_y + y],
                lambda v: near[v * inner + y - 1],
            )

        s, d = total(acc_se, acc_s), total(acc_de, acc_d)
        force = s - d + shift_up(s + d)
        scaled = force * inverse[x + 1, pl.ds(y - 1, 1), :]
        place_column(w_sums, w_diffs, x * len(core) + y - core[0], scaled)
        value = direction_at(x, planes, even, lambda w: start[w * ys + y + 1], middle[y - 1])
        keep_pair(both_out, place, value, scaled, cases)
        return force

    inner_columns, outer_columns, inner_own, outer_own = core_columns(planes, rows)
    count = len(inner_columns)
    for index, (x, y) in enumerate(inner_columns + outer_columns):
        force = image(x, y, index)
        if x < planes:
            ref, place = (again, index) if index < count else (right, index - count)
            keep_pair(ref, place, inside(own, x, y, rows, block), force, cases)
    width, two = 3 * LANES, 2 * cases
    again[: 2 * two, inner_own * width :] = jnp.zeros((2 * two, (count - inner_own) * width), bf16)

    find = whole(w_sums, w_diffs, len(core))
    kept = range(len(core))
    apply_elements(
        find, stiff_ref, acc2_s, acc2_d, planes, len(core) - 1, kept, 2, core[0], cases
    )
    for index, (x, y) in enumerate(inner_columns):
        column = x * len(core) + y - core[0]
        s, d = acc2_s[column], acc2_d[column]
        keep_split(again, 2 * two, index, s - d + shift_up(s + d), cases)
    product = products(again[...], both_out[:, : count * width], cases)
    outer_part = both_out[:, count * width : (count + outer_own) * width]
    gram_out[...] = folded(product[: 2 * two]) + folded(products(right[...], outer_part, cases))
    other_out[...] = folded(product[2 * two :])


def main_kernel(
    sizes, own, pair, edge, second, ym, yp, ym_pair, yp_pair, corners,
    start, sums_e, diffs_e, acc_se, acc_de,
    sums_m, diffs_m, middle_m, acc_sm, acc_dm, w_sm, w_dm, both_m, gram_m,
    other_m, acc2_sm, acc2_dm, both_out, system_out, stiff_ref, inverse,
    middle, sums, diffs, acc_s0, acc_d0, acc_s1, acc_d1, w_sums, w_diffs,
    acc2_s0, acc2_d0, acc2_s1, acc2_d1, right, second_m, table, dense,
):
    planes, rows, cases = sizes
    block = 3 * cases
    ys, nodes_y, inner = rows + 3, rows + 1, rows - 1
    core, rim = core_rows(rows), rim_rows(rows)
    columns, own_count = rim_columns(planes, rows)
    even = lax.axis_index("gx") % 2 == 0
    y_own, y_pair = (ym, yp), (ym_pair, yp_pair)

    def codes(x, y):
        def read(mine, plane):
            if y == 0:
                return lines(own if mine else pair, (planes * block + plane) * rows, rows)
            return beyond_codes(y_own if mine else y_pair, planes, plane, y, block)

        if 0 <= x < planes:
            return read(True, x)
        slot = x + 2 if x < 0 else x - planes
        if y == 0:
            outer = lines(edge, (block + slot) * rows, rows)
        else:
            outer = corner_codes(corners, slot, y, block)
        within = read(False, planes + x if x < 0 else x - planes)
        return jnp.where(even, outer, within) if x < 0 else jnp.where(even, within, outer)

    for x in range(-2, planes + 2):
        for y, count in ((-2, 2), (0, rows), (rows, 2)):
            stiff_ref[x + 2, y + 2 : y + 2 + count, :] = codes(x, y)
    node_inverse(stiff_ref, ys, inverse)

    sides = (-1, 0, rows, rows + 1)

    def place(v, x, ref, slot, beyond_at):
        for i, y in enumerate(sides):
            value = inside(ref, slot, y, rows, block) if y == 0 else beyond_at(y)
            value = value * inverse[x + 1, y + 1 : y + 2, :]
            if v == 1 and y in (0, rows):
                middle[y // rows] = value
            place_column(sums, diffs, v * 4 + i, value)

    def copy(v, w):
        for i, y in enumerate(sides):
            sums[v * 4 + i] = sums_e[w * ys + y + 1]
            diffs[v * 4 + i] = diffs_e[w * ys + y + 1]

    @pl.when(even)
    def _():
        place(0, -1, edge, 0, lambda y: corner(corners, 1, y, rows, block))
        place(1, 0, own, 0, lambda y: beyond(y_own, 0, y, rows, block))
        copy(2, 0)

    @pl.when(jnp.logical_not(even))
    def _():
        copy(0, planes)
        place(1, planes, edge, 0, lambda y: corner(corners, 0, y, rows, block))
        place(2, planes + 1, second, 0, lambda y: corner(corners, 1, y, rows, block))

    def find_low(row):
        return (sums, diffs, 4, row) if row < 2 else (sums_m, diffs_m, inner, 0)

    def find_high(row):
        return (sums, diffs, 4, row + 1) if row else (sums_m, diffs_m, inner, inner - 1)

    layer = jnp.where(even, 1, planes + 1)
    apply_elements(find_low, stiff_ref, acc_s0, acc_d0, 2, 2, range(1, 3), layer, 1, cases)
    apply_elements(find_high, stiff_ref, acc_s1, acc_d1, 2, 2, range(2), layer, rows + 1, cases)

    def image(x, y, place):
        def total(early, near, low, high):
            def outer(v):
                value = low[v * 2 + y] if y < 2 else high[v * 2 + y - inner]
                return value + near[v * inner + y - 1] if y in (1, inner) else value

            return merged(x, planes, even, lambda w: early[w * nodes_y + y], outer)

        s = total(acc_se, acc_sm, acc_s0, acc_s1)
        d = total(acc_de, acc_dm, acc_d0, acc_d1)
        force = s - d + shift_up(s + d)
        scaled = force * inverse[x + 1, y + 1 : y + 2, :]
        place_column(w_sums, w_diffs, x * len(rim) + rim.index(y), scaled)
        inner_middle = middle_m[y - 1] if y in (1, inner) else middle[y // rows]
        value = direction_at(x, planes, even, lambda w: start[w * ys + y + 1], inner_middle)
        keep_pair(both_out, place, value, scaled, cases)
        return force

    for index, (x, y) in enumerate(columns):
        force = image(x, y, index)
        if index < own_count:
            keep_pair(right, index, inside(own, x, y, rows, block), force, cases)

    def find(row):
        if row in rim:
            return w_sums, w_diffs, len(rim), rim.index(row)
        return w_sm, w_dm, len(core), row - core[0]

    def find_last(row):
        return find(row + rows - 2)

    low, high = (acc2_s0, acc2_d0), (acc2_s1, acc2_d1)
    apply_elements(find, stiff_ref, *low, planes, 2, range(3), 2, 2, cases)
    apply_elements(find_last, stiff_ref, *high, planes, 2, range(3), 2, rows, cases)

    def second_force(x, y):
        s, d = None, None
        for parts, width, first in (
            (low, 3, 0), ((acc2_sm, acc2_dm), len(core), core[0]), (high, 3, rows - 2)
        ):
            if first <= y < first + width:
                column = x * width + y - first
                more = parts[0][column], parts[1][column]
                s, d = more if s is None else (s + more[0], d + more[1])
        return s - d + shift_up(s + d)

    inner_columns, outer_columns, _, _ = core_columns(planes, rows)
    two = 2 * cases
    for index, (x, y) in enumerate(outer_columns):
        keep_split(second_m, 0, index, second_force(x, y), cases)
    for index, (x, y) in enumerate(columns):
        keep_split(right, 2 * two, index, second_force(x, y), cases)
    lane = own_count * 3 * LANES
    right[: 2 * two, lane:] = jnp.zeros((2 * two, right.shape[1] - lane), bf16)

    product = products(right[...], both_out[...], cases)
    more = products(second_m[...], both_m[:, len(inner_columns) * 3 * LANES :], cases)
    gram = folded(product[: 2 * two]) + gram_m[...]
    other = folded(product[2 * two :]) + folded(more) + other_m[...]
    row = lax.broadcasted_iota(jnp.int32, (cases, cases), 0)
    column = lax.broadcasted_iota(jnp.int32, (cases, cases), 1)
    load_load, load_image = gram[:cases, :cases], gram[cases:, :cases]
    mixed, image_image = other[:, :cases], other[:, cases:]
    table[:, 0:cases] = jnp.where(row <= column, load_load, load_image)
    table[:, cases:two] = jnp.where(row <= column, mixed, image_image)
    dense[...] = jnp.zeros(dense.shape, f32)
    for target, source in folds(cases):
        dense[target] = table[source]
    for index, value in enumerate((load_image, image_image)):
        diagonal = jnp.sum(jnp.where(row == column, value, 0.0), axis=0, keepdims=True)
        dense[diagonal_place(cases, index)] = diagonal
    depth = system_out.shape[2]
    for index in range(system_out.shape[0]):
        for part in range(system_out.shape[1]):
            system_out[index, part] = dense[part * depth : (part + 1) * depth, :]


def solve_kernel(
    sizes, system, both_m, both_r, codes, out, mixing, sums, diffs, energy, square, full, dense
):
    planes, rows, cases = sizes
    two = 2 * cases
    nodes_y = rows + 1
    count = planes * rows
    total = jnp.sum(system[...], axis=0)
    depth = system.shape[2]
    for part in range(system.shape[1]):
        dense[part * depth : (part + 1) * depth, :] = total[part]
    square[...] = jnp.zeros(square.shape, f32)
    for source, target in folds(cases):
        square[target] = dense[source]
    value, turned = square[0:cases, :], jnp.transpose(square[...])
    line = lax.broadcasted_iota(jnp.int32, (cases, cases), 0)
    place = lax.broadcasted_iota(jnp.int32, (cases, cases), 1)

    def mended(start, diagonal=None):
        kept, other = value[:, start : start + cases], turned[start : start + cases, :cases]
        if diagonal is None:
            return jnp.where(line <= place, kept, other)
        inner = jnp.where(line < place, other, dense[diagonal_place(cases, diagonal)])
        return jnp.where(line > place, kept, inner)

    load_image, mixed = mended(0, 0), mended(cases)
    parts = ((load_image, mixed), (mixed, mended(cases, 1)), (mended(0), load_image))
    full[...] = jnp.zeros(full.shape, f32)
    for index, (left, right) in enumerate(parts):
        full[index * cases : (index + 1) * cases, 0:cases] = left
        full[index * cases : (index + 1) * cases, cases:two] = right
    table = full[...]
    lane = lax.broadcasted_iota(jnp.int32, (1, LANES), 1)
    gone, wide = 0, 8
    for pivot in range(0, two, wide):
        drop = pivot // 8 * 8 - gone
        table = table[drop:]
        gone += drop
        line = pivot - gone
        inner = (lane >= pivot) & (lane < pivot + wide)
        found = [table[line + p : line + p + 1, :] for p in range(wide)]
        block = [
            [jnp.broadcast_to(row[:, pivot + q : pivot + q + 1], row.shape) for q in range(wide)]
            for row in found
        ]
        solved = [
            jnp.where(lane == pivot + p, -1.0, jnp.where(inner, 0.0, found[p]))
            for p in range(wide)
        ]
        for p in range(wide):
            inverse = 1.0 / block[p][p]
            solved[p] = solved[p] * inverse
            block[p] = [value * inverse for value in block[p]]
            for q in range(wide):
                if q != p:
                    factor = block[q][p]
                    solved[q] = solved[q] - factor * solved[p]
                    for r in range(p + 1, wide):
                        block[q][r] = block[q][r] - factor * block[p][r]
        update = None
        for q in range(wide):
            term = table[:, pivot + q : pivot + q + 1] * solved[q]
            update = term if update is None else update + term
        table = jnp.where(inner, 0.0, table) - update
    answer = table[two - gone :, :two]
    high = answer.astype(bf16).astype(f32)
    mixing[...] = jnp.zeros(mixing.shape, f32)
    mixing[0:cases, 0:two] = high
    mixing[0:cases, two : 2 * two] = high
    mixing[cases:two, 0:two] = answer - high
    mix = mixing[...][:, : 2 * two].astype(bf16)

    def combined(ref, place, width):
        value = jnp.dot(
            mix, ref[:, place * 3 * LANES : (place + width) * 3 * LANES], preferred_element_type=f32
        )
        return value[:cases] + value[cases:]

    def keep(value, index, column):
        for k in range(3):
            part = value[:, (index * 3 + k) * LANES : (index * 3 + k + 1) * LANES]
            moved = shift_down(part)
            sums[column, k * cases : (k + 1) * cases, :] = part + moved
            diffs[column, k * cases : (k + 1) * cases, :] = moved - part

    inner_columns, outer_columns, _, _ = core_columns(planes, rows)
    columns, _ = rim_columns(planes, rows)
    for ref, columns in ((both_m, inner_columns + outer_columns), (both_r, columns)):
        for start in range(0, len(columns), 6):
            some = columns[start : start + 6]
            value = combined(ref, start, len(some))
            for index, (x, y) in enumerate(some):
                keep(value, index, x * nodes_y + y)

    find = whole(sums, diffs, nodes_y)
    tiles = cases // 8

    def step(plane, _):
        for tile in range(tiles):
            lower = x_modes(find, plane, 0, tile, cases)
            for row in range(rows):
                upper = x_modes(find, plane, row + 1, tile, cases)
                part = mode_energy(modes_of(lower, upper))
                if tile == 0:
                    energy[row] = part
                else:
                    energy[row] += part
                lower = upper
        total = jnp.sum(energy[...], axis=1)
        total = (-3.0 / cases) * jnp.abs(codes[plane]) * total
        for index in range(out.shape[0]):
            out[index, plane] = total
        return 0

    lax.fori_loop(0, planes, step, 0)


def smooth(ref, x, rows):
    weight = [2.5 - math.sqrt(q) for q in range(7)]
    near = {}
    for dx in range(-2, 3):
        for dy in range(-2, 3):
            q = dx * dx + dy * dy
            if q <= 5:
                value = ref[x + 2 + dx, 2 + dy : 2 + dy + rows, :]
                near[q] = value if q not in near else near[q] + value
    result = None
    for dz in range(3):
        part = None
        for q, value in near.items():
            if q + dz * dz <= 6:
                term = weight[q + dz * dz] * value
                part = term if part is None else part + term
        if dz == 0:
            result = part
        else:
            place = lax.broadcasted_iota(jnp.int32, part.shape, 1)
            forward = jnp.where(place >= LANES - dz, 0.0, pltpu.roll(part, LANES - dz, 1))
            backward = jnp.where(place < dz, 0.0, pltpu.roll(part, dz, 1))
            result = result + (forward + backward)
    return result


def scale_kernel(sizes, counts, levels, out, there):
    planes, rows, _ = sizes
    y = lax.broadcasted_iota(jnp.int32, (rows + 4, LANES), 0)
    y = y + (lax.axis_index("gy") * rows - 2)
    in_y = (y >= 0) & (y < counts[1] * rows)
    for x in range(planes + 4):
        global_x = lax.axis_index("gx") * planes + (x - 2)
        in_x = (global_x >= 0) & (global_x < counts[0] * planes)
        there[x] = jnp.where(in_y & in_x, 1.0, 0.0)
    for x in range(planes):
        density = 0.3 + 0.7 * levels[x].astype(f32) / (LEVELS - 1)
        out[x] = 1.0 / (density * smooth(there, x, rows))


def filter_kernel(sizes, counts, blocks, blocks_pair, scale, out, wide):
    planes, rows, _ = sizes
    sides_x = ((-1, planes - 2, planes, 0), (0, 0, planes, 2), (1, 0, 2, 2 + planes))
    sides_y = ((-1, rows - 2, rows, 0), (0, 0, rows, 2), (1, 0, 2, 2 + rows))
    for step_x, x0, x1, to_x in sides_x:
        for step_y, y0, y1, to_y in sides_y:
            at_x = lax.axis_index("gx") + step_x
            at_y = lax.axis_index("gy") + step_y
            inside = (at_x >= 0) & (at_x < counts[0]) & (at_y >= 0) & (at_y < counts[1])
            index = jnp.where(inside, at_x // 2 * counts[1] + at_y, 0)
            value = (blocks_pair if step_x else blocks)[index, x0:x1, y0:y1, :]
            wide[to_x : to_x + x1 - x0, to_y : to_y + y1 - y0, :] = jnp.where(inside, value, 0.0)
    for x in range(planes):
        out[x] = smooth(wide, x, rows) * scale[x]


def local(forces, levels, supports):
    _, cases, planes, rows, _ = forces.shape
    sizes = (planes, rows, cases)
    block = 3 * cases
    count_x, count_y = lax.axis_size("gx"), lax.axis_size("gy")

    def shape(blocks, codes):
        return jax.ShapeDtypeStruct((blocks * block + up8(codes), LANES), f32)

    density = 0.3 + 0.7 * levels.astype(f32) / (LEVELS - 1)
    codes = density * density * density
    codes = jnp.where(supports == 0, codes, -codes)
    counts = (count_x, count_y)
    own, edge = pl.pallas_call(
        functools.partial(pack_kernel, sizes),
        out_shape=[shape(planes * rows, planes * rows), shape(rows, 2 * rows)],
        in_specs=[VMEM] * 2,
        out_specs=[VMEM] * 2,
        compiler_params=PARAMS,
        name="pack",
    )(forces, codes)
    scale = pl.pallas_call(
        functools.partial(scale_kernel, sizes, counts),
        out_shape=jax.ShapeDtypeStruct((planes, rows, LANES), f32),
        in_specs=[VMEM],
        out_specs=VMEM,
        scratch_shapes=[pltpu.VMEM((planes + 4, rows + 4, LANES), f32)],
        compiler_params=PARAMS,
        name="scale",
    )(levels)

    def moved(value, axis, step):
        count = lax.axis_size(axis)
        pairs = [(i, i + step) for i in range(count) if 0 <= i + step < count]
        return lax.ppermute(value, axis, pairs)

    def links(first, step):
        return [(i, i + step) for i in range(first, count_x, 2) if 0 <= i + step < count_x]

    def swapped(value):
        return lax.ppermute(value, "gx", links(0, 1) + links(1, -1))

    def across(value):
        return lax.ppermute(value, "gx", links(1, 1) + links(2, -1))

    edge = across(edge)
    pair = swapped(own)
    own, pair = lax.optimization_barrier((own, pair))
    ym, yp = pl.pallas_call(
        functools.partial(rows_kernel, sizes),
        out_shape=[shape(2 * planes, 2 * planes), shape(planes, 2 * planes)],
        in_specs=[VMEM],
        out_specs=[VMEM] * 2,
        compiler_params=PARAMS,
        name="rows",
    )(own)
    from_yp, from_ym = moved(ym, "gy", -1), moved(yp, "gy", 1)
    second = pl.pallas_call(
        functools.partial(second_kernel, sizes),
        out_shape=shape(rows, 0),
        in_specs=[VMEM] * 2,
        out_specs=VMEM,
        compiler_params=PARAMS,
        name="second",
    )(swapped(codes), own)
    second = lax.ppermute(second, "gx", links(2, -1))
    pair_yp, pair_ym = swapped(from_yp), swapped(from_ym)
    from_ym, from_yp, edge = lax.optimization_barrier((from_ym, from_yp, edge))
    corners = across(
        pl.pallas_call(
            functools.partial(corner_kernel, sizes),
            out_shape=jax.ShapeDtypeStruct((6 * block + 16, LANES), f32),
            in_specs=[VMEM] * 2,
            out_specs=VMEM,
            compiler_params=PARAMS,
            name="corners",
        )(from_ym, from_yp)
    )

    devices = count_x * count_y
    nodes = (planes + 1) * (rows + 1)
    window = jax.ShapeDtypeStruct(((planes + 1) * (rows + 3), block, LANES), f32)
    partial_forces = jax.ShapeDtypeStruct((nodes, block, LANES), f32)
    early = pl.pallas_call(
        functools.partial(early_kernel, sizes),
        out_shape=[window] * 3 + [partial_forces] * 2,
        in_specs=[VMEM] * 6,
        out_specs=[VMEM] * 5,
        scratch_shapes=[
            pltpu.VMEM((planes + 2, up8(rows + 4), LANES), f32),
            pltpu.VMEM((planes + 1, up8(rows + 3), LANES), f32),
        ],
        compiler_params=PARAMS,
        cost_estimate=pl.CostEstimate(
            flops=200 * planes * rows * block * LANES, bytes_accessed=2**23, transcendentals=0
        ),
        name="early",
    )(own, pair, from_ym, from_yp, pair_ym, pair_yp)

    def columns(count):
        return jax.ShapeDtypeStruct((count, block, LANES), f32)

    def fields(lines, count):
        return jax.ShapeDtypeStruct((lines * cases, count * 3 * LANES), bf16)

    def scratch(value):
        return pltpu.VMEM(value.shape, value.dtype)

    core = len(core_rows(rows))
    middle = pl.pallas_call(
        functools.partial(middle_kernel, sizes),
        out_shape=[columns(3 * (rows - 1))] * 2
        + [columns(rows - 1)]
        + [columns(3 * (rows - 1))] * 2
        + [columns((planes + 1) * core)] * 2
        + [fields(4, (planes + 1) * core), jax.ShapeDtypeStruct((2 * cases, 2 * cases), f32)]
        + [jax.ShapeDtypeStruct((cases, 2 * cases), f32)]
        + [columns((planes + 1) * core)] * 2,
        in_specs=[VMEM] * 9,
        out_specs=[VMEM] * 12,
        scratch_shapes=[
            pltpu.VMEM((planes + 4, up8(rows), LANES), f32),
            pltpu.VMEM((planes + 3, up8(rows), LANES), f32),
            scratch(fields(4, planes * 2)),
            scratch(fields(6, (planes + 1) * (core - 2))),
        ],
        compiler_params=PARAMS,
        name="middle",
    )(own, pair, edge, second, *early)

    rim, _ = rim_columns(planes, rows)
    both, system = pl.pallas_call(
        functools.partial(main_kernel, sizes),
        out_shape=[
            fields(4, len(rim)),
            jax.ShapeDtypeStruct((devices, 5 * cases // 24, 2, LANES), f32),
        ],
        in_specs=[VMEM] * 26,
        out_specs=[VMEM] * 2,
        scratch_shapes=[
            pltpu.VMEM((planes + 4, up8(rows + 4), LANES), f32),
            pltpu.VMEM((planes + 3, up8(rows + 3), LANES), f32),
            scratch(columns(2)),
            *[scratch(columns(12))] * 2,
            *[scratch(columns(6))] * 4,
            *[scratch(columns((planes + 1) * 4))] * 2,
            *[scratch(columns((planes + 1) * 3))] * 4,
            scratch(fields(6, len(rim))),
            scratch(fields(2, (planes + 1) * 2)),
            pltpu.VMEM((cases, LANES), f32),
            pltpu.VMEM((5 * cases // 12, LANES), f32),
        ],
        compiler_params=PARAMS,
        name="operator",
    )(
        own, pair, edge, second, from_ym, from_yp, pair_ym, pair_yp, corners,
        *early, *middle,
    )

    groups = [
        [x * count_y + y for x in range(side, count_x, 2) for y in range(count_y)]
        for side in range(2)
    ]

    def gathered(copies):
        mine = lax.all_to_all(copies, ("gx", "gy"), 0, 0, axis_index_groups=groups)
        return mine, swapped(mine)

    system = lax.all_to_all(system, ("gx", "gy"), 0, 0)

    weighted = pl.pallas_call(
        functools.partial(solve_kernel, sizes),
        out_shape=jax.ShapeDtypeStruct((devices // 2, planes, rows, LANES), f32),
        in_specs=[VMEM] * 4,
        out_specs=VMEM,
        scratch_shapes=[
            pltpu.VMEM((2 * cases, LANES), f32),
            scratch(columns(nodes)),
            scratch(columns(nodes)),
            pltpu.VMEM((rows, 8, LANES), f32),
            pltpu.VMEM((LANES, LANES), f32),
            pltpu.VMEM((3 * cases, LANES), f32),
            pltpu.VMEM((5 * cases // 12, LANES), f32),
        ],
        compiler_params=PARAMS,
        name="solve",
    )(system, middle[7], both, codes)

    blocks = gathered(weighted)
    return pl.pallas_call(
        functools.partial(filter_kernel, sizes, counts),
        out_shape=jax.ShapeDtypeStruct((planes, rows, LANES), f32),
        in_specs=[VMEM] * 3,
        out_specs=VMEM,
        scratch_shapes=[pltpu.VMEM((planes + 4, rows + 4, LANES), f32)],
        compiler_params=PARAMS,
        name="cone",
    )(*blocks, scale)


def solution(mesh):
    return jax.shard_map(
        local,
        mesh=mesh,
        in_specs=(P(None, None, "gx", "gy", None), P("gx", "gy", None), P("gx", "gy", None)),
        out_specs=P("gx", "gy", None),
        check_vma=False,
    )
```

```python
import functools
import math

import jax
import jax.numpy as jnp
from jax import lax
from jax.experimental import pallas as pl
from jax.experimental.pallas import tpu as pltpu
from jax.sharding import PartitionSpec as P

LEVELS = 16
LOAD = 0.2
LANES = 128
POISSON = 0.3
LAME = POISSON / ((1.0 + POISSON) * (1.0 - 2.0 * POISSON))
SHEAR = 1.0 / (2.0 * (1.0 + POISSON))
DIAGONAL = (LAME + 2.0 * SHEAR) / 9.0 + 2.0 * SHEAR / 9.0
VMEM = pl.BlockSpec(memory_space=pltpu.VMEM)
PARAMS = pltpu.CompilerParams(vmem_limit_bytes=30 * 2**20)
f32 = jnp.float32
bf16 = jnp.bfloat16


def up8(count):
    return -(-count // 8) * 8


def shift_down(value):
    lane = lax.broadcasted_iota(jnp.int32, value.shape, value.ndim - 1)
    rolled = pltpu.roll(value, LANES - 1, value.ndim - 1)
    return jnp.where(lane == LANES - 1, 0.0, rolled)


def shift_up(value):
    lane = lax.broadcasted_iota(jnp.int32, value.shape, value.ndim - 1)
    return jnp.where(lane == 0, 0.0, pltpu.roll(value, 1, value.ndim - 1))


def unrolled(count, factor, body):
    def turn(step, _):
        for offset in range(factor):
            body(step * factor + offset)
        return 0

    turns = count // factor
    if turns:
        lax.fori_loop(0, turns, turn, 0)
    for index in range(turns * factor, count):
        body(index)


def split(value):
    high = value.astype(bf16)
    return high, (value - high.astype(f32)).astype(bf16)


def modes_of(lower, upper):
    out = [[[[None] * 3 for _ in range(2)] for _ in range(2)] for _ in range(2)]
    for a in range(2):
        for c in range(2):
            for k in range(3):
                if a or c:
                    out[a][0][c][k] = lower[a][c][k] + upper[a][c][k]
                out[a][1][c][k] = upper[a][c][k] - lower[a][c][k]
    return out


PAIRS = (((1, 1, 0, 0), (0, 1, 1, 2)), ((1, 0, 1, 0), (0, 1, 1, 1)), ((1, 1, 0, 1), (1, 0, 1, 2)))
TRIPLE = ((0, 1, 1, 0), (1, 0, 1, 1), (1, 1, 0, 2))
SHEARS = (((0, 1, 0, 0), (1, 0, 0, 1)), ((0, 0, 1, 0), (1, 0, 0, 2)), ((0, 0, 1, 1), (0, 1, 0, 2)))
AXIAL = ((1, 0, 0, 0), (0, 1, 0, 1), (0, 0, 1, 2))


def at(modes, place):
    a, b, c, k = place
    return modes[a][b][c][k]


def mode_forces(modes, stiff):
    out = [[[[None] * 3 for _ in range(2)] for _ in range(2)] for _ in range(2)]

    def put(place, value):
        a, b, c, k = place
        out[a][b][c][k] = value

    shear = stiff * (SHEAR / 16)
    for first, second in SHEARS:
        force = shear * (at(modes, first) + at(modes, second))
        put(first, force)
        put(second, force)
    one, two, three = (at(modes, place) for place in AXIAL)
    volume = (stiff * (LAME / 16)) * (one + two + three)
    axial = stiff * (SHEAR / 8)
    for place in AXIAL:
        put(place, volume + axial * at(modes, place))
    own, cross = stiff * ((LAME + 3 * SHEAR) / 48), stiff * (LAME / 48)
    for first, second in PAIRS:
        one, two = at(modes, first), at(modes, second)
        put(first, own * one + cross * two)
        put(second, own * two + cross * one)
    twist = stiff * (SHEAR / 48)
    one, two, three = (at(modes, place) for place in TRIPLE)
    total = one + two + three
    for place in TRIPLE:
        put(place, twist * (total + at(modes, place)))
    last = stiff * ((LAME + 4 * SHEAR) / 144)
    for k in range(3):
        put((1, 1, 1, k), last * modes[1][1][1][k])
    return out


def mode_energy(modes):
    def square(value):
        return value * value

    shear = None
    for first, second in SHEARS:
        term = square(at(modes, first) + at(modes, second))
        shear = term if shear is None else shear + term
    one, two, three = (at(modes, place) for place in AXIAL)
    energy = (SHEAR / 16) * shear + (LAME / 16) * square(one + two + three)
    energy = energy + (SHEAR / 8) * (square(one) + square(two) + square(three))
    squares, products = None, None
    for first, second in PAIRS:
        one, two = at(modes, first), at(modes, second)
        term, product = square(one) + square(two), one * two
        squares = term if squares is None else squares + term
        products = product if products is None else products + product
    energy = energy + ((LAME + 3 * SHEAR) / 48) * squares + (LAME / 24) * products
    one, two, three = (at(modes, place) for place in TRIPLE)
    twist = square(one + two + three) + square(one) + square(two) + square(three)
    energy = energy + (SHEAR / 48) * twist
    last = square(modes[1][1][1][0]) + square(modes[1][1][1][1]) + square(modes[1][1][1][2])
    return energy + ((LAME + 4 * SHEAR) / 144) * last


def x_modes(find, plane, row, tile, cases):
    sums, diffs, columns, column = find(row)
    out = [[[None] * 3 for _ in range(2)] for _ in range(2)]
    for c, ref in enumerate((sums, diffs)):
        for k in range(3):
            rows = pl.ds(pl.multiple_of(k * cases + tile * 8, 8), 8)
            one = ref[plane * columns + column, rows, :]
            two = ref[(plane + 1) * columns + column, rows, :]
            out[0][c][k] = one + two
            out[1][c][k] = two - one
    return out


def whole(sums, diffs, columns):
    return lambda row: (sums, diffs, columns, row)


def apply_elements(find, stiff_ref, acc_s, acc_d, planes, rows, kept, stiff_x, stiff_y, cases):
    columns = len(kept)
    tiles = cases // 8
    for column in range(columns):
        acc_s[column] = jnp.zeros(acc_s.shape[1:], f32)
        acc_d[column] = jnp.zeros(acc_d.shape[1:], f32)

    def step(index, _):
        plane, tile = index // tiles, index % tiles

        def emit(row, total):
            if row not in kept:
                return
            for c, acc in enumerate((acc_s, acc_d)):
                for k in range(3):
                    lines = pl.ds(pl.multiple_of(k * cases + tile * 8, 8), 8)
                    low = plane * columns + row - kept[0]
                    acc[low, lines, :] += total[0][c][k] - total[1][c][k]
                    acc[low + columns, lines, :] = total[0][c][k] + total[1][c][k]

        lower = x_modes(find, plane, 0, tile, cases)
        carry = None
        for row in range(rows):
            upper = x_modes(find, plane, row + 1, tile, cases)
            stiff = jnp.broadcast_to(
                stiff_ref[plane + stiff_x, pl.ds(row + stiff_y, 1), :], (8, LANES)
            )
            forces = mode_forces(modes_of(lower, upper), stiff)
            here = [[[None] * 3 for _ in range(2)] for _ in range(2)]
            following = [[[None] * 3 for _ in range(2)] for _ in range(2)]
            for a in range(2):
                for c in range(2):
                    for k in range(3):
                        one, two = forces[a][0][c][k], forces[a][1][c][k]
                        if one is None:
                            here[a][c][k] = -two if carry is None else carry[a][c][k] - two
                            following[a][c][k] = two
                        else:
                            low = one - two
                            here[a][c][k] = low if carry is None else carry[a][c][k] + low
                            following[a][c][k] = one + two
            emit(row, here)
            carry, lower = following, upper
        emit(rows, carry)
        return 0

    lax.fori_loop(0, planes * tiles, step, 0)


def fill(source, base, sizes, ref, xs, ys, code_xs, code_ys):
    planes, rows, cases = sizes
    block = 3 * cases
    line = 0
    for x in xs:
        start = (x * rows + ys[0]) * block
        count = len(ys) * block
        ref[line : line + count, :] = source[start : start + count, :]
        line += count
    for x in code_xs:
        start = base + x * rows + code_ys[0]
        ref[line : line + len(code_ys), :] = source[start : start + len(code_ys), :]
        line += len(code_ys)
    if line < ref.shape[0]:
        ref[line:, :] = jnp.zeros((ref.shape[0] - line, LANES), f32)


def pack_kernel(sizes, forces, codes, own, edge):
    planes, rows, cases = sizes
    block = 3 * cases
    base = planes * rows * block
    for x in range(planes):
        own[base + x * rows : base + (x + 1) * rows, :] = codes[x]
        scale = jnp.where(codes[x] > 0.0, LOAD, 0.0)
        for k in range(3):
            for c in range(cases):
                start = x * rows * block + k * cases + c
                own[pl.ds(start, rows, stride=block), :] = forces[k, c, x] * scale

    even = lax.axis_index("gx") % 2 == 0
    size = rows * block
    for line in range(0, size, block):
        high = lines(own, (planes - 1) * size + line, block)
        edge[line : line + block, :] = jnp.where(even, lines(own, line, block), high)
    high = lines(own, base + (planes - 2) * rows, 2 * rows)
    edge[size:, :] = jnp.where(even, lines(own, base, 2 * rows), high)


def second_kernel(sizes, begun, own, second):
    _, rows, cases = sizes
    size = rows * 3 * cases
    second[...] = lines(own, size, size)


def rows_kernel(sizes, own, ym, yp):
    planes, rows, cases = sizes
    base = planes * rows * 3 * cases
    every_x = range(planes)
    fill(own, base, sizes, ym, every_x, (0, 1), every_x, (0, 1))
    fill(own, base, sizes, yp, every_x, (rows - 1,), every_x, (rows - 2, rows - 1))


def corner_kernel(sizes, ym, yp, out):
    planes, rows, cases = sizes
    block = 3 * cases
    even = lax.axis_index("gx") % 2 == 0
    line = 0
    for source, width in ((ym, 1), (yp, 2)):
        size = width * block
        parts = [(at, (planes - 2) * size + at, block) for at in range(0, 2 * size, block)]
        parts.append((planes * size, planes * size + (planes - 2) * 2, 4))
        for low, high, count in parts:
            value = lines(source, low, count)
            if low != high:
                value = jnp.where(even, value, lines(source, high, count))
            out[line : line + count, :] = value
            line += count
        out[line : line + 4, :] = jnp.zeros((4, LANES), f32)
        line += 4


def lines(ref, start, count):
    return ref[start : start + count, :]


def inside(ref, x, y, rows, block):
    return lines(ref, (x * rows + y) * block, block)


def beyond(refs, slot, y, rows, block):
    below, above, base = refs
    if y < 0:
        return lines(below, slot * block, block)
    return lines(above, base + (slot * 2 + y - rows) * block, block)


def beyond_codes(refs, slots, slot, y, block):
    below, above, base = refs
    if y < 0:
        return lines(below, slots * block + slot * 2, 2)
    return lines(above, base + slots * 2 * block + slot * 2, 2)


def pair_base(planes, block):
    return 2 * block + 8 if planes == 2 else 0


def corner(ref, slot, y, rows, block):
    start = slot * block if y < 0 else 2 * block + 8 + (slot * 2 + y - rows) * block
    return lines(ref, start, block)


def corner_codes(ref, slot, y, block):
    return lines(ref, (2 * block if y < 0 else 6 * block + 8) + slot * 2, 2)


def node_inverse(signed, count, out):
    planes = signed.shape[0]
    for x in range(1, planes):
        codes = signed[x, 0 : count + 1, :]
        total = jnp.abs(signed[x - 1, 0 : count + 1, :]) + jnp.abs(codes)
        total = total[:-1] + total[1:]
        total = total + shift_up(total)
        free = codes[1:] > 0.0
        value = 1.0 / (DIAGONAL * jnp.where(free, total, 1.0))
        out[x - 1, 0:count, :] = jnp.where(free, value, 0.0)
    for x in range(planes):
        signed[x] = jnp.abs(signed[x])


def place_column(sums, diffs, column, value):
    moved = shift_down(value)
    sums[column] = value + moved
    diffs[column] = moved - value


def early_kernel(
    sizes, own, pair, ym, yp, ym_pair, yp_pair, start, sums, diffs, acc_s, acc_d,
    stiff_ref, inverse,
):
    planes, rows, cases = sizes
    block = 3 * cases
    ys = rows + 3
    even = lax.axis_index("gx") % 2 == 0
    y_own, y_pair = (ym, yp, 0), (ym_pair, yp_pair, pair_base(planes, block))

    def both_ways(w, read):
        low = read(True, w + 1) if w + 1 < planes else read(False, w + 1 - planes)
        high = read(False, planes + w - 1) if w < 1 else read(True, w - 1)
        return jnp.where(even, low, high)

    def codes(w, y):
        def read(mine, x):
            if y == 0:
                return lines(own if mine else pair, (planes * block + x) * rows, rows)
            return beyond_codes(y_own if mine else y_pair, planes, x, y, block)

        return both_ways(w, read)

    for w in range(-1, planes + 1):
        for y, count in ((-2, 2), (0, rows), (rows, 2)):
            stiff_ref[w + 1, y + 2 : y + 2 + count, :] = codes(w, y)
    node_inverse(stiff_ref, ys, inverse)
    for w in range(planes + 1):
        for y in range(-1, rows + 2):

            def read(mine, x):
                if 0 <= y < rows:
                    return inside(own if mine else pair, x, y, rows, block)
                return beyond(y_own if mine else y_pair, x, y, rows, block)

            value = both_ways(w, read) * inverse[w, y + 1 : y + 2, :]
            column = w * ys + y + 1
            start[column] = value
            place_column(sums, diffs, column, value)
    kept = range(1, rows + 2)
    find = whole(sums, diffs, ys)
    apply_elements(find, stiff_ref, acc_s, acc_d, planes, rows + 2, kept, 1, 1, cases)


def core_rows(rows):
    return range(2, rows - 1)


def rim_rows(rows):
    return (0, 1, rows - 1, rows)


def core_columns(planes, rows):
    core = core_rows(rows)
    inner, outer = core[1:-1], (core[0], core[-1])
    first = [(x, y) for x in range(planes + 1) for y in inner]
    last = [(x, y) for x in range(planes + 1) for y in outer]
    return first, last, planes * len(inner), planes * len(outer)


def rim_columns(planes, rows):
    own = [(x, y) for x in range(planes) for y in rim_rows(rows) if y < rows]
    beyond_own = [(x, rows) for x in range(planes)] + [(planes, y) for y in rim_rows(rows)]
    return own + beyond_own, len(own)


def merged(x, planes, even, early, near):
    low = ([x - 1] if x >= 1 else [], [x + 1] if x <= 1 else [])
    high = ([x + 1] if x < planes else [], [x - planes + 1] if x >= planes - 1 else [])
    if low[0] and low[1] and high[0] and high[1]:
        one = early(jnp.where(even, low[0][0], high[0][0]))
        return one + near(jnp.where(even, low[1][0], high[1][0]))

    def read(places):
        found = [early(w) for w in places[0]] + [near(v) for v in places[1]]
        return found[0] if len(found) == 1 else found[0] + found[1]

    return jnp.where(even, read(low), read(high))


def direction_at(x, planes, even, early, middle):
    if x == 0:
        return jnp.where(even, middle, early(1))
    if x == planes:
        return jnp.where(even, early(planes - 1), middle)
    return early(jnp.where(even, x - 1, x + 1))


def keep_pair(ref, place, one, two, cases):
    for k in range(3):
        part = slice(k * cases, (k + 1) * cases)
        high, rest = split(jnp.concatenate([one[part], two[part]], 0))
        lane = pl.ds(pl.multiple_of((place * 3 + k) * LANES, LANES), LANES)
        ref[0 : 2 * cases, lane] = high
        ref[2 * cases : 4 * cases, lane] = rest


def keep_split(ref, line, place, value, cases):
    for k in range(3):
        part = value[k * cases : (k + 1) * cases]
        high = part.astype(bf16).astype(f32)
        lane = slice((place * 3 + k) * LANES, (place * 3 + k + 1) * LANES)
        both = jnp.concatenate([high, part - high], 0).astype(bf16)
        ref[line : line + 2 * cases, lane] = both


def folded(value):
    half = value.shape[0] // 2
    return value[:half] + value[half:]


def products(first, second, cases):
    contract = (((1,), (1,)), ((), ()))
    out = lax.dot_general(first, second, contract, preferred_element_type=f32)
    return out[:, : 2 * cases] + out[:, 2 * cases :]


def folds(cases):
    two, count, rest = 2 * cases, 5 * cases // 12, cases // 6
    first, part = 2 * two, LANES - 2 * two
    return (
        ((slice(0, count), slice(0, two)), (slice(0, count), slice(0, two))),
        ((slice(0, count), slice(two, first)), (slice(count, 2 * count), slice(0, two))),
        ((slice(0, rest), slice(first, LANES)), (slice(2 * count, cases), slice(0, part))),
        (
            (slice(rest, 2 * rest), slice(first, first + two - part)),
            (slice(2 * count, cases), slice(part, two)),
        ),
    )


def diagonal_place(cases, index):
    line = cases // 3 + index
    return slice(line, line + 1), slice(4 * cases, 5 * cases)


def middle_kernel(
    sizes, own, pair, edge, second, start, sums_e, diffs_e, acc_se, acc_de,
    sums, diffs, middle, acc_s, acc_d, w_sums, w_diffs, both_out, gram_out, other_out,
    acc2_s, acc2_d, stiff_ref, inverse, right, again,
):
    planes, rows, cases = sizes
    block = 3 * cases
    ys, nodes_y, inner = rows + 3, rows + 1, rows - 1
    core = core_rows(rows)
    even = lax.axis_index("gx") % 2 == 0

    def codes(x):
        if 0 <= x < planes:
            return lines(own, (planes * block + x) * rows, rows)
        slot = x + 2 if x < 0 else x - planes
        outer = lines(edge, (block + slot) * rows, rows)
        if x < 0:
            return jnp.where(even, outer, lines(pair, (planes * block + planes + x) * rows, rows))
        return jnp.where(even, lines(pair, (planes * block + slot) * rows, rows), outer)

    for x in range(-2, planes + 2):
        stiff_ref[x + 2, 0:rows, :] = codes(x)
    node_inverse(stiff_ref, inner, inverse)

    def place(v, x, ref, slot):
        for y in range(1, rows):
            value = inside(ref, slot, y, rows, block) * inverse[x + 1, y - 1 : y, :]
            if v == 1:
                middle[y - 1] = value
            place_column(sums, diffs, v * inner + y - 1, value)

    def copy(v, w):
        for y in range(1, rows):
            sums[v * inner + y - 1] = sums_e[w * ys + y + 1]
            diffs[v * inner + y - 1] = diffs_e[w * ys + y + 1]

    @pl.when(even)
    def _():
        place(0, -1, edge, 0)
        place(1, 0, own, 0)
        copy(2, 0)

    @pl.when(jnp.logical_not(even))
    def _():
        copy(0, planes)
        place(1, planes, edge, 0)
        place(2, planes + 1, second, 0)

    layer = jnp.where(even, 1, planes + 1)
    find = whole(sums, diffs, inner)
    apply_elements(find, stiff_ref, acc_s, acc_d, 2, rows - 2, range(inner), layer, 1, cases)

    def image(x, y, place):
        def total(early, near):
            return merged(
                x, planes, even, lambda w: early[w * nodes_y + y],
                lambda v: near[v * inner + y - 1],
            )

        s, d = total(acc_se, acc_s), total(acc_de, acc_d)
        force = s - d + shift_up(s + d)
        scaled = force * inverse[x + 1, pl.ds(y - 1, 1), :]
        place_column(w_sums, w_diffs, x * len(core) + y - core[0], scaled)
        value = direction_at(x, planes, even, lambda w: start[w * ys + y + 1], middle[y - 1])
        keep_pair(both_out, place, value, scaled, cases)
        return force

    inner_columns, outer_columns, inner_own, outer_own = core_columns(planes, rows)
    count = len(inner_columns)
    for index, (x, y) in enumerate(inner_columns + outer_columns):
        force = image(x, y, index)
        if x < planes:
            ref, place = (again, index) if index < count else (right, index - count)
            keep_pair(ref, place, inside(own, x, y, rows, block), force, cases)
    width, two = 3 * LANES, 2 * cases
    again[: 2 * two, inner_own * width :] = jnp.zeros((2 * two, (count - inner_own) * width), bf16)

    find = whole(w_sums, w_diffs, len(core))
    kept = range(len(core))
    apply_elements(
        find, stiff_ref, acc2_s, acc2_d, planes, len(core) - 1, kept, 2, core[0], cases
    )
    for index, (x, y) in enumerate(inner_columns):
        column = x * len(core) + y - core[0]
        s, d = acc2_s[column], acc2_d[column]
        keep_split(again, 2 * two, index, s - d + shift_up(s + d), cases)
    product = products(again[...], both_out[:, : count * width], cases)
    outer_part = both_out[:, count * width : (count + outer_own) * width]
    gram_out[...] = folded(product[: 2 * two]) + folded(products(right[...], outer_part, cases))
    other_out[...] = folded(product[2 * two :])


def main_kernel(
    sizes, own, pair, edge, second, ym, yp, ym_pair, yp_pair, corners,
    start, sums_e, diffs_e, acc_se, acc_de,
    sums_m, diffs_m, middle_m, acc_sm, acc_dm, w_sm, w_dm, both_m, gram_m,
    other_m, acc2_sm, acc2_dm, both_out, system_out, stiff_ref, inverse,
    middle, sums, diffs, acc_s0, acc_d0, acc_s1, acc_d1, w_sums, w_diffs,
    acc2_s0, acc2_d0, acc2_s1, acc2_d1, right, second_m, table, dense,
):
    planes, rows, cases = sizes
    block = 3 * cases
    ys, nodes_y, inner = rows + 3, rows + 1, rows - 1
    core, rim = core_rows(rows), rim_rows(rows)
    columns, own_count = rim_columns(planes, rows)
    even = lax.axis_index("gx") % 2 == 0
    y_own, y_pair = (ym, yp, 0), (ym_pair, yp_pair, pair_base(planes, block))

    def codes(x, y):
        def read(mine, plane):
            if y == 0:
                return lines(own if mine else pair, (planes * block + plane) * rows, rows)
            return beyond_codes(y_own if mine else y_pair, planes, plane, y, block)

        if 0 <= x < planes:
            return read(True, x)
        slot = x + 2 if x < 0 else x - planes
        if y == 0:
            outer = lines(edge, (block + slot) * rows, rows)
        else:
            outer = corner_codes(corners, slot, y, block)
        within = read(False, planes + x if x < 0 else x - planes)
        return jnp.where(even, outer, within) if x < 0 else jnp.where(even, within, outer)

    for x in range(-2, planes + 2):
        for y, count in ((-2, 2), (0, rows), (rows, 2)):
            stiff_ref[x + 2, y + 2 : y + 2 + count, :] = codes(x, y)
    node_inverse(stiff_ref, ys, inverse)

    sides = (-1, 0, rows, rows + 1)

    def place(v, x, ref, slot, beyond_at):
        for i, y in enumerate(sides):
            value = inside(ref, slot, y, rows, block) if y == 0 else beyond_at(y)
            value = value * inverse[x + 1, y + 1 : y + 2, :]
            if v == 1 and y in (0, rows):
                middle[y // rows] = value
            place_column(sums, diffs, v * 4 + i, value)

    def copy(v, w):
        for i, y in enumerate(sides):
            sums[v * 4 + i] = sums_e[w * ys + y + 1]
            diffs[v * 4 + i] = diffs_e[w * ys + y + 1]

    @pl.when(even)
    def _():
        place(0, -1, edge, 0, lambda y: corner(corners, 1, y, rows, block))
        place(1, 0, own, 0, lambda y: beyond(y_own, 0, y, rows, block))
        copy(2, 0)

    @pl.when(jnp.logical_not(even))
    def _():
        copy(0, planes)
        place(1, planes, edge, 0, lambda y: corner(corners, 0, y, rows, block))
        place(2, planes + 1, second, 0, lambda y: corner(corners, 1, y, rows, block))

    def find_low(row):
        return (sums, diffs, 4, row) if row < 2 else (sums_m, diffs_m, inner, 0)

    def find_high(row):
        return (sums, diffs, 4, row + 1) if row else (sums_m, diffs_m, inner, inner - 1)

    layer = jnp.where(even, 1, planes + 1)
    apply_elements(find_low, stiff_ref, acc_s0, acc_d0, 2, 2, range(1, 3), layer, 1, cases)
    apply_elements(find_high, stiff_ref, acc_s1, acc_d1, 2, 2, range(2), layer, rows + 1, cases)

    def image(x, y, place):
        def total(early, near, low, high):
            def outer(v):
                value = low[v * 2 + y] if y < 2 else high[v * 2 + y - inner]
                return value + near[v * inner + y - 1] if y in (1, inner) else value

            return merged(x, planes, even, lambda w: early[w * nodes_y + y], outer)

        s = total(acc_se, acc_sm, acc_s0, acc_s1)
        d = total(acc_de, acc_dm, acc_d0, acc_d1)
        force = s - d + shift_up(s + d)
        scaled = force * inverse[x + 1, y + 1 : y + 2, :]
        place_column(w_sums, w_diffs, x * len(rim) + rim.index(y), scaled)
        inner_middle = middle_m[y - 1] if y in (1, inner) else middle[y // rows]
        value = direction_at(x, planes, even, lambda w: start[w * ys + y + 1], inner_middle)
        keep_pair(both_out, place, value, scaled, cases)
        return force

    for index, (x, y) in enumerate(columns):
        force = image(x, y, index)
        if index < own_count:
            keep_pair(right, index, inside(own, x, y, rows, block), force, cases)

    def find(row):
        if row in rim:
            return w_sums, w_diffs, len(rim), rim.index(row)
        return w_sm, w_dm, len(core), row - core[0]

    def find_last(row):
        return find(row + rows - 2)

    low, high = (acc2_s0, acc2_d0), (acc2_s1, acc2_d1)
    apply_elements(find, stiff_ref, *low, planes, 2, range(3), 2, 2, cases)
    apply_elements(find_last, stiff_ref, *high, planes, 2, range(3), 2, rows, cases)

    def second_force(x, y):
        s, d = None, None
        for parts, width, first in (
            (low, 3, 0), ((acc2_sm, acc2_dm), len(core), core[0]), (high, 3, rows - 2)
        ):
            if first <= y < first + width:
                column = x * width + y - first
                more = parts[0][column], parts[1][column]
                s, d = more if s is None else (s + more[0], d + more[1])
        return s - d + shift_up(s + d)

    inner_columns, outer_columns, _, _ = core_columns(planes, rows)
    two = 2 * cases
    for index, (x, y) in enumerate(outer_columns):
        keep_split(second_m, 0, index, second_force(x, y), cases)
    for index, (x, y) in enumerate(columns):
        keep_split(right, 2 * two, index, second_force(x, y), cases)
    lane = own_count * 3 * LANES
    right[: 2 * two, lane:] = jnp.zeros((2 * two, right.shape[1] - lane), bf16)

    product = products(right[...], both_out[...], cases)
    more = products(second_m[...], both_m[:, len(inner_columns) * 3 * LANES :], cases)
    gram = folded(product[: 2 * two]) + gram_m[...]
    other = folded(product[2 * two :]) + folded(more) + other_m[...]
    row = lax.broadcasted_iota(jnp.int32, (cases, cases), 0)
    column = lax.broadcasted_iota(jnp.int32, (cases, cases), 1)
    load_load, load_image = gram[:cases, :cases], gram[cases:, :cases]
    mixed, image_image = other[:, :cases], other[:, cases:]
    table[:, 0:cases] = jnp.where(row <= column, load_load, load_image)
    table[:, cases:two] = jnp.where(row <= column, mixed, image_image)
    dense[...] = jnp.zeros(dense.shape, f32)
    for target, source in folds(cases):
        dense[target] = table[source]
    for index, value in enumerate((load_image, image_image)):
        diagonal = jnp.sum(jnp.where(row == column, value, 0.0), axis=0, keepdims=True)
        dense[diagonal_place(cases, index)] = diagonal
    depth = system_out.shape[2]
    for index in range(system_out.shape[0]):
        for part in range(system_out.shape[1]):
            system_out[index, part] = dense[part * depth : (part + 1) * depth, :]


def solve_kernel(
    sizes, system, both_m, both_r, codes, out, mixing, sums, diffs, energy, square, full, dense
):
    planes, rows, cases = sizes
    two = 2 * cases
    nodes_y = rows + 1
    count = planes * rows
    total = jnp.sum(system[...], axis=0)
    depth = system.shape[2]
    for part in range(system.shape[1]):
        dense[part * depth : (part + 1) * depth, :] = total[part]
    square[...] = jnp.zeros(square.shape, f32)
    for source, target in folds(cases):
        square[target] = dense[source]
    value, turned = square[0:cases, :], jnp.transpose(square[...])
    line = lax.broadcasted_iota(jnp.int32, (cases, cases), 0)
    place = lax.broadcasted_iota(jnp.int32, (cases, cases), 1)

    def mended(start, diagonal=None):
        kept, other = value[:, start : start + cases], turned[start : start + cases, :cases]
        if diagonal is None:
            return jnp.where(line <= place, kept, other)
        inner = jnp.where(line < place, other, dense[diagonal_place(cases, diagonal)])
        return jnp.where(line > place, kept, inner)

    load_image, mixed = mended(0, 0), mended(cases)
    parts = ((load_image, mixed), (mixed, mended(cases, 1)), (mended(0), load_image))
    full[...] = jnp.zeros(full.shape, f32)
    for index, (left, right) in enumerate(parts):
        full[index * cases : (index + 1) * cases, 0:cases] = left
        full[index * cases : (index + 1) * cases, cases:two] = right
    table = full[...]
    lane = lax.broadcasted_iota(jnp.int32, (1, LANES), 1)
    gone, wide = 0, 8
    for pivot in range(0, two, wide):
        drop = pivot // 8 * 8 - gone
        table = table[drop:]
        gone += drop
        line = pivot - gone
        inner = (lane >= pivot) & (lane < pivot + wide)
        found = [table[line + p : line + p + 1, :] for p in range(wide)]
        block = [
            [jnp.broadcast_to(row[:, pivot + q : pivot + q + 1], row.shape) for q in range(wide)]
            for row in found
        ]
        solved = [
            jnp.where(lane == pivot + p, -1.0, jnp.where(inner, 0.0, found[p]))
            for p in range(wide)
        ]
        for p in range(wide):
            inverse = 1.0 / block[p][p]
            solved[p] = solved[p] * inverse
            block[p] = [value * inverse for value in block[p]]
            for q in range(wide):
                if q != p:
                    factor = block[q][p]
                    solved[q] = solved[q] - factor * solved[p]
                    for r in range(p + 1, wide):
                        block[q][r] = block[q][r] - factor * block[p][r]
        update = None
        for q in range(wide):
            term = table[:, pivot + q : pivot + q + 1] * solved[q]
            update = term if update is None else update + term
        table = jnp.where(inner, 0.0, table) - update
    answer = table[two - gone :, :two]
    high = answer.astype(bf16).astype(f32)
    mixing[...] = jnp.zeros(mixing.shape, f32)
    mixing[0:cases, 0:two] = high
    mixing[0:cases, two : 2 * two] = high
    mixing[cases:two, 0:two] = answer - high
    mix = mixing[...][:, : 2 * two].astype(bf16)

    def combined(ref, place, width):
        value = jnp.dot(
            mix, ref[:, place * 3 * LANES : (place + width) * 3 * LANES], preferred_element_type=f32
        )
        return value[:cases] + value[cases:]

    def keep(value, index, column):
        for k in range(3):
            part = value[:, (index * 3 + k) * LANES : (index * 3 + k + 1) * LANES]
            moved = shift_down(part)
            sums[column, k * cases : (k + 1) * cases, :] = part + moved
            diffs[column, k * cases : (k + 1) * cases, :] = moved - part

    inner_columns, outer_columns, _, _ = core_columns(planes, rows)
    columns, _ = rim_columns(planes, rows)
    for ref, columns in ((both_m, inner_columns + outer_columns), (both_r, columns)):
        for start in range(0, len(columns), 6):
            some = columns[start : start + 6]
            value = combined(ref, start, len(some))
            for index, (x, y) in enumerate(some):
                keep(value, index, x * nodes_y + y)

    find = whole(sums, diffs, nodes_y)
    tiles = cases // 8

    def step(plane, _):
        for tile in range(tiles):
            lower = x_modes(find, plane, 0, tile, cases)
            for row in range(rows):
                upper = x_modes(find, plane, row + 1, tile, cases)
                part = mode_energy(modes_of(lower, upper))
                if tile == 0:
                    energy[row] = part
                else:
                    energy[row] += part
                lower = upper
        total = jnp.sum(energy[...], axis=1)
        total = (-3.0 / cases) * jnp.abs(codes[plane]) * total
        for index in range(out.shape[0]):
            out[index, plane] = total
        return 0

    lax.fori_loop(0, planes, step, 0)


def smooth(ref, x, rows):
    weight = [2.5 - math.sqrt(q) for q in range(7)]
    near = {}
    for dx in range(-2, 3):
        for dy in range(-2, 3):
            q = dx * dx + dy * dy
            if q <= 5:
                value = ref[x + 2 + dx, 2 + dy : 2 + dy + rows, :]
                near[q] = value if q not in near else near[q] + value
    result = None
    for dz in range(3):
        part = None
        for q, value in near.items():
            if q + dz * dz <= 6:
                term = weight[q + dz * dz] * value
                part = term if part is None else part + term
        if dz == 0:
            result = part
        else:
            place = lax.broadcasted_iota(jnp.int32, part.shape, 1)
            forward = jnp.where(place >= LANES - dz, 0.0, pltpu.roll(part, LANES - dz, 1))
            backward = jnp.where(place < dz, 0.0, pltpu.roll(part, dz, 1))
            result = result + (forward + backward)
    return result


def scale_kernel(sizes, counts, levels, out, there):
    planes, rows, _ = sizes
    y = lax.broadcasted_iota(jnp.int32, (rows + 4, LANES), 0)
    y = y + (lax.axis_index("gy") * rows - 2)
    in_y = (y >= 0) & (y < counts[1] * rows)
    for x in range(planes + 4):
        global_x = lax.axis_index("gx") * planes + (x - 2)
        in_x = (global_x >= 0) & (global_x < counts[0] * planes)
        there[x] = jnp.where(in_y & in_x, 1.0, 0.0)
    for x in range(planes):
        density = 0.3 + 0.7 * levels[x].astype(f32) / (LEVELS - 1)
        out[x] = 1.0 / (density * smooth(there, x, rows))


def filter_kernel(sizes, counts, blocks, blocks_pair, scale, out, wide):
    planes, rows, _ = sizes
    sides_x = ((-1, planes - 2, planes, 0), (0, 0, planes, 2), (1, 0, 2, 2 + planes))
    sides_y = ((-1, rows - 2, rows, 0), (0, 0, rows, 2), (1, 0, 2, 2 + rows))
    for step_x, x0, x1, to_x in sides_x:
        for step_y, y0, y1, to_y in sides_y:
            at_x = lax.axis_index("gx") + step_x
            at_y = lax.axis_index("gy") + step_y
            inside = (at_x >= 0) & (at_x < counts[0]) & (at_y >= 0) & (at_y < counts[1])
            index = jnp.where(inside, at_x // 2 * counts[1] + at_y, 0)
            value = (blocks_pair if step_x else blocks)[index, x0:x1, y0:y1, :]
            wide[to_x : to_x + x1 - x0, to_y : to_y + y1 - y0, :] = jnp.where(inside, value, 0.0)
    for x in range(planes):
        out[x] = smooth(wide, x, rows) * scale[x]


def local(forces, levels, supports):
    _, cases, planes, rows, _ = forces.shape
    sizes = (planes, rows, cases)
    block = 3 * cases
    count_x, count_y = lax.axis_size("gx"), lax.axis_size("gy")

    def shape(blocks, codes):
        return jax.ShapeDtypeStruct((blocks * block + up8(codes), LANES), f32)

    density = 0.3 + 0.7 * levels.astype(f32) / (LEVELS - 1)
    codes = density * density * density
    codes = jnp.where(supports == 0, codes, -codes)
    counts = (count_x, count_y)
    own, edge = pl.pallas_call(
        functools.partial(pack_kernel, sizes),
        out_shape=[shape(planes * rows, planes * rows), shape(rows, 2 * rows)],
        in_specs=[VMEM] * 2,
        out_specs=[VMEM] * 2,
        compiler_params=PARAMS,
        name="pack",
    )(forces, codes)
    scale = pl.pallas_call(
        functools.partial(scale_kernel, sizes, counts),
        out_shape=jax.ShapeDtypeStruct((planes, rows, LANES), f32),
        in_specs=[VMEM],
        out_specs=VMEM,
        scratch_shapes=[pltpu.VMEM((planes + 4, rows + 4, LANES), f32)],
        compiler_params=PARAMS,
        name="scale",
    )(levels)

    def moved(value, axis, step):
        count = lax.axis_size(axis)
        pairs = [(i, i + step) for i in range(count) if 0 <= i + step < count]
        return lax.ppermute(value, axis, pairs)

    def links(first, step):
        return [(i, i + step) for i in range(first, count_x, 2) if 0 <= i + step < count_x]

    def swapped(value):
        return lax.ppermute(value, "gx", links(0, 1) + links(1, -1))

    def across(value):
        return lax.ppermute(value, "gx", links(1, 1) + links(2, -1))

    edge = across(edge)
    pair = swapped(own)
    own, pair = lax.optimization_barrier((own, pair))
    ym, yp = pl.pallas_call(
        functools.partial(rows_kernel, sizes),
        out_shape=[shape(2 * planes, 2 * planes), shape(planes, 2 * planes)],
        in_specs=[VMEM],
        out_specs=[VMEM] * 2,
        compiler_params=PARAMS,
        name="rows",
    )(own)
    from_yp, from_ym = moved(ym, "gy", -1), moved(yp, "gy", 1)
    second = pl.pallas_call(
        functools.partial(second_kernel, sizes),
        out_shape=shape(rows, 0),
        in_specs=[VMEM] * 2,
        out_specs=VMEM,
        compiler_params=PARAMS,
        name="second",
    )(swapped(codes), own)
    second = lax.ppermute(second, "gx", links(2, -1))
    from_ym, from_yp, edge = lax.optimization_barrier((from_ym, from_yp, edge))
    corners = pl.pallas_call(
        functools.partial(corner_kernel, sizes),
        out_shape=jax.ShapeDtypeStruct((6 * block + 16, LANES), f32),
        in_specs=[VMEM] * 2,
        out_specs=VMEM,
        compiler_params=PARAMS,
        name="corners",
    )(from_ym, from_yp)
    if planes == 2:
        pair_ym = pair_yp = swapped(corners)
    else:
        pair_yp, pair_ym = swapped(from_yp), swapped(from_ym)
    corners = across(corners)

    devices = count_x * count_y
    nodes = (planes + 1) * (rows + 1)
    window = jax.ShapeDtypeStruct(((planes + 1) * (rows + 3), block, LANES), f32)
    partial_forces = jax.ShapeDtypeStruct((nodes, block, LANES), f32)
    early = pl.pallas_call(
        functools.partial(early_kernel, sizes),
        out_shape=[window] * 3 + [partial_forces] * 2,
        in_specs=[VMEM] * 6,
        out_specs=[VMEM] * 5,
        scratch_shapes=[
            pltpu.VMEM((planes + 2, up8(rows + 4), LANES), f32),
            pltpu.VMEM((planes + 1, up8(rows + 3), LANES), f32),
        ],
        compiler_params=PARAMS,
        cost_estimate=pl.CostEstimate(
            flops=200 * planes * rows * block * LANES, bytes_accessed=2**23, transcendentals=0
        ),
        name="early",
    )(own, pair, from_ym, from_yp, pair_ym, pair_yp)

    def columns(count):
        return jax.ShapeDtypeStruct((count, block, LANES), f32)

    def fields(lines, count):
        return jax.ShapeDtypeStruct((lines * cases, count * 3 * LANES), bf16)

    def scratch(value):
        return pltpu.VMEM(value.shape, value.dtype)

    core = len(core_rows(rows))
    middle = pl.pallas_call(
        functools.partial(middle_kernel, sizes),
        out_shape=[columns(3 * (rows - 1))] * 2
        + [columns(rows - 1)]
        + [columns(3 * (rows - 1))] * 2
        + [columns((planes + 1) * core)] * 2
        + [fields(4, (planes + 1) * core), jax.ShapeDtypeStruct((2 * cases, 2 * cases), f32)]
        + [jax.ShapeDtypeStruct((cases, 2 * cases), f32)]
        + [columns((planes + 1) * core)] * 2,
        in_specs=[VMEM] * 9,
        out_specs=[VMEM] * 12,
        scratch_shapes=[
            pltpu.VMEM((planes + 4, up8(rows), LANES), f32),
            pltpu.VMEM((planes + 3, up8(rows), LANES), f32),
            scratch(fields(4, planes * 2)),
            scratch(fields(6, (planes + 1) * (core - 2))),
        ],
        compiler_params=PARAMS,
        name="middle",
    )(own, pair, edge, second, *early)

    rim, _ = rim_columns(planes, rows)
    both, system = pl.pallas_call(
        functools.partial(main_kernel, sizes),
        out_shape=[
            fields(4, len(rim)),
            jax.ShapeDtypeStruct((devices, 5 * cases // 24, 2, LANES), f32),
        ],
        in_specs=[VMEM] * 26,
        out_specs=[VMEM] * 2,
        scratch_shapes=[
            pltpu.VMEM((planes + 4, up8(rows + 4), LANES), f32),
            pltpu.VMEM((planes + 3, up8(rows + 3), LANES), f32),
            scratch(columns(2)),
            *[scratch(columns(12))] * 2,
            *[scratch(columns(6))] * 4,
            *[scratch(columns((planes + 1) * 4))] * 2,
            *[scratch(columns((planes + 1) * 3))] * 4,
            scratch(fields(6, len(rim))),
            scratch(fields(2, (planes + 1) * 2)),
            pltpu.VMEM((cases, LANES), f32),
            pltpu.VMEM((5 * cases // 12, LANES), f32),
        ],
        compiler_params=PARAMS,
        name="operator",
    )(
        own, pair, edge, second, from_ym, from_yp, pair_ym, pair_yp, corners,
        *early, *middle,
    )

    groups = [
        [x * count_y + y for x in range(side, count_x, 2) for y in range(count_y)]
        for side in range(2)
    ]

    def gathered(copies):
        mine = lax.all_to_all(copies, ("gx", "gy"), 0, 0, axis_index_groups=groups)
        return mine, swapped(mine)

    system = lax.all_to_all(system, ("gx", "gy"), 0, 0)

    weighted = pl.pallas_call(
        functools.partial(solve_kernel, sizes),
        out_shape=jax.ShapeDtypeStruct((devices // 2, planes, rows, LANES), f32),
        in_specs=[VMEM] * 4,
        out_specs=VMEM,
        scratch_shapes=[
            pltpu.VMEM((2 * cases, LANES), f32),
            scratch(columns(nodes)),
            scratch(columns(nodes)),
            pltpu.VMEM((rows, 8, LANES), f32),
            pltpu.VMEM((LANES, LANES), f32),
            pltpu.VMEM((3 * cases, LANES), f32),
            pltpu.VMEM((5 * cases // 12, LANES), f32),
        ],
        compiler_params=PARAMS,
        name="solve",
    )(system, middle[7], both, codes)

    blocks = gathered(weighted)
    return pl.pallas_call(
        functools.partial(filter_kernel, sizes, counts),
        out_shape=jax.ShapeDtypeStruct((planes, rows, LANES), f32),
        in_specs=[VMEM] * 3,
        out_specs=VMEM,
        scratch_shapes=[pltpu.VMEM((planes + 4, rows + 4, LANES), f32)],
        compiler_params=PARAMS,
        name="cone",
    )(*blocks, scale)


def solution(mesh):
    return jax.shard_map(
        local,
        mesh=mesh,
        in_specs=(P(None, None, "gx", "gy", None), P("gx", "gy", None), P("gx", "gy", None)),
        out_specs=P("gx", "gy", None),
        check_vma=False,
    )
```

```python
import functools
import math

import jax
import jax.numpy as jnp
from jax import lax
from jax.experimental import pallas as pl
from jax.experimental.pallas import tpu as pltpu
from jax.sharding import PartitionSpec as P

LEVELS = 16
LOAD = 0.2
LANES = 128
POISSON = 0.3
LAME = POISSON / ((1.0 + POISSON) * (1.0 - 2.0 * POISSON))
SHEAR = 1.0 / (2.0 * (1.0 + POISSON))
DIAGONAL = (LAME + 2.0 * SHEAR) / 9.0 + 2.0 * SHEAR / 9.0
VMEM = pl.BlockSpec(memory_space=pltpu.VMEM)
PARAMS = pltpu.CompilerParams(vmem_limit_bytes=30 * 2**20)
f32 = jnp.float32
bf16 = jnp.bfloat16


def up8(count):
    return -(-count // 8) * 8


def shift_down(value):
    lane = lax.broadcasted_iota(jnp.int32, value.shape, value.ndim - 1)
    rolled = pltpu.roll(value, LANES - 1, value.ndim - 1)
    return jnp.where(lane == LANES - 1, 0.0, rolled)


def shift_up(value):
    lane = lax.broadcasted_iota(jnp.int32, value.shape, value.ndim - 1)
    return jnp.where(lane == 0, 0.0, pltpu.roll(value, 1, value.ndim - 1))


def unrolled(count, factor, body):
    def turn(step, _):
        for offset in range(factor):
            body(step * factor + offset)
        return 0

    turns = count // factor
    if turns:
        lax.fori_loop(0, turns, turn, 0)
    for index in range(turns * factor, count):
        body(index)


def split(value):
    high = value.astype(bf16)
    return high, (value - high.astype(f32)).astype(bf16)


def modes_of(lower, upper):
    out = [[[[None] * 3 for _ in range(2)] for _ in range(2)] for _ in range(2)]
    for a in range(2):
        for c in range(2):
            for k in range(3):
                if a or c:
                    out[a][0][c][k] = lower[a][c][k] + upper[a][c][k]
                out[a][1][c][k] = upper[a][c][k] - lower[a][c][k]
    return out


PAIRS = (((1, 1, 0, 0), (0, 1, 1, 2)), ((1, 0, 1, 0), (0, 1, 1, 1)), ((1, 1, 0, 1), (1, 0, 1, 2)))
TRIPLE = ((0, 1, 1, 0), (1, 0, 1, 1), (1, 1, 0, 2))
SHEARS = (((0, 1, 0, 0), (1, 0, 0, 1)), ((0, 0, 1, 0), (1, 0, 0, 2)), ((0, 0, 1, 1), (0, 1, 0, 2)))
AXIAL = ((1, 0, 0, 0), (0, 1, 0, 1), (0, 0, 1, 2))


def at(modes, place):
    a, b, c, k = place
    return modes[a][b][c][k]


def mode_forces(modes, stiff):
    out = [[[[None] * 3 for _ in range(2)] for _ in range(2)] for _ in range(2)]

    def put(place, value):
        a, b, c, k = place
        out[a][b][c][k] = value

    shear = stiff * (SHEAR / 16)
    for first, second in SHEARS:
        force = shear * (at(modes, first) + at(modes, second))
        put(first, force)
        put(second, force)
    one, two, three = (at(modes, place) for place in AXIAL)
    volume = (stiff * (LAME / 16)) * (one + two + three)
    axial = stiff * (SHEAR / 8)
    for place in AXIAL:
        put(place, volume + axial * at(modes, place))
    own, cross = stiff * ((LAME + 3 * SHEAR) / 48), stiff * (LAME / 48)
    for first, second in PAIRS:
        one, two = at(modes, first), at(modes, second)
        put(first, own * one + cross * two)
        put(second, own * two + cross * one)
    twist = stiff * (SHEAR / 48)
    one, two, three = (at(modes, place) for place in TRIPLE)
    total = one + two + three
    for place in TRIPLE:
        put(place, twist * (total + at(modes, place)))
    last = stiff * ((LAME + 4 * SHEAR) / 144)
    for k in range(3):
        put((1, 1, 1, k), last * modes[1][1][1][k])
    return out


def mode_energy(modes):
    def square(value):
        return value * value

    shear = None
    for first, second in SHEARS:
        term = square(at(modes, first) + at(modes, second))
        shear = term if shear is None else shear + term
    one, two, three = (at(modes, place) for place in AXIAL)
    energy = (SHEAR / 16) * shear + (LAME / 16) * square(one + two + three)
    energy = energy + (SHEAR / 8) * (square(one) + square(two) + square(three))
    squares, products = None, None
    for first, second in PAIRS:
        one, two = at(modes, first), at(modes, second)
        term, product = square(one) + square(two), one * two
        squares = term if squares is None else squares + term
        products = product if products is None else products + product
    energy = energy + ((LAME + 3 * SHEAR) / 48) * squares + (LAME / 24) * products
    one, two, three = (at(modes, place) for place in TRIPLE)
    twist = square(one + two + three) + square(one) + square(two) + square(three)
    energy = energy + (SHEAR / 48) * twist
    last = square(modes[1][1][1][0]) + square(modes[1][1][1][1]) + square(modes[1][1][1][2])
    return energy + ((LAME + 4 * SHEAR) / 144) * last


def x_modes(find, plane, row, tile, cases):
    sums, diffs, columns, column = find(row)
    out = [[[None] * 3 for _ in range(2)] for _ in range(2)]
    for c, ref in enumerate((sums, diffs)):
        for k in range(3):
            rows = pl.ds(pl.multiple_of(k * cases + tile * 8, 8), 8)
            one = ref[plane * columns + column, rows, :]
            two = ref[(plane + 1) * columns + column, rows, :]
            out[0][c][k] = one + two
            out[1][c][k] = two - one
    return out


def whole(sums, diffs, columns):
    return lambda row: (sums, diffs, columns, row)


def apply_elements(find, stiff_ref, acc_s, acc_d, planes, rows, kept, stiff_x, stiff_y, cases):
    columns = len(kept)
    tiles = cases // 8
    for column in range(columns):
        acc_s[column] = jnp.zeros(acc_s.shape[1:], f32)
        acc_d[column] = jnp.zeros(acc_d.shape[1:], f32)

    def step(index, _):
        plane, tile = index // tiles, index % tiles

        def emit(row, total):
            if row not in kept:
                return
            for c, acc in enumerate((acc_s, acc_d)):
                for k in range(3):
                    lines = pl.ds(pl.multiple_of(k * cases + tile * 8, 8), 8)
                    low = plane * columns + row - kept[0]
                    acc[low, lines, :] += total[0][c][k] - total[1][c][k]
                    acc[low + columns, lines, :] = total[0][c][k] + total[1][c][k]

        lower = x_modes(find, plane, 0, tile, cases)
        carry = None
        for row in range(rows):
            upper = x_modes(find, plane, row + 1, tile, cases)
            stiff = jnp.broadcast_to(
                stiff_ref[plane + stiff_x, pl.ds(row + stiff_y, 1), :], (8, LANES)
            )
            forces = mode_forces(modes_of(lower, upper), stiff)
            here = [[[None] * 3 for _ in range(2)] for _ in range(2)]
            following = [[[None] * 3 for _ in range(2)] for _ in range(2)]
            for a in range(2):
                for c in range(2):
                    for k in range(3):
                        one, two = forces[a][0][c][k], forces[a][1][c][k]
                        if one is None:
                            here[a][c][k] = -two if carry is None else carry[a][c][k] - two
                            following[a][c][k] = two
                        else:
                            low = one - two
                            here[a][c][k] = low if carry is None else carry[a][c][k] + low
                            following[a][c][k] = one + two
            emit(row, here)
            carry, lower = following, upper
        emit(rows, carry)
        return 0

    lax.fori_loop(0, planes * tiles, step, 0)


def fill(source, base, sizes, ref, xs, ys, code_xs, code_ys):
    planes, rows, cases = sizes
    block = 3 * cases
    line = 0
    for x in xs:
        start = (x * rows + ys[0]) * block
        count = len(ys) * block
        ref[line : line + count, :] = source[start : start + count, :]
        line += count
    for x in code_xs:
        start = base + x * rows + code_ys[0]
        ref[line : line + len(code_ys), :] = source[start : start + len(code_ys), :]
        line += len(code_ys)
    if line < ref.shape[0]:
        ref[line:, :] = jnp.zeros((ref.shape[0] - line, LANES), f32)


def pack_kernel(sizes, forces, codes, own, edge):
    planes, rows, cases = sizes
    block = 3 * cases
    base = planes * rows * block
    for x in range(planes):
        own[base + x * rows : base + (x + 1) * rows, :] = codes[x]
        scale = jnp.where(codes[x] > 0.0, LOAD, 0.0)
        for k in range(3):
            for c in range(cases):
                start = x * rows * block + k * cases + c
                own[pl.ds(start, rows, stride=block), :] = forces[k, c, x] * scale

    even = lax.axis_index("gx") % 2 == 0
    size = rows * block
    for line in range(0, size, block):
        high = lines(own, (planes - 1) * size + line, block)
        edge[line : line + block, :] = jnp.where(even, lines(own, line, block), high)
    high = lines(own, base + (planes - 2) * rows, 2 * rows)
    edge[size:, :] = jnp.where(even, lines(own, base, 2 * rows), high)


def second_kernel(sizes, begun, own, second):
    _, rows, cases = sizes
    size = rows * 3 * cases
    second[...] = lines(own, size, size)


def rows_kernel(sizes, own, ym, yp):
    planes, rows, cases = sizes
    base = planes * rows * 3 * cases
    every_x = range(planes)
    fill(own, base, sizes, ym, every_x, (0, 1), every_x, (0, 1))
    fill(own, base, sizes, yp, every_x, (rows - 1,), every_x, (rows - 2, rows - 1))


def corner_kernel(sizes, ym, yp, out):
    planes, rows, cases = sizes
    block = 3 * cases
    even = lax.axis_index("gx") % 2 == 0
    line = 0
    for source, width in ((ym, 1), (yp, 2)):
        size = width * block
        parts = [(at, (planes - 2) * size + at, block) for at in range(0, 2 * size, block)]
        parts.append((planes * size, planes * size + (planes - 2) * 2, 4))
        for low, high, count in parts:
            value = lines(source, low, count)
            if low != high:
                value = jnp.where(even, value, lines(source, high, count))
            out[line : line + count, :] = value
            line += count
        out[line : line + 4, :] = jnp.zeros((4, LANES), f32)
        line += 4


def lines(ref, start, count):
    return ref[start : start + count, :]


def inside(ref, x, y, rows, block):
    return lines(ref, (x * rows + y) * block, block)


def beyond(refs, slot, y, rows, block):
    below, above, base = refs
    if y < 0:
        return lines(below, slot * block, block)
    return lines(above, base + (slot * 2 + y - rows) * block, block)


def beyond_codes(refs, slots, slot, y, block):
    below, above, base = refs
    if y < 0:
        return lines(below, slots * block + slot * 2, 2)
    return lines(above, base + slots * 2 * block + slot * 2, 2)


def pair_base(planes, block):
    return 2 * block + 8 if planes == 2 else 0


def corner(ref, slot, y, rows, block):
    start = slot * block if y < 0 else 2 * block + 8 + (slot * 2 + y - rows) * block
    return lines(ref, start, block)


def corner_codes(ref, slot, y, block):
    return lines(ref, (2 * block if y < 0 else 6 * block + 8) + slot * 2, 2)


def node_inverse(signed, count, out):
    planes = signed.shape[0]
    for x in range(1, planes):
        codes = signed[x, 0 : count + 1, :]
        total = jnp.abs(signed[x - 1, 0 : count + 1, :]) + jnp.abs(codes)
        total = total[:-1] + total[1:]
        total = total + shift_up(total)
        free = codes[1:] > 0.0
        value = 1.0 / (DIAGONAL * jnp.where(free, total, 1.0))
        out[x - 1, 0:count, :] = jnp.where(free, value, 0.0)
    for x in range(planes):
        signed[x] = jnp.abs(signed[x])


def place_column(sums, diffs, column, value):
    moved = shift_down(value)
    sums[column] = value + moved
    diffs[column] = moved - value


def early_kernel(
    sizes, own, pair, ym, yp, ym_pair, yp_pair, start, sums, diffs, acc_s, acc_d,
    stiff_ref, inverse,
):
    planes, rows, cases = sizes
    block = 3 * cases
    ys = rows + 3
    even = lax.axis_index("gx") % 2 == 0
    y_own, y_pair = (ym, yp, 0), (ym_pair, yp_pair, pair_base(planes, block))

    def both_ways(w, read):
        low = read(True, w + 1) if w + 1 < planes else read(False, w + 1 - planes)
        high = read(False, planes + w - 1) if w < 1 else read(True, w - 1)
        return jnp.where(even, low, high)

    def codes(w, y):
        def read(mine, x):
            if y == 0:
                return lines(own if mine else pair, (planes * block + x) * rows, rows)
            return beyond_codes(y_own if mine else y_pair, planes, x, y, block)

        return both_ways(w, read)

    for w in range(-1, planes + 1):
        for y, count in ((-2, 2), (0, rows), (rows, 2)):
            stiff_ref[w + 1, y + 2 : y + 2 + count, :] = codes(w, y)
    node_inverse(stiff_ref, ys, inverse)
    for w in range(planes + 1):
        for y in range(-1, rows + 2):

            def read(mine, x):
                if 0 <= y < rows:
                    return inside(own if mine else pair, x, y, rows, block)
                return beyond(y_own if mine else y_pair, x, y, rows, block)

            value = both_ways(w, read) * inverse[w, y + 1 : y + 2, :]
            column = w * ys + y + 1
            start[column] = value
            place_column(sums, diffs, column, value)
    kept = range(1, rows + 2)
    find = whole(sums, diffs, ys)
    apply_elements(find, stiff_ref, acc_s, acc_d, planes, rows + 2, kept, 1, 1, cases)


def core_rows(rows):
    return range(2, rows - 1)


def rim_rows(rows):
    return (0, 1, rows - 1, rows)


def core_columns(planes, rows):
    core = core_rows(rows)
    inner, outer = core[1:-1], (core[0], core[-1])
    first = [(x, y) for x in range(planes + 1) for y in inner]
    last = [(x, y) for x in range(planes + 1) for y in outer]
    return first, last, planes * len(inner), planes * len(outer)


def rim_columns(planes, rows):
    own = [(x, y) for x in range(planes) for y in rim_rows(rows) if y < rows]
    beyond_own = [(x, rows) for x in range(planes)] + [(planes, y) for y in rim_rows(rows)]
    return own + beyond_own, len(own)


def merged(x, planes, even, early, near):
    low = ([x - 1] if x >= 1 else [], [x + 1] if x <= 1 else [])
    high = ([x + 1] if x < planes else [], [x - planes + 1] if x >= planes - 1 else [])
    if low[0] and low[1] and high[0] and high[1]:
        one = early(jnp.where(even, low[0][0], high[0][0]))
        return one + near(jnp.where(even, low[1][0], high[1][0]))

    def read(places):
        found = [early(w) for w in places[0]] + [near(v) for v in places[1]]
        return found[0] if len(found) == 1 else found[0] + found[1]

    return jnp.where(even, read(low), read(high))


def direction_at(x, planes, even, early, middle):
    if x == 0:
        return jnp.where(even, middle, early(1))
    if x == planes:
        return jnp.where(even, early(planes - 1), middle)
    return early(jnp.where(even, x - 1, x + 1))


def keep_pair(ref, place, one, two, cases):
    for k in range(3):
        part = slice(k * cases, (k + 1) * cases)
        high, rest = split(jnp.concatenate([one[part], two[part]], 0))
        lane = pl.ds(pl.multiple_of((place * 3 + k) * LANES, LANES), LANES)
        ref[0 : 2 * cases, lane] = high
        ref[2 * cases : 4 * cases, lane] = rest


def keep_split(ref, line, place, value, cases):
    for k in range(3):
        part = value[k * cases : (k + 1) * cases]
        high = part.astype(bf16).astype(f32)
        lane = slice((place * 3 + k) * LANES, (place * 3 + k + 1) * LANES)
        both = jnp.concatenate([high, part - high], 0).astype(bf16)
        ref[line : line + 2 * cases, lane] = both


def folded(value):
    half = value.shape[0] // 2
    return value[:half] + value[half:]


def products(first, second, cases):
    contract = (((1,), (1,)), ((), ()))
    out = lax.dot_general(first, second, contract, preferred_element_type=f32)
    return out[:, : 2 * cases] + out[:, 2 * cases :]


def folds(cases):
    two, count, rest = 2 * cases, 5 * cases // 12, cases // 6
    first, part = 2 * two, LANES - 2 * two
    return (
        ((slice(0, count), slice(0, two)), (slice(0, count), slice(0, two))),
        ((slice(0, count), slice(two, first)), (slice(count, 2 * count), slice(0, two))),
        ((slice(0, rest), slice(first, LANES)), (slice(2 * count, cases), slice(0, part))),
        (
            (slice(rest, 2 * rest), slice(first, first + two - part)),
            (slice(2 * count, cases), slice(part, two)),
        ),
    )


def diagonal_place(cases, index):
    line = cases // 3 + index
    return slice(line, line + 1), slice(4 * cases, 5 * cases)


def middle_kernel(
    sizes, own, pair, edge, second, start, sums_e, diffs_e, acc_se, acc_de,
    sums, diffs, middle, acc_s, acc_d, w_sums, w_diffs, both_out, gram_out, other_out,
    acc2_s, acc2_d, stiff_ref, inverse, right, again,
):
    planes, rows, cases = sizes
    block = 3 * cases
    ys, nodes_y, inner = rows + 3, rows + 1, rows - 1
    core = core_rows(rows)
    even = lax.axis_index("gx") % 2 == 0

    def codes(x):
        if 0 <= x < planes:
            return lines(own, (planes * block + x) * rows, rows)
        slot = x + 2 if x < 0 else x - planes
        outer = lines(edge, (block + slot) * rows, rows)
        if x < 0:
            return jnp.where(even, outer, lines(pair, (planes * block + planes + x) * rows, rows))
        return jnp.where(even, lines(pair, (planes * block + slot) * rows, rows), outer)

    for x in range(-2, planes + 2):
        stiff_ref[x + 2, 0:rows, :] = codes(x)
    node_inverse(stiff_ref, inner, inverse)

    def place(v, x, ref, slot):
        for y in range(1, rows):
            value = inside(ref, slot, y, rows, block) * inverse[x + 1, y - 1 : y, :]
            if v == 1:
                middle[y - 1] = value
            place_column(sums, diffs, v * inner + y - 1, value)

    def copy(v, w):
        for y in range(1, rows):
            sums[v * inner + y - 1] = sums_e[w * ys + y + 1]
            diffs[v * inner + y - 1] = diffs_e[w * ys + y + 1]

    @pl.when(even)
    def _():
        place(0, -1, edge, 0)
        place(1, 0, own, 0)
        copy(2, 0)

    @pl.when(jnp.logical_not(even))
    def _():
        copy(0, planes)
        place(1, planes, edge, 0)
        place(2, planes + 1, second, 0)

    layer = jnp.where(even, 1, planes + 1)
    find = whole(sums, diffs, inner)
    apply_elements(find, stiff_ref, acc_s, acc_d, 2, rows - 2, range(inner), layer, 1, cases)

    def image(x, y, place):
        def total(early, near):
            return merged(
                x, planes, even, lambda w: early[w * nodes_y + y],
                lambda v: near[v * inner + y - 1],
            )

        s, d = total(acc_se, acc_s), total(acc_de, acc_d)
        force = s - d + shift_up(s + d)
        scaled = force * inverse[x + 1, pl.ds(y - 1, 1), :]
        place_column(w_sums, w_diffs, x * len(core) + y - core[0], scaled)
        value = direction_at(x, planes, even, lambda w: start[w * ys + y + 1], middle[y - 1])
        keep_pair(both_out, place, value, scaled, cases)
        return force

    inner_columns, outer_columns, inner_own, outer_own = core_columns(planes, rows)
    count = len(inner_columns)
    for index, (x, y) in enumerate(inner_columns + outer_columns):
        force = image(x, y, index)
        if x < planes:
            ref, place = (again, index) if index < count else (right, index - count)
            keep_pair(ref, place, inside(own, x, y, rows, block), force, cases)
    width, two = 3 * LANES, 2 * cases
    again[: 2 * two, inner_own * width :] = jnp.zeros((2 * two, (count - inner_own) * width), bf16)

    find = whole(w_sums, w_diffs, len(core))
    kept = range(len(core))
    apply_elements(
        find, stiff_ref, acc2_s, acc2_d, planes, len(core) - 1, kept, 2, core[0], cases
    )
    for index, (x, y) in enumerate(inner_columns):
        column = x * len(core) + y - core[0]
        s, d = acc2_s[column], acc2_d[column]
        keep_split(again, 2 * two, index, s - d + shift_up(s + d), cases)
    product = products(again[...], both_out[:, : count * width], cases)
    outer_part = both_out[:, count * width : (count + outer_own) * width]
    gram_out[...] = folded(product[: 2 * two]) + folded(products(right[...], outer_part, cases))
    other_out[...] = folded(product[2 * two :])


def main_kernel(
    sizes, own, pair, edge, second, ym, yp, ym_pair, yp_pair, corners,
    start, sums_e, diffs_e, acc_se, acc_de,
    sums_m, diffs_m, middle_m, acc_sm, acc_dm, w_sm, w_dm, both_m, gram_m,
    other_m, acc2_sm, acc2_dm, both_out, system_out, stiff_ref, inverse,
    middle, sums, diffs, acc_s0, acc_d0, acc_s1, acc_d1, w_sums, w_diffs,
    acc2_s0, acc2_d0, acc2_s1, acc2_d1, right, second_m, table, dense,
):
    planes, rows, cases = sizes
    block = 3 * cases
    ys, nodes_y, inner = rows + 3, rows + 1, rows - 1
    core, rim = core_rows(rows), rim_rows(rows)
    columns, own_count = rim_columns(planes, rows)
    even = lax.axis_index("gx") % 2 == 0
    y_own, y_pair = (ym, yp, 0), (ym_pair, yp_pair, pair_base(planes, block))

    def codes(x, y):
        def read(mine, plane):
            if y == 0:
                return lines(own if mine else pair, (planes * block + plane) * rows, rows)
            return beyond_codes(y_own if mine else y_pair, planes, plane, y, block)

        if 0 <= x < planes:
            return read(True, x)
        slot = x + 2 if x < 0 else x - planes
        if y == 0:
            outer = lines(edge, (block + slot) * rows, rows)
        else:
            outer = corner_codes(corners, slot, y, block)
        within = read(False, planes + x if x < 0 else x - planes)
        return jnp.where(even, outer, within) if x < 0 else jnp.where(even, within, outer)

    for x in range(-2, planes + 2):
        for y, count in ((-2, 2), (0, rows), (rows, 2)):
            stiff_ref[x + 2, y + 2 : y + 2 + count, :] = codes(x, y)
    node_inverse(stiff_ref, ys, inverse)

    sides = (-1, 0, rows, rows + 1)

    def place(v, x, ref, slot, beyond_at):
        for i, y in enumerate(sides):
            value = inside(ref, slot, y, rows, block) if y == 0 else beyond_at(y)
            value = value * inverse[x + 1, y + 1 : y + 2, :]
            if v == 1 and y in (0, rows):
                middle[y // rows] = value
            place_column(sums, diffs, v * 4 + i, value)

    def copy(v, w):
        for i, y in enumerate(sides):
            sums[v * 4 + i] = sums_e[w * ys + y + 1]
            diffs[v * 4 + i] = diffs_e[w * ys + y + 1]

    @pl.when(even)
    def _():
        place(0, -1, edge, 0, lambda y: corner(corners, 1, y, rows, block))
        place(1, 0, own, 0, lambda y: beyond(y_own, 0, y, rows, block))
        copy(2, 0)

    @pl.when(jnp.logical_not(even))
    def _():
        copy(0, planes)
        place(1, planes, edge, 0, lambda y: corner(corners, 0, y, rows, block))
        place(2, planes + 1, second, 0, lambda y: corner(corners, 1, y, rows, block))

    def find_low(row):
        return (sums, diffs, 4, row) if row < 2 else (sums_m, diffs_m, inner, 0)

    def find_high(row):
        return (sums, diffs, 4, row + 1) if row else (sums_m, diffs_m, inner, inner - 1)

    layer = jnp.where(even, 1, planes + 1)
    apply_elements(find_low, stiff_ref, acc_s0, acc_d0, 2, 2, range(1, 3), layer, 1, cases)
    apply_elements(find_high, stiff_ref, acc_s1, acc_d1, 2, 2, range(2), layer, rows + 1, cases)

    def image(x, y, place):
        def total(early, near, low, high):
            def outer(v):
                value = low[v * 2 + y] if y < 2 else high[v * 2 + y - inner]
                return value + near[v * inner + y - 1] if y in (1, inner) else value

            return merged(x, planes, even, lambda w: early[w * nodes_y + y], outer)

        s = total(acc_se, acc_sm, acc_s0, acc_s1)
        d = total(acc_de, acc_dm, acc_d0, acc_d1)
        force = s - d + shift_up(s + d)
        scaled = force * inverse[x + 1, y + 1 : y + 2, :]
        place_column(w_sums, w_diffs, x * len(rim) + rim.index(y), scaled)
        inner_middle = middle_m[y - 1] if y in (1, inner) else middle[y // rows]
        value = direction_at(x, planes, even, lambda w: start[w * ys + y + 1], inner_middle)
        keep_pair(both_out, place, value, scaled, cases)
        return force

    for index, (x, y) in enumerate(columns):
        force = image(x, y, index)
        if index < own_count:
            keep_pair(right, index, inside(own, x, y, rows, block), force, cases)

    def find(row):
        if row in rim:
            return w_sums, w_diffs, len(rim), rim.index(row)
        return w_sm, w_dm, len(core), row - core[0]

    def find_last(row):
        return find(row + rows - 2)

    low, high = (acc2_s0, acc2_d0), (acc2_s1, acc2_d1)
    apply_elements(find, stiff_ref, *low, planes, 2, range(3), 2, 2, cases)
    apply_elements(find_last, stiff_ref, *high, planes, 2, range(3), 2, rows, cases)

    def second_force(x, y):
        s, d = None, None
        for parts, width, first in (
            (low, 3, 0), ((acc2_sm, acc2_dm), len(core), core[0]), (high, 3, rows - 2)
        ):
            if first <= y < first + width:
                column = x * width + y - first
                more = parts[0][column], parts[1][column]
                s, d = more if s is None else (s + more[0], d + more[1])
        return s - d + shift_up(s + d)

    inner_columns, outer_columns, _, _ = core_columns(planes, rows)
    two = 2 * cases
    for index, (x, y) in enumerate(outer_columns):
        keep_split(second_m, 0, index, second_force(x, y), cases)
    for index, (x, y) in enumerate(columns):
        keep_split(right, 2 * two, index, second_force(x, y), cases)
    lane = own_count * 3 * LANES
    right[: 2 * two, lane:] = jnp.zeros((2 * two, right.shape[1] - lane), bf16)

    product = products(right[...], both_out[...], cases)
    more = products(second_m[...], both_m[:, len(inner_columns) * 3 * LANES :], cases)
    gram = folded(product[: 2 * two]) + gram_m[...]
    other = folded(product[2 * two :]) + folded(more) + other_m[...]
    row = lax.broadcasted_iota(jnp.int32, (cases, cases), 0)
    column = lax.broadcasted_iota(jnp.int32, (cases, cases), 1)
    load_load, load_image = gram[:cases, :cases], gram[cases:, :cases]
    mixed, image_image = other[:, :cases], other[:, cases:]
    table[:, 0:cases] = jnp.where(row <= column, load_load, load_image)
    table[:, cases:two] = jnp.where(row <= column, mixed, image_image)
    dense[...] = jnp.zeros(dense.shape, f32)
    for target, source in folds(cases):
        dense[target] = table[source]
    for index, value in enumerate((load_image, image_image)):
        diagonal = jnp.sum(jnp.where(row == column, value, 0.0), axis=0, keepdims=True)
        dense[diagonal_place(cases, index)] = diagonal
    depth = system_out.shape[2]
    for index in range(system_out.shape[0]):
        for part in range(system_out.shape[1]):
            system_out[index, part] = dense[part * depth : (part + 1) * depth, :]


def solve_kernel(
    sizes, system, both_m, both_r, codes, out, mixing, sums, diffs, energy, square, full, dense
):
    planes, rows, cases = sizes
    two = 2 * cases
    nodes_y = rows + 1
    count = planes * rows
    total = jnp.sum(system[...], axis=0)
    depth = system.shape[2]
    for part in range(system.shape[1]):
        dense[part * depth : (part + 1) * depth, :] = total[part]
    square[...] = jnp.zeros(square.shape, f32)
    for source, target in folds(cases):
        square[target] = dense[source]
    value, turned = square[0:cases, :], jnp.transpose(square[...])
    line = lax.broadcasted_iota(jnp.int32, (cases, cases), 0)
    place = lax.broadcasted_iota(jnp.int32, (cases, cases), 1)

    def mended(start, diagonal=None):
        kept, other = value[:, start : start + cases], turned[start : start + cases, :cases]
        if diagonal is None:
            return jnp.where(line <= place, kept, other)
        inner = jnp.where(line < place, other, dense[diagonal_place(cases, diagonal)])
        return jnp.where(line > place, kept, inner)

    load_image, mixed = mended(0, 0), mended(cases)
    parts = ((load_image, mixed), (mixed, mended(cases, 1)), (mended(0), load_image))
    full[...] = jnp.zeros(full.shape, f32)
    for index, (left, right) in enumerate(parts):
        full[index * cases : (index + 1) * cases, 0:cases] = left
        full[index * cases : (index + 1) * cases, cases:two] = right
    table = full[...]
    lane = lax.broadcasted_iota(jnp.int32, (1, LANES), 1)
    gone, wide = 0, 16
    for pivot in range(0, two, wide):
        drop = pivot // 8 * 8 - gone
        table = table[drop:]
        gone += drop
        line = pivot - gone
        inner = (lane >= pivot) & (lane < pivot + wide)
        found = [table[line + p : line + p + 1, :] for p in range(wide)]
        block = [
            [jnp.broadcast_to(row[:, pivot + q : pivot + q + 1], row.shape) for q in range(wide)]
            for row in found
        ]
        solved = [
            jnp.where(lane == pivot + p, -1.0, jnp.where(inner, 0.0, found[p]))
            for p in range(wide)
        ]
        for p in range(wide):
            inverse = 1.0 / block[p][p]
            solved[p] = solved[p] * inverse
            block[p] = [value * inverse for value in block[p]]
            for q in range(wide):
                if q != p:
                    factor = block[q][p]
                    solved[q] = solved[q] - factor * solved[p]
                    for r in range(p + 1, wide):
                        block[q][r] = block[q][r] - factor * block[p][r]
        update = None
        for q in range(wide):
            term = table[:, pivot + q : pivot + q + 1] * solved[q]
            update = term if update is None else update + term
        table = jnp.where(inner, 0.0, table) - update
    answer = table[two - gone :, :two]
    high = answer.astype(bf16).astype(f32)
    mixing[...] = jnp.zeros(mixing.shape, f32)
    mixing[0:cases, 0:two] = high
    mixing[0:cases, two : 2 * two] = high
    mixing[cases:two, 0:two] = answer - high
    mix = mixing[...][:, : 2 * two].astype(bf16)

    def combined(ref, place, width):
        value = jnp.dot(
            mix, ref[:, place * 3 * LANES : (place + width) * 3 * LANES], preferred_element_type=f32
        )
        return value[:cases] + value[cases:]

    def keep(value, index, column):
        for k in range(3):
            part = value[:, (index * 3 + k) * LANES : (index * 3 + k + 1) * LANES]
            moved = shift_down(part)
            sums[column, k * cases : (k + 1) * cases, :] = part + moved
            diffs[column, k * cases : (k + 1) * cases, :] = moved - part

    inner_columns, outer_columns, _, _ = core_columns(planes, rows)
    columns, _ = rim_columns(planes, rows)
    for ref, columns in ((both_m, inner_columns + outer_columns), (both_r, columns)):
        for start in range(0, len(columns), 6):
            some = columns[start : start + 6]
            value = combined(ref, start, len(some))
            for index, (x, y) in enumerate(some):
                keep(value, index, x * nodes_y + y)

    find = whole(sums, diffs, nodes_y)
    tiles = cases // 8

    def step(plane, _):
        for tile in range(tiles):
            lower = x_modes(find, plane, 0, tile, cases)
            for row in range(rows):
                upper = x_modes(find, plane, row + 1, tile, cases)
                part = mode_energy(modes_of(lower, upper))
                if tile == 0:
                    energy[row] = part
                else:
                    energy[row] += part
                lower = upper
        total = jnp.sum(energy[...], axis=1)
        total = (-3.0 / cases) * jnp.abs(codes[plane]) * total
        for index in range(out.shape[0]):
            out[index, plane] = total
        return 0

    lax.fori_loop(0, planes, step, 0)


def smooth(ref, x, rows):
    weight = [2.5 - math.sqrt(q) for q in range(7)]
    near = {}
    for dx in range(-2, 3):
        for dy in range(-2, 3):
            q = dx * dx + dy * dy
            if q <= 5:
                value = ref[x + 2 + dx, 2 + dy : 2 + dy + rows, :]
                near[q] = value if q not in near else near[q] + value
    result = None
    for dz in range(3):
        part = None
        for q, value in near.items():
            if q + dz * dz <= 6:
                term = weight[q + dz * dz] * value
                part = term if part is None else part + term
        if dz == 0:
            result = part
        else:
            place = lax.broadcasted_iota(jnp.int32, part.shape, 1)
            forward = jnp.where(place >= LANES - dz, 0.0, pltpu.roll(part, LANES - dz, 1))
            backward = jnp.where(place < dz, 0.0, pltpu.roll(part, dz, 1))
            result = result + (forward + backward)
    return result


def scale_kernel(sizes, counts, levels, out, there):
    planes, rows, _ = sizes
    y = lax.broadcasted_iota(jnp.int32, (rows + 4, LANES), 0)
    y = y + (lax.axis_index("gy") * rows - 2)
    in_y = (y >= 0) & (y < counts[1] * rows)
    for x in range(planes + 4):
        global_x = lax.axis_index("gx") * planes + (x - 2)
        in_x = (global_x >= 0) & (global_x < counts[0] * planes)
        there[x] = jnp.where(in_y & in_x, 1.0, 0.0)
    for x in range(planes):
        density = 0.3 + 0.7 * levels[x].astype(f32) / (LEVELS - 1)
        out[x] = 1.0 / (density * smooth(there, x, rows))


def filter_kernel(sizes, counts, blocks, blocks_pair, scale, out, wide):
    planes, rows, _ = sizes
    sides_x = ((-1, planes - 2, planes, 0), (0, 0, planes, 2), (1, 0, 2, 2 + planes))
    sides_y = ((-1, rows - 2, rows, 0), (0, 0, rows, 2), (1, 0, 2, 2 + rows))
    for step_x, x0, x1, to_x in sides_x:
        for step_y, y0, y1, to_y in sides_y:
            at_x = lax.axis_index("gx") + step_x
            at_y = lax.axis_index("gy") + step_y
            inside = (at_x >= 0) & (at_x < counts[0]) & (at_y >= 0) & (at_y < counts[1])
            index = jnp.where(inside, at_x // 2 * counts[1] + at_y, 0)
            value = (blocks_pair if step_x else blocks)[index, x0:x1, y0:y1, :]
            wide[to_x : to_x + x1 - x0, to_y : to_y + y1 - y0, :] = jnp.where(inside, value, 0.0)
    for x in range(planes):
        out[x] = smooth(wide, x, rows) * scale[x]


def local(forces, levels, supports):
    _, cases, planes, rows, _ = forces.shape
    sizes = (planes, rows, cases)
    block = 3 * cases
    count_x, count_y = lax.axis_size("gx"), lax.axis_size("gy")

    def shape(blocks, codes):
        return jax.ShapeDtypeStruct((blocks * block + up8(codes), LANES), f32)

    density = 0.3 + 0.7 * levels.astype(f32) / (LEVELS - 1)
    codes = density * density * density
    codes = jnp.where(supports == 0, codes, -codes)
    counts = (count_x, count_y)
    own, edge = pl.pallas_call(
        functools.partial(pack_kernel, sizes),
        out_shape=[shape(planes * rows, planes * rows), shape(rows, 2 * rows)],
        in_specs=[VMEM] * 2,
        out_specs=[VMEM] * 2,
        compiler_params=PARAMS,
        name="pack",
    )(forces, codes)
    scale = pl.pallas_call(
        functools.partial(scale_kernel, sizes, counts),
        out_shape=jax.ShapeDtypeStruct((planes, rows, LANES), f32),
        in_specs=[VMEM],
        out_specs=VMEM,
        scratch_shapes=[pltpu.VMEM((planes + 4, rows + 4, LANES), f32)],
        compiler_params=PARAMS,
        name="scale",
    )(levels)

    def moved(value, axis, step):
        count = lax.axis_size(axis)
        pairs = [(i, i + step) for i in range(count) if 0 <= i + step < count]
        return lax.ppermute(value, axis, pairs)

    def links(first, step):
        return [(i, i + step) for i in range(first, count_x, 2) if 0 <= i + step < count_x]

    def swapped(value):
        return lax.ppermute(value, "gx", links(0, 1) + links(1, -1))

    def across(value):
        return lax.ppermute(value, "gx", links(1, 1) + links(2, -1))

    edge = across(edge)
    pair = swapped(own)
    own, pair = lax.optimization_barrier((own, pair))
    ym, yp = pl.pallas_call(
        functools.partial(rows_kernel, sizes),
        out_shape=[shape(2 * planes, 2 * planes), shape(planes, 2 * planes)],
        in_specs=[VMEM],
        out_specs=[VMEM] * 2,
        compiler_params=PARAMS,
        name="rows",
    )(own)
    from_yp, from_ym = moved(ym, "gy", -1), moved(yp, "gy", 1)
    second = pl.pallas_call(
        functools.partial(second_kernel, sizes),
        out_shape=shape(rows, 0),
        in_specs=[VMEM] * 2,
        out_specs=VMEM,
        compiler_params=PARAMS,
        name="second",
    )(swapped(codes), own)
    second = lax.ppermute(second, "gx", links(2, -1))
    from_ym, from_yp, edge = lax.optimization_barrier((from_ym, from_yp, edge))
    corners = pl.pallas_call(
        functools.partial(corner_kernel, sizes),
        out_shape=jax.ShapeDtypeStruct((6 * block + 16, LANES), f32),
        in_specs=[VMEM] * 2,
        out_specs=VMEM,
        compiler_params=PARAMS,
        name="corners",
    )(from_ym, from_yp)
    if planes == 2:
        pair_ym = pair_yp = swapped(corners)
    else:
        pair_yp, pair_ym = swapped(from_yp), swapped(from_ym)
    corners = across(corners)

    devices = count_x * count_y
    nodes = (planes + 1) * (rows + 1)
    window = jax.ShapeDtypeStruct(((planes + 1) * (rows + 3), block, LANES), f32)
    partial_forces = jax.ShapeDtypeStruct((nodes, block, LANES), f32)
    early = pl.pallas_call(
        functools.partial(early_kernel, sizes),
        out_shape=[window] * 3 + [partial_forces] * 2,
        in_specs=[VMEM] * 6,
        out_specs=[VMEM] * 5,
        scratch_shapes=[
            pltpu.VMEM((planes + 2, up8(rows + 4), LANES), f32),
            pltpu.VMEM((planes + 1, up8(rows + 3), LANES), f32),
        ],
        compiler_params=PARAMS,
        cost_estimate=pl.CostEstimate(
            flops=200 * planes * rows * block * LANES, bytes_accessed=2**23, transcendentals=0
        ),
        name="early",
    )(own, pair, from_ym, from_yp, pair_ym, pair_yp)

    def columns(count):
        return jax.ShapeDtypeStruct((count, block, LANES), f32)

    def fields(lines, count):
        return jax.ShapeDtypeStruct((lines * cases, count * 3 * LANES), bf16)

    def scratch(value):
        return pltpu.VMEM(value.shape, value.dtype)

    core = len(core_rows(rows))
    middle = pl.pallas_call(
        functools.partial(middle_kernel, sizes),
        out_shape=[columns(3 * (rows - 1))] * 2
        + [columns(rows - 1)]
        + [columns(3 * (rows - 1))] * 2
        + [columns((planes + 1) * core)] * 2
        + [fields(4, (planes + 1) * core), jax.ShapeDtypeStruct((2 * cases, 2 * cases), f32)]
        + [jax.ShapeDtypeStruct((cases, 2 * cases), f32)]
        + [columns((planes + 1) * core)] * 2,
        in_specs=[VMEM] * 9,
        out_specs=[VMEM] * 12,
        scratch_shapes=[
            pltpu.VMEM((planes + 4, up8(rows), LANES), f32),
            pltpu.VMEM((planes + 3, up8(rows), LANES), f32),
            scratch(fields(4, planes * 2)),
            scratch(fields(6, (planes + 1) * (core - 2))),
        ],
        compiler_params=PARAMS,
        name="middle",
    )(own, pair, edge, second, *early)

    rim, _ = rim_columns(planes, rows)
    both, system = pl.pallas_call(
        functools.partial(main_kernel, sizes),
        out_shape=[
            fields(4, len(rim)),
            jax.ShapeDtypeStruct((devices, 5 * cases // 24, 2, LANES), f32),
        ],
        in_specs=[VMEM] * 26,
        out_specs=[VMEM] * 2,
        scratch_shapes=[
            pltpu.VMEM((planes + 4, up8(rows + 4), LANES), f32),
            pltpu.VMEM((planes + 3, up8(rows + 3), LANES), f32),
            scratch(columns(2)),
            *[scratch(columns(12))] * 2,
            *[scratch(columns(6))] * 4,
            *[scratch(columns((planes + 1) * 4))] * 2,
            *[scratch(columns((planes + 1) * 3))] * 4,
            scratch(fields(6, len(rim))),
            scratch(fields(2, (planes + 1) * 2)),
            pltpu.VMEM((cases, LANES), f32),
            pltpu.VMEM((5 * cases // 12, LANES), f32),
        ],
        compiler_params=PARAMS,
        name="operator",
    )(
        own, pair, edge, second, from_ym, from_yp, pair_ym, pair_yp, corners,
        *early, *middle,
    )

    groups = [
        [x * count_y + y for x in range(side, count_x, 2) for y in range(count_y)]
        for side in range(2)
    ]

    def gathered(copies):
        mine = lax.all_to_all(copies, ("gx", "gy"), 0, 0, axis_index_groups=groups)
        return mine, swapped(mine)

    system = lax.all_to_all(system, ("gx", "gy"), 0, 0)

    weighted = pl.pallas_call(
        functools.partial(solve_kernel, sizes),
        out_shape=jax.ShapeDtypeStruct((devices // 2, planes, rows, LANES), f32),
        in_specs=[VMEM] * 4,
        out_specs=VMEM,
        scratch_shapes=[
            pltpu.VMEM((2 * cases, LANES), f32),
            scratch(columns(nodes)),
            scratch(columns(nodes)),
            pltpu.VMEM((rows, 8, LANES), f32),
            pltpu.VMEM((LANES, LANES), f32),
            pltpu.VMEM((3 * cases, LANES), f32),
            pltpu.VMEM((5 * cases // 12, LANES), f32),
        ],
        compiler_params=PARAMS,
        name="solve",
    )(system, middle[7], both, codes)

    blocks = gathered(weighted)
    return pl.pallas_call(
        functools.partial(filter_kernel, sizes, counts),
        out_shape=jax.ShapeDtypeStruct((planes, rows, LANES), f32),
        in_specs=[VMEM] * 3,
        out_specs=VMEM,
        scratch_shapes=[pltpu.VMEM((planes + 4, rows + 4, LANES), f32)],
        compiler_params=PARAMS,
        name="cone",
    )(*blocks, scale)


def solution(mesh):
    return jax.shard_map(
        local,
        mesh=mesh,
        in_specs=(P(None, None, "gx", "gy", None), P("gx", "gy", None), P("gx", "gy", None)),
        out_specs=P("gx", "gy", None),
        check_vma=False,
    )
```

```python
import functools
import math

import jax
import jax.numpy as jnp
from jax import lax
from jax.experimental import pallas as pl
from jax.experimental.pallas import tpu as pltpu
from jax.sharding import PartitionSpec as P

LEVELS = 16
LOAD = 0.2
LANES = 128
POISSON = 0.3
LAME = POISSON / ((1.0 + POISSON) * (1.0 - 2.0 * POISSON))
SHEAR = 1.0 / (2.0 * (1.0 + POISSON))
DIAGONAL = (LAME + 2.0 * SHEAR) / 9.0 + 2.0 * SHEAR / 9.0
VMEM = pl.BlockSpec(memory_space=pltpu.VMEM)
PARAMS = pltpu.CompilerParams(vmem_limit_bytes=30 * 2**20)
f32 = jnp.float32
bf16 = jnp.bfloat16


def up8(count):
    return -(-count // 8) * 8


def shift_down(value):
    lane = lax.broadcasted_iota(jnp.int32, value.shape, value.ndim - 1)
    rolled = pltpu.roll(value, LANES - 1, value.ndim - 1)
    return jnp.where(lane == LANES - 1, 0.0, rolled)


def shift_up(value):
    lane = lax.broadcasted_iota(jnp.int32, value.shape, value.ndim - 1)
    return jnp.where(lane == 0, 0.0, pltpu.roll(value, 1, value.ndim - 1))


def unrolled(count, factor, body):
    def turn(step, _):
        for offset in range(factor):
            body(step * factor + offset)
        return 0

    turns = count // factor
    if turns:
        lax.fori_loop(0, turns, turn, 0)
    for index in range(turns * factor, count):
        body(index)


def split(value):
    high = value.astype(bf16)
    return high, (value - high.astype(f32)).astype(bf16)


def modes_of(lower, upper):
    out = [[[[None] * 3 for _ in range(2)] for _ in range(2)] for _ in range(2)]
    for a in range(2):
        for c in range(2):
            for k in range(3):
                if a or c:
                    out[a][0][c][k] = lower[a][c][k] + upper[a][c][k]
                out[a][1][c][k] = upper[a][c][k] - lower[a][c][k]
    return out


PAIRS = (((1, 1, 0, 0), (0, 1, 1, 2)), ((1, 0, 1, 0), (0, 1, 1, 1)), ((1, 1, 0, 1), (1, 0, 1, 2)))
TRIPLE = ((0, 1, 1, 0), (1, 0, 1, 1), (1, 1, 0, 2))
SHEARS = (((0, 1, 0, 0), (1, 0, 0, 1)), ((0, 0, 1, 0), (1, 0, 0, 2)), ((0, 0, 1, 1), (0, 1, 0, 2)))
AXIAL = ((1, 0, 0, 0), (0, 1, 0, 1), (0, 0, 1, 2))


def at(modes, place):
    a, b, c, k = place
    return modes[a][b][c][k]


def mode_forces(modes, stiff):
    out = [[[[None] * 3 for _ in range(2)] for _ in range(2)] for _ in range(2)]

    def put(place, value):
        a, b, c, k = place
        out[a][b][c][k] = value

    shear = stiff * (SHEAR / 16)
    for first, second in SHEARS:
        force = shear * (at(modes, first) + at(modes, second))
        put(first, force)
        put(second, force)
    one, two, three = (at(modes, place) for place in AXIAL)
    volume = (stiff * (LAME / 16)) * (one + two + three)
    axial = stiff * (SHEAR / 8)
    for place in AXIAL:
        put(place, volume + axial * at(modes, place))
    own, cross = stiff * ((LAME + 3 * SHEAR) / 48), stiff * (LAME / 48)
    for first, second in PAIRS:
        one, two = at(modes, first), at(modes, second)
        put(first, own * one + cross * two)
        put(second, own * two + cross * one)
    twist = stiff * (SHEAR / 48)
    one, two, three = (at(modes, place) for place in TRIPLE)
    total = one + two + three
    for place in TRIPLE:
        put(place, twist * (total + at(modes, place)))
    last = stiff * ((LAME + 4 * SHEAR) / 144)
    for k in range(3):
        put((1, 1, 1, k), last * modes[1][1][1][k])
    return out


def mode_energy(modes):
    def square(value):
        return value * value

    shear = None
    for first, second in SHEARS:
        term = square(at(modes, first) + at(modes, second))
        shear = term if shear is None else shear + term
    one, two, three = (at(modes, place) for place in AXIAL)
    energy = (SHEAR / 16) * shear + (LAME / 16) * square(one + two + three)
    energy = energy + (SHEAR / 8) * (square(one) + square(two) + square(three))
    squares, products = None, None
    for first, second in PAIRS:
        one, two = at(modes, first), at(modes, second)
        term, product = square(one) + square(two), one * two
        squares = term if squares is None else squares + term
        products = product if products is None else products + product
    energy = energy + ((LAME + 3 * SHEAR) / 48) * squares + (LAME / 24) * products
    one, two, three = (at(modes, place) for place in TRIPLE)
    twist = square(one + two + three) + square(one) + square(two) + square(three)
    energy = energy + (SHEAR / 48) * twist
    last = square(modes[1][1][1][0]) + square(modes[1][1][1][1]) + square(modes[1][1][1][2])
    return energy + ((LAME + 4 * SHEAR) / 144) * last


def x_modes(find, plane, row, tile, cases):
    sums, diffs, columns, column = find(row)
    out = [[[None] * 3 for _ in range(2)] for _ in range(2)]
    for c, ref in enumerate((sums, diffs)):
        for k in range(3):
            rows = pl.ds(pl.multiple_of(k * cases + tile * 8, 8), 8)
            one = ref[plane * columns + column, rows, :]
            two = ref[(plane + 1) * columns + column, rows, :]
            out[0][c][k] = one + two
            out[1][c][k] = two - one
    return out


def whole(sums, diffs, columns):
    return lambda row: (sums, diffs, columns, row)


def apply_elements(find, stiff_ref, acc_s, acc_d, planes, rows, kept, stiff_x, stiff_y, cases):
    columns = len(kept)
    tiles = cases // 8
    for column in range(columns):
        acc_s[column] = jnp.zeros(acc_s.shape[1:], f32)
        acc_d[column] = jnp.zeros(acc_d.shape[1:], f32)

    def step(index, _):
        plane, tile = index // tiles, index % tiles

        def emit(row, total):
            if row not in kept:
                return
            for c, acc in enumerate((acc_s, acc_d)):
                for k in range(3):
                    lines = pl.ds(pl.multiple_of(k * cases + tile * 8, 8), 8)
                    low = plane * columns + row - kept[0]
                    acc[low, lines, :] += total[0][c][k] - total[1][c][k]
                    acc[low + columns, lines, :] = total[0][c][k] + total[1][c][k]

        lower = x_modes(find, plane, 0, tile, cases)
        carry = None
        for row in range(rows):
            upper = x_modes(find, plane, row + 1, tile, cases)
            stiff = jnp.broadcast_to(
                stiff_ref[plane + stiff_x, pl.ds(row + stiff_y, 1), :], (8, LANES)
            )
            forces = mode_forces(modes_of(lower, upper), stiff)
            here = [[[None] * 3 for _ in range(2)] for _ in range(2)]
            following = [[[None] * 3 for _ in range(2)] for _ in range(2)]
            for a in range(2):
                for c in range(2):
                    for k in range(3):
                        one, two = forces[a][0][c][k], forces[a][1][c][k]
                        if one is None:
                            here[a][c][k] = -two if carry is None else carry[a][c][k] - two
                            following[a][c][k] = two
                        else:
                            low = one - two
                            here[a][c][k] = low if carry is None else carry[a][c][k] + low
                            following[a][c][k] = one + two
            emit(row, here)
            carry, lower = following, upper
        emit(rows, carry)
        return 0

    lax.fori_loop(0, planes * tiles, step, 0)


def fill(source, base, sizes, ref, xs, ys, code_xs, code_ys):
    planes, rows, cases = sizes
    block = 3 * cases
    line = 0
    for x in xs:
        start = (x * rows + ys[0]) * block
        count = len(ys) * block
        ref[line : line + count, :] = source[start : start + count, :]
        line += count
    for x in code_xs:
        start = base + x * rows + code_ys[0]
        ref[line : line + len(code_ys), :] = source[start : start + len(code_ys), :]
        line += len(code_ys)
    if line < ref.shape[0]:
        ref[line:, :] = jnp.zeros((ref.shape[0] - line, LANES), f32)


def pack_kernel(sizes, forces, codes, own, edge):
    planes, rows, cases = sizes
    block = 3 * cases
    base = planes * rows * block
    for x in range(planes):
        own[base + x * rows : base + (x + 1) * rows, :] = codes[x]
        scale = jnp.where(codes[x] > 0.0, LOAD, 0.0)
        for k in range(3):
            for c in range(cases):
                start = x * rows * block + k * cases + c
                own[pl.ds(start, rows, stride=block), :] = forces[k, c, x] * scale

    even = lax.axis_index("gx") % 2 == 0
    size = rows * block
    for line in range(0, size, block):
        high = lines(own, (planes - 1) * size + line, block)
        edge[line : line + block, :] = jnp.where(even, lines(own, line, block), high)
    high = lines(own, base + (planes - 2) * rows, 2 * rows)
    edge[size:, :] = jnp.where(even, lines(own, base, 2 * rows), high)


def second_kernel(sizes, begun, own, second):
    _, rows, cases = sizes
    size = rows * 3 * cases
    second[...] = lines(own, size, size)


def rows_kernel(sizes, own, ym, yp):
    planes, rows, cases = sizes
    base = planes * rows * 3 * cases
    every_x = range(planes)
    fill(own, base, sizes, ym, every_x, (0, 1), every_x, (0, 1))
    fill(own, base, sizes, yp, every_x, (rows - 1,), every_x, (rows - 2, rows - 1))


def corner_kernel(sizes, ym, yp, out, copy):
    planes, rows, cases = sizes
    block = 3 * cases
    even = lax.axis_index("gx") % 2 == 0
    line = 0
    for source, width in ((ym, 1), (yp, 2)):
        size = width * block
        parts = [(at, (planes - 2) * size + at, block) for at in range(0, 2 * size, block)]
        parts.append((planes * size, planes * size + (planes - 2) * 2, 4))
        for low, high, count in parts:
            value = lines(source, low, count)
            if low != high:
                value = jnp.where(even, value, lines(source, high, count))
            out[line : line + count, :] = value
            line += count
        out[line : line + 4, :] = jnp.zeros((4, LANES), f32)
        line += 4
    copy[...] = lines(out, 0, line)
    out[line:, :] = jnp.zeros((out.shape[0] - line, LANES), f32)


def lines(ref, start, count):
    return ref[start : start + count, :]


def inside(ref, x, y, rows, block):
    return lines(ref, (x * rows + y) * block, block)


def beyond(refs, slot, y, rows, block):
    below, above, base = refs
    if y < 0:
        return lines(below, slot * block, block)
    return lines(above, base + (slot * 2 + y - rows) * block, block)


def beyond_codes(refs, slots, slot, y, block):
    below, above, base = refs
    if y < 0:
        return lines(below, slots * block + slot * 2, 2)
    return lines(above, base + slots * 2 * block + slot * 2, 2)


def pair_base(planes, block):
    return 2 * block + 8 if planes == 2 else 0


def corner(ref, slot, y, rows, block):
    start = slot * block if y < 0 else 2 * block + 8 + (slot * 2 + y - rows) * block
    return lines(ref, start, block)


def corner_codes(ref, slot, y, block):
    return lines(ref, (2 * block if y < 0 else 6 * block + 8) + slot * 2, 2)


def node_inverse(signed, count, out):
    planes = signed.shape[0]
    for x in range(1, planes):
        codes = signed[x, 0 : count + 1, :]
        total = jnp.abs(signed[x - 1, 0 : count + 1, :]) + jnp.abs(codes)
        total = total[:-1] + total[1:]
        total = total + shift_up(total)
        free = codes[1:] > 0.0
        value = 1.0 / (DIAGONAL * jnp.where(free, total, 1.0))
        out[x - 1, 0:count, :] = jnp.where(free, value, 0.0)
    for x in range(planes):
        signed[x] = jnp.abs(signed[x])


def place_column(sums, diffs, column, value):
    moved = shift_down(value)
    sums[column] = value + moved
    diffs[column] = moved - value


def early_kernel(
    sizes, own, pair, ym, yp, ym_pair, yp_pair, start, sums, diffs, acc_s, acc_d,
    stiff_ref, inverse,
):
    planes, rows, cases = sizes
    block = 3 * cases
    ys = rows + 3
    even = lax.axis_index("gx") % 2 == 0
    y_own, y_pair = (ym, yp, 0), (ym_pair, yp_pair, pair_base(planes, block))

    def both_ways(w, read):
        low = read(True, w + 1) if w + 1 < planes else read(False, w + 1 - planes)
        high = read(False, planes + w - 1) if w < 1 else read(True, w - 1)
        return jnp.where(even, low, high)

    def codes(w, y):
        def read(mine, x):
            if y == 0:
                return lines(own if mine else pair, (planes * block + x) * rows, rows)
            return beyond_codes(y_own if mine else y_pair, planes, x, y, block)

        return both_ways(w, read)

    for w in range(-1, planes + 1):
        for y, count in ((-2, 2), (0, rows), (rows, 2)):
            stiff_ref[w + 1, y + 2 : y + 2 + count, :] = codes(w, y)
    node_inverse(stiff_ref, ys, inverse)
    for w in range(planes + 1):
        for y in range(-1, rows + 2):

            def read(mine, x):
                if 0 <= y < rows:
                    return inside(own if mine else pair, x, y, rows, block)
                return beyond(y_own if mine else y_pair, x, y, rows, block)

            value = both_ways(w, read) * inverse[w, y + 1 : y + 2, :]
            column = w * ys + y + 1
            start[column] = value
            place_column(sums, diffs, column, value)
    kept = range(1, rows + 2)
    find = whole(sums, diffs, ys)
    apply_elements(find, stiff_ref, acc_s, acc_d, planes, rows + 2, kept, 1, 1, cases)


def core_rows(rows):
    return range(2, rows - 1)


def rim_rows(rows):
    return (0, 1, rows - 1, rows)


def core_columns(planes, rows):
    core = core_rows(rows)
    inner, outer = core[1:-1], (core[0], core[-1])
    first = [(x, y) for x in range(planes + 1) for y in inner]
    last = [(x, y) for x in range(planes + 1) for y in outer]
    return first, last, planes * len(inner), planes * len(outer)


def rim_columns(planes, rows):
    own = [(x, y) for x in range(planes) for y in rim_rows(rows) if y < rows]
    beyond_own = [(x, rows) for x in range(planes)] + [(planes, y) for y in rim_rows(rows)]
    return own + beyond_own, len(own)


def merged(x, planes, even, early, near):
    low = ([x - 1] if x >= 1 else [], [x + 1] if x <= 1 else [])
    high = ([x + 1] if x < planes else [], [x - planes + 1] if x >= planes - 1 else [])
    if low[0] and low[1] and high[0] and high[1]:
        one = early(jnp.where(even, low[0][0], high[0][0]))
        return one + near(jnp.where(even, low[1][0], high[1][0]))

    def read(places):
        found = [early(w) for w in places[0]] + [near(v) for v in places[1]]
        return found[0] if len(found) == 1 else found[0] + found[1]

    return jnp.where(even, read(low), read(high))


def direction_at(x, planes, even, early, middle):
    if x == 0:
        return jnp.where(even, middle, early(1))
    if x == planes:
        return jnp.where(even, early(planes - 1), middle)
    return early(jnp.where(even, x - 1, x + 1))


def keep_pair(ref, place, one, two, cases):
    for k in range(3):
        part = slice(k * cases, (k + 1) * cases)
        high, rest = split(jnp.concatenate([one[part], two[part]], 0))
        lane = pl.ds(pl.multiple_of((place * 3 + k) * LANES, LANES), LANES)
        ref[0 : 2 * cases, lane] = high
        ref[2 * cases : 4 * cases, lane] = rest


def keep_split(ref, line, place, value, cases):
    for k in range(3):
        part = value[k * cases : (k + 1) * cases]
        high = part.astype(bf16).astype(f32)
        lane = slice((place * 3 + k) * LANES, (place * 3 + k + 1) * LANES)
        both = jnp.concatenate([high, part - high], 0).astype(bf16)
        ref[line : line + 2 * cases, lane] = both


def folded(value):
    half = value.shape[0] // 2
    return value[:half] + value[half:]


def products(first, second, cases):
    contract = (((1,), (1,)), ((), ()))
    out = lax.dot_general(first, second, contract, preferred_element_type=f32)
    return out[:, : 2 * cases] + out[:, 2 * cases :]


def folds(cases):
    two, count, rest = 2 * cases, 5 * cases // 12, cases // 6
    first, part = 2 * two, LANES - 2 * two
    return (
        ((slice(0, count), slice(0, two)), (slice(0, count), slice(0, two))),
        ((slice(0, count), slice(two, first)), (slice(count, 2 * count), slice(0, two))),
        ((slice(0, rest), slice(first, LANES)), (slice(2 * count, cases), slice(0, part))),
        (
            (slice(rest, 2 * rest), slice(first, first + two - part)),
            (slice(2 * count, cases), slice(part, two)),
        ),
    )


def diagonal_place(cases, index):
    line = cases // 3 + index
    return slice(line, line + 1), slice(4 * cases, 5 * cases)


def middle_kernel(
    sizes, own, pair, edge, second, start, sums_e, diffs_e, acc_se, acc_de,
    sums, diffs, middle, acc_s, acc_d, w_sums, w_diffs, both_out, gram_out, other_out,
    acc2_s, acc2_d, stiff_ref, inverse, right, again,
):
    planes, rows, cases = sizes
    block = 3 * cases
    ys, nodes_y, inner = rows + 3, rows + 1, rows - 1
    core = core_rows(rows)
    even = lax.axis_index("gx") % 2 == 0

    def codes(x):
        if 0 <= x < planes:
            return lines(own, (planes * block + x) * rows, rows)
        slot = x + 2 if x < 0 else x - planes
        outer = lines(edge, (block + slot) * rows, rows)
        if x < 0:
            return jnp.where(even, outer, lines(pair, (planes * block + planes + x) * rows, rows))
        return jnp.where(even, lines(pair, (planes * block + slot) * rows, rows), outer)

    for x in range(-2, planes + 2):
        stiff_ref[x + 2, 0:rows, :] = codes(x)
    node_inverse(stiff_ref, inner, inverse)

    def place(v, x, ref, slot):
        for y in range(1, rows):
            value = inside(ref, slot, y, rows, block) * inverse[x + 1, y - 1 : y, :]
            if v == 1:
                middle[y - 1] = value
            place_column(sums, diffs, v * inner + y - 1, value)

    def copy(v, w):
        for y in range(1, rows):
            sums[v * inner + y - 1] = sums_e[w * ys + y + 1]
            diffs[v * inner + y - 1] = diffs_e[w * ys + y + 1]

    @pl.when(even)
    def _():
        place(0, -1, edge, 0)
        place(1, 0, own, 0)
        copy(2, 0)

    @pl.when(jnp.logical_not(even))
    def _():
        copy(0, planes)
        place(1, planes, edge, 0)
        place(2, planes + 1, second, 0)

    layer = jnp.where(even, 1, planes + 1)
    find = whole(sums, diffs, inner)
    apply_elements(find, stiff_ref, acc_s, acc_d, 2, rows - 2, range(inner), layer, 1, cases)

    def image(x, y, place):
        def total(early, near):
            return merged(
                x, planes, even, lambda w: early[w * nodes_y + y],
                lambda v: near[v * inner + y - 1],
            )

        s, d = total(acc_se, acc_s), total(acc_de, acc_d)
        force = s - d + shift_up(s + d)
        scaled = force * inverse[x + 1, pl.ds(y - 1, 1), :]
        place_column(w_sums, w_diffs, x * len(core) + y - core[0], scaled)
        value = direction_at(x, planes, even, lambda w: start[w * ys + y + 1], middle[y - 1])
        keep_pair(both_out, place, value, scaled, cases)
        return force

    inner_columns, outer_columns, inner_own, outer_own = core_columns(planes, rows)
    count = len(inner_columns)
    for index, (x, y) in enumerate(inner_columns + outer_columns):
        force = image(x, y, index)
        if x < planes:
            ref, place = (again, index) if index < count else (right, index - count)
            keep_pair(ref, place, inside(own, x, y, rows, block), force, cases)
    width, two = 3 * LANES, 2 * cases
    again[: 2 * two, inner_own * width :] = jnp.zeros((2 * two, (count - inner_own) * width), bf16)

    find = whole(w_sums, w_diffs, len(core))
    kept = range(len(core))
    apply_elements(
        find, stiff_ref, acc2_s, acc2_d, planes, len(core) - 1, kept, 2, core[0], cases
    )
    for index, (x, y) in enumerate(inner_columns):
        column = x * len(core) + y - core[0]
        s, d = acc2_s[column], acc2_d[column]
        keep_split(again, 2 * two, index, s - d + shift_up(s + d), cases)
    product = products(again[...], both_out[:, : count * width], cases)
    outer_part = both_out[:, count * width : (count + outer_own) * width]
    gram_out[...] = folded(product[: 2 * two]) + folded(products(right[...], outer_part, cases))
    other_out[...] = folded(product[2 * two :])


def main_kernel(
    sizes, own, pair, edge, second, ym, yp, ym_pair, yp_pair, corners,
    start, sums_e, diffs_e, acc_se, acc_de,
    sums_m, diffs_m, middle_m, acc_sm, acc_dm, w_sm, w_dm, both_m, gram_m,
    other_m, acc2_sm, acc2_dm, both_out, system_out, stiff_ref, inverse,
    middle, sums, diffs, acc_s0, acc_d0, acc_s1, acc_d1, w_sums, w_diffs,
    acc2_s0, acc2_d0, acc2_s1, acc2_d1, right, second_m, table, dense,
):
    planes, rows, cases = sizes
    block = 3 * cases
    ys, nodes_y, inner = rows + 3, rows + 1, rows - 1
    core, rim = core_rows(rows), rim_rows(rows)
    columns, own_count = rim_columns(planes, rows)
    even = lax.axis_index("gx") % 2 == 0
    y_own, y_pair = (ym, yp, 0), (ym_pair, yp_pair, pair_base(planes, block))

    def codes(x, y):
        def read(mine, plane):
            if y == 0:
                return lines(own if mine else pair, (planes * block + plane) * rows, rows)
            return beyond_codes(y_own if mine else y_pair, planes, plane, y, block)

        if 0 <= x < planes:
            return read(True, x)
        slot = x + 2 if x < 0 else x - planes
        if y == 0:
            outer = lines(edge, (block + slot) * rows, rows)
        else:
            outer = corner_codes(corners, slot, y, block)
        within = read(False, planes + x if x < 0 else x - planes)
        return jnp.where(even, outer, within) if x < 0 else jnp.where(even, within, outer)

    for x in range(-2, planes + 2):
        for y, count in ((-2, 2), (0, rows), (rows, 2)):
            stiff_ref[x + 2, y + 2 : y + 2 + count, :] = codes(x, y)
    node_inverse(stiff_ref, ys, inverse)

    sides = (-1, 0, rows, rows + 1)

    def place(v, x, ref, slot, beyond_at):
        for i, y in enumerate(sides):
            value = inside(ref, slot, y, rows, block) if y == 0 else beyond_at(y)
            value = value * inverse[x + 1, y + 1 : y + 2, :]
            if v == 1 and y in (0, rows):
                middle[y // rows] = value
            place_column(sums, diffs, v * 4 + i, value)

    def copy(v, w):
        for i, y in enumerate(sides):
            sums[v * 4 + i] = sums_e[w * ys + y + 1]
            diffs[v * 4 + i] = diffs_e[w * ys + y + 1]

    @pl.when(even)
    def _():
        place(0, -1, edge, 0, lambda y: corner(corners, 1, y, rows, block))
        place(1, 0, own, 0, lambda y: beyond(y_own, 0, y, rows, block))
        copy(2, 0)

    @pl.when(jnp.logical_not(even))
    def _():
        copy(0, planes)
        place(1, planes, edge, 0, lambda y: corner(corners, 0, y, rows, block))
        place(2, planes + 1, second, 0, lambda y: corner(corners, 1, y, rows, block))

    def find_low(row):
        return (sums, diffs, 4, row) if row < 2 else (sums_m, diffs_m, inner, 0)

    def find_high(row):
        return (sums, diffs, 4, row + 1) if row else (sums_m, diffs_m, inner, inner - 1)

    layer = jnp.where(even, 1, planes + 1)
    apply_elements(find_low, stiff_ref, acc_s0, acc_d0, 2, 2, range(1, 3), layer, 1, cases)
    apply_elements(find_high, stiff_ref, acc_s1, acc_d1, 2, 2, range(2), layer, rows + 1, cases)

    def image(x, y, place):
        def total(early, near, low, high):
            def outer(v):
                value = low[v * 2 + y] if y < 2 else high[v * 2 + y - inner]
                return value + near[v * inner + y - 1] if y in (1, inner) else value

            return merged(x, planes, even, lambda w: early[w * nodes_y + y], outer)

        s = total(acc_se, acc_sm, acc_s0, acc_s1)
        d = total(acc_de, acc_dm, acc_d0, acc_d1)
        force = s - d + shift_up(s + d)
        scaled = force * inverse[x + 1, y + 1 : y + 2, :]
        place_column(w_sums, w_diffs, x * len(rim) + rim.index(y), scaled)
        inner_middle = middle_m[y - 1] if y in (1, inner) else middle[y // rows]
        value = direction_at(x, planes, even, lambda w: start[w * ys + y + 1], inner_middle)
        keep_pair(both_out, place, value, scaled, cases)
        return force

    for index, (x, y) in enumerate(columns):
        force = image(x, y, index)
        if index < own_count:
            keep_pair(right, index, inside(own, x, y, rows, block), force, cases)

    def find(row):
        if row in rim:
            return w_sums, w_diffs, len(rim), rim.index(row)
        return w_sm, w_dm, len(core), row - core[0]

    def find_last(row):
        return find(row + rows - 2)

    low, high = (acc2_s0, acc2_d0), (acc2_s1, acc2_d1)
    apply_elements(find, stiff_ref, *low, planes, 2, range(3), 2, 2, cases)
    apply_elements(find_last, stiff_ref, *high, planes, 2, range(3), 2, rows, cases)

    def second_force(x, y):
        s, d = None, None
        for parts, width, first in (
            (low, 3, 0), ((acc2_sm, acc2_dm), len(core), core[0]), (high, 3, rows - 2)
        ):
            if first <= y < first + width:
                column = x * width + y - first
                more = parts[0][column], parts[1][column]
                s, d = more if s is None else (s + more[0], d + more[1])
        return s - d + shift_up(s + d)

    inner_columns, outer_columns, _, _ = core_columns(planes, rows)
    two = 2 * cases
    for index, (x, y) in enumerate(outer_columns):
        keep_split(second_m, 0, index, second_force(x, y), cases)
    for index, (x, y) in enumerate(columns):
        keep_split(right, 2 * two, index, second_force(x, y), cases)
    lane = own_count * 3 * LANES
    right[: 2 * two, lane:] = jnp.zeros((2 * two, right.shape[1] - lane), bf16)

    product = products(right[...], both_out[...], cases)
    more = products(second_m[...], both_m[:, len(inner_columns) * 3 * LANES :], cases)
    gram = folded(product[: 2 * two]) + gram_m[...]
    other = folded(product[2 * two :]) + folded(more) + other_m[...]
    row = lax.broadcasted_iota(jnp.int32, (cases, cases), 0)
    column = lax.broadcasted_iota(jnp.int32, (cases, cases), 1)
    load_load, load_image = gram[:cases, :cases], gram[cases:, :cases]
    mixed, image_image = other[:, :cases], other[:, cases:]
    table[:, 0:cases] = jnp.where(row <= column, load_load, load_image)
    table[:, cases:two] = jnp.where(row <= column, mixed, image_image)
    dense[...] = jnp.zeros(dense.shape, f32)
    for target, source in folds(cases):
        dense[target] = table[source]
    for index, value in enumerate((load_image, image_image)):
        diagonal = jnp.sum(jnp.where(row == column, value, 0.0), axis=0, keepdims=True)
        dense[diagonal_place(cases, index)] = diagonal
    depth = system_out.shape[2]
    for index in range(system_out.shape[0]):
        for part in range(system_out.shape[1]):
            system_out[index, part] = dense[part * depth : (part + 1) * depth, :]


def solve_kernel(
    sizes, system, both_m, both_r, codes, out, mixing, sums, diffs, energy, square, full, dense
):
    planes, rows, cases = sizes
    two = 2 * cases
    nodes_y = rows + 1
    count = planes * rows
    total = jnp.sum(system[...], axis=0)
    depth = system.shape[2]
    for part in range(system.shape[1]):
        dense[part * depth : (part + 1) * depth, :] = total[part]
    square[...] = jnp.zeros(square.shape, f32)
    for source, target in folds(cases):
        square[target] = dense[source]
    value, turned = square[0:cases, :], jnp.transpose(square[...])
    line = lax.broadcasted_iota(jnp.int32, (cases, cases), 0)
    place = lax.broadcasted_iota(jnp.int32, (cases, cases), 1)

    def mended(start, diagonal=None):
        kept, other = value[:, start : start + cases], turned[start : start + cases, :cases]
        if diagonal is None:
            return jnp.where(line <= place, kept, other)
        inner = jnp.where(line < place, other, dense[diagonal_place(cases, diagonal)])
        return jnp.where(line > place, kept, inner)

    load_image, mixed = mended(0, 0), mended(cases)
    parts = ((load_image, mixed), (mixed, mended(cases, 1)), (mended(0), load_image))
    full[...] = jnp.zeros(full.shape, f32)
    for index, (left, right) in enumerate(parts):
        full[index * cases : (index + 1) * cases, 0:cases] = left
        full[index * cases : (index + 1) * cases, cases:two] = right
    table = full[...]
    lane = lax.broadcasted_iota(jnp.int32, (1, LANES), 1)
    gone, wide = 0, 8
    for pivot in range(0, two, wide):
        drop = pivot // 8 * 8 - gone
        table = table[drop:]
        gone += drop
        line = pivot - gone
        inner = (lane >= pivot) & (lane < pivot + wide)
        found = [table[line + p : line + p + 1, :] for p in range(wide)]
        block = [
            [jnp.broadcast_to(row[:, pivot + q : pivot + q + 1], row.shape) for q in range(wide)]
            for row in found
        ]
        solved = [
            jnp.where(lane == pivot + p, -1.0, jnp.where(inner, 0.0, found[p]))
            for p in range(wide)
        ]
        for p in range(wide):
            inverse = 1.0 / block[p][p]
            solved[p] = solved[p] * inverse
            block[p] = [value * inverse for value in block[p]]
            for q in range(wide):
                if q != p:
                    factor = block[q][p]
                    solved[q] = solved[q] - factor * solved[p]
                    for r in range(p + 1, wide):
                        block[q][r] = block[q][r] - factor * block[p][r]
        update = None
        for q in range(wide):
            term = table[:, pivot + q : pivot + q + 1] * solved[q]
            update = term if update is None else update + term
        table = jnp.where(inner, 0.0, table) - update
    answer = table[two - gone :, :two]
    high = answer.astype(bf16).astype(f32)
    mixing[...] = jnp.zeros(mixing.shape, f32)
    mixing[0:cases, 0:two] = high
    mixing[0:cases, two : 2 * two] = high
    mixing[cases:two, 0:two] = answer - high
    mix = mixing[...][:, : 2 * two].astype(bf16)

    def combined(ref, place, width):
        value = jnp.dot(
            mix, ref[:, place * 3 * LANES : (place + width) * 3 * LANES], preferred_element_type=f32
        )
        return value[:cases] + value[cases:]

    def keep(value, index, column):
        for k in range(3):
            part = value[:, (index * 3 + k) * LANES : (index * 3 + k + 1) * LANES]
            moved = shift_down(part)
            sums[column, k * cases : (k + 1) * cases, :] = part + moved
            diffs[column, k * cases : (k + 1) * cases, :] = moved - part

    inner_columns, outer_columns, _, _ = core_columns(planes, rows)
    columns, _ = rim_columns(planes, rows)
    for ref, columns in ((both_m, inner_columns + outer_columns), (both_r, columns)):
        for start in range(0, len(columns), 6):
            some = columns[start : start + 6]
            value = combined(ref, start, len(some))
            for index, (x, y) in enumerate(some):
                keep(value, index, x * nodes_y + y)

    find = whole(sums, diffs, nodes_y)
    tiles = cases // 8

    def step(plane, _):
        for tile in range(tiles):
            lower = x_modes(find, plane, 0, tile, cases)
            for row in range(rows):
                upper = x_modes(find, plane, row + 1, tile, cases)
                part = mode_energy(modes_of(lower, upper))
                if tile == 0:
                    energy[row] = part
                else:
                    energy[row] += part
                lower = upper
        total = jnp.sum(energy[...], axis=1)
        total = (-3.0 / cases) * jnp.abs(codes[plane]) * total
        for index in range(out.shape[0]):
            out[index, plane] = total
        return 0

    lax.fori_loop(0, planes, step, 0)


def smooth(ref, x, rows):
    weight = [2.5 - math.sqrt(q) for q in range(7)]
    near = {}
    for dx in range(-2, 3):
        for dy in range(-2, 3):
            q = dx * dx + dy * dy
            if q <= 5:
                value = ref[x + 2 + dx, 2 + dy : 2 + dy + rows, :]
                near[q] = value if q not in near else near[q] + value
    result = None
    for dz in range(3):
        part = None
        for q, value in near.items():
            if q + dz * dz <= 6:
                term = weight[q + dz * dz] * value
                part = term if part is None else part + term
        if dz == 0:
            result = part
        else:
            place = lax.broadcasted_iota(jnp.int32, part.shape, 1)
            forward = jnp.where(place >= LANES - dz, 0.0, pltpu.roll(part, LANES - dz, 1))
            backward = jnp.where(place < dz, 0.0, pltpu.roll(part, dz, 1))
            result = result + (forward + backward)
    return result


def scale_kernel(sizes, counts, levels, out, there):
    planes, rows, _ = sizes
    y = lax.broadcasted_iota(jnp.int32, (rows + 4, LANES), 0)
    y = y + (lax.axis_index("gy") * rows - 2)
    in_y = (y >= 0) & (y < counts[1] * rows)
    for x in range(planes + 4):
        global_x = lax.axis_index("gx") * planes + (x - 2)
        in_x = (global_x >= 0) & (global_x < counts[0] * planes)
        there[x] = jnp.where(in_y & in_x, 1.0, 0.0)
    for x in range(planes):
        density = 0.3 + 0.7 * levels[x].astype(f32) / (LEVELS - 1)
        out[x] = 1.0 / (density * smooth(there, x, rows))


def filter_kernel(sizes, counts, blocks, blocks_pair, scale, out, wide):
    planes, rows, _ = sizes
    sides_x = ((-1, planes - 2, planes, 0), (0, 0, planes, 2), (1, 0, 2, 2 + planes))
    sides_y = ((-1, rows - 2, rows, 0), (0, 0, rows, 2), (1, 0, 2, 2 + rows))
    for step_x, x0, x1, to_x in sides_x:
        for step_y, y0, y1, to_y in sides_y:
            at_x = lax.axis_index("gx") + step_x
            at_y = lax.axis_index("gy") + step_y
            inside = (at_x >= 0) & (at_x < counts[0]) & (at_y >= 0) & (at_y < counts[1])
            index = jnp.where(inside, at_x // 2 * counts[1] + at_y, 0)
            value = (blocks_pair if step_x else blocks)[index, x0:x1, y0:y1, :]
            wide[to_x : to_x + x1 - x0, to_y : to_y + y1 - y0, :] = jnp.where(inside, value, 0.0)
    for x in range(planes):
        out[x] = smooth(wide, x, rows) * scale[x]


def local(forces, levels, supports):
    _, cases, planes, rows, _ = forces.shape
    sizes = (planes, rows, cases)
    block = 3 * cases
    count_x, count_y = lax.axis_size("gx"), lax.axis_size("gy")

    def shape(blocks, codes):
        return jax.ShapeDtypeStruct((blocks * block + up8(codes), LANES), f32)

    density = 0.3 + 0.7 * levels.astype(f32) / (LEVELS - 1)
    codes = density * density * density
    codes = jnp.where(supports == 0, codes, -codes)
    counts = (count_x, count_y)
    own, edge = pl.pallas_call(
        functools.partial(pack_kernel, sizes),
        out_shape=[shape(planes * rows, planes * rows), shape(rows, 2 * rows)],
        in_specs=[VMEM] * 2,
        out_specs=[VMEM] * 2,
        compiler_params=PARAMS,
        name="pack",
    )(forces, codes)
    scale = pl.pallas_call(
        functools.partial(scale_kernel, sizes, counts),
        out_shape=jax.ShapeDtypeStruct((planes, rows, LANES), f32),
        in_specs=[VMEM],
        out_specs=VMEM,
        scratch_shapes=[pltpu.VMEM((planes + 4, rows + 4, LANES), f32)],
        compiler_params=PARAMS,
        name="scale",
    )(levels)

    def moved(value, axis, step):
        count = lax.axis_size(axis)
        pairs = [(i, i + step) for i in range(count) if 0 <= i + step < count]
        return lax.ppermute(value, axis, pairs)

    def links(first, step):
        return [(i, i + step) for i in range(first, count_x, 2) if 0 <= i + step < count_x]

    def swapped(value):
        return lax.ppermute(value, "gx", links(0, 1) + links(1, -1))

    def across(value):
        return lax.ppermute(value, "gx", links(1, 1) + links(2, -1))

    edge = across(edge)
    pair = swapped(own)
    own, pair = lax.optimization_barrier((own, pair))
    ym, yp = pl.pallas_call(
        functools.partial(rows_kernel, sizes),
        out_shape=[shape(2 * planes, 2 * planes), shape(planes, 2 * planes)],
        in_specs=[VMEM],
        out_specs=[VMEM] * 2,
        compiler_params=PARAMS,
        name="rows",
    )(own)
    from_yp, from_ym = moved(ym, "gy", -1), moved(yp, "gy", 1)
    second = pl.pallas_call(
        functools.partial(second_kernel, sizes),
        out_shape=shape(rows, 0),
        in_specs=[VMEM] * 2,
        out_specs=VMEM,
        compiler_params=PARAMS,
        name="second",
    )(swapped(codes), own)
    second = lax.ppermute(second, "gx", links(2, -1))
    from_ym, from_yp, edge = lax.optimization_barrier((from_ym, from_yp, edge))
    corners, copy = pl.pallas_call(
        functools.partial(corner_kernel, sizes),
        out_shape=[
            jax.ShapeDtypeStruct((6 * block + 32, LANES), f32),
            jax.ShapeDtypeStruct((6 * block + 16, LANES), f32),
        ],
        in_specs=[VMEM] * 2,
        out_specs=[VMEM] * 2,
        compiler_params=PARAMS,
        name="corners",
    )(from_ym, from_yp)
    if planes == 2:
        pair_ym = pair_yp = swapped(copy)
    else:
        pair_yp, pair_ym = swapped(from_yp), swapped(from_ym)
    corners = across(corners)

    devices = count_x * count_y
    nodes = (planes + 1) * (rows + 1)
    window = jax.ShapeDtypeStruct(((planes + 1) * (rows + 3), block, LANES), f32)
    partial_forces = jax.ShapeDtypeStruct((nodes, block, LANES), f32)
    early = pl.pallas_call(
        functools.partial(early_kernel, sizes),
        out_shape=[window] * 3 + [partial_forces] * 2,
        in_specs=[VMEM] * 6,
        out_specs=[VMEM] * 5,
        scratch_shapes=[
            pltpu.VMEM((planes + 2, up8(rows + 4), LANES), f32),
            pltpu.VMEM((planes + 1, up8(rows + 3), LANES), f32),
        ],
        compiler_params=PARAMS,
        cost_estimate=pl.CostEstimate(
            flops=200 * planes * rows * block * LANES, bytes_accessed=2**23, transcendentals=0
        ),
        name="early",
    )(own, pair, from_ym, from_yp, pair_ym, pair_yp)

    def columns(count):
        return jax.ShapeDtypeStruct((count, block, LANES), f32)

    def fields(lines, count):
        return jax.ShapeDtypeStruct((lines * cases, count * 3 * LANES), bf16)

    def scratch(value):
        return pltpu.VMEM(value.shape, value.dtype)

    core = len(core_rows(rows))
    middle = pl.pallas_call(
        functools.partial(middle_kernel, sizes),
        out_shape=[columns(3 * (rows - 1))] * 2
        + [columns(rows - 1)]
        + [columns(3 * (rows - 1))] * 2
        + [columns((planes + 1) * core)] * 2
        + [fields(4, (planes + 1) * core), jax.ShapeDtypeStruct((2 * cases, 2 * cases), f32)]
        + [jax.ShapeDtypeStruct((cases, 2 * cases), f32)]
        + [columns((planes + 1) * core)] * 2,
        in_specs=[VMEM] * 9,
        out_specs=[VMEM] * 12,
        scratch_shapes=[
            pltpu.VMEM((planes + 4, up8(rows), LANES), f32),
            pltpu.VMEM((planes + 3, up8(rows), LANES), f32),
            scratch(fields(4, planes * 2)),
            scratch(fields(6, (planes + 1) * (core - 2))),
        ],
        compiler_params=PARAMS,
        name="middle",
    )(own, pair, edge, second, *early)

    rim, _ = rim_columns(planes, rows)
    both, system = pl.pallas_call(
        functools.partial(main_kernel, sizes),
        out_shape=[
            fields(4, len(rim)),
            jax.ShapeDtypeStruct((devices, 5 * cases // 24, 2, LANES), f32),
        ],
        in_specs=[VMEM] * 26,
        out_specs=[VMEM] * 2,
        scratch_shapes=[
            pltpu.VMEM((planes + 4, up8(rows + 4), LANES), f32),
            pltpu.VMEM((planes + 3, up8(rows + 3), LANES), f32),
            scratch(columns(2)),
            *[scratch(columns(12))] * 2,
            *[scratch(columns(6))] * 4,
            *[scratch(columns((planes + 1) * 4))] * 2,
            *[scratch(columns((planes + 1) * 3))] * 4,
            scratch(fields(6, len(rim))),
            scratch(fields(2, (planes + 1) * 2)),
            pltpu.VMEM((cases, LANES), f32),
            pltpu.VMEM((5 * cases // 12, LANES), f32),
        ],
        compiler_params=PARAMS,
        name="operator",
    )(
        own, pair, edge, second, from_ym, from_yp, pair_ym, pair_yp, corners,
        *early, *middle,
    )

    groups = [
        [x * count_y + y for x in range(side, count_x, 2) for y in range(count_y)]
        for side in range(2)
    ]

    def gathered(copies):
        mine = lax.all_to_all(copies, ("gx", "gy"), 0, 0, axis_index_groups=groups)
        return mine, swapped(mine)

    system = lax.all_to_all(system, ("gx", "gy"), 0, 0)

    weighted = pl.pallas_call(
        functools.partial(solve_kernel, sizes),
        out_shape=jax.ShapeDtypeStruct((devices // 2, planes, rows, LANES), f32),
        in_specs=[VMEM] * 4,
        out_specs=VMEM,
        scratch_shapes=[
            pltpu.VMEM((2 * cases, LANES), f32),
            scratch(columns(nodes)),
            scratch(columns(nodes)),
            pltpu.VMEM((rows, 8, LANES), f32),
            pltpu.VMEM((LANES, LANES), f32),
            pltpu.VMEM((3 * cases, LANES), f32),
            pltpu.VMEM((5 * cases // 12, LANES), f32),
        ],
        compiler_params=PARAMS,
        name="solve",
    )(system, middle[7], both, codes)

    blocks = gathered(weighted)
    return pl.pallas_call(
        functools.partial(filter_kernel, sizes, counts),
        out_shape=jax.ShapeDtypeStruct((planes, rows, LANES), f32),
        in_specs=[VMEM] * 3,
        out_specs=VMEM,
        scratch_shapes=[pltpu.VMEM((planes + 4, rows + 4, LANES), f32)],
        compiler_params=PARAMS,
        name="cone",
    )(*blocks, scale)


def solution(mesh):
    return jax.shard_map(
        local,
        mesh=mesh,
        in_specs=(P(None, None, "gx", "gy", None), P("gx", "gy", None), P("gx", "gy", None)),
        out_specs=P("gx", "gy", None),
        check_vma=False,
    )
```
